32 devices in a mesh: wide: 8 (over y, x, core), narrow: 4 (over z).
Axes of the slice: x: 2, y: 2, z: 4, core: 2. Of those that a mesh axis runs over, the one named last changes fastest.
Arguments:
- tokens: int32 [8, 1024], P('wide'), may hold values from 0 to 32767
- picks: int32 [8, 128], P('wide'), may hold values from 0 to 1023, as said below
- targets: int32 [8, 128], P('wide'), may hold values from -1 to 32767, as said below
- lengths: int32 [8, 2], P('wide'), may hold values from 256 to 768, as said below
- skip: int32 [8], P('wide'), may hold values 0 or 1
- embed: float32 [32768, 2048], P('narrow', 'wide'), may hold values from -0.26516504 to 0.26516504
- embed_m: float32 [32768, 2048], P('narrow', 'wide'), may hold values from -3.33786e-06 to 3.33786e-06
- embed_v: float32 [32768, 2048], P('narrow', 'wide'), may hold values from 1.8715948e-13 to 7.486379e-13
- attn_qo: float32 [2048, 2, 2048], P('wide', None, 'narrow'), may hold values from -0.125 to 0.125
- attn_qo_mom: float32 [2048, 2, 2048], P('wide', None, 'narrow'), may hold values from -2.670288e-05 to 2.670288e-05
- attn_kv: float32 [2048, 2, 512], P('wide', None, 'narrow'), may hold values from -0.125 to 0.125
- attn_kv_mom: float32 [2048, 2, 512], P('wide', None, 'narrow'), may hold values from -2.670288e-05 to 2.670288e-05
- ffn: float32 [5632, 3, 2048], P('wide', None, 'narrow'), may hold values from -0.125 to 0.125
- ffn_mom: float32 [5632, 3, 2048], P('wide', None, 'narrow'), may hold values from -2.670288e-05 to 2.670288e-05
- gains: float32 [3, 2048], P(None, ('wide', 'narrow')), may hold values from 0.24 to 1.8
- gains_m: float32 [3, 2048], P(None, ('wide', 'narrow')), may hold values from -1.335144e-05 to 1.335144e-05
- gains_v: float32 [3, 2048], P(None, ('wide', 'narrow')), may hold values from 3.030201e-12 to 1.1942557e-11
Outputs:
- loss_sum: float32 [], replicated
- loss_count: float32 [], replicated
- grad_norm: float32 [], replicated
- embed_new: float32 [32768, 2048], P('narrow', 'wide')
- embed_m_new: float32 [32768, 2048], P('narrow', 'wide')
- embed_v_new: float32 [32768, 2048], P('narrow', 'wide')
- attn_qo_new: float32 [2048, 2, 2048], P('wide', None, 'narrow')
- attn_qo_mom_new: float32 [2048, 2, 2048], P('wide', None, 'narrow')
- attn_kv_new: float32 [2048, 2, 512], P('wide', None, 'narrow')
- attn_kv_mom_new: float32 [2048, 2, 512], P('wide', None, 'narrow')
- ffn_new: float32 [5632, 3, 2048], P('wide', None, 'narrow')
- ffn_mom_new: float32 [5632, 3, 2048], P('wide', None, 'narrow')
- gains_new: float32 [3, 2048], P(None, ('wide', 'narrow'))
- gains_m_new: float32 [3, 2048], P(None, ('wide', 'narrow'))
- gains_v_new: float32 [3, 2048], P(None, ('wide', 'narrow'))
The draws below stay inside these ranges and needn't reach their ends.
Inputs may be any that keep to these rules, and one draw needn't show every extreme that they name: Within a pack the picks are distinct and increasing; the first is 0 and the last 1023. `targets`: -1 marks a picked position that does not count. Each pack's lengths sum to 1024; some pack holds a sequence of 768 tokens.
All inputs are finite; a program needn't handle non-finite values. No bound on the sum of `skip` on one device may be relied on, other than what follows from the above.
Results may differ from the reference program's by a relative error of at most 0.017.
The reference program's roundings to bfloat16 on the way count: a program that leaves them out, or rounds other values in their place, can miss the bound.
Values may be sent and summed in bfloat16 or wider, within the bound.
A program may use at most 440 MiB of HBM per device.

```python
import math
import jax
import jax.numpy as jnp
import numpy as np
from jax import lax

D = 2048
HEADS = 16
HD = 128
KVH = 4
FF = 5632
V = 32768
NS_STEPS = 5
STEP = 10
SEQ = 1024
SEL = 128
PACKS = 8
MOST = 768
NPARAM = 112203776
N_WIDE = 8


def pick_table(key):
    key = jax.random.fold_in(key, 14)
    keys = jax.random.split(key, PACKS)

    def one_pack(pack_key):
        inner = jax.random.permutation(pack_key, SEQ - 2)[:SEL - 2].astype(jnp.int32) + 1
        both_ends = jnp.array([0, SEQ - 1], dtype=jnp.int32)
        return jnp.sort(jnp.concatenate([both_ends, inner]))
    return jax.vmap(one_pack)(keys).astype(jnp.int32)


def draw_picks(key, part):
    return pick_table(key)


def draw_targets(key, part):
    chosen = pick_table(key)
    key = jax.random.fold_in(key, 11)
    id_key, roll_key = jax.random.split(key)
    next_ids = jax.random.randint(id_key, (PACKS, SEL), 0, V, dtype=jnp.int32)
    pack_at = jnp.arange(PACKS, dtype=jnp.int32)[:, None]
    share = 150 + 850 * (chosen * PACKS + pack_at * SEQ) // (2 * SEQ * PACKS)
    roll = jax.random.randint(roll_key, (PACKS, SEL), 0, 1000, dtype=jnp.int32)
    return jnp.where(roll < share, next_ids, -1).astype(jnp.int32)


def draw_lengths(key, part):
    key = jax.random.fold_in(key, 15)
    first_key, full_key = jax.random.split(key)
    first = jax.random.randint(first_key, (PACKS,), SEQ // 4, MOST + 1, dtype=jnp.int32)
    full_pack = jax.random.randint(full_key, (), 0, PACKS, dtype=jnp.int32)
    first = jnp.where(jnp.arange(PACKS, dtype=jnp.int32) == full_pack, MOST, first)
    return jnp.stack([first, SEQ - first], axis=1).astype(jnp.int32)


def draw_embed(key, part):
    key = jax.random.fold_in(key, 12)
    place = jnp.arange(V, dtype=jnp.float32)[:, None] / V
    rise = 1.0 + 2.0 * place
    noise = jnp.clip(jax.random.normal(key, (V, D), jnp.float32), -4.0, 4.0)
    return noise * rise / math.sqrt(D)


def draw_gains(key, part):
    key = jax.random.fold_in(key, 13)
    place = jnp.arange(D, dtype=jnp.float32)[None, :] / D
    jitter = jax.random.uniform(key, (3, D), jnp.float32, 0.8, 1.2)
    return (0.5 + place) * jitter


def touch_ends(result, rng, low, top_value):
    spot = [jax.random.randint(jax.random.fold_in(rng, axis), (), 0, length) for axis, length in enumerate(result.shape)]
    longest = result.shape.index(max(result.shape))
    next_to = spot[:longest] + [(spot[longest] + 1) % result.shape[longest]] + spot[longest + 1:]
    return result.at[tuple(spot)].set(low).at[tuple(next_to)].set(top_value)


def steps_of(own_key, dims, cuts, smallest, top_value):
    level = 1.0
    for dim, blocks in cuts:
        draws = jax.random.uniform(jax.random.fold_in(jax.random.fold_in(own_key, 6), dim), (blocks,), jnp.float32, smallest / len(cuts), top_value / len(cuts))
        level = level * jnp.repeat(jnp.exp(draws), dims[dim] // blocks).reshape((-1,) + (1,) * (len(dims) - 1 - dim))
    return level


def cumulative_ranks(number_of, lean):
    weights = [(1 << 20) // math.isqrt(grade ** lean) + 1 for grade in range(1, number_of + 1)]
    scale = 1 + sum(weights) // (1 << 30)
    return np.cumsum(np.array([max(1, weight // scale) for weight in weights]))


def ranked_ids(rng, dims, amount, skew):
    listing = cumulative_ranks(amount, skew)
    lot = jax.random.randint(jax.random.fold_in(rng, 1), dims, 0, int(listing[amount - 1]))
    rank = jnp.searchsorted(jnp.asarray(listing, jnp.int32), lot, side="right")
    return jax.random.permutation(jax.random.fold_in(rng, 2), amount)[rank].astype(jnp.int32)


def centred(own_key, dims, spread, bound, shards=(), kind=jnp.bfloat16):
    result = spread * jax.random.normal(own_key, dims, jnp.float32)
    if shards:
        result = result * steps_of(own_key, dims, shards, -0.22, 0.18)
    return jnp.clip(result, -bound, bound).astype(kind)


def setup_inputs(seed: int = 0) -> dict:
    seeds = jax.random.split(jax.random.key(seed), 18)
    tokens = touch_ends(ranked_ids(seeds[0], (PACKS, SEQ), V, 2), jax.random.fold_in(seeds[0], 3), 0, V - 1).astype(jnp.int32)
    picks = draw_picks(jax.random.fold_in(seeds[17], 71), 0)
    targets = draw_targets(jax.random.fold_in(seeds[17], 71), 0)
    lengths = draw_lengths(jax.random.fold_in(seeds[17], 71), 0)
    skip = touch_ends((jax.random.randint(seeds[4], (PACKS,), 0, 4) < 1).astype(jnp.int32), jax.random.fold_in(seeds[4], 1), 0, 1)
    embed = draw_embed(jax.random.fold_in(seeds[17], 71), 0)
    embed_m = centred(seeds[6], (V, D), (0.00222 * NPARAM ** -0.5), 3.337860107421875e-06, ((0, 4), (1, 8)), jnp.float32)
    embed_v = jnp.clip(jnp.exp(math.log(7.486379138138544e-13) - 1.3862944 * jax.random.uniform(seeds[7], (V, D), jnp.float32) ** steps_of(seeds[7], (V, D), ((0, 4), (1, 8)), -0.2, 0.2)), 1.871594784534636e-13, 7.486379138138544e-13)
    attn_qo = centred(seeds[8], (D, 2, HEADS * HD), D ** -0.5, 0.125, ((0, 8), (2, 4)), jnp.float32)
    attn_qo_mom = centred(seeds[9], (D, 2, HEADS * HD), (0.02 * NPARAM ** -0.5), 2.6702880859375e-05, ((0, 8), (2, 4)), jnp.float32)
    attn_kv = centred(seeds[10], (D, 2, KVH * HD), D ** -0.5, 0.125, ((0, 8), (2, 4)), jnp.float32)
    attn_kv_mom = centred(seeds[11], (D, 2, KVH * HD), (0.02 * NPARAM ** -0.5), 2.6702880859375e-05, ((0, 8), (2, 4)), jnp.float32)
    ffn = centred(seeds[12], (FF, 3, D), D ** -0.5, 0.125, ((0, 8), (2, 4)), jnp.float32)
    ffn_mom = centred(seeds[13], (FF, 3, D), (0.02 * NPARAM ** -0.5), 2.6702880859375e-05, ((0, 8), (2, 4)), jnp.float32)
    gains = draw_gains(jax.random.fold_in(seeds[17], 71), 0)
    gains_m = centred(seeds[15], (3, D), (0.0089 * NPARAM ** -0.5), 1.33514404296875e-05, ((1, 32),), jnp.float32)
    gains_v = jnp.clip(jnp.exp(math.log(1.1942557186228608e-11) - 1.3714793 * jax.random.uniform(seeds[16], (3, D), jnp.float32) ** steps_of(seeds[16], (3, D), ((1, 32),), -0.2, 0.2)), 3.030201090048479e-12, 1.1942557186228608e-11)
    return dict(tokens=tokens, picks=picks, targets=targets, lengths=lengths, skip=skip, embed=embed, embed_m=embed_m, embed_v=embed_v, attn_qo=attn_qo, attn_qo_mom=attn_qo_mom, attn_kv=attn_kv, attn_kv_mom=attn_kv_mom, ffn=ffn, ffn_mom=ffn_mom, gains=gains, gains_m=gains_m, gains_v=gains_v)


HIGHEST = lax.Precision.HIGHEST
NORM_EPS = 1e-05
ROPE_BASE = 10000.0
EXIT_EARLY = 0.25
EXIT_LAST = 1.0
CLIP_NORM = 0.02
BETA_ONE = 0.9
BETA_TWO = 0.95
ADAM_EPS = 1e-08
RATE_ADAM = 0.02
RATE_GAIN = 0.3
RATE_MUON = 0.3
WEIGHT_DECAY = 0.1
MOMENTUM = 0.95
NEWTON_A = 3.4445
NEWTON_B = -4.775
NEWTON_C = 2.0315
MASKED = -1e+30

@jax.custom_vjp
def low(v):
    return lax.optimization_barrier(v.astype(jnp.bfloat16)).astype(jnp.float32)

@jax.custom_vjp
def low_back(v):
    return v

def low_keep(v):
    return (low(v), None)

def low_pass(kept, grad):
    return (grad,)

def back_keep(v):
    return (v, None)

def back_low(kept, grad):
    return (low(grad),)
low.defvjp(low_keep, low_pass)
low_back.defvjp(back_keep, back_low)

def both_ways(value):
    return low(low_back(value))

def norm_rows(values, gain_row):
    return values * lax.rsqrt(lax.optimization_barrier(jnp.mean(values * values, axis=-1, keepdims=True)) + NORM_EPS) * gain_row

def positions(lens, seq_len):
    ends = jnp.cumsum(lens)
    where_at = jnp.arange(seq_len, dtype=jnp.int32)
    segment = lax.optimization_barrier(jnp.sum((where_at[:, None] >= ends[None, :]).astype(jnp.int32), axis=1))
    starts = ends - lens
    member = segment[:, None] == jnp.arange(lens.shape[0], dtype=jnp.int32)[None, :]
    begin = lax.optimization_barrier(jnp.sum(jnp.where(member, starts[None, :], 0), axis=1))
    offset_pos = (where_at - begin).astype(jnp.float32)
    inverse = ROPE_BASE ** (-2.0 * jnp.arange(HD // 2, dtype=jnp.float32) / HD)
    angle = offset_pos[:, None] * inverse[None, :]
    return (segment, jnp.cos(angle), jnp.sin(angle))

def rotate(values, cosine, sine):
    half = values.shape[-1] // 2
    first, second = (values[..., :half], values[..., half:])
    cosine, sine = (cosine[:, None, :], sine[:, None, :])
    return jnp.concatenate([first * cosine - second * sine, second * cosine + first * sine], axis=-1)

def attend(queries, keys, values, segment):
    seq_len = queries.shape[0]
    grouped = queries.reshape(seq_len, KVH, HEADS // KVH, HD)
    scores = jnp.einsum('qkgd,pkd->kgqp', grouped, keys, precision=HIGHEST) * HD ** (-0.5)
    where_at = jnp.arange(seq_len, dtype=jnp.int32)
    allowed = (segment[:, None] == segment[None, :]) & (where_at[:, None] >= where_at[None, :])
    scores = low_back(jnp.where(allowed, scores, MASKED))
    weights = low(jax.nn.softmax(scores, axis=-1))
    mixed = jnp.einsum('kgqp,pkd->qkgd', weights, values, precision=HIGHEST)
    return mixed.reshape(seq_len, HEADS * HD)

def exit_loss(features, table, target, counted):
    logits = low_back(jnp.dot(features, table.T, precision=HIGHEST))
    log_total = jax.nn.logsumexp(logits, axis=-1)
    picked = jnp.take_along_axis(logits, jnp.maximum(target, 0)[:, None], axis=1)[:, 0]
    return jnp.sum(counted * (log_total - picked))

def pack_loss(table, qo_w, kv_w, ffn_w, gain_w, token_ids, pick_ids, target, lens, skipped):
    segment, cosine, sine = positions(lens, SEQ)
    counted = (target >= 0).astype(jnp.float32)
    start_h = table[token_ids]
    normed = low(norm_rows(start_h, gain_w[0]))
    queries = low_back(jnp.dot(normed, qo_w[:, 0], precision=HIGHEST)).reshape(SEQ, HEADS, HD)
    keys = low_back(jnp.dot(normed, kv_w[:, 0], precision=HIGHEST)).reshape(SEQ, KVH, HD)
    values = both_ways(jnp.dot(normed, kv_w[:, 1], precision=HIGHEST)).reshape(SEQ, KVH, HD)
    queries = low(rotate(queries, cosine, sine))
    keys = low(rotate(keys, cosine, sine))
    mixed = both_ways(attend(queries, keys, values, segment))
    middle = start_h + low_back(jnp.dot(mixed, qo_w[:, 1].T, precision=HIGHEST))
    inner = low(norm_rows(middle, gain_w[1]))
    gate_pre = low_back(jnp.dot(inner, ffn_w[:, 0].T, precision=HIGHEST))
    up_pre = low_back(jnp.dot(inner, ffn_w[:, 1].T, precision=HIGHEST))
    hidden = low(jax.nn.silu(gate_pre) * up_pre)
    final_h = middle + low_back(jnp.dot(hidden, ffn_w[:, 2], precision=HIGHEST))
    final_h = jnp.where(skipped > 0, start_h, final_h)
    early = low(norm_rows(start_h, gain_w[2]))[pick_ids]
    late = low(norm_rows(final_h, gain_w[2]))[pick_ids]
    return EXIT_EARLY * exit_loss(early, table, target, counted) + EXIT_LAST * exit_loss(late, table, target, counted)

def adamw(weight, first_m, second_m, grad, rate, decay):
    first_new = BETA_ONE * first_m + (1.0 - BETA_ONE) * grad
    second_new = BETA_TWO * second_m + (1.0 - BETA_TWO) * grad * grad
    update = first_new / (1.0 - BETA_ONE ** STEP) / (jnp.sqrt(second_new / (1.0 - BETA_TWO ** STEP)) + ADAM_EPS)
    return (weight * (1.0 - rate * decay) - rate * update, first_new, second_new)

def orthogonal(matrix):
    rows, cols = matrix.shape
    blocks = matrix.reshape(N_WIDE, rows // N_WIDE, cols)
    blocks = blocks / (jnp.sqrt(lax.optimization_barrier(jnp.sum(blocks * blocks, axis=(1, 2), keepdims=True))) + 1e-07)
    for iteration in range(NS_STEPS):
        gram = jnp.einsum('brc,bsc->brs', blocks, blocks, precision=HIGHEST)
        square = jnp.einsum('brs,bst->brt', gram, gram, precision=HIGHEST)
        blocks = NEWTON_A * blocks + jnp.einsum('brs,bsc->brc', NEWTON_B * gram + NEWTON_C * square, blocks, precision=HIGHEST)
    return blocks.reshape(rows, cols)

def muon(weight, momentum, grad):
    mom_new = MOMENTUM * momentum + grad
    direction = jnp.stack([orthogonal(mom_new[:, member]) for member in range(mom_new.shape[1])], axis=1)
    return (weight * (1.0 - RATE_MUON * WEIGHT_DECAY) - RATE_MUON * direction, mom_new)

def reference(tokens, picks, targets, lengths, skip, embed, embed_m, embed_v, attn_qo, attn_qo_mom, attn_kv, attn_kv_mom, ffn, ffn_mom, gains, gains_m, gains_v):

    def total_loss(table, qo_w, kv_w, ffn_w, gain_w):
        table, qo_w, kv_w, ffn_w, gain_w = (low(table), low(qo_w), low(kv_w), low(ffn_w), low(gain_w))

        def one_pack(pack_data):
            return jax.checkpoint(pack_loss)(table, qo_w, kv_w, ffn_w, gain_w, *pack_data)
        return jnp.sum(lax.map(one_pack, (tokens, picks, targets, lengths, skip)))
    loss_sum, pull = jax.vjp(total_loss, embed, attn_qo, attn_kv, ffn, gains)
    grads = pull(jnp.ones_like(loss_sum))
    loss_count = jnp.sum((targets >= 0).astype(jnp.float32))
    grads = [grad / loss_count for grad in grads]
    grad_norm = jnp.sqrt(sum((jnp.sum(grad * grad) for grad in grads)))
    factor = jnp.minimum(1.0, CLIP_NORM / (grad_norm + 1e-06))
    grad_embed, grad_qo, grad_kv, grad_ffn, grad_gain = [grad * factor for grad in grads]
    embed_new, embed_m_new, embed_v_new = adamw(embed, embed_m, embed_v, grad_embed, RATE_ADAM, WEIGHT_DECAY)
    gains_new, gains_m_new, gains_v_new = adamw(gains, gains_m, gains_v, grad_gain, RATE_GAIN, 0.0)
    qo_new, qo_mom_new = muon(attn_qo, attn_qo_mom, grad_qo)
    kv_new, kv_mom_new = muon(attn_kv, attn_kv_mom, grad_kv)
    ffn_new, ffn_mom_new = muon(ffn, ffn_mom, grad_ffn)
    return (loss_sum, loss_count, grad_norm, embed_new, embed_m_new, embed_v_new, qo_new, qo_mom_new, kv_new, kv_mom_new, ffn_new, ffn_mom_new, gains_new, gains_m_new, gains_v_new)
```

```python
import functools

import jax
import jax.numpy as jnp
from jax import lax
from jax.experimental import pallas as pl
from jax.experimental.pallas import tpu as pltpu
from jax.sharding import PartitionSpec as P

HEADS = 16
HD = 128
KVH = 4
NS_STEPS = 5
STEP = 10


NORM_EPS = 1e-05
ROPE_BASE = 10000.0
EXIT_EARLY = 0.25
EXIT_LAST = 1.0
CLIP_NORM = 0.02
BETA_ONE = 0.9
BETA_TWO = 0.95
ADAM_EPS = 1e-08
RATE_ADAM = 0.02
RATE_GAIN = 0.3
RATE_MUON = 0.3
WEIGHT_DECAY = 0.1
MOMENTUM = 0.95
NEWTON_A = 3.4445
NEWTON_B = -4.775
NEWTON_C = 2.0315
MASKED = -1e30
LOW = jnp.bfloat16
FULL = jnp.float32
BOTH = ("wide", "narrow")
ROWS_IN_BLOCK = 1024
UNROLL = 16
VMEM_BYTES = 56 * 1024 * 1024


def dot(first, second, first_dim, second_dim):
    return lax.dot_general(
        first, second, (((first_dim,), (second_dim,)), ((), ())), preferred_element_type=FULL
    )


def norm_rows(values, gain_row):
    return (
        values * lax.rsqrt(jnp.mean(values * values, axis=-1, keepdims=True) + NORM_EPS) * gain_row
    )


def norm_back(values, gain_row, grad):
    output, pull = jax.vjp(norm_rows, values, gain_row)
    return pull(grad)


def segments_at(lens, where_at):
    ends = jnp.cumsum(lens)
    return jnp.sum((where_at[:, None] >= ends[None, :]).astype(jnp.int32), axis=1)


def angles_at(lens, where_at):
    segment = segments_at(lens, where_at)
    starts = jnp.cumsum(lens) - lens
    member = segment[:, None] == jnp.arange(lens.shape[0], dtype=jnp.int32)[None, :]
    begin = jnp.sum(jnp.where(member, starts[None, :], 0), axis=1)
    offset_pos = (where_at - begin).astype(FULL)
    inverse = ROPE_BASE ** (-2.0 * jnp.arange(HD // 2, dtype=FULL) / HD)
    angle = offset_pos[:, None] * inverse[None, :]
    return (segment, jnp.cos(angle), jnp.sin(angle))


def rotate(values, cosine, sine):
    half = values.shape[-1] // 2
    first, second = (values[..., :half], values[..., half:])
    return jnp.concatenate(
        [first * cosine - second * sine, second * cosine + first * sine], axis=-1
    )


def unrotate(values, cosine, sine):
    return rotate(values, cosine, -sine)


def lookup_body(ids_ref, table_ref, out_ref, held, rows, sem):
    block = pl.program_id(0)
    vocab = table_ref.shape[0]

    @pl.when(block == 0)
    def _():
        load = pltpu.make_async_copy(table_ref, held.at[pl.ds(0, vocab)], sem)
        load.start()
        held[pl.ds(vocab, 8), :] = jnp.zeros((8, held.shape[1]), FULL)
        load.wait()

    def step(group, carry):
        for member in range(UNROLL):
            at = group * UNROLL + member
            spot = ids_ref[block * ROWS_IN_BLOCK + at]
            rows[pl.ds(at, 1), :] = held[pl.ds(spot, 1), :]
        return carry

    lax.fori_loop(0, ROWS_IN_BLOCK // UNROLL, step, 0)
    out_ref[...] = rows[...].astype(LOW)


def lookup(table, ids):
    vocab, columns = table.shape
    count = ids.shape[0]
    return pl.pallas_call(
        lookup_body,
        grid_spec=pltpu.PrefetchScalarGridSpec(
            num_scalar_prefetch=1,
            grid=(count // ROWS_IN_BLOCK,),
            in_specs=[pl.BlockSpec(memory_space=pl.ANY)],
            out_specs=pl.BlockSpec((ROWS_IN_BLOCK, columns), lambda block, ids_ref: (block, 0)),
            scratch_shapes=[
                pltpu.VMEM((vocab + 8, columns), FULL),
                pltpu.VMEM((ROWS_IN_BLOCK, columns), FULL),
                pltpu.SemaphoreType.DMA,
            ],
        ),
        out_shape=jax.ShapeDtypeStruct((count, columns), LOW),
        compiler_params=pltpu.CompilerParams(vmem_limit_bytes=VMEM_BYTES),
        cost_estimate=pl.CostEstimate(
            flops=0, bytes_accessed=vocab * columns * 4 + count * columns * 32, transcendentals=0
        ),
        name="lookup",
    )(ids, table)


def spread_body(ids_ref, rows_ref, head_ref, out_ref, square_ref, even, odd, rows, sem):
    block = pl.program_id(0)
    vocab = out_ref.shape[0]

    @pl.when(block == 0)
    def _():
        even[...] = jnp.zeros_like(even)
        odd[...] = jnp.zeros_like(odd)

    rows[...] = rows_ref[...].astype(FULL)

    def step(group, carry):
        for member in range(UNROLL):
            at = group * UNROLL + member
            spot = pl.ds(ids_ref[block * ROWS_IN_BLOCK + at], 1)
            total = even if member % 2 == 0 else odd
            total[spot, :] = total[spot, :] + rows[pl.ds(at, 1), :]
        return carry

    lax.fori_loop(0, ROWS_IN_BLOCK // UNROLL, step, 0)

    @pl.when(block == pl.num_programs(0) - 1)
    def _():
        chunk = 256

        def finish(part, squares):
            spot = pl.ds(pl.multiple_of(part * chunk, chunk), chunk)
            value = even[spot, :] + odd[spot, :] + head_ref[spot, :].astype(FULL)
            even[spot, :] = value
            return squares + jnp.sum((value * value).reshape(chunk // 8, 8, -1), axis=0)

        squares = lax.fori_loop(
            0, vocab // chunk, finish, jnp.zeros((8, even.shape[1]), FULL)
        )
        square_ref[...] = squares
        store = pltpu.make_async_copy(even.at[pl.ds(0, vocab)], out_ref, sem)
        store.start()
        store.wait()


def spread(ids, rows, head):
    vocab, columns = head.shape
    count = ids.shape[0]
    return pl.pallas_call(
        spread_body,
        grid_spec=pltpu.PrefetchScalarGridSpec(
            num_scalar_prefetch=1,
            grid=(count // ROWS_IN_BLOCK,),
            in_specs=[
                pl.BlockSpec((ROWS_IN_BLOCK, columns), lambda block, ids_ref: (block, 0)),
                pl.BlockSpec((vocab, columns), lambda block, ids_ref: (0, 0)),
            ],
            out_specs=[
                pl.BlockSpec(memory_space=pl.ANY),
                pl.BlockSpec((8, columns), lambda block, ids_ref: (0, 0)),
            ],
            scratch_shapes=[
                pltpu.VMEM((vocab + 8, columns), FULL),
                pltpu.VMEM((vocab + 8, columns), FULL),
                pltpu.VMEM((ROWS_IN_BLOCK, columns), FULL),
                pltpu.SemaphoreType.DMA,
            ],
        ),
        out_shape=[
            jax.ShapeDtypeStruct((vocab, columns), FULL),
            jax.ShapeDtypeStruct((8, columns), FULL),
        ],
        compiler_params=pltpu.CompilerParams(vmem_limit_bytes=VMEM_BYTES),
        cost_estimate=pl.CostEstimate(
            flops=count * columns, bytes_accessed=count * columns * 64, transcendentals=0
        ),
        name="spread",
    )(ids, rows, head)


def orthogonalize(blocks):
    norm = jnp.sqrt(jnp.sum(blocks * blocks, axis=(1, 2), keepdims=True)) + 1e-07
    current = blocks / norm
    rows = blocks.shape[1]
    eye = jnp.eye(rows, dtype=FULL)[None]

    def centre(gram):
        middle = jnp.sum(gram * eye, axis=(1, 2), keepdims=True) / rows
        return (middle, gram - middle * eye)

    for iteration in range(NS_STEPS):
        low = current.astype(LOW)
        gram = jnp.einsum("jrc,jsc->jrs", low, low, preferred_element_type=FULL)
        middle, rest = centre(gram)
        rest_low = rest.astype(LOW)
        square = jnp.einsum("jrs,jst->jrt", rest_low, rest_low, preferred_element_type=FULL)
        square = square + 2.0 * middle * rest + middle * middle * eye
        middle, rest = centre(NEWTON_B * gram + NEWTON_C * square)
        current = (NEWTON_A + middle) * current + jnp.einsum(
            "jrs,jsc->jrc", rest.astype(LOW), low, preferred_element_type=FULL
        )
    return current


def adamw(weight, first_m, second_m, grad, rate, decay):
    first_new = BETA_ONE * first_m + (1.0 - BETA_ONE) * grad
    second_new = BETA_TWO * second_m + (1.0 - BETA_TWO) * grad * grad
    update = (
        first_new
        / (1.0 - BETA_ONE**STEP)
        / (jnp.sqrt(second_new / (1.0 - BETA_TWO**STEP)) + ADAM_EPS)
    )
    return (weight * (1.0 - rate * decay) - rate * update, first_new, second_new)


def exchange(parts, axis):
    return lax.all_to_all(parts, axis, 0, 0, tiled=True)


def side_by_side(parts):
    count, rows, columns = parts.shape
    return jnp.moveaxis(parts, 0, 1).reshape(rows, count * columns)


def cut_columns(values, count):
    rows, columns = values.shape
    return jnp.moveaxis(values.reshape(rows, count, columns // count), 1, 0)


def gather_rows(values, axis):
    return lax.all_gather(values, axis, axis=0, tiled=True)


def gather_columns(values, axis):
    return lax.all_gather(values, axis, axis=1, tiled=True)


def per_device(
    tokens,
    picks,
    targets,
    lengths,
    skip,
    embed,
    embed_m,
    embed_v,
    attn_qo,
    attn_qo_mom,
    attn_kv,
    attn_kv_mom,
    ffn,
    ffn_mom,
    gains,
    gains_m,
    gains_v,
):
    wide_count = lax.axis_size("wide")
    narrow_count = lax.axis_size("narrow")
    narrow_spot = lax.axis_index("narrow")
    wide_spot = lax.axis_index("wide")
    seq_len = tokens.shape[1]
    sel = picks.shape[1]
    vocab_rows, columns = embed.shape
    width = columns * wide_count
    own_rows = sel // narrow_count
    heads_own = HEADS // narrow_count
    repeat = max(1, narrow_count // KVH)
    ffn_rows = ffn.shape[0]
    lens = lengths[0]
    pick_ids = picks[0]
    keep_layer = (1 - skip[0]).astype(FULL)

    all_ints = gather_rows(
        jnp.concatenate([tokens[0], targets[0]])[None], "wide"
    )
    tokens_all = all_ints[:, :seq_len].reshape(-1)
    targets_all = all_ints[:, seq_len:].reshape(-1)
    gain_w = gather_columns(gains.astype(LOW), BOTH).astype(FULL)

    local_ids = tokens_all - narrow_spot * vocab_rows
    inside = (local_ids >= 0) & (local_ids < vocab_rows)
    spots = jnp.where(inside, local_ids, vocab_rows)
    found = lookup(embed, spots)
    hidden_rows = side_by_side(exchange(found.reshape(wide_count, seq_len, columns), "wide"))

    kv_low = jnp.moveaxis(attn_kv, 1, 0).astype(LOW)
    kv_w = lax.all_gather(
        lax.all_gather(kv_low, "narrow", axis=2, tiled=True), "wide", axis=1, tiled=True
    )
    qo_low = jnp.moveaxis(attn_qo, 1, 0).astype(LOW)
    q_w = gather_rows(qo_low[0], "wide")
    o_w = gather_rows(qo_low[1], "wide")
    ffn_low = jnp.moveaxis(ffn, 1, 0).astype(LOW)
    ffn_cut = ffn_low.reshape(3, narrow_count, ffn_rows // narrow_count, ffn_low.shape[2])
    ffn_sub = exchange(jnp.moveaxis(ffn_cut, 1, 0), "narrow")
    ffn_w = [gather_rows(side_by_side(ffn_sub[:, j]), "wide") for j in range(3)]
    table_own = side_by_side(
        exchange(embed.astype(LOW).reshape(wide_count, vocab_rows // wide_count, columns), "wide")
    )
    q_full = gather_rows(gather_columns(qo_low[0], "narrow"), "wide")

    mom_qo = jnp.moveaxis(attn_qo_mom, 1, 0)
    mom_kv = jnp.moveaxis(attn_kv_mom, 1, 0)
    mom_ffn = jnp.moveaxis(ffn_mom, 1, 0)
    slot = mom_ffn.shape[1] * mom_ffn.shape[2]

    def pack_small(qo_part, kv_part):
        flat = jnp.concatenate([qo_part.reshape(-1), kv_part.reshape(-1)])
        return jnp.pad(flat, (0, slot - flat.shape[0]))

    def unpack_small(flat):
        lead = flat.shape[:-1]
        qo_size, kv_size = mom_qo.size, mom_kv.size
        return (
            flat[..., :qo_size].reshape(lead + mom_qo.shape),
            flat[..., qo_size : qo_size + kv_size].reshape(lead + mom_kv.shape),
        )

    def one_per_owner(ffn_part, qo_part, kv_part):
        parts = [ffn_part[j].reshape(-1) for j in range(3)] + [pack_small(qo_part, kv_part)]
        parts = parts + [jnp.zeros_like(parts[0])] * (narrow_count - 4)
        return jnp.stack(parts)

    mom_owned = exchange(one_per_owner(mom_ffn, mom_qo, mom_kv), "narrow")

    seg_all, cosine_all, sine_all = angles_at(lens, jnp.arange(seq_len, dtype=jnp.int32))
    seg_mine, cosine, sine = angles_at(lens, pick_ids)
    inside_mine = lax.dynamic_slice_in_dim(inside, wide_spot * seq_len, seq_len, 0)
    pick_hot = (
        pick_ids[:, None] == jnp.arange(seq_len, dtype=jnp.int32)[None, :]
    ).astype(LOW)

    rows_full = hidden_rows.astype(FULL)
    normed_all = norm_rows(rows_full, gain_w[0]).astype(LOW)
    keys_part = dot(normed_all, kv_w[0], 1, 0).reshape(seq_len, KVH, HD)
    keys_part = rotate(keys_part, cosine_all[:, None], sine_all[:, None]).astype(LOW)
    values_part = dot(normed_all, kv_w[1], 1, 0).reshape(seq_len, KVH, HD).astype(LOW)
    by_head = jnp.moveaxis(jnp.stack([keys_part, values_part]), 2, 0)
    by_head = jnp.repeat(by_head, repeat, axis=0)
    own_head = lax.psum_scatter(by_head, "narrow", scatter_dimension=0, tiled=True)
    groups = own_head.shape[0]
    keys, values = own_head[:, 0], own_head[:, 1]
    start_h = lax.psum(dot(pick_hot, hidden_rows, 1, 0).astype(LOW), "narrow").astype(FULL)

    normed = norm_rows(start_h, gain_w[0]).astype(LOW)
    queries = dot(normed, q_w, 1, 0).reshape(sel, heads_own, HD)
    queries = rotate(queries, cosine[:, None], sine[:, None]).astype(LOW)
    grouped = queries.reshape(sel, groups, heads_own // groups, HD)
    scale = HD ** (-0.5)
    scores = jnp.einsum("tkgd,ksd->kgts", grouped, keys, preferred_element_type=FULL) * scale
    allowed = (seg_mine[:, None] == seg_all[None, :]) & (
        pick_ids[:, None] >= jnp.arange(seq_len, dtype=jnp.int32)[None, :]
    )
    scores = jnp.where(allowed, scores, MASKED)
    shifted_exp = jnp.exp(scores - jnp.max(scores, axis=-1, keepdims=True))
    probs = shifted_exp / jnp.sum(shifted_exp, axis=-1, keepdims=True)
    probs_low = probs.astype(LOW)
    mixed = jnp.einsum("kgts,ksd->tkgd", probs_low, values, preferred_element_type=FULL)
    mixed = mixed.reshape(sel, heads_own * HD).astype(LOW)

    def own(values_all):
        return lax.dynamic_slice_in_dim(values_all, narrow_spot * own_rows, own_rows, 0)

    start_own = own(start_h)
    middle = start_own + lax.psum_scatter(
        dot(mixed, o_w, 1, 1), "narrow", scatter_dimension=0, tiled=True
    )
    inner_own = norm_rows(middle, gain_w[1]).astype(LOW)
    inner = gather_rows(inner_own, "narrow")
    gate = dot(inner, ffn_w[0], 1, 1)
    up = dot(inner, ffn_w[1], 1, 1)
    hidden = (jax.nn.silu(gate) * up).astype(LOW)
    final_own = middle + lax.psum_scatter(
        dot(hidden, ffn_w[2], 1, 0), "narrow", scatter_dimension=0, tiled=True
    )
    final_own = jnp.where(keep_layer > 0, final_own, start_own)

    local_target = targets_all - (
        narrow_spot * vocab_rows + wide_spot * table_own.shape[0]
    )
    has_target = (
        local_target[:, None] == jnp.arange(table_own.shape[0], dtype=jnp.int32)[None, :]
    )
    counted = (targets_all >= 0).astype(FULL)
    loss_count = jnp.sum(counted)

    def exit_part(own_h, weight):
        features = gather_rows(norm_rows(own_h, gain_w[2]).astype(LOW), BOTH)
        logits = dot(features, table_own, 1, 1)
        peak = jnp.max(logits, axis=-1)
        total = jnp.sum(jnp.exp(logits - peak[:, None]), axis=-1)
        picked = jnp.sum(jnp.where(has_target, logits, 0.0), axis=-1)
        stats = lax.all_gather(jnp.stack([peak, total, picked]), BOTH)
        peak_all = jnp.max(stats[:, 0], axis=0)
        total_all = jnp.sum(stats[:, 1] * jnp.exp(stats[:, 0] - peak_all), axis=0)
        log_norm = peak_all + jnp.log(total_all)
        loss = weight * jnp.sum(counted * (log_norm - jnp.sum(stats[:, 2], axis=0)))
        grad_logits = (
            (jnp.exp(logits - log_norm[:, None]) - has_target.astype(FULL))
            * (weight * counted)[:, None]
        ).astype(LOW)
        grad_features = dot(grad_logits, table_own, 1, 0)
        grad_own = lax.psum_scatter(
            lax.psum_scatter(grad_features, "wide", scatter_dimension=0, tiled=True),
            "narrow",
            scatter_dimension=0,
            tiled=True,
        )
        return loss, grad_own, dot(grad_logits, features, 0, 0)

    loss_early, grad_early, head_early = exit_part(start_own, EXIT_EARLY)
    loss_late, grad_late, head_late = exit_part(final_own, EXIT_LAST)
    loss_sum = loss_early + loss_late
    grad_head = (head_early + head_late).astype(LOW)
    head_cols = exchange(cut_columns(grad_head, wide_count), "wide").reshape(vocab_rows, columns)

    grad_start_exit, gain_early = norm_back(start_own, gain_w[2], grad_early)
    grad_final, gain_late = norm_back(final_own, gain_w[2], grad_late)
    grad_layer = grad_final * keep_layer
    grad_out = gather_rows(grad_layer.astype(LOW), "narrow")
    grad_hidden = dot(grad_out, ffn_w[2], 1, 1)
    sigma = jax.nn.sigmoid(gate)
    grad_gate = (grad_hidden * up * sigma * (1.0 + gate * (1.0 - sigma))).astype(LOW)
    grad_up = (grad_hidden * gate * sigma).astype(LOW)
    grad_inner = lax.psum_scatter(
        dot(grad_gate, ffn_w[0], 1, 0) + dot(grad_up, ffn_w[1], 1, 0),
        "narrow",
        scatter_dimension=0,
        tiled=True,
    )
    extra_mid, gain_mid = norm_back(middle, gain_w[1], grad_inner)
    grad_mid = grad_layer + extra_mid
    grad_pass = grad_mid + grad_start_exit + grad_final * (1.0 - keep_layer)
    both_mid = lax.all_gather(
        jnp.stack([grad_mid.astype(LOW), grad_pass.astype(LOW)]), "narrow", axis=1, tiled=True
    )
    grad_branch, grad_extra = both_mid[0], both_mid[1]

    grad_mixed = dot(grad_branch, o_w, 1, 0).astype(LOW)
    grouped_grad = grad_mixed.reshape(sel, groups, heads_own // groups, HD)
    grad_probs = jnp.einsum("tkgd,ksd->kgts", grouped_grad, values, preferred_element_type=FULL)
    grad_scores = (
        probs * (grad_probs - jnp.sum(probs * grad_probs, axis=-1, keepdims=True))
    ).astype(LOW)
    grad_queries = (
        jnp.einsum("kgts,ksd->tkgd", grad_scores, keys, preferred_element_type=FULL) * scale
    ).reshape(sel, heads_own, HD)
    grad_queries = (
        unrotate(grad_queries, cosine[:, None], sine[:, None])
        .reshape(sel, heads_own * HD)
        .astype(LOW)
    )
    grad_keys = jnp.einsum("kgts,tkgd->ksd", grad_scores, grouped, preferred_element_type=FULL)
    grad_keys = unrotate(grad_keys * scale, cosine_all, sine_all).astype(LOW)
    grad_values = jnp.einsum(
        "kgts,tkgd->ksd", probs_low, grouped_grad, preferred_element_type=FULL
    ).astype(LOW)
    grad_kv_all = gather_rows(jnp.stack([grad_keys, grad_values], axis=1), "narrow")
    if repeat > 1:
        grad_kv_all = jnp.sum(
            grad_kv_all.reshape(KVH, repeat, 2, seq_len, HD).astype(FULL), axis=1
        ).astype(LOW)
    grad_kv_all = jnp.transpose(grad_kv_all, (1, 2, 0, 3)).reshape(2, seq_len, KVH * HD)
    grad_q_all = gather_columns(grad_queries, "narrow")

    pick_part = dot(grad_q_all, q_full, 1, 1)
    pick_high = pick_part.astype(LOW)
    pick_low = (pick_part - pick_high.astype(FULL)).astype(LOW)
    grad_normed = (
        dot(grad_kv_all[0], kv_w[0], 1, 1)
        + dot(grad_kv_all[1], kv_w[1], 1, 1)
        + dot(pick_hot, pick_high, 0, 0)
        + dot(pick_hot, pick_low, 0, 0)
    )
    grad_normed = jnp.where(inside_mine[:, None], grad_normed, 0.0)
    extra_start, gain_attn = norm_back(rows_full, gain_w[0], grad_normed)
    grad_start = jnp.where(
        inside_mine[:, None], extra_start + dot(pick_hot, grad_extra, 0, 0), 0.0
    ).astype(LOW)
    grad_rows = exchange(cut_columns(grad_start, wide_count), "wide").reshape(-1, columns)
    summed_table, table_squares = spread(spots, grad_rows, head_cols)

    grad_kv_w = jnp.stack(
        [dot(normed_all, grad_kv_all[0], 0, 0), dot(normed_all, grad_kv_all[1], 0, 0)], axis=1
    )
    grad_kv_w = lax.psum_scatter(grad_kv_w, "wide", scatter_dimension=0, tiled=True)
    summed_kv = lax.psum_scatter(
        jnp.moveaxis(grad_kv_w, 1, 0), "narrow", scatter_dimension=2, tiled=True
    )

    left_cols = exchange(
        jnp.moveaxis(
            jnp.stack([normed, grad_branch]).reshape(2, sel, wide_count, columns), 2, 0
        ),
        "wide",
    )
    left_cols = jnp.moveaxis(left_cols, 1, 0).reshape(2, wide_count * sel, columns)
    summed_qo = jnp.stack(
        [
            dot(left_cols[0], gather_rows(grad_queries, "wide"), 0, 0),
            dot(left_cols[1], gather_rows(mixed, "wide"), 0, 0),
        ]
    )

    inner_all = gather_rows(inner, "wide")
    out_all = gather_rows(grad_out, "wide")
    acts = jnp.stack([grad_gate, grad_up, hidden]).reshape(
        3, sel, wide_count, ffn_rows // narrow_count
    )
    acts = exchange(jnp.moveaxis(acts, 2, 0), "wide")
    acts = jnp.moveaxis(acts, 1, 0).reshape(3, wide_count * sel, ffn_rows // narrow_count)
    acts = lax.all_gather(acts, "narrow", axis=2, tiled=True)

    def cols_own(values_all):
        size = width // narrow_count
        return lax.dynamic_slice_in_dim(values_all, narrow_spot * size, size, 1)

    rights = (inner_all, inner_all, out_all)
    summed_ffn = jnp.stack([dot(acts[j], cols_own(rights[j]), 0, 0) for j in range(3)])
    small_all = lax.all_gather(
        pack_small(summed_qo, summed_kv).astype(LOW), "narrow", axis=0
    )

    gain_grads = jnp.stack([gain_attn, gain_mid, gain_early + gain_late])
    gain_sum = lax.psum(gain_grads, BOTH)
    gain_size = gains.shape[1]
    summed_gain = lax.dynamic_slice_in_dim(
        gain_sum, (wide_spot * narrow_count + narrow_spot) * gain_size, gain_size, 1
    )
    squares = (
        jnp.sum(summed_qo * summed_qo)
        + jnp.sum(summed_kv * summed_kv)
        + jnp.sum(summed_ffn * summed_ffn)
    )
    squares = squares + jnp.sum(summed_gain * summed_gain) + jnp.sum(table_squares)
    square_total = lax.psum(squares, BOTH)
    grad_norm = jnp.sqrt(square_total) / loss_count
    factor = jnp.minimum(1.0, CLIP_NORM / (grad_norm + 1e-06)) / loss_count

    def whole_columns(parts):
        return jnp.moveaxis(parts, 0, 2).reshape(
            parts.shape[1], parts.shape[2], parts.shape[0] * parts.shape[3]
        )

    def ffn_owner():
        left = lax.dynamic_index_in_dim(acts, jnp.minimum(narrow_spot, 2), 0, False)
        right = jnp.where(narrow_spot == 2, out_all, inner_all)
        grad = dot(left, right, 0, 0)
        mom = side_by_side(mom_owned.reshape((narrow_count,) + mom_ffn.shape[1:]))
        result = orthogonalize((MOMENTUM * mom + grad * factor)[None])[0]
        return cut_columns(result.astype(LOW), narrow_count).reshape(narrow_count, slot)

    def small_owner():
        mom_q, mom_k = unpack_small(mom_owned)
        grad_q, grad_k = unpack_small(small_all.astype(FULL))
        results = [
            orthogonalize(whole_columns(MOMENTUM * mom + grad * factor)).astype(LOW)
            for mom, grad in ((mom_q, grad_q), (mom_k, grad_k))
        ]
        parts = [
            jnp.moveaxis(
                result.reshape(2, result.shape[1], narrow_count, -1), 2, 0
            ).reshape(narrow_count, -1)
            for result in results
        ]
        flat = jnp.concatenate(parts, axis=1)
        return jnp.pad(flat, ((0, 0), (0, slot - flat.shape[1])))

    directions = lax.cond(narrow_spot == 3, small_owner, ffn_owner)
    directions = exchange(directions, "narrow")
    dir_ffn = directions[:3].reshape(mom_ffn.shape).astype(FULL)
    dir_qo, dir_kv = unpack_small(directions[3].astype(FULL))

    embed_new, embed_m_new, embed_v_new = adamw(
        embed, embed_m, embed_v, summed_table * factor, RATE_ADAM, WEIGHT_DECAY
    )
    gains_new, gains_m_new, gains_v_new = adamw(
        gains, gains_m, gains_v, summed_gain * factor, RATE_GAIN, 0.0
    )

    def mom_next(mom, grad):
        return MOMENTUM * mom + jnp.moveaxis(grad * factor, 0, 1)

    shrink = 1.0 - RATE_MUON * WEIGHT_DECAY

    def weight_next(weight, direction):
        return weight * shrink - RATE_MUON * jnp.moveaxis(direction, 0, 1)

    return (
        loss_sum,
        loss_count,
        grad_norm,
        embed_new,
        embed_m_new,
        embed_v_new,
        weight_next(attn_qo, dir_qo),
        mom_next(attn_qo_mom, summed_qo),
        weight_next(attn_kv, dir_kv),
        mom_next(attn_kv_mom, summed_kv),
        weight_next(ffn, dir_ffn),
        mom_next(ffn_mom, summed_ffn),
        gains_new,
        gains_m_new,
        gains_v_new,
    )


def solution(mesh):
    by_pack = P("wide", None)
    table = P("narrow", "wide")
    layer = P("wide", None, "narrow")
    gain = P(None, ("wide", "narrow"))
    return jax.shard_map(
        per_device,
        mesh=mesh,
        in_specs=(by_pack,) * 4 + (P("wide"),) + (table,) * 3 + (layer,) * 6 + (gain,) * 3,
        out_specs=(P(),) * 3 + (table,) * 3 + (layer,) * 6 + (gain,) * 3,
        check_vma=False,
    )
```

```python
import functools

import jax
import jax.numpy as jnp
from jax import lax
from jax.experimental import pallas as pl
from jax.experimental.pallas import tpu as pltpu
from jax.sharding import PartitionSpec as P

HEADS = 16
HD = 128
KVH = 4
NS_STEPS = 5
STEP = 10


NORM_EPS = 1e-05
ROPE_BASE = 10000.0
EXIT_EARLY = 0.25
EXIT_LAST = 1.0
CLIP_NORM = 0.02
BETA_ONE = 0.9
BETA_TWO = 0.95
ADAM_EPS = 1e-08
RATE_ADAM = 0.02
RATE_GAIN = 0.3
RATE_MUON = 0.3
WEIGHT_DECAY = 0.1
MOMENTUM = 0.95
NEWTON_A = 3.4445
NEWTON_B = -4.775
NEWTON_C = 2.0315
MASKED = -1e30
LOW = jnp.bfloat16
FULL = jnp.float32
BOTH = ("wide", "narrow")
ROWS_IN_BLOCK = 1024
UNROLL = 16
VMEM_BYTES = 56 * 1024 * 1024


def dot(first, second, first_dim, second_dim):
    return lax.dot_general(
        first, second, (((first_dim,), (second_dim,)), ((), ())), preferred_element_type=FULL
    )


def norm_rows(values, gain_row):
    return (
        values * lax.rsqrt(jnp.mean(values * values, axis=-1, keepdims=True) + NORM_EPS) * gain_row
    )


def norm_back(values, gain_row, grad):
    output, pull = jax.vjp(norm_rows, values, gain_row)
    return pull(grad)


def segments_at(lens, where_at):
    ends = jnp.cumsum(lens)
    return jnp.sum((where_at[:, None] >= ends[None, :]).astype(jnp.int32), axis=1)


def angles_at(lens, where_at):
    segment = segments_at(lens, where_at)
    starts = jnp.cumsum(lens) - lens
    member = segment[:, None] == jnp.arange(lens.shape[0], dtype=jnp.int32)[None, :]
    begin = jnp.sum(jnp.where(member, starts[None, :], 0), axis=1)
    offset_pos = (where_at - begin).astype(FULL)
    inverse = ROPE_BASE ** (-2.0 * jnp.arange(HD // 2, dtype=FULL) / HD)
    angle = offset_pos[:, None] * inverse[None, :]
    return (segment, jnp.cos(angle), jnp.sin(angle))


def rotate(values, cosine, sine):
    half = values.shape[-1] // 2
    first, second = (values[..., :half], values[..., half:])
    return jnp.concatenate(
        [first * cosine - second * sine, second * cosine + first * sine], axis=-1
    )


def unrotate(values, cosine, sine):
    return rotate(values, cosine, -sine)


MESH = pl.DeviceIdType.MESH
ANY = pl.BlockSpec(memory_space=pl.ANY)
VMEM = pl.BlockSpec(memory_space=pltpu.VMEM)


def greet(targets):
    barrier = pltpu.get_barrier_semaphore()
    for target in targets:
        pl.semaphore_signal(barrier, inc=1, device_id=target, device_id_type=MESH)
    pl.semaphore_wait(barrier, len(targets))


def others(axis, count):
    me = lax.axis_index(axis)
    return [{axis: lax.rem(me + step, count)} for step in range(1, count)]


def push(source, target, send, receive, device):
    return pltpu.make_async_remote_copy(
        src_ref=source,
        dst_ref=target,
        send_sem=send,
        recv_sem=receive,
        device_id=device,
        device_id_type=MESH,
    )


def call_kernel(body, ident, inputs, outputs, scratch, name, in_place=None, out_place=None):
    in_specs = [VMEM if in_place is None else in_place[i] for i in range(len(inputs))]
    out_specs = [VMEM if out_place is None else out_place[i] for i in range(len(outputs))]
    size = sum(a.size * a.dtype.itemsize for a in list(inputs) + list(outputs))
    return pl.pallas_call(
        body,
        out_shape=outputs,
        in_specs=in_specs,
        out_specs=out_specs,
        scratch_shapes=scratch,
        compiler_params=pltpu.CompilerParams(
            collective_id=ident, has_side_effects=True, vmem_limit_bytes=VMEM_BYTES
        ),
        cost_estimate=pl.CostEstimate(flops=0, bytes_accessed=8 * size, transcendentals=0),
        name=name,
    )(*inputs)


def gather_wide_body(count, x_ref, out_ref, send, receive, local):
    me = lax.axis_index("wide")
    mate = me + 1 - 2 * lax.rem(me, 2)
    chips = count // 2
    peers = [lax.rem(me + 2 * step, count) for step in range(1, chips)]
    greet([{"wide": mate}] + [{"wide": peer} for peer in peers])
    keep = pltpu.make_async_copy(x_ref, out_ref.at[me], local)
    keep.start()
    first = []
    for step, peer in enumerate(peers + [mate]):
        copy = push(x_ref, out_ref.at[me], send.at[step], receive.at[me], {"wide": peer})
        copy.start()
        first.append(copy)
    second = []
    for step in range(1, chips):
        source = lax.rem(me - 2 * step + count, count)
        block = out_ref.at[source]
        push(block, block, send.at[0], receive.at[source], {"wide": mate}).wait_recv()
        copy = push(block, block, send.at[chips + step - 1], receive.at[source], {"wide": mate})
        copy.start()
        second.append(copy)
    for step in range(chips):
        source = lax.rem(mate - 2 * step + count, count)
        block = out_ref.at[source]
        push(block, block, send.at[0], receive.at[source], {"wide": mate}).wait_recv()
    for copy in first + second:
        copy.wait_send()
    keep.wait()


def gather_wide(values, ident, name):
    count = lax.axis_size("wide")
    return call_kernel(
        functools.partial(gather_wide_body, count),
        ident,
        [values],
        [jax.ShapeDtypeStruct((count,) + values.shape, values.dtype)],
        [
            pltpu.SemaphoreType.DMA((count - 1,)),
            pltpu.SemaphoreType.DMA((count,)),
            pltpu.SemaphoreType.DMA,
        ],
        name,
        [ANY],
        [ANY],
    )[0]


def trade_body(count, splits, *refs):
    inputs = refs[: len(splits)]
    outputs = refs[len(splits) : 2 * len(splits)]
    send, receive, local = refs[2 * len(splits) :]
    me = lax.axis_index("narrow")
    greet(others("narrow", count))
    copies = []
    for at, split in enumerate(splits):
        for step in range(1, count):
            peer = lax.rem(me + step, count)
            source = inputs[at].at[peer] if split else inputs[at]
            copy = push(
                source,
                outputs[at].at[me],
                send.at[at, step - 1],
                receive.at[at, me],
                {"narrow": peer},
            )
            copy.start()
            copies.append(copy)
    keeps = []
    for at, split in enumerate(splits):
        keep = pltpu.make_async_copy(
            inputs[at].at[me] if split else inputs[at], outputs[at].at[me], local.at[at]
        )
        keep.start()
        keeps.append(keep)
    for at in range(len(splits)):
        for step in range(1, count):
            source = lax.rem(me - step + count, count)
            block = outputs[at].at[source]
            push(
                block, block, send.at[at, 0], receive.at[at, source], {"narrow": source}
            ).wait_recv()
    for copy in copies:
        copy.wait_send()
    for keep in keeps:
        keep.wait()


def trade(values, splits, ident, name):
    count = lax.axis_size("narrow")
    shapes = [a.shape if split else (count,) + a.shape for a, split in zip(values, splits)]
    return call_kernel(
        functools.partial(trade_body, count, splits),
        ident,
        values,
        [jax.ShapeDtypeStruct(shape, a.dtype) for shape, a in zip(shapes, values)],
        [
            pltpu.SemaphoreType.DMA((len(values), count - 1)),
            pltpu.SemaphoreType.DMA((len(values), count)),
            pltpu.SemaphoreType.DMA((len(values),)),
        ],
        name,
        [ANY] * len(values),
        [ANY] * len(values),
    )


def collect(count, parts_ref, slots, send, receive):
    me = lax.axis_index("narrow")
    copies = []
    for step in range(1, count):
        peer = lax.rem(me + step, count)
        copy = push(
            parts_ref.at[peer],
            slots.at[me],
            send.at[step - 1],
            receive.at[me],
            {"narrow": peer},
        )
        copy.start()
        copies.append(copy)
    total = parts_ref[me]
    for step in range(1, count):
        source = lax.rem(me - step + count, count)
        block = slots.at[source]
        push(block, block, send.at[0], receive.at[source], {"narrow": source}).wait_recv()
        total = total + slots[source]
    return total, copies


def share(count, low, all_ref, send, receive):
    me = lax.axis_index("narrow")
    all_ref[me] = low
    copies = []
    for step in range(1, count):
        peer = lax.rem(me + step, count)
        copy = push(
            all_ref.at[me], all_ref.at[me], send.at[step - 1], receive.at[me], {"narrow": peer}
        )
        copy.start()
        copies.append(copy)
    for step in range(1, count):
        source = lax.rem(me - step + count, count)
        block = all_ref.at[source]
        push(block, block, send.at[0], receive.at[source], {"narrow": source}).wait_recv()
    return copies


def settle_body(
    count, parts_ref, base_ref, other_ref, keep_ref, gain_ref, own_ref, all_ref, slots, *sems
):
    send, receive, send_all, receive_all = sems
    greet(others("narrow", count))
    total, copies = collect(count, parts_ref, slots, send, receive)
    total = jnp.where(keep_ref[...] > 0, total + base_ref[...], other_ref[...])
    own_ref[...] = total
    low = norm_rows(total, gain_ref[...]).astype(LOW)
    copies = copies + share(count, low, all_ref, send_all, receive_all)
    for copy in copies:
        copy.wait_send()


def narrow_sems(count):
    return [
        pltpu.SemaphoreType.DMA((count - 1,)),
        pltpu.SemaphoreType.DMA((count,)),
    ]


def settle(partial, base, other, keep_row, gain_row, ident, name):
    count = lax.axis_size("narrow")
    rows, width = base.shape
    own, shared = call_kernel(
        functools.partial(settle_body, count),
        ident,
        [partial.reshape(count, rows, width), base, other, keep_row, gain_row],
        [
            jax.ShapeDtypeStruct((rows, width), FULL),
            jax.ShapeDtypeStruct((count, rows, width), LOW),
        ],
        [pltpu.VMEM((count, rows, width), FULL)] + narrow_sems(count) + narrow_sems(count),
        name,
    )
    return own, shared.reshape(count * rows, width)


def settle_back_body(
    count,
    parts_ref,
    values_ref,
    add_ref,
    keep_ref,
    gain_ref,
    own_ref,
    gain_grad_ref,
    all_ref,
    slots,
    *sems
):
    send, receive, send_all, receive_all = sems
    greet(others("narrow", count))
    grad, copies = collect(count, parts_ref, slots, send, receive)
    values = values_ref[...]
    root = lax.rsqrt(jnp.mean(values * values, axis=-1, keepdims=True) + NORM_EPS)
    scaled = gain_ref[...] * grad
    inner = jnp.mean(values * scaled, axis=-1, keepdims=True)
    own = add_ref[...] + root * scaled - values * (root * root * root * inner)
    gain_grad_ref[...] = jnp.sum(values * root * grad, axis=0, keepdims=True)
    own_ref[...] = own
    low = (own * keep_ref[...]).astype(LOW)
    copies = copies + share(count, low, all_ref, send_all, receive_all)
    for copy in copies:
        copy.wait_send()


def settle_back(partial, values, add, keep_row, gain_row, ident, name):
    count = lax.axis_size("narrow")
    rows, width = values.shape
    own, gain_grad, shared = call_kernel(
        functools.partial(settle_back_body, count),
        ident,
        [partial.reshape(count, rows, width), values, add, keep_row, gain_row],
        [
            jax.ShapeDtypeStruct((rows, width), FULL),
            jax.ShapeDtypeStruct((1, width), FULL),
            jax.ShapeDtypeStruct((count, rows, width), LOW),
        ],
        [pltpu.VMEM((count, rows, width), FULL)] + narrow_sems(count) + narrow_sems(count),
        name,
    )
    return own, gain_grad[0], shared.reshape(count * rows, width)


def fetch_rows_body(deep, wide, found_ref, out_ref, rightward, leftward, final, *sems):
    send_right, receive_right, send_left, receive_left, send_wide, receive_wide, local = sems
    spot = lax.axis_index("narrow")
    me = lax.axis_index("wide")
    columns = found_ref.shape[2]
    rows = out_ref.shape[0]
    greet(others("narrow", deep) + others("wide", wide))

    def right_copy(part, source):
        return push(
            source,
            rightward.at[part],
            send_right.at[part],
            receive_right.at[part],
            {"narrow": lax.rem(spot + 1, deep)},
        )

    def left_copy(part, source):
        return push(
            source,
            leftward.at[part],
            send_left.at[part],
            receive_left.at[part],
            {"narrow": lax.rem(spot + deep - 1, deep)},
        )

    for step in range(deep - 1):
        right, left = deep - 1 - step, step

        @pl.when((spot == 0) & (right > 0))
        def _():
            right_copy(right, found_ref.at[right]).start()

        @pl.when((spot == deep - 1) & (left < deep - 1))
        def _():
            left_copy(left, found_ref.at[left]).start()

        @pl.when((spot > 0) & (right > spot))
        def _():
            right_copy(right, rightward.at[right]).wait_recv()
            rightward[right] = rightward[right] + found_ref[right]
            right_copy(right, rightward.at[right]).start()

        @pl.when((spot < deep - 1) & (left < spot))
        def _():
            left_copy(left, leftward.at[left]).wait_recv()
            leftward[left] = leftward[left] + found_ref[left]
            left_copy(left, leftward.at[left]).start()

    final[...] = found_ref[spot]

    @pl.when(spot > 0)
    def _():
        right_copy(spot, rightward.at[spot]).wait_recv()
        final[...] = final[...] + rightward[spot]

    @pl.when(spot < deep - 1)
    def _():
        left_copy(spot, leftward.at[spot]).wait_recv()
        final[...] = final[...] + leftward[spot]

    mine = pl.ds(pl.multiple_of(me * columns, columns), columns)
    copies = []
    for step in range(1, wide):
        peer = lax.rem(me + step, wide)
        copy = push(
            final.at[pl.ds(pl.multiple_of(peer * rows, rows), rows)],
            out_ref.at[:, mine],
            send_wide.at[step - 1],
            receive_wide.at[me],
            {"wide": peer},
        )
        copy.start()
        copies.append(copy)
    keep = pltpu.make_async_copy(
        final.at[pl.ds(pl.multiple_of(me * rows, rows), rows)], out_ref.at[:, mine], local
    )
    keep.start()
    for step in range(1, wide):
        source = lax.rem(me - step + wide, wide)
        block = out_ref.at[:, pl.ds(pl.multiple_of(source * columns, columns), columns)]
        push(block, block, send_wide.at[0], receive_wide.at[source], {"wide": source}).wait_recv()
    for copy in copies:
        copy.wait_send()
    keep.wait()
    for step in range(deep - 1):
        right, left = deep - 1 - step, step

        @pl.when(right > spot)
        def _():
            right_copy(right, found_ref.at[right]).wait_send()

        @pl.when(left < spot)
        def _():
            left_copy(left, found_ref.at[left]).wait_send()


def fetch_rows(found, rows, ident, name):
    deep, wide = lax.axis_size("narrow"), lax.axis_size("wide")
    columns = found.shape[2]
    return call_kernel(
        functools.partial(fetch_rows_body, deep, wide),
        ident,
        [found],
        [jax.ShapeDtypeStruct((rows, wide * columns), found.dtype)],
        [pltpu.VMEM(found.shape, found.dtype)] * 2
        + [pltpu.VMEM(found.shape[1:], found.dtype)]
        + [pltpu.SemaphoreType.DMA((deep,))] * 4
        + [
            pltpu.SemaphoreType.DMA((wide - 1,)),
            pltpu.SemaphoreType.DMA((wide,)),
            pltpu.SemaphoreType.DMA,
        ],
        name,
        None,
        [ANY],
    )[0]


def return_rows_body(deep, wide, rows_ref, out_ref, *sems):
    send_right, send_left, receive_deep, send_wide, receive_wide, local = sems
    spot = lax.axis_index("narrow")
    me = lax.axis_index("wide")
    columns = out_ref.shape[2]
    rows = rows_ref.shape[0]
    greet(others("narrow", deep) + others("wide", wide))
    mine = out_ref.at[spot, pl.ds(pl.multiple_of(me * rows, rows), rows)]

    def part_of(device):
        return rows_ref.at[:, pl.ds(pl.multiple_of(device * columns, columns), columns)]

    copies = []
    for step in range(1, wide):
        peer = lax.rem(me + step, wide)
        copy = push(
            part_of(peer), mine, send_wide.at[step - 1], receive_wide.at[me], {"wide": peer}
        )
        copy.start()
        copies.append(copy)
    keep = pltpu.make_async_copy(part_of(me), mine, local)
    keep.start()
    for step in range(1, wide):
        source = lax.rem(me - step + wide, wide)
        block = out_ref.at[spot, pl.ds(pl.multiple_of(source * rows, rows), rows)]
        push(block, block, send_wide.at[0], receive_wide.at[source], {"wide": source}).wait_recv()
    keep.wait()

    def right_copy(part):
        return push(
            out_ref.at[part],
            out_ref.at[part],
            send_right.at[part],
            receive_deep.at[part],
            {"narrow": lax.rem(spot + 1, deep)},
        )

    def left_copy(part):
        return push(
            out_ref.at[part],
            out_ref.at[part],
            send_left.at[part],
            receive_deep.at[part],
            {"narrow": lax.rem(spot + deep - 1, deep)},
        )

    @pl.when(spot < deep - 1)
    def _():
        right_copy(spot).start()

    @pl.when(spot > 0)
    def _():
        left_copy(spot).start()

    for step in range(1, deep):

        @pl.when(spot >= step)
        def _():
            right_copy(spot - step).wait_recv()

            @pl.when(spot < deep - 1)
            def _():
                right_copy(spot - step).start()

        @pl.when(spot + step < deep)
        def _():
            left_copy(spot + step).wait_recv()

            @pl.when(spot > 0)
            def _():
                left_copy(spot + step).start()

    for part in range(deep):

        @pl.when((part <= spot) & (spot < deep - 1))
        def _():
            right_copy(part).wait_send()

        @pl.when((part >= spot) & (spot > 0))
        def _():
            left_copy(part).wait_send()

    for copy in copies:
        copy.wait_send()


def return_rows(rows, ident, name):
    deep, wide = lax.axis_size("narrow"), lax.axis_size("wide")
    count, width = rows.shape
    return call_kernel(
        functools.partial(return_rows_body, deep, wide),
        ident,
        [rows],
        [jax.ShapeDtypeStruct((deep, wide * count, width // wide), rows.dtype)],
        [pltpu.SemaphoreType.DMA((deep,))] * 3
        + [
            pltpu.SemaphoreType.DMA((wide - 1,)),
            pltpu.SemaphoreType.DMA((wide,)),
            pltpu.SemaphoreType.DMA,
        ],
        name,
        [ANY],
        [ANY],
    )[0]


def sum_wide_body(count, parts_ref, out_ref, from_mate, paired, slots, *sems):
    send_mate, receive_mate, send, receive = sems
    me = lax.axis_index("wide")
    side = lax.rem(me, 2)
    mate = me + 1 - 2 * side
    chips = count // 2
    my_chip = me // 2
    greet([{"wide": mate}] + [{"wide": lax.rem(me + 2 * s, count)} for s in range(1, chips)])
    mate_copies = []
    for step in range(chips):
        chip = lax.rem(my_chip + 1 + step, chips)
        copy = push(
            parts_ref.at[2 * chip + 1 - side],
            from_mate.at[chip],
            send_mate.at[step],
            receive_mate.at[chip],
            {"wide": mate},
        )
        copy.start()
        mate_copies.append(copy)
    copies = []
    for step in range(chips):
        chip = lax.rem(my_chip + 1 + step, chips)
        block = from_mate.at[chip]
        push(block, block, send_mate.at[0], receive_mate.at[chip], {"wide": mate}).wait_recv()
        both = parts_ref[2 * chip + side].astype(FULL) + from_mate[chip].astype(FULL)
        if step < chips - 1:
            paired[chip] = both.astype(LOW)
            copy = push(
                paired.at[chip],
                slots.at[my_chip],
                send.at[step],
                receive.at[my_chip],
                {"wide": 2 * chip + side},
            )
            copy.start()
            copies.append(copy)
        else:
            out_ref[...] = both
    for step in range(1, chips):
        chip = lax.rem(my_chip - step + chips, chips)
        block = slots.at[chip]
        push(block, block, send.at[0], receive.at[chip], {"wide": 2 * chip + side}).wait_recv()
        out_ref[...] = out_ref[...] + slots[chip].astype(FULL)
    for copy in mate_copies + copies:
        copy.wait_send()


def sum_wide(partial, ident, name):
    count = lax.axis_size("wide")
    chips = count // 2
    rows, width = partial.shape[0] // count, partial.shape[1]
    return call_kernel(
        functools.partial(sum_wide_body, count),
        ident,
        [partial.reshape(count, rows, width)],
        [jax.ShapeDtypeStruct((rows, width), FULL)],
        [pltpu.VMEM((chips, rows, width), LOW)] * 3
        + [
            pltpu.SemaphoreType.DMA((chips,)),
            pltpu.SemaphoreType.DMA((chips,)),
            pltpu.SemaphoreType.DMA((max(chips - 1, 1),)),
            pltpu.SemaphoreType.DMA((chips,)),
        ],
        name,
    )[0]


def merge_two(first, second):
    peak = jnp.maximum(first[0:1], second[0:1])
    total = first[1:2] * jnp.exp(first[0:1] - peak) + second[1:2] * jnp.exp(second[0:1] - peak)
    return jnp.concatenate([peak, total, first[2:] + second[2:]], axis=0)


def add_two(first, second):
    return first + second


def combine_body(deep, wide, join, x_ref, out_ref, wide_slots, deep_slots, *sems):
    send_wide, receive_wide, send_deep, receive_deep = sems
    me = lax.axis_index("wide")
    spot = lax.axis_index("narrow")
    greet(others("narrow", deep) + others("wide", wide))

    def round_of(axis, at, count, slots, send, receive):
        copies = []
        for step in range(1, count):
            peer = lax.rem(at + step, count)
            copy = push(
                slots.at[at], slots.at[at], send.at[step - 1], receive.at[at], {axis: peer}
            )
            copy.start()
            copies.append(copy)
        for step in range(1, count):
            source = lax.rem(at - step + count, count)
            block = slots.at[source]
            push(block, block, send.at[0], receive.at[source], {axis: source}).wait_recv()
        total = slots[0]
        for source in range(1, count):
            total = join(total, slots[source])
        return total, copies

    wide_slots[me] = x_ref[...]
    total, first = round_of("wide", me, wide, wide_slots, send_wide, receive_wide)
    deep_slots[spot] = total
    total, second = round_of("narrow", spot, deep, deep_slots, send_deep, receive_deep)
    out_ref[...] = total
    for copy in first + second:
        copy.wait_send()


def combine(values, join, ident, name):
    deep, wide = lax.axis_size("narrow"), lax.axis_size("wide")
    return call_kernel(
        functools.partial(combine_body, deep, wide, join),
        ident,
        [values],
        [jax.ShapeDtypeStruct(values.shape, values.dtype)],
        [
            pltpu.VMEM((wide,) + values.shape, values.dtype),
            pltpu.VMEM((deep,) + values.shape, values.dtype),
            pltpu.SemaphoreType.DMA((wide - 1,)),
            pltpu.SemaphoreType.DMA((wide,)),
            pltpu.SemaphoreType.DMA((deep - 1,)),
            pltpu.SemaphoreType.DMA((deep,)),
        ],
        name,
    )[0]


def lookup_body(ids_ref, table_ref, out_ref, held, rows, sem):
    block = pl.program_id(0)
    vocab = table_ref.shape[0]

    @pl.when(block == 0)
    def _():
        load = pltpu.make_async_copy(table_ref, held.at[pl.ds(0, vocab)], sem)
        load.start()
        held[pl.ds(vocab, 8), :] = jnp.zeros((8, held.shape[1]), FULL)
        load.wait()

    def step(group, carry):
        for member in range(UNROLL):
            at = group * UNROLL + member
            spot = ids_ref[block * ROWS_IN_BLOCK + at]
            rows[pl.ds(at, 1), :] = held[pl.ds(spot, 1), :]
        return carry

    lax.fori_loop(0, ROWS_IN_BLOCK // UNROLL, step, 0)
    out_ref[...] = rows[...].astype(LOW)


def lookup(table, ids):
    vocab, columns = table.shape
    count = ids.shape[0]
    return pl.pallas_call(
        lookup_body,
        grid_spec=pltpu.PrefetchScalarGridSpec(
            num_scalar_prefetch=1,
            grid=(count // ROWS_IN_BLOCK,),
            in_specs=[pl.BlockSpec(memory_space=pl.ANY)],
            out_specs=pl.BlockSpec((ROWS_IN_BLOCK, columns), lambda block, ids_ref: (block, 0)),
            scratch_shapes=[
                pltpu.VMEM((vocab + 8, columns), FULL),
                pltpu.VMEM((ROWS_IN_BLOCK, columns), FULL),
                pltpu.SemaphoreType.DMA,
            ],
        ),
        out_shape=jax.ShapeDtypeStruct((count, columns), LOW),
        compiler_params=pltpu.CompilerParams(vmem_limit_bytes=VMEM_BYTES),
        cost_estimate=pl.CostEstimate(
            flops=0, bytes_accessed=vocab * columns * 4 + count * columns * 32, transcendentals=0
        ),
        name="lookup",
    )(ids, table)


def spread_body(ids_ref, rows_ref, head_ref, out_ref, square_ref, even, odd, rows, sem):
    block = pl.program_id(0)
    vocab = out_ref.shape[0]

    @pl.when(block == 0)
    def _():
        even[...] = jnp.zeros_like(even)
        odd[...] = jnp.zeros_like(odd)

    rows[...] = rows_ref[...].astype(FULL)

    def step(group, carry):
        for member in range(UNROLL):
            at = group * UNROLL + member
            spot = pl.ds(ids_ref[block * ROWS_IN_BLOCK + at], 1)
            total = even if member % 2 == 0 else odd
            total[spot, :] = total[spot, :] + rows[pl.ds(at, 1), :]
        return carry

    lax.fori_loop(0, ROWS_IN_BLOCK // UNROLL, step, 0)

    @pl.when(block == pl.num_programs(0) - 1)
    def _():
        chunk = 256

        def finish(part, squares):
            spot = pl.ds(pl.multiple_of(part * chunk, chunk), chunk)
            value = even[spot, :] + odd[spot, :] + head_ref[spot, :].astype(FULL)
            even[spot, :] = value
            return squares + jnp.sum((value * value).reshape(chunk // 8, 8, -1), axis=0)

        squares = lax.fori_loop(
            0, vocab // chunk, finish, jnp.zeros((8, even.shape[1]), FULL)
        )
        square_ref[...] = squares
        store = pltpu.make_async_copy(even.at[pl.ds(0, vocab)], out_ref, sem)
        store.start()
        store.wait()


def spread(ids, rows, head):
    vocab, columns = head.shape
    count = ids.shape[0]
    return pl.pallas_call(
        spread_body,
        grid_spec=pltpu.PrefetchScalarGridSpec(
            num_scalar_prefetch=1,
            grid=(count // ROWS_IN_BLOCK,),
            in_specs=[
                pl.BlockSpec((ROWS_IN_BLOCK, columns), lambda block, ids_ref: (block, 0)),
                pl.BlockSpec((vocab, columns), lambda block, ids_ref: (0, 0)),
            ],
            out_specs=[
                pl.BlockSpec(memory_space=pl.ANY),
                pl.BlockSpec((8, columns), lambda block, ids_ref: (0, 0)),
            ],
            scratch_shapes=[
                pltpu.VMEM((vocab + 8, columns), FULL),
                pltpu.VMEM((vocab + 8, columns), FULL),
                pltpu.VMEM((ROWS_IN_BLOCK, columns), FULL),
                pltpu.SemaphoreType.DMA,
            ],
        ),
        out_shape=[
            jax.ShapeDtypeStruct((vocab, columns), FULL),
            jax.ShapeDtypeStruct((8, columns), FULL),
        ],
        compiler_params=pltpu.CompilerParams(vmem_limit_bytes=VMEM_BYTES),
        cost_estimate=pl.CostEstimate(
            flops=count * columns, bytes_accessed=count * columns * 64, transcendentals=0
        ),
        name="spread",
    )(ids, rows, head)


def orthogonalize(blocks):
    norm = jnp.sqrt(jnp.sum(blocks * blocks, axis=(1, 2), keepdims=True)) + 1e-07
    current = blocks / norm
    rows = blocks.shape[1]
    eye = jnp.eye(rows, dtype=FULL)[None]

    def centre(gram):
        middle = jnp.sum(gram * eye, axis=(1, 2), keepdims=True) / rows
        return (middle, gram - middle * eye)

    for iteration in range(NS_STEPS):
        low = current.astype(LOW)
        gram = jnp.einsum("jrc,jsc->jrs", low, low, preferred_element_type=FULL)
        middle, rest = centre(gram)
        rest_low = rest.astype(LOW)
        square = jnp.einsum("jrs,jst->jrt", rest_low, rest_low, preferred_element_type=FULL)
        square = square + 2.0 * middle * rest + middle * middle * eye
        middle, rest = centre(NEWTON_B * gram + NEWTON_C * square)
        current = (NEWTON_A + middle) * current + jnp.einsum(
            "jrs,jsc->jrc", rest.astype(LOW), low, preferred_element_type=FULL
        )
    return current


def adamw(weight, first_m, second_m, grad, rate, decay):
    first_new = BETA_ONE * first_m + (1.0 - BETA_ONE) * grad
    second_new = BETA_TWO * second_m + (1.0 - BETA_TWO) * grad * grad
    update = (
        first_new
        / (1.0 - BETA_ONE**STEP)
        / (jnp.sqrt(second_new / (1.0 - BETA_TWO**STEP)) + ADAM_EPS)
    )
    return (weight * (1.0 - rate * decay) - rate * update, first_new, second_new)


def exchange(parts, axis):
    return lax.all_to_all(parts, axis, 0, 0, tiled=True)


def side_by_side(parts):
    count, rows, columns = parts.shape
    return jnp.moveaxis(parts, 0, 1).reshape(rows, count * columns)


def cut_columns(values, count):
    rows, columns = values.shape
    return jnp.moveaxis(values.reshape(rows, count, columns // count), 1, 0)


def gather_rows(values, axis):
    return lax.all_gather(values, axis, axis=0, tiled=True)


def gather_columns(values, axis):
    return lax.all_gather(values, axis, axis=1, tiled=True)


def per_device(
    tokens,
    picks,
    targets,
    lengths,
    skip,
    embed,
    embed_m,
    embed_v,
    attn_qo,
    attn_qo_mom,
    attn_kv,
    attn_kv_mom,
    ffn,
    ffn_mom,
    gains,
    gains_m,
    gains_v,
):
    wide_count = lax.axis_size("wide")
    narrow_count = lax.axis_size("narrow")
    narrow_spot = lax.axis_index("narrow")
    wide_spot = lax.axis_index("wide")
    seq_len = tokens.shape[1]
    sel = picks.shape[1]
    vocab_rows, columns = embed.shape
    width = columns * wide_count
    own_rows = sel // narrow_count
    tok_rows = seq_len // narrow_count
    all_rows = own_rows + tok_rows
    heads_own = HEADS // narrow_count
    repeat = max(1, narrow_count // KVH)
    groups = KVH * repeat // narrow_count
    ffn_rows = ffn.shape[0]
    lens = lengths[0]
    pick_ids = picks[0]
    keep_layer = (1 - skip[0]).astype(FULL)
    keep_row = jnp.full((1, width), keep_layer)
    always_row = jnp.ones((1, width), FULL)

    where_at = jnp.arange(seq_len, dtype=jnp.int32)
    pick_tokens = jnp.sum(
        jnp.where(pick_ids[:, None] == where_at[None, :], tokens[0][None, :], 0), axis=1
    )
    ints = jnp.concatenate([tokens[0], pick_tokens, targets[0]])
    lanes = 128
    height = -(-ints.shape[0] // (8 * lanes)) * 8
    ints_box = jnp.pad(ints, (0, height * lanes - ints.shape[0])).reshape(height, lanes)
    all_ints = gather_wide(ints_box, 0, "gather_ids").reshape(wide_count, -1)
    tokens_all = all_ints[:, :seq_len].reshape(wide_count, narrow_count, tok_rows)
    picked_all = all_ints[:, seq_len : seq_len + sel].reshape(wide_count, narrow_count, own_rows)
    targets_all = all_ints[:, seq_len + sel : seq_len + 2 * sel].reshape(-1)
    wanted = jnp.moveaxis(jnp.concatenate([tokens_all, picked_all], axis=2), 1, 0).reshape(-1)

    local_ids = wanted - narrow_spot * vocab_rows
    inside = (local_ids >= 0) & (local_ids < vocab_rows)
    spots = jnp.where(inside, local_ids, vocab_rows)
    found = lookup(embed, spots)
    rows_low = fetch_rows(
        found.reshape(narrow_count, wide_count * all_rows, columns), all_rows, 1, "fetch_rows"
    )

    gain_w = gather_columns(gains.astype(LOW), BOTH).astype(FULL)
    kv_low = jnp.moveaxis(attn_kv, 1, 0).astype(LOW)
    kv_w = lax.all_gather(
        lax.all_gather(kv_low, "narrow", axis=2, tiled=True), "wide", axis=1, tiled=True
    )
    qo_low = jnp.moveaxis(attn_qo, 1, 0).astype(LOW)
    qo_w = lax.all_gather(qo_low, "wide", axis=1, tiled=True)
    q_w, o_w = qo_w[0], qo_w[1]
    ffn_low = jnp.moveaxis(ffn, 1, 0).astype(LOW)
    ffn_cut = ffn_low.reshape(3, narrow_count, ffn_rows // narrow_count, ffn_low.shape[2])
    ffn_sub = exchange(jnp.moveaxis(ffn_cut, 1, 0), "narrow")
    ffn_w = [gather_rows(side_by_side(ffn_sub[:, j]), "wide") for j in range(3)]
    table_own = side_by_side(
        exchange(embed.astype(LOW).reshape(wide_count, vocab_rows // wide_count, columns), "wide")
    )

    mom_qo = jnp.moveaxis(attn_qo_mom, 1, 0)
    mom_kv = jnp.moveaxis(attn_kv_mom, 1, 0)
    mom_ffn = jnp.moveaxis(ffn_mom, 1, 0)
    slot = mom_ffn.shape[1] * mom_ffn.shape[2]

    def pack_small(qo_part, kv_part):
        flat = jnp.concatenate([qo_part.reshape(-1), kv_part.reshape(-1)])
        return jnp.pad(flat, (0, slot - flat.shape[0]))

    def unpack_small(flat):
        lead = flat.shape[:-1]
        qo_size, kv_size = mom_qo.size, mom_kv.size
        return (
            flat[..., :qo_size].reshape(lead + mom_qo.shape),
            flat[..., qo_size : qo_size + kv_size].reshape(lead + mom_kv.shape),
        )

    def one_per_owner(ffn_part, qo_part, kv_part):
        parts = [ffn_part[j].reshape(-1) for j in range(3)] + [pack_small(qo_part, kv_part)]
        parts = parts + [jnp.zeros_like(parts[0])] * (narrow_count - 4)
        return jnp.stack(parts)

    mom_owned = exchange(one_per_owner(mom_ffn, mom_qo, mom_kv), "narrow")

    tok_at = narrow_spot * tok_rows + jnp.arange(tok_rows, dtype=jnp.int32)
    seg_all = segments_at(lens, where_at)
    _, cosine_tok, sine_tok = angles_at(lens, tok_at)
    seg_mine, cosine, sine = angles_at(lens, pick_ids)

    rows_full = rows_low.astype(FULL)
    normed_all = norm_rows(rows_full, gain_w[0]).astype(LOW)
    normed_tok, normed_own = normed_all[:tok_rows], normed_all[tok_rows:]
    start_own = rows_full[tok_rows:]
    keys_part = dot(normed_tok, kv_w[0], 1, 0).reshape(tok_rows, KVH, HD)
    keys_part = rotate(keys_part, cosine_tok[:, None], sine_tok[:, None]).astype(LOW)
    values_part = dot(normed_tok, kv_w[1], 1, 0).reshape(tok_rows, KVH, HD).astype(LOW)
    by_head = jnp.moveaxis(jnp.stack([keys_part, values_part]), 2, 0)
    by_head = jnp.repeat(by_head, repeat, axis=0)
    by_head = by_head.reshape(narrow_count, groups, 2, tok_rows, HD)
    own_head, normed_parts = trade([by_head, normed_own], (True, False), 2, "trade_heads")
    own_head = jnp.transpose(own_head, (2, 1, 0, 3, 4)).reshape(2, groups, seq_len, HD)
    keys, values = own_head[0], own_head[1]
    normed = normed_parts.reshape(sel, width)

    queries = dot(normed, q_w, 1, 0).reshape(sel, heads_own, HD)
    queries = rotate(queries, cosine[:, None], sine[:, None]).astype(LOW)
    grouped = queries.reshape(sel, groups, heads_own // groups, HD)
    scale = HD ** (-0.5)
    scores = jnp.einsum("tkgd,ksd->kgts", grouped, keys, preferred_element_type=FULL) * scale
    allowed = (seg_mine[:, None] == seg_all[None, :]) & (pick_ids[:, None] >= where_at[None, :])
    scores = jnp.where(allowed, scores, MASKED)
    shifted_exp = jnp.exp(scores - jnp.max(scores, axis=-1, keepdims=True))
    probs = shifted_exp / jnp.sum(shifted_exp, axis=-1, keepdims=True)
    probs_low = probs.astype(LOW)
    mixed = jnp.einsum("kgts,ksd->tkgd", probs_low, values, preferred_element_type=FULL)
    mixed = mixed.reshape(sel, heads_own * HD).astype(LOW)

    middle, inner = settle(
        dot(mixed, o_w, 1, 1), start_own, start_own, always_row, gain_w[1:2], 3, "settle"
    )
    gate = dot(inner, ffn_w[0], 1, 1)
    up = dot(inner, ffn_w[1], 1, 1)
    hidden = (jax.nn.silu(gate) * up).astype(LOW)
    final_own, late_part = settle(
        dot(hidden, ffn_w[2], 1, 0), middle, start_own, keep_row, gain_w[2:3], 3, "settle"
    )

    table_count = table_own.shape[0]
    local_target = targets_all - (narrow_spot * vocab_rows + wide_spot * table_count)
    has_target = local_target[:, None] == jnp.arange(table_count, dtype=jnp.int32)[None, :]
    counted = (targets_all >= 0).astype(FULL)
    loss_count = jnp.sum(counted)
    total_rows = wide_count * sel

    early = gather_rows(norm_rows(start_own, gain_w[2]).astype(LOW), BOTH)
    late = gather_wide(late_part, 4, "gather_late").reshape(total_rows, width)

    def exit_logits(features):
        logits = dot(features, table_own, 1, 1)
        peak = jnp.max(logits, axis=-1)
        total = jnp.sum(jnp.exp(logits - peak[:, None]), axis=-1)
        picked = jnp.sum(jnp.where(has_target, logits, 0.0), axis=-1)
        return logits, jnp.stack([peak, total, picked])

    early_logits, early_stats = exit_logits(early)
    late_logits, late_stats = exit_logits(late)
    stats = jnp.pad(jnp.concatenate([early_stats, late_stats], axis=1), ((0, 5), (0, 0)))
    stats = combine(stats, merge_two, 5, "combine_stats")
    log_norms = stats[0] + jnp.log(stats[1])
    losses = log_norms - stats[2]
    loss_sum = jnp.sum(
        counted * (EXIT_EARLY * losses[:total_rows] + EXIT_LAST * losses[total_rows:])
    )

    def exit_back(logits, log_norm, weight, features):
        grad_logits = (
            (jnp.exp(logits - log_norm[:, None]) - has_target.astype(FULL))
            * (weight * counted)[:, None]
        ).astype(LOW)
        return dot(grad_logits, table_own, 1, 0), dot(grad_logits, features, 0, 0)

    late_back, late_head = exit_back(late_logits, log_norms[total_rows:], EXIT_LAST, late)
    early_back, early_head = exit_back(early_logits, log_norms[:total_rows], EXIT_EARLY, early)
    grad_late = sum_wide(late_back.astype(LOW), 6, "sum_late")
    grad_early = lax.psum_scatter(
        lax.psum_scatter(early_back, "wide", scatter_dimension=0, tiled=True),
        "narrow",
        scatter_dimension=0,
        tiled=True,
    )
    grad_head = (early_head + late_head).astype(LOW)
    head_cols = exchange(cut_columns(grad_head, wide_count), "wide").reshape(vocab_rows, columns)
    grad_start_exit, gain_early = norm_back(start_own, gain_w[2], grad_early)

    grad_final, gain_late, grad_out = settle_back(
        grad_late, final_own, jnp.zeros_like(final_own), keep_row, gain_w[2:3], 7, "settle_back"
    )
    grad_layer = grad_final * keep_layer
    grad_hidden = dot(grad_out, ffn_w[2], 1, 1)
    sigma = jax.nn.sigmoid(gate)
    grad_gate = (grad_hidden * up * sigma * (1.0 + gate * (1.0 - sigma))).astype(LOW)
    grad_up = (grad_hidden * gate * sigma).astype(LOW)
    grad_mid, gain_mid, grad_branch = settle_back(
        dot(grad_gate, ffn_w[0], 1, 0) + dot(grad_up, ffn_w[1], 1, 0),
        middle,
        grad_layer,
        keep_row,
        gain_w[1:2],
        7,
        "settle_back",
    )

    grad_mixed = dot(grad_branch, o_w, 1, 0).astype(LOW)
    grouped_grad = grad_mixed.reshape(sel, groups, heads_own // groups, HD)
    grad_probs = jnp.einsum("tkgd,ksd->kgts", grouped_grad, values, preferred_element_type=FULL)
    grad_scores = (
        probs * (grad_probs - jnp.sum(probs * grad_probs, axis=-1, keepdims=True))
    ).astype(LOW)
    grad_queries = (
        jnp.einsum("kgts,ksd->tkgd", grad_scores, keys, preferred_element_type=FULL) * scale
    ).reshape(sel, heads_own, HD)
    grad_queries = (
        unrotate(grad_queries, cosine[:, None], sine[:, None])
        .reshape(sel, heads_own * HD)
        .astype(LOW)
    )
    grad_keys = jnp.einsum("kgts,tkgd->ksd", grad_scores, grouped, preferred_element_type=FULL)
    _, cosine_all, sine_all = angles_at(lens, where_at)
    grad_keys = unrotate(grad_keys * scale, cosine_all, sine_all).astype(LOW)
    grad_values = jnp.einsum(
        "kgts,tkgd->ksd", probs_low, grouped_grad, preferred_element_type=FULL
    ).astype(LOW)
    kv_parts = jnp.stack([grad_keys, grad_values]).reshape(
        2, groups, narrow_count, tok_rows, HD
    )
    kv_parts = jnp.transpose(kv_parts, (2, 1, 0, 3, 4))
    pick_parts = dot(grad_queries, q_w, 1, 1).reshape(narrow_count, own_rows, width)
    grad_kv, pick_parts = trade([kv_parts, pick_parts], (True, True), 8, "trade_grads")
    grad_kv = grad_kv.reshape(KVH, repeat, 2, tok_rows, HD)
    if repeat > 1:
        grad_kv = jnp.sum(grad_kv.astype(FULL), axis=1, keepdims=True).astype(LOW)
    grad_kv = jnp.transpose(grad_kv[:, 0], (1, 2, 0, 3)).reshape(2, tok_rows, KVH * HD)

    grad_normed = jnp.concatenate(
        [
            dot(grad_kv[0], kv_w[0], 1, 1) + dot(grad_kv[1], kv_w[1], 1, 1),
            jnp.sum(pick_parts, axis=0),
        ]
    )
    grad_rows, gain_attn = norm_back(rows_full, gain_w[0], grad_normed)
    grad_pass = grad_mid + grad_start_exit + grad_final * (1.0 - keep_layer)
    grad_rows = jnp.concatenate([grad_rows[:tok_rows], grad_rows[tok_rows:] + grad_pass])
    grad_rows = return_rows(grad_rows.astype(LOW), 9, "return_rows").reshape(-1, columns)
    summed_table, table_squares = spread(spots, grad_rows, head_cols)

    tok_cols = exchange(cut_columns(normed_tok, wide_count), "wide").reshape(-1, columns)
    grad_kv_wide = lax.all_gather(grad_kv, "wide", axis=1, tiled=True)
    grad_kv_w = jnp.stack([dot(tok_cols, grad_kv_wide[j], 0, 0) for j in range(2)])
    summed_kv = lax.psum_scatter(grad_kv_w, "narrow", scatter_dimension=2, tiled=True)

    def left_cols(values_all):
        return exchange(cut_columns(values_all, wide_count), "wide").reshape(-1, columns)

    summed_qo = jnp.stack(
        [
            dot(left_cols(normed), gather_rows(grad_queries, "wide"), 0, 0),
            dot(left_cols(grad_branch), gather_rows(mixed, "wide"), 0, 0),
        ]
    )

    inner_all = gather_rows(inner, "wide")
    out_all = gather_rows(grad_out, "wide")
    acts = jnp.stack([grad_gate, grad_up, hidden]).reshape(
        3, sel, wide_count, ffn_rows // narrow_count
    )
    acts = exchange(jnp.moveaxis(acts, 2, 0), "wide")
    acts = jnp.moveaxis(acts, 1, 0).reshape(3, wide_count * sel, ffn_rows // narrow_count)
    acts = lax.all_gather(acts, "narrow", axis=2, tiled=True)

    def cols_own(values_all):
        size = width // narrow_count
        return lax.dynamic_slice_in_dim(values_all, narrow_spot * size, size, 1)

    rights = (inner_all, inner_all, out_all)
    summed_ffn = jnp.stack([dot(acts[j], cols_own(rights[j]), 0, 0) for j in range(3)])
    small_all = lax.all_gather(
        pack_small(summed_qo, summed_kv).astype(LOW), "narrow", axis=0
    )

    squares = (
        jnp.sum(summed_qo * summed_qo)
        + jnp.sum(summed_kv * summed_kv)
        + jnp.sum(summed_ffn * summed_ffn)
        + jnp.sum(table_squares)
    )
    sums = jnp.stack([gain_attn, gain_mid, gain_early + gain_late, jnp.full((width,), squares)])
    sums = combine(jnp.pad(sums, ((0, 4), (0, 0))), add_two, 10, "combine_sums")
    gain_size = gains.shape[1]
    summed_gain = lax.dynamic_slice_in_dim(
        sums[:3], (wide_spot * narrow_count + narrow_spot) * gain_size, gain_size, 1
    )
    square_total = sums[3, 0] + jnp.sum(sums[:3] * sums[:3])
    grad_norm = jnp.sqrt(square_total) / loss_count
    factor = jnp.minimum(1.0, CLIP_NORM / (grad_norm + 1e-06)) / loss_count

    def whole_columns(parts):
        return jnp.moveaxis(parts, 0, 2).reshape(
            parts.shape[1], parts.shape[2], parts.shape[0] * parts.shape[3]
        )

    def ffn_owner():
        left = lax.dynamic_index_in_dim(acts, jnp.minimum(narrow_spot, 2), 0, False)
        right = jnp.where(narrow_spot == 2, out_all, inner_all)
        grad = dot(left, right, 0, 0)
        mom = side_by_side(mom_owned.reshape((narrow_count,) + mom_ffn.shape[1:]))
        result = orthogonalize((MOMENTUM * mom + grad * factor)[None])[0]
        return cut_columns(result.astype(LOW), narrow_count).reshape(narrow_count, slot)

    def small_owner():
        mom_q, mom_k = unpack_small(mom_owned)
        grad_q, grad_k = unpack_small(small_all.astype(FULL))
        results = [
            orthogonalize(whole_columns(MOMENTUM * mom + grad * factor)).astype(LOW)
            for mom, grad in ((mom_q, grad_q), (mom_k, grad_k))
        ]
        parts = [
            jnp.moveaxis(
                result.reshape(2, result.shape[1], narrow_count, -1), 2, 0
            ).reshape(narrow_count, -1)
            for result in results
        ]
        flat = jnp.concatenate(parts, axis=1)
        return jnp.pad(flat, ((0, 0), (0, slot - flat.shape[1])))

    directions = lax.cond(narrow_spot == 3, small_owner, ffn_owner)
    directions = exchange(directions, "narrow")
    dir_ffn = directions[:3].reshape(mom_ffn.shape).astype(FULL)
    dir_qo, dir_kv = unpack_small(directions[3].astype(FULL))

    embed_new, embed_m_new, embed_v_new = adamw(
        embed, embed_m, embed_v, summed_table * factor, RATE_ADAM, WEIGHT_DECAY
    )
    gains_new, gains_m_new, gains_v_new = adamw(
        gains, gains_m, gains_v, summed_gain * factor, RATE_GAIN, 0.0
    )

    def mom_next(mom, grad):
        return MOMENTUM * mom + jnp.moveaxis(grad * factor, 0, 1)

    shrink = 1.0 - RATE_MUON * WEIGHT_DECAY

    def weight_next(weight, direction):
        return weight * shrink - RATE_MUON * jnp.moveaxis(direction, 0, 1)

    return (
        loss_sum,
        loss_count,
        grad_norm,
        embed_new,
        embed_m_new,
        embed_v_new,
        weight_next(attn_qo, dir_qo),
        mom_next(attn_qo_mom, summed_qo),
        weight_next(attn_kv, dir_kv),
        mom_next(attn_kv_mom, summed_kv),
        weight_next(ffn, dir_ffn),
        mom_next(ffn_mom, summed_ffn),
        gains_new,
        gains_m_new,
        gains_v_new,
    )


def solution(mesh):
    by_pack = P("wide", None)
    table = P("narrow", "wide")
    layer = P("wide", None, "narrow")
    gain = P(None, ("wide", "narrow"))
    return jax.shard_map(
        per_device,
        mesh=mesh,
        in_specs=(by_pack,) * 4 + (P("wide"),) + (table,) * 3 + (layer,) * 6 + (gain,) * 3,
        out_specs=(P(),) * 3 + (table,) * 3 + (layer,) * 6 + (gain,) * 3,
        check_vma=False,
    )
```

```python
import functools

import jax
import jax.numpy as jnp
from jax import lax
from jax.experimental import pallas as pl
from jax.experimental.pallas import tpu as pltpu
from jax.sharding import PartitionSpec as P

HEADS = 16
HD = 128
KVH = 4
NS_STEPS = 5
STEP = 10


NORM_EPS = 1e-05
ROPE_BASE = 10000.0
EXIT_EARLY = 0.25
EXIT_LAST = 1.0
CLIP_NORM = 0.02
BETA_ONE = 0.9
BETA_TWO = 0.95
ADAM_EPS = 1e-08
RATE_ADAM = 0.02
RATE_GAIN = 0.3
RATE_MUON = 0.3
WEIGHT_DECAY = 0.1
MOMENTUM = 0.95
NEWTON_A = 3.4445
NEWTON_B = -4.775
NEWTON_C = 2.0315
MASKED = -1e30
LOW = jnp.bfloat16
FULL = jnp.float32
BOTH = ("wide", "narrow")
ROWS_IN_BLOCK = 1024
UNROLL = 16
VMEM_BYTES = 56 * 1024 * 1024


def dot(first, second, first_dim, second_dim):
    return lax.dot_general(
        first, second, (((first_dim,), (second_dim,)), ((), ())), preferred_element_type=FULL
    )


def norm_rows(values, gain_row):
    return (
        values * lax.rsqrt(jnp.mean(values * values, axis=-1, keepdims=True) + NORM_EPS) * gain_row
    )


def norm_back(values, gain_row, grad):
    output, pull = jax.vjp(norm_rows, values, gain_row)
    return pull(grad)


def segments_at(lens, where_at):
    ends = jnp.cumsum(lens)
    return jnp.sum((where_at[:, None] >= ends[None, :]).astype(jnp.int32), axis=1)


def angles_at(lens, where_at):
    segment = segments_at(lens, where_at)
    starts = jnp.cumsum(lens) - lens
    member = segment[:, None] == jnp.arange(lens.shape[0], dtype=jnp.int32)[None, :]
    begin = jnp.sum(jnp.where(member, starts[None, :], 0), axis=1)
    offset_pos = (where_at - begin).astype(FULL)
    inverse = ROPE_BASE ** (-2.0 * jnp.arange(HD // 2, dtype=FULL) / HD)
    angle = offset_pos[:, None] * inverse[None, :]
    return (segment, jnp.cos(angle), jnp.sin(angle))


def rotate(values, cosine, sine):
    half = values.shape[-1] // 2
    first, second = (values[..., :half], values[..., half:])
    return jnp.concatenate(
        [first * cosine - second * sine, second * cosine + first * sine], axis=-1
    )


def unrotate(values, cosine, sine):
    return rotate(values, cosine, -sine)


MESH = pl.DeviceIdType.MESH
ANY = pl.BlockSpec(memory_space=pl.ANY)
VMEM = pl.BlockSpec(memory_space=pltpu.VMEM)


def others(axis, count):
    me = lax.axis_index(axis)
    return [{axis: lax.rem(me + step, count)} for step in range(1, count)]


def push(source, target, send, receive, device):
    return pltpu.make_async_remote_copy(
        src_ref=source,
        dst_ref=target,
        send_sem=send,
        recv_sem=receive,
        device_id=device,
        device_id_type=MESH,
    )


def arrived(block, send, receive, device):
    push(block, block, send, receive, device).wait_recv()


def like(values):
    return jax.ShapeDtypeStruct(values.shape, values.dtype)


def struct(shape, dtype):
    return jax.ShapeDtypeStruct(shape, dtype)


def sems(*shape):
    return pltpu.SemaphoreType.DMA(shape)


class Task:
    def __init__(self, inputs, outputs, scratch, steps, place_in, place_out, axes):
        self.inputs, self.outputs, self.scratch, self.steps = inputs, outputs, scratch, steps
        self.place_in = [place_in] * len(inputs)
        self.place_out = [place_out] * len(outputs)
        self.axes = axes


def launch(tasks, ident, name):
    axes = sorted(set(axis for task in tasks for axis in task.axes))
    inputs = [a for task in tasks for a in task.inputs]
    outputs = [a for task in tasks for a in task.outputs]
    scratch = [a for task in tasks for a in task.scratch]

    def body(*refs):
        refs = list(refs)
        ins = refs[: len(inputs)]
        outs = refs[len(inputs) : len(inputs) + len(outputs)]
        extra = refs[len(inputs) + len(outputs) :]
        barrier = pltpu.get_barrier_semaphore()
        targets = [device for axis in axes for device in others(axis, lax.axis_size(axis))]
        for device in targets:
            pl.semaphore_signal(barrier, inc=1, device_id=device, device_id_type=MESH)
        pl.semaphore_wait(barrier, len(targets))
        live = []
        for task in tasks:
            counts = (len(task.inputs), len(task.outputs), len(task.scratch))
            live.append(task.steps(ins[: counts[0]], outs[: counts[1]], extra[: counts[2]]))
            ins, outs, extra = ins[counts[0] :], outs[counts[1] :], extra[counts[2] :]
        while live:
            live = [steps for steps in live if next(steps, 0) is None]

    size = sum(a.size * a.dtype.itemsize for a in list(inputs) + list(outputs))
    return pl.pallas_call(
        body,
        out_shape=outputs,
        in_specs=[place for task in tasks for place in task.place_in],
        out_specs=[place for task in tasks for place in task.place_out],
        scratch_shapes=scratch,
        compiler_params=pltpu.CompilerParams(
            collective_id=ident, has_side_effects=True, vmem_limit_bytes=VMEM_BYTES
        ),
        cost_estimate=pl.CostEstimate(flops=0, bytes_accessed=8 * size, transcendentals=0),
        name=name,
    )(*inputs)


def gather_wide(values):
    count = lax.axis_size("wide")
    chips = count // 2

    def steps(ins, outs, scratch):
        (x_ref,), (out_ref,), (send, receive, local) = ins, outs, scratch
        me = lax.axis_index("wide")
        mate = me + 1 - 2 * lax.rem(me, 2)
        peers = [lax.rem(me + 2 * step, count) for step in range(1, chips)] + [mate]
        first = []
        for step, peer in enumerate(peers):
            copy = push(x_ref, out_ref.at[me], send.at[step], receive.at[me], {"wide": peer})
            copy.start()
            first.append(copy)
        keep = pltpu.make_async_copy(x_ref, out_ref.at[me], local)
        keep.start()
        yield
        second = []
        for step in range(1, chips):
            source = lax.rem(me - 2 * step + count, count)
            block = out_ref.at[source]
            arrived(block, send.at[0], receive.at[source], {"wide": mate})
            copy = push(
                block, block, send.at[chips + step - 1], receive.at[source], {"wide": mate}
            )
            copy.start()
            second.append(copy)
        yield
        for step in range(chips):
            source = lax.rem(mate - 2 * step + count, count)
            arrived(out_ref.at[source], send.at[0], receive.at[source], {"wide": mate})
        for copy in first + second:
            copy.wait_send()
        keep.wait()

    shape = struct((count,) + values.shape, values.dtype)
    return Task(
        [values], [shape], [sems(count - 1), sems(count), sems()], steps, ANY, ANY, ["wide"]
    )


def trade(axis, values, source_of, target_of, shape):
    count = lax.axis_size(axis)

    def steps(ins, outs, scratch):
        (x_ref,), (out_ref,), (send, receive, local) = ins, outs, scratch
        me = lax.axis_index(axis)
        copies = []
        for step in range(1, count):
            peer = lax.rem(me + step, count)
            copy = push(
                source_of(x_ref, peer),
                target_of(out_ref, me),
                send.at[step - 1],
                receive.at[me],
                {axis: peer},
            )
            copy.start()
            copies.append(copy)
        keep = pltpu.make_async_copy(source_of(x_ref, me), target_of(out_ref, me), local)
        keep.start()
        yield
        yield
        for step in range(1, count):
            source = lax.rem(me - step + count, count)
            arrived(
                target_of(out_ref, source), send.at[0], receive.at[source], {axis: source}
            )
        for copy in copies:
            copy.wait_send()
        keep.wait()

    return Task(
        [values],
        [struct(shape, values.dtype)],
        [sems(count - 1), sems(count), sems()],
        steps,
        ANY,
        ANY,
        [axis],
    )


def block_at(ref, spot):
    return ref.at[spot]


def whole_at(ref, spot):
    return ref


def columns_of(size):
    def at(ref, spot):
        return ref.at[:, pl.ds(pl.multiple_of(spot * size, size), size)]

    return at


def swap_blocks(axis, values):
    return trade(axis, values, block_at, block_at, values.shape)


def gather_blocks(axis, values):
    shape = (lax.axis_size(axis),) + values.shape
    return trade(axis, values, whole_at, block_at, shape)


def split_columns(axis, values):
    count = lax.axis_size(axis)
    rows, size = values.shape[0], values.shape[1] // count
    return trade(axis, values, columns_of(size), block_at, (count, rows, size))


def join_columns(axis, values):
    count, rows, size = values.shape
    return trade(axis, values, block_at, columns_of(size), (rows, count * size))


def collect(count, parts_ref, slots, send, receive):
    me = lax.axis_index("narrow")
    copies = []
    for step in range(1, count):
        peer = lax.rem(me + step, count)
        copy = push(
            parts_ref.at[peer],
            slots.at[me],
            send.at[step - 1],
            receive.at[me],
            {"narrow": peer},
        )
        copy.start()
        copies.append(copy)
    return copies


def collected(count, parts_ref, slots, send, receive):
    me = lax.axis_index("narrow")
    total = parts_ref[me].astype(FULL)
    for step in range(1, count):
        source = lax.rem(me - step + count, count)
        arrived(slots.at[source], send.at[0], receive.at[source], {"narrow": source})
        total = total + slots[source].astype(FULL)
    return total


def share(count, low, all_ref, send, receive):
    me = lax.axis_index("narrow")
    all_ref[me] = low
    copies = []
    for step in range(1, count):
        peer = lax.rem(me + step, count)
        copy = push(
            all_ref.at[me], all_ref.at[me], send.at[step - 1], receive.at[me], {"narrow": peer}
        )
        copy.start()
        copies.append(copy)
    return copies


def shared(count, all_ref, send, receive):
    me = lax.axis_index("narrow")
    for step in range(1, count):
        source = lax.rem(me - step + count, count)
        arrived(all_ref.at[source], send.at[0], receive.at[source], {"narrow": source})


def narrow_sems(count):
    return [sems(count - 1), sems(count)]


def settle(partial, base, other, keep_row, gain_row):
    count = lax.axis_size("narrow")
    rows, width = base.shape

    def steps(ins, outs, scratch):
        parts_ref, base_ref, other_ref, keep_ref, gain_ref = ins
        own_ref, all_ref = outs
        slots, send, receive, send_all, receive_all = scratch
        copies = collect(count, parts_ref, slots, send, receive)
        yield
        total = collected(count, parts_ref, slots, send, receive)
        total = jnp.where(keep_ref[...] > 0, total + base_ref[...], other_ref[...])
        own_ref[...] = total
        low = norm_rows(total, gain_ref[...]).astype(LOW)
        copies = copies + share(count, low, all_ref, send_all, receive_all)
        yield
        shared(count, all_ref, send_all, receive_all)
        for copy in copies:
            copy.wait_send()

    return Task(
        [partial.reshape(count, rows, width), base, other, keep_row, gain_row],
        [struct((rows, width), FULL), struct((count, rows, width), LOW)],
        [pltpu.VMEM((count, rows, width), partial.dtype)]
        + narrow_sems(count)
        + narrow_sems(count),
        steps,
        VMEM,
        VMEM,
        ["narrow"],
    )


def settle_back(partial, values, add, keep_row, gain_row):
    count = lax.axis_size("narrow")
    rows, width = values.shape

    def steps(ins, outs, scratch):
        parts_ref, values_ref, add_ref, keep_ref, gain_ref = ins
        own_ref, gain_grad_ref, all_ref = outs
        slots, send, receive, send_all, receive_all = scratch
        copies = collect(count, parts_ref, slots, send, receive)
        yield
        grad = collected(count, parts_ref, slots, send, receive)
        held = values_ref[...]
        root = lax.rsqrt(jnp.mean(held * held, axis=-1, keepdims=True) + NORM_EPS)
        scaled = gain_ref[...] * grad
        inner = jnp.mean(held * scaled, axis=-1, keepdims=True)
        own = add_ref[...] + root * scaled - held * (root * root * root * inner)
        gain_grad_ref[...] = jnp.sum(held * root * grad, axis=0, keepdims=True)
        own_ref[...] = own
        low = (own * keep_ref[...]).astype(LOW)
        copies = copies + share(count, low, all_ref, send_all, receive_all)
        yield
        shared(count, all_ref, send_all, receive_all)
        for copy in copies:
            copy.wait_send()

    return Task(
        [partial.reshape(count, rows, width), values, add, keep_row, gain_row],
        [
            struct((rows, width), FULL),
            struct((1, width), FULL),
            struct((count, rows, width), LOW),
        ],
        [pltpu.VMEM((count, rows, width), partial.dtype)]
        + narrow_sems(count)
        + narrow_sems(count),
        steps,
        VMEM,
        VMEM,
        ["narrow"],
    )


def sum_narrow(partial):
    count = lax.axis_size("narrow")
    rows, width = partial.shape[0] // count, partial.shape[1]

    def steps(ins, outs, scratch):
        (parts_ref,), (own_ref,), (slots, send, receive) = ins, outs, scratch
        copies = collect(count, parts_ref, slots, send, receive)
        yield
        yield
        own_ref[...] = collected(count, parts_ref, slots, send, receive)
        for copy in copies:
            copy.wait_send()

    return Task(
        [partial.reshape(count, rows, width)],
        [struct((rows, width), FULL)],
        [pltpu.VMEM((count, rows, width), partial.dtype)] + narrow_sems(count),
        steps,
        VMEM,
        VMEM,
        ["narrow"],
    )


def fetch_rows(found, rows):
    deep, wide = lax.axis_size("narrow"), lax.axis_size("wide")
    columns = found.shape[2]

    def steps(ins, outs, scratch):
        (found_ref,), (out_ref,) = ins, outs
        rightward, leftward, final = scratch[:3]
        send_right, receive_right, send_left, receive_left = scratch[3:7]
        send_wide, receive_wide, local = scratch[7:]
        spot = lax.axis_index("narrow")
        me = lax.axis_index("wide")

        def right_copy(part, source):
            return push(
                source,
                rightward.at[part],
                send_right.at[part],
                receive_right.at[part],
                {"narrow": lax.rem(spot + 1, deep)},
            )

        def left_copy(part, source):
            return push(
                source,
                leftward.at[part],
                send_left.at[part],
                receive_left.at[part],
                {"narrow": lax.rem(spot + deep - 1, deep)},
            )

        for step in range(deep - 1):
            right, left = deep - 1 - step, step

            @pl.when((spot == 0) & (right > 0))
            def _():
                right_copy(right, found_ref.at[right]).start()

            @pl.when((spot == deep - 1) & (left < deep - 1))
            def _():
                left_copy(left, found_ref.at[left]).start()

        yield
        for step in range(deep - 1):
            right, left = deep - 1 - step, step

            @pl.when((spot > 0) & (right > spot))
            def _():
                right_copy(right, rightward.at[right]).wait_recv()
                rightward[right] = rightward[right] + found_ref[right]
                right_copy(right, rightward.at[right]).start()

            @pl.when((spot < deep - 1) & (left < spot))
            def _():
                left_copy(left, leftward.at[left]).wait_recv()
                leftward[left] = leftward[left] + found_ref[left]
                left_copy(left, leftward.at[left]).start()

        final[...] = found_ref[spot]

        @pl.when(spot > 0)
        def _():
            right_copy(spot, rightward.at[spot]).wait_recv()
            final[...] = final[...] + rightward[spot]

        @pl.when(spot < deep - 1)
        def _():
            left_copy(spot, leftward.at[spot]).wait_recv()
            final[...] = final[...] + leftward[spot]

        def rows_for(device):
            return final.at[pl.ds(pl.multiple_of(device * rows, rows), rows)]

        def columns_from(device):
            return columns_of(columns)(out_ref, device)

        copies = []
        for step in range(1, wide):
            peer = lax.rem(me + step, wide)
            copy = push(
                rows_for(peer),
                columns_from(me),
                send_wide.at[step - 1],
                receive_wide.at[me],
                {"wide": peer},
            )
            copy.start()
            copies.append(copy)
        keep = pltpu.make_async_copy(rows_for(me), columns_from(me), local)
        keep.start()
        for step in range(1, wide):
            source = lax.rem(me - step + wide, wide)
            arrived(
                columns_from(source), send_wide.at[0], receive_wide.at[source], {"wide": source}
            )
        yield
        for copy in copies:
            copy.wait_send()
        keep.wait()
        for step in range(deep - 1):
            right, left = deep - 1 - step, step

            @pl.when(right > spot)
            def _():
                right_copy(right, found_ref.at[right]).wait_send()

            @pl.when(left < spot)
            def _():
                left_copy(left, found_ref.at[left]).wait_send()

    task = Task(
        [found],
        [struct((rows, wide * columns), found.dtype)],
        [pltpu.VMEM(found.shape, found.dtype)] * 2
        + [pltpu.VMEM(found.shape[1:], found.dtype)]
        + [sems(deep)] * 4
        + [sems(wide - 1), sems(wide), sems()],
        steps,
        VMEM,
        ANY,
        ["narrow", "wide"],
    )
    return task


def return_rows(rows):
    deep, wide = lax.axis_size("narrow"), lax.axis_size("wide")
    count, width = rows.shape
    columns = width // wide

    def steps(ins, outs, scratch):
        (rows_ref,), (out_ref,) = ins, outs
        send_right, send_left, receive_deep, send_wide, receive_wide, local = scratch
        spot = lax.axis_index("narrow")
        me = lax.axis_index("wide")
        part_of = functools.partial(columns_of(columns), rows_ref)

        def landing(device):
            return out_ref.at[spot, pl.ds(pl.multiple_of(device * count, count), count)]

        copies = []
        for step in range(1, wide):
            peer = lax.rem(me + step, wide)
            copy = push(
                part_of(peer),
                landing(me),
                send_wide.at[step - 1],
                receive_wide.at[me],
                {"wide": peer},
            )
            copy.start()
            copies.append(copy)
        keep = pltpu.make_async_copy(part_of(me), landing(me), local)
        keep.start()
        yield
        for step in range(1, wide):
            source = lax.rem(me - step + wide, wide)
            arrived(landing(source), send_wide.at[0], receive_wide.at[source], {"wide": source})
        keep.wait()

        def right_copy(part):
            return push(
                out_ref.at[part],
                out_ref.at[part],
                send_right.at[part],
                receive_deep.at[part],
                {"narrow": lax.rem(spot + 1, deep)},
            )

        def left_copy(part):
            return push(
                out_ref.at[part],
                out_ref.at[part],
                send_left.at[part],
                receive_deep.at[part],
                {"narrow": lax.rem(spot + deep - 1, deep)},
            )

        @pl.when(spot < deep - 1)
        def _():
            right_copy(spot).start()

        @pl.when(spot > 0)
        def _():
            left_copy(spot).start()

        for step in range(1, deep):
            yield

            @pl.when(spot >= step)
            def _():
                right_copy(spot - step).wait_recv()

                @pl.when(spot < deep - 1)
                def _():
                    right_copy(spot - step).start()

            @pl.when(spot + step < deep)
            def _():
                left_copy(spot + step).wait_recv()

                @pl.when(spot > 0)
                def _():
                    left_copy(spot + step).start()

        for part in range(deep):

            @pl.when((part <= spot) & (spot < deep - 1))
            def _():
                right_copy(part).wait_send()

            @pl.when((part >= spot) & (spot > 0))
            def _():
                left_copy(part).wait_send()

        for copy in copies:
            copy.wait_send()

    return Task(
        [rows],
        [struct((deep, wide * count, columns), rows.dtype)],
        [sems(deep)] * 3 + [sems(wide - 1), sems(wide), sems()],
        steps,
        ANY,
        ANY,
        ["narrow", "wide"],
    )


def sum_wide(partial):
    count = lax.axis_size("wide")
    chips = count // 2
    rows, width = partial.shape[0] // count, partial.shape[1]

    def steps(ins, outs, scratch):
        (parts_ref,), (out_ref,) = ins, outs
        from_mate, paired, slots, send_mate, receive_mate, send, receive = scratch
        me = lax.axis_index("wide")
        side = lax.rem(me, 2)
        mate = me + 1 - 2 * side
        my_chip = me // 2
        mate_copies = []
        for step in range(chips):
            chip = lax.rem(my_chip + 1 + step, chips)
            copy = push(
                parts_ref.at[2 * chip + 1 - side],
                from_mate.at[chip],
                send_mate.at[step],
                receive_mate.at[chip],
                {"wide": mate},
            )
            copy.start()
            mate_copies.append(copy)
        yield
        copies = []
        for step in range(chips):
            chip = lax.rem(my_chip + 1 + step, chips)
            arrived(from_mate.at[chip], send_mate.at[0], receive_mate.at[chip], {"wide": mate})
            both = parts_ref[2 * chip + side].astype(FULL) + from_mate[chip].astype(FULL)
            if step < chips - 1:
                paired[chip] = both.astype(LOW)
                copy = push(
                    paired.at[chip],
                    slots.at[my_chip],
                    send.at[step],
                    receive.at[my_chip],
                    {"wide": 2 * chip + side},
                )
                copy.start()
                copies.append(copy)
            else:
                out_ref[...] = both
        yield
        for step in range(1, chips):
            chip = lax.rem(my_chip - step + chips, chips)
            arrived(slots.at[chip], send.at[0], receive.at[chip], {"wide": 2 * chip + side})
            out_ref[...] = out_ref[...] + slots[chip].astype(FULL)
        for copy in mate_copies + copies:
            copy.wait_send()

    return Task(
        [partial.reshape(count, rows, width)],
        [struct((rows, width), FULL)],
        [pltpu.VMEM((chips, rows, width), LOW)] * 3
        + [sems(chips), sems(chips), sems(max(chips - 1, 1)), sems(chips)],
        steps,
        VMEM,
        VMEM,
        ["wide"],
    )


def merge_stats(first, second):
    peak = jnp.maximum(first[0:1], second[0:1])
    total = first[1:2] * jnp.exp(first[0:1] - peak) + second[1:2] * jnp.exp(second[0:1] - peak)
    return jnp.concatenate([peak, total, first[2:3] + second[2:3]], axis=0)


def add_two(first, second):
    return first + second


def combine(values, join):
    deep, wide = lax.axis_size("narrow"), lax.axis_size("wide")

    def steps(ins, outs, scratch):
        (x_ref,), (out_ref,) = ins, outs
        wide_slots, deep_slots, send_wide, receive_wide, send_deep, receive_deep = scratch

        def start(axis, count, slots, value, send, receive):
            me = lax.axis_index(axis)
            slots[me] = value
            copies = []
            for step in range(1, count):
                peer = lax.rem(me + step, count)
                copy = push(
                    slots.at[me], slots.at[me], send.at[step - 1], receive.at[me], {axis: peer}
                )
                copy.start()
                copies.append(copy)
            return copies

        def finish(axis, count, slots, send, receive):
            me = lax.axis_index(axis)
            for step in range(1, count):
                source = lax.rem(me - step + count, count)
                arrived(slots.at[source], send.at[0], receive.at[source], {axis: source})
            total = slots[0]
            for source in range(1, count):
                total = join(total, slots[source])
            return total

        first = start("wide", wide, wide_slots, x_ref[...], send_wide, receive_wide)
        yield
        total = finish("wide", wide, wide_slots, send_wide, receive_wide)
        second = start("narrow", deep, deep_slots, total, send_deep, receive_deep)
        yield
        out_ref[...] = finish("narrow", deep, deep_slots, send_deep, receive_deep)
        for copy in first + second:
            copy.wait_send()

    return Task(
        [values],
        [like(values)],
        [
            pltpu.VMEM((wide,) + values.shape, values.dtype),
            pltpu.VMEM((deep,) + values.shape, values.dtype),
            sems(wide - 1),
            sems(wide),
            sems(deep - 1),
            sems(deep),
        ],
        steps,
        VMEM,
        VMEM,
        ["narrow", "wide"],
    )


def gather_both(values):
    deep, wide = lax.axis_size("narrow"), lax.axis_size("wide")

    def steps(ins, outs, scratch):
        (x_ref,), (out_ref,) = ins, outs
        send_wide, receive_wide, send_deep, receive_deep = scratch
        me = lax.axis_index("wide")
        spot = lax.axis_index("narrow")
        out_ref[spot, me] = x_ref[...]
        copies = []
        for step in range(1, wide):
            peer = lax.rem(me + step, wide)
            block = out_ref.at[spot, me]
            copy = push(block, block, send_wide.at[step - 1], receive_wide.at[me], {"wide": peer})
            copy.start()
            copies.append(copy)
        yield
        for step in range(1, wide):
            source = lax.rem(me - step + wide, wide)
            block = out_ref.at[spot, source]
            arrived(block, send_wide.at[0], receive_wide.at[source], {"wide": source})
        for step in range(1, deep):
            peer = lax.rem(spot + step, deep)
            block = out_ref.at[spot]
            copy = push(
                block, block, send_deep.at[step - 1], receive_deep.at[spot], {"narrow": peer}
            )
            copy.start()
            copies.append(copy)
        yield
        for step in range(1, deep):
            source = lax.rem(spot - step + deep, deep)
            block = out_ref.at[source]
            arrived(block, send_deep.at[0], receive_deep.at[source], {"narrow": source})
        for copy in copies:
            copy.wait_send()

    return Task(
        [values],
        [struct((deep, wide) + values.shape, values.dtype)],
        [sems(wide - 1), sems(wide), sems(deep - 1), sems(deep)],
        steps,
        VMEM,
        VMEM,
        ["narrow", "wide"],
    )


def feed_body(inner_ref, weight_ref, gate_ref, up_ref, hidden_ref, out_ref, total):
    part = pl.program_id(0)
    inner = inner_ref[...]
    gate = dot(inner, weight_ref[0, 0], 1, 1)
    up = dot(inner, weight_ref[0, 1], 1, 1)
    hidden = (jax.nn.silu(gate) * up).astype(LOW)
    gate_ref[0] = gate
    up_ref[0] = up
    hidden_ref[0] = hidden
    product = dot(hidden, weight_ref[0, 2], 1, 0)

    @pl.when(part == 0)
    def _():
        total[...] = product

    @pl.when(part > 0)
    def _():
        total[...] = total[...] + product

    @pl.when(part == pl.num_programs(0) - 1)
    def _():
        out_ref[...] = total[...].astype(LOW)


def feed(inner, weight):
    parts, _, size, width = weight.shape
    sel = inner.shape[0]
    same = pl.BlockSpec((sel, width), lambda part: (0, 0))
    slab = pl.BlockSpec((1, sel, size), lambda part: (part, 0, 0))
    return pl.pallas_call(
        feed_body,
        grid=(parts,),
        in_specs=[same, pl.BlockSpec((1, 3, size, width), lambda part: (part, 0, 0, 0))],
        out_specs=[slab, slab, slab, same],
        out_shape=[
            struct((parts, sel, size), FULL),
            struct((parts, sel, size), FULL),
            struct((parts, sel, size), LOW),
            struct((sel, width), LOW),
        ],
        scratch_shapes=[pltpu.VMEM((sel, width), FULL)],
        compiler_params=pltpu.CompilerParams(vmem_limit_bytes=VMEM_BYTES),
        cost_estimate=pl.CostEstimate(
            flops=6 * sel * parts * size * width,
            bytes_accessed=weight.size * 2,
            transcendentals=0,
        ),
        name="feed",
    )(inner, weight)


def feed_back_body(grad_ref, weight_ref, gate_ref, up_ref, hidden_ref, acts_ref, out_ref, total):
    part = pl.program_id(0)
    grad_hidden = dot(grad_ref[...], weight_ref[0, 2], 1, 1)
    gate = gate_ref[0]
    sigma = jax.nn.sigmoid(gate)
    grad_gate = (grad_hidden * up_ref[0] * sigma * (1.0 + gate * (1.0 - sigma))).astype(LOW)
    grad_up = (grad_hidden * gate * sigma).astype(LOW)
    acts_ref[0, 0] = grad_gate
    acts_ref[0, 1] = grad_up
    acts_ref[0, 2] = hidden_ref[0]
    product = dot(grad_gate, weight_ref[0, 0], 1, 0) + dot(grad_up, weight_ref[0, 1], 1, 0)

    @pl.when(part == 0)
    def _():
        total[...] = product

    @pl.when(part > 0)
    def _():
        total[...] = total[...] + product

    @pl.when(part == pl.num_programs(0) - 1)
    def _():
        out_ref[...] = total[...].astype(LOW)


def feed_back(grad, weight, gate, up, hidden):
    parts, _, size, width = weight.shape
    sel = grad.shape[0]
    same = pl.BlockSpec((sel, width), lambda part: (0, 0))
    slab = pl.BlockSpec((1, sel, size), lambda part: (part, 0, 0))
    return pl.pallas_call(
        feed_back_body,
        grid=(parts,),
        in_specs=[same, pl.BlockSpec((1, 3, size, width), lambda part: (part, 0, 0, 0))]
        + [slab] * 3,
        out_specs=[pl.BlockSpec((1, 3, sel, size), lambda part: (part, 0, 0, 0)), same],
        out_shape=[struct((parts, 3, sel, size), LOW), struct((sel, width), LOW)],
        scratch_shapes=[pltpu.VMEM((sel, width), FULL)],
        compiler_params=pltpu.CompilerParams(vmem_limit_bytes=VMEM_BYTES),
        cost_estimate=pl.CostEstimate(
            flops=6 * sel * parts * size * width,
            bytes_accessed=weight.size * 2,
            transcendentals=0,
        ),
        name="feed_back",
    )(grad, weight, gate, up, hidden)


def newton_body(chunk, x_ref, out_ref, current, low, gram, rest_low):
    rows, width = current.shape
    parts = rows // chunk
    eye_rows = lax.broadcasted_iota(jnp.int32, (chunk, rows), 0)
    eye_columns = lax.broadcasted_iota(jnp.int32, (chunk, rows), 1)

    def strip(part):
        return pl.ds(pl.multiple_of(part * chunk, chunk), chunk)

    def eye(part):
        return eye_rows + part * chunk == eye_columns

    def over(function, start):
        return lax.fori_loop(0, parts, function, start)

    def square_sum(part, total):
        values = x_ref[0, strip(part), :]
        return total + jnp.sum(values * values)

    scale = 1.0 / (jnp.sqrt(over(square_sum, jnp.float32(0.0))) + 1e-07)

    def begin(part, carry):
        values = x_ref[0, strip(part), :] * scale
        current[strip(part), :] = values
        low[strip(part), :] = values.astype(LOW)
        return carry

    over(begin, 0)

    def iteration(turn, carry):
        def gram_rows(part, trace):
            rows_here = dot(low[strip(part), :], low[...], 1, 1)
            gram[strip(part), :] = rows_here
            return trace + jnp.sum(jnp.where(eye(part), rows_here, 0.0))

        middle = over(gram_rows, jnp.float32(0.0)) / rows

        def centre(part, carry):
            rest = gram[strip(part), :] - jnp.where(eye(part), middle, 0.0)
            rest_low[strip(part), :] = rest.astype(LOW)
            return carry

        over(centre, 0)

        def poly_rows(part, trace):
            square = dot(rest_low[strip(part), :], rest_low[...], 1, 0)
            rows_here = gram[strip(part), :]
            rest = rows_here - jnp.where(eye(part), middle, 0.0)
            square = square + 2.0 * middle * rest + jnp.where(eye(part), middle * middle, 0.0)
            rows_here = NEWTON_B * rows_here + NEWTON_C * square
            gram[strip(part), :] = rows_here
            return trace + jnp.sum(jnp.where(eye(part), rows_here, 0.0))

        second = over(poly_rows, jnp.float32(0.0)) / rows

        def centre_again(part, carry):
            rest = gram[strip(part), :] - jnp.where(eye(part), second, 0.0)
            rest_low[strip(part), :] = rest.astype(LOW)
            return carry

        over(centre_again, 0)

        def apply(part, carry):
            current[strip(part), :] = (NEWTON_A + second) * current[strip(part), :] + dot(
                rest_low[strip(part), :], low[...], 1, 0
            )
            return carry

        over(apply, 0)

        def lower(part, carry):
            low[strip(part), :] = current[strip(part), :].astype(LOW)
            return carry

        over(lower, 0)
        return carry

    lax.fori_loop(0, NS_STEPS, iteration, 0)
    out_ref[0] = low[...]


def newton(blocks):
    count, rows, width = blocks.shape
    chunk = next(size for size in (176, 128, 88, 64, rows) if rows % size == 0)
    spec = pl.BlockSpec((1, rows, width), lambda block: (block, 0, 0))
    return pl.pallas_call(
        functools.partial(newton_body, chunk),
        grid=(count,),
        in_specs=[spec],
        out_specs=spec,
        out_shape=struct(blocks.shape, LOW),
        scratch_shapes=[
            pltpu.VMEM((rows, width), FULL),
            pltpu.VMEM((rows, width), LOW),
            pltpu.VMEM((rows, rows), FULL),
            pltpu.VMEM((rows, rows), LOW),
        ],
        compiler_params=pltpu.CompilerParams(vmem_limit_bytes=VMEM_BYTES),
        cost_estimate=pl.CostEstimate(
            flops=NS_STEPS * count * (4 * rows * rows * width + 2 * rows * rows * rows),
            bytes_accessed=6 * blocks.size,
            transcendentals=0,
        ),
        name="newton",
    )(blocks)


def lookup_body(ids_ref, table_ref, out_ref, held, rows, sem):
    block = pl.program_id(0)
    vocab = table_ref.shape[0]

    @pl.when(block == 0)
    def _():
        load = pltpu.make_async_copy(table_ref, held.at[pl.ds(0, vocab)], sem)
        load.start()
        held[pl.ds(vocab, 8), :] = jnp.zeros((8, held.shape[1]), FULL)
        load.wait()

    def step(group, carry):
        for member in range(UNROLL):
            at = group * UNROLL + member
            spot = ids_ref[block * ROWS_IN_BLOCK + at]
            rows[pl.ds(at, 1), :] = held[pl.ds(spot, 1), :]
        return carry

    lax.fori_loop(0, ROWS_IN_BLOCK // UNROLL, step, 0)
    out_ref[...] = rows[...].astype(LOW)


def lookup(table, ids):
    vocab, columns = table.shape
    count = ids.shape[0]
    return pl.pallas_call(
        lookup_body,
        grid_spec=pltpu.PrefetchScalarGridSpec(
            num_scalar_prefetch=1,
            grid=(count // ROWS_IN_BLOCK,),
            in_specs=[pl.BlockSpec(memory_space=pl.ANY)],
            out_specs=pl.BlockSpec((ROWS_IN_BLOCK, columns), lambda block, ids_ref: (block, 0)),
            scratch_shapes=[
                pltpu.VMEM((vocab + 8, columns), FULL),
                pltpu.VMEM((ROWS_IN_BLOCK, columns), FULL),
                pltpu.SemaphoreType.DMA,
            ],
        ),
        out_shape=jax.ShapeDtypeStruct((count, columns), LOW),
        compiler_params=pltpu.CompilerParams(vmem_limit_bytes=VMEM_BYTES),
        cost_estimate=pl.CostEstimate(
            flops=0, bytes_accessed=vocab * columns * 4 + count * columns * 32, transcendentals=0
        ),
        name="lookup",
    )(ids, table)


def spread_body(ids_ref, rows_ref, head_ref, out_ref, square_ref, even, odd, rows, sem):
    block = pl.program_id(0)
    vocab = out_ref.shape[0]

    @pl.when(block == 0)
    def _():
        even[...] = jnp.zeros_like(even)
        odd[...] = jnp.zeros_like(odd)

    rows[...] = rows_ref[...].astype(FULL)

    def step(group, carry):
        for member in range(UNROLL):
            at = group * UNROLL + member
            spot = pl.ds(ids_ref[block * ROWS_IN_BLOCK + at], 1)
            total = even if member % 2 == 0 else odd
            total[spot, :] = total[spot, :] + rows[pl.ds(at, 1), :]
        return carry

    lax.fori_loop(0, ROWS_IN_BLOCK // UNROLL, step, 0)

    @pl.when(block == pl.num_programs(0) - 1)
    def _():
        chunk = 256

        def finish(part, squares):
            spot = pl.ds(pl.multiple_of(part * chunk, chunk), chunk)
            value = even[spot, :] + odd[spot, :] + head_ref[spot, :].astype(FULL)
            even[spot, :] = value
            return squares + jnp.sum((value * value).reshape(chunk // 8, 8, -1), axis=0)

        squares = lax.fori_loop(
            0, vocab // chunk, finish, jnp.zeros((8, even.shape[1]), FULL)
        )
        square_ref[...] = squares
        store = pltpu.make_async_copy(even.at[pl.ds(0, vocab)], out_ref, sem)
        store.start()
        store.wait()


def spread(ids, rows, head):
    vocab, columns = head.shape
    count = ids.shape[0]
    return pl.pallas_call(
        spread_body,
        grid_spec=pltpu.PrefetchScalarGridSpec(
            num_scalar_prefetch=1,
            grid=(count // ROWS_IN_BLOCK,),
            in_specs=[
                pl.BlockSpec((ROWS_IN_BLOCK, columns), lambda block, ids_ref: (block, 0)),
                pl.BlockSpec((vocab, columns), lambda block, ids_ref: (0, 0)),
            ],
            out_specs=[
                pl.BlockSpec(memory_space=pl.ANY),
                pl.BlockSpec((8, columns), lambda block, ids_ref: (0, 0)),
            ],
            scratch_shapes=[
                pltpu.VMEM((vocab + 8, columns), FULL),
                pltpu.VMEM((vocab + 8, columns), FULL),
                pltpu.VMEM((ROWS_IN_BLOCK, columns), FULL),
                pltpu.SemaphoreType.DMA,
            ],
        ),
        out_shape=[
            jax.ShapeDtypeStruct((vocab, columns), FULL),
            jax.ShapeDtypeStruct((8, columns), FULL),
        ],
        compiler_params=pltpu.CompilerParams(vmem_limit_bytes=VMEM_BYTES),
        cost_estimate=pl.CostEstimate(
            flops=count * columns, bytes_accessed=count * columns * 64, transcendentals=0
        ),
        name="spread",
    )(ids, rows, head)


def adamw(weight, first_m, second_m, grad, rate, decay):
    first_new = BETA_ONE * first_m + (1.0 - BETA_ONE) * grad
    second_new = BETA_TWO * second_m + (1.0 - BETA_TWO) * grad * grad
    update = (
        first_new
        / (1.0 - BETA_ONE**STEP)
        / (jnp.sqrt(second_new / (1.0 - BETA_TWO**STEP)) + ADAM_EPS)
    )
    return (weight * (1.0 - rate * decay) - rate * update, first_new, second_new)


def cut_columns(values, count):
    rows, columns = values.shape
    return jnp.moveaxis(values.reshape(rows, count, columns // count), 1, 0)


def side_by_side(parts):
    count, rows, columns = parts.shape
    return jnp.moveaxis(parts, 0, 1).reshape(rows, count * columns)


def swap_by_shifts(parts, axis):
    count = lax.axis_size(axis)
    me = lax.axis_index(axis)
    result = parts
    for step in range(1, count):
        pairs = [(source, (source + step) % count) for source in range(count)]
        part = lax.dynamic_index_in_dim(parts, lax.rem(me + step, count), 0, False)
        part = lax.ppermute(part, axis, pairs)
        result = lax.dynamic_update_index_in_dim(
            result, part, lax.rem(me - step + count, count), 0
        )
    return result


def per_device(
    tokens,
    picks,
    targets,
    lengths,
    skip,
    embed,
    embed_m,
    embed_v,
    attn_qo,
    attn_qo_mom,
    attn_kv,
    attn_kv_mom,
    ffn,
    ffn_mom,
    gains,
    gains_m,
    gains_v,
):
    wide_count = lax.axis_size("wide")
    narrow_count = lax.axis_size("narrow")
    narrow_spot = lax.axis_index("narrow")
    wide_spot = lax.axis_index("wide")
    seq_len = tokens.shape[1]
    sel = picks.shape[1]
    vocab_rows, columns = embed.shape
    width = columns * wide_count
    own_rows = sel // narrow_count
    tok_rows = seq_len // narrow_count
    all_rows = own_rows + tok_rows
    heads_own = HEADS // narrow_count
    head_cols = heads_own * HD
    repeat = max(1, narrow_count // KVH)
    groups = KVH * repeat // narrow_count
    ffn_rows = ffn.shape[0]
    ffn_size = ffn_rows // narrow_count
    total_rows = wide_count * sel
    lens = lengths[0]
    pick_ids = picks[0]
    keep_layer = (1 - skip[0]).astype(FULL)
    keep_row = jnp.full((1, width), keep_layer)
    lanes = 128

    def box(flat):
        height = -(-flat.shape[0] // (8 * lanes)) * 8
        return jnp.pad(flat, (0, height * lanes - flat.shape[0])).reshape(height, lanes)

    ffn_low = jnp.moveaxis(ffn, 1, 0).astype(LOW)
    ffn_cut = ffn_low.reshape(3, narrow_count, ffn_size, ffn_low.shape[2])
    ffn_sub = swap_by_shifts(jnp.moveaxis(ffn_cut, 1, 0), "narrow")
    proj_own = jnp.concatenate(
        [attn_qo.reshape(columns, -1), attn_kv.reshape(columns, -1)], axis=1
    ).astype(LOW)
    proj = lax.all_gather(
        lax.all_gather(proj_own, "narrow", axis=0), "wide", axis=1, tiled=True
    )
    ffn_sub = jnp.moveaxis(ffn_sub, 0, 2).reshape(3, ffn_size, width)
    ffn_w = lax.all_gather(ffn_sub, "wide", axis=0)

    where_at = jnp.arange(seq_len, dtype=jnp.int32)
    pick_tokens = jnp.sum(
        jnp.where(pick_ids[:, None] == where_at[None, :], tokens[0][None, :], 0), axis=1
    )
    ints = box(jnp.concatenate([tokens[0], pick_tokens, targets[0]]))
    all_ints, all_gains = launch(
        [gather_wide(ints), gather_both(box(gains.astype(LOW).astype(FULL).reshape(-1)))],
        0,
        "gather_ids",
    )
    gain_size = gains.shape[1]
    gain_w = all_gains.reshape(narrow_count, wide_count, -1)[:, :, : 3 * gain_size]
    gain_w = gain_w.reshape(narrow_count, wide_count, 3, gain_size)
    gain_w = jnp.transpose(gain_w, (2, 1, 0, 3)).reshape(3, width)
    all_ints = all_ints.reshape(wide_count, -1)
    tokens_all = all_ints[:, :seq_len].reshape(wide_count, narrow_count, tok_rows)
    picked_all = all_ints[:, seq_len : seq_len + sel].reshape(wide_count, narrow_count, own_rows)
    targets_all = all_ints[:, seq_len + sel : seq_len + 2 * sel].reshape(-1)
    wanted = jnp.moveaxis(jnp.concatenate([tokens_all, picked_all], axis=2), 1, 0).reshape(-1)
    local_ids = wanted - narrow_spot * vocab_rows
    inside = (local_ids >= 0) & (local_ids < vocab_rows)
    spots = jnp.where(inside, local_ids, vocab_rows)
    found = lookup(embed, spots).reshape(narrow_count, wide_count * all_rows, columns)
    embed_cut = embed.astype(LOW).reshape(wide_count, vocab_rows // wide_count, columns)
    rows_low, table_own = launch(
        [fetch_rows(found, all_rows), join_columns("wide", embed_cut)], 1, "fetch_rows"
    )

    mom_qo = jnp.moveaxis(attn_qo_mom, 1, 0)
    mom_kv = jnp.moveaxis(attn_kv_mom, 1, 0)
    mom_ffn = jnp.moveaxis(ffn_mom, 1, 0)
    slot_rows, slot_cols = mom_ffn.shape[1:]

    def pack_small(qo_part, kv_part):
        flat = jnp.concatenate([qo_part.reshape(-1), kv_part.reshape(-1)])
        return jnp.pad(flat, (0, slot_rows * slot_cols - flat.shape[0])).reshape(
            slot_rows, slot_cols
        )

    def unpack_small(box_values):
        lead = box_values.shape[:-2]
        flat = box_values.reshape(lead + (-1,))
        qo_size, kv_size = mom_qo.size, mom_kv.size
        return (
            flat[..., :qo_size].reshape(lead + mom_qo.shape),
            flat[..., qo_size : qo_size + kv_size].reshape(lead + mom_kv.shape),
        )

    mom_parts = [mom_ffn[0], mom_ffn[1], mom_ffn[2], pack_small(mom_qo, mom_kv)]
    mom_parts = mom_parts + [jnp.zeros_like(mom_parts[0])] * (narrow_count - 4)
    mom_parts = jnp.stack(mom_parts).astype(LOW)

    seg_all = segments_at(lens, where_at)
    tok_at = narrow_spot * tok_rows + jnp.arange(tok_rows, dtype=jnp.int32)
    own_at = lax.dynamic_slice_in_dim(pick_ids, narrow_spot * own_rows, own_rows, 0)
    _, cosine_all, sine_all = angles_at(lens, where_at)
    _, cosine_tok, sine_tok = angles_at(lens, tok_at)
    _, cosine_own, sine_own = angles_at(lens, own_at)
    seg_mine, cosine, sine = angles_at(lens, pick_ids)

    q_w, o_w = proj[:, :, :head_cols], proj[:, :, head_cols : 2 * head_cols]
    kv_size = attn_kv.shape[2]
    k_w = proj[:, :, 2 * head_cols : 2 * head_cols + kv_size]
    v_w = proj[:, :, 2 * head_cols + kv_size :]

    def each_owner(rows, weight):
        return jnp.einsum("td,ndf->ntf", rows, weight, preferred_element_type=FULL)

    def by_heads(parts):
        return jnp.moveaxis(parts, 0, 1).reshape(tok_rows, KVH, HD)

    rows_full = rows_low.astype(FULL)
    normed_all = norm_rows(rows_full, gain_w[0]).astype(LOW)
    normed_tok, normed_own = normed_all[:tok_rows], normed_all[tok_rows:]
    keys_part = by_heads(each_owner(normed_tok, k_w))
    keys_part = rotate(keys_part, cosine_tok[:, None], sine_tok[:, None]).astype(LOW)
    values_part = by_heads(each_owner(normed_tok, v_w)).astype(LOW)
    by_head = jnp.moveaxis(jnp.stack([keys_part, values_part]), 2, 0)
    by_head = jnp.repeat(by_head, repeat, axis=0)
    by_head = by_head.reshape(narrow_count, groups, 2, tok_rows, HD)
    queries_part = each_owner(normed_own, q_w).reshape(narrow_count, own_rows, heads_own, HD)
    queries_part = rotate(queries_part, cosine_own[:, None], sine_own[:, None])
    queries_part = queries_part.astype(LOW).reshape(narrow_count, own_rows, head_cols)
    own_head, queries, start_low, tok_cols, pick_cols = launch(
        [
            swap_blocks("narrow", by_head),
            swap_blocks("narrow", queries_part),
            gather_blocks("narrow", rows_low[tok_rows:]),
            split_columns("wide", normed_tok),
            split_columns("wide", normed_own),
        ],
        2,
        "trade_heads",
    )
    own_head = jnp.transpose(own_head, (2, 1, 0, 3, 4)).reshape(2, groups, seq_len, HD)
    keys, values = own_head[0], own_head[1]
    start_h = start_low.reshape(sel, width).astype(FULL)

    grouped = queries.reshape(sel, groups, heads_own // groups, HD)
    scale = HD ** (-0.5)
    scores = jnp.einsum("tkgd,ksd->kgts", grouped, keys, preferred_element_type=FULL) * scale
    allowed = (seg_mine[:, None] == seg_all[None, :]) & (pick_ids[:, None] >= where_at[None, :])
    scores = jnp.where(allowed, scores, MASKED)
    shifted_exp = jnp.exp(scores - jnp.max(scores, axis=-1, keepdims=True))
    probs = shifted_exp / jnp.sum(shifted_exp, axis=-1, keepdims=True)
    probs_low = probs.astype(LOW)
    mixed = jnp.einsum("kgts,ksd->tkgd", probs_low, values, preferred_element_type=FULL)
    mixed = mixed.reshape(sel, head_cols).astype(LOW)

    early_part = norm_rows(start_h, gain_w[2]).astype(LOW)
    mixed_all, early, mixed_wide = launch(
        [
            gather_blocks("narrow", mixed),
            gather_wide(early_part),
            gather_wide(mixed),
        ],
        3,
        "gather_mixed",
    )
    early = early.reshape(total_rows, width)

    def own(values_all):
        return lax.dynamic_slice_in_dim(values_all, narrow_spot * own_rows, own_rows, 0)

    start_own = own(start_h)
    middle_all = start_h + jnp.einsum(
        "ntf,ndf->td", mixed_all, o_w, preferred_element_type=FULL
    )
    middle = own(middle_all)
    inner = norm_rows(middle_all, gain_w[1]).astype(LOW)
    gate, up, hidden, fed = feed(inner, ffn_w)
    final_own, late_part, inner_all = launch(
        [settle(fed, middle, start_own, keep_row, gain_w[2:3]), gather_wide(inner)], 4, "settle"
    )
    inner_all = inner_all.reshape(total_rows, width)

    table_count = table_own.shape[0]
    local_target = targets_all - (narrow_spot * vocab_rows + wide_spot * table_count)
    has_target = local_target[:, None] == jnp.arange(table_count, dtype=jnp.int32)[None, :]
    counted = (targets_all >= 0).astype(FULL)
    loss_count = jnp.sum(counted)

    def exit_logits(features):
        logits = dot(features, table_own, 1, 1)
        peak = jnp.max(logits, axis=-1)
        total = jnp.sum(jnp.exp(logits - peak[:, None]), axis=-1)
        picked = jnp.sum(jnp.where(has_target, logits, 0.0), axis=-1)
        return logits, jnp.stack([peak, total, picked])

    half = slot_rows // 2
    late, mom_top = launch(
        [
            gather_wide(late_part.reshape(sel, width)),
            swap_blocks("narrow", mom_parts[:, :half]),
        ],
        5,
        "gather_late",
    )
    late = late.reshape(total_rows, width)
    early_logits, early_stats = exit_logits(early)
    late_logits, late_stats = exit_logits(late)
    stats = jnp.concatenate([early_stats, late_stats], axis=1).reshape(3, 8, -1)
    stats = launch([combine(stats, merge_stats)], 6, "combine_stats")[0].reshape(3, -1)
    log_norms = stats[0] + jnp.log(stats[1])
    losses = log_norms - stats[2]
    loss_sum = jnp.sum(
        counted * (EXIT_EARLY * losses[:total_rows] + EXIT_LAST * losses[total_rows:])
    )

    def exit_back(logits, log_norm, weight, features):
        grad_logits = (
            (jnp.exp(logits - log_norm[:, None]) - has_target.astype(FULL))
            * (weight * counted)[:, None]
        ).astype(LOW)
        return dot(grad_logits, table_own, 1, 0).astype(LOW), dot(grad_logits, features, 0, 0)

    late_back, late_head = exit_back(late_logits, log_norms[total_rows:], EXIT_LAST, late)
    early_back, early_head = exit_back(early_logits, log_norms[:total_rows], EXIT_EARLY, early)
    grad_late, mom_low = launch(
        [sum_wide(late_back), swap_blocks("narrow", mom_parts[:, half:])], 7, "sum_late"
    )
    mom_owned = jnp.concatenate([mom_top, mom_low], axis=1)
    grad_head = (early_head + late_head).astype(LOW)

    grad_final, gain_late, grad_out, grad_early = launch(
        [
            settle_back(
                grad_late.astype(LOW),
                final_own,
                jnp.zeros_like(final_own),
                keep_row,
                gain_w[2:3],
            ),
            sum_wide(early_back),
        ],
        8,
        "settle_late",
    )
    grad_layer = grad_final * keep_layer
    grad_out = grad_out.reshape(sel, width)
    acts, fed_back = feed_back(grad_out, ffn_w, gate, up, hidden)
    grad_mid, gain_mid, grad_branch, grad_early, out_all = launch(
        [
            settle_back(fed_back, middle, grad_layer, keep_row, gain_w[1:2]),
            sum_narrow(grad_early.astype(LOW)),
            gather_wide(grad_out),
        ],
        9,
        "settle_middle",
    )
    grad_branch = grad_branch.reshape(sel, width)
    out_all = out_all.reshape(total_rows, width)
    grad_start_exit, gain_early = norm_back(start_own, gain_w[2], grad_early)

    o_own = lax.dynamic_index_in_dim(o_w, narrow_spot, 0, False)
    grad_mixed = dot(grad_branch, o_own, 1, 0).astype(LOW)
    grouped_grad = grad_mixed.reshape(sel, groups, heads_own // groups, HD)
    grad_probs = jnp.einsum("tkgd,ksd->kgts", grouped_grad, values, preferred_element_type=FULL)
    grad_scores = (
        probs * (grad_probs - jnp.sum(probs * grad_probs, axis=-1, keepdims=True))
    ).astype(LOW)
    grad_queries = (
        jnp.einsum("kgts,ksd->tkgd", grad_scores, keys, preferred_element_type=FULL) * scale
    ).reshape(sel, heads_own, HD)
    grad_queries = (
        unrotate(grad_queries, cosine[:, None], sine[:, None])
        .reshape(sel, head_cols)
        .astype(LOW)
    )
    grad_keys = jnp.einsum("kgts,tkgd->ksd", grad_scores, grouped, preferred_element_type=FULL)
    grad_keys = unrotate(grad_keys * scale, cosine_all, sine_all).astype(LOW)
    grad_values = jnp.einsum(
        "kgts,tkgd->ksd", probs_low, grouped_grad, preferred_element_type=FULL
    ).astype(LOW)
    kv_parts = jnp.stack([grad_keys, grad_values]).reshape(
        2, groups, narrow_count, tok_rows, HD
    )
    kv_parts = jnp.transpose(kv_parts, (2, 1, 0, 3, 4))
    grad_kv, grad_q, acts, queries_wide, branch_cols = launch(
        [
            swap_blocks("narrow", kv_parts),
            swap_blocks("narrow", grad_queries.reshape(narrow_count, own_rows, head_cols)),
            swap_blocks("wide", acts),
            gather_wide(grad_queries),
            split_columns("wide", grad_branch),
        ],
        10,
        "trade_grads",
    )
    grad_kv = grad_kv.reshape(KVH, repeat, 2, tok_rows, HD)
    if repeat > 1:
        grad_kv = jnp.sum(grad_kv.astype(FULL), axis=1, keepdims=True).astype(LOW)
    grad_kv = grad_kv[:, 0]
    kv_rows = jnp.transpose(grad_kv, (1, 2, 0, 3)).reshape(2, tok_rows, narrow_count, kv_size)

    def from_owners(parts, weight):
        return jnp.einsum("tnf,ndf->td", parts, weight, preferred_element_type=FULL)

    grad_normed = jnp.concatenate(
        [
            from_owners(kv_rows[0], k_w) + from_owners(kv_rows[1], v_w),
            jnp.einsum("ntf,ndf->td", grad_q, q_w, preferred_element_type=FULL),
        ]
    )
    grad_rows, gain_attn = norm_back(rows_full, gain_w[0], grad_normed)
    grad_pass = grad_mid + grad_start_exit + grad_final * (1.0 - keep_layer)
    grad_rows = jnp.concatenate([grad_rows[:tok_rows], grad_rows[tok_rows:] + grad_pass])
    grad_kv_flat = kv_rows.reshape(2 * tok_rows, narrow_count * kv_size)
    grad_rows, head_cols_all, kv_wide = launch(
        [
            return_rows(grad_rows.astype(LOW)),
            split_columns("wide", grad_head),
            gather_wide(grad_kv_flat),
        ],
        11,
        "return_rows",
    )
    acts = jnp.moveaxis(acts, 1, 0).reshape(3, total_rows, ffn_size)
    acts = lax.all_gather(acts, "narrow", axis=2, tiled=True)
    summed_table, table_squares = spread(
        spots, grad_rows.reshape(-1, columns), head_cols_all.reshape(vocab_rows, columns)
    )

    kv_wide = kv_wide.reshape(wide_count, 2, tok_rows, narrow_count * kv_size)
    grad_kv_w = jnp.einsum(
        "wtc,wjtf->jcf", tok_cols, kv_wide, preferred_element_type=FULL
    )
    summed_kv = lax.psum_scatter(grad_kv_w, "narrow", scatter_dimension=2, tiled=True)
    pick_cols = lax.all_gather(pick_cols, "narrow", axis=1, tiled=True)
    summed_qo = jnp.stack(
        [
            jnp.einsum("wtc,wtf->cf", pick_cols, queries_wide, preferred_element_type=FULL),
            jnp.einsum("wtc,wtf->cf", branch_cols, mixed_wide, preferred_element_type=FULL),
        ]
    )

    def cols_own(values_all):
        size = width // narrow_count
        return lax.dynamic_slice_in_dim(values_all, narrow_spot * size, size, 1)

    rights = (inner_all, inner_all, out_all)
    summed_ffn = jnp.stack([dot(acts[j], cols_own(rights[j]), 0, 0) for j in range(3)])
    small_all = lax.all_gather(
        pack_small(summed_qo, summed_kv).astype(LOW), "narrow", axis=0
    )

    squares = (
        jnp.sum(summed_qo * summed_qo)
        + jnp.sum(summed_kv * summed_kv)
        + jnp.sum(summed_ffn * summed_ffn)
        + jnp.sum(table_squares)
    )
    sums = jnp.stack(
        [gain_attn, gain_mid[0], gain_early + gain_late[0], jnp.full((width,), squares)]
    )
    sums = launch([combine(sums.reshape(4, 8, -1), add_two)], 12, "combine_sums")[0]
    sums = sums.reshape(4, width)
    summed_gain = lax.dynamic_slice_in_dim(
        sums[:3], (wide_spot * narrow_count + narrow_spot) * gain_size, gain_size, 1
    )
    square_total = sums[3, 0] + jnp.sum(sums[:3] * sums[:3])
    grad_norm = jnp.sqrt(square_total) / loss_count
    factor = jnp.minimum(1.0, CLIP_NORM / (grad_norm + 1e-06)) / loss_count

    def whole_columns(parts):
        return jnp.moveaxis(parts, 0, 2).reshape(
            parts.shape[1], parts.shape[2], parts.shape[0] * parts.shape[3]
        )

    def ffn_owner():
        left = lax.dynamic_index_in_dim(acts, jnp.minimum(narrow_spot, 2), 0, False)
        right = jnp.where(narrow_spot == 2, out_all, inner_all)
        grad = dot(left, right, 0, 0)
        mom = side_by_side(mom_owned).astype(FULL)
        result = newton((MOMENTUM * mom + grad * factor)[None])[0]
        return cut_columns(result, narrow_count)

    def small_owner():
        mom_q, mom_k = unpack_small(mom_owned.astype(FULL))
        grad_q, grad_k = unpack_small(small_all.astype(FULL))
        results = [
            newton(whole_columns(MOMENTUM * mom + grad * factor))
            for mom, grad in ((mom_q, grad_q), (mom_k, grad_k))
        ]
        parts = [
            jnp.moveaxis(
                result.reshape(2, result.shape[1], narrow_count, -1), 2, 0
            ).reshape(narrow_count, -1)
            for result in results
        ]
        flat = jnp.concatenate(parts, axis=1)
        flat = jnp.pad(flat, ((0, 0), (0, slot_rows * slot_cols - flat.shape[1])))
        return flat.reshape(narrow_count, slot_rows, slot_cols)

    directions = lax.cond(narrow_spot == 3, small_owner, ffn_owner)
    directions = swap_by_shifts(directions, "narrow")
    dir_ffn = directions[:3].astype(FULL)
    dir_qo, dir_kv = unpack_small(directions[3].astype(FULL))

    embed_new, embed_m_new, embed_v_new = adamw(
        embed, embed_m, embed_v, summed_table * factor, RATE_ADAM, WEIGHT_DECAY
    )
    gains_new, gains_m_new, gains_v_new = adamw(
        gains, gains_m, gains_v, summed_gain * factor, RATE_GAIN, 0.0
    )

    def mom_next(mom, grad):
        return MOMENTUM * mom + jnp.moveaxis(grad * factor, 0, 1)

    shrink = 1.0 - RATE_MUON * WEIGHT_DECAY

    def weight_next(weight, direction):
        return weight * shrink - RATE_MUON * jnp.moveaxis(direction, 0, 1)

    return (
        loss_sum,
        loss_count,
        grad_norm,
        embed_new,
        embed_m_new,
        embed_v_new,
        weight_next(attn_qo, dir_qo),
        mom_next(attn_qo_mom, summed_qo),
        weight_next(attn_kv, dir_kv),
        mom_next(attn_kv_mom, summed_kv),
        weight_next(ffn, dir_ffn),
        mom_next(ffn_mom, summed_ffn),
        gains_new,
        gains_m_new,
        gains_v_new,
    )


def solution(mesh):
    by_pack = P("wide", None)
    table = P("narrow", "wide")
    layer = P("wide", None, "narrow")
    gain = P(None, ("wide", "narrow"))
    return jax.shard_map(
        per_device,
        mesh=mesh,
        in_specs=(by_pack,) * 4 + (P("wide"),) + (table,) * 3 + (layer,) * 6 + (gain,) * 3,
        out_specs=(P(),) * 3 + (table,) * 3 + (layer,) * 6 + (gain,) * 3,
        check_vma=False,
    )
```

```python
import functools

import jax
import jax.numpy as jnp
from jax import lax
from jax.experimental import pallas as pl
from jax.experimental.pallas import tpu as pltpu
from jax.sharding import PartitionSpec as P

HEADS = 16
HD = 128
KVH = 4
NS_STEPS = 5
STEP = 10


NORM_EPS = 1e-05
ROPE_BASE = 10000.0
EXIT_EARLY = 0.25
EXIT_LAST = 1.0
CLIP_NORM = 0.02
BETA_ONE = 0.9
BETA_TWO = 0.95
ADAM_EPS = 1e-08
RATE_ADAM = 0.02
RATE_GAIN = 0.3
RATE_MUON = 0.3
WEIGHT_DECAY = 0.1
MOMENTUM = 0.95
NEWTON_A = 3.4445
NEWTON_B = -4.775
NEWTON_C = 2.0315
MASKED = -1e30
LOW = jnp.bfloat16
FULL = jnp.float32
BOTH = ("wide", "narrow")
UNROLL = 16
VMEM_BYTES = 56 * 1024 * 1024


def dot(first, second, first_dim, second_dim):
    return lax.dot_general(
        first, second, (((first_dim,), (second_dim,)), ((), ())), preferred_element_type=FULL
    )


def norm_rows(values, gain_row):
    return (
        values * lax.rsqrt(jnp.mean(values * values, axis=-1, keepdims=True) + NORM_EPS) * gain_row
    )


def norm_back(values, gain_row, grad):
    output, pull = jax.vjp(norm_rows, values, gain_row)
    return pull(grad)


def segments_at(lens, where_at):
    ends = jnp.cumsum(lens)
    return jnp.sum((where_at[:, None] >= ends[None, :]).astype(jnp.int32), axis=1)


def angles_at(lens, where_at):
    segment = segments_at(lens, where_at)
    starts = jnp.cumsum(lens) - lens
    member = segment[:, None] == jnp.arange(lens.shape[0], dtype=jnp.int32)[None, :]
    begin = jnp.sum(jnp.where(member, starts[None, :], 0), axis=1)
    offset_pos = (where_at - begin).astype(FULL)
    inverse = ROPE_BASE ** (-2.0 * jnp.arange(HD // 2, dtype=FULL) / HD)
    angle = offset_pos[:, None] * inverse[None, :]
    return (segment, jnp.cos(angle), jnp.sin(angle))


def rotate(values, cosine, sine):
    half = values.shape[-1] // 2
    first, second = (values[..., :half], values[..., half:])
    return jnp.concatenate(
        [first * cosine - second * sine, second * cosine + first * sine], axis=-1
    )


def unrotate(values, cosine, sine):
    return rotate(values, cosine, -sine)


MESH = pl.DeviceIdType.MESH
ANY = pl.BlockSpec(memory_space=pl.ANY)
VMEM = pl.BlockSpec(memory_space=pltpu.VMEM)


def others(axis, count):
    me = lax.axis_index(axis)
    return [{axis: lax.rem(me + step, count)} for step in range(1, count)]


def push(source, target, send, receive, device):
    return pltpu.make_async_remote_copy(
        src_ref=source,
        dst_ref=target,
        send_sem=send,
        recv_sem=receive,
        device_id=device,
        device_id_type=MESH,
    )


def arrived(block, send, receive, device):
    push(block, block, send, receive, device).wait_recv()


def like(values):
    return jax.ShapeDtypeStruct(values.shape, values.dtype)


def struct(shape, dtype):
    return jax.ShapeDtypeStruct(shape, dtype)


def sems(*shape):
    return pltpu.SemaphoreType.DMA(shape)


class Task:
    def __init__(self, inputs, outputs, scratch, steps, place_in, place_out, axes):
        self.inputs, self.outputs, self.scratch, self.steps = inputs, outputs, scratch, steps
        self.place_in = [place_in] * len(inputs)
        self.place_out = [place_out] * len(outputs)
        self.axes = axes


def launch(tasks, ident, name):
    axes = sorted(set(axis for task in tasks for axis in task.axes))
    inputs = [a for task in tasks for a in task.inputs]
    outputs = [a for task in tasks for a in task.outputs]
    scratch = [a for task in tasks for a in task.scratch]

    def body(*refs):
        refs = list(refs)
        ins = refs[: len(inputs)]
        outs = refs[len(inputs) : len(inputs) + len(outputs)]
        extra = refs[len(inputs) + len(outputs) :]
        barrier = pltpu.get_barrier_semaphore()
        targets = [device for axis in axes for device in others(axis, lax.axis_size(axis))]
        for device in targets:
            pl.semaphore_signal(barrier, inc=1, device_id=device, device_id_type=MESH)
        pl.semaphore_wait(barrier, len(targets))
        live = []
        for task in tasks:
            counts = (len(task.inputs), len(task.outputs), len(task.scratch))
            live.append(task.steps(ins[: counts[0]], outs[: counts[1]], extra[: counts[2]]))
            ins, outs, extra = ins[counts[0] :], outs[counts[1] :], extra[counts[2] :]
        while live:
            live = [steps for steps in live if next(steps, 0) is None]

    size = sum(a.size * a.dtype.itemsize for a in list(inputs) + list(outputs))
    return pl.pallas_call(
        body,
        out_shape=outputs,
        in_specs=[place for task in tasks for place in task.place_in],
        out_specs=[place for task in tasks for place in task.place_out],
        scratch_shapes=scratch,
        compiler_params=pltpu.CompilerParams(
            collective_id=ident, has_side_effects=True, vmem_limit_bytes=VMEM_BYTES
        ),
        cost_estimate=pl.CostEstimate(flops=0, bytes_accessed=8 * size, transcendentals=0),
        name=name,
    )(*inputs)


def later(task, turns):
    begin = task.steps

    def steps(ins, outs, scratch):
        for turn in range(turns):
            yield
        yield from begin(ins, outs, scratch)

    task.steps = steps
    return task


def gather_wide(values):
    count = lax.axis_size("wide")
    chips = count // 2

    def steps(ins, outs, scratch):
        (x_ref,), (out_ref,), (send, receive, local) = ins, outs, scratch
        me = lax.axis_index("wide")
        mate = me + 1 - 2 * lax.rem(me, 2)
        peers = [lax.rem(me + 2 * step, count) for step in range(1, chips)] + [mate]
        first = []
        for step, peer in enumerate(peers):
            copy = push(x_ref, out_ref.at[me], send.at[step], receive.at[me], {"wide": peer})
            copy.start()
            first.append(copy)
        keep = pltpu.make_async_copy(x_ref, out_ref.at[me], local)
        keep.start()
        yield
        second = []
        for step in range(1, chips):
            source = lax.rem(me - 2 * step + count, count)
            block = out_ref.at[source]
            arrived(block, send.at[0], receive.at[source], {"wide": mate})
            copy = push(
                block, block, send.at[chips + step - 1], receive.at[source], {"wide": mate}
            )
            copy.start()
            second.append(copy)
        yield
        for step in range(chips):
            source = lax.rem(mate - 2 * step + count, count)
            arrived(out_ref.at[source], send.at[0], receive.at[source], {"wide": mate})
        for copy in first + second:
            copy.wait_send()
        keep.wait()

    shape = struct((count,) + values.shape, values.dtype)
    return Task(
        [values], [shape], [sems(count - 1), sems(count), sems()], steps, ANY, ANY, ["wide"]
    )


def trade(axis, values, source_of, target_of, shape):
    count = lax.axis_size(axis)

    def steps(ins, outs, scratch):
        (x_ref,), (out_ref,), (send, receive, local) = ins, outs, scratch
        me = lax.axis_index(axis)
        copies = []
        for step in range(1, count):
            peer = lax.rem(me + step, count)
            copy = push(
                source_of(x_ref, peer),
                target_of(out_ref, me),
                send.at[step - 1],
                receive.at[me],
                {axis: peer},
            )
            copy.start()
            copies.append(copy)
        keep = pltpu.make_async_copy(source_of(x_ref, me), target_of(out_ref, me), local)
        keep.start()
        yield
        yield
        for step in range(1, count):
            source = lax.rem(me - step + count, count)
            arrived(
                target_of(out_ref, source), send.at[0], receive.at[source], {axis: source}
            )
        for copy in copies:
            copy.wait_send()
        keep.wait()

    return Task(
        [values],
        [struct(shape, values.dtype)],
        [sems(count - 1), sems(count), sems()],
        steps,
        ANY,
        ANY,
        [axis],
    )


def block_at(ref, spot):
    return ref.at[spot]


def whole_at(ref, spot):
    return ref


def columns_of(size):
    def at(ref, spot):
        return ref.at[:, pl.ds(pl.multiple_of(spot * size, size), size)]

    return at


def turned(ref, spot):
    count = lax.axis_size("narrow")
    return ref.at[lax.rem(spot + count - lax.rem(lax.axis_index("wide"), 2), count)]


def swap_turned(values):
    return trade("narrow", values, turned, block_at, values.shape)


def send_owner(values):
    count = lax.axis_size("narrow")

    def steps(ins, outs, scratch):
        (x_ref,), (out_ref,), (send, receive, local) = ins, outs, scratch
        me = lax.axis_index("narrow")
        owner = lax.rem(3 + lax.rem(lax.axis_index("wide"), 2), count)
        keep = pltpu.make_async_copy(x_ref, out_ref.at[me], local)
        keep.start()

        def to_owner():
            return push(x_ref, out_ref.at[me], send.at[0], receive.at[me], {"narrow": owner})

        @pl.when(me != owner)
        def _():
            to_owner().start()

        yield
        yield

        @pl.when(me != owner)
        def _():
            to_owner().wait_send()

        @pl.when(me == owner)
        def _():
            for step in range(1, count):
                source = lax.rem(owner + step, count)
                arrived(out_ref.at[source], send.at[0], receive.at[source], {"narrow": source})

        keep.wait()

    return Task(
        [values],
        [struct((count,) + values.shape, values.dtype)],
        [sems(1), sems(count), sems()],
        steps,
        ANY,
        ANY,
        ["narrow"],
    )


def swap_blocks(axis, values):
    return trade(axis, values, block_at, block_at, values.shape)


def gather_blocks(axis, values):
    shape = (lax.axis_size(axis),) + values.shape
    return trade(axis, values, whole_at, block_at, shape)


def split_columns(axis, values):
    count = lax.axis_size(axis)
    rows, size = values.shape[0], values.shape[1] // count
    return trade(axis, values, columns_of(size), block_at, (count, rows, size))


def join_columns(axis, values):
    count, rows, size = values.shape
    return trade(axis, values, block_at, columns_of(size), (rows, count * size))


def collect(count, parts_ref, slots, send, receive):
    me = lax.axis_index("narrow")
    copies = []
    for step in range(1, count):
        peer = lax.rem(me + step, count)
        copy = push(
            parts_ref.at[peer],
            slots.at[me],
            send.at[step - 1],
            receive.at[me],
            {"narrow": peer},
        )
        copy.start()
        copies.append(copy)
    return copies


def collected(count, parts_ref, slots, send, receive):
    me = lax.axis_index("narrow")
    total = parts_ref[me].astype(FULL)
    for step in range(1, count):
        source = lax.rem(me - step + count, count)
        arrived(slots.at[source], send.at[0], receive.at[source], {"narrow": source})
        total = total + slots[source].astype(FULL)
    return total


def share(count, low, all_ref, send, receive):
    me = lax.axis_index("narrow")
    all_ref[me] = low
    copies = []
    for step in range(1, count):
        peer = lax.rem(me + step, count)
        copy = push(
            all_ref.at[me], all_ref.at[me], send.at[step - 1], receive.at[me], {"narrow": peer}
        )
        copy.start()
        copies.append(copy)
    return copies


def shared(count, all_ref, send, receive):
    me = lax.axis_index("narrow")
    for step in range(1, count):
        source = lax.rem(me - step + count, count)
        arrived(all_ref.at[source], send.at[0], receive.at[source], {"narrow": source})


def narrow_sems(count):
    return [sems(count - 1), sems(count)]


def settle(partial, base, other, keep_row, gain_row):
    count = lax.axis_size("narrow")
    rows, width = base.shape

    def steps(ins, outs, scratch):
        parts_ref, base_ref, other_ref, keep_ref, gain_ref = ins
        own_ref, all_ref = outs
        slots, send, receive, send_all, receive_all = scratch
        copies = collect(count, parts_ref, slots, send, receive)
        yield
        total = collected(count, parts_ref, slots, send, receive)
        total = jnp.where(keep_ref[...] > 0, total + base_ref[...], other_ref[...])
        own_ref[...] = total
        low = norm_rows(total, gain_ref[...]).astype(LOW)
        copies = copies + share(count, low, all_ref, send_all, receive_all)
        yield
        shared(count, all_ref, send_all, receive_all)
        for copy in copies:
            copy.wait_send()

    return Task(
        [partial.reshape(count, rows, width), base, other, keep_row, gain_row],
        [struct((rows, width), FULL), struct((count, rows, width), LOW)],
        [pltpu.VMEM((count, rows, width), partial.dtype)]
        + narrow_sems(count)
        + narrow_sems(count),
        steps,
        VMEM,
        VMEM,
        ["narrow"],
    )


def settle_back(partial, values, add, keep_row, gain_row):
    count = lax.axis_size("narrow")
    rows, width = values.shape

    def steps(ins, outs, scratch):
        parts_ref, values_ref, add_ref, keep_ref, gain_ref = ins
        own_ref, gain_grad_ref, all_ref = outs
        slots, send, receive, send_all, receive_all = scratch
        copies = collect(count, parts_ref, slots, send, receive)
        yield
        grad = collected(count, parts_ref, slots, send, receive)
        held = values_ref[...]
        root = lax.rsqrt(jnp.mean(held * held, axis=-1, keepdims=True) + NORM_EPS)
        scaled = gain_ref[...] * grad
        inner = jnp.mean(held * scaled, axis=-1, keepdims=True)
        own = add_ref[...] + root * scaled - held * (root * root * root * inner)
        gain_grad_ref[...] = jnp.sum(held * root * grad, axis=0, keepdims=True)
        own_ref[...] = own
        low = (own * keep_ref[...]).astype(LOW)
        copies = copies + share(count, low, all_ref, send_all, receive_all)
        yield
        shared(count, all_ref, send_all, receive_all)
        for copy in copies:
            copy.wait_send()

    return Task(
        [partial.reshape(count, rows, width), values, add, keep_row, gain_row],
        [
            struct((rows, width), FULL),
            struct((1, width), FULL),
            struct((count, rows, width), LOW),
        ],
        [pltpu.VMEM((count, rows, width), partial.dtype)]
        + narrow_sems(count)
        + narrow_sems(count),
        steps,
        VMEM,
        VMEM,
        ["narrow"],
    )


def sum_narrow(partial):
    count = lax.axis_size("narrow")
    rows, width = partial.shape[0] // count, partial.shape[1]

    def steps(ins, outs, scratch):
        (parts_ref,), (own_ref,), (slots, send, receive) = ins, outs, scratch
        copies = collect(count, parts_ref, slots, send, receive)
        yield
        yield
        own_ref[...] = collected(count, parts_ref, slots, send, receive)
        for copy in copies:
            copy.wait_send()

    return Task(
        [partial.reshape(count, rows, width)],
        [struct((rows, width), FULL)],
        [pltpu.VMEM((count, rows, width), partial.dtype)] + narrow_sems(count),
        steps,
        VMEM,
        VMEM,
        ["narrow"],
    )


def fetch_rows(found, rows):
    deep, wide = lax.axis_size("narrow"), lax.axis_size("wide")
    columns = found.shape[2]

    def steps(ins, outs, scratch):
        (found_ref,), (out_ref,) = ins, outs
        rightward, leftward, final = scratch[:3]
        send_right, receive_right, send_left, receive_left = scratch[3:7]
        send_wide, receive_wide, local = scratch[7:]
        spot = lax.axis_index("narrow")
        me = lax.axis_index("wide")

        def right_copy(part, source):
            return push(
                source,
                rightward.at[part],
                send_right.at[part],
                receive_right.at[part],
                {"narrow": lax.rem(spot + 1, deep)},
            )

        def left_copy(part, source):
            return push(
                source,
                leftward.at[part],
                send_left.at[part],
                receive_left.at[part],
                {"narrow": lax.rem(spot + deep - 1, deep)},
            )

        for step in range(deep - 1):
            right, left = deep - 1 - step, step

            @pl.when((spot == 0) & (right > 0))
            def _():
                right_copy(right, found_ref.at[right]).start()

            @pl.when((spot == deep - 1) & (left < deep - 1))
            def _():
                left_copy(left, found_ref.at[left]).start()

        yield
        for step in range(deep - 1):
            right, left = deep - 1 - step, step

            @pl.when((spot > 0) & (right > spot))
            def _():
                right_copy(right, rightward.at[right]).wait_recv()
                rightward[right] = rightward[right] + found_ref[right]
                right_copy(right, rightward.at[right]).start()

            @pl.when((spot < deep - 1) & (left < spot))
            def _():
                left_copy(left, leftward.at[left]).wait_recv()
                leftward[left] = leftward[left] + found_ref[left]
                left_copy(left, leftward.at[left]).start()

        final[...] = found_ref[spot]

        @pl.when(spot > 0)
        def _():
            right_copy(spot, rightward.at[spot]).wait_recv()
            final[...] = final[...] + rightward[spot]

        @pl.when(spot < deep - 1)
        def _():
            left_copy(spot, leftward.at[spot]).wait_recv()
            final[...] = final[...] + leftward[spot]

        def rows_for(device):
            return final.at[pl.ds(pl.multiple_of(device * rows, rows), rows)]

        def columns_from(device):
            return columns_of(columns)(out_ref, device)

        copies = []
        for step in range(1, wide):
            peer = lax.rem(me + step, wide)
            copy = push(
                rows_for(peer),
                columns_from(me),
                send_wide.at[step - 1],
                receive_wide.at[me],
                {"wide": peer},
            )
            copy.start()
            copies.append(copy)
        keep = pltpu.make_async_copy(rows_for(me), columns_from(me), local)
        keep.start()
        for step in range(1, wide):
            source = lax.rem(me - step + wide, wide)
            arrived(
                columns_from(source), send_wide.at[0], receive_wide.at[source], {"wide": source}
            )
        yield
        for copy in copies:
            copy.wait_send()
        keep.wait()
        for step in range(deep - 1):
            right, left = deep - 1 - step, step

            @pl.when(right > spot)
            def _():
                right_copy(right, found_ref.at[right]).wait_send()

            @pl.when(left < spot)
            def _():
                left_copy(left, found_ref.at[left]).wait_send()

    task = Task(
        [found],
        [struct((rows, wide * columns), found.dtype)],
        [pltpu.VMEM(found.shape, found.dtype)] * 2
        + [pltpu.VMEM(found.shape[1:], found.dtype)]
        + [sems(deep)] * 4
        + [sems(wide - 1), sems(wide), sems()],
        steps,
        VMEM,
        ANY,
        ["narrow", "wide"],
    )
    return task


def return_rows(rows):
    deep, wide = lax.axis_size("narrow"), lax.axis_size("wide")
    count, width = rows.shape
    columns = width // wide

    def steps(ins, outs, scratch):
        (rows_ref,), (out_ref,) = ins, outs
        send_right, send_left, receive_deep, send_wide, receive_wide, local = scratch
        spot = lax.axis_index("narrow")
        me = lax.axis_index("wide")
        part_of = functools.partial(columns_of(columns), rows_ref)

        def landing(device):
            return out_ref.at[spot, pl.ds(pl.multiple_of(device * count, count), count)]

        copies = []
        for step in range(1, wide):
            peer = lax.rem(me + step, wide)
            copy = push(
                part_of(peer),
                landing(me),
                send_wide.at[step - 1],
                receive_wide.at[me],
                {"wide": peer},
            )
            copy.start()
            copies.append(copy)
        keep = pltpu.make_async_copy(part_of(me), landing(me), local)
        keep.start()
        yield
        for step in range(1, wide):
            source = lax.rem(me - step + wide, wide)
            arrived(landing(source), send_wide.at[0], receive_wide.at[source], {"wide": source})
        keep.wait()

        def right_copy(part):
            return push(
                out_ref.at[part],
                out_ref.at[part],
                send_right.at[part],
                receive_deep.at[part],
                {"narrow": lax.rem(spot + 1, deep)},
            )

        def left_copy(part):
            return push(
                out_ref.at[part],
                out_ref.at[part],
                send_left.at[part],
                receive_deep.at[part],
                {"narrow": lax.rem(spot + deep - 1, deep)},
            )

        @pl.when(spot < deep - 1)
        def _():
            right_copy(spot).start()

        @pl.when(spot > 0)
        def _():
            left_copy(spot).start()

        for step in range(1, deep):
            yield

            @pl.when(spot >= step)
            def _():
                right_copy(spot - step).wait_recv()

                @pl.when(spot < deep - 1)
                def _():
                    right_copy(spot - step).start()

            @pl.when(spot + step < deep)
            def _():
                left_copy(spot + step).wait_recv()

                @pl.when(spot > 0)
                def _():
                    left_copy(spot + step).start()

        for part in range(deep):

            @pl.when((part <= spot) & (spot < deep - 1))
            def _():
                right_copy(part).wait_send()

            @pl.when((part >= spot) & (spot > 0))
            def _():
                left_copy(part).wait_send()

        for copy in copies:
            copy.wait_send()

    return Task(
        [rows],
        [struct((deep, wide * count, columns), rows.dtype)],
        [sems(deep)] * 3 + [sems(wide - 1), sems(wide), sems()],
        steps,
        ANY,
        ANY,
        ["narrow", "wide"],
    )


def sum_wide(partial):
    count = lax.axis_size("wide")
    chips = count // 2
    rows, width = partial.shape[0] // count, partial.shape[1]

    def steps(ins, outs, scratch):
        (parts_ref,), (out_ref,) = ins, outs
        from_mate, paired, slots, send_mate, receive_mate, send, receive = scratch
        me = lax.axis_index("wide")
        side = lax.rem(me, 2)
        mate = me + 1 - 2 * side
        my_chip = me // 2
        mate_copies = []
        for step in range(chips):
            chip = lax.rem(my_chip + 1 + step, chips)
            copy = push(
                parts_ref.at[2 * chip + 1 - side],
                from_mate.at[chip],
                send_mate.at[step],
                receive_mate.at[chip],
                {"wide": mate},
            )
            copy.start()
            mate_copies.append(copy)
        yield
        copies = []
        for step in range(chips):
            chip = lax.rem(my_chip + 1 + step, chips)
            arrived(from_mate.at[chip], send_mate.at[0], receive_mate.at[chip], {"wide": mate})
            both = parts_ref[2 * chip + side].astype(FULL) + from_mate[chip].astype(FULL)
            if step < chips - 1:
                paired[chip] = both.astype(LOW)
                copy = push(
                    paired.at[chip],
                    slots.at[my_chip],
                    send.at[step],
                    receive.at[my_chip],
                    {"wide": 2 * chip + side},
                )
                copy.start()
                copies.append(copy)
            else:
                out_ref[...] = both
        yield
        for step in range(1, chips):
            chip = lax.rem(my_chip - step + chips, chips)
            arrived(slots.at[chip], send.at[0], receive.at[chip], {"wide": 2 * chip + side})
            out_ref[...] = out_ref[...] + slots[chip].astype(FULL)
        for copy in mate_copies + copies:
            copy.wait_send()

    return Task(
        [partial.reshape(count, rows, width)],
        [struct((rows, width), FULL)],
        [pltpu.VMEM((chips, rows, width), LOW)] * 3
        + [sems(chips), sems(chips), sems(max(chips - 1, 1)), sems(chips)],
        steps,
        VMEM,
        VMEM,
        ["wide"],
    )


def merge_stats(first, second):
    peak = jnp.maximum(first[0:1], second[0:1])
    total = first[1:2] * jnp.exp(first[0:1] - peak) + second[1:2] * jnp.exp(second[0:1] - peak)
    return jnp.concatenate([peak, total, first[2:3] + second[2:3]], axis=0)


def add_two(first, second):
    return first + second


def combine(values, join):
    deep, wide = lax.axis_size("narrow"), lax.axis_size("wide")

    def steps(ins, outs, scratch):
        (x_ref,), (out_ref,) = ins, outs
        wide_slots, deep_slots, send_wide, receive_wide, send_deep, receive_deep = scratch

        def start(axis, count, slots, value, send, receive):
            me = lax.axis_index(axis)
            slots[me] = value
            copies = []
            for step in range(1, count):
                peer = lax.rem(me + step, count)
                copy = push(
                    slots.at[me], slots.at[me], send.at[step - 1], receive.at[me], {axis: peer}
                )
                copy.start()
                copies.append(copy)
            return copies

        def finish(axis, count, slots, send, receive):
            me = lax.axis_index(axis)
            for step in range(1, count):
                source = lax.rem(me - step + count, count)
                arrived(slots.at[source], send.at[0], receive.at[source], {axis: source})
            total = slots[0]
            for source in range(1, count):
                total = join(total, slots[source])
            return total

        first = start("wide", wide, wide_slots, x_ref[...], send_wide, receive_wide)
        yield
        total = finish("wide", wide, wide_slots, send_wide, receive_wide)
        second = start("narrow", deep, deep_slots, total, send_deep, receive_deep)
        yield
        out_ref[...] = finish("narrow", deep, deep_slots, send_deep, receive_deep)
        for copy in first + second:
            copy.wait_send()

    return Task(
        [values],
        [like(values)],
        [
            pltpu.VMEM((wide,) + values.shape, values.dtype),
            pltpu.VMEM((deep,) + values.shape, values.dtype),
            sems(wide - 1),
            sems(wide),
            sems(deep - 1),
            sems(deep),
        ],
        steps,
        VMEM,
        VMEM,
        ["narrow", "wide"],
    )


def gather_both(values):
    deep, wide = lax.axis_size("narrow"), lax.axis_size("wide")

    def steps(ins, outs, scratch):
        (x_ref,), (out_ref,) = ins, outs
        send_wide, receive_wide, send_deep, receive_deep = scratch
        me = lax.axis_index("wide")
        spot = lax.axis_index("narrow")
        out_ref[spot, me] = x_ref[...]
        copies = []
        for step in range(1, wide):
            peer = lax.rem(me + step, wide)
            block = out_ref.at[spot, me]
            copy = push(block, block, send_wide.at[step - 1], receive_wide.at[me], {"wide": peer})
            copy.start()
            copies.append(copy)
        yield
        for step in range(1, wide):
            source = lax.rem(me - step + wide, wide)
            block = out_ref.at[spot, source]
            arrived(block, send_wide.at[0], receive_wide.at[source], {"wide": source})
        for step in range(1, deep):
            peer = lax.rem(spot + step, deep)
            block = out_ref.at[spot]
            copy = push(
                block, block, send_deep.at[step - 1], receive_deep.at[spot], {"narrow": peer}
            )
            copy.start()
            copies.append(copy)
        yield
        for step in range(1, deep):
            source = lax.rem(spot - step + deep, deep)
            block = out_ref.at[source]
            arrived(block, send_deep.at[0], receive_deep.at[source], {"narrow": source})
        for copy in copies:
            copy.wait_send()

    return Task(
        [values],
        [struct((deep, wide) + values.shape, values.dtype)],
        [sems(wide - 1), sems(wide), sems(deep - 1), sems(deep)],
        steps,
        VMEM,
        VMEM,
        ["narrow", "wide"],
    )


def feed_body(inner_ref, weight_ref, gate_ref, up_ref, hidden_ref, out_ref, total):
    part = pl.program_id(0)
    inner = inner_ref[...]
    gate = dot(inner, weight_ref[0, 0], 1, 1)
    up = dot(inner, weight_ref[0, 1], 1, 1)
    hidden = (jax.nn.silu(gate) * up).astype(LOW)
    gate_ref[0] = gate
    up_ref[0] = up
    hidden_ref[0] = hidden
    product = dot(hidden, weight_ref[0, 2], 1, 0)

    @pl.when(part == 0)
    def _():
        total[...] = product

    @pl.when(part > 0)
    def _():
        total[...] = total[...] + product

    @pl.when(part == pl.num_programs(0) - 1)
    def _():
        out_ref[...] = total[...].astype(LOW)


def feed(inner, weight):
    parts, _, size, width = weight.shape
    sel = inner.shape[0]
    same = pl.BlockSpec((sel, width), lambda part: (0, 0))
    slab = pl.BlockSpec((1, sel, size), lambda part: (part, 0, 0))
    return pl.pallas_call(
        feed_body,
        grid=(parts,),
        in_specs=[same, pl.BlockSpec((1, 3, size, width), lambda part: (part, 0, 0, 0))],
        out_specs=[slab, slab, slab, same],
        out_shape=[
            struct((parts, sel, size), FULL),
            struct((parts, sel, size), FULL),
            struct((parts, sel, size), LOW),
            struct((sel, width), LOW),
        ],
        scratch_shapes=[pltpu.VMEM((sel, width), FULL)],
        compiler_params=pltpu.CompilerParams(vmem_limit_bytes=VMEM_BYTES),
        cost_estimate=pl.CostEstimate(
            flops=6 * sel * parts * size * width,
            bytes_accessed=weight.size * 2,
            transcendentals=0,
        ),
        name="feed",
    )(inner, weight)


def feed_back_body(grad_ref, weight_ref, gate_ref, up_ref, hidden_ref, acts_ref, out_ref, total):
    part = pl.program_id(0)
    grad_hidden = dot(grad_ref[...], weight_ref[0, 2], 1, 1)
    gate = gate_ref[0]
    sigma = jax.nn.sigmoid(gate)
    grad_gate = (grad_hidden * up_ref[0] * sigma * (1.0 + gate * (1.0 - sigma))).astype(LOW)
    grad_up = (grad_hidden * gate * sigma).astype(LOW)
    acts_ref[0, 0] = grad_gate
    acts_ref[0, 1] = grad_up
    acts_ref[0, 2] = hidden_ref[0]
    product = dot(grad_gate, weight_ref[0, 0], 1, 0) + dot(grad_up, weight_ref[0, 1], 1, 0)

    @pl.when(part == 0)
    def _():
        total[...] = product

    @pl.when(part > 0)
    def _():
        total[...] = total[...] + product

    @pl.when(part == pl.num_programs(0) - 1)
    def _():
        out_ref[...] = total[...].astype(LOW)


def feed_back(grad, weight, gate, up, hidden):
    parts, _, size, width = weight.shape
    sel = grad.shape[0]
    same = pl.BlockSpec((sel, width), lambda part: (0, 0))
    slab = pl.BlockSpec((1, sel, size), lambda part: (part, 0, 0))
    return pl.pallas_call(
        feed_back_body,
        grid=(parts,),
        in_specs=[same, pl.BlockSpec((1, 3, size, width), lambda part: (part, 0, 0, 0))]
        + [slab] * 3,
        out_specs=[pl.BlockSpec((1, 3, sel, size), lambda part: (part, 0, 0, 0)), same],
        out_shape=[struct((parts, 3, sel, size), LOW), struct((sel, width), LOW)],
        scratch_shapes=[pltpu.VMEM((sel, width), FULL)],
        compiler_params=pltpu.CompilerParams(vmem_limit_bytes=VMEM_BYTES),
        cost_estimate=pl.CostEstimate(
            flops=6 * sel * parts * size * width,
            bytes_accessed=weight.size * 2,
            transcendentals=0,
        ),
        name="feed_back",
    )(grad, weight, gate, up, hidden)


def newton_steps(current, low, gram, rest_low):
    rows, width = current.shape
    block = min(512, width)
    eye = lax.broadcasted_iota(jnp.int32, (rows, rows), 0) == lax.broadcasted_iota(
        jnp.int32, (rows, rows), 1
    )

    def strip(part):
        return pl.ds(pl.multiple_of(part * block, block), block)

    def over(function, start):
        return lax.fori_loop(0, width // block, function, start)

    def add_squares(part, total):
        values = current[:, strip(part)]
        return total + jnp.sum(values * values)

    scale = 1.0 / (jnp.sqrt(over(add_squares, jnp.float32(0.0))) + 1e-07)

    def begin(part, carry):
        values = current[:, strip(part)] * scale
        current[:, strip(part)] = values
        low[:, strip(part)] = values.astype(LOW)
        return carry

    over(begin, 0)

    def iteration(turn, carry):
        gram[...] = jnp.zeros_like(gram)

        def add_gram(part, carry):
            values = low[:, strip(part)]
            gram[...] = gram[...] + dot(values, values, 1, 1)
            return carry

        over(add_gram, 0)
        whole = gram[...]
        middle = jnp.sum(jnp.where(eye, whole, 0.0)) / rows
        rest_low[...] = (whole - jnp.where(eye, middle, 0.0)).astype(LOW)
        square = dot(rest_low[...], rest_low[...], 1, 0)
        whole = gram[...]
        rest = whole - jnp.where(eye, middle, 0.0)
        square = square + 2.0 * middle * rest + jnp.where(eye, middle * middle, 0.0)
        whole = NEWTON_B * whole + NEWTON_C * square
        second = jnp.sum(jnp.where(eye, whole, 0.0)) / rows
        rest_low[...] = (whole - jnp.where(eye, second, 0.0)).astype(LOW)

        def apply(part, carry):
            values = (NEWTON_A + second) * current[:, strip(part)] + dot(
                rest_low[...], low[:, strip(part)], 1, 0
            )
            current[:, strip(part)] = values
            low[:, strip(part)] = values.astype(LOW)
            return carry

        over(apply, 0)
        return carry

    lax.fori_loop(0, NS_STEPS, iteration, 0)


def newton_scratch(rows, width):
    return [
        pltpu.VMEM((rows, width), FULL),
        pltpu.VMEM((rows, width), LOW),
        pltpu.VMEM((rows, rows), FULL),
        pltpu.VMEM((rows, rows), LOW),
    ]


def newton_cost(count, rows, width):
    return pl.CostEstimate(
        flops=NS_STEPS * count * (4 * rows * rows * width + 2 * rows * rows * rows),
        bytes_accessed=6 * count * rows * width,
        transcendentals=0,
    )


def newton_small_body(x_ref, out_ref, current, low, gram, rest_low):
    current[...] = x_ref[0]
    newton_steps(current, low, gram, rest_low)
    out_ref[0] = low[...]


def newton_small(blocks):
    count, rows, width = blocks.shape
    spec = pl.BlockSpec((1, rows, width), lambda block: (block, 0, 0))
    return pl.pallas_call(
        newton_small_body,
        grid=(count,),
        in_specs=[spec],
        out_specs=spec,
        out_shape=struct(blocks.shape, LOW),
        scratch_shapes=newton_scratch(rows, width),
        compiler_params=pltpu.CompilerParams(vmem_limit_bytes=VMEM_BYTES),
        cost_estimate=newton_cost(count, rows, width),
        name="newton_small",
    )(blocks)


def newton_body(factor_ref, mom_ref, *refs):
    parts = mom_ref.shape[0]
    pieces, (out_ref, current, low, gram, rest_low) = refs[:parts], refs[parts:]
    me = lax.axis_index("narrow")
    columns = mom_ref.shape[2]
    rows = pieces[0].shape[0]
    for part in range(parts):
        current[:, part * columns : (part + 1) * columns] = MOMENTUM * mom_ref[part].astype(FULL)
    factor = factor_ref[0]
    for step, piece in enumerate(pieces):
        source = lax.rem(me - step + parts, parts)
        added = factor * piece[...].astype(FULL)
        if rows % 8 == 0:
            spot = pl.ds(pl.multiple_of(source * rows, 8), rows)
            current[spot, :] = current[spot, :] + added
            continue
        for at in range(parts):

            @pl.when(source == at)
            def _():
                spot = slice(at * rows, (at + 1) * rows)
                current[spot, :] = current[spot, :] + added

    newton_steps(current, low, gram, rest_low)
    for part in range(parts):
        out_ref[part] = low[:, part * columns : (part + 1) * columns]


def newton(factor, mom, pieces):
    parts, rows, columns = mom.shape
    width = parts * columns
    return pl.pallas_call(
        newton_body,
        in_specs=[pl.BlockSpec(memory_space=pltpu.SMEM), VMEM] + [VMEM] * parts,
        out_specs=VMEM,
        out_shape=struct(mom.shape, LOW),
        scratch_shapes=newton_scratch(rows, width),
        compiler_params=pltpu.CompilerParams(vmem_limit_bytes=VMEM_BYTES),
        cost_estimate=newton_cost(1, rows, width),
        name="newton",
    )(factor.reshape(1), mom, *pieces)


def lookup_body(ids_ref, table_ref, out_ref, low_ref, list_ref, held, rows, sem):
    vocab = table_ref.shape[0]
    count = out_ref.shape[0]
    load = pltpu.make_async_copy(table_ref, held, sem)
    load.start()
    rows[...] = jnp.zeros_like(rows)

    def note(group, found):
        for member in range(UNROLL):
            at = group * UNROLL + member
            list_ref[found] = at
            found = found + (ids_ref[at] < vocab).astype(jnp.int32)
        return found

    found = lax.fori_loop(0, count // UNROLL, note, jnp.int32(0))
    for member in range(UNROLL):
        list_ref[found + member] = count
    list_ref[count + UNROLL] = found
    load.wait()

    def step(group, carry):
        for member in range(UNROLL):
            at = list_ref[group * UNROLL + member]
            spot = jnp.minimum(ids_ref[jnp.minimum(at, count - 1)], vocab - 1)
            rows[pl.ds(at, 1), :] = held[pl.ds(spot, 1), :]
        return carry

    lax.fori_loop(0, (found + UNROLL - 1) // UNROLL, step, 0)
    out_ref[...] = rows[pl.ds(0, count), :].astype(LOW)
    low_ref[...] = held[...].astype(LOW)


def lookup(table, ids):
    vocab, columns = table.shape
    count = ids.shape[0]
    return pl.pallas_call(
        lookup_body,
        in_specs=[pl.BlockSpec(memory_space=pltpu.SMEM), ANY],
        out_specs=[VMEM, VMEM, pl.BlockSpec(memory_space=pltpu.SMEM)],
        scratch_shapes=[
            pltpu.VMEM((vocab, columns), FULL),
            pltpu.VMEM((count + 8, columns), FULL),
            pltpu.SemaphoreType.DMA,
        ],
        out_shape=[
            struct((count, columns), LOW),
            struct((vocab, columns), LOW),
            struct((count + 2 * UNROLL,), jnp.int32),
        ],
        compiler_params=pltpu.CompilerParams(vmem_limit_bytes=VMEM_BYTES),
        cost_estimate=pl.CostEstimate(
            flops=0, bytes_accessed=vocab * columns * 4 + count * columns * 24, transcendentals=0
        ),
        name="lookup",
    )(ids, table)


def spread_body(
    ids_ref, list_ref, rows_ref, head_ref, out_ref, square_ref, even, odd, rows, sem
):
    vocab = out_ref.shape[0]
    count = rows_ref.shape[0]
    chunk = 256

    def strip(part):
        return pl.ds(pl.multiple_of(part * chunk, chunk), chunk)

    def begin(part, carry):
        even[strip(part), :] = head_ref[strip(part), :].astype(FULL)
        odd[strip(part), :] = jnp.zeros((chunk, odd.shape[1]), FULL)
        return carry

    lax.fori_loop(0, vocab // chunk, begin, 0)

    def widen(part, carry):
        rows[strip(part), :] = rows_ref[strip(part), :].astype(FULL)
        return carry

    lax.fori_loop(0, count // chunk, widen, 0)
    rows[pl.ds(count, 8), :] = jnp.zeros((8, rows.shape[1]), FULL)

    def step(group, carry):
        for member in range(UNROLL):
            at = list_ref[group * UNROLL + member]
            spot = jnp.minimum(ids_ref[jnp.minimum(at, count - 1)], vocab - 1)
            total = even if member % 2 == 0 else odd
            total[pl.ds(spot, 1), :] = total[pl.ds(spot, 1), :] + rows[pl.ds(at, 1), :]
        return carry

    found = list_ref[count + UNROLL]
    lax.fori_loop(0, (found + UNROLL - 1) // UNROLL, step, 0)

    def finish(part, squares):
        value = even[strip(part), :] + odd[strip(part), :]
        even[strip(part), :] = value
        return squares + jnp.sum((value * value).reshape(chunk // 8, 8, -1), axis=0)

    square_ref[...] = lax.fori_loop(
        0, vocab // chunk, finish, jnp.zeros((8, even.shape[1]), FULL)
    )
    store = pltpu.make_async_copy(even, out_ref, sem)
    store.start()
    store.wait()


def spread(ids, listed, rows, head):
    vocab, columns = head.shape
    count = ids.shape[0]
    smem = pl.BlockSpec(memory_space=pltpu.SMEM)
    return pl.pallas_call(
        spread_body,
        in_specs=[smem, smem, VMEM, VMEM],
        out_specs=[ANY, VMEM],
        scratch_shapes=[
            pltpu.VMEM((vocab, columns), FULL),
            pltpu.VMEM((vocab, columns), FULL),
            pltpu.VMEM((count + 8, columns), FULL),
            pltpu.SemaphoreType.DMA,
        ],
        out_shape=[struct((vocab, columns), FULL), struct((8, columns), FULL)],
        compiler_params=pltpu.CompilerParams(vmem_limit_bytes=VMEM_BYTES),
        cost_estimate=pl.CostEstimate(
            flops=count * columns, bytes_accessed=count * columns * 48, transcendentals=0
        ),
        name="spread",
    )(ids, listed, rows, head)


def adamw(weight, first_m, second_m, grad, rate, decay):
    first_new = BETA_ONE * first_m + (1.0 - BETA_ONE) * grad
    second_new = BETA_TWO * second_m + (1.0 - BETA_TWO) * grad * grad
    update = (
        first_new
        / (1.0 - BETA_ONE**STEP)
        / (jnp.sqrt(second_new / (1.0 - BETA_TWO**STEP)) + ADAM_EPS)
    )
    return (weight * (1.0 - rate * decay) - rate * update, first_new, second_new)


def cut_columns(values, count):
    rows, columns = values.shape
    return jnp.moveaxis(values.reshape(rows, count, columns // count), 1, 0)


def shifted(parts, axis, step):
    count = lax.axis_size(axis)
    pairs = [(source, (source + step) % count) for source in range(count)]
    return lax.ppermute(parts, axis, pairs)


def per_device(
    tokens,
    picks,
    targets,
    lengths,
    skip,
    embed,
    embed_m,
    embed_v,
    attn_qo,
    attn_qo_mom,
    attn_kv,
    attn_kv_mom,
    ffn,
    ffn_mom,
    gains,
    gains_m,
    gains_v,
):
    wide_count = lax.axis_size("wide")
    narrow_count = lax.axis_size("narrow")
    narrow_spot = lax.axis_index("narrow")
    wide_spot = lax.axis_index("wide")
    seq_len = tokens.shape[1]
    sel = picks.shape[1]
    vocab_rows, columns = embed.shape
    width = columns * wide_count
    own_rows = sel // narrow_count
    tok_rows = seq_len // narrow_count
    all_rows = own_rows + tok_rows
    heads_own = HEADS // narrow_count
    head_cols = heads_own * HD
    repeat = max(1, narrow_count // KVH)
    groups = KVH * repeat // narrow_count
    ffn_rows = ffn.shape[0]
    ffn_size = ffn_rows // narrow_count
    total_rows = wide_count * sel
    lens = lengths[0]
    pick_ids = picks[0]
    keep_layer = (1 - skip[0]).astype(FULL)
    keep_row = jnp.full((1, width), keep_layer)
    lanes = 128

    def box(flat):
        height = -(-flat.shape[0] // (8 * lanes)) * 8
        return jnp.pad(flat, (0, height * lanes - flat.shape[0])).reshape(height, lanes)

    ffn_low = jnp.moveaxis(ffn, 1, 0).astype(LOW)
    ffn_cut = ffn_low.reshape(3, narrow_count, ffn_size, ffn_low.shape[2])
    ffn_cut = jnp.moveaxis(ffn_cut, 1, 0).reshape(narrow_count, 3 * ffn_size, -1)
    proj_own = jnp.concatenate(
        [attn_qo.reshape(columns, -1), attn_kv.reshape(columns, -1)], axis=1
    ).astype(LOW)
    proj_part = lax.all_gather(proj_own, "narrow", axis=0)

    where_at = jnp.arange(seq_len, dtype=jnp.int32)
    pick_tokens = jnp.sum(
        jnp.where(pick_ids[:, None] == where_at[None, :], tokens[0][None, :], 0), axis=1
    )
    ints = box(jnp.concatenate([tokens[0], pick_tokens, targets[0]]))
    all_ints, all_gains = launch(
        [gather_wide(ints), gather_both(box(gains.astype(LOW).astype(FULL).reshape(-1)))],
        0,
        "gather_ids",
    )
    gain_size = gains.shape[1]
    gain_w = all_gains.reshape(narrow_count, wide_count, -1)[:, :, : 3 * gain_size]
    gain_w = gain_w.reshape(narrow_count, wide_count, 3, gain_size)
    gain_w = jnp.transpose(gain_w, (2, 1, 0, 3)).reshape(3, width)
    all_ints = all_ints.reshape(wide_count, -1)
    tokens_all = all_ints[:, :seq_len].reshape(wide_count, narrow_count, tok_rows)
    picked_all = all_ints[:, seq_len : seq_len + sel].reshape(wide_count, narrow_count, own_rows)
    targets_all = all_ints[:, seq_len + sel : seq_len + 2 * sel].reshape(-1)
    wanted = jnp.moveaxis(jnp.concatenate([tokens_all, picked_all], axis=2), 1, 0).reshape(-1)
    local_ids = wanted - narrow_spot * vocab_rows
    inside = (local_ids >= 0) & (local_ids < vocab_rows)
    spots = jnp.where(inside, local_ids, vocab_rows)
    found, embed_low, listed = lookup(embed, spots)
    proj_part, found = lax.optimization_barrier((proj_part, found))
    proj = lax.all_gather(proj_part, "wide", axis=1, tiled=True)
    found = found.reshape(narrow_count, wide_count * all_rows, columns)
    embed_cut = embed_low.reshape(wide_count, vocab_rows // wide_count, columns)
    rows_low, ffn_sub, table_own = launch(
        [
            fetch_rows(found, all_rows),
            join_columns("narrow", ffn_cut),
            join_columns("wide", embed_cut),
        ],
        1,
        "fetch_rows",
    )
    ffn_w = lax.all_gather(ffn_sub.reshape(3, ffn_size, width), "wide", axis=0)

    mom_qo = jnp.moveaxis(attn_qo_mom, 1, 0)
    mom_kv = jnp.moveaxis(attn_kv_mom, 1, 0)
    mom_ffn = jnp.moveaxis(ffn_mom, 1, 0)
    slot_rows, slot_cols = mom_ffn.shape[1:]

    def pack_small(qo_part, kv_part):
        flat = jnp.concatenate([qo_part.reshape(-1), kv_part.reshape(-1)])
        return jnp.pad(flat, (0, slot_rows * slot_cols - flat.shape[0])).reshape(
            slot_rows, slot_cols
        )

    def unpack_small(box_values):
        lead = box_values.shape[:-2]
        flat = box_values.reshape(lead + (-1,))
        qo_size, kv_size = mom_qo.size, mom_kv.size
        return (
            flat[..., :qo_size].reshape(lead + mom_qo.shape),
            flat[..., qo_size : qo_size + kv_size].reshape(lead + mom_kv.shape),
        )

    mom_parts = [mom_ffn[0], mom_ffn[1], mom_ffn[2], pack_small(mom_qo, mom_kv)]
    mom_parts = mom_parts + [jnp.zeros_like(mom_parts[0])] * (narrow_count - 4)
    mom_parts = jnp.stack(mom_parts).astype(LOW)

    seg_all = segments_at(lens, where_at)
    tok_at = narrow_spot * tok_rows + jnp.arange(tok_rows, dtype=jnp.int32)
    own_at = lax.dynamic_slice_in_dim(pick_ids, narrow_spot * own_rows, own_rows, 0)
    _, cosine_all, sine_all = angles_at(lens, where_at)
    _, cosine_tok, sine_tok = angles_at(lens, tok_at)
    _, cosine_own, sine_own = angles_at(lens, own_at)
    seg_mine, cosine, sine = angles_at(lens, pick_ids)

    q_w, o_w = proj[:, :, :head_cols], proj[:, :, head_cols : 2 * head_cols]
    kv_size = attn_kv.shape[2]
    k_w = proj[:, :, 2 * head_cols : 2 * head_cols + kv_size]
    v_w = proj[:, :, 2 * head_cols + kv_size :]

    def each_owner(rows, weight):
        return jnp.einsum("td,ndf->ntf", rows, weight, preferred_element_type=FULL)

    def by_heads(parts):
        return jnp.moveaxis(parts, 0, 1).reshape(tok_rows, KVH, HD)

    rows_full = rows_low.astype(FULL)
    normed_all = norm_rows(rows_full, gain_w[0]).astype(LOW)
    normed_tok, normed_own = normed_all[:tok_rows], normed_all[tok_rows:]
    keys_part = by_heads(each_owner(normed_tok, k_w))
    keys_part = rotate(keys_part, cosine_tok[:, None], sine_tok[:, None]).astype(LOW)
    values_part = by_heads(each_owner(normed_tok, v_w)).astype(LOW)
    by_head = jnp.moveaxis(jnp.stack([keys_part, values_part]), 2, 0)
    by_head = jnp.repeat(by_head, repeat, axis=0)
    by_head = by_head.reshape(narrow_count, groups, 2, tok_rows, HD)
    queries_part = each_owner(normed_own, q_w).reshape(narrow_count, own_rows, heads_own, HD)
    queries_part = rotate(queries_part, cosine_own[:, None], sine_own[:, None])
    queries_part = queries_part.astype(LOW).reshape(narrow_count, own_rows, head_cols)
    own_head, queries, start_low = launch(
        [
            swap_blocks("narrow", by_head),
            swap_blocks("narrow", queries_part),
            gather_blocks("narrow", rows_low[tok_rows:]),
        ],
        2,
        "trade_heads",
    )
    own_head = jnp.transpose(own_head, (2, 1, 0, 3, 4)).reshape(2, groups, seq_len, HD)
    keys, values = own_head[0], own_head[1]
    start_h = start_low.reshape(sel, width).astype(FULL)

    grouped = queries.reshape(sel, groups, heads_own // groups, HD)
    scale = HD ** (-0.5)
    scores = jnp.einsum("tkgd,ksd->kgts", grouped, keys, preferred_element_type=FULL) * scale
    allowed = (seg_mine[:, None] == seg_all[None, :]) & (pick_ids[:, None] >= where_at[None, :])
    scores = jnp.where(allowed, scores, MASKED)
    shifted_exp = jnp.exp(scores - jnp.max(scores, axis=-1, keepdims=True))
    probs = shifted_exp / jnp.sum(shifted_exp, axis=-1, keepdims=True)
    probs_low = probs.astype(LOW)
    mixed = jnp.einsum("kgts,ksd->tkgd", probs_low, values, preferred_element_type=FULL)
    mixed = mixed.reshape(sel, head_cols).astype(LOW)

    early_part = norm_rows(start_h, gain_w[2]).astype(LOW)
    mixed_all, early, mixed_wide = launch(
        [
            gather_blocks("narrow", mixed),
            gather_wide(early_part),
            gather_wide(mixed),
        ],
        3,
        "gather_mixed",
    )
    early = early.reshape(total_rows, width)

    def own(values_all):
        return lax.dynamic_slice_in_dim(values_all, narrow_spot * own_rows, own_rows, 0)

    start_own = own(start_h)
    middle_all = start_h + jnp.einsum(
        "ntf,ndf->td", mixed_all, o_w, preferred_element_type=FULL
    )
    middle = own(middle_all)
    inner = norm_rows(middle_all, gain_w[1]).astype(LOW)
    gate, up, hidden, fed = feed(inner, ffn_w)
    final_own, late_part, inner_all = launch(
        [settle(fed, middle, start_own, keep_row, gain_w[2:3]), gather_wide(inner)], 4, "settle"
    )
    inner_all = inner_all.reshape(total_rows, width)

    table_count = table_own.shape[0]
    local_target = targets_all - (narrow_spot * vocab_rows + wide_spot * table_count)
    has_target = local_target[:, None] == jnp.arange(table_count, dtype=jnp.int32)[None, :]
    counted = (targets_all >= 0).astype(FULL)
    loss_count = jnp.sum(counted)

    def exit_logits(features):
        logits = dot(features, table_own, 1, 1)
        peak = jnp.max(logits, axis=-1)
        total = jnp.sum(jnp.exp(logits - peak[:, None]), axis=-1)
        picked = jnp.sum(jnp.where(has_target, logits, 0.0), axis=-1)
        return logits, jnp.stack([peak, total, picked])

    half = slot_rows // 2
    late, mom_top = launch(
        [
            gather_wide(late_part.reshape(sel, width)),
            swap_turned(mom_parts[:, :half]),
        ],
        5,
        "gather_late",
    )
    late = late.reshape(total_rows, width)
    early_logits, early_stats = exit_logits(early)
    late_logits, late_stats = exit_logits(late)
    stats = jnp.concatenate([early_stats, late_stats], axis=1).reshape(3, 8, -1)
    normed_picks = norm_rows(start_h, gain_w[0]).astype(LOW)
    stats, tok_cols, pick_cols = launch(
        [
            combine(stats, merge_stats),
            split_columns("wide", normed_tok),
            split_columns("wide", normed_picks),
        ],
        6,
        "combine_stats",
    )
    stats = stats.reshape(3, -1)
    log_norms = stats[0] + jnp.log(stats[1])
    losses = log_norms - stats[2]
    loss_sum = jnp.sum(
        counted * (EXIT_EARLY * losses[:total_rows] + EXIT_LAST * losses[total_rows:])
    )

    def exit_back(logits, log_norm, weight, features):
        grad_logits = (
            (jnp.exp(logits - log_norm[:, None]) - has_target.astype(FULL))
            * (weight * counted)[:, None]
        ).astype(LOW)
        return dot(grad_logits, table_own, 1, 0).astype(LOW), dot(grad_logits, features, 0, 0)

    late_back, late_head = exit_back(late_logits, log_norms[total_rows:], EXIT_LAST, late)
    early_back, early_head = exit_back(early_logits, log_norms[:total_rows], EXIT_EARLY, early)
    grad_late, mom_low = launch(
        [sum_wide(late_back), swap_turned(mom_parts[:, half:])], 7, "sum_late"
    )
    mom_owned = jnp.concatenate([mom_top, mom_low], axis=1)
    grad_head = (early_head + late_head).astype(LOW)

    grad_early, grad_final, gain_late, grad_out = launch(
        [
            sum_wide(early_back),
            settle_back(
                grad_late.astype(LOW),
                final_own,
                jnp.zeros_like(final_own),
                keep_row,
                gain_w[2:3],
            ),
        ],
        8,
        "settle_late",
    )
    grad_layer = grad_final * keep_layer
    grad_out = grad_out.reshape(sel, width)
    acts, fed_back = feed_back(grad_out, ffn_w, gate, up, hidden)
    grad_mid, gain_mid, grad_branch, out_all = launch(
        [
            settle_back(fed_back, middle, grad_layer, keep_row, gain_w[1:2]),
            gather_wide(grad_out),
        ],
        9,
        "settle_middle",
    )
    grad_branch = grad_branch.reshape(sel, width)
    out_all = out_all.reshape(total_rows, width)

    o_own = lax.dynamic_slice(proj, (narrow_spot, 0, head_cols), (1, width, head_cols))[0]
    grad_mixed = dot(grad_branch, o_own, 1, 0).astype(LOW)
    grouped_grad = grad_mixed.reshape(sel, groups, heads_own // groups, HD)
    grad_probs = jnp.einsum("tkgd,ksd->kgts", grouped_grad, values, preferred_element_type=FULL)
    grad_scores = (
        probs * (grad_probs - jnp.sum(probs * grad_probs, axis=-1, keepdims=True))
    ).astype(LOW)
    grad_queries = (
        jnp.einsum("kgts,ksd->tkgd", grad_scores, keys, preferred_element_type=FULL) * scale
    ).reshape(sel, heads_own, HD)
    grad_queries = (
        unrotate(grad_queries, cosine[:, None], sine[:, None])
        .reshape(sel, head_cols)
        .astype(LOW)
    )
    grad_keys = jnp.einsum("kgts,tkgd->ksd", grad_scores, grouped, preferred_element_type=FULL)
    grad_keys = unrotate(grad_keys * scale, cosine_all, sine_all).astype(LOW)
    grad_values = jnp.einsum(
        "kgts,tkgd->ksd", probs_low, grouped_grad, preferred_element_type=FULL
    ).astype(LOW)
    kv_parts = jnp.stack([grad_keys, grad_values]).reshape(
        2, groups, narrow_count, tok_rows, HD
    )
    kv_parts = jnp.transpose(kv_parts, (2, 1, 0, 3, 4))
    grad_kv, grad_q, grad_early, acts, queries_wide, branch_cols = launch(
        [
            swap_blocks("narrow", kv_parts),
            swap_blocks("narrow", grad_queries.reshape(narrow_count, own_rows, head_cols)),
            sum_narrow(grad_early.astype(LOW)),
            swap_blocks("wide", acts),
            gather_wide(grad_queries),
            split_columns("wide", grad_branch),
        ],
        10,
        "trade_grads",
    )
    grad_start_exit, gain_early = norm_back(start_own, gain_w[2], grad_early)
    grad_kv = grad_kv.reshape(KVH, repeat, 2, tok_rows, HD)
    if repeat > 1:
        grad_kv = jnp.sum(grad_kv.astype(FULL), axis=1, keepdims=True).astype(LOW)
    grad_kv = grad_kv[:, 0]
    kv_rows = jnp.transpose(grad_kv, (1, 2, 0, 3)).reshape(2, tok_rows, narrow_count, kv_size)

    def from_owners(parts, weight):
        return jnp.einsum("tnf,ndf->td", parts, weight, preferred_element_type=FULL)

    grad_normed = jnp.concatenate(
        [
            from_owners(kv_rows[0], k_w) + from_owners(kv_rows[1], v_w),
            jnp.einsum("ntf,ndf->td", grad_q, q_w, preferred_element_type=FULL),
        ]
    )
    grad_rows, gain_attn = norm_back(rows_full, gain_w[0], grad_normed)
    grad_pass = grad_mid + grad_start_exit + grad_final * (1.0 - keep_layer)
    grad_rows = jnp.concatenate([grad_rows[:tok_rows], grad_rows[tok_rows:] + grad_pass])
    grad_kv_flat = kv_rows.reshape(2 * tok_rows, narrow_count * kv_size)
    grad_rows, head_cols_all, kv_wide = launch(
        [
            return_rows(grad_rows.astype(LOW)),
            later(split_columns("wide", grad_head), 2),
            later(gather_wide(grad_kv_flat), 2),
        ],
        11,
        "return_rows",
    )
    acts = jnp.moveaxis(acts, 1, 0).reshape(3, total_rows, ffn_size)
    rights = (inner_all, inner_all, out_all)
    grad_ffn = [dot(acts[j], rights[j], 0, 0) for j in range(3)]
    ffn_squares = sum(jnp.sum(part * part) for part in grad_ffn)
    summed_qo = jnp.stack(
        [
            jnp.einsum("wtc,wtf->cf", pick_cols, queries_wide, preferred_element_type=FULL),
            jnp.einsum("wtc,wtf->cf", branch_cols, mixed_wide, preferred_element_type=FULL),
        ]
    )
    qo_flat = summed_qo.astype(LOW).reshape(-1)
    qo_flat = jnp.pad(qo_flat, (0, ffn_size * width - qo_flat.shape[0]))
    for_owners = jnp.stack(
        [part.astype(LOW) for part in grad_ffn] + [qo_flat.reshape(ffn_size, width)]
    )
    for_owners, grad_rows = lax.optimization_barrier((for_owners, grad_rows))
    turn = lax.rem(wide_spot, 2)

    def for_device(spot):
        matrix = lax.rem(spot + narrow_count - turn, narrow_count)
        return lax.dynamic_index_in_dim(for_owners, jnp.minimum(matrix, 3), 0, False)

    owned = [for_device(narrow_spot)] + [
        shifted(for_device(lax.rem(narrow_spot + step, narrow_count)), "narrow", step)
        for step in range(1, narrow_count)
    ]
    kv_wide = kv_wide.reshape(wide_count, 2, tok_rows, narrow_count * kv_size)
    grad_kv_w = jnp.einsum(
        "wtc,wjtf->jcf", tok_cols, kv_wide, preferred_element_type=FULL
    )
    summed_kv = lax.psum_scatter(grad_kv_w, "narrow", scatter_dimension=2, tiled=True)
    summed_table, table_squares = spread(
        spots, listed, grad_rows.reshape(-1, columns), head_cols_all.reshape(vocab_rows, columns)
    )

    squares = (
        jnp.sum(summed_qo * summed_qo)
        + jnp.sum(summed_kv * summed_kv)
        + ffn_squares
        + jnp.sum(table_squares)
    )
    sums = jnp.stack(
        [gain_attn, gain_mid[0], gain_early + gain_late[0], jnp.full((width,), squares)]
    )
    sums, kv_owned = launch(
        [
            combine(sums.reshape(4, 8, -1), add_two),
            send_owner(summed_kv.astype(LOW).reshape(-1, lanes)),
        ],
        12,
        "combine_sums",
    )
    sums = sums.reshape(4, width)
    summed_gain = lax.dynamic_slice_in_dim(
        sums[:3], (wide_spot * narrow_count + narrow_spot) * gain_size, gain_size, 1
    )
    square_total = sums[3, 0] + jnp.sum(sums[:3] * sums[:3])
    grad_norm = jnp.sqrt(square_total) / loss_count
    factor = jnp.minimum(1.0, CLIP_NORM / (grad_norm + 1e-06)) / loss_count

    def whole_columns(parts):
        return jnp.moveaxis(parts, 0, 2).reshape(
            parts.shape[1], parts.shape[2], parts.shape[0] * parts.shape[3]
        )

    final_parts, factor = lax.optimization_barrier((for_owners[:3], factor))
    size = width // narrow_count

    def final_piece(spot):
        return lax.dynamic_slice_in_dim(final_parts, spot * size, size, 2)

    summed_ffn = jnp.zeros((3, narrow_count, ffn_size, size), LOW)
    for step in range(narrow_count):
        piece = final_piece(lax.rem(narrow_spot + step, narrow_count))
        if step:
            piece = shifted(piece, "narrow", step)
        source = lax.rem(narrow_spot - step + narrow_count, narrow_count)
        summed_ffn = lax.dynamic_update_index_in_dim(summed_ffn, piece, source, 1)
    summed_ffn = summed_ffn.reshape(3, ffn_rows, size).astype(FULL)

    def ffn_owner():
        return newton(factor, mom_owned, owned)

    def small_owner():
        mom_q, mom_k = unpack_small(mom_owned.astype(FULL))
        order = lax.rem(
            narrow_spot - jnp.arange(narrow_count, dtype=jnp.int32) + narrow_count, narrow_count
        )
        grad_q = jnp.stack(owned).reshape(narrow_count, -1)[:, : mom_qo.size]
        grad_q = jnp.take(grad_q, order, axis=0).reshape((narrow_count,) + mom_qo.shape)
        grad_k = kv_owned.reshape((narrow_count,) + mom_kv.shape)
        results = [
            newton_small(whole_columns(MOMENTUM * mom + grad.astype(FULL) * factor))
            for mom, grad in ((mom_q, grad_q), (mom_k, grad_k))
        ]
        parts = [
            jnp.moveaxis(
                result.reshape(2, result.shape[1], narrow_count, -1), 2, 0
            ).reshape(narrow_count, -1)
            for result in results
        ]
        flat = jnp.concatenate(parts, axis=1)
        flat = jnp.pad(flat, ((0, 0), (0, slot_rows * slot_cols - flat.shape[1])))
        return flat.reshape(narrow_count, slot_rows, slot_cols)

    small_spot = lax.rem(3 + turn, narrow_count)
    directions = lax.cond(narrow_spot == small_spot, small_owner, ffn_owner)
    received = [lax.dynamic_index_in_dim(directions, narrow_spot, 0, False)] + [
        shifted(
            lax.dynamic_index_in_dim(
                directions, lax.rem(narrow_spot + step, narrow_count), 0, False
            ),
            "narrow",
            step,
        )
        for step in range(1, narrow_count)
    ]

    def direction_of(matrix):
        step = lax.rem(narrow_spot - matrix - turn + 2 * narrow_count, narrow_count)
        result = received[0]
        for at in range(1, narrow_count):
            result = jnp.where(step == at, received[at], result)
        return result

    dir_ffn = jnp.stack([direction_of(matrix) for matrix in range(3)]).astype(FULL)
    dir_qo, dir_kv = unpack_small(direction_of(3).astype(FULL))

    embed_new, embed_m_new, embed_v_new = adamw(
        embed, embed_m, embed_v, summed_table * factor, RATE_ADAM, WEIGHT_DECAY
    )
    gains_new, gains_m_new, gains_v_new = adamw(
        gains, gains_m, gains_v, summed_gain * factor, RATE_GAIN, 0.0
    )

    def mom_next(mom, grad):
        return MOMENTUM * mom + jnp.moveaxis(grad * factor, 0, 1)

    shrink = 1.0 - RATE_MUON * WEIGHT_DECAY

    def weight_next(weight, direction):
        return weight * shrink - RATE_MUON * jnp.moveaxis(direction, 0, 1)

    return (
        loss_sum,
        loss_count,
        grad_norm,
        embed_new,
        embed_m_new,
        embed_v_new,
        weight_next(attn_qo, dir_qo),
        mom_next(attn_qo_mom, summed_qo),
        weight_next(attn_kv, dir_kv),
        mom_next(attn_kv_mom, summed_kv),
        weight_next(ffn, dir_ffn),
        mom_next(ffn_mom, summed_ffn),
        gains_new,
        gains_m_new,
        gains_v_new,
    )


def solution(mesh):
    by_pack = P("wide", None)
    table = P("narrow", "wide")
    layer = P("wide", None, "narrow")
    gain = P(None, ("wide", "narrow"))
    return jax.shard_map(
        per_device,
        mesh=mesh,
        in_specs=(by_pack,) * 4 + (P("wide"),) + (table,) * 3 + (layer,) * 6 + (gain,) * 3,
        out_specs=(P(),) * 3 + (table,) * 3 + (layer,) * 6 + (gain,) * 3,
        check_vma=False,
    )
```

```python
import functools

import jax
import jax.numpy as jnp
from jax import lax
from jax.experimental import pallas as pl
from jax.experimental.pallas import tpu as pltpu
from jax.sharding import PartitionSpec as P

HEADS = 16
HD = 128
KVH = 4
NS_STEPS = 5
STEP = 10


NORM_EPS = 1e-05
ROPE_BASE = 10000.0
EXIT_EARLY = 0.25
EXIT_LAST = 1.0
CLIP_NORM = 0.02
BETA_ONE = 0.9
BETA_TWO = 0.95
ADAM_EPS = 1e-08
RATE_ADAM = 0.02
RATE_GAIN = 0.3
RATE_MUON = 0.3
WEIGHT_DECAY = 0.1
MOMENTUM = 0.95
NEWTON_A = 3.4445
NEWTON_B = -4.775
NEWTON_C = 2.0315
MASKED = -1e30
LOW = jnp.bfloat16
FULL = jnp.float32
BOTH = ("wide", "narrow")
UNROLL = 16
VMEM_BYTES = 56 * 1024 * 1024


def dot(first, second, first_dim, second_dim):
    return lax.dot_general(
        first, second, (((first_dim,), (second_dim,)), ((), ())), preferred_element_type=FULL
    )


def norm_rows(values, gain_row):
    return (
        values * lax.rsqrt(jnp.mean(values * values, axis=-1, keepdims=True) + NORM_EPS) * gain_row
    )


def norm_back(values, gain_row, grad):
    output, pull = jax.vjp(norm_rows, values, gain_row)
    return pull(grad)


def segments_at(lens, where_at):
    ends = jnp.cumsum(lens)
    return jnp.sum((where_at[:, None] >= ends[None, :]).astype(jnp.int32), axis=1)


def angles_at(lens, where_at):
    segment = segments_at(lens, where_at)
    starts = jnp.cumsum(lens) - lens
    member = segment[:, None] == jnp.arange(lens.shape[0], dtype=jnp.int32)[None, :]
    begin = jnp.sum(jnp.where(member, starts[None, :], 0), axis=1)
    offset_pos = (where_at - begin).astype(FULL)
    inverse = ROPE_BASE ** (-2.0 * jnp.arange(HD // 2, dtype=FULL) / HD)
    angle = offset_pos[:, None] * inverse[None, :]
    return (segment, jnp.cos(angle), jnp.sin(angle))


def rotate(values, cosine, sine):
    half = values.shape[-1] // 2
    first, second = (values[..., :half], values[..., half:])
    return jnp.concatenate(
        [first * cosine - second * sine, second * cosine + first * sine], axis=-1
    )


def unrotate(values, cosine, sine):
    return rotate(values, cosine, -sine)


MESH = pl.DeviceIdType.MESH
ANY = pl.BlockSpec(memory_space=pl.ANY)
VMEM = pl.BlockSpec(memory_space=pltpu.VMEM)


def others(axis, count):
    me = lax.axis_index(axis)
    return [{axis: lax.rem(me + step, count)} for step in range(1, count)]


def push(source, target, send, receive, device):
    return pltpu.make_async_remote_copy(
        src_ref=source,
        dst_ref=target,
        send_sem=send,
        recv_sem=receive,
        device_id=device,
        device_id_type=MESH,
    )


def arrived(block, send, receive, device):
    push(block, block, send, receive, device).wait_recv()


def like(values):
    return jax.ShapeDtypeStruct(values.shape, values.dtype)


def struct(shape, dtype):
    return jax.ShapeDtypeStruct(shape, dtype)


def sems(*shape):
    return pltpu.SemaphoreType.DMA(shape)


class Task:
    def __init__(self, inputs, outputs, scratch, steps, place_in, place_out, axes):
        self.inputs, self.outputs, self.scratch, self.steps = inputs, outputs, scratch, steps
        self.place_in = [place_in] * len(inputs)
        self.place_out = [place_out] * len(outputs)
        self.axes = axes


def launch(tasks, ident, name):
    axes = sorted(set(axis for task in tasks for axis in task.axes))
    inputs = [a for task in tasks for a in task.inputs]
    outputs = [a for task in tasks for a in task.outputs]
    scratch = [a for task in tasks for a in task.scratch]

    def body(*refs):
        refs = list(refs)
        ins = refs[: len(inputs)]
        outs = refs[len(inputs) : len(inputs) + len(outputs)]
        extra = refs[len(inputs) + len(outputs) :]
        barrier = pltpu.get_barrier_semaphore()
        targets = [device for axis in axes for device in others(axis, lax.axis_size(axis))]
        for device in targets:
            pl.semaphore_signal(barrier, inc=1, device_id=device, device_id_type=MESH)
        pl.semaphore_wait(barrier, len(targets))
        live = []
        for task in tasks:
            counts = (len(task.inputs), len(task.outputs), len(task.scratch))
            live.append(task.steps(ins[: counts[0]], outs[: counts[1]], extra[: counts[2]]))
            ins, outs, extra = ins[counts[0] :], outs[counts[1] :], extra[counts[2] :]
        while live:
            live = [steps for steps in live if next(steps, 0) is None]

    size = sum(a.size * a.dtype.itemsize for a in list(inputs) + list(outputs))
    return pl.pallas_call(
        body,
        out_shape=outputs,
        in_specs=[place for task in tasks for place in task.place_in],
        out_specs=[place for task in tasks for place in task.place_out],
        scratch_shapes=scratch,
        compiler_params=pltpu.CompilerParams(
            collective_id=ident, has_side_effects=True, vmem_limit_bytes=VMEM_BYTES
        ),
        cost_estimate=pl.CostEstimate(flops=0, bytes_accessed=8 * size, transcendentals=0),
        name=name,
    )(*inputs)


def later(task, turns):
    begin = task.steps

    def steps(ins, outs, scratch):
        for turn in range(turns):
            yield
        yield from begin(ins, outs, scratch)

    task.steps = steps
    return task


def gather_wide(values, patience=1):
    count = lax.axis_size("wide")
    chips = count // 2

    def steps(ins, outs, scratch):
        (x_ref,), (out_ref,), (send, receive, local) = ins, outs, scratch
        me = lax.axis_index("wide")
        mate = me + 1 - 2 * lax.rem(me, 2)
        peers = [lax.rem(me + 2 * step, count) for step in range(1, chips)] + [mate]
        first = []
        for step, peer in enumerate(peers):
            copy = push(x_ref, out_ref.at[me], send.at[step], receive.at[me], {"wide": peer})
            copy.start()
            first.append(copy)
        keep = pltpu.make_async_copy(x_ref, out_ref.at[me], local)
        keep.start()
        for turn in range(patience):
            yield
        second = []
        for step in range(1, chips):
            source = lax.rem(me - 2 * step + count, count)
            block = out_ref.at[source]
            arrived(block, send.at[0], receive.at[source], {"wide": mate})
            copy = push(
                block, block, send.at[chips + step - 1], receive.at[source], {"wide": mate}
            )
            copy.start()
            second.append(copy)
        yield
        for step in range(chips):
            source = lax.rem(mate - 2 * step + count, count)
            arrived(out_ref.at[source], send.at[0], receive.at[source], {"wide": mate})
        for copy in first + second:
            copy.wait_send()
        keep.wait()

    shape = struct((count,) + values.shape, values.dtype)
    return Task(
        [values], [shape], [sems(count - 1), sems(count), sems()], steps, ANY, ANY, ["wide"]
    )


def trade(axis, values, source_of, target_of, shape, patience=2):
    count = lax.axis_size(axis)

    def steps(ins, outs, scratch):
        (x_ref,), (out_ref,), (send, receive, local) = ins, outs, scratch
        me = lax.axis_index(axis)
        copies = []
        for step in range(1, count):
            peer = lax.rem(me + step, count)
            copy = push(
                source_of(x_ref, peer),
                target_of(out_ref, me),
                send.at[step - 1],
                receive.at[me],
                {axis: peer},
            )
            copy.start()
            copies.append(copy)
        keep = pltpu.make_async_copy(source_of(x_ref, me), target_of(out_ref, me), local)
        keep.start()
        for turn in range(patience):
            yield
        for step in range(1, count):
            source = lax.rem(me - step + count, count)
            arrived(
                target_of(out_ref, source), send.at[0], receive.at[source], {axis: source}
            )
        for copy in copies:
            copy.wait_send()
        keep.wait()

    return Task(
        [values],
        [struct(shape, values.dtype)],
        [sems(count - 1), sems(count), sems()],
        steps,
        ANY,
        ANY,
        [axis],
    )


def block_at(ref, spot):
    return ref.at[spot]


def whole_at(ref, spot):
    return ref


def columns_of(size):
    def at(ref, spot):
        return ref.at[:, pl.ds(pl.multiple_of(spot * size, size), size)]

    return at


def turned(ref, spot):
    count = lax.axis_size("narrow")
    matrix = lax.rem(spot + count - lax.rem(lax.axis_index("wide"), 2), count)
    return ref.at[jnp.minimum(matrix, 3)]


def swap_turned(values, patience=2):
    shape = (lax.axis_size("narrow"),) + values.shape[1:]
    return trade("narrow", values, turned, block_at, shape, patience)


def send_owner(values):
    count = lax.axis_size("narrow")

    def steps(ins, outs, scratch):
        (x_ref,), (out_ref,), (send, receive, local) = ins, outs, scratch
        me = lax.axis_index("narrow")
        owner = lax.rem(3 + lax.rem(lax.axis_index("wide"), 2), count)
        keep = pltpu.make_async_copy(x_ref, out_ref.at[me], local)
        keep.start()

        def to_owner():
            return push(x_ref, out_ref.at[me], send.at[0], receive.at[me], {"narrow": owner})

        @pl.when(me != owner)
        def _():
            to_owner().start()

        yield
        yield

        @pl.when(me != owner)
        def _():
            to_owner().wait_send()

        @pl.when(me == owner)
        def _():
            for step in range(1, count):
                source = lax.rem(owner + step, count)
                arrived(out_ref.at[source], send.at[0], receive.at[source], {"narrow": source})

        keep.wait()

    return Task(
        [values],
        [struct((count,) + values.shape, values.dtype)],
        [sems(1), sems(count), sems()],
        steps,
        ANY,
        ANY,
        ["narrow"],
    )


def swap_blocks(axis, values):
    return trade(axis, values, block_at, block_at, values.shape)


def gather_blocks(axis, values):
    shape = (lax.axis_size(axis),) + values.shape
    return trade(axis, values, whole_at, block_at, shape)


def split_columns(axis, values, patience=2):
    count = lax.axis_size(axis)
    rows, size = values.shape[0], values.shape[1] // count
    return trade(axis, values, columns_of(size), block_at, (count, rows, size), patience)


def join_columns(axis, values):
    count, rows, size = values.shape
    return trade(axis, values, block_at, columns_of(size), (rows, count * size))


def collect(count, parts_ref, slots, send, receive):
    me = lax.axis_index("narrow")
    copies = []
    for step in range(1, count):
        peer = lax.rem(me + step, count)
        copy = push(
            parts_ref.at[peer],
            slots.at[me],
            send.at[step - 1],
            receive.at[me],
            {"narrow": peer},
        )
        copy.start()
        copies.append(copy)
    return copies


def collected(count, parts_ref, slots, send, receive):
    me = lax.axis_index("narrow")
    total = parts_ref[me].astype(FULL)
    for step in range(1, count):
        source = lax.rem(me - step + count, count)
        arrived(slots.at[source], send.at[0], receive.at[source], {"narrow": source})
        total = total + slots[source].astype(FULL)
    return total


def share(count, low, all_ref, send, receive):
    me = lax.axis_index("narrow")
    all_ref[me] = low
    copies = []
    for step in range(1, count):
        peer = lax.rem(me + step, count)
        copy = push(
            all_ref.at[me], all_ref.at[me], send.at[step - 1], receive.at[me], {"narrow": peer}
        )
        copy.start()
        copies.append(copy)
    return copies


def shared(count, all_ref, send, receive):
    me = lax.axis_index("narrow")
    for step in range(1, count):
        source = lax.rem(me - step + count, count)
        arrived(all_ref.at[source], send.at[0], receive.at[source], {"narrow": source})


def narrow_sems(count):
    return [sems(count - 1), sems(count)]


def settle(partial, base, other, keep_row, gain_row):
    count = lax.axis_size("narrow")
    rows, width = base.shape

    def steps(ins, outs, scratch):
        parts_ref, base_ref, other_ref, keep_ref, gain_ref = ins
        own_ref, all_ref = outs
        slots, send, receive, send_all, receive_all = scratch
        copies = collect(count, parts_ref, slots, send, receive)
        yield
        total = collected(count, parts_ref, slots, send, receive)
        total = jnp.where(keep_ref[...] > 0, total + base_ref[...], other_ref[...])
        own_ref[...] = total
        low = norm_rows(total, gain_ref[...]).astype(LOW)
        copies = copies + share(count, low, all_ref, send_all, receive_all)
        yield
        shared(count, all_ref, send_all, receive_all)
        for copy in copies:
            copy.wait_send()

    return Task(
        [partial.reshape(count, rows, width), base, other, keep_row, gain_row],
        [struct((rows, width), FULL), struct((count, rows, width), LOW)],
        [pltpu.VMEM((count, rows, width), partial.dtype)]
        + narrow_sems(count)
        + narrow_sems(count),
        steps,
        VMEM,
        VMEM,
        ["narrow"],
    )


def settle_back(partial, values, add, keep_row, gain_row):
    count = lax.axis_size("narrow")
    rows, width = values.shape

    def steps(ins, outs, scratch):
        parts_ref, values_ref, add_ref, keep_ref, gain_ref = ins
        own_ref, gain_grad_ref, all_ref = outs
        slots, send, receive, send_all, receive_all = scratch
        copies = collect(count, parts_ref, slots, send, receive)
        yield
        grad = collected(count, parts_ref, slots, send, receive)
        held = values_ref[...]
        root = lax.rsqrt(jnp.mean(held * held, axis=-1, keepdims=True) + NORM_EPS)
        scaled = gain_ref[...] * grad
        inner = jnp.mean(held * scaled, axis=-1, keepdims=True)
        own = add_ref[...] + root * scaled - held * (root * root * root * inner)
        gain_grad_ref[...] = jnp.sum(held * root * grad, axis=0, keepdims=True)
        own_ref[...] = own
        low = (own * keep_ref[...]).astype(LOW)
        copies = copies + share(count, low, all_ref, send_all, receive_all)
        yield
        shared(count, all_ref, send_all, receive_all)
        for copy in copies:
            copy.wait_send()

    return Task(
        [partial.reshape(count, rows, width), values, add, keep_row, gain_row],
        [
            struct((rows, width), FULL),
            struct((1, width), FULL),
            struct((count, rows, width), LOW),
        ],
        [pltpu.VMEM((count, rows, width), partial.dtype)]
        + narrow_sems(count)
        + narrow_sems(count),
        steps,
        VMEM,
        VMEM,
        ["narrow"],
    )


def sum_narrow(partial):
    count = lax.axis_size("narrow")
    rows, width = partial.shape[0] // count, partial.shape[1]

    def steps(ins, outs, scratch):
        (parts_ref,), (own_ref,), (slots, send, receive) = ins, outs, scratch
        copies = collect(count, parts_ref, slots, send, receive)
        yield
        yield
        own_ref[...] = collected(count, parts_ref, slots, send, receive)
        for copy in copies:
            copy.wait_send()

    return Task(
        [partial.reshape(count, rows, width)],
        [struct((rows, width), FULL)],
        [pltpu.VMEM((count, rows, width), partial.dtype)] + narrow_sems(count),
        steps,
        VMEM,
        VMEM,
        ["narrow"],
    )


def fetch_rows(found, rows):
    deep, wide = lax.axis_size("narrow"), lax.axis_size("wide")
    columns = found.shape[2]

    def steps(ins, outs, scratch):
        (found_ref,), (out_ref,) = ins, outs
        rightward, leftward, final = scratch[:3]
        send_right, receive_right, send_left, receive_left = scratch[3:7]
        send_wide, receive_wide, local = scratch[7:]
        spot = lax.axis_index("narrow")
        me = lax.axis_index("wide")

        def right_copy(part, source):
            return push(
                source,
                rightward.at[part],
                send_right.at[part],
                receive_right.at[part],
                {"narrow": lax.rem(spot + 1, deep)},
            )

        def left_copy(part, source):
            return push(
                source,
                leftward.at[part],
                send_left.at[part],
                receive_left.at[part],
                {"narrow": lax.rem(spot + deep - 1, deep)},
            )

        for step in range(deep - 1):
            right, left = deep - 1 - step, step

            @pl.when((spot == 0) & (right > 0))
            def _():
                right_copy(right, found_ref.at[right]).start()

            @pl.when((spot == deep - 1) & (left < deep - 1))
            def _():
                left_copy(left, found_ref.at[left]).start()

        yield
        for step in range(deep - 1):
            right, left = deep - 1 - step, step

            @pl.when((spot > 0) & (right > spot))
            def _():
                right_copy(right, rightward.at[right]).wait_recv()
                rightward[right] = rightward[right] + found_ref[right]
                right_copy(right, rightward.at[right]).start()

            @pl.when((spot < deep - 1) & (left < spot))
            def _():
                left_copy(left, leftward.at[left]).wait_recv()
                leftward[left] = leftward[left] + found_ref[left]
                left_copy(left, leftward.at[left]).start()

        final[...] = found_ref[spot]

        @pl.when(spot > 0)
        def _():
            right_copy(spot, rightward.at[spot]).wait_recv()
            final[...] = final[...] + rightward[spot]

        @pl.when(spot < deep - 1)
        def _():
            left_copy(spot, leftward.at[spot]).wait_recv()
            final[...] = final[...] + leftward[spot]

        def rows_for(device):
            return final.at[pl.ds(pl.multiple_of(device * rows, rows), rows)]

        def columns_from(device):
            return columns_of(columns)(out_ref, device)

        copies = []
        for step in range(1, wide):
            peer = lax.rem(me + step, wide)
            copy = push(
                rows_for(peer),
                columns_from(me),
                send_wide.at[step - 1],
                receive_wide.at[me],
                {"wide": peer},
            )
            copy.start()
            copies.append(copy)
        keep = pltpu.make_async_copy(rows_for(me), columns_from(me), local)
        keep.start()
        for step in range(1, wide):
            source = lax.rem(me - step + wide, wide)
            arrived(
                columns_from(source), send_wide.at[0], receive_wide.at[source], {"wide": source}
            )
        yield
        for copy in copies:
            copy.wait_send()
        keep.wait()
        for step in range(deep - 1):
            right, left = deep - 1 - step, step

            @pl.when(right > spot)
            def _():
                right_copy(right, found_ref.at[right]).wait_send()

            @pl.when(left < spot)
            def _():
                left_copy(left, found_ref.at[left]).wait_send()

    task = Task(
        [found],
        [struct((rows, wide * columns), found.dtype)],
        [pltpu.VMEM(found.shape, found.dtype)] * 2
        + [pltpu.VMEM(found.shape[1:], found.dtype)]
        + [sems(deep)] * 4
        + [sems(wide - 1), sems(wide), sems()],
        steps,
        VMEM,
        ANY,
        ["narrow", "wide"],
    )
    return task


def return_rows(rows):
    deep, wide = lax.axis_size("narrow"), lax.axis_size("wide")
    count, width = rows.shape
    columns = width // wide

    def steps(ins, outs, scratch):
        (rows_ref,), (out_ref,) = ins, outs
        send_right, send_left, receive_deep, send_wide, receive_wide, local = scratch
        spot = lax.axis_index("narrow")
        me = lax.axis_index("wide")
        part_of = functools.partial(columns_of(columns), rows_ref)

        def landing(device):
            return out_ref.at[spot, pl.ds(pl.multiple_of(device * count, count), count)]

        copies = []
        for step in range(1, wide):
            peer = lax.rem(me + step, wide)
            copy = push(
                part_of(peer),
                landing(me),
                send_wide.at[step - 1],
                receive_wide.at[me],
                {"wide": peer},
            )
            copy.start()
            copies.append(copy)
        keep = pltpu.make_async_copy(part_of(me), landing(me), local)
        keep.start()
        yield
        for step in range(1, wide):
            source = lax.rem(me - step + wide, wide)
            arrived(landing(source), send_wide.at[0], receive_wide.at[source], {"wide": source})
        keep.wait()

        def right_copy(part):
            return push(
                out_ref.at[part],
                out_ref.at[part],
                send_right.at[part],
                receive_deep.at[part],
                {"narrow": lax.rem(spot + 1, deep)},
            )

        def left_copy(part):
            return push(
                out_ref.at[part],
                out_ref.at[part],
                send_left.at[part],
                receive_deep.at[part],
                {"narrow": lax.rem(spot + deep - 1, deep)},
            )

        @pl.when(spot < deep - 1)
        def _():
            right_copy(spot).start()

        @pl.when(spot > 0)
        def _():
            left_copy(spot).start()

        for step in range(1, deep):
            yield

            @pl.when(spot >= step)
            def _():
                right_copy(spot - step).wait_recv()

                @pl.when(spot < deep - 1)
                def _():
                    right_copy(spot - step).start()

            @pl.when(spot + step < deep)
            def _():
                left_copy(spot + step).wait_recv()

                @pl.when(spot > 0)
                def _():
                    left_copy(spot + step).start()

        for part in range(deep):

            @pl.when((part <= spot) & (spot < deep - 1))
            def _():
                right_copy(part).wait_send()

            @pl.when((part >= spot) & (spot > 0))
            def _():
                left_copy(part).wait_send()

        for copy in copies:
            copy.wait_send()

    return Task(
        [rows],
        [struct((deep, wide * count, columns), rows.dtype)],
        [sems(deep)] * 3 + [sems(wide - 1), sems(wide), sems()],
        steps,
        ANY,
        ANY,
        ["narrow", "wide"],
    )


def sum_wide(partial):
    count = lax.axis_size("wide")
    chips = count // 2
    rows, width = partial.shape[0] // count, partial.shape[1]

    def steps(ins, outs, scratch):
        (parts_ref,), (out_ref,) = ins, outs
        from_mate, paired, slots, send_mate, receive_mate, send, receive = scratch
        me = lax.axis_index("wide")
        side = lax.rem(me, 2)
        mate = me + 1 - 2 * side
        my_chip = me // 2
        mate_copies = []
        for step in range(chips):
            chip = lax.rem(my_chip + 1 + step, chips)
            copy = push(
                parts_ref.at[2 * chip + 1 - side],
                from_mate.at[chip],
                send_mate.at[step],
                receive_mate.at[chip],
                {"wide": mate},
            )
            copy.start()
            mate_copies.append(copy)
        yield
        copies = []
        for step in range(chips):
            chip = lax.rem(my_chip + 1 + step, chips)
            arrived(from_mate.at[chip], send_mate.at[0], receive_mate.at[chip], {"wide": mate})
            both = parts_ref[2 * chip + side].astype(FULL) + from_mate[chip].astype(FULL)
            if step < chips - 1:
                paired[chip] = both.astype(LOW)
                copy = push(
                    paired.at[chip],
                    slots.at[my_chip],
                    send.at[step],
                    receive.at[my_chip],
                    {"wide": 2 * chip + side},
                )
                copy.start()
                copies.append(copy)
            else:
                out_ref[...] = both
        yield
        for step in range(1, chips):
            chip = lax.rem(my_chip - step + chips, chips)
            arrived(slots.at[chip], send.at[0], receive.at[chip], {"wide": 2 * chip + side})
            out_ref[...] = out_ref[...] + slots[chip].astype(FULL)
        for copy in mate_copies + copies:
            copy.wait_send()

    return Task(
        [partial.reshape(count, rows, width)],
        [struct((rows, width), FULL)],
        [pltpu.VMEM((chips, rows, width), LOW)] * 3
        + [sems(chips), sems(chips), sems(max(chips - 1, 1)), sems(chips)],
        steps,
        VMEM,
        VMEM,
        ["wide"],
    )


def merge_stats(first, second):
    peak = jnp.maximum(first[0:1], second[0:1])
    total = first[1:2] * jnp.exp(first[0:1] - peak) + second[1:2] * jnp.exp(second[0:1] - peak)
    return jnp.concatenate([peak, total, first[2:3] + second[2:3]], axis=0)


def add_two(first, second):
    return first + second


def combine(values, join):
    deep, wide = lax.axis_size("narrow"), lax.axis_size("wide")

    def steps(ins, outs, scratch):
        (x_ref,), (out_ref,) = ins, outs
        wide_slots, deep_slots, send_wide, receive_wide, send_deep, receive_deep = scratch

        def start(axis, count, slots, value, send, receive):
            me = lax.axis_index(axis)
            slots[me] = value
            copies = []
            for step in range(1, count):
                peer = lax.rem(me + step, count)
                copy = push(
                    slots.at[me], slots.at[me], send.at[step - 1], receive.at[me], {axis: peer}
                )
                copy.start()
                copies.append(copy)
            return copies

        def finish(axis, count, slots, send, receive):
            me = lax.axis_index(axis)
            for step in range(1, count):
                source = lax.rem(me - step + count, count)
                arrived(slots.at[source], send.at[0], receive.at[source], {axis: source})
            total = slots[0]
            for source in range(1, count):
                total = join(total, slots[source])
            return total

        first = start("wide", wide, wide_slots, x_ref[...], send_wide, receive_wide)
        yield
        total = finish("wide", wide, wide_slots, send_wide, receive_wide)
        second = start("narrow", deep, deep_slots, total, send_deep, receive_deep)
        yield
        out_ref[...] = finish("narrow", deep, deep_slots, send_deep, receive_deep)
        for copy in first + second:
            copy.wait_send()

    return Task(
        [values],
        [like(values)],
        [
            pltpu.VMEM((wide,) + values.shape, values.dtype),
            pltpu.VMEM((deep,) + values.shape, values.dtype),
            sems(wide - 1),
            sems(wide),
            sems(deep - 1),
            sems(deep),
        ],
        steps,
        VMEM,
        VMEM,
        ["narrow", "wide"],
    )


def gather_both(values):
    deep, wide = lax.axis_size("narrow"), lax.axis_size("wide")

    def steps(ins, outs, scratch):
        (x_ref,), (out_ref,) = ins, outs
        send_wide, receive_wide, send_deep, receive_deep = scratch
        me = lax.axis_index("wide")
        spot = lax.axis_index("narrow")
        out_ref[spot, me] = x_ref[...]
        copies = []
        for step in range(1, wide):
            peer = lax.rem(me + step, wide)
            block = out_ref.at[spot, me]
            copy = push(block, block, send_wide.at[step - 1], receive_wide.at[me], {"wide": peer})
            copy.start()
            copies.append(copy)
        yield
        for step in range(1, wide):
            source = lax.rem(me - step + wide, wide)
            block = out_ref.at[spot, source]
            arrived(block, send_wide.at[0], receive_wide.at[source], {"wide": source})
        for step in range(1, deep):
            peer = lax.rem(spot + step, deep)
            block = out_ref.at[spot]
            copy = push(
                block, block, send_deep.at[step - 1], receive_deep.at[spot], {"narrow": peer}
            )
            copy.start()
            copies.append(copy)
        yield
        for step in range(1, deep):
            source = lax.rem(spot - step + deep, deep)
            block = out_ref.at[source]
            arrived(block, send_deep.at[0], receive_deep.at[source], {"narrow": source})
        for copy in copies:
            copy.wait_send()

    return Task(
        [values],
        [struct((deep, wide) + values.shape, values.dtype)],
        [sems(wide - 1), sems(wide), sems(deep - 1), sems(deep)],
        steps,
        VMEM,
        VMEM,
        ["narrow", "wide"],
    )


def feed_body(inner_ref, weight_ref, gate_ref, up_ref, hidden_ref, out_ref, total):
    part = pl.program_id(0)
    inner = inner_ref[...]
    gate = dot(inner, weight_ref[0, 0], 1, 1)
    up = dot(inner, weight_ref[0, 1], 1, 1)
    hidden = (jax.nn.silu(gate) * up).astype(LOW)
    gate_ref[0] = gate
    up_ref[0] = up
    hidden_ref[0] = hidden
    product = dot(hidden, weight_ref[0, 2], 1, 0)

    @pl.when(part == 0)
    def _():
        total[...] = product

    @pl.when(part > 0)
    def _():
        total[...] = total[...] + product

    @pl.when(part == pl.num_programs(0) - 1)
    def _():
        out_ref[...] = total[...].astype(LOW)


def feed(inner, weight):
    parts, _, size, width = weight.shape
    sel = inner.shape[0]
    same = pl.BlockSpec((sel, width), lambda part: (0, 0))
    slab = pl.BlockSpec((1, sel, size), lambda part: (part, 0, 0))
    return pl.pallas_call(
        feed_body,
        grid=(parts,),
        in_specs=[same, pl.BlockSpec((1, 3, size, width), lambda part: (part, 0, 0, 0))],
        out_specs=[slab, slab, slab, same],
        out_shape=[
            struct((parts, sel, size), FULL),
            struct((parts, sel, size), FULL),
            struct((parts, sel, size), LOW),
            struct((sel, width), LOW),
        ],
        scratch_shapes=[pltpu.VMEM((sel, width), FULL)],
        compiler_params=pltpu.CompilerParams(vmem_limit_bytes=VMEM_BYTES),
        cost_estimate=pl.CostEstimate(
            flops=6 * sel * parts * size * width,
            bytes_accessed=weight.size * 2,
            transcendentals=0,
        ),
        name="feed",
    )(inner, weight)


def feed_back_body(grad_ref, weight_ref, gate_ref, up_ref, hidden_ref, acts_ref, out_ref, total):
    part = pl.program_id(0)
    grad_hidden = dot(grad_ref[...], weight_ref[0, 2], 1, 1)
    gate = gate_ref[0]
    sigma = jax.nn.sigmoid(gate)
    grad_gate = (grad_hidden * up_ref[0] * sigma * (1.0 + gate * (1.0 - sigma))).astype(LOW)
    grad_up = (grad_hidden * gate * sigma).astype(LOW)
    acts_ref[0, 0] = grad_gate
    acts_ref[0, 1] = grad_up
    acts_ref[0, 2] = hidden_ref[0]
    product = dot(grad_gate, weight_ref[0, 0], 1, 0) + dot(grad_up, weight_ref[0, 1], 1, 0)

    @pl.when(part == 0)
    def _():
        total[...] = product

    @pl.when(part > 0)
    def _():
        total[...] = total[...] + product

    @pl.when(part == pl.num_programs(0) - 1)
    def _():
        out_ref[...] = total[...].astype(LOW)


def feed_back(grad, weight, gate, up, hidden):
    parts, _, size, width = weight.shape
    sel = grad.shape[0]
    same = pl.BlockSpec((sel, width), lambda part: (0, 0))
    slab = pl.BlockSpec((1, sel, size), lambda part: (part, 0, 0))
    return pl.pallas_call(
        feed_back_body,
        grid=(parts,),
        in_specs=[same, pl.BlockSpec((1, 3, size, width), lambda part: (part, 0, 0, 0))]
        + [slab] * 3,
        out_specs=[pl.BlockSpec((1, 3, sel, size), lambda part: (part, 0, 0, 0)), same],
        out_shape=[struct((parts, 3, sel, size), LOW), struct((sel, width), LOW)],
        scratch_shapes=[pltpu.VMEM((sel, width), FULL)],
        compiler_params=pltpu.CompilerParams(vmem_limit_bytes=VMEM_BYTES),
        cost_estimate=pl.CostEstimate(
            flops=6 * sel * parts * size * width,
            bytes_accessed=weight.size * 2,
            transcendentals=0,
        ),
        name="feed_back",
    )(grad, weight, gate, up, hidden)


def newton_steps(problems):
    rows, width = problems[0][0].shape
    block = min(512, width)
    eye = lax.broadcasted_iota(jnp.int32, (rows, rows), 0) == lax.broadcasted_iota(
        jnp.int32, (rows, rows), 1
    )

    def strip(part):
        return pl.ds(pl.multiple_of(part * block, block), block)

    def over(function, start):
        return lax.fori_loop(0, width // block, function, start)

    def add_squares(part, totals):
        values = [current[:, strip(part)] for current, low, gram, rest in problems]
        return [total + jnp.sum(value * value) for total, value in zip(totals, values)]

    totals = over(add_squares, [jnp.float32(0.0)] * len(problems))
    scales = [1.0 / (jnp.sqrt(total) + 1e-07) for total in totals]

    def begin(part, carry):
        for scale, (current, low, gram, rest) in zip(scales, problems):
            values = current[:, strip(part)] * scale
            current[:, strip(part)] = values
            low[:, strip(part)] = values.astype(LOW)
        return carry

    over(begin, 0)

    def iteration(turn, carry):
        for current, low, gram, rest in problems:
            gram[...] = jnp.zeros_like(gram)

        def add_gram(part, carry):
            for current, low, gram, rest in problems:
                values = low[:, strip(part)]
                gram[...] = gram[...] + dot(values, values, 1, 1)
            return carry

        over(add_gram, 0)
        seconds = []
        for current, low, gram, rest in problems:
            whole = gram[...]
            middle = jnp.sum(jnp.where(eye, whole, 0.0)) / rows
            rest[...] = (whole - jnp.where(eye, middle, 0.0)).astype(LOW)
            square = dot(rest[...], rest[...], 1, 0)
            whole = gram[...]
            centred = whole - jnp.where(eye, middle, 0.0)
            square = square + 2.0 * middle * centred + jnp.where(eye, middle * middle, 0.0)
            whole = NEWTON_B * whole + NEWTON_C * square
            second = jnp.sum(jnp.where(eye, whole, 0.0)) / rows
            rest[...] = (whole - jnp.where(eye, second, 0.0)).astype(LOW)
            seconds.append(second)

        def apply(part, carry):
            for second, (current, low, gram, rest) in zip(seconds, problems):
                values = (NEWTON_A + second) * current[:, strip(part)] + dot(
                    rest[...], low[:, strip(part)], 1, 0
                )
                current[:, strip(part)] = values
                low[:, strip(part)] = values.astype(LOW)
            return carry

        over(apply, 0)
        return carry

    lax.fori_loop(0, NS_STEPS, iteration, 0)


def newton_scratch(rows, width):
    return [
        pltpu.VMEM((rows, width), FULL),
        pltpu.VMEM((rows, width), LOW),
        pltpu.VMEM((rows, rows), FULL),
        pltpu.VMEM((rows, rows), LOW),
    ]


def newton_cost(count, rows, width):
    return pl.CostEstimate(
        flops=NS_STEPS * count * (4 * rows * rows * width + 2 * rows * rows * rows),
        bytes_accessed=6 * count * rows * width,
        transcendentals=0,
    )


def newton_body(factor_ref, mom_ref, grad_ref, out_ref, *problem):
    current, low = problem[:2]
    parts, rows, columns = mom_ref.shape
    factor = factor_ref[0]
    for part in range(parts):
        spot = slice(part * columns, (part + 1) * columns)
        current[:, spot] = MOMENTUM * mom_ref[part].astype(FULL) + factor * grad_ref[
            :, spot
        ].astype(FULL)
    newton_steps([problem])
    for part in range(parts):
        out_ref[part] = low[:, part * columns : (part + 1) * columns]


def newton(factor, mom, grad):
    parts, rows, columns = mom.shape
    width = parts * columns
    return pl.pallas_call(
        newton_body,
        in_specs=[pl.BlockSpec(memory_space=pltpu.SMEM), VMEM, VMEM],
        out_specs=VMEM,
        out_shape=struct(mom.shape, LOW),
        scratch_shapes=newton_scratch(rows, width),
        compiler_params=pltpu.CompilerParams(vmem_limit_bytes=VMEM_BYTES),
        cost_estimate=newton_cost(1, rows, width),
        name="newton",
    )(factor.reshape(1), mom, grad)


def newton_small_body(rows, factor_ref, mom_ref, grad_ref, kv_ref, out_ref, *scratch):
    problems = [scratch[4 * at : 4 * at + 4] for at in range(4)]
    parts, _, columns = mom_ref.shape
    piece_rows = 2 * rows // parts
    kv_columns = kv_ref.shape[2]
    half = rows // 2
    factor = factor_ref[0]
    for part in range(parts):
        spot = slice(part * columns, (part + 1) * columns)
        for member in range(2):
            current = problems[member][0]
            current[:, spot] = MOMENTUM * mom_ref[
                part, member * rows : (member + 1) * rows, :
            ].astype(FULL)
        for block in range(parts):
            current = problems[block // (parts // 2)][0]
            at = block % (parts // 2) * piece_rows
            piece = grad_ref[part, 0:piece_rows, block * columns : (block + 1) * columns]
            current[at : at + piece_rows, spot] = (
                current[at : at + piece_rows, spot] + factor * piece.astype(FULL)
            )
        spot = slice(part * kv_columns, (part + 1) * kv_columns)
        for member in range(2):
            current = problems[2 + member][0]
            piece = kv_ref[part, member * rows : (member + 1) * rows, :].astype(FULL)
            for side in range(2):
                lane = (2 * member + side) * kv_columns
                mom = mom_ref[part, 2 * rows : 2 * rows + half, lane : lane + kv_columns]
                here = slice(side * half, (side + 1) * half)
                current[here, spot] = MOMENTUM * mom.astype(FULL) + factor * piece[here]
    newton_steps(problems[:2])
    newton_steps(problems[2:])
    out_ref[...] = jnp.zeros_like(out_ref)
    for part in range(parts):
        for member in range(2):
            out_ref[part, member * rows : (member + 1) * rows, :] = problems[member][1][
                :, part * columns : (part + 1) * columns
            ]
            low = problems[2 + member][1]
            for side in range(2):
                lane = (2 * member + side) * kv_columns
                out_ref[part, 2 * rows : 2 * rows + half, lane : lane + kv_columns] = low[
                    side * half : (side + 1) * half,
                    part * kv_columns : (part + 1) * kv_columns,
                ]


def newton_small(factor, mom, grad, kv_grad):
    parts, _, columns = mom.shape
    rows = kv_grad.shape[1] // 2
    kv_width = parts * kv_grad.shape[2]
    return pl.pallas_call(
        functools.partial(newton_small_body, rows),
        in_specs=[pl.BlockSpec(memory_space=pltpu.SMEM), VMEM, VMEM, VMEM],
        out_specs=VMEM,
        out_shape=struct(mom.shape, LOW),
        scratch_shapes=newton_scratch(rows, parts * columns) * 2
        + newton_scratch(rows, kv_width) * 2,
        compiler_params=pltpu.CompilerParams(vmem_limit_bytes=VMEM_BYTES),
        cost_estimate=newton_cost(2, rows, parts * columns),
        name="newton_small",
    )(factor.reshape(1), mom, grad, kv_grad)


def lookup_body(ids_ref, turn_ref, table_ref, out_ref, low_ref, list_ref, held, rows, sem):
    vocab = table_ref.shape[0]
    count = out_ref.shape[0]
    load = pltpu.make_async_copy(table_ref, held, sem)
    load.start()
    rows[...] = jnp.zeros_like(rows)

    found = turn_ref[count]

    def note(group, carry):
        for member in range(UNROLL):
            at = group * UNROLL + member
            list_ref[turn_ref[at]] = at
        return carry

    lax.fori_loop(0, count // UNROLL, note, 0)
    for member in range(UNROLL):
        list_ref[found + member] = count
    list_ref[count + UNROLL] = found
    load.wait()

    def step(group, carry):
        for member in range(UNROLL):
            at = list_ref[group * UNROLL + member]
            spot = jnp.minimum(ids_ref[jnp.minimum(at, count - 1)], vocab - 1)
            rows[pl.ds(at, 1), :] = held[pl.ds(spot, 1), :]
        return carry

    lax.fori_loop(0, (found + UNROLL - 1) // UNROLL, step, 0)
    out_ref[...] = rows[pl.ds(0, count), :].astype(LOW)
    low_ref[...] = held[...].astype(LOW)


def lookup(table, ids):
    vocab, columns = table.shape
    count = ids.shape[0]
    mine = (ids < vocab).reshape(-1, 128)
    before = jnp.arange(128)[:, None] < jnp.arange(128)[None, :]
    in_row = dot(mine.astype(LOW), before.astype(LOW), 1, 0)
    per_row = jnp.sum(mine.astype(FULL), axis=1)
    lines = jnp.arange(mine.shape[0])
    ahead = jnp.sum(jnp.where(lines[:, None] > lines[None, :], per_row[None, :], 0.0), axis=1)
    found = jnp.sum(per_row).astype(jnp.int32)
    turns = (in_row + ahead[:, None]).astype(jnp.int32)
    turns = jnp.where(mine, turns, count + UNROLL + 1).reshape(-1)
    turns = jnp.concatenate([turns, jnp.full((128,), found)])
    return pl.pallas_call(
        lookup_body,
        in_specs=[pl.BlockSpec(memory_space=pltpu.SMEM)] * 2 + [ANY],
        out_specs=[VMEM, VMEM, pl.BlockSpec(memory_space=pltpu.SMEM)],
        scratch_shapes=[
            pltpu.VMEM((vocab, columns), FULL),
            pltpu.VMEM((count + 8, columns), FULL),
            pltpu.SemaphoreType.DMA,
        ],
        out_shape=[
            struct((count, columns), LOW),
            struct((vocab, columns), LOW),
            struct((count + 2 * UNROLL,), jnp.int32),
        ],
        compiler_params=pltpu.CompilerParams(vmem_limit_bytes=VMEM_BYTES),
        cost_estimate=pl.CostEstimate(
            flops=0, bytes_accessed=vocab * columns * 4 + count * columns * 24, transcendentals=0
        ),
        name="lookup",
    )(ids, turns, table)


def spread_body(
    ids_ref, list_ref, rows_ref, head_ref, out_ref, square_ref, even, odd, rows, sem
):
    vocab = out_ref.shape[0]
    count = rows_ref.shape[0]
    chunk = 256

    def strip(part):
        return pl.ds(pl.multiple_of(part * chunk, chunk), chunk)

    def begin(part, carry):
        even[strip(part), :] = head_ref[strip(part), :].astype(FULL)
        odd[strip(part), :] = jnp.zeros((chunk, odd.shape[1]), FULL)
        return carry

    lax.fori_loop(0, vocab // chunk, begin, 0)

    def widen(part, carry):
        rows[strip(part), :] = rows_ref[strip(part), :].astype(FULL)
        return carry

    lax.fori_loop(0, count // chunk, widen, 0)
    rows[pl.ds(count, 8), :] = jnp.zeros((8, rows.shape[1]), FULL)

    def step(group, carry):
        for member in range(UNROLL):
            at = list_ref[group * UNROLL + member]
            spot = jnp.minimum(ids_ref[jnp.minimum(at, count - 1)], vocab - 1)
            total = even if member % 2 == 0 else odd
            total[pl.ds(spot, 1), :] = total[pl.ds(spot, 1), :] + rows[pl.ds(at, 1), :]
        return carry

    found = list_ref[count + UNROLL]
    lax.fori_loop(0, (found + UNROLL - 1) // UNROLL, step, 0)

    def finish(part, squares):
        value = even[strip(part), :] + odd[strip(part), :]
        even[strip(part), :] = value
        return squares + jnp.sum((value * value).reshape(chunk // 8, 8, -1), axis=0)

    square_ref[...] = lax.fori_loop(
        0, vocab // chunk, finish, jnp.zeros((8, even.shape[1]), FULL)
    )
    store = pltpu.make_async_copy(even, out_ref, sem)
    store.start()
    store.wait()


def spread(ids, listed, rows, head):
    vocab, columns = head.shape
    count = ids.shape[0]
    smem = pl.BlockSpec(memory_space=pltpu.SMEM)
    return pl.pallas_call(
        spread_body,
        in_specs=[smem, smem, VMEM, VMEM],
        out_specs=[ANY, VMEM],
        scratch_shapes=[
            pltpu.VMEM((vocab, columns), FULL),
            pltpu.VMEM((vocab, columns), FULL),
            pltpu.VMEM((count + 8, columns), FULL),
            pltpu.SemaphoreType.DMA,
        ],
        out_shape=[struct((vocab, columns), FULL), struct((8, columns), FULL)],
        compiler_params=pltpu.CompilerParams(vmem_limit_bytes=VMEM_BYTES),
        cost_estimate=pl.CostEstimate(
            flops=count * columns, bytes_accessed=count * columns * 48, transcendentals=0
        ),
        name="spread",
    )(ids, listed, rows, head)


def adamw(weight, first_m, second_m, grad, rate, decay):
    first_new = BETA_ONE * first_m + (1.0 - BETA_ONE) * grad
    second_new = BETA_TWO * second_m + (1.0 - BETA_TWO) * grad * grad
    update = (
        first_new
        / (1.0 - BETA_ONE**STEP)
        / (jnp.sqrt(second_new / (1.0 - BETA_TWO**STEP)) + ADAM_EPS)
    )
    return (weight * (1.0 - rate * decay) - rate * update, first_new, second_new)


def cut_columns(values, count):
    rows, columns = values.shape
    return jnp.moveaxis(values.reshape(rows, count, columns // count), 1, 0)


def shifted(parts, axis, step):
    count = lax.axis_size(axis)
    pairs = [(source, (source + step) % count) for source in range(count)]
    return lax.ppermute(parts, axis, pairs)


def per_device(
    tokens,
    picks,
    targets,
    lengths,
    skip,
    embed,
    embed_m,
    embed_v,
    attn_qo,
    attn_qo_mom,
    attn_kv,
    attn_kv_mom,
    ffn,
    ffn_mom,
    gains,
    gains_m,
    gains_v,
):
    wide_count = lax.axis_size("wide")
    narrow_count = lax.axis_size("narrow")
    narrow_spot = lax.axis_index("narrow")
    wide_spot = lax.axis_index("wide")
    seq_len = tokens.shape[1]
    sel = picks.shape[1]
    vocab_rows, columns = embed.shape
    width = columns * wide_count
    own_rows = sel // narrow_count
    tok_rows = seq_len // narrow_count
    all_rows = own_rows + tok_rows
    heads_own = HEADS // narrow_count
    head_cols = heads_own * HD
    repeat = max(1, narrow_count // KVH)
    groups = KVH * repeat // narrow_count
    ffn_rows = ffn.shape[0]
    ffn_size = ffn_rows // narrow_count
    total_rows = wide_count * sel
    lens = lengths[0]
    pick_ids = picks[0]
    keep_layer = (1 - skip[0]).astype(FULL)
    keep_row = jnp.full((1, width), keep_layer)
    lanes = 128

    def box(flat):
        height = -(-flat.shape[0] // (8 * lanes)) * 8
        return jnp.pad(flat, (0, height * lanes - flat.shape[0])).reshape(height, lanes)

    ffn_low = jnp.moveaxis(ffn, 1, 0).astype(LOW)
    ffn_cut = ffn_low.reshape(3, narrow_count, ffn_size, ffn_low.shape[2])
    ffn_cut = jnp.moveaxis(ffn_cut, 1, 0).reshape(narrow_count, 3 * ffn_size, -1)
    kv_part = lax.all_gather(attn_kv.reshape(columns, -1).astype(LOW), "narrow", axis=0)
    kv_part = jnp.moveaxis(kv_part, 0, 1).reshape(columns, -1)
    proj_own = jnp.concatenate([attn_qo.reshape(columns, -1).astype(LOW), kv_part], axis=1)
    proj = lax.all_gather(proj_own, "wide", axis=0, tiled=True)

    where_at = jnp.arange(seq_len, dtype=jnp.int32)
    pick_tokens = jnp.sum(
        jnp.where(pick_ids[:, None] == where_at[None, :], tokens[0][None, :], 0), axis=1
    )
    ints = box(jnp.concatenate([tokens[0], pick_tokens, targets[0]]))
    all_ints, all_gains, ffn_sub = launch(
        [
            gather_wide(ints),
            gather_both(box(gains.astype(LOW).astype(FULL).reshape(-1))),
            join_columns("narrow", ffn_cut),
        ],
        0,
        "gather_ids",
    )
    ffn_w = lax.all_gather(ffn_sub.reshape(3, ffn_size, width), "wide", axis=0)
    gain_size = gains.shape[1]
    gain_w = all_gains.reshape(narrow_count, wide_count, -1)[:, :, : 3 * gain_size]
    gain_w = gain_w.reshape(narrow_count, wide_count, 3, gain_size)
    gain_w = jnp.transpose(gain_w, (2, 1, 0, 3)).reshape(3, width)
    all_ints = all_ints.reshape(wide_count, -1)
    tokens_all = all_ints[:, :seq_len].reshape(wide_count, narrow_count, tok_rows)
    picked_all = all_ints[:, seq_len : seq_len + sel].reshape(wide_count, narrow_count, own_rows)
    targets_all = all_ints[:, seq_len + sel : seq_len + 2 * sel].reshape(-1)
    wanted = jnp.moveaxis(jnp.concatenate([tokens_all, picked_all], axis=2), 1, 0).reshape(-1)
    local_ids = wanted - narrow_spot * vocab_rows
    inside = (local_ids >= 0) & (local_ids < vocab_rows)
    spots = jnp.where(inside, local_ids, vocab_rows)
    found, embed_low, listed = lookup(embed, spots)
    found = found.reshape(narrow_count, wide_count * all_rows, columns)
    embed_cut = embed_low.reshape(wide_count, vocab_rows // wide_count, columns)
    rows_low, table_own = launch(
        [fetch_rows(found, all_rows), join_columns("wide", embed_cut)], 1, "fetch_rows"
    )

    mom_qo = jnp.moveaxis(attn_qo_mom, 1, 0)
    mom_kv = jnp.moveaxis(attn_kv_mom, 1, 0)
    mom_ffn = jnp.moveaxis(ffn_mom, 1, 0)
    slot_rows, slot_cols = mom_ffn.shape[1:]

    block_rows, q_size = mom_qo.shape[1:]
    kv_size = mom_kv.shape[2]
    half_rows = block_rows // 2
    kv_box = jnp.moveaxis(mom_kv.reshape(4, half_rows, kv_size), 0, 1).reshape(half_rows, -1)
    small_box = jnp.concatenate([mom_qo.reshape(2 * block_rows, q_size), kv_box])
    small_box = jnp.pad(small_box, ((0, slot_rows - small_box.shape[0]), (0, 0)))
    mom_parts = jnp.concatenate([mom_ffn, small_box[None]]).astype(LOW)

    seg_all = segments_at(lens, where_at)
    tok_at = narrow_spot * tok_rows + jnp.arange(tok_rows, dtype=jnp.int32)
    _, cosine_all, sine_all = angles_at(lens, where_at)
    _, cosine_tok, sine_tok = angles_at(lens, tok_at)
    seg_mine, cosine, sine = angles_at(lens, pick_ids)

    q_w, o_w, kv_w = (
        proj[:, :head_cols],
        proj[:, head_cols : 2 * head_cols],
        proj[:, 2 * head_cols :],
    )

    rows_full = rows_low.astype(FULL)
    normed_all = norm_rows(rows_full, gain_w[0]).astype(LOW)
    normed_tok, normed_own = normed_all[:tok_rows], normed_all[tok_rows:]
    kv_part = dot(normed_tok, kv_w, 1, 0).reshape(tok_rows, narrow_count, 2, kv_size)
    kv_part = jnp.moveaxis(kv_part, 2, 0).reshape(2, tok_rows, KVH, HD)
    keys_part = rotate(kv_part[0], cosine_tok[:, None], sine_tok[:, None]).astype(LOW)
    values_part = kv_part[1].astype(LOW)
    by_head = jnp.moveaxis(jnp.stack([keys_part, values_part]), 2, 0)
    by_head = jnp.repeat(by_head, repeat, axis=0)
    by_head = by_head.reshape(narrow_count, groups, 2, tok_rows, HD)
    own_head, start_low, tok_cols = launch(
        [
            swap_blocks("narrow", by_head),
            gather_blocks("narrow", rows_low[tok_rows:]),
            split_columns("wide", normed_tok),
        ],
        2,
        "trade_heads",
    )
    own_head = jnp.transpose(own_head, (2, 1, 0, 3, 4)).reshape(2, groups, seq_len, HD)
    keys, values = own_head[0], own_head[1]
    start_h = start_low.reshape(sel, width).astype(FULL)

    normed = norm_rows(start_h, gain_w[0]).astype(LOW)
    queries = dot(normed, q_w, 1, 0).reshape(sel, heads_own, HD)
    queries = rotate(queries, cosine[:, None], sine[:, None]).astype(LOW)
    grouped = queries.reshape(sel, groups, heads_own // groups, HD)
    scale = HD ** (-0.5)
    scores = jnp.einsum("tkgd,ksd->kgts", grouped, keys, preferred_element_type=FULL) * scale
    allowed = (seg_mine[:, None] == seg_all[None, :]) & (pick_ids[:, None] >= where_at[None, :])
    scores = jnp.where(allowed, scores, MASKED)
    shifted_exp = jnp.exp(scores - jnp.max(scores, axis=-1, keepdims=True))
    probs = shifted_exp / jnp.sum(shifted_exp, axis=-1, keepdims=True)
    probs_low = probs.astype(LOW)
    mixed = jnp.einsum("kgts,ksd->tkgd", probs_low, values, preferred_element_type=FULL)
    mixed = mixed.reshape(sel, head_cols).astype(LOW)

    early_part = norm_rows(start_h, gain_w[2]).astype(LOW)
    early = lax.all_gather(early_part, "wide", axis=0, tiled=True)
    start_own = lax.dynamic_slice_in_dim(start_h, narrow_spot * own_rows, own_rows, 0)
    middle, inner, mixed_wide, pick_cols = launch(
        [
            settle(
                dot(mixed, o_w, 1, 1).astype(LOW),
                start_own,
                start_own,
                jnp.ones((1, width), FULL),
                gain_w[1:2],
            ),
            gather_wide(mixed),
            split_columns("wide", normed),
        ],
        3,
        "settle_middle",
    )
    inner = inner.reshape(sel, width)
    inner_all = lax.all_gather(inner, "wide", axis=0, tiled=True)
    gate, up, hidden, fed = feed(inner, ffn_w)
    final_own, late_part = launch(
        [settle(fed, middle, start_own, keep_row, gain_w[2:3])], 4, "settle_late"
    )

    table_count = table_own.shape[0]
    local_target = targets_all - (narrow_spot * vocab_rows + wide_spot * table_count)
    has_target = local_target[:, None] == jnp.arange(table_count, dtype=jnp.int32)[None, :]
    counted = (targets_all >= 0).astype(FULL)
    loss_count = jnp.sum(counted)

    def exit_logits(features):
        logits = dot(features, table_own, 1, 1)
        peak = jnp.max(logits, axis=-1)
        total = jnp.sum(jnp.exp(logits - peak[:, None]), axis=-1)
        picked = jnp.sum(jnp.where(has_target, logits, 0.0), axis=-1)
        return logits, jnp.stack([peak, total, picked])

    half = slot_rows // 2
    late, mom_top = launch(
        [
            gather_wide(late_part.reshape(sel, width)),
            swap_turned(mom_parts[:, :half]),
        ],
        5,
        "gather_late",
    )
    late = late.reshape(total_rows, width)
    early_logits, early_stats = exit_logits(early)
    late_logits, late_stats = exit_logits(late)
    stats = jnp.concatenate([early_stats, late_stats], axis=1).reshape(3, 8, -1)
    stats = launch([combine(stats, merge_stats)], 6, "combine_stats")[0]
    stats, inner_all = lax.optimization_barrier((stats, inner_all))
    stats = stats.reshape(3, -1)
    log_norms = stats[0] + jnp.log(stats[1])
    losses = log_norms - stats[2]
    loss_sum = jnp.sum(
        counted * (EXIT_EARLY * losses[:total_rows] + EXIT_LAST * losses[total_rows:])
    )

    def exit_back(logits, log_norm, weight, features):
        grad_logits = (
            (jnp.exp(logits - log_norm[:, None]) - has_target.astype(FULL))
            * (weight * counted)[:, None]
        ).astype(LOW)
        return dot(grad_logits, table_own, 1, 0).astype(LOW), dot(grad_logits, features, 0, 0)

    late_back, late_head = exit_back(late_logits, log_norms[total_rows:], EXIT_LAST, late)
    early_back, early_head = exit_back(early_logits, log_norms[:total_rows], EXIT_EARLY, early)
    grad_late, mom_low = launch(
        [sum_wide(late_back), swap_turned(mom_parts[:, half:])], 7, "sum_late"
    )
    mom_owned = jnp.concatenate([mom_top, mom_low], axis=1)
    grad_head = (early_head + late_head).astype(LOW)

    grad_early = lax.psum_scatter(early_back, "wide", scatter_dimension=0, tiled=True)
    grad_final, gain_late, grad_out = launch(
        [
            settle_back(
                grad_late.astype(LOW),
                final_own,
                jnp.zeros_like(final_own),
                keep_row,
                gain_w[2:3],
            ),
        ],
        8,
        "back_late",
    )
    grad_layer = grad_final * keep_layer
    grad_out = grad_out.reshape(sel, width)
    out_all = lax.all_gather(grad_out, "wide", axis=0, tiled=True)
    acts, fed_back = feed_back(grad_out, ffn_w, gate, up, hidden)
    grad_mid, gain_mid, grad_branch = launch(
        [settle_back(fed_back, middle, grad_layer, keep_row, gain_w[1:2])], 9, "back_middle"
    )
    grad_branch, grad_early = lax.optimization_barrier((grad_branch, grad_early))
    grad_branch = grad_branch.reshape(sel, width)

    grad_mixed = dot(grad_branch, o_w, 1, 0).astype(LOW)
    grouped_grad = grad_mixed.reshape(sel, groups, heads_own // groups, HD)
    grad_probs = jnp.einsum("tkgd,ksd->kgts", grouped_grad, values, preferred_element_type=FULL)
    grad_scores = (
        probs * (grad_probs - jnp.sum(probs * grad_probs, axis=-1, keepdims=True))
    ).astype(LOW)
    grad_queries = (
        jnp.einsum("kgts,ksd->tkgd", grad_scores, keys, preferred_element_type=FULL) * scale
    ).reshape(sel, heads_own, HD)
    grad_queries = (
        unrotate(grad_queries, cosine[:, None], sine[:, None])
        .reshape(sel, head_cols)
        .astype(LOW)
    )
    grad_keys = jnp.einsum("kgts,tkgd->ksd", grad_scores, grouped, preferred_element_type=FULL)
    grad_keys = unrotate(grad_keys * scale, cosine_all, sine_all).astype(LOW)
    grad_values = jnp.einsum(
        "kgts,tkgd->ksd", probs_low, grouped_grad, preferred_element_type=FULL
    ).astype(LOW)
    kv_parts = jnp.stack([grad_keys, grad_values]).reshape(
        2, groups, narrow_count, tok_rows, HD
    )
    kv_parts = jnp.transpose(kv_parts, (2, 1, 0, 3, 4))
    pick_part = dot(grad_queries, q_w, 1, 1).astype(LOW)
    grad_kv, grad_pick, grad_early, acts, queries_wide, branch_cols = launch(
        [
            swap_blocks("narrow", kv_parts),
            sum_narrow(pick_part),
            sum_narrow(grad_early),
            swap_blocks("wide", acts),
            gather_wide(grad_queries),
            split_columns("wide", grad_branch),
        ],
        10,
        "trade_grads",
    )
    grad_start_exit, gain_early = norm_back(start_own, gain_w[2], grad_early)
    grad_kv = grad_kv.reshape(KVH, repeat, 2, tok_rows, HD)
    if repeat > 1:
        grad_kv = jnp.sum(grad_kv.astype(FULL), axis=1, keepdims=True).astype(LOW)
    grad_kv = grad_kv[:, 0]
    kv_rows = jnp.transpose(grad_kv, (1, 2, 0, 3)).reshape(2, tok_rows, narrow_count, kv_size)
    kv_rows = jnp.moveaxis(kv_rows, 0, 2).reshape(tok_rows, -1)
    grad_kv, out_all = lax.optimization_barrier((kv_rows, out_all))
    grad_normed = jnp.concatenate([dot(grad_kv, kv_w, 1, 1), grad_pick])
    grad_rows, gain_attn = norm_back(rows_full, gain_w[0], grad_normed)
    grad_pass = grad_mid + grad_start_exit + grad_final * (1.0 - keep_layer)
    grad_rows = jnp.concatenate([grad_rows[:tok_rows], grad_rows[tok_rows:] + grad_pass])
    acts = jnp.moveaxis(acts, 1, 0).reshape(3, total_rows, ffn_size)
    rights = (inner_all, inner_all, out_all)
    grad_ffn = [dot(acts[j], rights[j], 0, 0) for j in range(3)]
    ffn_squares = sum(jnp.sum(part * part) for part in grad_ffn)
    summed_qo = jnp.stack(
        [
            jnp.einsum("wtc,wtf->cf", pick_cols, queries_wide, preferred_element_type=FULL),
            jnp.einsum("wtc,wtf->cf", branch_cols, mixed_wide, preferred_element_type=FULL),
        ]
    )
    qo_box = summed_qo.astype(LOW).reshape(narrow_count, -1, q_size)
    qo_box = jnp.moveaxis(qo_box, 0, 1).reshape(-1, width)
    qo_box = jnp.pad(qo_box, ((0, ffn_size - qo_box.shape[0]), (0, 0)))
    for_owners = jnp.stack([part.astype(LOW) for part in grad_ffn] + [qo_box])
    grad_rows, owned, kv_wide, head_cols_all = launch(
        [
            return_rows(grad_rows.astype(LOW)),
            swap_turned(for_owners, 5),
            later(gather_wide(grad_kv, 3), 2),
            later(split_columns("wide", grad_head, 3), 2),
        ],
        11,
        "return_rows",
    )
    turn = lax.rem(wide_spot, 2)
    grad_kv_w = jnp.einsum(
        "wtc,wtf->cf", tok_cols, kv_wide, preferred_element_type=FULL
    ).reshape(columns, narrow_count, 2, kv_size)
    grad_kv_w = jnp.moveaxis(grad_kv_w, 0, 2)
    summed_kv = lax.psum_scatter(grad_kv_w, "narrow", scatter_dimension=0, tiled=True)[0]
    summed_table, table_squares = spread(
        spots, listed, grad_rows.reshape(-1, columns), head_cols_all.reshape(vocab_rows, columns)
    )

    squares = (
        jnp.sum(summed_qo * summed_qo)
        + jnp.sum(summed_kv * summed_kv)
        + ffn_squares
        + jnp.sum(table_squares)
    )
    sums = jnp.stack(
        [gain_attn, gain_mid[0], gain_early + gain_late[0], jnp.full((width,), squares)]
    )
    sums, kv_owned = launch(
        [
            combine(sums.reshape(4, 8, -1), add_two),
            send_owner(summed_kv.astype(LOW).reshape(2 * block_rows, kv_size)),
        ],
        12,
        "combine_sums",
    )
    sums = sums.reshape(4, width)
    summed_gain = lax.dynamic_slice_in_dim(
        sums[:3], (wide_spot * narrow_count + narrow_spot) * gain_size, gain_size, 1
    )
    square_total = sums[3, 0] + jnp.sum(sums[:3] * sums[:3])
    grad_norm = jnp.sqrt(square_total) / loss_count
    factor = jnp.minimum(1.0, CLIP_NORM / (grad_norm + 1e-06)) / loss_count

    final_parts, factor = lax.optimization_barrier((for_owners[:3], factor))
    size = width // narrow_count

    def final_piece(spot):
        return lax.dynamic_slice_in_dim(final_parts, spot * size, size, 2)

    summed_ffn = jnp.zeros((3, narrow_count, ffn_size, size), LOW)
    for step in range(narrow_count):
        piece = final_piece(lax.rem(narrow_spot + step, narrow_count))
        if step:
            piece = shifted(piece, "narrow", step)
        source = lax.rem(narrow_spot - step + narrow_count, narrow_count)
        summed_ffn = lax.dynamic_update_index_in_dim(summed_ffn, piece, source, 1)
    summed_ffn = summed_ffn.reshape(3, ffn_rows, size).astype(FULL)

    def ffn_owner():
        return newton(factor, mom_owned, owned.reshape(ffn_rows, width))

    def small_owner():
        return newton_small(factor, mom_owned, owned, kv_owned)

    small_spot = lax.rem(3 + turn, narrow_count)
    directions = lax.cond(narrow_spot == small_spot, small_owner, ffn_owner)
    received = [lax.dynamic_index_in_dim(directions, narrow_spot, 0, False)] + [
        shifted(
            lax.dynamic_index_in_dim(
                directions, lax.rem(narrow_spot + step, narrow_count), 0, False
            ),
            "narrow",
            step,
        )
        for step in range(1, narrow_count)
    ]

    def direction_of(matrix):
        step = lax.rem(narrow_spot - matrix - turn + 2 * narrow_count, narrow_count)
        result = received[0]
        for at in range(1, narrow_count):
            result = jnp.where(step == at, received[at], result)
        return result

    dir_ffn = jnp.stack([direction_of(matrix) for matrix in range(3)]).astype(FULL)
    small = direction_of(3).astype(FULL)
    dir_qo = small[: 2 * block_rows].reshape(mom_qo.shape)
    dir_kv = small[2 * block_rows : 2 * block_rows + half_rows].reshape(half_rows, 4, kv_size)
    dir_kv = jnp.moveaxis(dir_kv, 1, 0).reshape(mom_kv.shape)

    embed_new, embed_m_new, embed_v_new = adamw(
        embed, embed_m, embed_v, summed_table * factor, RATE_ADAM, WEIGHT_DECAY
    )
    gains_new, gains_m_new, gains_v_new = adamw(
        gains, gains_m, gains_v, summed_gain * factor, RATE_GAIN, 0.0
    )

    def mom_next(mom, grad):
        return MOMENTUM * mom + jnp.moveaxis(grad * factor, 0, 1)

    shrink = 1.0 - RATE_MUON * WEIGHT_DECAY

    def weight_next(weight, direction):
        return weight * shrink - RATE_MUON * jnp.moveaxis(direction, 0, 1)

    return (
        loss_sum,
        loss_count,
        grad_norm,
        embed_new,
        embed_m_new,
        embed_v_new,
        weight_next(attn_qo, dir_qo),
        mom_next(attn_qo_mom, summed_qo),
        weight_next(attn_kv, dir_kv),
        mom_next(attn_kv_mom, summed_kv),
        weight_next(ffn, dir_ffn),
        mom_next(ffn_mom, summed_ffn),
        gains_new,
        gains_m_new,
        gains_v_new,
    )


def solution(mesh):
    by_pack = P("wide", None)
    table = P("narrow", "wide")
    layer = P("wide", None, "narrow")
    gain = P(None, ("wide", "narrow"))
    return jax.shard_map(
        per_device,
        mesh=mesh,
        in_specs=(by_pack,) * 4 + (P("wide"),) + (table,) * 3 + (layer,) * 6 + (gain,) * 3,
        out_specs=(P(),) * 3 + (table,) * 3 + (layer,) * 6 + (gain,) * 3,
        check_vma=False,
    )
```

```python
import functools

import jax
import jax.numpy as jnp
from jax import lax
from jax.experimental import pallas as pl
from jax.experimental.pallas import tpu as pltpu
from jax.sharding import PartitionSpec as P

HEADS = 16
HD = 128
KVH = 4
NS_STEPS = 5
STEP = 10


NORM_EPS = 1e-05
ROPE_BASE = 10000.0
EXIT_EARLY = 0.25
EXIT_LAST = 1.0
CLIP_NORM = 0.02
BETA_ONE = 0.9
BETA_TWO = 0.95
ADAM_EPS = 1e-08
RATE_ADAM = 0.02
RATE_GAIN = 0.3
RATE_MUON = 0.3
WEIGHT_DECAY = 0.1
MOMENTUM = 0.95
NEWTON_A = 3.4445
NEWTON_B = -4.775
NEWTON_C = 2.0315
MASKED = -1e30
LOW = jnp.bfloat16
FULL = jnp.float32
BOTH = ("wide", "narrow")
UNROLL = 16
VMEM_BYTES = 56 * 1024 * 1024


def dot(first, second, first_dim, second_dim):
    return lax.dot_general(
        first, second, (((first_dim,), (second_dim,)), ((), ())), preferred_element_type=FULL
    )


def norm_rows(values, gain_row):
    return (
        values * lax.rsqrt(jnp.mean(values * values, axis=-1, keepdims=True) + NORM_EPS) * gain_row
    )


def norm_back(values, gain_row, grad):
    output, pull = jax.vjp(norm_rows, values, gain_row)
    return pull(grad)


def segments_at(lens, where_at):
    ends = jnp.cumsum(lens)
    return jnp.sum((where_at[:, None] >= ends[None, :]).astype(jnp.int32), axis=1)


def angles_at(lens, where_at):
    segment = segments_at(lens, where_at)
    starts = jnp.cumsum(lens) - lens
    member = segment[:, None] == jnp.arange(lens.shape[0], dtype=jnp.int32)[None, :]
    begin = jnp.sum(jnp.where(member, starts[None, :], 0), axis=1)
    offset_pos = (where_at - begin).astype(FULL)
    inverse = ROPE_BASE ** (-2.0 * jnp.arange(HD // 2, dtype=FULL) / HD)
    angle = offset_pos[:, None] * inverse[None, :]
    return (segment, jnp.cos(angle), jnp.sin(angle))


def rotate(values, cosine, sine):
    half = values.shape[-1] // 2
    first, second = (values[..., :half], values[..., half:])
    return jnp.concatenate(
        [first * cosine - second * sine, second * cosine + first * sine], axis=-1
    )


def unrotate(values, cosine, sine):
    return rotate(values, cosine, -sine)


MESH = pl.DeviceIdType.MESH
ANY = pl.BlockSpec(memory_space=pl.ANY)
VMEM = pl.BlockSpec(memory_space=pltpu.VMEM)


def others(axis, count):
    me = lax.axis_index(axis)
    return [{axis: lax.rem(me + step, count)} for step in range(1, count)]


def push(source, target, send, receive, device):
    return pltpu.make_async_remote_copy(
        src_ref=source,
        dst_ref=target,
        send_sem=send,
        recv_sem=receive,
        device_id=device,
        device_id_type=MESH,
    )


def arrived(block, send, receive, device):
    push(block, block, send, receive, device).wait_recv()


def like(values):
    return jax.ShapeDtypeStruct(values.shape, values.dtype)


def struct(shape, dtype):
    return jax.ShapeDtypeStruct(shape, dtype)


def sems(*shape):
    return pltpu.SemaphoreType.DMA(shape)


class Task:
    def __init__(self, inputs, outputs, scratch, steps, place_in, place_out, axes):
        self.inputs, self.outputs, self.scratch, self.steps = inputs, outputs, scratch, steps
        self.place_in = [place_in] * len(inputs)
        self.place_out = [place_out] * len(outputs)
        self.axes = axes


def launch(tasks, ident, name):
    axes = sorted(set(axis for task in tasks for axis in task.axes))
    inputs = [a for task in tasks for a in task.inputs]
    outputs = [a for task in tasks for a in task.outputs]
    scratch = [a for task in tasks for a in task.scratch]

    def body(*refs):
        refs = list(refs)
        ins = refs[: len(inputs)]
        outs = refs[len(inputs) : len(inputs) + len(outputs)]
        extra = refs[len(inputs) + len(outputs) :]
        barrier = pltpu.get_barrier_semaphore()
        targets = [device for axis in axes for device in others(axis, lax.axis_size(axis))]
        for device in targets:
            pl.semaphore_signal(barrier, inc=1, device_id=device, device_id_type=MESH)
        pl.semaphore_wait(barrier, len(targets))
        live = []
        for task in tasks:
            counts = (len(task.inputs), len(task.outputs), len(task.scratch))
            live.append(task.steps(ins[: counts[0]], outs[: counts[1]], extra[: counts[2]]))
            ins, outs, extra = ins[counts[0] :], outs[counts[1] :], extra[counts[2] :]
        while live:
            live = [steps for steps in live if next(steps, 0) is None]

    size = sum(a.size * a.dtype.itemsize for a in list(inputs) + list(outputs))
    return pl.pallas_call(
        body,
        out_shape=outputs,
        in_specs=[place for task in tasks for place in task.place_in],
        out_specs=[place for task in tasks for place in task.place_out],
        scratch_shapes=scratch,
        compiler_params=pltpu.CompilerParams(
            collective_id=ident, has_side_effects=True, vmem_limit_bytes=VMEM_BYTES
        ),
        cost_estimate=pl.CostEstimate(flops=0, bytes_accessed=size // 8, transcendentals=0),
        name=name,
    )(*inputs)


def later(task, turns):
    begin = task.steps

    def steps(ins, outs, scratch):
        for turn in range(turns):
            yield
        yield from begin(ins, outs, scratch)

    task.steps = steps
    return task


def gather_wide(values, patience=1):
    count = lax.axis_size("wide")
    chips = count // 2

    def steps(ins, outs, scratch):
        (x_ref,), (out_ref,), (send, receive, local) = ins, outs, scratch
        me = lax.axis_index("wide")
        mate = me + 1 - 2 * lax.rem(me, 2)
        peers = [lax.rem(me + 2 * step, count) for step in range(1, chips)] + [mate]
        first = []
        for step, peer in enumerate(peers):
            copy = push(x_ref, out_ref.at[me], send.at[step], receive.at[me], {"wide": peer})
            copy.start()
            first.append(copy)
        keep = pltpu.make_async_copy(x_ref, out_ref.at[me], local)
        keep.start()
        for turn in range(patience):
            yield
        second = []
        for step in range(1, chips):
            source = lax.rem(me - 2 * step + count, count)
            block = out_ref.at[source]
            arrived(block, send.at[0], receive.at[source], {"wide": mate})
            copy = push(
                block, block, send.at[chips + step - 1], receive.at[source], {"wide": mate}
            )
            copy.start()
            second.append(copy)
        yield
        for step in range(chips):
            source = lax.rem(mate - 2 * step + count, count)
            arrived(out_ref.at[source], send.at[0], receive.at[source], {"wide": mate})
        for copy in first + second:
            copy.wait_send()
        keep.wait()

    shape = struct((count,) + values.shape, values.dtype)
    return Task(
        [values], [shape], [sems(count - 1), sems(count), sems()], steps, ANY, ANY, ["wide"]
    )


def trade(axis, values, source_of, target_of, shape, patience=2):
    count = lax.axis_size(axis)

    def steps(ins, outs, scratch):
        (x_ref,), (out_ref,), (send, receive, local) = ins, outs, scratch
        me = lax.axis_index(axis)
        copies = []
        for step in range(1, count):
            peer = lax.rem(me + step, count)
            copy = push(
                source_of(x_ref, peer),
                target_of(out_ref, me),
                send.at[step - 1],
                receive.at[me],
                {axis: peer},
            )
            copy.start()
            copies.append(copy)
        keep = pltpu.make_async_copy(source_of(x_ref, me), target_of(out_ref, me), local)
        keep.start()
        for turn in range(patience):
            yield
        for step in range(1, count):
            source = lax.rem(me - step + count, count)
            arrived(
                target_of(out_ref, source), send.at[0], receive.at[source], {axis: source}
            )
        for copy in copies:
            copy.wait_send()
        keep.wait()

    return Task(
        [values],
        [struct(shape, values.dtype)],
        [sems(count - 1), sems(count), sems()],
        steps,
        ANY,
        ANY,
        [axis],
    )


def block_at(ref, spot):
    return ref.at[spot]


def whole_at(ref, spot):
    return ref


def columns_of(size):
    def at(ref, spot):
        return ref.at[:, pl.ds(pl.multiple_of(spot * size, size), size)]

    return at


def turned(ref, spot):
    count = lax.axis_size("narrow")
    matrix = lax.rem(spot + count - lax.rem(lax.axis_index("wide"), 2), count)
    return ref.at[jnp.minimum(matrix, 3)]


def swap_turned(values, patience=2):
    shape = (lax.axis_size("narrow"),) + values.shape[1:]
    return trade("narrow", values, turned, block_at, shape, patience)


def send_owner(values):
    count = lax.axis_size("narrow")

    def steps(ins, outs, scratch):
        (x_ref,), (out_ref,), (send, receive, local) = ins, outs, scratch
        me = lax.axis_index("narrow")
        owner = lax.rem(3 + lax.rem(lax.axis_index("wide"), 2), count)
        keep = pltpu.make_async_copy(x_ref, out_ref.at[me], local)
        keep.start()

        def to_owner():
            return push(x_ref, out_ref.at[me], send.at[0], receive.at[me], {"narrow": owner})

        @pl.when(me != owner)
        def _():
            to_owner().start()

        yield
        yield

        @pl.when(me != owner)
        def _():
            to_owner().wait_send()

        @pl.when(me == owner)
        def _():
            for step in range(1, count):
                source = lax.rem(owner + step, count)
                arrived(out_ref.at[source], send.at[0], receive.at[source], {"narrow": source})

        keep.wait()

    return Task(
        [values],
        [struct((count,) + values.shape, values.dtype)],
        [sems(1), sems(count), sems()],
        steps,
        ANY,
        ANY,
        ["narrow"],
    )


def swap_blocks(axis, values):
    return trade(axis, values, block_at, block_at, values.shape)


def gather_blocks(axis, values):
    shape = (lax.axis_size(axis),) + values.shape
    return trade(axis, values, whole_at, block_at, shape)


def split_columns(axis, values, patience=2):
    count = lax.axis_size(axis)
    rows, size = values.shape[0], values.shape[1] // count
    return trade(axis, values, columns_of(size), block_at, (count, rows, size), patience)


def join_columns(axis, values):
    count, rows, size = values.shape
    return trade(axis, values, block_at, columns_of(size), (rows, count * size))


def collect(count, parts_ref, slots, send, receive):
    me = lax.axis_index("narrow")
    copies = []
    for step in range(1, count):
        peer = lax.rem(me + step, count)
        copy = push(
            parts_ref.at[peer],
            slots.at[me],
            send.at[step - 1],
            receive.at[me],
            {"narrow": peer},
        )
        copy.start()
        copies.append(copy)
    return copies


def collected(count, parts_ref, slots, send, receive):
    me = lax.axis_index("narrow")
    total = parts_ref[me].astype(FULL)
    for step in range(1, count):
        source = lax.rem(me - step + count, count)
        arrived(slots.at[source], send.at[0], receive.at[source], {"narrow": source})
        total = total + slots[source].astype(FULL)
    return total


def share(count, low, all_ref, send, receive):
    me = lax.axis_index("narrow")
    all_ref[me] = low
    copies = []
    for step in range(1, count):
        peer = lax.rem(me + step, count)
        copy = push(
            all_ref.at[me], all_ref.at[me], send.at[step - 1], receive.at[me], {"narrow": peer}
        )
        copy.start()
        copies.append(copy)
    return copies


def shared(count, all_ref, send, receive):
    me = lax.axis_index("narrow")
    for step in range(1, count):
        source = lax.rem(me - step + count, count)
        arrived(all_ref.at[source], send.at[0], receive.at[source], {"narrow": source})


def narrow_sems(count):
    return [sems(count - 1), sems(count)]


def settle(partial, base, other, keep_row, gain_row):
    count = lax.axis_size("narrow")
    rows, width = base.shape

    def steps(ins, outs, scratch):
        parts_ref, base_ref, other_ref, keep_ref, gain_ref = ins
        own_ref, all_ref = outs
        slots, send, receive, send_all, receive_all = scratch
        copies = collect(count, parts_ref, slots, send, receive)
        yield
        total = collected(count, parts_ref, slots, send, receive)
        total = jnp.where(keep_ref[...] > 0, total + base_ref[...], other_ref[...])
        own_ref[...] = total
        low = norm_rows(total, gain_ref[...]).astype(LOW)
        copies = copies + share(count, low, all_ref, send_all, receive_all)
        yield
        shared(count, all_ref, send_all, receive_all)
        for copy in copies:
            copy.wait_send()

    return Task(
        [partial.reshape(count, rows, width), base, other, keep_row, gain_row],
        [struct((rows, width), FULL), struct((count, rows, width), LOW)],
        [pltpu.VMEM((count, rows, width), partial.dtype)]
        + narrow_sems(count)
        + narrow_sems(count),
        steps,
        VMEM,
        VMEM,
        ["narrow"],
    )


def settle_back(partial, values, add, keep_row, gain_row):
    count = lax.axis_size("narrow")
    rows, width = values.shape

    def steps(ins, outs, scratch):
        parts_ref, values_ref, add_ref, keep_ref, gain_ref = ins
        own_ref, gain_grad_ref, all_ref = outs
        slots, send, receive, send_all, receive_all = scratch
        copies = collect(count, parts_ref, slots, send, receive)
        yield
        grad = collected(count, parts_ref, slots, send, receive)
        held = values_ref[...]
        root = lax.rsqrt(jnp.mean(held * held, axis=-1, keepdims=True) + NORM_EPS)
        scaled = gain_ref[...] * grad
        inner = jnp.mean(held * scaled, axis=-1, keepdims=True)
        own = add_ref[...] + root * scaled - held * (root * root * root * inner)
        gain_grad_ref[...] = jnp.sum(held * root * grad, axis=0, keepdims=True)
        own_ref[...] = own
        low = (own * keep_ref[...]).astype(LOW)
        copies = copies + share(count, low, all_ref, send_all, receive_all)
        yield
        shared(count, all_ref, send_all, receive_all)
        for copy in copies:
            copy.wait_send()

    return Task(
        [partial.reshape(count, rows, width), values, add, keep_row, gain_row],
        [
            struct((rows, width), FULL),
            struct((1, width), FULL),
            struct((count, rows, width), LOW),
        ],
        [pltpu.VMEM((count, rows, width), partial.dtype)]
        + narrow_sems(count)
        + narrow_sems(count),
        steps,
        VMEM,
        VMEM,
        ["narrow"],
    )


def sum_narrow(partial):
    count = lax.axis_size("narrow")
    rows, width = partial.shape[0] // count, partial.shape[1]

    def steps(ins, outs, scratch):
        (parts_ref,), (own_ref,), (slots, send, receive) = ins, outs, scratch
        copies = collect(count, parts_ref, slots, send, receive)
        yield
        yield
        own_ref[...] = collected(count, parts_ref, slots, send, receive)
        for copy in copies:
            copy.wait_send()

    return Task(
        [partial.reshape(count, rows, width)],
        [struct((rows, width), FULL)],
        [pltpu.VMEM((count, rows, width), partial.dtype)] + narrow_sems(count),
        steps,
        VMEM,
        VMEM,
        ["narrow"],
    )


def fetch_rows(found, rows):
    deep, wide = lax.axis_size("narrow"), lax.axis_size("wide")
    columns = found.shape[2]

    def steps(ins, outs, scratch):
        (found_ref,), (out_ref,) = ins, outs
        rightward, leftward, final = scratch[:3]
        send_right, receive_right, send_left, receive_left = scratch[3:7]
        send_wide, receive_wide, local = scratch[7:]
        spot = lax.axis_index("narrow")
        me = lax.axis_index("wide")

        def right_copy(part, source):
            return push(
                source,
                rightward.at[part],
                send_right.at[part],
                receive_right.at[part],
                {"narrow": lax.rem(spot + 1, deep)},
            )

        def left_copy(part, source):
            return push(
                source,
                leftward.at[part],
                send_left.at[part],
                receive_left.at[part],
                {"narrow": lax.rem(spot + deep - 1, deep)},
            )

        for step in range(deep - 1):
            right, left = deep - 1 - step, step

            @pl.when((spot == 0) & (right > 0))
            def _():
                right_copy(right, found_ref.at[right]).start()

            @pl.when((spot == deep - 1) & (left < deep - 1))
            def _():
                left_copy(left, found_ref.at[left]).start()

        yield
        for step in range(deep - 1):
            right, left = deep - 1 - step, step

            @pl.when((spot > 0) & (right > spot))
            def _():
                right_copy(right, rightward.at[right]).wait_recv()
                rightward[right] = rightward[right] + found_ref[right]
                right_copy(right, rightward.at[right]).start()

            @pl.when((spot < deep - 1) & (left < spot))
            def _():
                left_copy(left, leftward.at[left]).wait_recv()
                leftward[left] = leftward[left] + found_ref[left]
                left_copy(left, leftward.at[left]).start()

        final[...] = found_ref[spot]

        @pl.when(spot > 0)
        def _():
            right_copy(spot, rightward.at[spot]).wait_recv()
            final[...] = final[...] + rightward[spot]

        @pl.when(spot < deep - 1)
        def _():
            left_copy(spot, leftward.at[spot]).wait_recv()
            final[...] = final[...] + leftward[spot]

        def rows_for(device):
            return final.at[pl.ds(pl.multiple_of(device * rows, rows), rows)]

        def columns_from(device):
            return columns_of(columns)(out_ref, device)

        copies = []
        for step in range(1, wide):
            peer = lax.rem(me + step, wide)
            copy = push(
                rows_for(peer),
                columns_from(me),
                send_wide.at[step - 1],
                receive_wide.at[me],
                {"wide": peer},
            )
            copy.start()
            copies.append(copy)
        keep = pltpu.make_async_copy(rows_for(me), columns_from(me), local)
        keep.start()
        for step in range(1, wide):
            source = lax.rem(me - step + wide, wide)
            arrived(
                columns_from(source), send_wide.at[0], receive_wide.at[source], {"wide": source}
            )
        yield
        for copy in copies:
            copy.wait_send()
        keep.wait()
        for step in range(deep - 1):
            right, left = deep - 1 - step, step

            @pl.when(right > spot)
            def _():
                right_copy(right, found_ref.at[right]).wait_send()

            @pl.when(left < spot)
            def _():
                left_copy(left, found_ref.at[left]).wait_send()

    task = Task(
        [found],
        [struct((rows, wide * columns), found.dtype)],
        [pltpu.VMEM(found.shape, found.dtype)] * 2
        + [pltpu.VMEM(found.shape[1:], found.dtype)]
        + [sems(deep)] * 4
        + [sems(wide - 1), sems(wide), sems()],
        steps,
        VMEM,
        ANY,
        ["narrow", "wide"],
    )
    return task


def return_rows(rows):
    deep, wide = lax.axis_size("narrow"), lax.axis_size("wide")
    count, width = rows.shape
    columns = width // wide

    def steps(ins, outs, scratch):
        (rows_ref,), (out_ref,) = ins, outs
        send_right, send_left, receive_deep, send_wide, receive_wide, local = scratch
        spot = lax.axis_index("narrow")
        me = lax.axis_index("wide")
        part_of = functools.partial(columns_of(columns), rows_ref)

        def landing(device):
            return out_ref.at[spot, pl.ds(pl.multiple_of(device * count, count), count)]

        copies = []
        for step in range(1, wide):
            peer = lax.rem(me + step, wide)
            copy = push(
                part_of(peer),
                landing(me),
                send_wide.at[step - 1],
                receive_wide.at[me],
                {"wide": peer},
            )
            copy.start()
            copies.append(copy)
        keep = pltpu.make_async_copy(part_of(me), landing(me), local)
        keep.start()
        yield
        for step in range(1, wide):
            source = lax.rem(me - step + wide, wide)
            arrived(landing(source), send_wide.at[0], receive_wide.at[source], {"wide": source})
        keep.wait()

        def right_copy(part):
            return push(
                out_ref.at[part],
                out_ref.at[part],
                send_right.at[part],
                receive_deep.at[part],
                {"narrow": lax.rem(spot + 1, deep)},
            )

        def left_copy(part):
            return push(
                out_ref.at[part],
                out_ref.at[part],
                send_left.at[part],
                receive_deep.at[part],
                {"narrow": lax.rem(spot + deep - 1, deep)},
            )

        @pl.when(spot < deep - 1)
        def _():
            right_copy(spot).start()

        @pl.when(spot > 0)
        def _():
            left_copy(spot).start()

        for step in range(1, deep):
            yield

            @pl.when(spot >= step)
            def _():
                right_copy(spot - step).wait_recv()

                @pl.when(spot < deep - 1)
                def _():
                    right_copy(spot - step).start()

            @pl.when(spot + step < deep)
            def _():
                left_copy(spot + step).wait_recv()

                @pl.when(spot > 0)
                def _():
                    left_copy(spot + step).start()

        for part in range(deep):

            @pl.when((part <= spot) & (spot < deep - 1))
            def _():
                right_copy(part).wait_send()

            @pl.when((part >= spot) & (spot > 0))
            def _():
                left_copy(part).wait_send()

        for copy in copies:
            copy.wait_send()

    return Task(
        [rows],
        [struct((deep, wide * count, columns), rows.dtype)],
        [sems(deep)] * 3 + [sems(wide - 1), sems(wide), sems()],
        steps,
        ANY,
        ANY,
        ["narrow", "wide"],
    )


def sum_wide(partial):
    count = lax.axis_size("wide")
    chips = count // 2
    rows, width = partial.shape[0] // count, partial.shape[1]

    def steps(ins, outs, scratch):
        (parts_ref,), (out_ref,) = ins, outs
        from_mate, paired, slots, send_mate, receive_mate, send, receive = scratch
        me = lax.axis_index("wide")
        side = lax.rem(me, 2)
        mate = me + 1 - 2 * side
        my_chip = me // 2
        mate_copies = []
        for step in range(chips):
            chip = lax.rem(my_chip + 1 + step, chips)
            copy = push(
                parts_ref.at[2 * chip + 1 - side],
                from_mate.at[chip],
                send_mate.at[step],
                receive_mate.at[chip],
                {"wide": mate},
            )
            copy.start()
            mate_copies.append(copy)
        yield
        copies = []
        for step in range(chips):
            chip = lax.rem(my_chip + 1 + step, chips)
            arrived(from_mate.at[chip], send_mate.at[0], receive_mate.at[chip], {"wide": mate})
            both = parts_ref[2 * chip + side].astype(FULL) + from_mate[chip].astype(FULL)
            if step < chips - 1:
                paired[chip] = both.astype(LOW)
                copy = push(
                    paired.at[chip],
                    slots.at[my_chip],
                    send.at[step],
                    receive.at[my_chip],
                    {"wide": 2 * chip + side},
                )
                copy.start()
                copies.append(copy)
            else:
                out_ref[...] = both
        yield
        for step in range(1, chips):
            chip = lax.rem(my_chip - step + chips, chips)
            arrived(slots.at[chip], send.at[0], receive.at[chip], {"wide": 2 * chip + side})
            out_ref[...] = out_ref[...] + slots[chip].astype(FULL)
        for copy in mate_copies + copies:
            copy.wait_send()

    return Task(
        [partial.reshape(count, rows, width)],
        [struct((rows, width), FULL)],
        [pltpu.VMEM((chips, rows, width), LOW)] * 3
        + [sems(chips), sems(chips), sems(max(chips - 1, 1)), sems(chips)],
        steps,
        VMEM,
        VMEM,
        ["wide"],
    )


def merge_stats(first, second):
    peak = jnp.maximum(first[0:1], second[0:1])
    total = first[1:2] * jnp.exp(first[0:1] - peak) + second[1:2] * jnp.exp(second[0:1] - peak)
    return jnp.concatenate([peak, total, first[2:3] + second[2:3]], axis=0)


def add_two(first, second):
    return first + second


def combine(values, join):
    deep, wide = lax.axis_size("narrow"), lax.axis_size("wide")

    def steps(ins, outs, scratch):
        (x_ref,), (out_ref,) = ins, outs
        wide_slots, deep_slots, send_wide, receive_wide, send_deep, receive_deep = scratch

        def start(axis, count, slots, value, send, receive):
            me = lax.axis_index(axis)
            slots[me] = value
            copies = []
            for step in range(1, count):
                peer = lax.rem(me + step, count)
                copy = push(
                    slots.at[me], slots.at[me], send.at[step - 1], receive.at[me], {axis: peer}
                )
                copy.start()
                copies.append(copy)
            return copies

        def finish(axis, count, slots, send, receive):
            me = lax.axis_index(axis)
            for step in range(1, count):
                source = lax.rem(me - step + count, count)
                arrived(slots.at[source], send.at[0], receive.at[source], {axis: source})
            total = slots[0]
            for source in range(1, count):
                total = join(total, slots[source])
            return total

        first = start("wide", wide, wide_slots, x_ref[...], send_wide, receive_wide)
        yield
        total = finish("wide", wide, wide_slots, send_wide, receive_wide)
        second = start("narrow", deep, deep_slots, total, send_deep, receive_deep)
        yield
        out_ref[...] = finish("narrow", deep, deep_slots, send_deep, receive_deep)
        for copy in first + second:
            copy.wait_send()

    return Task(
        [values],
        [like(values)],
        [
            pltpu.VMEM((wide,) + values.shape, values.dtype),
            pltpu.VMEM((deep,) + values.shape, values.dtype),
            sems(wide - 1),
            sems(wide),
            sems(deep - 1),
            sems(deep),
        ],
        steps,
        VMEM,
        VMEM,
        ["narrow", "wide"],
    )


def gather_both(values):
    deep, wide = lax.axis_size("narrow"), lax.axis_size("wide")

    def steps(ins, outs, scratch):
        (x_ref,), (out_ref,) = ins, outs
        send_wide, receive_wide, send_deep, receive_deep = scratch
        me = lax.axis_index("wide")
        spot = lax.axis_index("narrow")
        out_ref[spot, me] = x_ref[...]
        copies = []
        for step in range(1, wide):
            peer = lax.rem(me + step, wide)
            block = out_ref.at[spot, me]
            copy = push(block, block, send_wide.at[step - 1], receive_wide.at[me], {"wide": peer})
            copy.start()
            copies.append(copy)
        yield
        for step in range(1, wide):
            source = lax.rem(me - step + wide, wide)
            block = out_ref.at[spot, source]
            arrived(block, send_wide.at[0], receive_wide.at[source], {"wide": source})
        for step in range(1, deep):
            peer = lax.rem(spot + step, deep)
            block = out_ref.at[spot]
            copy = push(
                block, block, send_deep.at[step - 1], receive_deep.at[spot], {"narrow": peer}
            )
            copy.start()
            copies.append(copy)
        yield
        for step in range(1, deep):
            source = lax.rem(spot - step + deep, deep)
            block = out_ref.at[source]
            arrived(block, send_deep.at[0], receive_deep.at[source], {"narrow": source})
        for copy in copies:
            copy.wait_send()

    return Task(
        [values],
        [struct((deep, wide) + values.shape, values.dtype)],
        [sems(wide - 1), sems(wide), sems(deep - 1), sems(deep)],
        steps,
        VMEM,
        VMEM,
        ["narrow", "wide"],
    )


def feed_body(inner_ref, weight_ref, gate_ref, up_ref, hidden_ref, out_ref, total):
    part = pl.program_id(0)
    inner = inner_ref[...]
    gate = dot(inner, weight_ref[0, 0], 1, 1)
    up = dot(inner, weight_ref[0, 1], 1, 1)
    hidden = (jax.nn.silu(gate) * up).astype(LOW)
    gate_ref[0] = gate
    up_ref[0] = up
    hidden_ref[0] = hidden
    product = dot(hidden, weight_ref[0, 2], 1, 0)

    @pl.when(part == 0)
    def _():
        total[...] = product

    @pl.when(part > 0)
    def _():
        total[...] = total[...] + product

    @pl.when(part == pl.num_programs(0) - 1)
    def _():
        out_ref[...] = total[...].astype(LOW)


def feed(inner, weight):
    parts, _, size, width = weight.shape
    sel = inner.shape[0]
    same = pl.BlockSpec((sel, width), lambda part: (0, 0))
    slab = pl.BlockSpec((1, sel, size), lambda part: (part, 0, 0))
    return pl.pallas_call(
        feed_body,
        grid=(parts,),
        in_specs=[same, pl.BlockSpec((1, 3, size, width), lambda part: (part, 0, 0, 0))],
        out_specs=[slab, slab, slab, same],
        out_shape=[
            struct((parts, sel, size), FULL),
            struct((parts, sel, size), FULL),
            struct((parts, sel, size), LOW),
            struct((sel, width), LOW),
        ],
        scratch_shapes=[pltpu.VMEM((sel, width), FULL)],
        compiler_params=pltpu.CompilerParams(vmem_limit_bytes=VMEM_BYTES),
        cost_estimate=pl.CostEstimate(
            flops=6 * sel * parts * size * width,
            bytes_accessed=weight.size * 2,
            transcendentals=0,
        ),
        name="feed",
    )(inner, weight)


def feed_back_body(grad_ref, weight_ref, gate_ref, up_ref, hidden_ref, acts_ref, out_ref, total):
    part = pl.program_id(0)
    grad_hidden = dot(grad_ref[...], weight_ref[0, 2], 1, 1)
    gate = gate_ref[0]
    sigma = jax.nn.sigmoid(gate)
    grad_gate = (grad_hidden * up_ref[0] * sigma * (1.0 + gate * (1.0 - sigma))).astype(LOW)
    grad_up = (grad_hidden * gate * sigma).astype(LOW)
    acts_ref[0, 0] = grad_gate
    acts_ref[0, 1] = grad_up
    acts_ref[0, 2] = hidden_ref[0]
    product = dot(grad_gate, weight_ref[0, 0], 1, 0) + dot(grad_up, weight_ref[0, 1], 1, 0)

    @pl.when(part == 0)
    def _():
        total[...] = product

    @pl.when(part > 0)
    def _():
        total[...] = total[...] + product

    @pl.when(part == pl.num_programs(0) - 1)
    def _():
        out_ref[...] = total[...].astype(LOW)


def feed_back(grad, weight, gate, up, hidden):
    parts, _, size, width = weight.shape
    sel = grad.shape[0]
    same = pl.BlockSpec((sel, width), lambda part: (0, 0))
    slab = pl.BlockSpec((1, sel, size), lambda part: (part, 0, 0))
    return pl.pallas_call(
        feed_back_body,
        grid=(parts,),
        in_specs=[same, pl.BlockSpec((1, 3, size, width), lambda part: (part, 0, 0, 0))]
        + [slab] * 3,
        out_specs=[pl.BlockSpec((1, 3, sel, size), lambda part: (part, 0, 0, 0)), same],
        out_shape=[struct((parts, 3, sel, size), LOW), struct((sel, width), LOW)],
        scratch_shapes=[pltpu.VMEM((sel, width), FULL)],
        compiler_params=pltpu.CompilerParams(vmem_limit_bytes=VMEM_BYTES),
        cost_estimate=pl.CostEstimate(
            flops=6 * sel * parts * size * width,
            bytes_accessed=weight.size * 2,
            transcendentals=0,
        ),
        name="feed_back",
    )(grad, weight, gate, up, hidden)


def newton_steps(problems):
    rows, width = problems[0][0].shape
    block = min(512, width)
    eye = lax.broadcasted_iota(jnp.int32, (rows, rows), 0) == lax.broadcasted_iota(
        jnp.int32, (rows, rows), 1
    )

    def strip(part):
        return pl.ds(pl.multiple_of(part * block, block), block)

    def over(function, start):
        return lax.fori_loop(0, width // block, function, start)

    def add_squares(part, totals):
        values = [current[:, strip(part)] for current, low, gram, rest in problems]
        return [total + jnp.sum(value * value) for total, value in zip(totals, values)]

    totals = over(add_squares, [jnp.float32(0.0)] * len(problems))
    scales = [1.0 / (jnp.sqrt(total) + 1e-07) for total in totals]

    def begin(part, carry):
        for scale, (current, low, gram, rest) in zip(scales, problems):
            values = current[:, strip(part)] * scale
            current[:, strip(part)] = values
            low[:, strip(part)] = values.astype(LOW)
        return carry

    over(begin, 0)

    def iteration(turn, carry):
        for current, low, gram, rest in problems:
            gram[...] = jnp.zeros_like(gram)

        def add_gram(part, carry):
            for current, low, gram, rest in problems:
                values = low[:, strip(part)]
                gram[...] = gram[...] + dot(values, values, 1, 1)
            return carry

        over(add_gram, 0)
        seconds = []
        for current, low, gram, rest in problems:
            whole = gram[...]
            middle = jnp.sum(jnp.where(eye, whole, 0.0)) / rows
            rest[...] = (whole - jnp.where(eye, middle, 0.0)).astype(LOW)
            square = dot(rest[...], rest[...], 1, 0)
            whole = gram[...]
            centred = whole - jnp.where(eye, middle, 0.0)
            square = square + 2.0 * middle * centred + jnp.where(eye, middle * middle, 0.0)
            whole = NEWTON_B * whole + NEWTON_C * square
            second = jnp.sum(jnp.where(eye, whole, 0.0)) / rows
            rest[...] = (whole - jnp.where(eye, second, 0.0)).astype(LOW)
            seconds.append(second)

        def apply(part, carry):
            for second, (current, low, gram, rest) in zip(seconds, problems):
                values = (NEWTON_A + second) * current[:, strip(part)] + dot(
                    rest[...], low[:, strip(part)], 1, 0
                )
                current[:, strip(part)] = values
                low[:, strip(part)] = values.astype(LOW)
            return carry

        over(apply, 0)
        return carry

    lax.fori_loop(0, NS_STEPS, iteration, 0)


def newton_scratch(rows, width):
    return [
        pltpu.VMEM((rows, width), FULL),
        pltpu.VMEM((rows, width), LOW),
        pltpu.VMEM((rows, rows), FULL),
        pltpu.VMEM((rows, rows), LOW),
    ]


def newton_cost(count, rows, width):
    return pl.CostEstimate(
        flops=NS_STEPS * count * (4 * rows * rows * width + 2 * rows * rows * rows),
        bytes_accessed=6 * count * rows * width,
        transcendentals=0,
    )


def newton_body(factor_ref, mom_ref, grad_ref, out_ref, *problem):
    current, low = problem[:2]
    parts, rows, columns = mom_ref.shape
    factor = factor_ref[0]
    for part in range(parts):
        spot = slice(part * columns, (part + 1) * columns)
        current[:, spot] = MOMENTUM * mom_ref[part].astype(FULL) + factor * grad_ref[
            :, spot
        ].astype(FULL)
    newton_steps([problem])
    for part in range(parts):
        out_ref[part] = low[:, part * columns : (part + 1) * columns]


def newton(factor, mom, grad):
    parts, rows, columns = mom.shape
    width = parts * columns
    return pl.pallas_call(
        newton_body,
        in_specs=[pl.BlockSpec(memory_space=pltpu.SMEM), VMEM, VMEM],
        out_specs=VMEM,
        out_shape=struct(mom.shape, LOW),
        scratch_shapes=newton_scratch(rows, width),
        compiler_params=pltpu.CompilerParams(vmem_limit_bytes=VMEM_BYTES),
        cost_estimate=newton_cost(1, rows, width),
        name="newton",
    )(factor.reshape(1), mom, grad)


def newton_small_body(rows, factor_ref, mom_ref, grad_ref, kv_ref, out_ref, *scratch):
    problems = [scratch[4 * at : 4 * at + 4] for at in range(4)]
    parts, _, columns = mom_ref.shape
    piece_rows = 2 * rows // parts
    kv_columns = kv_ref.shape[2]
    half = rows // 2
    factor = factor_ref[0]
    for part in range(parts):
        spot = slice(part * columns, (part + 1) * columns)
        for member in range(2):
            current = problems[member][0]
            current[:, spot] = MOMENTUM * mom_ref[
                part, member * rows : (member + 1) * rows, :
            ].astype(FULL)
        for block in range(parts):
            current = problems[block // (parts // 2)][0]
            at = block % (parts // 2) * piece_rows
            piece = grad_ref[part, 0:piece_rows, block * columns : (block + 1) * columns]
            current[at : at + piece_rows, spot] = (
                current[at : at + piece_rows, spot] + factor * piece.astype(FULL)
            )
        spot = slice(part * kv_columns, (part + 1) * kv_columns)
        for member in range(2):
            current = problems[2 + member][0]
            piece = kv_ref[part, member * rows : (member + 1) * rows, :].astype(FULL)
            for side in range(2):
                lane = (2 * member + side) * kv_columns
                mom = mom_ref[part, 2 * rows : 2 * rows + half, lane : lane + kv_columns]
                here = slice(side * half, (side + 1) * half)
                current[here, spot] = MOMENTUM * mom.astype(FULL) + factor * piece[here]
    newton_steps(problems[:2])
    newton_steps(problems[2:])
    out_ref[...] = jnp.zeros_like(out_ref)
    for part in range(parts):
        for member in range(2):
            out_ref[part, member * rows : (member + 1) * rows, :] = problems[member][1][
                :, part * columns : (part + 1) * columns
            ]
            low = problems[2 + member][1]
            for side in range(2):
                lane = (2 * member + side) * kv_columns
                out_ref[part, 2 * rows : 2 * rows + half, lane : lane + kv_columns] = low[
                    side * half : (side + 1) * half,
                    part * kv_columns : (part + 1) * kv_columns,
                ]


def newton_small(factor, mom, grad, kv_grad):
    parts, _, columns = mom.shape
    rows = kv_grad.shape[1] // 2
    kv_width = parts * kv_grad.shape[2]
    return pl.pallas_call(
        functools.partial(newton_small_body, rows),
        in_specs=[pl.BlockSpec(memory_space=pltpu.SMEM), VMEM, VMEM, VMEM],
        out_specs=VMEM,
        out_shape=struct(mom.shape, LOW),
        scratch_shapes=newton_scratch(rows, parts * columns) * 2
        + newton_scratch(rows, kv_width) * 2,
        compiler_params=pltpu.CompilerParams(vmem_limit_bytes=VMEM_BYTES),
        cost_estimate=newton_cost(2, rows, parts * columns),
        name="newton_small",
    )(factor.reshape(1), mom, grad, kv_grad)


def lookup_body(ids_ref, turn_ref, table_ref, out_ref, low_ref, list_ref, held, rows, sem):
    vocab = table_ref.shape[0]
    count = out_ref.shape[0]
    load = pltpu.make_async_copy(table_ref, held, sem)
    load.start()
    rows[...] = jnp.zeros_like(rows)

    found = turn_ref[count]

    def note(group, carry):
        for member in range(UNROLL):
            at = group * UNROLL + member
            list_ref[turn_ref[at]] = at
        return carry

    lax.fori_loop(0, count // UNROLL, note, 0)
    for member in range(UNROLL):
        list_ref[found + member] = count
    list_ref[count + UNROLL] = found
    load.wait()

    def step(group, carry):
        for member in range(UNROLL):
            at = list_ref[group * UNROLL + member]
            spot = jnp.minimum(ids_ref[jnp.minimum(at, count - 1)], vocab - 1)
            rows[pl.ds(at, 1), :] = held[pl.ds(spot, 1), :]
        return carry

    lax.fori_loop(0, (found + UNROLL - 1) // UNROLL, step, 0)
    out_ref[...] = rows[pl.ds(0, count), :].astype(LOW)
    low_ref[...] = held[...].astype(LOW)


def lookup(table, ids):
    vocab, columns = table.shape
    count = ids.shape[0]
    mine = (ids < vocab).reshape(-1, 128)
    before = jnp.arange(128)[:, None] < jnp.arange(128)[None, :]
    in_row = dot(mine.astype(LOW), before.astype(LOW), 1, 0)
    per_row = jnp.sum(mine.astype(FULL), axis=1)
    lines = jnp.arange(mine.shape[0])
    ahead = jnp.sum(jnp.where(lines[:, None] > lines[None, :], per_row[None, :], 0.0), axis=1)
    found = jnp.sum(per_row).astype(jnp.int32)
    turns = (in_row + ahead[:, None]).astype(jnp.int32)
    turns = jnp.where(mine, turns, count + UNROLL + 1).reshape(-1)
    turns = jnp.concatenate([turns, jnp.full((128,), found)])
    return pl.pallas_call(
        lookup_body,
        in_specs=[pl.BlockSpec(memory_space=pltpu.SMEM)] * 2 + [ANY],
        out_specs=[VMEM, VMEM, pl.BlockSpec(memory_space=pltpu.SMEM)],
        scratch_shapes=[
            pltpu.VMEM((vocab, columns), FULL),
            pltpu.VMEM((count + 8, columns), FULL),
            pltpu.SemaphoreType.DMA,
        ],
        out_shape=[
            struct((count, columns), LOW),
            struct((vocab, columns), LOW),
            struct((count + 2 * UNROLL,), jnp.int32),
        ],
        compiler_params=pltpu.CompilerParams(vmem_limit_bytes=VMEM_BYTES),
        cost_estimate=pl.CostEstimate(
            flops=0, bytes_accessed=vocab * columns * 4, transcendentals=0
        ),
        name="lookup",
    )(ids, turns, table)


def spread_body(
    ids_ref, list_ref, rows_ref, head_ref, out_ref, square_ref, even, odd, rows, sem
):
    vocab = out_ref.shape[0]
    count = rows_ref.shape[0]
    chunk = 256

    def strip(part):
        return pl.ds(pl.multiple_of(part * chunk, chunk), chunk)

    def begin(part, carry):
        even[strip(part), :] = head_ref[strip(part), :].astype(FULL)
        odd[strip(part), :] = jnp.zeros((chunk, odd.shape[1]), FULL)
        return carry

    lax.fori_loop(0, vocab // chunk, begin, 0)

    def widen(part, carry):
        rows[strip(part), :] = rows_ref[strip(part), :].astype(FULL)
        return carry

    lax.fori_loop(0, count // chunk, widen, 0)
    rows[pl.ds(count, 8), :] = jnp.zeros((8, rows.shape[1]), FULL)

    def step(group, carry):
        for member in range(UNROLL):
            at = list_ref[group * UNROLL + member]
            spot = jnp.minimum(ids_ref[jnp.minimum(at, count - 1)], vocab - 1)
            total = even if member % 2 == 0 else odd
            total[pl.ds(spot, 1), :] = total[pl.ds(spot, 1), :] + rows[pl.ds(at, 1), :]
        return carry

    found = list_ref[count + UNROLL]
    lax.fori_loop(0, (found + UNROLL - 1) // UNROLL, step, 0)

    def finish(part, squares):
        value = even[strip(part), :] + odd[strip(part), :]
        even[strip(part), :] = value
        return squares + jnp.sum((value * value).reshape(chunk // 8, 8, -1), axis=0)

    square_ref[...] = lax.fori_loop(
        0, vocab // chunk, finish, jnp.zeros((8, even.shape[1]), FULL)
    )
    store = pltpu.make_async_copy(even, out_ref, sem)
    store.start()
    store.wait()


def spread(ids, listed, rows, head):
    vocab, columns = head.shape
    count = ids.shape[0]
    smem = pl.BlockSpec(memory_space=pltpu.SMEM)
    return pl.pallas_call(
        spread_body,
        in_specs=[smem, smem, VMEM, VMEM],
        out_specs=[ANY, VMEM],
        scratch_shapes=[
            pltpu.VMEM((vocab, columns), FULL),
            pltpu.VMEM((vocab, columns), FULL),
            pltpu.VMEM((count + 8, columns), FULL),
            pltpu.SemaphoreType.DMA,
        ],
        out_shape=[struct((vocab, columns), FULL), struct((8, columns), FULL)],
        compiler_params=pltpu.CompilerParams(vmem_limit_bytes=VMEM_BYTES),
        cost_estimate=pl.CostEstimate(
            flops=count * columns, bytes_accessed=vocab * columns * 8, transcendentals=0
        ),
        name="spread",
    )(ids, listed, rows, head)


def adamw(weight, first_m, second_m, grad, rate, decay):
    first_new = BETA_ONE * first_m + (1.0 - BETA_ONE) * grad
    second_new = BETA_TWO * second_m + (1.0 - BETA_TWO) * grad * grad
    update = (
        first_new
        / (1.0 - BETA_ONE**STEP)
        / (jnp.sqrt(second_new / (1.0 - BETA_TWO**STEP)) + ADAM_EPS)
    )
    return (weight * (1.0 - rate * decay) - rate * update, first_new, second_new)


def cut_columns(values, count):
    rows, columns = values.shape
    return jnp.moveaxis(values.reshape(rows, count, columns // count), 1, 0)


def shifted(parts, axis, step):
    count = lax.axis_size(axis)
    pairs = [(source, (source + step) % count) for source in range(count)]
    return lax.ppermute(parts, axis, pairs)


def per_device(
    tokens,
    picks,
    targets,
    lengths,
    skip,
    embed,
    embed_m,
    embed_v,
    attn_qo,
    attn_qo_mom,
    attn_kv,
    attn_kv_mom,
    ffn,
    ffn_mom,
    gains,
    gains_m,
    gains_v,
):
    wide_count = lax.axis_size("wide")
    narrow_count = lax.axis_size("narrow")
    narrow_spot = lax.axis_index("narrow")
    wide_spot = lax.axis_index("wide")
    seq_len = tokens.shape[1]
    sel = picks.shape[1]
    vocab_rows, columns = embed.shape
    width = columns * wide_count
    own_rows = sel // narrow_count
    tok_rows = seq_len // narrow_count
    all_rows = own_rows + tok_rows
    heads_own = HEADS // narrow_count
    head_cols = heads_own * HD
    repeat = max(1, narrow_count // KVH)
    groups = KVH * repeat // narrow_count
    ffn_rows = ffn.shape[0]
    ffn_size = ffn_rows // narrow_count
    total_rows = wide_count * sel
    lens = lengths[0]
    pick_ids = picks[0]
    keep_layer = (1 - skip[0]).astype(FULL)
    keep_row = jnp.full((1, width), keep_layer)
    lanes = 128

    def box(flat):
        height = -(-flat.shape[0] // (8 * lanes)) * 8
        return jnp.pad(flat, (0, height * lanes - flat.shape[0])).reshape(height, lanes)

    ffn_low = jnp.moveaxis(ffn, 1, 0).astype(LOW)
    ffn_cut = ffn_low.reshape(3, narrow_count, ffn_size, ffn_low.shape[2])
    ffn_cut = jnp.moveaxis(ffn_cut, 1, 0).reshape(narrow_count, 3 * ffn_size, -1)
    kv_own = attn_kv.reshape(columns, -1).astype(LOW)

    where_at = jnp.arange(seq_len, dtype=jnp.int32)
    pick_tokens = jnp.sum(
        jnp.where(pick_ids[:, None] == where_at[None, :], tokens[0][None, :], 0), axis=1
    )
    ints = box(jnp.concatenate([tokens[0], pick_tokens, targets[0]]))
    all_ints, all_gains, kv_part, ffn_sub = launch(
        [
            gather_wide(ints),
            gather_both(box(gains.astype(LOW).astype(FULL).reshape(-1))),
            gather_blocks("narrow", kv_own),
            join_columns("narrow", ffn_cut),
        ],
        0,
        "gather_ids",
    )
    kv_part = jnp.moveaxis(kv_part, 0, 1).reshape(columns, -1)
    proj_own = jnp.concatenate([attn_qo.reshape(columns, -1).astype(LOW), kv_part], axis=1)
    proj = lax.all_gather(proj_own, "wide", axis=0, tiled=True)
    ffn_w = lax.all_gather(ffn_sub.reshape(3, ffn_size, width), "wide", axis=0)
    gain_size = gains.shape[1]
    gain_w = all_gains.reshape(narrow_count, wide_count, -1)[:, :, : 3 * gain_size]
    gain_w = gain_w.reshape(narrow_count, wide_count, 3, gain_size)
    gain_w = jnp.transpose(gain_w, (2, 1, 0, 3)).reshape(3, width)
    all_ints = all_ints.reshape(wide_count, -1)
    tokens_all = all_ints[:, :seq_len].reshape(wide_count, narrow_count, tok_rows)
    picked_all = all_ints[:, seq_len : seq_len + sel].reshape(wide_count, narrow_count, own_rows)
    targets_all = all_ints[:, seq_len + sel : seq_len + 2 * sel].reshape(-1)
    wanted = jnp.moveaxis(jnp.concatenate([tokens_all, picked_all], axis=2), 1, 0).reshape(-1)
    local_ids = wanted - narrow_spot * vocab_rows
    inside = (local_ids >= 0) & (local_ids < vocab_rows)
    spots = jnp.where(inside, local_ids, vocab_rows)
    found, embed_low, listed = lookup(embed, spots)
    found = found.reshape(narrow_count, wide_count * all_rows, columns)
    embed_cut = embed_low.reshape(wide_count, vocab_rows // wide_count, columns)
    rows_low, table_own = launch(
        [fetch_rows(found, all_rows), join_columns("wide", embed_cut)], 1, "fetch_rows"
    )

    mom_qo = jnp.moveaxis(attn_qo_mom, 1, 0)
    mom_kv = jnp.moveaxis(attn_kv_mom, 1, 0)
    mom_ffn = jnp.moveaxis(ffn_mom, 1, 0)
    slot_rows, slot_cols = mom_ffn.shape[1:]

    block_rows, q_size = mom_qo.shape[1:]
    kv_size = mom_kv.shape[2]
    half_rows = block_rows // 2
    kv_box = jnp.moveaxis(mom_kv.reshape(4, half_rows, kv_size), 0, 1).reshape(half_rows, -1)
    small_box = jnp.concatenate([mom_qo.reshape(2 * block_rows, q_size), kv_box])
    small_box = jnp.pad(small_box, ((0, slot_rows - small_box.shape[0]), (0, 0)))
    mom_parts = jnp.concatenate([mom_ffn, small_box[None]]).astype(LOW)

    seg_all = segments_at(lens, where_at)
    tok_at = narrow_spot * tok_rows + jnp.arange(tok_rows, dtype=jnp.int32)
    _, cosine_all, sine_all = angles_at(lens, where_at)
    _, cosine_tok, sine_tok = angles_at(lens, tok_at)
    seg_mine, cosine, sine = angles_at(lens, pick_ids)

    q_w, o_w, kv_w = (
        proj[:, :head_cols],
        proj[:, head_cols : 2 * head_cols],
        proj[:, 2 * head_cols :],
    )

    rows_full = rows_low.astype(FULL)
    normed_all = norm_rows(rows_full, gain_w[0]).astype(LOW)
    normed_tok, normed_own = normed_all[:tok_rows], normed_all[tok_rows:]
    kv_part = dot(normed_tok, kv_w, 1, 0).reshape(tok_rows, narrow_count, 2, kv_size)
    kv_part = jnp.moveaxis(kv_part, 2, 0).reshape(2, tok_rows, KVH, HD)
    keys_part = rotate(kv_part[0], cosine_tok[:, None], sine_tok[:, None]).astype(LOW)
    values_part = kv_part[1].astype(LOW)
    by_head = jnp.moveaxis(jnp.stack([keys_part, values_part]), 2, 0)
    by_head = jnp.repeat(by_head, repeat, axis=0)
    by_head = by_head.reshape(narrow_count, groups, 2, tok_rows, HD)
    own_head, start_low, tok_cols = launch(
        [
            swap_blocks("narrow", by_head),
            gather_blocks("narrow", rows_low[tok_rows:]),
            split_columns("wide", normed_tok),
        ],
        2,
        "trade_heads",
    )
    start_low, ffn_w = lax.optimization_barrier((start_low, ffn_w))
    own_head = jnp.transpose(own_head, (2, 1, 0, 3, 4)).reshape(2, groups, seq_len, HD)
    keys, values = own_head[0], own_head[1]
    start_h = start_low.reshape(sel, width).astype(FULL)

    normed = norm_rows(start_h, gain_w[0]).astype(LOW)
    queries = dot(normed, q_w, 1, 0).reshape(sel, heads_own, HD)
    queries = rotate(queries, cosine[:, None], sine[:, None]).astype(LOW)
    grouped = queries.reshape(sel, groups, heads_own // groups, HD)
    scale = HD ** (-0.5)
    scores = jnp.einsum("tkgd,ksd->kgts", grouped, keys, preferred_element_type=FULL) * scale
    allowed = (seg_mine[:, None] == seg_all[None, :]) & (pick_ids[:, None] >= where_at[None, :])
    scores = jnp.where(allowed, scores, MASKED)
    shifted_exp = jnp.exp(scores - jnp.max(scores, axis=-1, keepdims=True))
    probs = shifted_exp / jnp.sum(shifted_exp, axis=-1, keepdims=True)
    probs_low = probs.astype(LOW)
    mixed = jnp.einsum("kgts,ksd->tkgd", probs_low, values, preferred_element_type=FULL)
    mixed = mixed.reshape(sel, head_cols).astype(LOW)

    early_part = norm_rows(start_h, gain_w[2]).astype(LOW)
    early = lax.all_gather(early_part, "wide", axis=0, tiled=True)
    start_own = lax.dynamic_slice_in_dim(start_h, narrow_spot * own_rows, own_rows, 0)
    middle, inner, mixed_wide, pick_cols = launch(
        [
            settle(
                dot(mixed, o_w, 1, 1).astype(LOW),
                start_own,
                start_own,
                jnp.ones((1, width), FULL),
                gain_w[1:2],
            ),
            gather_wide(mixed),
            split_columns("wide", normed),
        ],
        3,
        "settle_middle",
    )
    inner = inner.reshape(sel, width)
    inner_all = lax.all_gather(inner, "wide", axis=0, tiled=True)
    gate, up, hidden, fed = feed(inner, ffn_w)
    final_own, late_part = launch(
        [settle(fed, middle, start_own, keep_row, gain_w[2:3])], 4, "settle_late"
    )

    table_count = table_own.shape[0]
    local_target = targets_all - (narrow_spot * vocab_rows + wide_spot * table_count)
    has_target = local_target[:, None] == jnp.arange(table_count, dtype=jnp.int32)[None, :]
    counted = (targets_all >= 0).astype(FULL)
    loss_count = jnp.sum(counted)

    def exit_logits(features):
        logits = dot(features, table_own, 1, 1)
        peak = jnp.max(logits, axis=-1)
        total = jnp.sum(jnp.exp(logits - peak[:, None]), axis=-1)
        picked = jnp.sum(jnp.where(has_target, logits, 0.0), axis=-1)
        return logits, jnp.stack([peak, total, picked])

    half = slot_rows // 2
    late, mom_top = launch(
        [
            gather_wide(late_part.reshape(sel, width)),
            swap_turned(mom_parts[:, :half]),
        ],
        5,
        "gather_late",
    )
    late = late.reshape(total_rows, width)
    early_logits, early_stats = exit_logits(early)
    late_logits, late_stats = exit_logits(late)
    stats = jnp.concatenate([early_stats, late_stats], axis=1).reshape(3, 8, -1)
    stats = launch([combine(stats, merge_stats)], 6, "combine_stats")[0]
    stats, inner_all = lax.optimization_barrier((stats, inner_all))
    stats = stats.reshape(3, -1)
    log_norms = stats[0] + jnp.log(stats[1])
    losses = log_norms - stats[2]
    loss_sum = jnp.sum(
        counted * (EXIT_EARLY * losses[:total_rows] + EXIT_LAST * losses[total_rows:])
    )

    def exit_back(logits, log_norm, weight, features):
        grad_logits = (
            (jnp.exp(logits - log_norm[:, None]) - has_target.astype(FULL))
            * (weight * counted)[:, None]
        ).astype(LOW)
        return dot(grad_logits, table_own, 1, 0).astype(LOW), dot(grad_logits, features, 0, 0)

    late_back, late_head = exit_back(late_logits, log_norms[total_rows:], EXIT_LAST, late)
    early_back, early_head = exit_back(early_logits, log_norms[:total_rows], EXIT_EARLY, early)
    grad_late, mom_low = launch(
        [sum_wide(late_back), swap_turned(mom_parts[:, half:])], 7, "sum_late"
    )
    mom_owned = jnp.concatenate([mom_top, mom_low], axis=1)
    grad_head = (early_head + late_head).astype(LOW)

    grad_early = lax.psum_scatter(early_back, "wide", scatter_dimension=0, tiled=True)
    grad_final, gain_late, grad_out = launch(
        [
            settle_back(
                grad_late.astype(LOW),
                final_own,
                jnp.zeros_like(final_own),
                keep_row,
                gain_w[2:3],
            ),
        ],
        8,
        "back_late",
    )
    grad_layer = grad_final * keep_layer
    grad_out = grad_out.reshape(sel, width)
    out_all = lax.all_gather(grad_out, "wide", axis=0, tiled=True)
    acts, fed_back = feed_back(grad_out, ffn_w, gate, up, hidden)
    grad_mid, gain_mid, grad_branch = launch(
        [settle_back(fed_back, middle, grad_layer, keep_row, gain_w[1:2])], 9, "back_middle"
    )
    grad_branch, grad_early = lax.optimization_barrier((grad_branch, grad_early))
    grad_branch = grad_branch.reshape(sel, width)

    grad_mixed = dot(grad_branch, o_w, 1, 0).astype(LOW)
    grouped_grad = grad_mixed.reshape(sel, groups, heads_own // groups, HD)
    grad_probs = jnp.einsum("tkgd,ksd->kgts", grouped_grad, values, preferred_element_type=FULL)
    grad_scores = (
        probs * (grad_probs - jnp.sum(probs * grad_probs, axis=-1, keepdims=True))
    ).astype(LOW)
    grad_queries = (
        jnp.einsum("kgts,ksd->tkgd", grad_scores, keys, preferred_element_type=FULL) * scale
    ).reshape(sel, heads_own, HD)
    grad_queries = (
        unrotate(grad_queries, cosine[:, None], sine[:, None])
        .reshape(sel, head_cols)
        .astype(LOW)
    )
    grad_keys = jnp.einsum("kgts,tkgd->ksd", grad_scores, grouped, preferred_element_type=FULL)
    grad_keys = unrotate(grad_keys * scale, cosine_all, sine_all).astype(LOW)
    grad_values = jnp.einsum(
        "kgts,tkgd->ksd", probs_low, grouped_grad, preferred_element_type=FULL
    ).astype(LOW)
    kv_parts = jnp.stack([grad_keys, grad_values]).reshape(
        2, groups, narrow_count, tok_rows, HD
    )
    kv_parts = jnp.transpose(kv_parts, (2, 1, 0, 3, 4))
    pick_part = dot(grad_queries, q_w, 1, 1).astype(LOW)
    grad_kv, grad_pick, grad_early, acts, queries_wide, branch_cols = launch(
        [
            swap_blocks("narrow", kv_parts),
            sum_narrow(pick_part),
            sum_narrow(grad_early),
            swap_blocks("wide", acts),
            gather_wide(grad_queries),
            split_columns("wide", grad_branch),
        ],
        10,
        "trade_grads",
    )
    grad_start_exit, gain_early = norm_back(start_own, gain_w[2], grad_early)
    grad_kv = grad_kv.reshape(KVH, repeat, 2, tok_rows, HD)
    if repeat > 1:
        grad_kv = jnp.sum(grad_kv.astype(FULL), axis=1, keepdims=True).astype(LOW)
    grad_kv = grad_kv[:, 0]
    kv_rows = jnp.transpose(grad_kv, (1, 2, 0, 3)).reshape(2, tok_rows, narrow_count, kv_size)
    kv_rows = jnp.moveaxis(kv_rows, 0, 2).reshape(tok_rows, -1)
    grad_kv, out_all = lax.optimization_barrier((kv_rows, out_all))
    grad_normed = jnp.concatenate([dot(grad_kv, kv_w, 1, 1), grad_pick])
    grad_rows, gain_attn = norm_back(rows_full, gain_w[0], grad_normed)
    grad_pass = grad_mid + grad_start_exit + grad_final * (1.0 - keep_layer)
    grad_rows = jnp.concatenate([grad_rows[:tok_rows], grad_rows[tok_rows:] + grad_pass])
    acts = jnp.moveaxis(acts, 1, 0).reshape(3, total_rows, ffn_size)
    rights = (inner_all, inner_all, out_all)
    grad_ffn = [dot(acts[j], rights[j], 0, 0) for j in range(3)]
    ffn_squares = sum(jnp.sum(part * part) for part in grad_ffn)
    summed_qo = jnp.stack(
        [
            jnp.einsum("wtc,wtf->cf", pick_cols, queries_wide, preferred_element_type=FULL),
            jnp.einsum("wtc,wtf->cf", branch_cols, mixed_wide, preferred_element_type=FULL),
        ]
    )
    qo_box = summed_qo.astype(LOW).reshape(narrow_count, -1, q_size)
    qo_box = jnp.moveaxis(qo_box, 0, 1).reshape(-1, width)
    qo_box = jnp.pad(qo_box, ((0, ffn_size - qo_box.shape[0]), (0, 0)))
    for_owners = jnp.stack([part.astype(LOW) for part in grad_ffn] + [qo_box])
    grad_rows, owned, kv_wide, head_cols_all = launch(
        [
            return_rows(grad_rows.astype(LOW)),
            swap_turned(for_owners, 5),
            later(gather_wide(grad_kv, 3), 2),
            later(split_columns("wide", grad_head, 3), 2),
        ],
        11,
        "return_rows",
    )
    final_parts, grad_rows = lax.optimization_barrier((for_owners[:3], grad_rows))
    size = width // narrow_count

    def final_piece(spot):
        return lax.dynamic_slice_in_dim(final_parts, spot * size, size, 2)

    summed_ffn = jnp.zeros((3, narrow_count, ffn_size, size), LOW)
    for step in range(narrow_count):
        piece = final_piece(lax.rem(narrow_spot + step, narrow_count))
        if step:
            piece = shifted(piece, "narrow", step)
        source = lax.rem(narrow_spot - step + narrow_count, narrow_count)
        summed_ffn = lax.dynamic_update_index_in_dim(summed_ffn, piece, source, 1)
    turn = lax.rem(wide_spot, 2)
    grad_kv_w = jnp.einsum(
        "wtc,wtf->cf", tok_cols, kv_wide, preferred_element_type=FULL
    ).reshape(columns, narrow_count, 2, kv_size)
    grad_kv_w = jnp.moveaxis(grad_kv_w, 0, 2)
    summed_kv = lax.psum_scatter(grad_kv_w, "narrow", scatter_dimension=0, tiled=True)[0]
    summed_table, table_squares = spread(
        spots, listed, grad_rows.reshape(-1, columns), head_cols_all.reshape(vocab_rows, columns)
    )

    squares = (
        jnp.sum(summed_qo * summed_qo)
        + jnp.sum(summed_kv * summed_kv)
        + ffn_squares
        + jnp.sum(table_squares)
    )
    sums = jnp.stack(
        [gain_attn, gain_mid[0], gain_early + gain_late[0], jnp.full((width,), squares)]
    )
    sums, summed_ffn = lax.optimization_barrier((sums, summed_ffn))
    summed_ffn = summed_ffn.reshape(3, ffn_rows, size).astype(FULL)
    sums, kv_owned = launch(
        [
            combine(sums.reshape(4, 8, -1), add_two),
            send_owner(summed_kv.astype(LOW).reshape(2 * block_rows, kv_size)),
        ],
        12,
        "combine_sums",
    )
    sums = sums.reshape(4, width)
    summed_gain = lax.dynamic_slice_in_dim(
        sums[:3], (wide_spot * narrow_count + narrow_spot) * gain_size, gain_size, 1
    )
    square_total = sums[3, 0] + jnp.sum(sums[:3] * sums[:3])
    grad_norm = jnp.sqrt(square_total) / loss_count
    factor = jnp.minimum(1.0, CLIP_NORM / (grad_norm + 1e-06)) / loss_count

    def ffn_owner():
        return newton(factor, mom_owned, owned.reshape(ffn_rows, width))

    def small_owner():
        return newton_small(factor, mom_owned, owned, kv_owned)

    small_spot = lax.rem(3 + turn, narrow_count)
    directions = lax.cond(narrow_spot == small_spot, small_owner, ffn_owner)
    received = [lax.dynamic_index_in_dim(directions, narrow_spot, 0, False)] + [
        shifted(
            lax.dynamic_index_in_dim(
                directions, lax.rem(narrow_spot + step, narrow_count), 0, False
            ),
            "narrow",
            step,
        )
        for step in range(1, narrow_count)
    ]

    def direction_of(matrix):
        step = lax.rem(narrow_spot - matrix - turn + 2 * narrow_count, narrow_count)
        result = received[0]
        for at in range(1, narrow_count):
            result = jnp.where(step == at, received[at], result)
        return result

    dir_ffn = jnp.stack([direction_of(matrix) for matrix in range(3)]).astype(FULL)
    small = direction_of(3).astype(FULL)
    dir_qo = small[: 2 * block_rows].reshape(mom_qo.shape)
    dir_kv = small[2 * block_rows : 2 * block_rows + half_rows].reshape(half_rows, 4, kv_size)
    dir_kv = jnp.moveaxis(dir_kv, 1, 0).reshape(mom_kv.shape)

    embed_new, embed_m_new, embed_v_new = adamw(
        embed, embed_m, embed_v, summed_table * factor, RATE_ADAM, WEIGHT_DECAY
    )
    gains_new, gains_m_new, gains_v_new = adamw(
        gains, gains_m, gains_v, summed_gain * factor, RATE_GAIN, 0.0
    )

    def mom_next(mom, grad):
        return MOMENTUM * mom + jnp.moveaxis(grad * factor, 0, 1)

    shrink = 1.0 - RATE_MUON * WEIGHT_DECAY

    def weight_next(weight, direction):
        return weight * shrink - RATE_MUON * jnp.moveaxis(direction, 0, 1)

    return (
        loss_sum,
        loss_count,
        grad_norm,
        embed_new,
        embed_m_new,
        embed_v_new,
        weight_next(attn_qo, dir_qo),
        mom_next(attn_qo_mom, summed_qo),
        weight_next(attn_kv, dir_kv),
        mom_next(attn_kv_mom, summed_kv),
        weight_next(ffn, dir_ffn),
        mom_next(ffn_mom, summed_ffn),
        gains_new,
        gains_m_new,
        gains_v_new,
    )


def solution(mesh):
    by_pack = P("wide", None)
    table = P("narrow", "wide")
    layer = P("wide", None, "narrow")
    gain = P(None, ("wide", "narrow"))
    return jax.shard_map(
        per_device,
        mesh=mesh,
        in_specs=(by_pack,) * 4 + (P("wide"),) + (table,) * 3 + (layer,) * 6 + (gain,) * 3,
        out_specs=(P(),) * 3 + (table,) * 3 + (layer,) * 6 + (gain,) * 3,
        check_vma=False,
    )
```

```python
import functools

import jax
import jax.numpy as jnp
from jax import lax
from jax.experimental import pallas as pl
from jax.experimental.pallas import tpu as pltpu
from jax.sharding import PartitionSpec as P

HEADS = 16
HD = 128
KVH = 4
NS_STEPS = 5
STEP = 10


NORM_EPS = 1e-05
ROPE_BASE = 10000.0
EXIT_EARLY = 0.25
EXIT_LAST = 1.0
CLIP_NORM = 0.02
BETA_ONE = 0.9
BETA_TWO = 0.95
ADAM_EPS = 1e-08
RATE_ADAM = 0.02
RATE_GAIN = 0.3
RATE_MUON = 0.3
WEIGHT_DECAY = 0.1
MOMENTUM = 0.95
NEWTON_A = 3.4445
NEWTON_B = -4.775
NEWTON_C = 2.0315
MASKED = -1e30
LOW = jnp.bfloat16
FULL = jnp.float32
BOTH = ("wide", "narrow")
UNROLL = 16
VMEM_BYTES = 56 * 1024 * 1024


def dot(first, second, first_dim, second_dim):
    return lax.dot_general(
        first, second, (((first_dim,), (second_dim,)), ((), ())), preferred_element_type=FULL
    )


def norm_rows(values, gain_row):
    return (
        values * lax.rsqrt(jnp.mean(values * values, axis=-1, keepdims=True) + NORM_EPS) * gain_row
    )


def segments_at(lens, where_at):
    ends = jnp.cumsum(lens)
    return jnp.sum((where_at[:, None] >= ends[None, :]).astype(jnp.int32), axis=1)


def angles_at(lens, where_at):
    segment = segments_at(lens, where_at)
    starts = jnp.cumsum(lens) - lens
    member = segment[:, None] == jnp.arange(lens.shape[0], dtype=jnp.int32)[None, :]
    begin = jnp.sum(jnp.where(member, starts[None, :], 0), axis=1)
    offset_pos = (where_at - begin).astype(FULL)
    inverse = ROPE_BASE ** (-2.0 * jnp.arange(HD // 2, dtype=FULL) / HD)
    angle = offset_pos[:, None] * inverse[None, :]
    return (segment, jnp.cos(angle), jnp.sin(angle))


MESH = pl.DeviceIdType.MESH
ANY = pl.BlockSpec(memory_space=pl.ANY)
VMEM = pl.BlockSpec(memory_space=pltpu.VMEM)


def others(axis, count):
    me = lax.axis_index(axis)
    return [{axis: lax.rem(me + step, count)} for step in range(1, count)]


def push(source, target, send, receive, device):
    return pltpu.make_async_remote_copy(
        src_ref=source,
        dst_ref=target,
        send_sem=send,
        recv_sem=receive,
        device_id=device,
        device_id_type=MESH,
    )


def arrived(block, send, receive, device):
    push(block, block, send, receive, device).wait_recv()


def like(values):
    return jax.ShapeDtypeStruct(values.shape, values.dtype)


def struct(shape, dtype):
    return jax.ShapeDtypeStruct(shape, dtype)


def sems(*shape):
    return pltpu.SemaphoreType.DMA(shape)


class Task:
    def __init__(self, inputs, outputs, scratch, steps, place_in, place_out, axes):
        self.inputs, self.outputs, self.scratch, self.steps = inputs, outputs, scratch, steps
        self.place_in = [place_in] * len(inputs)
        self.place_out = [place_out] * len(outputs)
        self.axes = axes


def launch(tasks, ident, name):
    axes = sorted(set(axis for task in tasks for axis in task.axes))
    inputs = [a for task in tasks for a in task.inputs]
    outputs = [a for task in tasks for a in task.outputs]
    scratch = [a for task in tasks for a in task.scratch]

    def body(*refs):
        refs = list(refs)
        ins = refs[: len(inputs)]
        outs = refs[len(inputs) : len(inputs) + len(outputs)]
        extra = refs[len(inputs) + len(outputs) :]
        barrier = pltpu.get_barrier_semaphore()
        targets = [device for axis in axes for device in others(axis, lax.axis_size(axis))]
        for device in targets:
            pl.semaphore_signal(barrier, inc=1, device_id=device, device_id_type=MESH)
        pl.semaphore_wait(barrier, len(targets))
        live = []
        for task in tasks:
            counts = (len(task.inputs), len(task.outputs), len(task.scratch))
            live.append(task.steps(ins[: counts[0]], outs[: counts[1]], extra[: counts[2]]))
            ins, outs, extra = ins[counts[0] :], outs[counts[1] :], extra[counts[2] :]
        while live:
            live = [steps for steps in live if next(steps, 0) is None]

    size = sum(a.size * a.dtype.itemsize for a in list(inputs) + list(outputs))
    return pl.pallas_call(
        body,
        out_shape=outputs,
        in_specs=[place for task in tasks for place in task.place_in],
        out_specs=[place for task in tasks for place in task.place_out],
        scratch_shapes=scratch,
        compiler_params=pltpu.CompilerParams(
            collective_id=ident, has_side_effects=True, vmem_limit_bytes=VMEM_BYTES
        ),
        cost_estimate=pl.CostEstimate(flops=0, bytes_accessed=size // 8, transcendentals=0),
        name=name,
    )(*inputs)


def later(task, turns):
    begin = task.steps

    def steps(ins, outs, scratch):
        for turn in range(turns):
            yield
        yield from begin(ins, outs, scratch)

    task.steps = steps
    return task


def gather_wide(values, patience=1):
    count = lax.axis_size("wide")
    chips = count // 2

    def steps(ins, outs, scratch):
        (x_ref,), (out_ref,), (send, receive, local) = ins, outs, scratch
        me = lax.axis_index("wide")
        mate = me + 1 - 2 * lax.rem(me, 2)
        peers = [lax.rem(me + 2 * step, count) for step in range(1, chips)] + [mate]
        first = []
        for step, peer in enumerate(peers):
            copy = push(x_ref, out_ref.at[me], send.at[step], receive.at[me], {"wide": peer})
            copy.start()
            first.append(copy)
        keep = pltpu.make_async_copy(x_ref, out_ref.at[me], local)
        keep.start()
        for turn in range(patience):
            yield
        second = []
        for step in range(1, chips):
            source = lax.rem(me - 2 * step + count, count)
            block = out_ref.at[source]
            arrived(block, send.at[0], receive.at[source], {"wide": mate})
            copy = push(
                block, block, send.at[chips + step - 1], receive.at[source], {"wide": mate}
            )
            copy.start()
            second.append(copy)
        yield
        for step in range(chips):
            source = lax.rem(mate - 2 * step + count, count)
            arrived(out_ref.at[source], send.at[0], receive.at[source], {"wide": mate})
        for copy in first + second:
            copy.wait_send()
        keep.wait()

    shape = struct((count,) + values.shape, values.dtype)
    return Task(
        [values], [shape], [sems(count - 1), sems(count), sems()], steps, ANY, ANY, ["wide"]
    )


def trade(axis, values, source_of, target_of, shape, patience=2):
    count = lax.axis_size(axis)

    def steps(ins, outs, scratch):
        (x_ref,), (out_ref,), (send, receive, local) = ins, outs, scratch
        me = lax.axis_index(axis)
        copies = []
        for step in range(1, count):
            peer = lax.rem(me + step, count)
            copy = push(
                source_of(x_ref, peer),
                target_of(out_ref, me),
                send.at[step - 1],
                receive.at[me],
                {axis: peer},
            )
            copy.start()
            copies.append(copy)
        keep = pltpu.make_async_copy(source_of(x_ref, me), target_of(out_ref, me), local)
        keep.start()
        for turn in range(patience):
            yield
        for step in range(1, count):
            source = lax.rem(me - step + count, count)
            arrived(
                target_of(out_ref, source), send.at[0], receive.at[source], {axis: source}
            )
        for copy in copies:
            copy.wait_send()
        keep.wait()

    return Task(
        [values],
        [struct(shape, values.dtype)],
        [sems(count - 1), sems(count), sems()],
        steps,
        ANY,
        ANY,
        [axis],
    )


def block_at(ref, spot):
    return ref.at[spot]


def whole_at(ref, spot):
    return ref


def columns_of(size):
    def at(ref, spot):
        return ref.at[:, pl.ds(pl.multiple_of(spot * size, size), size)]

    return at


def turned(ref, spot):
    count = lax.axis_size("narrow")
    matrix = lax.rem(spot + count - lax.rem(lax.axis_index("wide"), 2), count)
    return ref.at[jnp.minimum(matrix, 3)]


def swap_turned(values, patience=2):
    shape = (lax.axis_size("narrow"),) + values.shape[1:]
    return trade("narrow", values, turned, block_at, shape, patience)


def send_owner(values):
    count = lax.axis_size("narrow")

    def steps(ins, outs, scratch):
        (x_ref,), (out_ref,), (send, receive, local) = ins, outs, scratch
        me = lax.axis_index("narrow")
        owner = lax.rem(3 + lax.rem(lax.axis_index("wide"), 2), count)
        keep = pltpu.make_async_copy(x_ref, out_ref.at[me], local)
        keep.start()

        def to_owner():
            return push(x_ref, out_ref.at[me], send.at[0], receive.at[me], {"narrow": owner})

        @pl.when(me != owner)
        def _():
            to_owner().start()

        yield
        yield

        @pl.when(me != owner)
        def _():
            to_owner().wait_send()

        @pl.when(me == owner)
        def _():
            for step in range(1, count):
                source = lax.rem(owner + step, count)
                arrived(out_ref.at[source], send.at[0], receive.at[source], {"narrow": source})

        keep.wait()

    return Task(
        [values],
        [struct((count,) + values.shape, values.dtype)],
        [sems(1), sems(count), sems()],
        steps,
        ANY,
        ANY,
        ["narrow"],
    )


def swap_blocks(axis, values):
    return trade(axis, values, block_at, block_at, values.shape)


def gather_blocks(axis, values):
    shape = (lax.axis_size(axis),) + values.shape
    return trade(axis, values, whole_at, block_at, shape)


def split_columns(axis, values, patience=2):
    count = lax.axis_size(axis)
    rows, size = values.shape[0], values.shape[1] // count
    return trade(axis, values, columns_of(size), block_at, (count, rows, size), patience)


def join_columns(axis, values):
    count, rows, size = values.shape
    return trade(axis, values, block_at, columns_of(size), (rows, count * size))


def collect(count, parts_ref, slots, send, receive):
    me = lax.axis_index("narrow")
    copies = []
    for step in range(1, count):
        peer = lax.rem(me + step, count)
        copy = push(
            parts_ref.at[peer],
            slots.at[me],
            send.at[step - 1],
            receive.at[me],
            {"narrow": peer},
        )
        copy.start()
        copies.append(copy)
    return copies


def collected(count, parts_ref, slots, send, receive):
    me = lax.axis_index("narrow")
    total = parts_ref[me].astype(FULL)
    for step in range(1, count):
        source = lax.rem(me - step + count, count)
        arrived(slots.at[source], send.at[0], receive.at[source], {"narrow": source})
        total = total + slots[source].astype(FULL)
    return total


def share(count, low, all_ref, send, receive):
    me = lax.axis_index("narrow")
    all_ref[me] = low
    copies = []
    for step in range(1, count):
        peer = lax.rem(me + step, count)
        copy = push(
            all_ref.at[me], all_ref.at[me], send.at[step - 1], receive.at[me], {"narrow": peer}
        )
        copy.start()
        copies.append(copy)
    return copies


def shared(count, all_ref, send, receive):
    me = lax.axis_index("narrow")
    for step in range(1, count):
        source = lax.rem(me - step + count, count)
        arrived(all_ref.at[source], send.at[0], receive.at[source], {"narrow": source})


def narrow_sems(count):
    return [sems(count - 1), sems(count)]


def settle(partial, base, other, keep_row, gain_row):
    count = lax.axis_size("narrow")
    rows, width = base.shape

    def steps(ins, outs, scratch):
        parts_ref, base_ref, other_ref, keep_ref, gain_ref = ins
        own_ref, all_ref = outs
        slots, send, receive, send_all, receive_all = scratch
        copies = collect(count, parts_ref, slots, send, receive)
        yield
        total = collected(count, parts_ref, slots, send, receive)
        total = jnp.where(keep_ref[...] > 0, total + base_ref[...], other_ref[...])
        own_ref[...] = total
        low = norm_rows(total, gain_ref[...]).astype(LOW)
        copies = copies + share(count, low, all_ref, send_all, receive_all)
        yield
        shared(count, all_ref, send_all, receive_all)
        for copy in copies:
            copy.wait_send()

    return Task(
        [partial.reshape(count, rows, width), base, other, keep_row, gain_row],
        [struct((rows, width), FULL), struct((count, rows, width), LOW)],
        [pltpu.VMEM((count, rows, width), partial.dtype)]
        + narrow_sems(count)
        + narrow_sems(count),
        steps,
        VMEM,
        VMEM,
        ["narrow"],
    )


def settle_back(partial, values, add, keep_row, gain_row):
    count = lax.axis_size("narrow")
    rows, width = values.shape

    def steps(ins, outs, scratch):
        parts_ref, values_ref, add_ref, keep_ref, gain_ref = ins
        own_ref, gain_grad_ref, all_ref = outs
        slots, send, receive, send_all, receive_all = scratch
        copies = collect(count, parts_ref, slots, send, receive)
        yield
        grad = collected(count, parts_ref, slots, send, receive)
        held = values_ref[...]
        root = lax.rsqrt(jnp.mean(held * held, axis=-1, keepdims=True) + NORM_EPS)
        scaled = gain_ref[...] * grad
        inner = jnp.mean(held * scaled, axis=-1, keepdims=True)
        own = add_ref[...] + root * scaled - held * (root * root * root * inner)
        gain_grad_ref[...] = jnp.sum(held * root * grad, axis=0, keepdims=True)
        own_ref[...] = own
        low = (own * keep_ref[...]).astype(LOW)
        copies = copies + share(count, low, all_ref, send_all, receive_all)
        yield
        shared(count, all_ref, send_all, receive_all)
        for copy in copies:
            copy.wait_send()

    return Task(
        [partial.reshape(count, rows, width), values, add, keep_row, gain_row],
        [
            struct((rows, width), FULL),
            struct((1, width), FULL),
            struct((count, rows, width), LOW),
        ],
        [pltpu.VMEM((count, rows, width), partial.dtype)]
        + narrow_sems(count)
        + narrow_sems(count),
        steps,
        VMEM,
        VMEM,
        ["narrow"],
    )


def sum_narrow(partial):
    count = lax.axis_size("narrow")
    rows, width = partial.shape[0] // count, partial.shape[1]

    def steps(ins, outs, scratch):
        (parts_ref,), (own_ref,), (slots, send, receive) = ins, outs, scratch
        copies = collect(count, parts_ref, slots, send, receive)
        yield
        yield
        own_ref[...] = collected(count, parts_ref, slots, send, receive)
        for copy in copies:
            copy.wait_send()

    return Task(
        [partial.reshape(count, rows, width)],
        [struct((rows, width), FULL)],
        [pltpu.VMEM((count, rows, width), partial.dtype)] + narrow_sems(count),
        steps,
        VMEM,
        VMEM,
        ["narrow"],
    )


def fetch_rows(found, rows):
    deep, wide = lax.axis_size("narrow"), lax.axis_size("wide")
    columns = found.shape[2]

    def steps(ins, outs, scratch):
        (found_ref,), (out_ref,) = ins, outs
        rightward, leftward, final = scratch[:3]
        send_right, receive_right, send_left, receive_left = scratch[3:7]
        send_wide, receive_wide, local = scratch[7:]
        spot = lax.axis_index("narrow")
        me = lax.axis_index("wide")

        def right_copy(part, source):
            return push(
                source,
                rightward.at[part],
                send_right.at[part],
                receive_right.at[part],
                {"narrow": lax.rem(spot + 1, deep)},
            )

        def left_copy(part, source):
            return push(
                source,
                leftward.at[part],
                send_left.at[part],
                receive_left.at[part],
                {"narrow": lax.rem(spot + deep - 1, deep)},
            )

        for step in range(deep - 1):
            right, left = deep - 1 - step, step

            @pl.when((spot == 0) & (right > 0))
            def _():
                right_copy(right, found_ref.at[right]).start()

            @pl.when((spot == deep - 1) & (left < deep - 1))
            def _():
                left_copy(left, found_ref.at[left]).start()

        yield
        for step in range(deep - 1):
            right, left = deep - 1 - step, step

            @pl.when((spot > 0) & (right > spot))
            def _():
                right_copy(right, rightward.at[right]).wait_recv()
                rightward[right] = rightward[right] + found_ref[right]
                right_copy(right, rightward.at[right]).start()

            @pl.when((spot < deep - 1) & (left < spot))
            def _():
                left_copy(left, leftward.at[left]).wait_recv()
                leftward[left] = leftward[left] + found_ref[left]
                left_copy(left, leftward.at[left]).start()

        final[...] = found_ref[spot]

        @pl.when(spot > 0)
        def _():
            right_copy(spot, rightward.at[spot]).wait_recv()
            final[...] = final[...] + rightward[spot]

        @pl.when(spot < deep - 1)
        def _():
            left_copy(spot, leftward.at[spot]).wait_recv()
            final[...] = final[...] + leftward[spot]

        def rows_for(device):
            return final.at[pl.ds(pl.multiple_of(device * rows, rows), rows)]

        def columns_from(device):
            return columns_of(columns)(out_ref, device)

        copies = []
        for step in range(1, wide):
            peer = lax.rem(me + step, wide)
            copy = push(
                rows_for(peer),
                columns_from(me),
                send_wide.at[step - 1],
                receive_wide.at[me],
                {"wide": peer},
            )
            copy.start()
            copies.append(copy)
        keep = pltpu.make_async_copy(rows_for(me), columns_from(me), local)
        keep.start()
        yield
        for step in range(1, wide):
            source = lax.rem(me - step + wide, wide)
            arrived(
                columns_from(source), send_wide.at[0], receive_wide.at[source], {"wide": source}
            )
        yield
        for copy in copies:
            copy.wait_send()
        keep.wait()
        for step in range(deep - 1):
            right, left = deep - 1 - step, step

            @pl.when(right > spot)
            def _():
                right_copy(right, found_ref.at[right]).wait_send()

            @pl.when(left < spot)
            def _():
                left_copy(left, found_ref.at[left]).wait_send()

    task = Task(
        [found],
        [struct((rows, wide * columns), found.dtype)],
        [pltpu.VMEM(found.shape, found.dtype)] * 2
        + [pltpu.VMEM(found.shape[1:], found.dtype)]
        + [sems(deep)] * 4
        + [sems(wide - 1), sems(wide), sems()],
        steps,
        VMEM,
        ANY,
        ["narrow", "wide"],
    )
    return task


def return_rows(rows):
    deep, wide = lax.axis_size("narrow"), lax.axis_size("wide")
    count, width = rows.shape
    columns = width // wide

    def steps(ins, outs, scratch):
        (rows_ref,), (out_ref,) = ins, outs
        send_right, send_left, receive_deep, send_wide, receive_wide, local = scratch
        spot = lax.axis_index("narrow")
        me = lax.axis_index("wide")
        part_of = functools.partial(columns_of(columns), rows_ref)

        def landing(device):
            return out_ref.at[spot, pl.ds(pl.multiple_of(device * count, count), count)]

        copies = []
        for step in range(1, wide):
            peer = lax.rem(me + step, wide)
            copy = push(
                part_of(peer),
                landing(me),
                send_wide.at[step - 1],
                receive_wide.at[me],
                {"wide": peer},
            )
            copy.start()
            copies.append(copy)
        keep = pltpu.make_async_copy(part_of(me), landing(me), local)
        keep.start()
        yield
        for step in range(1, wide):
            source = lax.rem(me - step + wide, wide)
            arrived(landing(source), send_wide.at[0], receive_wide.at[source], {"wide": source})
        keep.wait()

        def right_copy(part):
            return push(
                out_ref.at[part],
                out_ref.at[part],
                send_right.at[part],
                receive_deep.at[part],
                {"narrow": lax.rem(spot + 1, deep)},
            )

        def left_copy(part):
            return push(
                out_ref.at[part],
                out_ref.at[part],
                send_left.at[part],
                receive_deep.at[part],
                {"narrow": lax.rem(spot + deep - 1, deep)},
            )

        @pl.when(spot < deep - 1)
        def _():
            right_copy(spot).start()

        @pl.when(spot > 0)
        def _():
            left_copy(spot).start()

        for step in range(1, deep):
            yield

            @pl.when(spot >= step)
            def _():
                right_copy(spot - step).wait_recv()

                @pl.when(spot < deep - 1)
                def _():
                    right_copy(spot - step).start()

            @pl.when(spot + step < deep)
            def _():
                left_copy(spot + step).wait_recv()

                @pl.when(spot > 0)
                def _():
                    left_copy(spot + step).start()

        for part in range(deep):

            @pl.when((part <= spot) & (spot < deep - 1))
            def _():
                right_copy(part).wait_send()

            @pl.when((part >= spot) & (spot > 0))
            def _():
                left_copy(part).wait_send()

        for copy in copies:
            copy.wait_send()

    return Task(
        [rows],
        [struct((deep, wide * count, columns), rows.dtype)],
        [sems(deep)] * 3 + [sems(wide - 1), sems(wide), sems()],
        steps,
        ANY,
        ANY,
        ["narrow", "wide"],
    )


def sum_wide(partial):
    count = lax.axis_size("wide")
    chips = count // 2
    rows, width = partial.shape[0] // count, partial.shape[1]

    def steps(ins, outs, scratch):
        (parts_ref,), (out_ref,) = ins, outs
        from_mate, paired, slots, send_mate, receive_mate, send, receive = scratch
        me = lax.axis_index("wide")
        side = lax.rem(me, 2)
        mate = me + 1 - 2 * side
        my_chip = me // 2
        mate_copies = []
        for step in range(chips):
            chip = lax.rem(my_chip + 1 + step, chips)
            copy = push(
                parts_ref.at[2 * chip + 1 - side],
                from_mate.at[chip],
                send_mate.at[step],
                receive_mate.at[chip],
                {"wide": mate},
            )
            copy.start()
            mate_copies.append(copy)
        yield
        copies = []
        for step in range(chips):
            chip = lax.rem(my_chip + 1 + step, chips)
            arrived(from_mate.at[chip], send_mate.at[0], receive_mate.at[chip], {"wide": mate})
            both = parts_ref[2 * chip + side].astype(FULL) + from_mate[chip].astype(FULL)
            if step < chips - 1:
                paired[chip] = both.astype(LOW)
                copy = push(
                    paired.at[chip],
                    slots.at[my_chip],
                    send.at[step],
                    receive.at[my_chip],
                    {"wide": 2 * chip + side},
                )
                copy.start()
                copies.append(copy)
            else:
                out_ref[...] = both
        yield
        for step in range(1, chips):
            chip = lax.rem(my_chip - step + chips, chips)
            arrived(slots.at[chip], send.at[0], receive.at[chip], {"wide": 2 * chip + side})
            out_ref[...] = out_ref[...] + slots[chip].astype(FULL)
        for copy in mate_copies + copies:
            copy.wait_send()

    return Task(
        [partial.reshape(count, rows, width)],
        [struct((rows, width), FULL)],
        [pltpu.VMEM((chips, rows, width), LOW)] * 3
        + [sems(chips), sems(chips), sems(max(chips - 1, 1)), sems(chips)],
        steps,
        VMEM,
        VMEM,
        ["wide"],
    )


def merge_stats(first, second):
    peak = jnp.maximum(first[0:1], second[0:1])
    total = first[1:2] * jnp.exp(first[0:1] - peak) + second[1:2] * jnp.exp(second[0:1] - peak)
    return jnp.concatenate([peak, total, first[2:3] + second[2:3]], axis=0)


def add_two(first, second):
    return first + second


def combine(values, join):
    deep, wide = lax.axis_size("narrow"), lax.axis_size("wide")

    def steps(ins, outs, scratch):
        (x_ref,), (out_ref,) = ins, outs
        wide_slots, deep_slots, send_wide, receive_wide, send_deep, receive_deep = scratch

        def start(axis, count, slots, value, send, receive):
            me = lax.axis_index(axis)
            slots[me] = value
            copies = []
            for step in range(1, count):
                peer = lax.rem(me + step, count)
                copy = push(
                    slots.at[me], slots.at[me], send.at[step - 1], receive.at[me], {axis: peer}
                )
                copy.start()
                copies.append(copy)
            return copies

        def finish(axis, count, slots, send, receive):
            me = lax.axis_index(axis)
            for step in range(1, count):
                source = lax.rem(me - step + count, count)
                arrived(slots.at[source], send.at[0], receive.at[source], {axis: source})
            total = slots[0]
            for source in range(1, count):
                total = join(total, slots[source])
            return total

        first = start("wide", wide, wide_slots, x_ref[...], send_wide, receive_wide)
        yield
        total = finish("wide", wide, wide_slots, send_wide, receive_wide)
        second = start("narrow", deep, deep_slots, total, send_deep, receive_deep)
        yield
        out_ref[...] = finish("narrow", deep, deep_slots, send_deep, receive_deep)
        for copy in first + second:
            copy.wait_send()

    return Task(
        [values],
        [like(values)],
        [
            pltpu.VMEM((wide,) + values.shape, values.dtype),
            pltpu.VMEM((deep,) + values.shape, values.dtype),
            sems(wide - 1),
            sems(wide),
            sems(deep - 1),
            sems(deep),
        ],
        steps,
        VMEM,
        VMEM,
        ["narrow", "wide"],
    )


def gather_both(values):
    deep, wide = lax.axis_size("narrow"), lax.axis_size("wide")

    def steps(ins, outs, scratch):
        (x_ref,), (out_ref,) = ins, outs
        send_wide, receive_wide, send_deep, receive_deep = scratch
        me = lax.axis_index("wide")
        spot = lax.axis_index("narrow")
        out_ref[spot, me] = x_ref[...]
        copies = []
        for step in range(1, wide):
            peer = lax.rem(me + step, wide)
            block = out_ref.at[spot, me]
            copy = push(block, block, send_wide.at[step - 1], receive_wide.at[me], {"wide": peer})
            copy.start()
            copies.append(copy)
        yield
        for step in range(1, wide):
            source = lax.rem(me - step + wide, wide)
            block = out_ref.at[spot, source]
            arrived(block, send_wide.at[0], receive_wide.at[source], {"wide": source})
        for step in range(1, deep):
            peer = lax.rem(spot + step, deep)
            block = out_ref.at[spot]
            copy = push(
                block, block, send_deep.at[step - 1], receive_deep.at[spot], {"narrow": peer}
            )
            copy.start()
            copies.append(copy)
        yield
        for step in range(1, deep):
            source = lax.rem(spot - step + deep, deep)
            block = out_ref.at[source]
            arrived(block, send_deep.at[0], receive_deep.at[source], {"narrow": source})
        for copy in copies:
            copy.wait_send()

    return Task(
        [values],
        [struct((deep, wide) + values.shape, values.dtype)],
        [sems(wide - 1), sems(wide), sems(deep - 1), sems(deep)],
        steps,
        VMEM,
        VMEM,
        ["narrow", "wide"],
    )


def turn_heads(values, cosine, sine):
    half = values.shape[1] // 2
    swapped = jnp.concatenate([values[:, half:], values[:, :half]], axis=1)
    return values * cosine + swapped * sine


def wide_angles(cosine, sine):
    return jnp.concatenate([cosine, cosine], axis=1), jnp.concatenate([-sine, sine], axis=1)


def local_call(body, inputs, specs, outputs, flops, name):
    return pl.pallas_call(
        body,
        grid=(1,),
        in_specs=specs,
        out_specs=[
            pl.BlockSpec(a.shape, lambda step, rank=len(a.shape): (0,) * rank) for a in outputs
        ],
        out_shape=outputs,
        compiler_params=pltpu.CompilerParams(vmem_limit_bytes=VMEM_BYTES),
        cost_estimate=pl.CostEstimate(flops=flops, bytes_accessed=8 << 20, transcendentals=0),
        name=name,
    )(*inputs)


def entire(values):
    return pl.BlockSpec(values.shape, lambda step: (0,) * values.ndim)


def column_block(values, size, index):
    return pl.BlockSpec((values.shape[0], size), lambda step: (0, index))


def heads_body(groups, rep, rows_ref, gain_ref, kv_ref, cos_ref, sin_ref, out_ref, normed_ref):
    count, _, _, tok_rows, head = out_ref.shape
    size = kv_ref.shape[1] // (2 * count)
    per_head = head // size
    rows = rows_ref[0:tok_rows, :].astype(FULL)
    normed = norm_rows(rows, gain_ref[...]).astype(LOW)
    normed_ref[...] = normed
    both = dot(normed, kv_ref[...], 1, 0)

    def head_of(kind, index):
        pieces = [
            both[:, (2 * part + kind) * size : (2 * part + kind + 1) * size]
            for part in range(index * per_head, (index + 1) * per_head)
        ]
        return pieces[0] if per_head == 1 else jnp.concatenate(pieces, axis=1)

    for owner in range(count):
        for group in range(groups):
            index = (owner * groups + group) // rep
            keys = turn_heads(head_of(0, index), cos_ref[...], sin_ref[...])
            out_ref[owner, group, 0] = keys.astype(LOW)
            out_ref[owner, group, 1] = head_of(1, index).astype(LOW)


def make_heads(rows_low, gain_row, proj, cosine, sine, groups, rep):
    count = lax.axis_size("narrow")
    tok_rows, head = cosine.shape
    width = rows_low.shape[1]
    size = 2 * KVH * HD
    return local_call(
        functools.partial(heads_body, groups, rep),
        [rows_low, gain_row, proj, cosine, sine],
        [entire(rows_low), entire(gain_row), column_block(proj, size, 0)]
        + [entire(cosine), entire(sine)],
        [struct((count, groups, 2, tok_rows, head), LOW), struct((tok_rows, width), LOW)],
        2 * tok_rows * width * size,
        "make_heads",
    )


def attend_body(
    start_ref,
    gains_ref,
    q_ref,
    o_ref,
    kv_ref,
    cos_ref,
    sin_ref,
    seg_ref,
    seg_all_ref,
    pick_ref,
    queries_ref,
    probs_ref,
    mixed_ref,
    part_ref,
    normed_ref,
    early_ref,
):
    count, groups, _, tok_rows, head = kv_ref.shape
    heads_own = probs_ref.shape[0]
    start = start_ref[...].astype(FULL)
    root = lax.rsqrt(jnp.mean(start * start, axis=-1, keepdims=True) + NORM_EPS)
    normed = (start * root * gains_ref[0:1, :]).astype(LOW)
    normed_ref[...] = normed
    early_ref[...] = (start * root * gains_ref[2:3, :]).astype(LOW)
    queries = dot(normed, q_ref[...], 1, 0)
    spots = lax.broadcasted_iota(jnp.int32, (1, count * tok_rows), 1)
    allowed = (seg_ref[...] == seg_all_ref[...]) & (pick_ref[...] >= spots)
    for group in range(groups):
        keys = jnp.concatenate([kv_ref[part, group, 0] for part in range(count)], axis=0)
        values = jnp.concatenate([kv_ref[part, group, 1] for part in range(count)], axis=0)
        for member in range(heads_own // groups):
            at = group * (heads_own // groups) + member
            spot = slice(at * head, (at + 1) * head)
            query = turn_heads(queries[:, spot], cos_ref[...], sin_ref[...]).astype(LOW)
            queries_ref[:, spot] = query
            scores = jnp.where(allowed, dot(query, keys, 1, 1) * head ** (-0.5), MASKED)
            shifted = jnp.exp(scores - jnp.max(scores, axis=-1, keepdims=True))
            probs = shifted / jnp.sum(shifted, axis=-1, keepdims=True)
            probs_ref[at] = probs
            mixed_ref[:, spot] = dot(probs.astype(LOW), values, 1, 0).astype(LOW)
    part_ref[...] = dot(mixed_ref[...], o_ref[...], 1, 1).astype(LOW)


def attend(start_low, gains, proj, own_head, cosine, sine, seg, seg_all, picks):
    count, groups, _, tok_rows, head = own_head.shape
    sel, width = start_low.shape
    heads_own = HEADS // count
    size = heads_own * head
    first = 2 * KVH * HD // size
    seq_len = count * tok_rows
    return local_call(
        attend_body,
        [start_low, gains, proj, proj, own_head, cosine, sine, seg, seg_all, picks],
        [
            entire(start_low),
            entire(gains),
            column_block(proj, size, first),
            column_block(proj, size, first + 1),
        ]
        + [entire(a) for a in (own_head, cosine, sine, seg, seg_all, picks)],
        [
            struct((sel, size), LOW),
            struct((heads_own, sel, seq_len), FULL),
            struct((sel, size), LOW),
            struct((sel, width), LOW),
            struct((sel, width), LOW),
            struct((sel, width), LOW),
        ],
        4 * sel * size * (width + seq_len),
        "attend",
    )


def attend_back_body(
    grad_ref,
    q_ref,
    o_ref,
    kv_ref,
    queries_ref,
    probs_ref,
    cos_ref,
    sin_ref,
    cos_all_ref,
    sin_all_ref,
    out_ref,
    grad_q_ref,
    part_ref,
):
    count, groups, _, tok_rows, head = kv_ref.shape
    heads_own = probs_ref.shape[0]
    scale = head ** (-0.5)
    grad_mixed = dot(grad_ref[...], o_ref[...], 1, 0).astype(LOW)
    for group in range(groups):
        keys = jnp.concatenate([kv_ref[part, group, 0] for part in range(count)], axis=0)
        values = jnp.concatenate([kv_ref[part, group, 1] for part in range(count)], axis=0)
        grad_keys = jnp.zeros(keys.shape, FULL)
        grad_values = jnp.zeros(keys.shape, FULL)
        for member in range(heads_own // groups):
            at = group * (heads_own // groups) + member
            spot = slice(at * head, (at + 1) * head)
            probs = probs_ref[at]
            grad_probs = dot(grad_mixed[:, spot], values, 1, 1)
            inner = jnp.sum(probs * grad_probs, axis=-1, keepdims=True)
            grad_scores = (probs * (grad_probs - inner)).astype(LOW)
            grad_query = dot(grad_scores, keys, 1, 0) * scale
            grad_q_ref[:, spot] = turn_heads(grad_query, cos_ref[...], -sin_ref[...]).astype(LOW)
            grad_keys = grad_keys + dot(grad_scores, queries_ref[:, spot], 0, 0)
            grad_values = grad_values + dot(probs.astype(LOW), grad_mixed[:, spot], 0, 0)
        grad_keys = turn_heads(grad_keys * scale, cos_all_ref[...], -sin_all_ref[...])
        for part in range(count):
            rows = slice(part * tok_rows, (part + 1) * tok_rows)
            out_ref[part, group, 0] = grad_keys[rows].astype(LOW)
            out_ref[part, group, 1] = grad_values[rows].astype(LOW)
    part_ref[...] = dot(grad_q_ref[...], q_ref[...], 1, 1).astype(LOW)


def attend_back(grad, proj, own_head, queries, probs, cosine, sine, cosine_all, sine_all):
    count, groups, _, tok_rows, head = own_head.shape
    sel, width = grad.shape
    size = queries.shape[1]
    first = 2 * KVH * HD // size
    return local_call(
        attend_back_body,
        [grad, proj, proj, own_head, queries, probs, cosine, sine, cosine_all, sine_all],
        [entire(grad), column_block(proj, size, first), column_block(proj, size, first + 1)]
        + [
            entire(a)
            for a in (own_head, queries, probs, cosine, sine, cosine_all, sine_all)
        ],
        [struct(own_head.shape, LOW), struct((sel, size), LOW), struct((sel, width), LOW)],
        8 * sel * size * width,
        "attend_back",
    )


def norm_back_rows(values, gain_row, grad):
    root = lax.rsqrt(jnp.mean(values * values, axis=-1, keepdims=True) + NORM_EPS)
    scaled = gain_row * grad
    inner = jnp.mean(values * scaled, axis=-1, keepdims=True)
    result = root * scaled - values * (root * root * root * inner)
    return result, jnp.sum(values * root * grad, axis=0, keepdims=True)


def rows_back_body(
    rep,
    rows_ref,
    gains_ref,
    kv_ref,
    heads_ref,
    pick_ref,
    early_ref,
    base_ref,
    out_ref,
    attn_gain_ref,
    early_gain_ref,
    grad_kv_ref,
):
    count, groups, _, tok_rows, head = heads_ref.shape
    size = kv_ref.shape[1] // (2 * count)
    per_head = head // size
    for index in range(KVH):
        for kind in range(2):
            copies = [
                heads_ref[at // groups, at % groups, kind]
                for at in range(index * rep, (index + 1) * rep)
            ]
            total = copies[0]
            if rep > 1:
                total = sum(copy.astype(FULL) for copy in copies).astype(LOW)
            for piece in range(per_head):
                lane = (2 * (index * per_head + piece) + kind) * size
                grad_kv_ref[:, lane : lane + size] = total[:, piece * size : (piece + 1) * size]
    values = rows_ref[...].astype(FULL)
    own = values[tok_rows:]
    tok_part, tok_gain = norm_back_rows(
        values[:tok_rows], gains_ref[0:1, :], dot(grad_kv_ref[...], kv_ref[...], 1, 1)
    )
    pick_part, pick_gain = norm_back_rows(own, gains_ref[0:1, :], pick_ref[...])
    early_part, early_gain = norm_back_rows(own, gains_ref[2:3, :], early_ref[...])
    attn_gain_ref[...] = tok_gain + pick_gain
    early_gain_ref[...] = early_gain
    out_ref[0:tok_rows, :] = tok_part.astype(LOW)
    out_ref[tok_rows:, :] = (pick_part + early_part + base_ref[...]).astype(LOW)


def rows_back(rows_low, gains, proj, heads, grad_pick, grad_early, base, rep):
    tok_rows = heads.shape[3]
    width = rows_low.shape[1]
    size = 2 * KVH * HD
    return local_call(
        functools.partial(rows_back_body, rep),
        [rows_low, gains, proj, heads, grad_pick, grad_early, base],
        [entire(rows_low), entire(gains), column_block(proj, size, 0)]
        + [entire(a) for a in (heads, grad_pick, grad_early, base)],
        [
            struct(rows_low.shape, LOW),
            struct((1, width), FULL),
            struct((1, width), FULL),
            struct((tok_rows, size), LOW),
        ],
        2 * tok_rows * width * size,
        "rows_back",
    )


def assemble_body(out_columns, *refs):
    pieces, out_ref = refs[:-1], refs[-1]
    count = len(pieces)
    me = lax.axis_index("narrow")
    for step, piece in enumerate(pieces):
        source = lax.rem(me - step + count, count)
        spot = pl.ds(pl.multiple_of(source * out_columns, out_columns), out_columns)
        out_ref[:, spot] = piece[...]


def assemble(pieces):
    rows, columns = pieces[0].shape
    outputs = [struct((rows, columns * len(pieces)), pieces[0].dtype)]
    return local_call(
        functools.partial(assemble_body, columns),
        list(pieces),
        [entire(piece) for piece in pieces],
        outputs,
        0,
        "assemble",
    )[0]


def feed_body(inner_ref, weight_ref, gate_ref, up_ref, hidden_ref, out_ref, total):
    part = pl.program_id(0)
    inner = inner_ref[...]
    gate = dot(inner, weight_ref[0, 0], 1, 1)
    up = dot(inner, weight_ref[0, 1], 1, 1)
    hidden = (jax.nn.silu(gate) * up).astype(LOW)
    gate_ref[0] = gate
    up_ref[0] = up
    hidden_ref[0] = hidden
    product = dot(hidden, weight_ref[0, 2], 1, 0)

    @pl.when(part == 0)
    def _():
        total[...] = product

    @pl.when(part > 0)
    def _():
        total[...] = total[...] + product

    @pl.when(part == pl.num_programs(0) - 1)
    def _():
        out_ref[...] = total[...].astype(LOW)


def feed(inner, weight):
    parts, _, size, width = weight.shape
    sel = inner.shape[0]
    same = pl.BlockSpec((sel, width), lambda part: (0, 0))
    slab = pl.BlockSpec((1, sel, size), lambda part: (part, 0, 0))
    return pl.pallas_call(
        feed_body,
        grid=(parts,),
        in_specs=[same, pl.BlockSpec((1, 3, size, width), lambda part: (part, 0, 0, 0))],
        out_specs=[slab, slab, slab, same],
        out_shape=[
            struct((parts, sel, size), FULL),
            struct((parts, sel, size), FULL),
            struct((parts, sel, size), LOW),
            struct((sel, width), LOW),
        ],
        scratch_shapes=[pltpu.VMEM((sel, width), FULL)],
        compiler_params=pltpu.CompilerParams(vmem_limit_bytes=VMEM_BYTES),
        cost_estimate=pl.CostEstimate(
            flops=6 * sel * parts * size * width,
            bytes_accessed=weight.size * 2,
            transcendentals=0,
        ),
        name="feed",
    )(inner, weight)


def feed_back_body(grad_ref, weight_ref, gate_ref, up_ref, hidden_ref, acts_ref, out_ref, total):
    part = pl.program_id(0)
    grad_hidden = dot(grad_ref[...], weight_ref[0, 2], 1, 1)
    gate = gate_ref[0]
    sigma = jax.nn.sigmoid(gate)
    grad_gate = (grad_hidden * up_ref[0] * sigma * (1.0 + gate * (1.0 - sigma))).astype(LOW)
    grad_up = (grad_hidden * gate * sigma).astype(LOW)
    acts_ref[0, 0] = grad_gate
    acts_ref[0, 1] = grad_up
    acts_ref[0, 2] = hidden_ref[0]
    product = dot(grad_gate, weight_ref[0, 0], 1, 0) + dot(grad_up, weight_ref[0, 1], 1, 0)

    @pl.when(part == 0)
    def _():
        total[...] = product

    @pl.when(part > 0)
    def _():
        total[...] = total[...] + product

    @pl.when(part == pl.num_programs(0) - 1)
    def _():
        out_ref[...] = total[...].astype(LOW)


def feed_back(grad, weight, gate, up, hidden):
    parts, _, size, width = weight.shape
    sel = grad.shape[0]
    same = pl.BlockSpec((sel, width), lambda part: (0, 0))
    slab = pl.BlockSpec((1, sel, size), lambda part: (part, 0, 0))
    return pl.pallas_call(
        feed_back_body,
        grid=(parts,),
        in_specs=[same, pl.BlockSpec((1, 3, size, width), lambda part: (part, 0, 0, 0))]
        + [slab] * 3,
        out_specs=[pl.BlockSpec((1, 3, sel, size), lambda part: (part, 0, 0, 0)), same],
        out_shape=[struct((parts, 3, sel, size), LOW), struct((sel, width), LOW)],
        scratch_shapes=[pltpu.VMEM((sel, width), FULL)],
        compiler_params=pltpu.CompilerParams(vmem_limit_bytes=VMEM_BYTES),
        cost_estimate=pl.CostEstimate(
            flops=6 * sel * parts * size * width,
            bytes_accessed=weight.size * 2,
            transcendentals=0,
        ),
        name="feed_back",
    )(grad, weight, gate, up, hidden)


def newton_steps(problems):
    rows, width = problems[0][0].shape
    block = min(512, width)
    eye = lax.broadcasted_iota(jnp.int32, (rows, rows), 0) == lax.broadcasted_iota(
        jnp.int32, (rows, rows), 1
    )

    def strip(part):
        return pl.ds(pl.multiple_of(part * block, block), block)

    def over(function, start):
        return lax.fori_loop(0, width // block, function, start)

    def add_squares(part, totals):
        values = [current[:, strip(part)] for current, low, gram, rest in problems]
        return [total + jnp.sum(value * value) for total, value in zip(totals, values)]

    totals = over(add_squares, [jnp.float32(0.0)] * len(problems))
    scales = [1.0 / (jnp.sqrt(total) + 1e-07) for total in totals]

    def begin(part, carry):
        for scale, (current, low, gram, rest) in zip(scales, problems):
            values = current[:, strip(part)] * scale
            current[:, strip(part)] = values
            low[:, strip(part)] = values.astype(LOW)
        return carry

    over(begin, 0)

    def iteration(turn, carry):
        for current, low, gram, rest in problems:
            gram[...] = jnp.zeros_like(gram)

        def add_gram(part, carry):
            for current, low, gram, rest in problems:
                values = low[:, strip(part)]
                gram[...] = gram[...] + dot(values, values, 1, 1)
            return carry

        over(add_gram, 0)
        seconds = []
        for current, low, gram, rest in problems:
            whole = gram[...]
            middle = jnp.sum(jnp.where(eye, whole, 0.0)) / rows
            rest[...] = (whole - jnp.where(eye, middle, 0.0)).astype(LOW)
            square = dot(rest[...], rest[...], 1, 0)
            whole = gram[...]
            centred = whole - jnp.where(eye, middle, 0.0)
            square = square + 2.0 * middle * centred + jnp.where(eye, middle * middle, 0.0)
            whole = NEWTON_B * whole + NEWTON_C * square
            second = jnp.sum(jnp.where(eye, whole, 0.0)) / rows
            rest[...] = (whole - jnp.where(eye, second, 0.0)).astype(LOW)
            seconds.append(second)

        def apply(part, carry):
            for second, (current, low, gram, rest) in zip(seconds, problems):
                values = (NEWTON_A + second) * current[:, strip(part)] + dot(
                    rest[...], low[:, strip(part)], 1, 0
                )
                current[:, strip(part)] = values
                low[:, strip(part)] = values.astype(LOW)
            return carry

        over(apply, 0)
        return carry

    lax.fori_loop(0, NS_STEPS, iteration, 0)


def newton_scratch(rows, width):
    return [
        pltpu.VMEM((rows, width), FULL),
        pltpu.VMEM((rows, width), LOW),
        pltpu.VMEM((rows, rows), FULL),
        pltpu.VMEM((rows, rows), LOW),
    ]


def newton_cost(count, rows, width):
    return pl.CostEstimate(
        flops=NS_STEPS * count * (4 * rows * rows * width + 2 * rows * rows * rows),
        bytes_accessed=6 * count * rows * width,
        transcendentals=0,
    )


def newton_body(factor_ref, mom_ref, grad_ref, out_ref, *problem):
    current, low = problem[:2]
    parts, rows, columns = mom_ref.shape
    factor = factor_ref[0]
    for part in range(parts):
        spot = slice(part * columns, (part + 1) * columns)
        current[:, spot] = MOMENTUM * mom_ref[part].astype(FULL) + factor * grad_ref[
            :, spot
        ].astype(FULL)
    newton_steps([problem])
    for part in range(parts):
        out_ref[part] = low[:, part * columns : (part + 1) * columns]


def newton(factor, mom, grad):
    parts, rows, columns = mom.shape
    width = parts * columns
    return pl.pallas_call(
        newton_body,
        in_specs=[pl.BlockSpec(memory_space=pltpu.SMEM), VMEM, VMEM],
        out_specs=VMEM,
        out_shape=struct(mom.shape, LOW),
        scratch_shapes=newton_scratch(rows, width),
        compiler_params=pltpu.CompilerParams(vmem_limit_bytes=VMEM_BYTES),
        cost_estimate=newton_cost(1, rows, width),
        name="newton",
    )(factor.reshape(1), mom, grad)


def newton_small_body(rows, factor_ref, mom_ref, grad_ref, kv_ref, out_ref, *scratch):
    problems = [scratch[4 * at : 4 * at + 4] for at in range(4)]
    parts, _, columns = mom_ref.shape
    piece_rows = 2 * rows // parts
    kv_columns = kv_ref.shape[2]
    half = rows // 2
    factor = factor_ref[0]
    for part in range(parts):
        spot = slice(part * columns, (part + 1) * columns)
        for member in range(2):
            current = problems[member][0]
            current[:, spot] = MOMENTUM * mom_ref[
                part, member * rows : (member + 1) * rows, :
            ].astype(FULL)
        for block in range(parts):
            current = problems[block // (parts // 2)][0]
            at = block % (parts // 2) * piece_rows
            piece = grad_ref[part, 0:piece_rows, block * columns : (block + 1) * columns]
            current[at : at + piece_rows, spot] = (
                current[at : at + piece_rows, spot] + factor * piece.astype(FULL)
            )
        spot = slice(part * kv_columns, (part + 1) * kv_columns)
        for member in range(2):
            current = problems[2 + member][0]
            piece = kv_ref[part, member * rows : (member + 1) * rows, :].astype(FULL)
            for side in range(2):
                lane = (2 * member + side) * kv_columns
                mom = mom_ref[part, 2 * rows : 2 * rows + half, lane : lane + kv_columns]
                here = slice(side * half, (side + 1) * half)
                current[here, spot] = MOMENTUM * mom.astype(FULL) + factor * piece[here]
    newton_steps(problems[:2])
    newton_steps(problems[2:])
    out_ref[...] = jnp.zeros_like(out_ref)
    for part in range(parts):
        for member in range(2):
            out_ref[part, member * rows : (member + 1) * rows, :] = problems[member][1][
                :, part * columns : (part + 1) * columns
            ]
            low = problems[2 + member][1]
            for side in range(2):
                lane = (2 * member + side) * kv_columns
                out_ref[part, 2 * rows : 2 * rows + half, lane : lane + kv_columns] = low[
                    side * half : (side + 1) * half,
                    part * kv_columns : (part + 1) * kv_columns,
                ]


def newton_small(factor, mom, grad, kv_grad):
    parts, _, columns = mom.shape
    rows = kv_grad.shape[1] // 2
    kv_width = parts * kv_grad.shape[2]
    return pl.pallas_call(
        functools.partial(newton_small_body, rows),
        in_specs=[pl.BlockSpec(memory_space=pltpu.SMEM), VMEM, VMEM, VMEM],
        out_specs=VMEM,
        out_shape=struct(mom.shape, LOW),
        scratch_shapes=newton_scratch(rows, parts * columns) * 2
        + newton_scratch(rows, kv_width) * 2,
        compiler_params=pltpu.CompilerParams(vmem_limit_bytes=VMEM_BYTES),
        cost_estimate=newton_cost(2, rows, parts * columns),
        name="newton_small",
    )(factor.reshape(1), mom, grad, kv_grad)


def lookup_body(ids_ref, turn_ref, table_ref, out_ref, low_ref, list_ref, held, rows, sem):
    vocab = table_ref.shape[0]
    count = out_ref.shape[0]
    load = pltpu.make_async_copy(table_ref, held, sem)
    load.start()
    rows[...] = jnp.zeros_like(rows)

    found = turn_ref[count]

    def note(group, carry):
        for member in range(UNROLL):
            at = group * UNROLL + member
            list_ref[turn_ref[at]] = at
        return carry

    lax.fori_loop(0, count // UNROLL, note, 0)
    for member in range(UNROLL):
        list_ref[found + member] = count
    list_ref[count + UNROLL] = found
    load.wait()

    def step(group, carry):
        for member in range(UNROLL):
            at = list_ref[group * UNROLL + member]
            spot = jnp.minimum(ids_ref[jnp.minimum(at, count - 1)], vocab - 1)
            rows[pl.ds(at, 1), :] = held[pl.ds(spot, 1), :]
        return carry

    lax.fori_loop(0, (found + UNROLL - 1) // UNROLL, step, 0)
    out_ref[...] = rows[pl.ds(0, count), :].astype(LOW)
    low_ref[...] = held[...].astype(LOW)


def lookup(table, ids):
    vocab, columns = table.shape
    count = ids.shape[0]
    mine = (ids < vocab).reshape(-1, 128)
    before = jnp.arange(128)[:, None] < jnp.arange(128)[None, :]
    in_row = dot(mine.astype(LOW), before.astype(LOW), 1, 0)
    per_row = jnp.sum(mine.astype(FULL), axis=1)
    lines = jnp.arange(mine.shape[0])
    ahead = jnp.sum(jnp.where(lines[:, None] > lines[None, :], per_row[None, :], 0.0), axis=1)
    found = jnp.sum(per_row).astype(jnp.int32)
    turns = (in_row + ahead[:, None]).astype(jnp.int32)
    turns = jnp.where(mine, turns, count + UNROLL + 1).reshape(-1)
    turns = jnp.concatenate([turns, jnp.full((128,), found)])
    return pl.pallas_call(
        lookup_body,
        in_specs=[pl.BlockSpec(memory_space=pltpu.SMEM)] * 2 + [ANY],
        out_specs=[VMEM, VMEM, pl.BlockSpec(memory_space=pltpu.SMEM)],
        scratch_shapes=[
            pltpu.VMEM((vocab, columns), FULL),
            pltpu.VMEM((count + 8, columns), FULL),
            pltpu.SemaphoreType.DMA,
        ],
        out_shape=[
            struct((count, columns), LOW),
            struct((vocab, columns), LOW),
            struct((count + 2 * UNROLL,), jnp.int32),
        ],
        compiler_params=pltpu.CompilerParams(vmem_limit_bytes=VMEM_BYTES),
        cost_estimate=pl.CostEstimate(
            flops=0, bytes_accessed=vocab * columns * 4, transcendentals=0
        ),
        name="lookup",
    )(ids, turns, table)


def spread_body(
    ids_ref, list_ref, rows_ref, head_ref, out_ref, square_ref, even, odd, rows, sem
):
    vocab = out_ref.shape[0]
    count = rows_ref.shape[0]
    chunk = 256

    def strip(part):
        return pl.ds(pl.multiple_of(part * chunk, chunk), chunk)

    def begin(part, carry):
        even[strip(part), :] = head_ref[strip(part), :].astype(FULL)
        odd[strip(part), :] = jnp.zeros((chunk, odd.shape[1]), FULL)
        return carry

    lax.fori_loop(0, vocab // chunk, begin, 0)

    def widen(part, carry):
        rows[strip(part), :] = rows_ref[strip(part), :].astype(FULL)
        return carry

    lax.fori_loop(0, count // chunk, widen, 0)
    rows[pl.ds(count, 8), :] = jnp.zeros((8, rows.shape[1]), FULL)

    def step(group, carry):
        for member in range(UNROLL):
            at = list_ref[group * UNROLL + member]
            spot = jnp.minimum(ids_ref[jnp.minimum(at, count - 1)], vocab - 1)
            total = even if member % 2 == 0 else odd
            total[pl.ds(spot, 1), :] = total[pl.ds(spot, 1), :] + rows[pl.ds(at, 1), :]
        return carry

    found = list_ref[count + UNROLL]
    lax.fori_loop(0, (found + UNROLL - 1) // UNROLL, step, 0)

    def finish(part, squares):
        value = even[strip(part), :] + odd[strip(part), :]
        even[strip(part), :] = value
        return squares + jnp.sum((value * value).reshape(chunk // 8, 8, -1), axis=0)

    square_ref[...] = lax.fori_loop(
        0, vocab // chunk, finish, jnp.zeros((8, even.shape[1]), FULL)
    )
    store = pltpu.make_async_copy(even, out_ref, sem)
    store.start()
    store.wait()


def spread(ids, listed, rows, head):
    vocab, columns = head.shape
    count = ids.shape[0]
    smem = pl.BlockSpec(memory_space=pltpu.SMEM)
    return pl.pallas_call(
        spread_body,
        in_specs=[smem, smem, VMEM, VMEM],
        out_specs=[ANY, VMEM],
        scratch_shapes=[
            pltpu.VMEM((vocab, columns), FULL),
            pltpu.VMEM((vocab, columns), FULL),
            pltpu.VMEM((count + 8, columns), FULL),
            pltpu.SemaphoreType.DMA,
        ],
        out_shape=[struct((vocab, columns), FULL), struct((8, columns), FULL)],
        compiler_params=pltpu.CompilerParams(vmem_limit_bytes=VMEM_BYTES),
        cost_estimate=pl.CostEstimate(
            flops=count * columns, bytes_accessed=vocab * columns * 8, transcendentals=0
        ),
        name="spread",
    )(ids, listed, rows, head)


def adamw(weight, first_m, second_m, grad, rate, decay):
    first_new = BETA_ONE * first_m + (1.0 - BETA_ONE) * grad
    second_new = BETA_TWO * second_m + (1.0 - BETA_TWO) * grad * grad
    update = (
        first_new
        / (1.0 - BETA_ONE**STEP)
        / (jnp.sqrt(second_new / (1.0 - BETA_TWO**STEP)) + ADAM_EPS)
    )
    return (weight * (1.0 - rate * decay) - rate * update, first_new, second_new)


def cut_columns(values, count):
    rows, columns = values.shape
    return jnp.moveaxis(values.reshape(rows, count, columns // count), 1, 0)


def shifted(parts, axis, step):
    count = lax.axis_size(axis)
    pairs = [(source, (source + step) % count) for source in range(count)]
    return lax.ppermute(parts, axis, pairs)


def per_device(
    tokens,
    picks,
    targets,
    lengths,
    skip,
    embed,
    embed_m,
    embed_v,
    attn_qo,
    attn_qo_mom,
    attn_kv,
    attn_kv_mom,
    ffn,
    ffn_mom,
    gains,
    gains_m,
    gains_v,
):
    wide_count = lax.axis_size("wide")
    narrow_count = lax.axis_size("narrow")
    narrow_spot = lax.axis_index("narrow")
    wide_spot = lax.axis_index("wide")
    seq_len = tokens.shape[1]
    sel = picks.shape[1]
    vocab_rows, columns = embed.shape
    width = columns * wide_count
    own_rows = sel // narrow_count
    tok_rows = seq_len // narrow_count
    all_rows = own_rows + tok_rows
    heads_own = HEADS // narrow_count
    head_cols = heads_own * HD
    repeat = max(1, narrow_count // KVH)
    groups = KVH * repeat // narrow_count
    ffn_rows = ffn.shape[0]
    ffn_size = ffn_rows // narrow_count
    total_rows = wide_count * sel
    lens = lengths[0]
    pick_ids = picks[0]
    keep_layer = (1 - skip[0]).astype(FULL)
    keep_row = jnp.full((1, width), keep_layer)
    lanes = 128

    def box(flat):
        height = -(-flat.shape[0] // (8 * lanes)) * 8
        return jnp.pad(flat, (0, height * lanes - flat.shape[0])).reshape(height, lanes)

    ffn_low = jnp.moveaxis(ffn, 1, 0).astype(LOW)
    ffn_cut = ffn_low.reshape(3, narrow_count, ffn_size, ffn_low.shape[2])
    ffn_cut = jnp.moveaxis(ffn_cut, 1, 0).reshape(narrow_count, 3 * ffn_size, -1)
    kv_own = attn_kv.reshape(columns, -1).astype(LOW)

    where_at = jnp.arange(seq_len, dtype=jnp.int32)
    pick_tokens = jnp.sum(
        jnp.where(pick_ids[:, None] == where_at[None, :], tokens[0][None, :], 0), axis=1
    )
    ints = box(jnp.concatenate([tokens[0], pick_tokens, targets[0]]))
    all_ints, all_gains, kv_part = launch(
        [
            gather_wide(ints),
            gather_both(box(gains.astype(LOW).astype(FULL).reshape(-1))),
            gather_blocks("narrow", kv_own),
        ],
        0,
        "gather_ids",
    )
    kv_part = jnp.moveaxis(kv_part, 0, 1).reshape(columns, -1)
    proj_own = jnp.concatenate([kv_part, attn_qo.reshape(columns, -1).astype(LOW)], axis=1)
    proj = lax.all_gather(proj_own, "wide", axis=0, tiled=True)
    ffn_cut, all_ints = lax.optimization_barrier((ffn_cut, all_ints))
    ffn_pieces = [lax.dynamic_index_in_dim(ffn_cut, narrow_spot, 0, False)] + [
        shifted(
            lax.dynamic_index_in_dim(
                ffn_cut, lax.rem(narrow_spot + step, narrow_count), 0, False
            ),
            "narrow",
            step,
        )
        for step in range(1, narrow_count)
    ]
    gain_size = gains.shape[1]
    gain_w = all_gains.reshape(narrow_count, wide_count, -1)[:, :, : 3 * gain_size]
    gain_w = gain_w.reshape(narrow_count, wide_count, 3, gain_size)
    gain_w = jnp.transpose(gain_w, (2, 1, 0, 3)).reshape(3, width)
    all_ints = all_ints.reshape(wide_count, -1)
    tokens_all = all_ints[:, :seq_len].reshape(wide_count, narrow_count, tok_rows)
    picked_all = all_ints[:, seq_len : seq_len + sel].reshape(wide_count, narrow_count, own_rows)
    targets_all = all_ints[:, seq_len + sel : seq_len + 2 * sel].reshape(-1)
    wanted = jnp.moveaxis(jnp.concatenate([tokens_all, picked_all], axis=2), 1, 0).reshape(-1)
    local_ids = wanted - narrow_spot * vocab_rows
    inside = (local_ids >= 0) & (local_ids < vocab_rows)
    spots = jnp.where(inside, local_ids, vocab_rows)
    found, embed_low, listed = lookup(embed, spots)
    ffn_pieces, found = lax.optimization_barrier((ffn_pieces, found))
    ffn_sub = assemble(ffn_pieces).reshape(3, ffn_size, width)
    ffn_sub, found = lax.optimization_barrier((ffn_sub, found))
    ffn_w = lax.all_gather(ffn_sub, "wide", axis=0)
    found = found.reshape(narrow_count, wide_count * all_rows, columns)
    embed_cut = embed_low.reshape(wide_count, vocab_rows // wide_count, columns)
    rows_low, table_own = launch(
        [fetch_rows(found, all_rows), join_columns("wide", embed_cut)], 1, "fetch_rows"
    )

    mom_qo = jnp.moveaxis(attn_qo_mom, 1, 0)
    mom_kv = jnp.moveaxis(attn_kv_mom, 1, 0)
    mom_ffn = jnp.moveaxis(ffn_mom, 1, 0)
    slot_rows, slot_cols = mom_ffn.shape[1:]

    block_rows, q_size = mom_qo.shape[1:]
    kv_size = mom_kv.shape[2]
    half_rows = block_rows // 2
    kv_box = jnp.moveaxis(mom_kv.reshape(4, half_rows, kv_size), 0, 1).reshape(half_rows, -1)
    small_box = jnp.concatenate([mom_qo.reshape(2 * block_rows, q_size), kv_box])
    small_box = jnp.pad(small_box, ((0, slot_rows - small_box.shape[0]), (0, 0)))
    mom_parts = jnp.concatenate([mom_ffn, small_box[None]]).astype(LOW)

    seg_all, cosine_all, sine_all = angles_at(lens, where_at)
    cosine_all, sine_all = wide_angles(cosine_all, sine_all)
    seg_mine, cosine, sine = angles_at(lens, pick_ids)
    cosine, sine = wide_angles(cosine, sine)

    def tok_part(angles):
        return lax.dynamic_slice_in_dim(angles, narrow_spot * tok_rows, tok_rows, 0)

    by_head, normed_tok = make_heads(
        rows_low, gain_w[0:1], proj, tok_part(cosine_all), tok_part(sine_all), groups, repeat
    )
    own_head, start_low, tok_cols = launch(
        [
            swap_blocks("narrow", by_head),
            gather_blocks("narrow", rows_low[tok_rows:]),
            split_columns("wide", normed_tok),
        ],
        2,
        "trade_heads",
    )
    start_low, ffn_w = lax.optimization_barrier((start_low, ffn_w))
    start_low = start_low.reshape(sel, width)
    queries, probs, mixed, attn_part, normed, early_part = attend(
        start_low,
        gain_w,
        proj,
        own_head,
        cosine,
        sine,
        seg_mine[:, None],
        seg_all[None, :],
        pick_ids[:, None],
    )
    early = lax.all_gather(early_part, "wide", axis=0, tiled=True)
    start_own = rows_low[tok_rows:].astype(FULL)
    middle, inner, mixed_wide, pick_cols = launch(
        [
            settle(
                attn_part,
                start_own,
                start_own,
                jnp.ones((1, width), FULL),
                gain_w[1:2],
            ),
            gather_wide(mixed),
            split_columns("wide", normed),
        ],
        3,
        "settle_middle",
    )
    inner = inner.reshape(sel, width)
    inner_all = lax.all_gather(inner, "wide", axis=0, tiled=True)
    gate, up, hidden, fed = feed(inner, ffn_w)
    final_own, late_part = launch(
        [settle(fed, middle, start_own, keep_row, gain_w[2:3])], 4, "settle_late"
    )

    table_count = table_own.shape[0]
    local_target = targets_all - (narrow_spot * vocab_rows + wide_spot * table_count)
    has_target = local_target[:, None] == jnp.arange(table_count, dtype=jnp.int32)[None, :]
    counted = (targets_all >= 0).astype(FULL)
    loss_count = jnp.sum(counted)

    def exit_logits(features):
        logits = dot(features, table_own, 1, 1)
        peak = jnp.max(logits, axis=-1)
        total = jnp.sum(jnp.exp(logits - peak[:, None]), axis=-1)
        picked = jnp.sum(jnp.where(has_target, logits, 0.0), axis=-1)
        return logits, jnp.stack([peak, total, picked])

    half = slot_rows // 2
    late, mom_top = launch(
        [
            gather_wide(late_part.reshape(sel, width)),
            swap_turned(mom_parts[:, :half]),
        ],
        5,
        "gather_late",
    )
    late = late.reshape(total_rows, width)
    early_logits, early_stats = exit_logits(early)
    late_logits, late_stats = exit_logits(late)
    stats = jnp.concatenate([early_stats, late_stats], axis=1).reshape(3, 8, -1)
    stats = launch([combine(stats, merge_stats)], 6, "combine_stats")[0]
    stats, inner_all = lax.optimization_barrier((stats, inner_all))
    stats = stats.reshape(3, -1)
    log_norms = stats[0] + jnp.log(stats[1])
    losses = log_norms - stats[2]
    loss_sum = jnp.sum(
        counted * (EXIT_EARLY * losses[:total_rows] + EXIT_LAST * losses[total_rows:])
    )

    def exit_back(logits, log_norm, weight, features):
        grad_logits = (
            (jnp.exp(logits - log_norm[:, None]) - has_target.astype(FULL))
            * (weight * counted)[:, None]
        ).astype(LOW)
        return dot(grad_logits, table_own, 1, 0).astype(LOW), dot(grad_logits, features, 0, 0)

    late_back, late_head = exit_back(late_logits, log_norms[total_rows:], EXIT_LAST, late)
    grad_late, mom_low = launch(
        [sum_wide(late_back), swap_turned(mom_parts[:, half:])], 7, "sum_late"
    )
    early_norms, grad_late = lax.optimization_barrier((log_norms[:total_rows], grad_late))
    early_back, early_head = exit_back(early_logits, early_norms, EXIT_EARLY, early)
    mom_owned = jnp.concatenate([mom_top, mom_low], axis=1)
    grad_head = (early_head + late_head).astype(LOW)

    grad_early = lax.psum_scatter(early_back, "wide", scatter_dimension=0, tiled=True)
    grad_final, gain_late, grad_out = launch(
        [
            settle_back(
                grad_late.astype(LOW),
                final_own,
                jnp.zeros_like(final_own),
                keep_row,
                gain_w[2:3],
            ),
        ],
        8,
        "back_late",
    )
    grad_layer = grad_final * keep_layer
    grad_out = grad_out.reshape(sel, width)
    out_all = lax.all_gather(grad_out, "wide", axis=0, tiled=True)
    acts, fed_back = feed_back(grad_out, ffn_w, gate, up, hidden)
    grad_mid, gain_mid, grad_branch = launch(
        [settle_back(fed_back, middle, grad_layer, keep_row, gain_w[1:2])], 9, "back_middle"
    )
    grad_branch, grad_early = lax.optimization_barrier((grad_branch, grad_early))
    grad_branch = grad_branch.reshape(sel, width)

    kv_parts, grad_queries, pick_part = attend_back(
        grad_branch, proj, own_head, queries, probs, cosine, sine, cosine_all, sine_all
    )
    grad_kv, grad_pick, grad_early, acts, queries_wide, branch_cols = launch(
        [
            swap_blocks("narrow", kv_parts),
            sum_narrow(pick_part),
            sum_narrow(grad_early),
            swap_blocks("wide", acts),
            gather_wide(grad_queries),
            split_columns("wide", grad_branch),
        ],
        10,
        "trade_grads",
    )
    grad_kv, out_all = lax.optimization_barrier((grad_kv, out_all))
    grad_base = grad_mid + grad_final * (1.0 - keep_layer)
    grad_rows, gain_attn, gain_early, grad_kv = rows_back(
        rows_low, gain_w, proj, grad_kv, grad_pick, grad_early, grad_base, repeat
    )
    acts = jnp.moveaxis(acts, 1, 0).reshape(3, total_rows, ffn_size)
    rights = (inner_all, inner_all, out_all)
    grad_ffn = [dot(acts[j], rights[j], 0, 0) for j in range(3)]
    ffn_squares = sum(jnp.sum(part * part) for part in grad_ffn)
    summed_qo = jnp.stack(
        [
            jnp.einsum("wtc,wtf->cf", pick_cols, queries_wide, preferred_element_type=FULL),
            jnp.einsum("wtc,wtf->cf", branch_cols, mixed_wide, preferred_element_type=FULL),
        ]
    )
    qo_box = summed_qo.astype(LOW).reshape(narrow_count, -1, q_size)
    qo_box = jnp.moveaxis(qo_box, 0, 1).reshape(-1, width)
    qo_box = jnp.pad(qo_box, ((0, ffn_size - qo_box.shape[0]), (0, 0)))
    for_owners = jnp.stack([part.astype(LOW) for part in grad_ffn] + [qo_box])
    grad_rows, owned, kv_wide, head_cols_all = launch(
        [
            return_rows(grad_rows),
            swap_turned(for_owners, 5),
            later(gather_wide(grad_kv, 3), 2),
            later(split_columns("wide", grad_head, 3), 2),
        ],
        11,
        "return_rows",
    )
    final_parts, grad_rows = lax.optimization_barrier((for_owners[:3], grad_rows))
    size = width // narrow_count

    def final_piece(spot):
        return lax.dynamic_slice_in_dim(final_parts, spot * size, size, 2)

    summed_ffn = jnp.zeros((3, narrow_count, ffn_size, size), LOW)
    for step in range(narrow_count):
        piece = final_piece(lax.rem(narrow_spot + step, narrow_count))
        if step:
            piece = shifted(piece, "narrow", step)
        source = lax.rem(narrow_spot - step + narrow_count, narrow_count)
        summed_ffn = lax.dynamic_update_index_in_dim(summed_ffn, piece, source, 1)
    turn = lax.rem(wide_spot, 2)
    grad_kv_w = jnp.einsum(
        "wtc,wtf->cf", tok_cols, kv_wide, preferred_element_type=FULL
    ).reshape(columns, narrow_count, 2, kv_size)
    grad_kv_w = jnp.moveaxis(grad_kv_w, 0, 2)
    summed_kv = lax.psum_scatter(grad_kv_w, "narrow", scatter_dimension=0, tiled=True)[0]
    summed_table, table_squares = spread(
        spots, listed, grad_rows.reshape(-1, columns), head_cols_all.reshape(vocab_rows, columns)
    )

    squares = (
        jnp.sum(summed_qo * summed_qo)
        + jnp.sum(summed_kv * summed_kv)
        + ffn_squares
        + jnp.sum(table_squares)
    )
    sums = jnp.stack(
        [gain_attn[0], gain_mid[0], gain_early[0] + gain_late[0], jnp.full((width,), squares)]
    )
    sums, summed_ffn = lax.optimization_barrier((sums, summed_ffn))
    summed_ffn = summed_ffn.reshape(3, ffn_rows, size).astype(FULL)
    sums, kv_owned = launch(
        [
            combine(sums.reshape(4, 8, -1), add_two),
            send_owner(summed_kv.astype(LOW).reshape(2 * block_rows, kv_size)),
        ],
        12,
        "combine_sums",
    )
    sums = sums.reshape(4, width)
    summed_gain = lax.dynamic_slice_in_dim(
        sums[:3], (wide_spot * narrow_count + narrow_spot) * gain_size, gain_size, 1
    )
    square_total = sums[3, 0] + jnp.sum(sums[:3] * sums[:3])
    grad_norm = jnp.sqrt(square_total) / loss_count
    factor = jnp.minimum(1.0, CLIP_NORM / (grad_norm + 1e-06)) / loss_count

    def ffn_owner():
        return newton(factor, mom_owned, owned.reshape(ffn_rows, width))

    def small_owner():
        return newton_small(factor, mom_owned, owned, kv_owned)

    small_spot = lax.rem(3 + turn, narrow_count)
    directions = lax.cond(narrow_spot == small_spot, small_owner, ffn_owner)
    received = [lax.dynamic_index_in_dim(directions, narrow_spot, 0, False)] + [
        shifted(
            lax.dynamic_index_in_dim(
                directions, lax.rem(narrow_spot + step, narrow_count), 0, False
            ),
            "narrow",
            step,
        )
        for step in range(1, narrow_count)
    ]

    def direction_of(matrix):
        step = lax.rem(narrow_spot - matrix - turn + 2 * narrow_count, narrow_count)
        result = received[0]
        for at in range(1, narrow_count):
            result = jnp.where(step == at, received[at], result)
        return result

    dir_ffn = jnp.stack([direction_of(matrix) for matrix in range(3)]).astype(FULL)
    small = direction_of(3).astype(FULL)
    dir_qo = small[: 2 * block_rows].reshape(mom_qo.shape)
    dir_kv = small[2 * block_rows : 2 * block_rows + half_rows].reshape(half_rows, 4, kv_size)
    dir_kv = jnp.moveaxis(dir_kv, 1, 0).reshape(mom_kv.shape)

    embed_new, embed_m_new, embed_v_new = adamw(
        embed, embed_m, embed_v, summed_table * factor, RATE_ADAM, WEIGHT_DECAY
    )
    gains_new, gains_m_new, gains_v_new = adamw(
        gains, gains_m, gains_v, summed_gain * factor, RATE_GAIN, 0.0
    )

    def mom_next(mom, grad):
        return MOMENTUM * mom + jnp.moveaxis(grad * factor, 0, 1)

    shrink = 1.0 - RATE_MUON * WEIGHT_DECAY

    def weight_next(weight, direction):
        return weight * shrink - RATE_MUON * jnp.moveaxis(direction, 0, 1)

    return (
        loss_sum,
        loss_count,
        grad_norm,
        embed_new,
        embed_m_new,
        embed_v_new,
        weight_next(attn_qo, dir_qo),
        mom_next(attn_qo_mom, summed_qo),
        weight_next(attn_kv, dir_kv),
        mom_next(attn_kv_mom, summed_kv),
        weight_next(ffn, dir_ffn),
        mom_next(ffn_mom, summed_ffn),
        gains_new,
        gains_m_new,
        gains_v_new,
    )


def solution(mesh):
    by_pack = P("wide", None)
    table = P("narrow", "wide")
    layer = P("wide", None, "narrow")
    gain = P(None, ("wide", "narrow"))
    return jax.shard_map(
        per_device,
        mesh=mesh,
        in_specs=(by_pack,) * 4 + (P("wide"),) + (table,) * 3 + (layer,) * 6 + (gain,) * 3,
        out_specs=(P(),) * 3 + (table,) * 3 + (layer,) * 6 + (gain,) * 3,
        check_vma=False,
    )
```

```python
import functools

import jax
import jax.numpy as jnp
from jax import lax
from jax.experimental import pallas as pl
from jax.experimental.pallas import tpu as pltpu
from jax.sharding import PartitionSpec as P

HEADS = 16
HD = 128
KVH = 4
NS_STEPS = 5
STEP = 10


NORM_EPS = 1e-05
ROPE_BASE = 10000.0
EXIT_EARLY = 0.25
EXIT_LAST = 1.0
CLIP_NORM = 0.02
BETA_ONE = 0.9
BETA_TWO = 0.95
ADAM_EPS = 1e-08
RATE_ADAM = 0.02
RATE_GAIN = 0.3
RATE_MUON = 0.3
WEIGHT_DECAY = 0.1
MOMENTUM = 0.95
NEWTON_A = 3.4445
NEWTON_B = -4.775
NEWTON_C = 2.0315
MASKED = -1e30
LOW = jnp.bfloat16
FULL = jnp.float32
BOTH = ("wide", "narrow")
UNROLL = 16
VMEM_BYTES = 56 * 1024 * 1024


def dot(first, second, first_dim, second_dim):
    return lax.dot_general(
        first, second, (((first_dim,), (second_dim,)), ((), ())), preferred_element_type=FULL
    )


def norm_rows(values, gain_row):
    return (
        values * lax.rsqrt(jnp.mean(values * values, axis=-1, keepdims=True) + NORM_EPS) * gain_row
    )


def segments_at(lens, where_at):
    ends = jnp.cumsum(lens)
    return jnp.sum((where_at[:, None] >= ends[None, :]).astype(jnp.int32), axis=1)


def angles_at(lens, where_at):
    segment = segments_at(lens, where_at)
    starts = jnp.cumsum(lens) - lens
    member = segment[:, None] == jnp.arange(lens.shape[0], dtype=jnp.int32)[None, :]
    begin = jnp.sum(jnp.where(member, starts[None, :], 0), axis=1)
    offset_pos = (where_at - begin).astype(FULL)
    inverse = ROPE_BASE ** (-2.0 * jnp.arange(HD // 2, dtype=FULL) / HD)
    angle = offset_pos[:, None] * inverse[None, :]
    return (segment, jnp.cos(angle), jnp.sin(angle))


MESH = pl.DeviceIdType.MESH
ANY = pl.BlockSpec(memory_space=pl.ANY)
VMEM = pl.BlockSpec(memory_space=pltpu.VMEM)


def others(axis, count):
    me = lax.axis_index(axis)
    return [{axis: lax.rem(me + step, count)} for step in range(1, count)]


def push(source, target, send, receive, device):
    return pltpu.make_async_remote_copy(
        src_ref=source,
        dst_ref=target,
        send_sem=send,
        recv_sem=receive,
        device_id=device,
        device_id_type=MESH,
    )


def arrived(block, send, receive, device):
    push(block, block, send, receive, device).wait_recv()


def like(values):
    return jax.ShapeDtypeStruct(values.shape, values.dtype)


def struct(shape, dtype):
    return jax.ShapeDtypeStruct(shape, dtype)


def sems(*shape):
    return pltpu.SemaphoreType.DMA(shape)


class Task:
    def __init__(self, inputs, outputs, scratch, steps, place_in, place_out, axes):
        self.inputs, self.outputs, self.scratch, self.steps = inputs, outputs, scratch, steps
        self.place_in = [place_in] * len(inputs)
        self.place_out = [place_out] * len(outputs)
        self.axes = axes


def launch(tasks, ident, name):
    axes = sorted(set(axis for task in tasks for axis in task.axes))
    inputs = [a for task in tasks for a in task.inputs]
    outputs = [a for task in tasks for a in task.outputs]
    scratch = [a for task in tasks for a in task.scratch]

    def body(*refs):
        refs = list(refs)
        ins = refs[: len(inputs)]
        outs = refs[len(inputs) : len(inputs) + len(outputs)]
        extra = refs[len(inputs) + len(outputs) :]
        barrier = pltpu.get_barrier_semaphore()
        targets = [device for axis in axes for device in others(axis, lax.axis_size(axis))]
        for device in targets:
            pl.semaphore_signal(barrier, inc=1, device_id=device, device_id_type=MESH)
        pl.semaphore_wait(barrier, len(targets))
        live = []
        for task in tasks:
            counts = (len(task.inputs), len(task.outputs), len(task.scratch))
            live.append(task.steps(ins[: counts[0]], outs[: counts[1]], extra[: counts[2]]))
            ins, outs, extra = ins[counts[0] :], outs[counts[1] :], extra[counts[2] :]
        while live:
            live = [steps for steps in live if next(steps, 0) is None]

    size = sum(a.size * a.dtype.itemsize for a in list(inputs) + list(outputs))
    return pl.pallas_call(
        body,
        out_shape=outputs,
        in_specs=[place for task in tasks for place in task.place_in],
        out_specs=[place for task in tasks for place in task.place_out],
        scratch_shapes=scratch,
        compiler_params=pltpu.CompilerParams(
            collective_id=ident, has_side_effects=True, vmem_limit_bytes=VMEM_BYTES
        ),
        cost_estimate=pl.CostEstimate(flops=0, bytes_accessed=size // 8, transcendentals=0),
        name=name,
    )(*inputs)


def later(task, turns):
    begin = task.steps

    def steps(ins, outs, scratch):
        for turn in range(turns):
            yield
        yield from begin(ins, outs, scratch)

    task.steps = steps
    return task


def gather_wide(values, patience=1):
    count = lax.axis_size("wide")
    chips = count // 2

    def steps(ins, outs, scratch):
        (x_ref,), (out_ref,), (send, receive, local) = ins, outs, scratch
        me = lax.axis_index("wide")
        mate = me + 1 - 2 * lax.rem(me, 2)
        peers = [lax.rem(me + 2 * step, count) for step in range(1, chips)] + [mate]
        first = []
        for step, peer in enumerate(peers):
            copy = push(x_ref, out_ref.at[me], send.at[step], receive.at[me], {"wide": peer})
            copy.start()
            first.append(copy)
        keep = pltpu.make_async_copy(x_ref, out_ref.at[me], local)
        keep.start()
        for turn in range(patience):
            yield
        second = []
        for step in range(1, chips):
            source = lax.rem(me - 2 * step + count, count)
            block = out_ref.at[source]
            arrived(block, send.at[0], receive.at[source], {"wide": mate})
            copy = push(
                block, block, send.at[chips + step - 1], receive.at[source], {"wide": mate}
            )
            copy.start()
            second.append(copy)
        yield
        for step in range(chips):
            source = lax.rem(mate - 2 * step + count, count)
            arrived(out_ref.at[source], send.at[0], receive.at[source], {"wide": mate})
        for copy in first + second:
            copy.wait_send()
        keep.wait()

    shape = struct((count,) + values.shape, values.dtype)
    return Task(
        [values], [shape], [sems(count - 1), sems(count), sems()], steps, ANY, ANY, ["wide"]
    )


def trade(axis, values, source_of, target_of, shape, patience=2):
    count = lax.axis_size(axis)

    def steps(ins, outs, scratch):
        (x_ref,), (out_ref,), (send, receive, local) = ins, outs, scratch
        me = lax.axis_index(axis)
        copies = []
        for step in range(1, count):
            peer = lax.rem(me + step, count)
            copy = push(
                source_of(x_ref, peer),
                target_of(out_ref, me),
                send.at[step - 1],
                receive.at[me],
                {axis: peer},
            )
            copy.start()
            copies.append(copy)
        keep = pltpu.make_async_copy(source_of(x_ref, me), target_of(out_ref, me), local)
        keep.start()
        for turn in range(patience):
            yield
        for step in range(1, count):
            source = lax.rem(me - step + count, count)
            arrived(
                target_of(out_ref, source), send.at[0], receive.at[source], {axis: source}
            )
        for copy in copies:
            copy.wait_send()
        keep.wait()

    return Task(
        [values],
        [struct(shape, values.dtype)],
        [sems(count - 1), sems(count), sems()],
        steps,
        ANY,
        ANY,
        [axis],
    )


def block_at(ref, spot):
    return ref.at[spot]


def whole_at(ref, spot):
    return ref


def columns_of(size):
    def at(ref, spot):
        return ref.at[:, pl.ds(pl.multiple_of(spot * size, size), size)]

    return at


def turned(ref, spot):
    count = lax.axis_size("narrow")
    matrix = lax.rem(spot + count - lax.rem(lax.axis_index("wide"), 2), count)
    return ref.at[jnp.minimum(matrix, 3)]


def swap_turned(values, patience=2):
    shape = (lax.axis_size("narrow"),) + values.shape[1:]
    return trade("narrow", values, turned, block_at, shape, patience)


def send_owner(values):
    count = lax.axis_size("narrow")

    def steps(ins, outs, scratch):
        (x_ref,), (out_ref,), (send, receive, local) = ins, outs, scratch
        me = lax.axis_index("narrow")
        owner = lax.rem(3 + lax.rem(lax.axis_index("wide"), 2), count)
        keep = pltpu.make_async_copy(x_ref, out_ref.at[me], local)
        keep.start()

        def to_owner():
            return push(x_ref, out_ref.at[me], send.at[0], receive.at[me], {"narrow": owner})

        @pl.when(me != owner)
        def _():
            to_owner().start()

        yield
        yield

        @pl.when(me != owner)
        def _():
            to_owner().wait_send()

        @pl.when(me == owner)
        def _():
            for step in range(1, count):
                source = lax.rem(owner + step, count)
                arrived(out_ref.at[source], send.at[0], receive.at[source], {"narrow": source})

        keep.wait()

    return Task(
        [values],
        [struct((count,) + values.shape, values.dtype)],
        [sems(1), sems(count), sems()],
        steps,
        ANY,
        ANY,
        ["narrow"],
    )


def swap_blocks(axis, values):
    return trade(axis, values, block_at, block_at, values.shape)


def gather_blocks(axis, values):
    shape = (lax.axis_size(axis),) + values.shape
    return trade(axis, values, whole_at, block_at, shape)


def split_columns(axis, values, patience=2):
    count = lax.axis_size(axis)
    rows, size = values.shape[0], values.shape[1] // count
    return trade(axis, values, columns_of(size), block_at, (count, rows, size), patience)


def join_columns(axis, values):
    count, rows, size = values.shape
    return trade(axis, values, block_at, columns_of(size), (rows, count * size))


def collect(count, parts_ref, slots, send, receive):
    me = lax.axis_index("narrow")
    copies = []
    for step in range(1, count):
        peer = lax.rem(me + step, count)
        copy = push(
            parts_ref.at[peer],
            slots.at[me],
            send.at[step - 1],
            receive.at[me],
            {"narrow": peer},
        )
        copy.start()
        copies.append(copy)
    return copies


def collected(count, parts_ref, slots, send, receive):
    me = lax.axis_index("narrow")
    total = parts_ref[me].astype(FULL)
    for step in range(1, count):
        source = lax.rem(me - step + count, count)
        arrived(slots.at[source], send.at[0], receive.at[source], {"narrow": source})
        total = total + slots[source].astype(FULL)
    return total


def share(count, low, all_ref, send, receive):
    me = lax.axis_index("narrow")
    all_ref[me] = low
    copies = []
    for step in range(1, count):
        peer = lax.rem(me + step, count)
        copy = push(
            all_ref.at[me], all_ref.at[me], send.at[step - 1], receive.at[me], {"narrow": peer}
        )
        copy.start()
        copies.append(copy)
    return copies


def shared(count, all_ref, send, receive):
    me = lax.axis_index("narrow")
    for step in range(1, count):
        source = lax.rem(me - step + count, count)
        arrived(all_ref.at[source], send.at[0], receive.at[source], {"narrow": source})


def narrow_sems(count):
    return [sems(count - 1), sems(count)]


def settle(partial, base, other, keep_row, gain_row):
    count = lax.axis_size("narrow")
    rows, width = base.shape

    def steps(ins, outs, scratch):
        parts_ref, base_ref, other_ref, keep_ref, gain_ref = ins
        own_ref, all_ref = outs
        slots, send, receive, send_all, receive_all = scratch
        copies = collect(count, parts_ref, slots, send, receive)
        yield
        total = collected(count, parts_ref, slots, send, receive)
        total = jnp.where(keep_ref[...] > 0, total + base_ref[...], other_ref[...])
        own_ref[...] = total
        low = norm_rows(total, gain_ref[...]).astype(LOW)
        copies = copies + share(count, low, all_ref, send_all, receive_all)
        yield
        shared(count, all_ref, send_all, receive_all)
        for copy in copies:
            copy.wait_send()

    return Task(
        [partial.reshape(count, rows, width), base, other, keep_row, gain_row],
        [struct((rows, width), FULL), struct((count, rows, width), LOW)],
        [pltpu.VMEM((count, rows, width), partial.dtype)]
        + narrow_sems(count)
        + narrow_sems(count),
        steps,
        VMEM,
        VMEM,
        ["narrow"],
    )


def settle_back(partial, values, add, keep_row, gain_row):
    count = lax.axis_size("narrow")
    rows, width = values.shape

    def steps(ins, outs, scratch):
        parts_ref, values_ref, add_ref, keep_ref, gain_ref = ins
        own_ref, gain_grad_ref, all_ref = outs
        slots, send, receive, send_all, receive_all = scratch
        copies = collect(count, parts_ref, slots, send, receive)
        yield
        grad = collected(count, parts_ref, slots, send, receive)
        held = values_ref[...]
        root = lax.rsqrt(jnp.mean(held * held, axis=-1, keepdims=True) + NORM_EPS)
        scaled = gain_ref[...] * grad
        inner = jnp.mean(held * scaled, axis=-1, keepdims=True)
        own = add_ref[...] + root * scaled - held * (root * root * root * inner)
        gain_grad_ref[...] = jnp.sum(held * root * grad, axis=0, keepdims=True)
        own_ref[...] = own
        low = (own * keep_ref[...]).astype(LOW)
        copies = copies + share(count, low, all_ref, send_all, receive_all)
        yield
        shared(count, all_ref, send_all, receive_all)
        for copy in copies:
            copy.wait_send()

    return Task(
        [partial.reshape(count, rows, width), values, add, keep_row, gain_row],
        [
            struct((rows, width), FULL),
            struct((1, width), FULL),
            struct((count, rows, width), LOW),
        ],
        [pltpu.VMEM((count, rows, width), partial.dtype)]
        + narrow_sems(count)
        + narrow_sems(count),
        steps,
        VMEM,
        VMEM,
        ["narrow"],
    )


def sum_narrow(partial):
    count = lax.axis_size("narrow")
    rows, width = partial.shape[0] // count, partial.shape[1]

    def steps(ins, outs, scratch):
        (parts_ref,), (own_ref,), (slots, send, receive) = ins, outs, scratch
        copies = collect(count, parts_ref, slots, send, receive)
        yield
        yield
        own_ref[...] = collected(count, parts_ref, slots, send, receive)
        for copy in copies:
            copy.wait_send()

    return Task(
        [partial.reshape(count, rows, width)],
        [struct((rows, width), FULL)],
        [pltpu.VMEM((count, rows, width), partial.dtype)] + narrow_sems(count),
        steps,
        VMEM,
        VMEM,
        ["narrow"],
    )


def fetch_rows(found, rows):
    deep, wide = lax.axis_size("narrow"), lax.axis_size("wide")
    columns = found.shape[2]

    def steps(ins, outs, scratch):
        (found_ref,), (out_ref,) = ins, outs
        rightward, leftward, final = scratch[:3]
        send_right, receive_right, send_left, receive_left = scratch[3:7]
        send_wide, receive_wide, local = scratch[7:]
        spot = lax.axis_index("narrow")
        me = lax.axis_index("wide")

        def right_copy(part, source):
            return push(
                source,
                rightward.at[part],
                send_right.at[part],
                receive_right.at[part],
                {"narrow": lax.rem(spot + 1, deep)},
            )

        def left_copy(part, source):
            return push(
                source,
                leftward.at[part],
                send_left.at[part],
                receive_left.at[part],
                {"narrow": lax.rem(spot + deep - 1, deep)},
            )

        for step in range(deep - 1):
            right, left = deep - 1 - step, step

            @pl.when((spot == 0) & (right > 0))
            def _():
                right_copy(right, found_ref.at[right]).start()

            @pl.when((spot == deep - 1) & (left < deep - 1))
            def _():
                left_copy(left, found_ref.at[left]).start()

        yield
        for step in range(deep - 1):
            right, left = deep - 1 - step, step

            @pl.when((spot > 0) & (right > spot))
            def _():
                right_copy(right, rightward.at[right]).wait_recv()
                rightward[right] = rightward[right] + found_ref[right]
                right_copy(right, rightward.at[right]).start()

            @pl.when((spot < deep - 1) & (left < spot))
            def _():
                left_copy(left, leftward.at[left]).wait_recv()
                leftward[left] = leftward[left] + found_ref[left]
                left_copy(left, leftward.at[left]).start()

        final[...] = found_ref[spot]

        @pl.when(spot > 0)
        def _():
            right_copy(spot, rightward.at[spot]).wait_recv()
            final[...] = final[...] + rightward[spot]

        @pl.when(spot < deep - 1)
        def _():
            left_copy(spot, leftward.at[spot]).wait_recv()
            final[...] = final[...] + leftward[spot]

        def rows_for(device):
            return final.at[pl.ds(pl.multiple_of(device * rows, rows), rows)]

        def columns_from(device):
            return columns_of(columns)(out_ref, device)

        copies = []
        for step in range(1, wide):
            peer = lax.rem(me + step, wide)
            copy = push(
                rows_for(peer),
                columns_from(me),
                send_wide.at[step - 1],
                receive_wide.at[me],
                {"wide": peer},
            )
            copy.start()
            copies.append(copy)
        keep = pltpu.make_async_copy(rows_for(me), columns_from(me), local)
        keep.start()
        yield
        for step in range(1, wide):
            source = lax.rem(me - step + wide, wide)
            arrived(
                columns_from(source), send_wide.at[0], receive_wide.at[source], {"wide": source}
            )
        yield
        for copy in copies:
            copy.wait_send()
        keep.wait()
        for step in range(deep - 1):
            right, left = deep - 1 - step, step

            @pl.when(right > spot)
            def _():
                right_copy(right, found_ref.at[right]).wait_send()

            @pl.when(left < spot)
            def _():
                left_copy(left, found_ref.at[left]).wait_send()

    task = Task(
        [found],
        [struct((rows, wide * columns), found.dtype)],
        [pltpu.VMEM(found.shape, found.dtype)] * 2
        + [pltpu.VMEM(found.shape[1:], found.dtype)]
        + [sems(deep)] * 4
        + [sems(wide - 1), sems(wide), sems()],
        steps,
        VMEM,
        ANY,
        ["narrow", "wide"],
    )
    return task


def return_rows(rows):
    deep, wide = lax.axis_size("narrow"), lax.axis_size("wide")
    count, width = rows.shape
    columns = width // wide

    def steps(ins, outs, scratch):
        (rows_ref,), (out_ref,) = ins, outs
        send_right, send_left, receive_deep, send_wide, receive_wide, local = scratch
        spot = lax.axis_index("narrow")
        me = lax.axis_index("wide")
        part_of = functools.partial(columns_of(columns), rows_ref)

        def landing(device):
            return out_ref.at[spot, pl.ds(pl.multiple_of(device * count, count), count)]

        copies = []
        for step in range(1, wide):
            peer = lax.rem(me + step, wide)
            copy = push(
                part_of(peer),
                landing(me),
                send_wide.at[step - 1],
                receive_wide.at[me],
                {"wide": peer},
            )
            copy.start()
            copies.append(copy)
        keep = pltpu.make_async_copy(part_of(me), landing(me), local)
        keep.start()
        yield
        for step in range(1, wide):
            source = lax.rem(me - step + wide, wide)
            arrived(landing(source), send_wide.at[0], receive_wide.at[source], {"wide": source})
        keep.wait()

        def right_copy(part):
            return push(
                out_ref.at[part],
                out_ref.at[part],
                send_right.at[part],
                receive_deep.at[part],
                {"narrow": lax.rem(spot + 1, deep)},
            )

        def left_copy(part):
            return push(
                out_ref.at[part],
                out_ref.at[part],
                send_left.at[part],
                receive_deep.at[part],
                {"narrow": lax.rem(spot + deep - 1, deep)},
            )

        @pl.when(spot < deep - 1)
        def _():
            right_copy(spot).start()

        @pl.when(spot > 0)
        def _():
            left_copy(spot).start()

        for step in range(1, deep):
            yield

            @pl.when(spot >= step)
            def _():
                right_copy(spot - step).wait_recv()

                @pl.when(spot < deep - 1)
                def _():
                    right_copy(spot - step).start()

            @pl.when(spot + step < deep)
            def _():
                left_copy(spot + step).wait_recv()

                @pl.when(spot > 0)
                def _():
                    left_copy(spot + step).start()

        for part in range(deep):

            @pl.when((part <= spot) & (spot < deep - 1))
            def _():
                right_copy(part).wait_send()

            @pl.when((part >= spot) & (spot > 0))
            def _():
                left_copy(part).wait_send()

        for copy in copies:
            copy.wait_send()

    return Task(
        [rows],
        [struct((deep, wide * count, columns), rows.dtype)],
        [sems(deep)] * 3 + [sems(wide - 1), sems(wide), sems()],
        steps,
        ANY,
        ANY,
        ["narrow", "wide"],
    )


def sum_wide(partial):
    count = lax.axis_size("wide")
    chips = count // 2
    rows, width = partial.shape[0] // count, partial.shape[1]

    def steps(ins, outs, scratch):
        (parts_ref,), (out_ref,) = ins, outs
        from_mate, paired, slots, send_mate, receive_mate, send, receive = scratch
        me = lax.axis_index("wide")
        side = lax.rem(me, 2)
        mate = me + 1 - 2 * side
        my_chip = me // 2
        mate_copies = []
        for step in range(chips):
            chip = lax.rem(my_chip + 1 + step, chips)
            copy = push(
                parts_ref.at[2 * chip + 1 - side],
                from_mate.at[chip],
                send_mate.at[step],
                receive_mate.at[chip],
                {"wide": mate},
            )
            copy.start()
            mate_copies.append(copy)
        yield
        copies = []
        for step in range(chips):
            chip = lax.rem(my_chip + 1 + step, chips)
            arrived(from_mate.at[chip], send_mate.at[0], receive_mate.at[chip], {"wide": mate})
            both = parts_ref[2 * chip + side].astype(FULL) + from_mate[chip].astype(FULL)
            if step < chips - 1:
                paired[chip] = both.astype(LOW)
                copy = push(
                    paired.at[chip],
                    slots.at[my_chip],
                    send.at[step],
                    receive.at[my_chip],
                    {"wide": 2 * chip + side},
                )
                copy.start()
                copies.append(copy)
            else:
                out_ref[...] = both
        yield
        for step in range(1, chips):
            chip = lax.rem(my_chip - step + chips, chips)
            arrived(slots.at[chip], send.at[0], receive.at[chip], {"wide": 2 * chip + side})
            out_ref[...] = out_ref[...] + slots[chip].astype(FULL)
        for copy in mate_copies + copies:
            copy.wait_send()

    return Task(
        [partial.reshape(count, rows, width)],
        [struct((rows, width), FULL)],
        [pltpu.VMEM((chips, rows, width), LOW)] * 3
        + [sems(chips), sems(chips), sems(max(chips - 1, 1)), sems(chips)],
        steps,
        VMEM,
        VMEM,
        ["wide"],
    )


def merge_stats(first, second):
    peak = jnp.maximum(first[0:1], second[0:1])
    total = first[1:2] * jnp.exp(first[0:1] - peak) + second[1:2] * jnp.exp(second[0:1] - peak)
    return jnp.concatenate([peak, total, first[2:3] + second[2:3]], axis=0)


def add_two(first, second):
    return first + second


def combine(values, join):
    deep, wide = lax.axis_size("narrow"), lax.axis_size("wide")

    def steps(ins, outs, scratch):
        (x_ref,), (out_ref,) = ins, outs
        wide_slots, deep_slots, send_wide, receive_wide, send_deep, receive_deep = scratch

        def start(axis, count, slots, value, send, receive):
            me = lax.axis_index(axis)
            slots[me] = value
            copies = []
            for step in range(1, count):
                peer = lax.rem(me + step, count)
                copy = push(
                    slots.at[me], slots.at[me], send.at[step - 1], receive.at[me], {axis: peer}
                )
                copy.start()
                copies.append(copy)
            return copies

        def finish(axis, count, slots, send, receive):
            me = lax.axis_index(axis)
            for step in range(1, count):
                source = lax.rem(me - step + count, count)
                arrived(slots.at[source], send.at[0], receive.at[source], {axis: source})
            total = slots[0]
            for source in range(1, count):
                total = join(total, slots[source])
            return total

        first = start("wide", wide, wide_slots, x_ref[...], send_wide, receive_wide)
        yield
        total = finish("wide", wide, wide_slots, send_wide, receive_wide)
        second = start("narrow", deep, deep_slots, total, send_deep, receive_deep)
        yield
        out_ref[...] = finish("narrow", deep, deep_slots, send_deep, receive_deep)
        for copy in first + second:
            copy.wait_send()

    return Task(
        [values],
        [like(values)],
        [
            pltpu.VMEM((wide,) + values.shape, values.dtype),
            pltpu.VMEM((deep,) + values.shape, values.dtype),
            sems(wide - 1),
            sems(wide),
            sems(deep - 1),
            sems(deep),
        ],
        steps,
        VMEM,
        VMEM,
        ["narrow", "wide"],
    )


def gather_both(values):
    deep, wide = lax.axis_size("narrow"), lax.axis_size("wide")

    def steps(ins, outs, scratch):
        (x_ref,), (out_ref,) = ins, outs
        send_wide, receive_wide, send_deep, receive_deep = scratch
        me = lax.axis_index("wide")
        spot = lax.axis_index("narrow")
        out_ref[spot, me] = x_ref[...]
        copies = []
        for step in range(1, wide):
            peer = lax.rem(me + step, wide)
            block = out_ref.at[spot, me]
            copy = push(block, block, send_wide.at[step - 1], receive_wide.at[me], {"wide": peer})
            copy.start()
            copies.append(copy)
        yield
        for step in range(1, wide):
            source = lax.rem(me - step + wide, wide)
            block = out_ref.at[spot, source]
            arrived(block, send_wide.at[0], receive_wide.at[source], {"wide": source})
        for step in range(1, deep):
            peer = lax.rem(spot + step, deep)
            block = out_ref.at[spot]
            copy = push(
                block, block, send_deep.at[step - 1], receive_deep.at[spot], {"narrow": peer}
            )
            copy.start()
            copies.append(copy)
        yield
        for step in range(1, deep):
            source = lax.rem(spot - step + deep, deep)
            block = out_ref.at[source]
            arrived(block, send_deep.at[0], receive_deep.at[source], {"narrow": source})
        for copy in copies:
            copy.wait_send()

    return Task(
        [values],
        [struct((deep, wide) + values.shape, values.dtype)],
        [sems(wide - 1), sems(wide), sems(deep - 1), sems(deep)],
        steps,
        VMEM,
        VMEM,
        ["narrow", "wide"],
    )


def turn_heads(values, cosine, sine):
    half = values.shape[1] // 2
    swapped = jnp.concatenate([values[:, half:], values[:, :half]], axis=1)
    return values * cosine + swapped * sine


def wide_angles(cosine, sine):
    return jnp.concatenate([cosine, cosine], axis=1), jnp.concatenate([-sine, sine], axis=1)


def local_call(body, inputs, specs, outputs, flops, name):
    return pl.pallas_call(
        body,
        grid=(1,),
        in_specs=specs,
        out_specs=[
            pl.BlockSpec(a.shape, lambda step, rank=len(a.shape): (0,) * rank) for a in outputs
        ],
        out_shape=outputs,
        compiler_params=pltpu.CompilerParams(vmem_limit_bytes=VMEM_BYTES),
        cost_estimate=pl.CostEstimate(flops=flops, bytes_accessed=8 << 20, transcendentals=0),
        name=name,
    )(*inputs)


def entire(values):
    return pl.BlockSpec(values.shape, lambda step: (0,) * values.ndim)


def column_block(values, size, index):
    return pl.BlockSpec((values.shape[0], size), lambda step: (0, index))


def heads_body(groups, rep, rows_ref, gain_ref, kv_ref, cos_ref, sin_ref, out_ref, normed_ref):
    count, _, _, tok_rows, head = out_ref.shape
    size = kv_ref.shape[1] // (2 * count)
    per_head = head // size
    rows = rows_ref[0:tok_rows, :].astype(FULL)
    normed = norm_rows(rows, gain_ref[...]).astype(LOW)
    normed_ref[...] = normed
    both = dot(normed, kv_ref[...], 1, 0)

    def head_of(kind, index):
        pieces = [
            both[:, (2 * part + kind) * size : (2 * part + kind + 1) * size]
            for part in range(index * per_head, (index + 1) * per_head)
        ]
        return pieces[0] if per_head == 1 else jnp.concatenate(pieces, axis=1)

    for owner in range(count):
        for group in range(groups):
            index = (owner * groups + group) // rep
            keys = turn_heads(head_of(0, index), cos_ref[...], sin_ref[...])
            out_ref[owner, group, 0] = keys.astype(LOW)
            out_ref[owner, group, 1] = head_of(1, index).astype(LOW)


def make_heads(rows_low, gain_row, proj, cosine, sine, groups, rep):
    count = lax.axis_size("narrow")
    tok_rows, head = cosine.shape
    width = rows_low.shape[1]
    size = 2 * KVH * HD
    return local_call(
        functools.partial(heads_body, groups, rep),
        [rows_low, gain_row, proj, cosine, sine],
        [entire(rows_low), entire(gain_row), column_block(proj, size, 0)]
        + [entire(cosine), entire(sine)],
        [struct((count, groups, 2, tok_rows, head), LOW), struct((tok_rows, width), LOW)],
        2 * tok_rows * width * size,
        "make_heads",
    )


def attend_body(
    start_ref,
    gains_ref,
    q_ref,
    o_ref,
    kv_ref,
    cos_ref,
    sin_ref,
    seg_ref,
    seg_all_ref,
    pick_ref,
    queries_ref,
    probs_ref,
    mixed_ref,
    part_ref,
    normed_ref,
    early_ref,
):
    count, groups, _, tok_rows, head = kv_ref.shape
    heads_own = probs_ref.shape[0]
    start = start_ref[...].astype(FULL)
    root = lax.rsqrt(jnp.mean(start * start, axis=-1, keepdims=True) + NORM_EPS)
    normed = (start * root * gains_ref[0:1, :]).astype(LOW)
    normed_ref[...] = normed
    early_ref[...] = (start * root * gains_ref[2:3, :]).astype(LOW)
    queries = dot(normed, q_ref[...], 1, 0)
    spots = lax.broadcasted_iota(jnp.int32, (1, count * tok_rows), 1)
    allowed = (seg_ref[...] == seg_all_ref[...]) & (pick_ref[...] >= spots)
    for group in range(groups):
        keys = jnp.concatenate([kv_ref[part, group, 0] for part in range(count)], axis=0)
        values = jnp.concatenate([kv_ref[part, group, 1] for part in range(count)], axis=0)
        for member in range(heads_own // groups):
            at = group * (heads_own // groups) + member
            spot = slice(at * head, (at + 1) * head)
            query = turn_heads(queries[:, spot], cos_ref[...], sin_ref[...]).astype(LOW)
            queries_ref[:, spot] = query
            scores = jnp.where(allowed, dot(query, keys, 1, 1) * head ** (-0.5), MASKED)
            shifted = jnp.exp(scores - jnp.max(scores, axis=-1, keepdims=True))
            probs = shifted / jnp.sum(shifted, axis=-1, keepdims=True)
            probs_ref[at] = probs
            mixed_ref[:, spot] = dot(probs.astype(LOW), values, 1, 0).astype(LOW)
    part_ref[...] = dot(mixed_ref[...], o_ref[...], 1, 1).astype(LOW)


def attend(start_low, gains, proj, own_head, cosine, sine, seg, seg_all, picks):
    count, groups, _, tok_rows, head = own_head.shape
    sel, width = start_low.shape
    heads_own = HEADS // count
    size = heads_own * head
    first = 2 * KVH * HD // size
    seq_len = count * tok_rows
    return local_call(
        attend_body,
        [start_low, gains, proj, proj, own_head, cosine, sine, seg, seg_all, picks],
        [
            entire(start_low),
            entire(gains),
            column_block(proj, size, first),
            column_block(proj, size, first + 1),
        ]
        + [entire(a) for a in (own_head, cosine, sine, seg, seg_all, picks)],
        [
            struct((sel, size), LOW),
            struct((heads_own, sel, seq_len), FULL),
            struct((sel, size), LOW),
            struct((sel, width), LOW),
            struct((sel, width), LOW),
            struct((sel, width), LOW),
        ],
        4 * sel * size * (width + seq_len),
        "attend",
    )


def attend_back_body(
    grad_ref,
    q_ref,
    o_ref,
    kv_ref,
    queries_ref,
    probs_ref,
    cos_ref,
    sin_ref,
    cos_all_ref,
    sin_all_ref,
    out_ref,
    grad_q_ref,
    part_ref,
):
    count, groups, _, tok_rows, head = kv_ref.shape
    heads_own = probs_ref.shape[0]
    scale = head ** (-0.5)
    grad_mixed = dot(grad_ref[...], o_ref[...], 1, 0).astype(LOW)
    for group in range(groups):
        keys = jnp.concatenate([kv_ref[part, group, 0] for part in range(count)], axis=0)
        values = jnp.concatenate([kv_ref[part, group, 1] for part in range(count)], axis=0)
        grad_keys = jnp.zeros(keys.shape, FULL)
        grad_values = jnp.zeros(keys.shape, FULL)
        for member in range(heads_own // groups):
            at = group * (heads_own // groups) + member
            spot = slice(at * head, (at + 1) * head)
            probs = probs_ref[at]
            grad_probs = dot(grad_mixed[:, spot], values, 1, 1)
            inner = jnp.sum(probs * grad_probs, axis=-1, keepdims=True)
            grad_scores = (probs * (grad_probs - inner)).astype(LOW)
            grad_query = dot(grad_scores, keys, 1, 0) * scale
            grad_q_ref[:, spot] = turn_heads(grad_query, cos_ref[...], -sin_ref[...]).astype(LOW)
            grad_keys = grad_keys + dot(grad_scores, queries_ref[:, spot], 0, 0)
            grad_values = grad_values + dot(probs.astype(LOW), grad_mixed[:, spot], 0, 0)
        grad_keys = turn_heads(grad_keys * scale, cos_all_ref[...], -sin_all_ref[...])
        for part in range(count):
            rows = slice(part * tok_rows, (part + 1) * tok_rows)
            out_ref[part, group, 0] = grad_keys[rows].astype(LOW)
            out_ref[part, group, 1] = grad_values[rows].astype(LOW)
    part_ref[...] = dot(grad_q_ref[...], q_ref[...], 1, 1).astype(LOW)


def attend_back(grad, proj, own_head, queries, probs, cosine, sine, cosine_all, sine_all):
    count, groups, _, tok_rows, head = own_head.shape
    sel, width = grad.shape
    size = queries.shape[1]
    first = 2 * KVH * HD // size
    return local_call(
        attend_back_body,
        [grad, proj, proj, own_head, queries, probs, cosine, sine, cosine_all, sine_all],
        [entire(grad), column_block(proj, size, first), column_block(proj, size, first + 1)]
        + [
            entire(a)
            for a in (own_head, queries, probs, cosine, sine, cosine_all, sine_all)
        ],
        [struct(own_head.shape, LOW), struct((sel, size), LOW), struct((sel, width), LOW)],
        8 * sel * size * width,
        "attend_back",
    )


def norm_back_rows(values, gain_row, grad):
    root = lax.rsqrt(jnp.mean(values * values, axis=-1, keepdims=True) + NORM_EPS)
    scaled = gain_row * grad
    inner = jnp.mean(values * scaled, axis=-1, keepdims=True)
    result = root * scaled - values * (root * root * root * inner)
    return result, jnp.sum(values * root * grad, axis=0, keepdims=True)


def rows_back_body(
    rep,
    rows_ref,
    gains_ref,
    kv_ref,
    heads_ref,
    pick_ref,
    early_ref,
    base_ref,
    out_ref,
    attn_gain_ref,
    early_gain_ref,
    grad_kv_ref,
):
    count, groups, _, tok_rows, head = heads_ref.shape
    size = kv_ref.shape[1] // (2 * count)
    per_head = head // size
    for index in range(KVH):
        for kind in range(2):
            copies = [
                heads_ref[at // groups, at % groups, kind]
                for at in range(index * rep, (index + 1) * rep)
            ]
            total = copies[0]
            if rep > 1:
                total = sum(copy.astype(FULL) for copy in copies).astype(LOW)
            for piece in range(per_head):
                lane = (2 * (index * per_head + piece) + kind) * size
                grad_kv_ref[:, lane : lane + size] = total[:, piece * size : (piece + 1) * size]
    values = rows_ref[...].astype(FULL)
    own = values[tok_rows:]
    tok_part, tok_gain = norm_back_rows(
        values[:tok_rows], gains_ref[0:1, :], dot(grad_kv_ref[...], kv_ref[...], 1, 1)
    )
    pick_part, pick_gain = norm_back_rows(own, gains_ref[0:1, :], pick_ref[...])
    early_part, early_gain = norm_back_rows(own, gains_ref[2:3, :], early_ref[...])
    attn_gain_ref[...] = tok_gain + pick_gain
    early_gain_ref[...] = early_gain
    out_ref[0:tok_rows, :] = tok_part.astype(LOW)
    out_ref[tok_rows:, :] = (pick_part + early_part + base_ref[...]).astype(LOW)


def rows_back(rows_low, gains, proj, heads, grad_pick, grad_early, base, rep):
    tok_rows = heads.shape[3]
    width = rows_low.shape[1]
    size = 2 * KVH * HD
    return local_call(
        functools.partial(rows_back_body, rep),
        [rows_low, gains, proj, heads, grad_pick, grad_early, base],
        [entire(rows_low), entire(gains), column_block(proj, size, 0)]
        + [entire(a) for a in (heads, grad_pick, grad_early, base)],
        [
            struct(rows_low.shape, LOW),
            struct((1, width), FULL),
            struct((1, width), FULL),
            struct((tok_rows, size), LOW),
        ],
        2 * tok_rows * width * size,
        "rows_back",
    )


def assemble_body(out_columns, *refs):
    pieces, out_ref = refs[:-1], refs[-1]
    count = len(pieces)
    me = lax.axis_index("narrow")
    for step, piece in enumerate(pieces):
        source = lax.rem(me - step + count, count)
        spot = pl.ds(pl.multiple_of(source * out_columns, out_columns), out_columns)
        out_ref[:, spot] = piece[...]


def assemble(pieces):
    rows, columns = pieces[0].shape
    outputs = [struct((rows, columns * len(pieces)), pieces[0].dtype)]
    return local_call(
        functools.partial(assemble_body, columns),
        list(pieces),
        [entire(piece) for piece in pieces],
        outputs,
        0,
        "assemble",
    )[0]


def feed_body(inner_ref, weight_ref, gate_ref, up_ref, hidden_ref, out_ref, total):
    part = pl.program_id(0)
    inner = inner_ref[...]
    gate = dot(inner, weight_ref[0, 0], 1, 1)
    up = dot(inner, weight_ref[0, 1], 1, 1)
    hidden = (jax.nn.silu(gate) * up).astype(LOW)
    gate_ref[0] = gate
    up_ref[0] = up
    hidden_ref[0] = hidden
    product = dot(hidden, weight_ref[0, 2], 1, 0)

    @pl.when(part == 0)
    def _():
        total[...] = product

    @pl.when(part > 0)
    def _():
        total[...] = total[...] + product

    @pl.when(part == pl.num_programs(0) - 1)
    def _():
        out_ref[...] = total[...].astype(LOW)


def feed(inner, weight):
    parts, _, size, width = weight.shape
    sel = inner.shape[0]
    same = pl.BlockSpec((sel, width), lambda part: (0, 0))
    slab = pl.BlockSpec((1, sel, size), lambda part: (part, 0, 0))
    return pl.pallas_call(
        feed_body,
        grid=(parts,),
        in_specs=[same, pl.BlockSpec((1, 3, size, width), lambda part: (part, 0, 0, 0))],
        out_specs=[slab, slab, slab, same],
        out_shape=[
            struct((parts, sel, size), FULL),
            struct((parts, sel, size), FULL),
            struct((parts, sel, size), LOW),
            struct((sel, width), LOW),
        ],
        scratch_shapes=[pltpu.VMEM((sel, width), FULL)],
        compiler_params=pltpu.CompilerParams(vmem_limit_bytes=VMEM_BYTES),
        cost_estimate=pl.CostEstimate(
            flops=6 * sel * parts * size * width,
            bytes_accessed=weight.size * 2,
            transcendentals=0,
        ),
        name="feed",
    )(inner, weight)


def feed_back_body(grad_ref, weight_ref, gate_ref, up_ref, hidden_ref, acts_ref, out_ref, total):
    part = pl.program_id(0)
    grad_hidden = dot(grad_ref[...], weight_ref[0, 2], 1, 1)
    gate = gate_ref[0]
    sigma = jax.nn.sigmoid(gate)
    grad_gate = (grad_hidden * up_ref[0] * sigma * (1.0 + gate * (1.0 - sigma))).astype(LOW)
    grad_up = (grad_hidden * gate * sigma).astype(LOW)
    acts_ref[0, 0] = grad_gate
    acts_ref[0, 1] = grad_up
    acts_ref[0, 2] = hidden_ref[0]
    product = dot(grad_gate, weight_ref[0, 0], 1, 0) + dot(grad_up, weight_ref[0, 1], 1, 0)

    @pl.when(part == 0)
    def _():
        total[...] = product

    @pl.when(part > 0)
    def _():
        total[...] = total[...] + product

    @pl.when(part == pl.num_programs(0) - 1)
    def _():
        out_ref[...] = total[...].astype(LOW)


def feed_back(grad, weight, gate, up, hidden):
    parts, _, size, width = weight.shape
    sel = grad.shape[0]
    same = pl.BlockSpec((sel, width), lambda part: (0, 0))
    slab = pl.BlockSpec((1, sel, size), lambda part: (part, 0, 0))
    return pl.pallas_call(
        feed_back_body,
        grid=(parts,),
        in_specs=[same, pl.BlockSpec((1, 3, size, width), lambda part: (part, 0, 0, 0))]
        + [slab] * 3,
        out_specs=[pl.BlockSpec((1, 3, sel, size), lambda part: (part, 0, 0, 0)), same],
        out_shape=[struct((parts, 3, sel, size), LOW), struct((sel, width), LOW)],
        scratch_shapes=[pltpu.VMEM((sel, width), FULL)],
        compiler_params=pltpu.CompilerParams(vmem_limit_bytes=VMEM_BYTES),
        cost_estimate=pl.CostEstimate(
            flops=6 * sel * parts * size * width,
            bytes_accessed=weight.size * 2,
            transcendentals=0,
        ),
        name="feed_back",
    )(grad, weight, gate, up, hidden)


def newton_steps(problems):
    rows, width = problems[0][0].shape
    block = min(512, width)
    eye = lax.broadcasted_iota(jnp.int32, (rows, rows), 0) == lax.broadcasted_iota(
        jnp.int32, (rows, rows), 1
    )

    def strip(part):
        return pl.ds(pl.multiple_of(part * block, block), block)

    def over(function, start):
        return lax.fori_loop(0, width // block, function, start)

    def add_squares(part, totals):
        values = [current[:, strip(part)] for current, low, gram, rest in problems]
        return [total + jnp.sum(value * value) for total, value in zip(totals, values)]

    totals = over(add_squares, [jnp.float32(0.0)] * len(problems))
    scales = [1.0 / (jnp.sqrt(total) + 1e-07) for total in totals]

    def begin(part, carry):
        for scale, (current, low, gram, rest) in zip(scales, problems):
            values = current[:, strip(part)] * scale
            current[:, strip(part)] = values
            low[:, strip(part)] = values.astype(LOW)
        return carry

    over(begin, 0)

    def iteration(turn, carry):
        for current, low, gram, rest in problems:
            gram[...] = jnp.zeros_like(gram)

        def add_gram(part, carry):
            for current, low, gram, rest in problems:
                values = low[:, strip(part)]
                gram[...] = gram[...] + dot(values, values, 1, 1)
            return carry

        over(add_gram, 0)
        seconds = []
        for current, low, gram, rest in problems:
            whole = gram[...]
            middle = jnp.sum(jnp.where(eye, whole, 0.0)) / rows
            rest[...] = (whole - jnp.where(eye, middle, 0.0)).astype(LOW)
            square = dot(rest[...], rest[...], 1, 0)
            whole = gram[...]
            centred = whole - jnp.where(eye, middle, 0.0)
            square = square + 2.0 * middle * centred + jnp.where(eye, middle * middle, 0.0)
            whole = NEWTON_B * whole + NEWTON_C * square
            second = jnp.sum(jnp.where(eye, whole, 0.0)) / rows
            rest[...] = (whole - jnp.where(eye, second, 0.0)).astype(LOW)
            seconds.append(second)

        def apply(part, carry):
            for second, (current, low, gram, rest) in zip(seconds, problems):
                values = (NEWTON_A + second) * current[:, strip(part)] + dot(
                    rest[...], low[:, strip(part)], 1, 0
                )
                current[:, strip(part)] = values
                low[:, strip(part)] = values.astype(LOW)
            return carry

        over(apply, 0)
        return carry

    lax.fori_loop(0, NS_STEPS, iteration, 0)


def newton_scratch(rows, width):
    return [
        pltpu.VMEM((rows, width), FULL),
        pltpu.VMEM((rows, width), LOW),
        pltpu.VMEM((rows, rows), FULL),
        pltpu.VMEM((rows, rows), LOW),
    ]


def newton_cost(count, rows, width):
    return pl.CostEstimate(
        flops=NS_STEPS * count * (4 * rows * rows * width + 2 * rows * rows * rows),
        bytes_accessed=6 * count * rows * width,
        transcendentals=0,
    )


def newton_body(factor_ref, mom_ref, grad_ref, out_ref, *problem):
    current, low = problem[:2]
    parts, rows, columns = mom_ref.shape
    factor = factor_ref[0]
    for part in range(parts):
        spot = slice(part * columns, (part + 1) * columns)
        current[:, spot] = MOMENTUM * mom_ref[part].astype(FULL) + factor * grad_ref[
            :, spot
        ].astype(FULL)
    newton_steps([problem])
    for part in range(parts):
        out_ref[part] = low[:, part * columns : (part + 1) * columns]


def newton(factor, mom, grad):
    parts, rows, columns = mom.shape
    width = parts * columns
    return pl.pallas_call(
        newton_body,
        in_specs=[pl.BlockSpec(memory_space=pltpu.SMEM), VMEM, VMEM],
        out_specs=VMEM,
        out_shape=struct(mom.shape, LOW),
        scratch_shapes=newton_scratch(rows, width),
        compiler_params=pltpu.CompilerParams(vmem_limit_bytes=VMEM_BYTES),
        cost_estimate=newton_cost(1, rows, width),
        name="newton",
    )(factor.reshape(1), mom, grad)


def newton_small_body(rows, factor_ref, mom_ref, grad_ref, kv_ref, out_ref, *scratch):
    problems = [scratch[4 * at : 4 * at + 4] for at in range(4)]
    parts, _, columns = mom_ref.shape
    kv_columns = kv_ref.shape[2]
    half = rows // 2
    factor = factor_ref[0]
    for part in range(parts):
        spot = slice(part * columns, (part + 1) * columns)
        for member in range(2):
            current = problems[member][0]
            here = slice(member * rows, (member + 1) * rows)
            mom, grad = mom_ref[part, here, :], grad_ref[part, here, :]
            current[:, spot] = MOMENTUM * mom.astype(FULL) + factor * grad.astype(FULL)
        spot = slice(part * kv_columns, (part + 1) * kv_columns)
        for member in range(2):
            current = problems[2 + member][0]
            piece = kv_ref[part, member * rows : (member + 1) * rows, :].astype(FULL)
            for side in range(2):
                lane = (2 * member + side) * kv_columns
                mom = mom_ref[part, 2 * rows : 2 * rows + half, lane : lane + kv_columns]
                here = slice(side * half, (side + 1) * half)
                current[here, spot] = MOMENTUM * mom.astype(FULL) + factor * piece[here]
    newton_steps(problems[:2])
    newton_steps(problems[2:])
    out_ref[...] = jnp.zeros_like(out_ref)
    for part in range(parts):
        for member in range(2):
            out_ref[part, member * rows : (member + 1) * rows, :] = problems[member][1][
                :, part * columns : (part + 1) * columns
            ]
            low = problems[2 + member][1]
            for side in range(2):
                lane = (2 * member + side) * kv_columns
                out_ref[part, 2 * rows : 2 * rows + half, lane : lane + kv_columns] = low[
                    side * half : (side + 1) * half,
                    part * kv_columns : (part + 1) * kv_columns,
                ]


def newton_small(factor, mom, grad, kv_grad):
    parts, _, columns = mom.shape
    rows = kv_grad.shape[1] // 2
    kv_width = parts * kv_grad.shape[2]
    return pl.pallas_call(
        functools.partial(newton_small_body, rows),
        in_specs=[pl.BlockSpec(memory_space=pltpu.SMEM), VMEM, VMEM, VMEM],
        out_specs=VMEM,
        out_shape=struct(mom.shape, LOW),
        scratch_shapes=newton_scratch(rows, parts * columns) * 2
        + newton_scratch(rows, kv_width) * 2,
        compiler_params=pltpu.CompilerParams(vmem_limit_bytes=VMEM_BYTES),
        cost_estimate=newton_cost(2, rows, parts * columns),
        name="newton_small",
    )(factor.reshape(1), mom, grad, kv_grad)


def lookup_body(ids_ref, turn_ref, table_ref, out_ref, low_ref, list_ref, held, rows, sem):
    vocab = table_ref.shape[0]
    count = out_ref.shape[0]
    load = pltpu.make_async_copy(table_ref, held, sem)
    load.start()
    rows[...] = jnp.zeros_like(rows)

    found = turn_ref[count]

    def note(group, carry):
        for member in range(UNROLL):
            at = group * UNROLL + member
            list_ref[turn_ref[at]] = at
        return carry

    lax.fori_loop(0, count // UNROLL, note, 0)
    for member in range(UNROLL):
        list_ref[found + member] = count
    list_ref[count + UNROLL] = found
    load.wait()

    def step(group, carry):
        for member in range(UNROLL):
            at = list_ref[group * UNROLL + member]
            spot = jnp.minimum(ids_ref[jnp.minimum(at, count - 1)], vocab - 1)
            rows[pl.ds(at, 1), :] = held[pl.ds(spot, 1), :]
        return carry

    lax.fori_loop(0, (found + UNROLL - 1) // UNROLL, step, 0)
    out_ref[...] = rows[pl.ds(0, count), :].astype(LOW)
    low_ref[...] = held[...].astype(LOW)


def lookup(table, ids):
    vocab, columns = table.shape
    count = ids.shape[0]
    mine = (ids < vocab).reshape(-1, 128)
    before = jnp.arange(128)[:, None] < jnp.arange(128)[None, :]
    in_row = dot(mine.astype(LOW), before.astype(LOW), 1, 0)
    per_row = jnp.sum(mine.astype(FULL), axis=1)
    lines = jnp.arange(mine.shape[0])
    ahead = jnp.sum(jnp.where(lines[:, None] > lines[None, :], per_row[None, :], 0.0), axis=1)
    found = jnp.sum(per_row).astype(jnp.int32)
    turns = (in_row + ahead[:, None]).astype(jnp.int32)
    turns = jnp.where(mine, turns, count + UNROLL + 1).reshape(-1)
    turns = jnp.concatenate([turns, jnp.full((128,), found)])
    return pl.pallas_call(
        lookup_body,
        in_specs=[pl.BlockSpec(memory_space=pltpu.SMEM)] * 2 + [ANY],
        out_specs=[VMEM, VMEM, pl.BlockSpec(memory_space=pltpu.SMEM)],
        scratch_shapes=[
            pltpu.VMEM((vocab, columns), FULL),
            pltpu.VMEM((count + 8, columns), FULL),
            pltpu.SemaphoreType.DMA,
        ],
        out_shape=[
            struct((count, columns), LOW),
            struct((vocab, columns), LOW),
            struct((count + 2 * UNROLL,), jnp.int32),
        ],
        compiler_params=pltpu.CompilerParams(vmem_limit_bytes=VMEM_BYTES),
        cost_estimate=pl.CostEstimate(
            flops=0, bytes_accessed=vocab * columns * 4, transcendentals=0
        ),
        name="lookup",
    )(ids, turns, table)


def spread_body(
    ids_ref, list_ref, rows_ref, head_ref, out_ref, square_ref, even, odd, rows, sem
):
    vocab = out_ref.shape[0]
    count = rows_ref.shape[0]
    chunk = 256

    def strip(part):
        return pl.ds(pl.multiple_of(part * chunk, chunk), chunk)

    def begin(part, carry):
        even[strip(part), :] = head_ref[strip(part), :].astype(FULL)
        odd[strip(part), :] = jnp.zeros((chunk, odd.shape[1]), FULL)
        return carry

    lax.fori_loop(0, vocab // chunk, begin, 0)

    def widen(part, carry):
        rows[strip(part), :] = rows_ref[strip(part), :].astype(FULL)
        return carry

    lax.fori_loop(0, count // chunk, widen, 0)
    rows[pl.ds(count, 8), :] = jnp.zeros((8, rows.shape[1]), FULL)

    def step(group, carry):
        for member in range(UNROLL):
            at = list_ref[group * UNROLL + member]
            spot = jnp.minimum(ids_ref[jnp.minimum(at, count - 1)], vocab - 1)
            total = even if member % 2 == 0 else odd
            total[pl.ds(spot, 1), :] = total[pl.ds(spot, 1), :] + rows[pl.ds(at, 1), :]
        return carry

    found = list_ref[count + UNROLL]
    lax.fori_loop(0, (found + UNROLL - 1) // UNROLL, step, 0)

    def finish(part, squares):
        value = even[strip(part), :] + odd[strip(part), :]
        even[strip(part), :] = value
        return squares + jnp.sum((value * value).reshape(chunk // 8, 8, -1), axis=0)

    square_ref[...] = lax.fori_loop(
        0, vocab // chunk, finish, jnp.zeros((8, even.shape[1]), FULL)
    )
    store = pltpu.make_async_copy(even, out_ref, sem)
    store.start()
    store.wait()


def spread(ids, listed, rows, head):
    vocab, columns = head.shape
    count = ids.shape[0]
    smem = pl.BlockSpec(memory_space=pltpu.SMEM)
    return pl.pallas_call(
        spread_body,
        in_specs=[smem, smem, VMEM, VMEM],
        out_specs=[ANY, VMEM],
        scratch_shapes=[
            pltpu.VMEM((vocab, columns), FULL),
            pltpu.VMEM((vocab, columns), FULL),
            pltpu.VMEM((count + 8, columns), FULL),
            pltpu.SemaphoreType.DMA,
        ],
        out_shape=[struct((vocab, columns), FULL), struct((8, columns), FULL)],
        compiler_params=pltpu.CompilerParams(vmem_limit_bytes=VMEM_BYTES),
        cost_estimate=pl.CostEstimate(
            flops=count * columns, bytes_accessed=vocab * columns * 8, transcendentals=0
        ),
        name="spread",
    )(ids, listed, rows, head)


def adamw(weight, first_m, second_m, grad, rate, decay):
    first_new = BETA_ONE * first_m + (1.0 - BETA_ONE) * grad
    second_new = BETA_TWO * second_m + (1.0 - BETA_TWO) * grad * grad
    update = (
        first_new
        / (1.0 - BETA_ONE**STEP)
        / (jnp.sqrt(second_new / (1.0 - BETA_TWO**STEP)) + ADAM_EPS)
    )
    return (weight * (1.0 - rate * decay) - rate * update, first_new, second_new)


def cut_columns(values, count):
    rows, columns = values.shape
    return jnp.moveaxis(values.reshape(rows, count, columns // count), 1, 0)


def shifted(parts, axis, step):
    count = lax.axis_size(axis)
    pairs = [(source, (source + step) % count) for source in range(count)]
    return lax.ppermute(parts, axis, pairs)


def per_device(
    tokens,
    picks,
    targets,
    lengths,
    skip,
    embed,
    embed_m,
    embed_v,
    attn_qo,
    attn_qo_mom,
    attn_kv,
    attn_kv_mom,
    ffn,
    ffn_mom,
    gains,
    gains_m,
    gains_v,
):
    wide_count = lax.axis_size("wide")
    narrow_count = lax.axis_size("narrow")
    narrow_spot = lax.axis_index("narrow")
    wide_spot = lax.axis_index("wide")
    seq_len = tokens.shape[1]
    sel = picks.shape[1]
    vocab_rows, columns = embed.shape
    width = columns * wide_count
    own_rows = sel // narrow_count
    tok_rows = seq_len // narrow_count
    all_rows = own_rows + tok_rows
    heads_own = HEADS // narrow_count
    head_cols = heads_own * HD
    repeat = max(1, narrow_count // KVH)
    groups = KVH * repeat // narrow_count
    ffn_rows = ffn.shape[0]
    ffn_size = ffn_rows // narrow_count
    total_rows = wide_count * sel
    lens = lengths[0]
    pick_ids = picks[0]
    keep_layer = (1 - skip[0]).astype(FULL)
    keep_row = jnp.full((1, width), keep_layer)
    lanes = 128

    def box(flat):
        height = -(-flat.shape[0] // (8 * lanes)) * 8
        return jnp.pad(flat, (0, height * lanes - flat.shape[0])).reshape(height, lanes)

    ffn_low = jnp.moveaxis(ffn, 1, 0).astype(LOW)
    ffn_cut = ffn_low.reshape(3, narrow_count, ffn_size, ffn_low.shape[2])
    ffn_cut = jnp.moveaxis(ffn_cut, 1, 0).reshape(narrow_count, 3 * ffn_size, -1)
    kv_own = attn_kv.reshape(columns, -1).astype(LOW)

    where_at = jnp.arange(seq_len, dtype=jnp.int32)
    pick_tokens = jnp.sum(
        jnp.where(pick_ids[:, None] == where_at[None, :], tokens[0][None, :], 0), axis=1
    )
    ints = box(jnp.concatenate([tokens[0], pick_tokens, targets[0]]))
    all_ints, all_gains, kv_part = launch(
        [
            gather_wide(ints),
            gather_both(box(gains.astype(LOW).astype(FULL).reshape(-1))),
            gather_blocks("narrow", kv_own),
        ],
        0,
        "gather_ids",
    )
    kv_part = jnp.moveaxis(kv_part, 0, 1).reshape(columns, -1)
    proj_own = jnp.concatenate([kv_part, attn_qo.reshape(columns, -1).astype(LOW)], axis=1)
    proj = lax.all_gather(proj_own, "wide", axis=0, tiled=True)
    ffn_cut, all_ints = lax.optimization_barrier((ffn_cut, all_ints))
    ffn_pieces = [lax.dynamic_index_in_dim(ffn_cut, narrow_spot, 0, False)] + [
        shifted(
            lax.dynamic_index_in_dim(
                ffn_cut, lax.rem(narrow_spot + step, narrow_count), 0, False
            ),
            "narrow",
            step,
        )
        for step in range(1, narrow_count)
    ]
    gain_size = gains.shape[1]
    gain_w = all_gains.reshape(narrow_count, wide_count, -1)[:, :, : 3 * gain_size]
    gain_w = gain_w.reshape(narrow_count, wide_count, 3, gain_size)
    gain_w = jnp.transpose(gain_w, (2, 1, 0, 3)).reshape(3, width)
    all_ints = all_ints.reshape(wide_count, -1)
    tokens_all = all_ints[:, :seq_len].reshape(wide_count, narrow_count, tok_rows)
    picked_all = all_ints[:, seq_len : seq_len + sel].reshape(wide_count, narrow_count, own_rows)
    targets_all = all_ints[:, seq_len + sel : seq_len + 2 * sel].reshape(-1)
    wanted = jnp.moveaxis(jnp.concatenate([tokens_all, picked_all], axis=2), 1, 0).reshape(-1)
    local_ids = wanted - narrow_spot * vocab_rows
    inside = (local_ids >= 0) & (local_ids < vocab_rows)
    spots = jnp.where(inside, local_ids, vocab_rows)
    found, embed_low, listed = lookup(embed, spots)
    ffn_pieces, found = lax.optimization_barrier((ffn_pieces, found))
    ffn_sub = assemble(ffn_pieces).reshape(3, ffn_size, width)
    ffn_sub, found = lax.optimization_barrier((ffn_sub, found))
    ffn_w = lax.all_gather(ffn_sub, "wide", axis=0)
    found = found.reshape(narrow_count, wide_count * all_rows, columns)
    embed_cut = embed_low.reshape(wide_count, vocab_rows // wide_count, columns)
    table_half = embed_cut.shape[1] // 2
    rows_low = launch([fetch_rows(found, all_rows)], 1, "fetch_rows")[0]

    mom_qo = jnp.moveaxis(attn_qo_mom, 1, 0)
    mom_kv = jnp.moveaxis(attn_kv_mom, 1, 0)
    mom_ffn = jnp.moveaxis(ffn_mom, 1, 0)
    slot_rows, slot_cols = mom_ffn.shape[1:]

    block_rows, q_size = mom_qo.shape[1:]
    kv_size = mom_kv.shape[2]
    half_rows = block_rows // 2
    kv_box = jnp.moveaxis(mom_kv.reshape(4, half_rows, kv_size), 0, 1).reshape(half_rows, -1)
    small_box = jnp.concatenate([mom_qo.reshape(2 * block_rows, q_size), kv_box])
    small_box = jnp.pad(small_box, ((0, slot_rows - small_box.shape[0]), (0, 0)))
    mom_parts = jnp.concatenate([mom_ffn, small_box[None]]).astype(LOW)

    seg_all, cosine_all, sine_all = angles_at(lens, where_at)
    cosine_all, sine_all = wide_angles(cosine_all, sine_all)
    seg_mine, cosine, sine = angles_at(lens, pick_ids)
    cosine, sine = wide_angles(cosine, sine)

    def tok_part(angles):
        return lax.dynamic_slice_in_dim(angles, narrow_spot * tok_rows, tok_rows, 0)

    by_head, normed_tok = make_heads(
        rows_low, gain_w[0:1], proj, tok_part(cosine_all), tok_part(sine_all), groups, repeat
    )
    own_head, start_low, tok_cols = launch(
        [
            swap_blocks("narrow", by_head),
            gather_blocks("narrow", rows_low[tok_rows:]),
            split_columns("wide", normed_tok),
        ],
        2,
        "trade_heads",
    )
    start_low, ffn_w = lax.optimization_barrier((start_low, ffn_w))
    start_low = start_low.reshape(sel, width)
    queries, probs, mixed, attn_part, normed, early_part = attend(
        start_low,
        gain_w,
        proj,
        own_head,
        cosine,
        sine,
        seg_mine[:, None],
        seg_all[None, :],
        pick_ids[:, None],
    )
    early = lax.all_gather(early_part, "wide", axis=0, tiled=True)
    start_own = rows_low[tok_rows:].astype(FULL)
    middle, inner, mixed_wide, pick_cols, table_top = launch(
        [
            settle(
                attn_part,
                start_own,
                start_own,
                jnp.ones((1, width), FULL),
                gain_w[1:2],
            ),
            gather_wide(mixed),
            split_columns("wide", normed),
            join_columns("wide", embed_cut[:, :table_half]),
        ],
        3,
        "settle_middle",
    )
    inner = inner.reshape(sel, width)
    inner_all = lax.all_gather(inner, "wide", axis=0, tiled=True)
    gate, up, hidden, fed = feed(inner, ffn_w)
    final_own, late_part, table_low = launch(
        [
            settle(fed, middle, start_own, keep_row, gain_w[2:3]),
            join_columns("wide", embed_cut[:, table_half:]),
        ],
        4,
        "settle_late",
    )
    table_own = jnp.concatenate([table_top, table_low])

    table_count = table_own.shape[0]
    local_target = targets_all - (narrow_spot * vocab_rows + wide_spot * table_count)
    has_target = local_target[:, None] == jnp.arange(table_count, dtype=jnp.int32)[None, :]
    counted = (targets_all >= 0).astype(FULL)
    loss_count = jnp.sum(counted)

    def exit_logits(features):
        logits = dot(features, table_own, 1, 1)
        peak = jnp.max(logits, axis=-1)
        total = jnp.sum(jnp.exp(logits - peak[:, None]), axis=-1)
        picked = jnp.sum(jnp.where(has_target, logits, 0.0), axis=-1)
        return logits, jnp.stack([peak, total, picked])

    half = slot_rows // 2
    late, mom_top = launch(
        [
            gather_wide(late_part.reshape(sel, width)),
            swap_turned(mom_parts[:, :half]),
        ],
        5,
        "gather_late",
    )
    late = late.reshape(total_rows, width)
    early_logits, early_stats = exit_logits(early)
    late_logits, late_stats = exit_logits(late)
    stats = jnp.concatenate([early_stats, late_stats], axis=1).reshape(3, 8, -1)
    stats = launch([combine(stats, merge_stats)], 6, "combine_stats")[0]
    stats, inner_all = lax.optimization_barrier((stats, inner_all))
    stats = stats.reshape(3, -1)
    log_norms = stats[0] + jnp.log(stats[1])
    losses = log_norms - stats[2]
    loss_sum = jnp.sum(
        counted * (EXIT_EARLY * losses[:total_rows] + EXIT_LAST * losses[total_rows:])
    )

    def exit_back(logits, log_norm, weight, features):
        grad_logits = (
            (jnp.exp(logits - log_norm[:, None]) - has_target.astype(FULL))
            * (weight * counted)[:, None]
        ).astype(LOW)
        return dot(grad_logits, table_own, 1, 0).astype(LOW), dot(grad_logits, features, 0, 0)

    late_back, late_head = exit_back(late_logits, log_norms[total_rows:], EXIT_LAST, late)
    grad_late, mom_low = launch(
        [sum_wide(late_back), swap_turned(mom_parts[:, half:])], 7, "sum_late"
    )
    early_norms, grad_late = lax.optimization_barrier((log_norms[:total_rows], grad_late))
    early_back, early_head = exit_back(early_logits, early_norms, EXIT_EARLY, early)
    mom_owned = jnp.concatenate([mom_top, mom_low], axis=1)
    grad_head = (early_head + late_head).astype(LOW)

    grad_early = lax.psum_scatter(early_back, "wide", scatter_dimension=0, tiled=True)
    grad_final, gain_late, grad_out = launch(
        [
            settle_back(
                grad_late.astype(LOW),
                final_own,
                jnp.zeros_like(final_own),
                keep_row,
                gain_w[2:3],
            ),
        ],
        8,
        "back_late",
    )
    grad_layer = grad_final * keep_layer
    grad_out = grad_out.reshape(sel, width)
    out_all = lax.all_gather(grad_out, "wide", axis=0, tiled=True)
    acts, fed_back = feed_back(grad_out, ffn_w, gate, up, hidden)
    grad_mid, gain_mid, grad_branch, acts = launch(
        [
            settle_back(fed_back, middle, grad_layer, keep_row, gain_w[1:2]),
            swap_blocks("wide", acts),
        ],
        9,
        "back_middle",
    )
    acts = jnp.moveaxis(acts, 1, 0).reshape(3, total_rows, ffn_size)
    acts = lax.all_gather(acts, "narrow", axis=0)
    grad_branch, grad_early = lax.optimization_barrier((grad_branch, grad_early))
    grad_branch = grad_branch.reshape(sel, width)

    kv_parts, grad_queries, pick_part = attend_back(
        grad_branch, proj, own_head, queries, probs, cosine, sine, cosine_all, sine_all
    )
    grad_kv, grad_pick, grad_early, queries_wide, branch_cols = launch(
        [
            swap_blocks("narrow", kv_parts),
            sum_narrow(pick_part),
            sum_narrow(grad_early),
            gather_wide(grad_queries),
            split_columns("wide", grad_branch),
        ],
        10,
        "trade_grads",
    )
    grad_kv, out_all = lax.optimization_barrier((grad_kv, out_all))
    grad_base = grad_mid + grad_final * (1.0 - keep_layer)
    grad_rows, gain_attn, gain_early, grad_kv = rows_back(
        rows_low, gain_w, proj, grad_kv, grad_pick, grad_early, grad_base, repeat
    )
    grad_rows, acts = lax.optimization_barrier((grad_rows, acts))
    summed_qo = jnp.stack(
        [
            jnp.einsum("wtc,wtf->cf", pick_cols, queries_wide, preferred_element_type=FULL),
            jnp.einsum("wtc,wtf->cf", branch_cols, mixed_wide, preferred_element_type=FULL),
        ]
    )
    qo_owned = lax.all_gather(
        summed_qo.astype(LOW).reshape(2 * columns, q_size), "narrow", axis=0
    )
    grad_rows, kv_wide, head_cols_all = launch(
        [
            return_rows(grad_rows),
            later(gather_wide(grad_kv, 3), 2),
            later(split_columns("wide", grad_head, 3), 2),
        ],
        11,
        "return_rows",
    )
    size = width // narrow_count

    def cols_own(values_all):
        return lax.dynamic_slice_in_dim(values_all, narrow_spot * size, size, 1)

    rights = (inner_all, inner_all, out_all)
    summed_ffn = jnp.stack(
        [
            jnp.einsum(
                "stf,td->sfd", acts[:, j], cols_own(rights[j]), preferred_element_type=FULL
            ).reshape(ffn_rows, size)
            for j in range(3)
        ]
    )
    turn = lax.rem(wide_spot, 2)
    grad_kv_w = jnp.einsum(
        "wtc,wtf->cf", tok_cols, kv_wide, preferred_element_type=FULL
    ).reshape(columns, narrow_count, 2, kv_size)
    grad_kv_w = jnp.moveaxis(grad_kv_w, 0, 2)
    summed_kv = lax.psum_scatter(grad_kv_w, "narrow", scatter_dimension=0, tiled=True)[0]
    summed_table, table_squares = spread(
        spots, listed, grad_rows.reshape(-1, columns), head_cols_all.reshape(vocab_rows, columns)
    )

    squares = (
        jnp.sum(summed_qo * summed_qo)
        + jnp.sum(summed_kv * summed_kv)
        + jnp.sum(summed_ffn * summed_ffn)
        + jnp.sum(table_squares)
    )
    sums = jnp.stack(
        [gain_attn[0], gain_mid[0], gain_early[0] + gain_late[0], jnp.full((width,), squares)]
    )
    sums, kv_owned = launch(
        [
            combine(sums.reshape(4, 8, -1), add_two),
            send_owner(summed_kv.astype(LOW).reshape(2 * block_rows, kv_size)),
        ],
        12,
        "combine_sums",
    )
    sums = sums.reshape(4, width)
    summed_gain = lax.dynamic_slice_in_dim(
        sums[:3], (wide_spot * narrow_count + narrow_spot) * gain_size, gain_size, 1
    )
    square_total = sums[3, 0] + jnp.sum(sums[:3] * sums[:3])
    grad_norm = jnp.sqrt(square_total) / loss_count
    factor = jnp.minimum(1.0, CLIP_NORM / (grad_norm + 1e-06)) / loss_count

    def ffn_owner():
        matrix = jnp.minimum(lax.rem(narrow_spot + narrow_count - turn, narrow_count), 2)
        left = lax.dynamic_index_in_dim(acts, matrix, 1, False)
        right = jnp.where(matrix == 2, out_all, inner_all)
        grad = jnp.einsum("stf,td->sfd", left, right, preferred_element_type=FULL)
        return newton(factor, mom_owned, grad.reshape(ffn_rows, width))

    def small_owner():
        return newton_small(factor, mom_owned, qo_owned, kv_owned)

    small_spot = lax.rem(3 + turn, narrow_count)
    directions = lax.cond(narrow_spot == small_spot, small_owner, ffn_owner)
    received = [lax.dynamic_index_in_dim(directions, narrow_spot, 0, False)] + [
        shifted(
            lax.dynamic_index_in_dim(
                directions, lax.rem(narrow_spot + step, narrow_count), 0, False
            ),
            "narrow",
            step,
        )
        for step in range(1, narrow_count)
    ]

    def direction_of(matrix):
        step = lax.rem(narrow_spot - matrix - turn + 2 * narrow_count, narrow_count)
        result = received[0]
        for at in range(1, narrow_count):
            result = jnp.where(step == at, received[at], result)
        return result

    dir_ffn = jnp.stack([direction_of(matrix) for matrix in range(3)]).astype(FULL)
    small = direction_of(3).astype(FULL)
    dir_qo = small[: 2 * block_rows].reshape(mom_qo.shape)
    dir_kv = small[2 * block_rows : 2 * block_rows + half_rows].reshape(half_rows, 4, kv_size)
    dir_kv = jnp.moveaxis(dir_kv, 1, 0).reshape(mom_kv.shape)

    embed_new, embed_m_new, embed_v_new = adamw(
        embed, embed_m, embed_v, summed_table * factor, RATE_ADAM, WEIGHT_DECAY
    )
    gains_new, gains_m_new, gains_v_new = adamw(
        gains, gains_m, gains_v, summed_gain * factor, RATE_GAIN, 0.0
    )

    def mom_next(mom, grad):
        return MOMENTUM * mom + jnp.moveaxis(grad * factor, 0, 1)

    shrink = 1.0 - RATE_MUON * WEIGHT_DECAY

    def weight_next(weight, direction):
        return weight * shrink - RATE_MUON * jnp.moveaxis(direction, 0, 1)

    return (
        loss_sum,
        loss_count,
        grad_norm,
        embed_new,
        embed_m_new,
        embed_v_new,
        weight_next(attn_qo, dir_qo),
        mom_next(attn_qo_mom, summed_qo),
        weight_next(attn_kv, dir_kv),
        mom_next(attn_kv_mom, summed_kv),
        weight_next(ffn, dir_ffn),
        mom_next(ffn_mom, summed_ffn),
        gains_new,
        gains_m_new,
        gains_v_new,
    )


def solution(mesh):
    by_pack = P("wide", None)
    table = P("narrow", "wide")
    layer = P("wide", None, "narrow")
    gain = P(None, ("wide", "narrow"))
    return jax.shard_map(
        per_device,
        mesh=mesh,
        in_specs=(by_pack,) * 4 + (P("wide"),) + (table,) * 3 + (layer,) * 6 + (gain,) * 3,
        out_specs=(P(),) * 3 + (table,) * 3 + (layer,) * 6 + (gain,) * 3,
        check_vma=False,
    )
```

```python
import functools

import jax
import jax.numpy as jnp
from jax import lax
from jax.experimental import pallas as pl
from jax.experimental.pallas import tpu as pltpu
from jax.sharding import PartitionSpec as P

HEADS = 16
HD = 128
KVH = 4
NS_STEPS = 5
STEP = 10


NORM_EPS = 1e-05
ROPE_BASE = 10000.0
EXIT_EARLY = 0.25
EXIT_LAST = 1.0
CLIP_NORM = 0.02
BETA_ONE = 0.9
BETA_TWO = 0.95
ADAM_EPS = 1e-08
RATE_ADAM = 0.02
RATE_GAIN = 0.3
RATE_MUON = 0.3
WEIGHT_DECAY = 0.1
MOMENTUM = 0.95
NEWTON_A = 3.4445
NEWTON_B = -4.775
NEWTON_C = 2.0315
MASKED = -1e30
LOW = jnp.bfloat16
FULL = jnp.float32
BOTH = ("wide", "narrow")
UNROLL = 16
VMEM_BYTES = 56 * 1024 * 1024


def dot(first, second, first_dim, second_dim):
    return lax.dot_general(
        first, second, (((first_dim,), (second_dim,)), ((), ())), preferred_element_type=FULL
    )


def norm_rows(values, gain_row):
    return (
        values * lax.rsqrt(jnp.mean(values * values, axis=-1, keepdims=True) + NORM_EPS) * gain_row
    )


def segments_at(lens, where_at):
    ends = jnp.cumsum(lens)
    return jnp.sum((where_at[:, None] >= ends[None, :]).astype(jnp.int32), axis=1)


def angles_at(lens, where_at):
    segment = segments_at(lens, where_at)
    starts = jnp.cumsum(lens) - lens
    member = segment[:, None] == jnp.arange(lens.shape[0], dtype=jnp.int32)[None, :]
    begin = jnp.sum(jnp.where(member, starts[None, :], 0), axis=1)
    offset_pos = (where_at - begin).astype(FULL)
    inverse = ROPE_BASE ** (-2.0 * jnp.arange(HD // 2, dtype=FULL) / HD)
    angle = offset_pos[:, None] * inverse[None, :]
    return (segment, jnp.cos(angle), jnp.sin(angle))


MESH = pl.DeviceIdType.MESH
ANY = pl.BlockSpec(memory_space=pl.ANY)
VMEM = pl.BlockSpec(memory_space=pltpu.VMEM)


def others(axis, count):
    me = lax.axis_index(axis)
    return [{axis: lax.rem(me + step, count)} for step in range(1, count)]


def push(source, target, send, receive, device):
    return pltpu.make_async_remote_copy(
        src_ref=source,
        dst_ref=target,
        send_sem=send,
        recv_sem=receive,
        device_id=device,
        device_id_type=MESH,
    )


def arrived(block, send, receive, device):
    push(block, block, send, receive, device).wait_recv()


def like(values):
    return jax.ShapeDtypeStruct(values.shape, values.dtype)


def struct(shape, dtype):
    return jax.ShapeDtypeStruct(shape, dtype)


def sems(*shape):
    return pltpu.SemaphoreType.DMA(shape)


class Task:
    def __init__(self, inputs, outputs, scratch, steps, place_in, place_out, axes):
        self.inputs, self.outputs, self.scratch, self.steps = inputs, outputs, scratch, steps
        self.place_in = [place_in] * len(inputs)
        self.place_out = [place_out] * len(outputs)
        self.axes = axes


def launch(tasks, ident, name):
    axes = sorted(set(axis for task in tasks for axis in task.axes))
    inputs = [a for task in tasks for a in task.inputs]
    outputs = [a for task in tasks for a in task.outputs]
    scratch = [a for task in tasks for a in task.scratch]

    def body(*refs):
        refs = list(refs)
        ins = refs[: len(inputs)]
        outs = refs[len(inputs) : len(inputs) + len(outputs)]
        extra = refs[len(inputs) + len(outputs) :]
        barrier = pltpu.get_barrier_semaphore()
        targets = [device for axis in axes for device in others(axis, lax.axis_size(axis))]
        for device in targets:
            pl.semaphore_signal(barrier, inc=1, device_id=device, device_id_type=MESH)
        pl.semaphore_wait(barrier, len(targets))
        live = []
        for task in tasks:
            counts = (len(task.inputs), len(task.outputs), len(task.scratch))
            live.append(task.steps(ins[: counts[0]], outs[: counts[1]], extra[: counts[2]]))
            ins, outs, extra = ins[counts[0] :], outs[counts[1] :], extra[counts[2] :]
        while live:
            live = [steps for steps in live if next(steps, 0) is None]

    size = sum(a.size * a.dtype.itemsize for a in list(inputs) + list(outputs))
    return pl.pallas_call(
        body,
        out_shape=outputs,
        in_specs=[place for task in tasks for place in task.place_in],
        out_specs=[place for task in tasks for place in task.place_out],
        scratch_shapes=scratch,
        compiler_params=pltpu.CompilerParams(
            collective_id=ident, has_side_effects=True, vmem_limit_bytes=VMEM_BYTES
        ),
        cost_estimate=pl.CostEstimate(flops=0, bytes_accessed=size // 8, transcendentals=0),
        name=name,
    )(*inputs)


def later(task, turns):
    begin = task.steps

    def steps(ins, outs, scratch):
        for turn in range(turns):
            yield
        yield from begin(ins, outs, scratch)

    task.steps = steps
    return task


def gather_wide(values, patience=1):
    count = lax.axis_size("wide")
    chips = count // 2

    def steps(ins, outs, scratch):
        (x_ref,), (out_ref,), (send, receive, local) = ins, outs, scratch
        me = lax.axis_index("wide")
        mate = me + 1 - 2 * lax.rem(me, 2)
        peers = [lax.rem(me + 2 * step, count) for step in range(1, chips)] + [mate]
        first = []
        for step, peer in enumerate(peers):
            copy = push(x_ref, out_ref.at[me], send.at[step], receive.at[me], {"wide": peer})
            copy.start()
            first.append(copy)
        keep = pltpu.make_async_copy(x_ref, out_ref.at[me], local)
        keep.start()
        for turn in range(patience):
            yield
        second = []
        for step in range(1, chips):
            source = lax.rem(me - 2 * step + count, count)
            block = out_ref.at[source]
            arrived(block, send.at[0], receive.at[source], {"wide": mate})
            copy = push(
                block, block, send.at[chips + step - 1], receive.at[source], {"wide": mate}
            )
            copy.start()
            second.append(copy)
        yield
        for step in range(chips):
            source = lax.rem(mate - 2 * step + count, count)
            arrived(out_ref.at[source], send.at[0], receive.at[source], {"wide": mate})
        for copy in first + second:
            copy.wait_send()
        keep.wait()

    shape = struct((count,) + values.shape, values.dtype)
    return Task(
        [values], [shape], [sems(count - 1), sems(count), sems()], steps, ANY, ANY, ["wide"]
    )


def trade(axis, values, source_of, target_of, shape, patience=2):
    count = lax.axis_size(axis)

    def steps(ins, outs, scratch):
        (x_ref,), (out_ref,), (send, receive, local) = ins, outs, scratch
        me = lax.axis_index(axis)
        copies = []
        for step in range(1, count):
            peer = lax.rem(me + step, count)
            copy = push(
                source_of(x_ref, peer),
                target_of(out_ref, me),
                send.at[step - 1],
                receive.at[me],
                {axis: peer},
            )
            copy.start()
            copies.append(copy)
        keep = pltpu.make_async_copy(source_of(x_ref, me), target_of(out_ref, me), local)
        keep.start()
        for turn in range(patience):
            yield
        for step in range(1, count):
            source = lax.rem(me - step + count, count)
            arrived(
                target_of(out_ref, source), send.at[0], receive.at[source], {axis: source}
            )
        for copy in copies:
            copy.wait_send()
        keep.wait()

    return Task(
        [values],
        [struct(shape, values.dtype)],
        [sems(count - 1), sems(count), sems()],
        steps,
        ANY,
        ANY,
        [axis],
    )


def block_at(ref, spot):
    return ref.at[spot]


def whole_at(ref, spot):
    return ref


def columns_of(size):
    def at(ref, spot):
        return ref.at[:, pl.ds(pl.multiple_of(spot * size, size), size)]

    return at


def turned(ref, spot):
    count = lax.axis_size("narrow")
    matrix = lax.rem(spot + count - lax.rem(lax.axis_index("wide"), 2), count)
    return ref.at[jnp.minimum(matrix, 3)]


def swap_turned(values, patience=2):
    shape = (lax.axis_size("narrow"),) + values.shape[1:]
    return trade("narrow", values, turned, block_at, shape, patience)


def swap_owned(values, patience):
    count = lax.axis_size("narrow")

    def steps(ins, outs, scratch):
        (x_ref,), (out_ref,), (send, receive, local) = ins, outs, scratch
        me = lax.axis_index("narrow")
        turn = lax.rem(lax.axis_index("wide"), 2)

        def matrix_of(device):
            return lax.rem(device + count - turn, count)

        def copy_to(step):
            peer = lax.rem(me + step, count)
            return push(
                x_ref.at[jnp.minimum(matrix_of(peer), 2)],
                out_ref.at[me],
                send.at[step - 1],
                receive.at[me],
                {"narrow": peer},
            )

        def keep():
            return pltpu.make_async_copy(
                x_ref.at[jnp.minimum(matrix_of(me), 2)], out_ref.at[me], local
            )

        keep().start()
        for step in range(1, count):

            @pl.when(matrix_of(lax.rem(me + step, count)) < 3)
            def _():
                copy_to(step).start()

        for turn_at in range(patience):
            yield

        @pl.when(matrix_of(me) < 3)
        def _():
            for step in range(1, count):
                source = lax.rem(me - step + count, count)
                arrived(out_ref.at[source], send.at[0], receive.at[source], {"narrow": source})

        for step in range(1, count):

            @pl.when(matrix_of(lax.rem(me + step, count)) < 3)
            def _():
                copy_to(step).wait_send()

        keep().wait()

    return Task(
        [values],
        [struct((count,) + values.shape[1:], values.dtype)],
        [sems(count - 1), sems(count), sems()],
        steps,
        ANY,
        ANY,
        ["narrow"],
    )


def send_owner(values):
    count = lax.axis_size("narrow")

    def steps(ins, outs, scratch):
        (x_ref,), (out_ref,), (send, receive, local) = ins, outs, scratch
        me = lax.axis_index("narrow")
        owner = lax.rem(3 + lax.rem(lax.axis_index("wide"), 2), count)
        keep = pltpu.make_async_copy(x_ref, out_ref.at[me], local)
        keep.start()

        def to_owner():
            return push(x_ref, out_ref.at[me], send.at[0], receive.at[me], {"narrow": owner})

        @pl.when(me != owner)
        def _():
            to_owner().start()

        yield
        yield

        @pl.when(me != owner)
        def _():
            to_owner().wait_send()

        @pl.when(me == owner)
        def _():
            for step in range(1, count):
                source = lax.rem(owner + step, count)
                arrived(out_ref.at[source], send.at[0], receive.at[source], {"narrow": source})

        keep.wait()

    return Task(
        [values],
        [struct((count,) + values.shape, values.dtype)],
        [sems(1), sems(count), sems()],
        steps,
        ANY,
        ANY,
        ["narrow"],
    )


def swap_blocks(axis, values):
    return trade(axis, values, block_at, block_at, values.shape)


def gather_blocks(axis, values):
    shape = (lax.axis_size(axis),) + values.shape
    return trade(axis, values, whole_at, block_at, shape)


def split_columns(axis, values, patience=2):
    count = lax.axis_size(axis)
    rows, size = values.shape[0], values.shape[1] // count
    return trade(axis, values, columns_of(size), block_at, (count, rows, size), patience)


def join_columns(axis, values):
    count, rows, size = values.shape
    return trade(axis, values, block_at, columns_of(size), (rows, count * size))


def collect(count, parts_ref, slots, send, receive):
    me = lax.axis_index("narrow")
    copies = []
    for step in range(1, count):
        peer = lax.rem(me + step, count)
        copy = push(
            parts_ref.at[peer],
            slots.at[me],
            send.at[step - 1],
            receive.at[me],
            {"narrow": peer},
        )
        copy.start()
        copies.append(copy)
    return copies


def collected(count, parts_ref, slots, send, receive):
    me = lax.axis_index("narrow")
    total = parts_ref[me].astype(FULL)
    for step in range(1, count):
        source = lax.rem(me - step + count, count)
        arrived(slots.at[source], send.at[0], receive.at[source], {"narrow": source})
        total = total + slots[source].astype(FULL)
    return total


def share(count, low, all_ref, send, receive):
    me = lax.axis_index("narrow")
    all_ref[me] = low
    copies = []
    for step in range(1, count):
        peer = lax.rem(me + step, count)
        copy = push(
            all_ref.at[me], all_ref.at[me], send.at[step - 1], receive.at[me], {"narrow": peer}
        )
        copy.start()
        copies.append(copy)
    return copies


def shared(count, all_ref, send, receive):
    me = lax.axis_index("narrow")
    for step in range(1, count):
        source = lax.rem(me - step + count, count)
        arrived(all_ref.at[source], send.at[0], receive.at[source], {"narrow": source})


def narrow_sems(count):
    return [sems(count - 1), sems(count)]


def settle(partial, base, other, keep_row, gain_row):
    count = lax.axis_size("narrow")
    rows, width = base.shape

    def steps(ins, outs, scratch):
        parts_ref, base_ref, other_ref, keep_ref, gain_ref = ins
        own_ref, all_ref = outs
        slots, send, receive, send_all, receive_all = scratch
        copies = collect(count, parts_ref, slots, send, receive)
        yield
        total = collected(count, parts_ref, slots, send, receive)
        total = jnp.where(keep_ref[...] > 0, total + base_ref[...], other_ref[...])
        own_ref[...] = total
        low = norm_rows(total, gain_ref[...]).astype(LOW)
        copies = copies + share(count, low, all_ref, send_all, receive_all)
        yield
        shared(count, all_ref, send_all, receive_all)
        for copy in copies:
            copy.wait_send()

    return Task(
        [partial.reshape(count, rows, width), base, other, keep_row, gain_row],
        [struct((rows, width), FULL), struct((count, rows, width), LOW)],
        [pltpu.VMEM((count, rows, width), partial.dtype)]
        + narrow_sems(count)
        + narrow_sems(count),
        steps,
        VMEM,
        VMEM,
        ["narrow"],
    )


def settle_back(partial, values, add, keep_row, gain_row):
    count = lax.axis_size("narrow")
    rows, width = values.shape

    def steps(ins, outs, scratch):
        parts_ref, values_ref, add_ref, keep_ref, gain_ref = ins
        own_ref, gain_grad_ref, all_ref = outs
        slots, send, receive, send_all, receive_all = scratch
        copies = collect(count, parts_ref, slots, send, receive)
        yield
        grad = collected(count, parts_ref, slots, send, receive)
        held = values_ref[...]
        root = lax.rsqrt(jnp.mean(held * held, axis=-1, keepdims=True) + NORM_EPS)
        scaled = gain_ref[...] * grad
        inner = jnp.mean(held * scaled, axis=-1, keepdims=True)
        own = add_ref[...] + root * scaled - held * (root * root * root * inner)
        gain_grad_ref[...] = jnp.sum(held * root * grad, axis=0, keepdims=True)
        own_ref[...] = own
        low = (own * keep_ref[...]).astype(LOW)
        copies = copies + share(count, low, all_ref, send_all, receive_all)
        yield
        shared(count, all_ref, send_all, receive_all)
        for copy in copies:
            copy.wait_send()

    return Task(
        [partial.reshape(count, rows, width), values, add, keep_row, gain_row],
        [
            struct((rows, width), FULL),
            struct((1, width), FULL),
            struct((count, rows, width), LOW),
        ],
        [pltpu.VMEM((count, rows, width), partial.dtype)]
        + narrow_sems(count)
        + narrow_sems(count),
        steps,
        VMEM,
        VMEM,
        ["narrow"],
    )


def sum_narrow(partial):
    count = lax.axis_size("narrow")
    rows, width = partial.shape[0] // count, partial.shape[1]

    def steps(ins, outs, scratch):
        (parts_ref,), (own_ref,), (slots, send, receive) = ins, outs, scratch
        copies = collect(count, parts_ref, slots, send, receive)
        yield
        yield
        own_ref[...] = collected(count, parts_ref, slots, send, receive)
        for copy in copies:
            copy.wait_send()

    return Task(
        [partial.reshape(count, rows, width)],
        [struct((rows, width), FULL)],
        [pltpu.VMEM((count, rows, width), partial.dtype)] + narrow_sems(count),
        steps,
        VMEM,
        VMEM,
        ["narrow"],
    )


def fetch_rows(found, rows):
    deep, wide = lax.axis_size("narrow"), lax.axis_size("wide")
    columns = found.shape[2]

    def steps(ins, outs, scratch):
        (found_ref,), (out_ref,) = ins, outs
        rightward, leftward, final = scratch[:3]
        send_right, receive_right, send_left, receive_left = scratch[3:7]
        send_wide, receive_wide, local = scratch[7:]
        spot = lax.axis_index("narrow")
        me = lax.axis_index("wide")

        def right_copy(part, source):
            return push(
                source,
                rightward.at[part],
                send_right.at[part],
                receive_right.at[part],
                {"narrow": lax.rem(spot + 1, deep)},
            )

        def left_copy(part, source):
            return push(
                source,
                leftward.at[part],
                send_left.at[part],
                receive_left.at[part],
                {"narrow": lax.rem(spot + deep - 1, deep)},
            )

        for step in range(deep - 1):
            right, left = deep - 1 - step, step

            @pl.when((spot == 0) & (right > 0))
            def _():
                right_copy(right, found_ref.at[right]).start()

            @pl.when((spot == deep - 1) & (left < deep - 1))
            def _():
                left_copy(left, found_ref.at[left]).start()

        yield
        for step in range(deep - 1):
            right, left = deep - 1 - step, step

            def pass_right():
                right_copy(right, rightward.at[right]).wait_recv()
                rightward[right] = rightward[right] + found_ref[right]
                right_copy(right, rightward.at[right]).start()

            pl.when((spot > 0) & (right > spot) & (2 * spot < deep))(pass_right)

            @pl.when((spot < deep - 1) & (left < spot))
            def _():
                left_copy(left, leftward.at[left]).wait_recv()
                leftward[left] = leftward[left] + found_ref[left]
                left_copy(left, leftward.at[left]).start()

            pl.when((right > spot) & (2 * spot >= deep))(pass_right)

        final[...] = found_ref[spot]

        @pl.when(spot > 0)
        def _():
            right_copy(spot, rightward.at[spot]).wait_recv()
            final[...] = final[...] + rightward[spot]

        @pl.when(spot < deep - 1)
        def _():
            left_copy(spot, leftward.at[spot]).wait_recv()
            final[...] = final[...] + leftward[spot]

        def rows_for(device):
            return final.at[pl.ds(pl.multiple_of(device * rows, rows), rows)]

        def columns_from(device):
            return columns_of(columns)(out_ref, device)

        copies = []
        for step in range(1, wide):
            peer = lax.rem(me + step, wide)
            copy = push(
                rows_for(peer),
                columns_from(me),
                send_wide.at[step - 1],
                receive_wide.at[me],
                {"wide": peer},
            )
            copy.start()
            copies.append(copy)
        keep = pltpu.make_async_copy(rows_for(me), columns_from(me), local)
        keep.start()
        yield
        for step in range(1, wide):
            source = lax.rem(me - step + wide, wide)
            arrived(
                columns_from(source), send_wide.at[0], receive_wide.at[source], {"wide": source}
            )
        yield
        for copy in copies:
            copy.wait_send()
        keep.wait()
        for step in range(deep - 1):
            right, left = deep - 1 - step, step

            @pl.when(right > spot)
            def _():
                right_copy(right, found_ref.at[right]).wait_send()

            @pl.when(left < spot)
            def _():
                left_copy(left, found_ref.at[left]).wait_send()

    task = Task(
        [found],
        [struct((rows, wide * columns), found.dtype)],
        [pltpu.VMEM(found.shape, found.dtype)] * 2
        + [pltpu.VMEM(found.shape[1:], found.dtype)]
        + [sems(deep)] * 4
        + [sems(wide - 1), sems(wide), sems()],
        steps,
        VMEM,
        ANY,
        ["narrow", "wide"],
    )
    return task


def return_rows(rows):
    deep, wide = lax.axis_size("narrow"), lax.axis_size("wide")
    count, width = rows.shape
    columns = width // wide

    def steps(ins, outs, scratch):
        (rows_ref,), (out_ref,) = ins, outs
        send_right, send_left, receive_deep, send_wide, receive_wide, local = scratch
        spot = lax.axis_index("narrow")
        me = lax.axis_index("wide")
        part_of = functools.partial(columns_of(columns), rows_ref)

        def landing(device):
            return out_ref.at[spot, pl.ds(pl.multiple_of(device * count, count), count)]

        copies = []
        for step in range(1, wide):
            peer = lax.rem(me + step, wide)
            copy = push(
                part_of(peer),
                landing(me),
                send_wide.at[step - 1],
                receive_wide.at[me],
                {"wide": peer},
            )
            copy.start()
            copies.append(copy)
        keep = pltpu.make_async_copy(part_of(me), landing(me), local)
        keep.start()
        yield
        for step in range(1, wide):
            source = lax.rem(me - step + wide, wide)
            arrived(landing(source), send_wide.at[0], receive_wide.at[source], {"wide": source})
        keep.wait()

        def right_copy(part):
            return push(
                out_ref.at[part],
                out_ref.at[part],
                send_right.at[part],
                receive_deep.at[part],
                {"narrow": lax.rem(spot + 1, deep)},
            )

        def left_copy(part):
            return push(
                out_ref.at[part],
                out_ref.at[part],
                send_left.at[part],
                receive_deep.at[part],
                {"narrow": lax.rem(spot + deep - 1, deep)},
            )

        @pl.when(spot < deep - 1)
        def _():
            right_copy(spot).start()

        @pl.when(spot > 0)
        def _():
            left_copy(spot).start()

        for step in range(1, deep):
            yield

            @pl.when(spot >= step)
            def _():
                right_copy(spot - step).wait_recv()

                @pl.when(spot < deep - 1)
                def _():
                    right_copy(spot - step).start()

            @pl.when(spot + step < deep)
            def _():
                left_copy(spot + step).wait_recv()

                @pl.when(spot > 0)
                def _():
                    left_copy(spot + step).start()

        for part in range(deep):

            @pl.when((part <= spot) & (spot < deep - 1))
            def _():
                right_copy(part).wait_send()

            @pl.when((part >= spot) & (spot > 0))
            def _():
                left_copy(part).wait_send()

        for copy in copies:
            copy.wait_send()

    return Task(
        [rows],
        [struct((deep, wide * count, columns), rows.dtype)],
        [sems(deep)] * 3 + [sems(wide - 1), sems(wide), sems()],
        steps,
        ANY,
        ANY,
        ["narrow", "wide"],
    )


def sum_wide(partial):
    count = lax.axis_size("wide")
    chips = count // 2
    rows, width = partial.shape[0] // count, partial.shape[1]

    def steps(ins, outs, scratch):
        (parts_ref,), (out_ref,) = ins, outs
        from_mate, paired, slots, send_mate, receive_mate, send, receive = scratch
        me = lax.axis_index("wide")
        side = lax.rem(me, 2)
        mate = me + 1 - 2 * side
        my_chip = me // 2
        mate_copies = []
        for step in range(chips):
            chip = lax.rem(my_chip + 1 + step, chips)
            copy = push(
                parts_ref.at[2 * chip + 1 - side],
                from_mate.at[chip],
                send_mate.at[step],
                receive_mate.at[chip],
                {"wide": mate},
            )
            copy.start()
            mate_copies.append(copy)
        yield
        copies = []
        for step in range(chips):
            chip = lax.rem(my_chip + 1 + step, chips)
            arrived(from_mate.at[chip], send_mate.at[0], receive_mate.at[chip], {"wide": mate})
            both = parts_ref[2 * chip + side].astype(FULL) + from_mate[chip].astype(FULL)
            if step < chips - 1:
                paired[chip] = both.astype(LOW)
                copy = push(
                    paired.at[chip],
                    slots.at[my_chip],
                    send.at[step],
                    receive.at[my_chip],
                    {"wide": 2 * chip + side},
                )
                copy.start()
                copies.append(copy)
            else:
                out_ref[...] = both
        yield
        for step in range(1, chips):
            chip = lax.rem(my_chip - step + chips, chips)
            arrived(slots.at[chip], send.at[0], receive.at[chip], {"wide": 2 * chip + side})
            out_ref[...] = out_ref[...] + slots[chip].astype(FULL)
        for copy in mate_copies + copies:
            copy.wait_send()

    return Task(
        [partial.reshape(count, rows, width)],
        [struct((rows, width), FULL)],
        [pltpu.VMEM((chips, rows, width), LOW)] * 3
        + [sems(chips), sems(chips), sems(max(chips - 1, 1)), sems(chips)],
        steps,
        VMEM,
        VMEM,
        ["wide"],
    )


def merge_stats(first, second):
    peak = jnp.maximum(first[0:1], second[0:1])
    total = first[1:2] * jnp.exp(first[0:1] - peak) + second[1:2] * jnp.exp(second[0:1] - peak)
    return jnp.concatenate([peak, total, first[2:3] + second[2:3]], axis=0)


def add_two(first, second):
    return first + second


def combine(values, join):
    deep, wide = lax.axis_size("narrow"), lax.axis_size("wide")

    def steps(ins, outs, scratch):
        (x_ref,), (out_ref,) = ins, outs
        wide_slots, deep_slots, send_wide, receive_wide, send_deep, receive_deep = scratch

        def start(axis, count, slots, value, send, receive):
            me = lax.axis_index(axis)
            slots[me] = value
            copies = []
            for step in range(1, count):
                peer = lax.rem(me + step, count)
                copy = push(
                    slots.at[me], slots.at[me], send.at[step - 1], receive.at[me], {axis: peer}
                )
                copy.start()
                copies.append(copy)
            return copies

        def finish(axis, count, slots, send, receive):
            me = lax.axis_index(axis)
            for step in range(1, count):
                source = lax.rem(me - step + count, count)
                arrived(slots.at[source], send.at[0], receive.at[source], {axis: source})
            total = slots[0]
            for source in range(1, count):
                total = join(total, slots[source])
            return total

        first = start("wide", wide, wide_slots, x_ref[...], send_wide, receive_wide)
        yield
        total = finish("wide", wide, wide_slots, send_wide, receive_wide)
        second = start("narrow", deep, deep_slots, total, send_deep, receive_deep)
        yield
        out_ref[...] = finish("narrow", deep, deep_slots, send_deep, receive_deep)
        for copy in first + second:
            copy.wait_send()

    return Task(
        [values],
        [like(values)],
        [
            pltpu.VMEM((wide,) + values.shape, values.dtype),
            pltpu.VMEM((deep,) + values.shape, values.dtype),
            sems(wide - 1),
            sems(wide),
            sems(deep - 1),
            sems(deep),
        ],
        steps,
        VMEM,
        VMEM,
        ["narrow", "wide"],
    )


def gather_both(values):
    deep, wide = lax.axis_size("narrow"), lax.axis_size("wide")

    def steps(ins, outs, scratch):
        (x_ref,), (out_ref,) = ins, outs
        send_wide, receive_wide, send_deep, receive_deep = scratch
        me = lax.axis_index("wide")
        spot = lax.axis_index("narrow")
        out_ref[spot, me] = x_ref[...]
        copies = []
        for step in range(1, wide):
            peer = lax.rem(me + step, wide)
            block = out_ref.at[spot, me]
            copy = push(block, block, send_wide.at[step - 1], receive_wide.at[me], {"wide": peer})
            copy.start()
            copies.append(copy)
        yield
        for step in range(1, wide):
            source = lax.rem(me - step + wide, wide)
            block = out_ref.at[spot, source]
            arrived(block, send_wide.at[0], receive_wide.at[source], {"wide": source})
        for step in range(1, deep):
            peer = lax.rem(spot + step, deep)
            block = out_ref.at[spot]
            copy = push(
                block, block, send_deep.at[step - 1], receive_deep.at[spot], {"narrow": peer}
            )
            copy.start()
            copies.append(copy)
        yield
        for step in range(1, deep):
            source = lax.rem(spot - step + deep, deep)
            block = out_ref.at[source]
            arrived(block, send_deep.at[0], receive_deep.at[source], {"narrow": source})
        for copy in copies:
            copy.wait_send()

    return Task(
        [values],
        [struct((deep, wide) + values.shape, values.dtype)],
        [sems(wide - 1), sems(wide), sems(deep - 1), sems(deep)],
        steps,
        VMEM,
        VMEM,
        ["narrow", "wide"],
    )


def turn_heads(values, cosine, sine):
    half = values.shape[1] // 2
    swapped = jnp.concatenate([values[:, half:], values[:, :half]], axis=1)
    return values * cosine + swapped * sine


def wide_angles(cosine, sine):
    return jnp.concatenate([cosine, cosine], axis=1), jnp.concatenate([-sine, sine], axis=1)


def local_call(body, inputs, specs, outputs, flops, name):
    return pl.pallas_call(
        body,
        grid=(1,),
        in_specs=specs,
        out_specs=[
            pl.BlockSpec(a.shape, lambda step, rank=len(a.shape): (0,) * rank) for a in outputs
        ],
        out_shape=outputs,
        compiler_params=pltpu.CompilerParams(vmem_limit_bytes=VMEM_BYTES),
        cost_estimate=pl.CostEstimate(flops=flops, bytes_accessed=8 << 20, transcendentals=0),
        name=name,
    )(*inputs)


def entire(values):
    return pl.BlockSpec(values.shape, lambda step: (0,) * values.ndim)


def column_block(values, size, index):
    return pl.BlockSpec((values.shape[0], size), lambda step: (0, index))


def heads_body(groups, rep, rows_ref, gain_ref, kv_ref, cos_ref, sin_ref, out_ref, normed_ref):
    count, _, _, tok_rows, head = out_ref.shape
    size = kv_ref.shape[1] // (2 * count)
    per_head = head // size
    rows = rows_ref[0:tok_rows, :].astype(FULL)
    normed = norm_rows(rows, gain_ref[...]).astype(LOW)
    normed_ref[...] = normed
    both = dot(normed, kv_ref[...], 1, 0)

    def head_of(kind, index):
        pieces = [
            both[:, (2 * part + kind) * size : (2 * part + kind + 1) * size]
            for part in range(index * per_head, (index + 1) * per_head)
        ]
        return pieces[0] if per_head == 1 else jnp.concatenate(pieces, axis=1)

    for owner in range(count):
        for group in range(groups):
            index = (owner * groups + group) // rep
            keys = turn_heads(head_of(0, index), cos_ref[...], sin_ref[...])
            out_ref[owner, group, 0] = keys.astype(LOW)
            out_ref[owner, group, 1] = head_of(1, index).astype(LOW)


def make_heads(rows_low, gain_row, proj, cosine, sine, groups, rep):
    count = lax.axis_size("narrow")
    tok_rows, head = cosine.shape
    width = rows_low.shape[1]
    size = 2 * KVH * HD
    return local_call(
        functools.partial(heads_body, groups, rep),
        [rows_low, gain_row, proj, cosine, sine],
        [entire(rows_low), entire(gain_row), column_block(proj, size, 0)]
        + [entire(cosine), entire(sine)],
        [struct((count, groups, 2, tok_rows, head), LOW), struct((tok_rows, width), LOW)],
        2 * tok_rows * width * size,
        "make_heads",
    )


def attend_body(
    start_ref,
    gains_ref,
    q_ref,
    o_ref,
    kv_ref,
    cos_ref,
    sin_ref,
    seg_ref,
    seg_all_ref,
    pick_ref,
    queries_ref,
    probs_ref,
    mixed_ref,
    part_ref,
    normed_ref,
    early_ref,
):
    count, groups, _, tok_rows, head = kv_ref.shape
    heads_own = probs_ref.shape[0]
    start = start_ref[...].astype(FULL)
    root = lax.rsqrt(jnp.mean(start * start, axis=-1, keepdims=True) + NORM_EPS)
    normed = (start * root * gains_ref[0:1, :]).astype(LOW)
    normed_ref[...] = normed
    early_ref[...] = (start * root * gains_ref[2:3, :]).astype(LOW)
    queries = dot(normed, q_ref[...], 1, 0)
    spots = lax.broadcasted_iota(jnp.int32, (1, count * tok_rows), 1)
    allowed = (seg_ref[...] == seg_all_ref[...]) & (pick_ref[...] >= spots)
    for group in range(groups):
        keys = jnp.concatenate([kv_ref[part, group, 0] for part in range(count)], axis=0)
        values = jnp.concatenate([kv_ref[part, group, 1] for part in range(count)], axis=0)
        for member in range(heads_own // groups):
            at = group * (heads_own // groups) + member
            spot = slice(at * head, (at + 1) * head)
            query = turn_heads(queries[:, spot], cos_ref[...], sin_ref[...]).astype(LOW)
            queries_ref[:, spot] = query
            scores = jnp.where(allowed, dot(query, keys, 1, 1) * head ** (-0.5), MASKED)
            shifted = jnp.exp(scores - jnp.max(scores, axis=-1, keepdims=True))
            probs = shifted / jnp.sum(shifted, axis=-1, keepdims=True)
            probs_ref[at] = probs
            mixed_ref[:, spot] = dot(probs.astype(LOW), values, 1, 0).astype(LOW)
    part_ref[...] = dot(mixed_ref[...], o_ref[...], 1, 1).astype(LOW)


def attend(start_low, gains, proj, own_head, cosine, sine, seg, seg_all, picks):
    count, groups, _, tok_rows, head = own_head.shape
    sel, width = start_low.shape
    heads_own = HEADS // count
    size = heads_own * head
    first = 2 * KVH * HD // size
    seq_len = count * tok_rows
    return local_call(
        attend_body,
        [start_low, gains, proj, proj, own_head, cosine, sine, seg, seg_all, picks],
        [
            entire(start_low),
            entire(gains),
            column_block(proj, size, first),
            column_block(proj, size, first + 1),
        ]
        + [entire(a) for a in (own_head, cosine, sine, seg, seg_all, picks)],
        [
            struct((sel, size), LOW),
            struct((heads_own, sel, seq_len), FULL),
            struct((sel, size), LOW),
            struct((sel, width), LOW),
            struct((sel, width), LOW),
            struct((sel, width), LOW),
        ],
        4 * sel * size * (width + seq_len),
        "attend",
    )


def attend_back_body(
    grad_ref,
    q_ref,
    o_ref,
    kv_ref,
    queries_ref,
    probs_ref,
    cos_ref,
    sin_ref,
    cos_all_ref,
    sin_all_ref,
    out_ref,
    grad_q_ref,
    part_ref,
):
    count, groups, _, tok_rows, head = kv_ref.shape
    heads_own = probs_ref.shape[0]
    scale = head ** (-0.5)
    grad_mixed = dot(grad_ref[...], o_ref[...], 1, 0).astype(LOW)
    for group in range(groups):
        keys = jnp.concatenate([kv_ref[part, group, 0] for part in range(count)], axis=0)
        values = jnp.concatenate([kv_ref[part, group, 1] for part in range(count)], axis=0)
        grad_keys = jnp.zeros(keys.shape, FULL)
        grad_values = jnp.zeros(keys.shape, FULL)
        for member in range(heads_own // groups):
            at = group * (heads_own // groups) + member
            spot = slice(at * head, (at + 1) * head)
            probs = probs_ref[at]
            grad_probs = dot(grad_mixed[:, spot], values, 1, 1)
            inner = jnp.sum(probs * grad_probs, axis=-1, keepdims=True)
            grad_scores = (probs * (grad_probs - inner)).astype(LOW)
            grad_query = dot(grad_scores, keys, 1, 0) * scale
            grad_q_ref[:, spot] = turn_heads(grad_query, cos_ref[...], -sin_ref[...]).astype(LOW)
            grad_keys = grad_keys + dot(grad_scores, queries_ref[:, spot], 0, 0)
            grad_values = grad_values + dot(probs.astype(LOW), grad_mixed[:, spot], 0, 0)
        grad_keys = turn_heads(grad_keys * scale, cos_all_ref[...], -sin_all_ref[...])
        for part in range(count):
            rows = slice(part * tok_rows, (part + 1) * tok_rows)
            out_ref[part, group, 0] = grad_keys[rows].astype(LOW)
            out_ref[part, group, 1] = grad_values[rows].astype(LOW)
    part_ref[...] = dot(grad_q_ref[...], q_ref[...], 1, 1).astype(LOW)


def attend_back(grad, proj, own_head, queries, probs, cosine, sine, cosine_all, sine_all):
    count, groups, _, tok_rows, head = own_head.shape
    sel, width = grad.shape
    size = queries.shape[1]
    first = 2 * KVH * HD // size
    return local_call(
        attend_back_body,
        [grad, proj, proj, own_head, queries, probs, cosine, sine, cosine_all, sine_all],
        [entire(grad), column_block(proj, size, first), column_block(proj, size, first + 1)]
        + [
            entire(a)
            for a in (own_head, queries, probs, cosine, sine, cosine_all, sine_all)
        ],
        [struct(own_head.shape, LOW), struct((sel, size), LOW), struct((sel, width), LOW)],
        8 * sel * size * width,
        "attend_back",
    )


def norm_back_rows(values, gain_row, grad):
    root = lax.rsqrt(jnp.mean(values * values, axis=-1, keepdims=True) + NORM_EPS)
    scaled = gain_row * grad
    inner = jnp.mean(values * scaled, axis=-1, keepdims=True)
    result = root * scaled - values * (root * root * root * inner)
    return result, jnp.sum(values * root * grad, axis=0, keepdims=True)


def rows_back_body(
    rep,
    rows_ref,
    gains_ref,
    kv_ref,
    heads_ref,
    pick_ref,
    early_ref,
    base_ref,
    out_ref,
    attn_gain_ref,
    early_gain_ref,
    grad_kv_ref,
):
    count, groups, _, tok_rows, head = heads_ref.shape
    size = kv_ref.shape[1] // (2 * count)
    per_head = head // size
    for index in range(KVH):
        for kind in range(2):
            copies = [
                heads_ref[at // groups, at % groups, kind]
                for at in range(index * rep, (index + 1) * rep)
            ]
            total = copies[0]
            if rep > 1:
                total = sum(copy.astype(FULL) for copy in copies).astype(LOW)
            for piece in range(per_head):
                lane = (2 * (index * per_head + piece) + kind) * size
                grad_kv_ref[:, lane : lane + size] = total[:, piece * size : (piece + 1) * size]
    values = rows_ref[...].astype(FULL)
    own = values[tok_rows:]
    tok_part, tok_gain = norm_back_rows(
        values[:tok_rows], gains_ref[0:1, :], dot(grad_kv_ref[...], kv_ref[...], 1, 1)
    )
    pick_part, pick_gain = norm_back_rows(own, gains_ref[0:1, :], pick_ref[...])
    early_part, early_gain = norm_back_rows(own, gains_ref[2:3, :], early_ref[...])
    attn_gain_ref[...] = tok_gain + pick_gain
    early_gain_ref[...] = early_gain
    out_ref[0:tok_rows, :] = tok_part.astype(LOW)
    out_ref[tok_rows:, :] = (pick_part + early_part + base_ref[...]).astype(LOW)


def rows_back(rows_low, gains, proj, heads, grad_pick, grad_early, base, rep):
    tok_rows = heads.shape[3]
    width = rows_low.shape[1]
    size = 2 * KVH * HD
    return local_call(
        functools.partial(rows_back_body, rep),
        [rows_low, gains, proj, heads, grad_pick, grad_early, base],
        [entire(rows_low), entire(gains), column_block(proj, size, 0)]
        + [entire(a) for a in (heads, grad_pick, grad_early, base)],
        [
            struct(rows_low.shape, LOW),
            struct((1, width), FULL),
            struct((1, width), FULL),
            struct((tok_rows, size), LOW),
        ],
        2 * tok_rows * width * size,
        "rows_back",
    )


def assemble_body(out_columns, *refs):
    pieces, out_ref = refs[:-1], refs[-1]
    count = len(pieces)
    me = lax.axis_index("narrow")
    for step, piece in enumerate(pieces):
        source = lax.rem(me - step + count, count)
        spot = pl.ds(pl.multiple_of(source * out_columns, out_columns), out_columns)
        out_ref[:, spot] = piece[...]


def assemble(pieces):
    rows, columns = pieces[0].shape
    outputs = [struct((rows, columns * len(pieces)), pieces[0].dtype)]
    return local_call(
        functools.partial(assemble_body, columns),
        list(pieces),
        [entire(piece) for piece in pieces],
        outputs,
        0,
        "assemble",
    )[0]


def feed_body(inner_ref, weight_ref, gate_ref, up_ref, hidden_ref, out_ref, total):
    part = pl.program_id(0)
    inner = inner_ref[...]
    gate = dot(inner, weight_ref[0, 0], 1, 1)
    up = dot(inner, weight_ref[0, 1], 1, 1)
    hidden = (jax.nn.silu(gate) * up).astype(LOW)
    gate_ref[0] = gate
    up_ref[0] = up
    hidden_ref[0] = hidden
    product = dot(hidden, weight_ref[0, 2], 1, 0)

    @pl.when(part == 0)
    def _():
        total[...] = product

    @pl.when(part > 0)
    def _():
        total[...] = total[...] + product

    @pl.when(part == pl.num_programs(0) - 1)
    def _():
        out_ref[...] = total[...].astype(LOW)


def feed(inner, weight):
    parts, _, size, width = weight.shape
    sel = inner.shape[0]
    same = pl.BlockSpec((sel, width), lambda part: (0, 0))
    slab = pl.BlockSpec((1, sel, size), lambda part: (part, 0, 0))
    return pl.pallas_call(
        feed_body,
        grid=(parts,),
        in_specs=[same, pl.BlockSpec((1, 3, size, width), lambda part: (part, 0, 0, 0))],
        out_specs=[slab, slab, slab, same],
        out_shape=[
            struct((parts, sel, size), FULL),
            struct((parts, sel, size), FULL),
            struct((parts, sel, size), LOW),
            struct((sel, width), LOW),
        ],
        scratch_shapes=[pltpu.VMEM((sel, width), FULL)],
        compiler_params=pltpu.CompilerParams(vmem_limit_bytes=VMEM_BYTES),
        cost_estimate=pl.CostEstimate(
            flops=6 * sel * parts * size * width,
            bytes_accessed=weight.size * 2,
            transcendentals=0,
        ),
        name="feed",
    )(inner, weight)


def feed_back_body(grad_ref, weight_ref, gate_ref, up_ref, hidden_ref, acts_ref, out_ref, total):
    part = pl.program_id(0)
    grad_hidden = dot(grad_ref[...], weight_ref[0, 2], 1, 1)
    gate = gate_ref[0]
    sigma = jax.nn.sigmoid(gate)
    grad_gate = (grad_hidden * up_ref[0] * sigma * (1.0 + gate * (1.0 - sigma))).astype(LOW)
    grad_up = (grad_hidden * gate * sigma).astype(LOW)
    acts_ref[0, 0] = grad_gate
    acts_ref[0, 1] = grad_up
    acts_ref[0, 2] = hidden_ref[0]
    product = dot(grad_gate, weight_ref[0, 0], 1, 0) + dot(grad_up, weight_ref[0, 1], 1, 0)

    @pl.when(part == 0)
    def _():
        total[...] = product

    @pl.when(part > 0)
    def _():
        total[...] = total[...] + product

    @pl.when(part == pl.num_programs(0) - 1)
    def _():
        out_ref[...] = total[...].astype(LOW)


def feed_back(grad, weight, gate, up, hidden):
    parts, _, size, width = weight.shape
    sel = grad.shape[0]
    same = pl.BlockSpec((sel, width), lambda part: (0, 0))
    slab = pl.BlockSpec((1, sel, size), lambda part: (part, 0, 0))
    return pl.pallas_call(
        feed_back_body,
        grid=(parts,),
        in_specs=[same, pl.BlockSpec((1, 3, size, width), lambda part: (part, 0, 0, 0))]
        + [slab] * 3,
        out_specs=[pl.BlockSpec((1, 3, sel, size), lambda part: (part, 0, 0, 0)), same],
        out_shape=[struct((parts, 3, sel, size), LOW), struct((sel, width), LOW)],
        scratch_shapes=[pltpu.VMEM((sel, width), FULL)],
        compiler_params=pltpu.CompilerParams(vmem_limit_bytes=VMEM_BYTES),
        cost_estimate=pl.CostEstimate(
            flops=6 * sel * parts * size * width,
            bytes_accessed=weight.size * 2,
            transcendentals=0,
        ),
        name="feed_back",
    )(grad, weight, gate, up, hidden)


def newton_steps(problems):
    rows, width = problems[0][0].shape
    block = min(512, width)
    eye = lax.broadcasted_iota(jnp.int32, (rows, rows), 0) == lax.broadcasted_iota(
        jnp.int32, (rows, rows), 1
    )

    def strip(part):
        return pl.ds(pl.multiple_of(part * block, block), block)

    def over(function, start):
        return lax.fori_loop(0, width // block, function, start)

    def add_squares(part, totals):
        values = [current[:, strip(part)] for current, low, gram, rest in problems]
        return [total + jnp.sum(value * value) for total, value in zip(totals, values)]

    totals = over(add_squares, [jnp.float32(0.0)] * len(problems))
    scales = [1.0 / (jnp.sqrt(total) + 1e-07) for total in totals]

    def begin(part, carry):
        for scale, (current, low, gram, rest) in zip(scales, problems):
            values = current[:, strip(part)] * scale
            current[:, strip(part)] = values
            low[:, strip(part)] = values.astype(LOW)
        return carry

    over(begin, 0)

    def iteration(turn, carry):
        for current, low, gram, rest in problems:
            gram[...] = jnp.zeros_like(gram)

        def add_gram(part, carry):
            for current, low, gram, rest in problems:
                values = low[:, strip(part)]
                gram[...] = gram[...] + dot(values, values, 1, 1)
            return carry

        over(add_gram, 0)
        seconds = []
        for current, low, gram, rest in problems:
            whole = gram[...]
            middle = jnp.sum(jnp.where(eye, whole, 0.0)) / rows
            rest[...] = (whole - jnp.where(eye, middle, 0.0)).astype(LOW)
            square = dot(rest[...], rest[...], 1, 0)
            whole = gram[...]
            centred = whole - jnp.where(eye, middle, 0.0)
            square = square + 2.0 * middle * centred + jnp.where(eye, middle * middle, 0.0)
            whole = NEWTON_B * whole + NEWTON_C * square
            second = jnp.sum(jnp.where(eye, whole, 0.0)) / rows
            rest[...] = (whole - jnp.where(eye, second, 0.0)).astype(LOW)
            seconds.append(second)

        def apply(part, carry):
            for second, (current, low, gram, rest) in zip(seconds, problems):
                values = (NEWTON_A + second) * current[:, strip(part)] + dot(
                    rest[...], low[:, strip(part)], 1, 0
                )
                current[:, strip(part)] = values
                low[:, strip(part)] = values.astype(LOW)
            return carry

        over(apply, 0)
        return carry

    lax.fori_loop(0, NS_STEPS, iteration, 0)


def newton_scratch(rows, width):
    return [
        pltpu.VMEM((rows, width), FULL),
        pltpu.VMEM((rows, width), LOW),
        pltpu.VMEM((rows, rows), FULL),
        pltpu.VMEM((rows, rows), LOW),
    ]


def newton_cost(count, rows, width):
    return pl.CostEstimate(
        flops=NS_STEPS * count * (4 * rows * rows * width + 2 * rows * rows * rows),
        bytes_accessed=6 * count * rows * width,
        transcendentals=0,
    )


def newton_body(factor_ref, mom_ref, grad_ref, out_ref, *problem):
    current, low = problem[:2]
    parts, rows, columns = mom_ref.shape
    factor = factor_ref[0]
    for part in range(parts):
        spot = slice(part * columns, (part + 1) * columns)
        current[:, spot] = MOMENTUM * mom_ref[part].astype(FULL) + factor * grad_ref[
            :, spot
        ].astype(FULL)
    newton_steps([problem])
    for part in range(parts):
        out_ref[part] = low[:, part * columns : (part + 1) * columns]


def newton_small_body(rows, factor_ref, mom_ref, grad_ref, kv_ref, out_ref, *scratch):
    problems = [scratch[4 * at : 4 * at + 4] for at in range(4)]
    parts, _, columns = mom_ref.shape
    kv_columns = kv_ref.shape[2]
    half = rows // 2
    factor = factor_ref[0]
    for part in range(parts):
        spot = slice(part * columns, (part + 1) * columns)
        for member in range(2):
            current = problems[member][0]
            here = slice(member * rows, (member + 1) * rows)
            mom, grad = mom_ref[part, here, :], grad_ref[part, here, :]
            current[:, spot] = MOMENTUM * mom.astype(FULL) + factor * grad.astype(FULL)
        spot = slice(part * kv_columns, (part + 1) * kv_columns)
        for member in range(2):
            current = problems[2 + member][0]
            piece = kv_ref[part, member * rows : (member + 1) * rows, :].astype(FULL)
            for side in range(2):
                lane = (2 * member + side) * kv_columns
                mom = mom_ref[part, 2 * rows : 2 * rows + half, lane : lane + kv_columns]
                here = slice(side * half, (side + 1) * half)
                current[here, spot] = MOMENTUM * mom.astype(FULL) + factor * piece[here]
    newton_steps(problems[:2])
    newton_steps(problems[2:])
    out_ref[...] = jnp.zeros_like(out_ref)
    for part in range(parts):
        for member in range(2):
            out_ref[part, member * rows : (member + 1) * rows, :] = problems[member][1][
                :, part * columns : (part + 1) * columns
            ]
            low = problems[2 + member][1]
            for side in range(2):
                lane = (2 * member + side) * kv_columns
                out_ref[part, 2 * rows : 2 * rows + half, lane : lane + kv_columns] = low[
                    side * half : (side + 1) * half,
                    part * kv_columns : (part + 1) * kv_columns,
                ]


def newton_any_body(rows, factor_ref, mom_ref, grad_ref, qo_ref, kv_ref, out_ref, *scratch):
    parts = mom_ref.shape[0]
    owner = lax.rem(3 + lax.rem(lax.axis_index("wide"), 2), parts)
    small = lax.axis_index("narrow") == owner

    @pl.when(small)
    def _():
        newton_small_body(rows, factor_ref, mom_ref, qo_ref, kv_ref, out_ref, *scratch[4:])

    @pl.when(jnp.logical_not(small))
    def _():
        newton_body(factor_ref, mom_ref, grad_ref, out_ref, *scratch[:4])


def newton(factor, mom, grad, qo_grad, kv_grad):
    parts, slot_rows, columns = mom.shape
    width = parts * columns
    rows = kv_grad.shape[1] // 2
    kv_width = parts * kv_grad.shape[2]
    return pl.pallas_call(
        functools.partial(newton_any_body, rows),
        in_specs=[pl.BlockSpec(memory_space=pltpu.SMEM)] + [VMEM] * 4,
        out_specs=VMEM,
        out_shape=struct(mom.shape, LOW),
        scratch_shapes=newton_scratch(slot_rows, width)
        + newton_scratch(rows, width) * 2
        + newton_scratch(rows, kv_width) * 2,
        compiler_params=pltpu.CompilerParams(vmem_limit_bytes=VMEM_BYTES),
        cost_estimate=newton_cost(1, slot_rows, width),
        name="newton",
    )(factor.reshape(1), mom, grad, qo_grad, kv_grad)


def lookup_body(ids_ref, turn_ref, table_ref, out_ref, low_ref, list_ref, held, rows, sem):
    vocab = table_ref.shape[0]
    count = out_ref.shape[0]
    load = pltpu.make_async_copy(table_ref, held, sem)
    load.start()
    rows[...] = jnp.zeros_like(rows)

    found = turn_ref[count]

    def note(group, carry):
        for member in range(UNROLL):
            at = group * UNROLL + member
            list_ref[turn_ref[at]] = at
        return carry

    lax.fori_loop(0, count // UNROLL, note, 0)
    for member in range(UNROLL):
        list_ref[found + member] = count
    list_ref[count + UNROLL] = found
    load.wait()

    def step(group, carry):
        for member in range(UNROLL):
            at = list_ref[group * UNROLL + member]
            spot = jnp.minimum(ids_ref[jnp.minimum(at, count - 1)], vocab - 1)
            rows[pl.ds(at, 1), :] = held[pl.ds(spot, 1), :]
        return carry

    lax.fori_loop(0, (found + UNROLL - 1) // UNROLL, step, 0)
    out_ref[...] = rows[pl.ds(0, count), :].astype(LOW)
    low_ref[...] = held[...].astype(LOW)


def lookup(table, ids):
    vocab, columns = table.shape
    count = ids.shape[0]
    mine = (ids < vocab).reshape(-1, 128)
    before = jnp.arange(128)[:, None] < jnp.arange(128)[None, :]
    in_row = dot(mine.astype(LOW), before.astype(LOW), 1, 0)
    per_row = jnp.sum(mine.astype(FULL), axis=1)
    lines = jnp.arange(mine.shape[0])
    ahead = jnp.sum(jnp.where(lines[:, None] > lines[None, :], per_row[None, :], 0.0), axis=1)
    found = jnp.sum(per_row).astype(jnp.int32)
    turns = (in_row + ahead[:, None]).astype(jnp.int32)
    turns = jnp.where(mine, turns, count + UNROLL + 1).reshape(-1)
    turns = jnp.concatenate([turns, jnp.full((128,), found)])
    return pl.pallas_call(
        lookup_body,
        in_specs=[pl.BlockSpec(memory_space=pltpu.SMEM)] * 2 + [ANY],
        out_specs=[VMEM, VMEM, pl.BlockSpec(memory_space=pltpu.SMEM)],
        scratch_shapes=[
            pltpu.VMEM((vocab, columns), FULL),
            pltpu.VMEM((count + 8, columns), FULL),
            pltpu.SemaphoreType.DMA,
        ],
        out_shape=[
            struct((count, columns), LOW),
            struct((vocab, columns), LOW),
            struct((count + 2 * UNROLL,), jnp.int32),
        ],
        compiler_params=pltpu.CompilerParams(vmem_limit_bytes=VMEM_BYTES),
        cost_estimate=pl.CostEstimate(
            flops=0, bytes_accessed=vocab * columns * 4, transcendentals=0
        ),
        name="lookup",
    )(ids, turns, table)


def spread_body(
    ids_ref, list_ref, rows_ref, head_ref, out_ref, square_ref, even, odd, rows, sem
):
    vocab = out_ref.shape[0]
    count = rows_ref.shape[0]
    chunk = 256

    def strip(part):
        return pl.ds(pl.multiple_of(part * chunk, chunk), chunk)

    def begin(part, carry):
        even[strip(part), :] = head_ref[strip(part), :].astype(FULL)
        odd[strip(part), :] = jnp.zeros((chunk, odd.shape[1]), FULL)
        return carry

    lax.fori_loop(0, vocab // chunk, begin, 0)

    def widen(part, carry):
        rows[strip(part), :] = rows_ref[strip(part), :].astype(FULL)
        return carry

    lax.fori_loop(0, count // chunk, widen, 0)
    rows[pl.ds(count, 8), :] = jnp.zeros((8, rows.shape[1]), FULL)

    def step(group, carry):
        for member in range(UNROLL):
            at = list_ref[group * UNROLL + member]
            spot = jnp.minimum(ids_ref[jnp.minimum(at, count - 1)], vocab - 1)
            total = even if member % 2 == 0 else odd
            total[pl.ds(spot, 1), :] = total[pl.ds(spot, 1), :] + rows[pl.ds(at, 1), :]
        return carry

    found = list_ref[count + UNROLL]
    lax.fori_loop(0, (found + UNROLL - 1) // UNROLL, step, 0)

    def finish(part, squares):
        value = even[strip(part), :] + odd[strip(part), :]
        even[strip(part), :] = value
        return squares + jnp.sum((value * value).reshape(chunk // 8, 8, -1), axis=0)

    square_ref[...] = lax.fori_loop(
        0, vocab // chunk, finish, jnp.zeros((8, even.shape[1]), FULL)
    )
    store = pltpu.make_async_copy(even, out_ref, sem)
    store.start()
    store.wait()


def spread(ids, listed, rows, head):
    vocab, columns = head.shape
    count = ids.shape[0]
    smem = pl.BlockSpec(memory_space=pltpu.SMEM)
    return pl.pallas_call(
        spread_body,
        in_specs=[smem, smem, VMEM, VMEM],
        out_specs=[ANY, VMEM],
        scratch_shapes=[
            pltpu.VMEM((vocab, columns), FULL),
            pltpu.VMEM((vocab, columns), FULL),
            pltpu.VMEM((count + 8, columns), FULL),
            pltpu.SemaphoreType.DMA,
        ],
        out_shape=[struct((vocab, columns), FULL), struct((8, columns), FULL)],
        compiler_params=pltpu.CompilerParams(vmem_limit_bytes=VMEM_BYTES),
        cost_estimate=pl.CostEstimate(
            flops=count * columns, bytes_accessed=vocab * columns * 8, transcendentals=0
        ),
        name="spread",
    )(ids, listed, rows, head)


def adamw(weight, first_m, second_m, grad, rate, decay):
    first_new = BETA_ONE * first_m + (1.0 - BETA_ONE) * grad
    second_new = BETA_TWO * second_m + (1.0 - BETA_TWO) * grad * grad
    update = (
        first_new
        / (1.0 - BETA_ONE**STEP)
        / (jnp.sqrt(second_new / (1.0 - BETA_TWO**STEP)) + ADAM_EPS)
    )
    return (weight * (1.0 - rate * decay) - rate * update, first_new, second_new)


def cut_columns(values, count):
    rows, columns = values.shape
    return jnp.moveaxis(values.reshape(rows, count, columns // count), 1, 0)


def shifted(parts, axis, step):
    count = lax.axis_size(axis)
    pairs = [(source, (source + step) % count) for source in range(count)]
    return lax.ppermute(parts, axis, pairs)


def per_device(
    tokens,
    picks,
    targets,
    lengths,
    skip,
    embed,
    embed_m,
    embed_v,
    attn_qo,
    attn_qo_mom,
    attn_kv,
    attn_kv_mom,
    ffn,
    ffn_mom,
    gains,
    gains_m,
    gains_v,
):
    wide_count = lax.axis_size("wide")
    narrow_count = lax.axis_size("narrow")
    narrow_spot = lax.axis_index("narrow")
    wide_spot = lax.axis_index("wide")
    seq_len = tokens.shape[1]
    sel = picks.shape[1]
    vocab_rows, columns = embed.shape
    width = columns * wide_count
    own_rows = sel // narrow_count
    tok_rows = seq_len // narrow_count
    all_rows = own_rows + tok_rows
    heads_own = HEADS // narrow_count
    head_cols = heads_own * HD
    repeat = max(1, narrow_count // KVH)
    groups = KVH * repeat // narrow_count
    ffn_rows = ffn.shape[0]
    ffn_size = ffn_rows // narrow_count
    total_rows = wide_count * sel
    lens = lengths[0]
    pick_ids = picks[0]
    keep_layer = (1 - skip[0]).astype(FULL)
    keep_row = jnp.full((1, width), keep_layer)
    lanes = 128

    def box(flat):
        height = -(-flat.shape[0] // (8 * lanes)) * 8
        return jnp.pad(flat, (0, height * lanes - flat.shape[0])).reshape(height, lanes)

    ffn_low = jnp.moveaxis(ffn, 1, 0).astype(LOW)
    ffn_cut = ffn_low.reshape(3, narrow_count, ffn_size, ffn_low.shape[2])
    ffn_cut = jnp.moveaxis(ffn_cut, 1, 0).reshape(narrow_count, 3 * ffn_size, -1)
    kv_own = attn_kv.reshape(columns, -1).astype(LOW)

    where_at = jnp.arange(seq_len, dtype=jnp.int32)
    pick_tokens = jnp.sum(
        jnp.where(pick_ids[:, None] == where_at[None, :], tokens[0][None, :], 0), axis=1
    )
    ints = box(jnp.concatenate([tokens[0], pick_tokens, targets[0]]))
    all_ints, all_gains, kv_part = launch(
        [
            gather_wide(ints),
            gather_both(box(gains.astype(LOW).astype(FULL).reshape(-1))),
            gather_blocks("narrow", kv_own),
        ],
        0,
        "gather_ids",
    )
    kv_part = jnp.moveaxis(kv_part, 0, 1).reshape(columns, -1)
    proj_own = jnp.concatenate([kv_part, attn_qo.reshape(columns, -1).astype(LOW)], axis=1)
    proj = lax.all_gather(proj_own, "wide", axis=0, tiled=True)
    ffn_cut, all_ints = lax.optimization_barrier((ffn_cut, all_ints))
    ffn_pieces = [lax.dynamic_index_in_dim(ffn_cut, narrow_spot, 0, False)] + [
        shifted(
            lax.dynamic_index_in_dim(
                ffn_cut, lax.rem(narrow_spot + step, narrow_count), 0, False
            ),
            "narrow",
            step,
        )
        for step in range(1, narrow_count)
    ]
    gain_size = gains.shape[1]
    gain_w = all_gains.reshape(narrow_count, wide_count, -1)[:, :, : 3 * gain_size]
    gain_w = gain_w.reshape(narrow_count, wide_count, 3, gain_size)
    gain_w = jnp.transpose(gain_w, (2, 1, 0, 3)).reshape(3, width)
    all_ints = all_ints.reshape(wide_count, -1)
    tokens_all = all_ints[:, :seq_len].reshape(wide_count, narrow_count, tok_rows)
    picked_all = all_ints[:, seq_len : seq_len + sel].reshape(wide_count, narrow_count, own_rows)
    targets_all = all_ints[:, seq_len + sel : seq_len + 2 * sel].reshape(-1)
    wanted = jnp.moveaxis(jnp.concatenate([tokens_all, picked_all], axis=2), 1, 0).reshape(-1)
    local_ids = wanted - narrow_spot * vocab_rows
    inside = (local_ids >= 0) & (local_ids < vocab_rows)
    spots = jnp.where(inside, local_ids, vocab_rows)
    found, embed_low, listed = lookup(embed, spots)
    ffn_pieces, found = lax.optimization_barrier((ffn_pieces, found))
    ffn_sub = assemble(ffn_pieces).reshape(3, ffn_size, width)
    ffn_sub, found = lax.optimization_barrier((ffn_sub, found))
    ffn_w = lax.all_gather(ffn_sub, "wide", axis=0)
    found = found.reshape(narrow_count, wide_count * all_rows, columns)
    embed_cut = embed_low.reshape(wide_count, vocab_rows // wide_count, columns)
    table_half = embed_cut.shape[1] // 2
    rows_low, table_top = launch(
        [fetch_rows(found, all_rows), join_columns("wide", embed_cut[:, :table_half])],
        1,
        "fetch_rows",
    )

    mom_qo = jnp.moveaxis(attn_qo_mom, 1, 0)
    mom_kv = jnp.moveaxis(attn_kv_mom, 1, 0)
    mom_ffn = jnp.moveaxis(ffn_mom, 1, 0)
    slot_rows, slot_cols = mom_ffn.shape[1:]

    block_rows, q_size = mom_qo.shape[1:]
    kv_size = mom_kv.shape[2]
    half_rows = block_rows // 2
    kv_box = jnp.moveaxis(mom_kv.reshape(4, half_rows, kv_size), 0, 1).reshape(half_rows, -1)
    small_box = jnp.concatenate([mom_qo.reshape(2 * block_rows, q_size), kv_box])
    small_box = jnp.pad(small_box, ((0, slot_rows - small_box.shape[0]), (0, 0)))
    mom_parts = jnp.concatenate([mom_ffn, small_box[None]]).astype(LOW)

    seg_all, cosine_all, sine_all = angles_at(lens, where_at)
    cosine_all, sine_all = wide_angles(cosine_all, sine_all)
    seg_mine, cosine, sine = angles_at(lens, pick_ids)
    cosine, sine = wide_angles(cosine, sine)

    def tok_part(angles):
        return lax.dynamic_slice_in_dim(angles, narrow_spot * tok_rows, tok_rows, 0)

    by_head, normed_tok = make_heads(
        rows_low, gain_w[0:1], proj, tok_part(cosine_all), tok_part(sine_all), groups, repeat
    )
    own_head, start_low, tok_cols, table_low = launch(
        [
            swap_blocks("narrow", by_head),
            gather_blocks("narrow", rows_low[tok_rows:]),
            split_columns("wide", normed_tok),
            join_columns("wide", embed_cut[:, table_half:]),
        ],
        2,
        "trade_heads",
    )
    start_low, ffn_w = lax.optimization_barrier((start_low, ffn_w))
    start_low = start_low.reshape(sel, width)
    queries, probs, mixed, attn_part, normed, early_part = attend(
        start_low,
        gain_w,
        proj,
        own_head,
        cosine,
        sine,
        seg_mine[:, None],
        seg_all[None, :],
        pick_ids[:, None],
    )
    early = lax.all_gather(early_part, "wide", axis=0, tiled=True)
    start_own = rows_low[tok_rows:].astype(FULL)
    middle, inner, mixed_wide, pick_cols = launch(
        [
            settle(
                attn_part,
                start_own,
                start_own,
                jnp.ones((1, width), FULL),
                gain_w[1:2],
            ),
            gather_wide(mixed),
            split_columns("wide", normed),
        ],
        3,
        "settle_middle",
    )
    inner = inner.reshape(sel, width)
    inner_all = lax.all_gather(inner, "wide", axis=0, tiled=True)
    gate, up, hidden, fed = feed(inner, ffn_w)
    final_own, late_part = launch(
        [settle(fed, middle, start_own, keep_row, gain_w[2:3])], 4, "settle_late"
    )
    table_own = jnp.concatenate([table_top, table_low])

    table_count = table_own.shape[0]
    local_target = targets_all - (narrow_spot * vocab_rows + wide_spot * table_count)
    has_target = local_target[:, None] == jnp.arange(table_count, dtype=jnp.int32)[None, :]
    counted = (targets_all >= 0).astype(FULL)
    loss_count = jnp.sum(counted)

    def exit_logits(features):
        logits = dot(features, table_own, 1, 1)
        peak = jnp.max(logits, axis=-1)
        total = jnp.sum(jnp.exp(logits - peak[:, None]), axis=-1)
        picked = jnp.sum(jnp.where(has_target, logits, 0.0), axis=-1)
        return logits, jnp.stack([peak, total, picked])

    half = slot_rows // 2
    late, mom_top = launch(
        [
            gather_wide(late_part.reshape(sel, width)),
            swap_turned(mom_parts[:, :half]),
        ],
        5,
        "gather_late",
    )
    late = late.reshape(total_rows, width)
    early_logits, early_stats = exit_logits(early)
    late_logits, late_stats = exit_logits(late)
    stats = jnp.concatenate([early_stats, late_stats], axis=1).reshape(3, 8, -1)
    stats = launch([combine(stats, merge_stats)], 6, "combine_stats")[0]
    stats, inner_all = lax.optimization_barrier((stats, inner_all))
    stats = stats.reshape(3, -1)
    log_norms = stats[0] + jnp.log(stats[1])
    losses = log_norms - stats[2]
    loss_sum = jnp.sum(
        counted * (EXIT_EARLY * losses[:total_rows] + EXIT_LAST * losses[total_rows:])
    )

    def exit_back(logits, log_norm, weight, features):
        grad_logits = (
            (jnp.exp(logits - log_norm[:, None]) - has_target.astype(FULL))
            * (weight * counted)[:, None]
        ).astype(LOW)
        return dot(grad_logits, table_own, 1, 0).astype(LOW), dot(grad_logits, features, 0, 0)

    late_back, late_head = exit_back(late_logits, log_norms[total_rows:], EXIT_LAST, late)
    grad_late, mom_low = launch(
        [sum_wide(late_back), swap_turned(mom_parts[:, half:])], 7, "sum_late"
    )
    early_norms, grad_late = lax.optimization_barrier((log_norms[:total_rows], grad_late))
    early_back, early_head = exit_back(early_logits, early_norms, EXIT_EARLY, early)
    mom_owned = jnp.concatenate([mom_top, mom_low], axis=1)
    grad_head = (early_head + late_head).astype(LOW)

    grad_early = lax.psum_scatter(early_back, "wide", scatter_dimension=0, tiled=True)
    grad_final, gain_late, grad_out = launch(
        [
            settle_back(
                grad_late.astype(LOW),
                final_own,
                jnp.zeros_like(final_own),
                keep_row,
                gain_w[2:3],
            ),
        ],
        8,
        "back_late",
    )
    grad_layer = grad_final * keep_layer
    grad_out = grad_out.reshape(sel, width)
    out_all = lax.all_gather(grad_out, "wide", axis=0, tiled=True)
    acts, fed_back = feed_back(grad_out, ffn_w, gate, up, hidden)
    grad_mid, gain_mid, grad_branch, acts = launch(
        [
            settle_back(fed_back, middle, grad_layer, keep_row, gain_w[1:2]),
            swap_blocks("wide", acts),
        ],
        9,
        "back_middle",
    )
    acts = jnp.moveaxis(acts, 1, 0).reshape(3, total_rows, ffn_size)
    grad_branch, grad_early = lax.optimization_barrier((grad_branch, grad_early))
    grad_branch = grad_branch.reshape(sel, width)

    kv_parts, grad_queries, pick_part = attend_back(
        grad_branch, proj, own_head, queries, probs, cosine, sine, cosine_all, sine_all
    )
    grad_kv, grad_pick, grad_early, queries_wide, branch_cols = launch(
        [
            swap_blocks("narrow", kv_parts),
            sum_narrow(pick_part),
            sum_narrow(grad_early),
            gather_wide(grad_queries),
            split_columns("wide", grad_branch),
        ],
        10,
        "trade_grads",
    )
    grad_kv, out_all = lax.optimization_barrier((grad_kv, out_all))
    grad_base = grad_mid + grad_final * (1.0 - keep_layer)
    grad_rows, gain_attn, gain_early, grad_kv = rows_back(
        rows_low, gain_w, proj, grad_kv, grad_pick, grad_early, grad_base, repeat
    )
    rights = (inner_all, inner_all, out_all)
    grad_ffn = [dot(acts[j], rights[j], 0, 0) for j in range(3)]
    ffn_squares = sum(jnp.sum(part * part) for part in grad_ffn)
    final_parts = jnp.stack([part.astype(LOW) for part in grad_ffn])
    summed_qo = jnp.stack(
        [
            jnp.einsum("wtc,wtf->cf", pick_cols, queries_wide, preferred_element_type=FULL),
            jnp.einsum("wtc,wtf->cf", branch_cols, mixed_wide, preferred_element_type=FULL),
        ]
    )
    qo_owned = lax.all_gather(
        summed_qo.astype(LOW).reshape(2 * columns, q_size), "narrow", axis=0
    )
    grad_rows, acts_owned, kv_wide, head_cols_all = launch(
        [
            return_rows(grad_rows),
            swap_owned(acts, 5),
            later(gather_wide(grad_kv, 3), 2),
            later(split_columns("wide", grad_head, 3), 2),
        ],
        11,
        "return_rows",
    )
    turn = lax.rem(wide_spot, 2)
    grad_kv_w = jnp.einsum(
        "wtc,wtf->cf", tok_cols, kv_wide, preferred_element_type=FULL
    ).reshape(columns, narrow_count, 2, kv_size)
    grad_kv_w = jnp.moveaxis(grad_kv_w, 0, 2)
    summed_kv = lax.psum_scatter(grad_kv_w, "narrow", scatter_dimension=0, tiled=True)[0]
    summed_table, table_squares = spread(
        spots, listed, grad_rows.reshape(-1, columns), head_cols_all.reshape(vocab_rows, columns)
    )

    squares = (
        jnp.sum(summed_qo * summed_qo)
        + jnp.sum(summed_kv * summed_kv)
        + ffn_squares
        + jnp.sum(table_squares)
    )
    sums = jnp.stack(
        [gain_attn[0], gain_mid[0], gain_early[0] + gain_late[0], jnp.full((width,), squares)]
    )
    sums, kv_owned = launch(
        [
            combine(sums.reshape(4, 8, -1), add_two),
            send_owner(summed_kv.astype(LOW).reshape(2 * block_rows, kv_size)),
        ],
        12,
        "combine_sums",
    )
    sums = sums.reshape(4, width)
    summed_gain = lax.dynamic_slice_in_dim(
        sums[:3], (wide_spot * narrow_count + narrow_spot) * gain_size, gain_size, 1
    )
    square_total = sums[3, 0] + jnp.sum(sums[:3] * sums[:3])
    grad_norm = jnp.sqrt(square_total) / loss_count
    factor = jnp.minimum(1.0, CLIP_NORM / (grad_norm + 1e-06)) / loss_count

    matrix = jnp.minimum(lax.rem(narrow_spot + narrow_count - turn, narrow_count), 2)
    right = jnp.where(matrix == 2, out_all, inner_all)
    owned = jnp.einsum("stf,td->sfd", acts_owned, right, preferred_element_type=FULL)
    final_parts, factor = lax.optimization_barrier((final_parts, factor))
    size = width // narrow_count

    def final_piece(spot):
        return lax.dynamic_slice_in_dim(final_parts, spot * size, size, 2)

    pieces = [final_piece(narrow_spot)] + [
        shifted(final_piece(lax.rem(narrow_spot + step, narrow_count)), "narrow", step)
        for step in range(1, narrow_count)
    ]
    directions = newton(
        factor, mom_owned, owned.reshape(ffn_rows, width), qo_owned, kv_owned
    )
    directions, pieces, ffn = lax.optimization_barrier((directions, pieces, ffn))
    summed_ffn = jnp.zeros((3, narrow_count, ffn_size, size), LOW)
    for step, piece in enumerate(pieces):
        source = lax.rem(narrow_spot - step + narrow_count, narrow_count)
        summed_ffn = lax.dynamic_update_index_in_dim(summed_ffn, piece, source, 1)
    summed_ffn = summed_ffn.reshape(3, ffn_rows, size).astype(FULL)
    received = [lax.dynamic_index_in_dim(directions, narrow_spot, 0, False)] + [
        shifted(
            lax.dynamic_index_in_dim(
                directions, lax.rem(narrow_spot + step, narrow_count), 0, False
            ),
            "narrow",
            step,
        )
        for step in range(1, narrow_count)
    ]

    def direction_of(matrix):
        step = lax.rem(narrow_spot - matrix - turn + 2 * narrow_count, narrow_count)
        result = received[0]
        for at in range(1, narrow_count):
            result = jnp.where(step == at, received[at], result)
        return result

    dir_ffn = jnp.stack([direction_of(matrix) for matrix in range(3)]).astype(FULL)
    small = direction_of(3).astype(FULL)
    dir_qo = small[: 2 * block_rows].reshape(mom_qo.shape)
    dir_kv = small[2 * block_rows : 2 * block_rows + half_rows].reshape(half_rows, 4, kv_size)
    dir_kv = jnp.moveaxis(dir_kv, 1, 0).reshape(mom_kv.shape)

    embed_new, embed_m_new, embed_v_new = adamw(
        embed, embed_m, embed_v, summed_table * factor, RATE_ADAM, WEIGHT_DECAY
    )
    gains_new, gains_m_new, gains_v_new = adamw(
        gains, gains_m, gains_v, summed_gain * factor, RATE_GAIN, 0.0
    )

    def mom_next(mom, grad):
        return MOMENTUM * mom + jnp.moveaxis(grad * factor, 0, 1)

    shrink = 1.0 - RATE_MUON * WEIGHT_DECAY

    def weight_next(weight, direction):
        return weight * shrink - RATE_MUON * jnp.moveaxis(direction, 0, 1)

    return (
        loss_sum,
        loss_count,
        grad_norm,
        embed_new,
        embed_m_new,
        embed_v_new,
        weight_next(attn_qo, dir_qo),
        mom_next(attn_qo_mom, summed_qo),
        weight_next(attn_kv, dir_kv),
        mom_next(attn_kv_mom, summed_kv),
        weight_next(ffn, dir_ffn),
        mom_next(ffn_mom, summed_ffn),
        gains_new,
        gains_m_new,
        gains_v_new,
    )


def solution(mesh):
    by_pack = P("wide", None)
    table = P("narrow", "wide")
    layer = P("wide", None, "narrow")
    gain = P(None, ("wide", "narrow"))
    return jax.shard_map(
        per_device,
        mesh=mesh,
        in_specs=(by_pack,) * 4 + (P("wide"),) + (table,) * 3 + (layer,) * 6 + (gain,) * 3,
        out_specs=(P(),) * 3 + (table,) * 3 + (layer,) * 6 + (gain,) * 3,
        check_vma=False,
    )
```

```python
import functools

import jax
import jax.numpy as jnp
from jax import lax
from jax.experimental import pallas as pl
from jax.experimental.pallas import tpu as pltpu
from jax.sharding import PartitionSpec as P

HEADS = 16
HD = 128
KVH = 4
NS_STEPS = 5
STEP = 10


NORM_EPS = 1e-05
ROPE_BASE = 10000.0
EXIT_EARLY = 0.25
EXIT_LAST = 1.0
CLIP_NORM = 0.02
BETA_ONE = 0.9
BETA_TWO = 0.95
ADAM_EPS = 1e-08
RATE_ADAM = 0.02
RATE_GAIN = 0.3
RATE_MUON = 0.3
WEIGHT_DECAY = 0.1
MOMENTUM = 0.95
NEWTON_A = 3.4445
NEWTON_B = -4.775
NEWTON_C = 2.0315
MASKED = -1e30
LOW = jnp.bfloat16
FULL = jnp.float32
BOTH = ("wide", "narrow")
UNROLL = 16
VMEM_BYTES = 56 * 1024 * 1024


def dot(first, second, first_dim, second_dim):
    return lax.dot_general(
        first, second, (((first_dim,), (second_dim,)), ((), ())), preferred_element_type=FULL
    )


def norm_rows(values, gain_row):
    return (
        values * lax.rsqrt(jnp.mean(values * values, axis=-1, keepdims=True) + NORM_EPS) * gain_row
    )


def segments_at(lens, where_at):
    ends = jnp.cumsum(lens)
    return jnp.sum((where_at[:, None] >= ends[None, :]).astype(jnp.int32), axis=1)


def angles_at(lens, where_at):
    segment = segments_at(lens, where_at)
    starts = jnp.cumsum(lens) - lens
    member = segment[:, None] == jnp.arange(lens.shape[0], dtype=jnp.int32)[None, :]
    begin = jnp.sum(jnp.where(member, starts[None, :], 0), axis=1)
    offset_pos = (where_at - begin).astype(FULL)
    inverse = ROPE_BASE ** (-2.0 * jnp.arange(HD // 2, dtype=FULL) / HD)
    angle = offset_pos[:, None] * inverse[None, :]
    return (segment, jnp.cos(angle), jnp.sin(angle))


MESH = pl.DeviceIdType.MESH
ANY = pl.BlockSpec(memory_space=pl.ANY)
VMEM = pl.BlockSpec(memory_space=pltpu.VMEM)


def others(axis, count):
    me = lax.axis_index(axis)
    return [{axis: lax.rem(me + step, count)} for step in range(1, count)]


def push(source, target, send, receive, device):
    return pltpu.make_async_remote_copy(
        src_ref=source,
        dst_ref=target,
        send_sem=send,
        recv_sem=receive,
        device_id=device,
        device_id_type=MESH,
    )


def arrived(block, send, receive, device):
    push(block, block, send, receive, device).wait_recv()


def like(values):
    return jax.ShapeDtypeStruct(values.shape, values.dtype)


def struct(shape, dtype):
    return jax.ShapeDtypeStruct(shape, dtype)


def sems(*shape):
    return pltpu.SemaphoreType.DMA(shape)


class Task:
    def __init__(self, inputs, outputs, scratch, steps, place_in, place_out, axes):
        self.inputs, self.outputs, self.scratch, self.steps = inputs, outputs, scratch, steps
        self.place_in = [place_in] * len(inputs)
        self.place_out = [place_out] * len(outputs)
        self.axes = axes


def launch(tasks, ident, name):
    axes = sorted(set(axis for task in tasks for axis in task.axes))
    inputs = [a for task in tasks for a in task.inputs]
    outputs = [a for task in tasks for a in task.outputs]
    scratch = [a for task in tasks for a in task.scratch]

    def body(*refs):
        refs = list(refs)
        ins = refs[: len(inputs)]
        outs = refs[len(inputs) : len(inputs) + len(outputs)]
        extra = refs[len(inputs) + len(outputs) :]
        barrier = pltpu.get_barrier_semaphore()
        targets = [device for axis in axes for device in others(axis, lax.axis_size(axis))]
        for device in targets:
            pl.semaphore_signal(barrier, inc=1, device_id=device, device_id_type=MESH)
        pl.semaphore_wait(barrier, len(targets))
        live = []
        for task in tasks:
            counts = (len(task.inputs), len(task.outputs), len(task.scratch))
            live.append(task.steps(ins[: counts[0]], outs[: counts[1]], extra[: counts[2]]))
            ins, outs, extra = ins[counts[0] :], outs[counts[1] :], extra[counts[2] :]
        while live:
            live = [steps for steps in live if next(steps, 0) is None]

    size = sum(a.size * a.dtype.itemsize for a in list(inputs) + list(outputs))
    return pl.pallas_call(
        body,
        out_shape=outputs,
        in_specs=[place for task in tasks for place in task.place_in],
        out_specs=[place for task in tasks for place in task.place_out],
        scratch_shapes=scratch,
        compiler_params=pltpu.CompilerParams(
            collective_id=ident, has_side_effects=True, vmem_limit_bytes=VMEM_BYTES
        ),
        cost_estimate=pl.CostEstimate(flops=0, bytes_accessed=size // 8, transcendentals=0),
        name=name,
    )(*inputs)


def later(task, turns):
    begin = task.steps

    def steps(ins, outs, scratch):
        for turn in range(turns):
            yield
        yield from begin(ins, outs, scratch)

    task.steps = steps
    return task


def gather_wide(values, patience=1):
    count = lax.axis_size("wide")
    chips = count // 2

    def steps(ins, outs, scratch):
        (x_ref,), (out_ref,), (send, receive, local) = ins, outs, scratch
        me = lax.axis_index("wide")
        mate = me + 1 - 2 * lax.rem(me, 2)
        peers = [lax.rem(me + 2 * step, count) for step in range(1, chips)] + [mate]
        first = []
        for step, peer in enumerate(peers):
            copy = push(x_ref, out_ref.at[me], send.at[step], receive.at[me], {"wide": peer})
            copy.start()
            first.append(copy)
        keep = pltpu.make_async_copy(x_ref, out_ref.at[me], local)
        keep.start()
        for turn in range(patience):
            yield
        second = []
        for step in range(1, chips):
            source = lax.rem(me - 2 * step + count, count)
            block = out_ref.at[source]
            arrived(block, send.at[0], receive.at[source], {"wide": mate})
            copy = push(
                block, block, send.at[chips + step - 1], receive.at[source], {"wide": mate}
            )
            copy.start()
            second.append(copy)
        yield
        for step in range(chips):
            source = lax.rem(mate - 2 * step + count, count)
            arrived(out_ref.at[source], send.at[0], receive.at[source], {"wide": mate})
        for copy in first + second:
            copy.wait_send()
        keep.wait()

    shape = struct((count,) + values.shape, values.dtype)
    return Task(
        [values], [shape], [sems(count - 1), sems(count), sems()], steps, ANY, ANY, ["wide"]
    )


def trade(axis, values, source_of, target_of, shape, patience=2):
    count = lax.axis_size(axis)

    def steps(ins, outs, scratch):
        (x_ref,), (out_ref,), (send, receive, local) = ins, outs, scratch
        me = lax.axis_index(axis)
        copies = []
        for step in range(1, count):
            peer = lax.rem(me + step, count)
            copy = push(
                source_of(x_ref, peer),
                target_of(out_ref, me),
                send.at[step - 1],
                receive.at[me],
                {axis: peer},
            )
            copy.start()
            copies.append(copy)
        keep = pltpu.make_async_copy(source_of(x_ref, me), target_of(out_ref, me), local)
        keep.start()
        for turn in range(patience):
            yield
        for step in range(1, count):
            source = lax.rem(me - step + count, count)
            arrived(
                target_of(out_ref, source), send.at[0], receive.at[source], {axis: source}
            )
        for copy in copies:
            copy.wait_send()
        keep.wait()

    return Task(
        [values],
        [struct(shape, values.dtype)],
        [sems(count - 1), sems(count), sems()],
        steps,
        ANY,
        ANY,
        [axis],
    )


def block_at(ref, spot):
    return ref.at[spot]


def whole_at(ref, spot):
    return ref


def columns_of(size):
    def at(ref, spot):
        return ref.at[:, pl.ds(pl.multiple_of(spot * size, size), size)]

    return at


def turned(ref, spot):
    count = lax.axis_size("narrow")
    matrix = lax.rem(spot + count - lax.rem(lax.axis_index("wide"), 2), count)
    return ref.at[jnp.minimum(matrix, 3)]


def swap_turned(values, patience=2):
    shape = (lax.axis_size("narrow"),) + values.shape[1:]
    return trade("narrow", values, turned, block_at, shape, patience)


def product(lefts, rights, sums):
    count = len(lefts)
    columns = rights[0].shape[1]
    block = min(512, columns)
    outputs = 1 if sums else count
    rows = lefts[0].shape[1]

    def steps(ins, outs, scratch):
        left_refs, right_refs = ins[:count], ins[count:]
        result_refs, square_ref = outs[:outputs], outs[outputs]
        yield
        square_ref[...] = jnp.zeros_like(square_ref)
        for at in range(outputs):
            members = range(count) if sums else [at]

            def strip(part, carry):
                spot = pl.ds(pl.multiple_of(part * block, block), block)
                value = jnp.zeros((rows, block), FULL)
                for member in members:
                    value = value + dot(left_refs[member][...], right_refs[member][:, spot], 0, 0)
                result_refs[at][:, spot] = value.astype(LOW)
                if not sums:
                    square_ref[:, spot] = square_ref[:, spot] + jnp.sum(
                        value * value, axis=0, keepdims=True
                    )
                return carry

            lax.fori_loop(0, columns // block, strip, 0)
            yield

    return Task(
        list(lefts) + list(rights),
        [struct((rows, columns), LOW)] * outputs + [struct((1, columns), FULL)],
        [],
        steps,
        VMEM,
        VMEM,
        [],
    )


def swap_owned(values, patience):
    count = lax.axis_size("narrow")

    def steps(ins, outs, scratch):
        (x_ref,), (out_ref,), (send, receive, local) = ins, outs, scratch
        me = lax.axis_index("narrow")
        turn = lax.rem(lax.axis_index("wide"), 2)

        def matrix_of(device):
            return lax.rem(device + count - turn, count)

        def copy_to(step):
            peer = lax.rem(me + step, count)
            return push(
                x_ref.at[jnp.minimum(matrix_of(peer), 2)],
                out_ref.at[me],
                send.at[step - 1],
                receive.at[me],
                {"narrow": peer},
            )

        def keep():
            return pltpu.make_async_copy(
                x_ref.at[jnp.minimum(matrix_of(me), 2)], out_ref.at[me], local
            )

        keep().start()
        for step in range(1, count):

            @pl.when(matrix_of(lax.rem(me + step, count)) < 3)
            def _():
                copy_to(step).start()

        for turn_at in range(patience):
            yield

        @pl.when(matrix_of(me) < 3)
        def _():
            for step in range(1, count):
                source = lax.rem(me - step + count, count)
                arrived(out_ref.at[source], send.at[0], receive.at[source], {"narrow": source})

        for step in range(1, count):

            @pl.when(matrix_of(lax.rem(me + step, count)) < 3)
            def _():
                copy_to(step).wait_send()

        keep().wait()

    return Task(
        [values],
        [struct((count,) + values.shape[1:], values.dtype)],
        [sems(count - 1), sems(count), sems()],
        steps,
        ANY,
        ANY,
        ["narrow"],
    )


def send_owner(values):
    count = lax.axis_size("narrow")

    def steps(ins, outs, scratch):
        (x_ref,), (out_ref,), (send, receive, local) = ins, outs, scratch
        me = lax.axis_index("narrow")
        owner = lax.rem(3 + lax.rem(lax.axis_index("wide"), 2), count)
        keep = pltpu.make_async_copy(x_ref, out_ref.at[me], local)
        keep.start()

        def to_owner():
            return push(x_ref, out_ref.at[me], send.at[0], receive.at[me], {"narrow": owner})

        @pl.when(me != owner)
        def _():
            to_owner().start()

        yield
        yield

        @pl.when(me != owner)
        def _():
            to_owner().wait_send()

        @pl.when(me == owner)
        def _():
            for step in range(1, count):
                source = lax.rem(owner + step, count)
                arrived(out_ref.at[source], send.at[0], receive.at[source], {"narrow": source})

        keep.wait()

    return Task(
        [values],
        [struct((count,) + values.shape, values.dtype)],
        [sems(1), sems(count), sems()],
        steps,
        ANY,
        ANY,
        ["narrow"],
    )


def swap_blocks(axis, values):
    return trade(axis, values, block_at, block_at, values.shape)


def gather_blocks(axis, values):
    shape = (lax.axis_size(axis),) + values.shape
    return trade(axis, values, whole_at, block_at, shape)


def split_columns(axis, values, patience=2):
    count = lax.axis_size(axis)
    rows, size = values.shape[0], values.shape[1] // count
    return trade(axis, values, columns_of(size), block_at, (count, rows, size), patience)


def join_columns(axis, values):
    count, rows, size = values.shape
    return trade(axis, values, block_at, columns_of(size), (rows, count * size))


def collect(count, parts_ref, slots, send, receive):
    me = lax.axis_index("narrow")
    copies = []
    for step in range(1, count):
        peer = lax.rem(me + step, count)
        copy = push(
            parts_ref.at[peer],
            slots.at[me],
            send.at[step - 1],
            receive.at[me],
            {"narrow": peer},
        )
        copy.start()
        copies.append(copy)
    return copies


def collected(count, parts_ref, slots, send, receive):
    me = lax.axis_index("narrow")
    total = parts_ref[me].astype(FULL)
    for step in range(1, count):
        source = lax.rem(me - step + count, count)
        arrived(slots.at[source], send.at[0], receive.at[source], {"narrow": source})
        total = total + slots[source].astype(FULL)
    return total


def share(count, low, all_ref, send, receive):
    me = lax.axis_index("narrow")
    all_ref[me] = low
    copies = []
    for step in range(1, count):
        peer = lax.rem(me + step, count)
        copy = push(
            all_ref.at[me], all_ref.at[me], send.at[step - 1], receive.at[me], {"narrow": peer}
        )
        copy.start()
        copies.append(copy)
    return copies


def shared(count, all_ref, send, receive):
    me = lax.axis_index("narrow")
    for step in range(1, count):
        source = lax.rem(me - step + count, count)
        arrived(all_ref.at[source], send.at[0], receive.at[source], {"narrow": source})


def narrow_sems(count):
    return [sems(count - 1), sems(count)]


def settle(partial, base, other, keep_row, gain_row):
    count = lax.axis_size("narrow")
    rows, width = base.shape

    def steps(ins, outs, scratch):
        parts_ref, base_ref, other_ref, keep_ref, gain_ref = ins
        own_ref, all_ref = outs
        slots, send, receive, send_all, receive_all = scratch
        copies = collect(count, parts_ref, slots, send, receive)
        yield
        total = collected(count, parts_ref, slots, send, receive)
        total = jnp.where(keep_ref[...] > 0, total + base_ref[...], other_ref[...])
        own_ref[...] = total
        low = norm_rows(total, gain_ref[...]).astype(LOW)
        copies = copies + share(count, low, all_ref, send_all, receive_all)
        yield
        shared(count, all_ref, send_all, receive_all)
        for copy in copies:
            copy.wait_send()

    return Task(
        [partial.reshape(count, rows, width), base, other, keep_row, gain_row],
        [struct((rows, width), FULL), struct((count, rows, width), LOW)],
        [pltpu.VMEM((count, rows, width), partial.dtype)]
        + narrow_sems(count)
        + narrow_sems(count),
        steps,
        VMEM,
        VMEM,
        ["narrow"],
    )


def settle_back(partial, values, add, keep_row, gain_row):
    count = lax.axis_size("narrow")
    rows, width = values.shape

    def steps(ins, outs, scratch):
        parts_ref, values_ref, add_ref, keep_ref, gain_ref = ins
        own_ref, gain_grad_ref, all_ref = outs
        slots, send, receive, send_all, receive_all = scratch
        copies = collect(count, parts_ref, slots, send, receive)
        yield
        grad = collected(count, parts_ref, slots, send, receive)
        held = values_ref[...]
        root = lax.rsqrt(jnp.mean(held * held, axis=-1, keepdims=True) + NORM_EPS)
        scaled = gain_ref[...] * grad
        inner = jnp.mean(held * scaled, axis=-1, keepdims=True)
        own = add_ref[...] + root * scaled - held * (root * root * root * inner)
        gain_grad_ref[...] = jnp.sum(held * root * grad, axis=0, keepdims=True)
        own_ref[...] = own
        low = (own * keep_ref[...]).astype(LOW)
        copies = copies + share(count, low, all_ref, send_all, receive_all)
        yield
        shared(count, all_ref, send_all, receive_all)
        for copy in copies:
            copy.wait_send()

    return Task(
        [partial.reshape(count, rows, width), values, add, keep_row, gain_row],
        [
            struct((rows, width), FULL),
            struct((1, width), FULL),
            struct((count, rows, width), LOW),
        ],
        [pltpu.VMEM((count, rows, width), partial.dtype)]
        + narrow_sems(count)
        + narrow_sems(count),
        steps,
        VMEM,
        VMEM,
        ["narrow"],
    )


def sum_narrow(partial):
    count = lax.axis_size("narrow")
    rows, width = partial.shape[0] // count, partial.shape[1]

    def steps(ins, outs, scratch):
        (parts_ref,), (own_ref,), (slots, send, receive) = ins, outs, scratch
        copies = collect(count, parts_ref, slots, send, receive)
        yield
        yield
        own_ref[...] = collected(count, parts_ref, slots, send, receive)
        for copy in copies:
            copy.wait_send()

    return Task(
        [partial.reshape(count, rows, width)],
        [struct((rows, width), FULL)],
        [pltpu.VMEM((count, rows, width), partial.dtype)] + narrow_sems(count),
        steps,
        VMEM,
        VMEM,
        ["narrow"],
    )


def fetch_rows(found, rows):
    deep, wide = lax.axis_size("narrow"), lax.axis_size("wide")
    columns = found.shape[2]

    def steps(ins, outs, scratch):
        (found_ref,), (out_ref,) = ins, outs
        rightward, leftward, final = scratch[:3]
        send_right, receive_right, send_left, receive_left = scratch[3:7]
        send_wide, receive_wide, local = scratch[7:]
        spot = lax.axis_index("narrow")
        me = lax.axis_index("wide")

        def right_copy(part, source):
            return push(
                source,
                rightward.at[part],
                send_right.at[part],
                receive_right.at[part],
                {"narrow": lax.rem(spot + 1, deep)},
            )

        def left_copy(part, source):
            return push(
                source,
                leftward.at[part],
                send_left.at[part],
                receive_left.at[part],
                {"narrow": lax.rem(spot + deep - 1, deep)},
            )

        for step in range(deep - 1):
            right, left = deep - 1 - step, step

            @pl.when((spot == 0) & (right > 0))
            def _():
                right_copy(right, found_ref.at[right]).start()

            @pl.when((spot == deep - 1) & (left < deep - 1))
            def _():
                left_copy(left, found_ref.at[left]).start()

        yield
        for step in range(deep - 1):
            right, left = deep - 1 - step, step

            def pass_right():
                right_copy(right, rightward.at[right]).wait_recv()
                rightward[right] = rightward[right] + found_ref[right]
                right_copy(right, rightward.at[right]).start()

            pl.when((spot > 0) & (right > spot) & (2 * spot < deep))(pass_right)

            @pl.when((spot < deep - 1) & (left < spot))
            def _():
                left_copy(left, leftward.at[left]).wait_recv()
                leftward[left] = leftward[left] + found_ref[left]
                left_copy(left, leftward.at[left]).start()

            pl.when((right > spot) & (2 * spot >= deep))(pass_right)

        final[...] = found_ref[spot]

        @pl.when(spot > 0)
        def _():
            right_copy(spot, rightward.at[spot]).wait_recv()
            final[...] = final[...] + rightward[spot]

        @pl.when(spot < deep - 1)
        def _():
            left_copy(spot, leftward.at[spot]).wait_recv()
            final[...] = final[...] + leftward[spot]

        def rows_for(device):
            return final.at[pl.ds(pl.multiple_of(device * rows, rows), rows)]

        def columns_from(device):
            return columns_of(columns)(out_ref, device)

        copies = []
        for step in range(1, wide):
            peer = lax.rem(me + step, wide)
            copy = push(
                rows_for(peer),
                columns_from(me),
                send_wide.at[step - 1],
                receive_wide.at[me],
                {"wide": peer},
            )
            copy.start()
            copies.append(copy)
        keep = pltpu.make_async_copy(rows_for(me), columns_from(me), local)
        keep.start()
        yield
        for step in range(1, wide):
            source = lax.rem(me - step + wide, wide)
            arrived(
                columns_from(source), send_wide.at[0], receive_wide.at[source], {"wide": source}
            )
        yield
        for copy in copies:
            copy.wait_send()
        keep.wait()
        for step in range(deep - 1):
            right, left = deep - 1 - step, step

            @pl.when(right > spot)
            def _():
                right_copy(right, found_ref.at[right]).wait_send()

            @pl.when(left < spot)
            def _():
                left_copy(left, found_ref.at[left]).wait_send()

    task = Task(
        [found],
        [struct((rows, wide * columns), found.dtype)],
        [pltpu.VMEM(found.shape, found.dtype)] * 2
        + [pltpu.VMEM(found.shape[1:], found.dtype)]
        + [sems(deep)] * 4
        + [sems(wide - 1), sems(wide), sems()],
        steps,
        VMEM,
        ANY,
        ["narrow", "wide"],
    )
    return task


def return_rows(rows):
    deep, wide = lax.axis_size("narrow"), lax.axis_size("wide")
    count, width = rows.shape
    columns = width // wide

    def steps(ins, outs, scratch):
        (rows_ref,), (out_ref,) = ins, outs
        send_right, send_left, receive_deep, send_wide, receive_wide, local = scratch
        spot = lax.axis_index("narrow")
        me = lax.axis_index("wide")
        part_of = functools.partial(columns_of(columns), rows_ref)

        def landing(device):
            return out_ref.at[spot, pl.ds(pl.multiple_of(device * count, count), count)]

        copies = []
        for step in range(1, wide):
            peer = lax.rem(me + step, wide)
            copy = push(
                part_of(peer),
                landing(me),
                send_wide.at[step - 1],
                receive_wide.at[me],
                {"wide": peer},
            )
            copy.start()
            copies.append(copy)
        keep = pltpu.make_async_copy(part_of(me), landing(me), local)
        keep.start()
        yield
        for step in range(1, wide):
            source = lax.rem(me - step + wide, wide)
            arrived(landing(source), send_wide.at[0], receive_wide.at[source], {"wide": source})
        keep.wait()

        def right_copy(part):
            return push(
                out_ref.at[part],
                out_ref.at[part],
                send_right.at[part],
                receive_deep.at[part],
                {"narrow": lax.rem(spot + 1, deep)},
            )

        def left_copy(part):
            return push(
                out_ref.at[part],
                out_ref.at[part],
                send_left.at[part],
                receive_deep.at[part],
                {"narrow": lax.rem(spot + deep - 1, deep)},
            )

        @pl.when(spot < deep - 1)
        def _():
            right_copy(spot).start()

        @pl.when(spot > 0)
        def _():
            left_copy(spot).start()

        for step in range(1, deep):
            yield

            @pl.when(spot >= step)
            def _():
                right_copy(spot - step).wait_recv()

                @pl.when(spot < deep - 1)
                def _():
                    right_copy(spot - step).start()

            @pl.when(spot + step < deep)
            def _():
                left_copy(spot + step).wait_recv()

                @pl.when(spot > 0)
                def _():
                    left_copy(spot + step).start()

        for part in range(deep):

            @pl.when((part <= spot) & (spot < deep - 1))
            def _():
                right_copy(part).wait_send()

            @pl.when((part >= spot) & (spot > 0))
            def _():
                left_copy(part).wait_send()

        for copy in copies:
            copy.wait_send()

    return Task(
        [rows],
        [struct((deep, wide * count, columns), rows.dtype)],
        [sems(deep)] * 3 + [sems(wide - 1), sems(wide), sems()],
        steps,
        ANY,
        ANY,
        ["narrow", "wide"],
    )


def sum_wide(partial):
    count = lax.axis_size("wide")
    chips = count // 2
    rows, width = partial.shape[0] // count, partial.shape[1]

    def steps(ins, outs, scratch):
        (parts_ref,), (out_ref,) = ins, outs
        from_mate, paired, slots, send_mate, receive_mate, send, receive = scratch
        me = lax.axis_index("wide")
        side = lax.rem(me, 2)
        mate = me + 1 - 2 * side
        my_chip = me // 2
        mate_copies = []
        for step in range(chips):
            chip = lax.rem(my_chip + 1 + step, chips)
            copy = push(
                parts_ref.at[2 * chip + 1 - side],
                from_mate.at[chip],
                send_mate.at[step],
                receive_mate.at[chip],
                {"wide": mate},
            )
            copy.start()
            mate_copies.append(copy)
        yield
        copies = []
        for step in range(chips):
            chip = lax.rem(my_chip + 1 + step, chips)
            arrived(from_mate.at[chip], send_mate.at[0], receive_mate.at[chip], {"wide": mate})
            both = parts_ref[2 * chip + side].astype(FULL) + from_mate[chip].astype(FULL)
            if step < chips - 1:
                paired[chip] = both.astype(LOW)
                copy = push(
                    paired.at[chip],
                    slots.at[my_chip],
                    send.at[step],
                    receive.at[my_chip],
                    {"wide": 2 * chip + side},
                )
                copy.start()
                copies.append(copy)
            else:
                out_ref[...] = both
        yield
        for step in range(1, chips):
            chip = lax.rem(my_chip - step + chips, chips)
            arrived(slots.at[chip], send.at[0], receive.at[chip], {"wide": 2 * chip + side})
            out_ref[...] = out_ref[...] + slots[chip].astype(FULL)
        for copy in mate_copies + copies:
            copy.wait_send()

    return Task(
        [partial.reshape(count, rows, width)],
        [struct((rows, width), FULL)],
        [pltpu.VMEM((chips, rows, width), LOW)] * 3
        + [sems(chips), sems(chips), sems(max(chips - 1, 1)), sems(chips)],
        steps,
        VMEM,
        VMEM,
        ["wide"],
    )


def merge_stats(first, second):
    peak = jnp.maximum(first[0:1], second[0:1])
    total = first[1:2] * jnp.exp(first[0:1] - peak) + second[1:2] * jnp.exp(second[0:1] - peak)
    return jnp.concatenate([peak, total, first[2:3] + second[2:3]], axis=0)


def add_two(first, second):
    return first + second


def combine(values, join):
    deep, wide = lax.axis_size("narrow"), lax.axis_size("wide")

    def steps(ins, outs, scratch):
        (x_ref,), (out_ref,) = ins, outs
        wide_slots, deep_slots, send_wide, receive_wide, send_deep, receive_deep = scratch

        def start(axis, count, slots, value, send, receive):
            me = lax.axis_index(axis)
            slots[me] = value
            copies = []
            for step in range(1, count):
                peer = lax.rem(me + step, count)
                copy = push(
                    slots.at[me], slots.at[me], send.at[step - 1], receive.at[me], {axis: peer}
                )
                copy.start()
                copies.append(copy)
            return copies

        def finish(axis, count, slots, send, receive):
            me = lax.axis_index(axis)
            for step in range(1, count):
                source = lax.rem(me - step + count, count)
                arrived(slots.at[source], send.at[0], receive.at[source], {axis: source})
            total = slots[0]
            for source in range(1, count):
                total = join(total, slots[source])
            return total

        first = start("wide", wide, wide_slots, x_ref[...], send_wide, receive_wide)
        yield
        total = finish("wide", wide, wide_slots, send_wide, receive_wide)
        second = start("narrow", deep, deep_slots, total, send_deep, receive_deep)
        yield
        out_ref[...] = finish("narrow", deep, deep_slots, send_deep, receive_deep)
        for copy in first + second:
            copy.wait_send()

    return Task(
        [values],
        [like(values)],
        [
            pltpu.VMEM((wide,) + values.shape, values.dtype),
            pltpu.VMEM((deep,) + values.shape, values.dtype),
            sems(wide - 1),
            sems(wide),
            sems(deep - 1),
            sems(deep),
        ],
        steps,
        VMEM,
        VMEM,
        ["narrow", "wide"],
    )


def gather_both(values):
    deep, wide = lax.axis_size("narrow"), lax.axis_size("wide")

    def steps(ins, outs, scratch):
        (x_ref,), (out_ref,) = ins, outs
        send_wide, receive_wide, send_deep, receive_deep = scratch
        me = lax.axis_index("wide")
        spot = lax.axis_index("narrow")
        out_ref[spot, me] = x_ref[...]
        copies = []
        for step in range(1, wide):
            peer = lax.rem(me + step, wide)
            block = out_ref.at[spot, me]
            copy = push(block, block, send_wide.at[step - 1], receive_wide.at[me], {"wide": peer})
            copy.start()
            copies.append(copy)
        yield
        for step in range(1, wide):
            source = lax.rem(me - step + wide, wide)
            block = out_ref.at[spot, source]
            arrived(block, send_wide.at[0], receive_wide.at[source], {"wide": source})
        for step in range(1, deep):
            peer = lax.rem(spot + step, deep)
            block = out_ref.at[spot]
            copy = push(
                block, block, send_deep.at[step - 1], receive_deep.at[spot], {"narrow": peer}
            )
            copy.start()
            copies.append(copy)
        yield
        for step in range(1, deep):
            source = lax.rem(spot - step + deep, deep)
            block = out_ref.at[source]
            arrived(block, send_deep.at[0], receive_deep.at[source], {"narrow": source})
        for copy in copies:
            copy.wait_send()

    return Task(
        [values],
        [struct((deep, wide) + values.shape, values.dtype)],
        [sems(wide - 1), sems(wide), sems(deep - 1), sems(deep)],
        steps,
        VMEM,
        VMEM,
        ["narrow", "wide"],
    )


def turn_heads(values, cosine, sine):
    half = values.shape[1] // 2
    swapped = jnp.concatenate([values[:, half:], values[:, :half]], axis=1)
    return values * cosine + swapped * sine


def wide_angles(cosine, sine):
    return jnp.concatenate([cosine, cosine], axis=1), jnp.concatenate([-sine, sine], axis=1)


def local_call(body, inputs, specs, outputs, flops, name):
    return pl.pallas_call(
        body,
        grid=(1,),
        in_specs=specs,
        out_specs=[
            pl.BlockSpec(a.shape, lambda step, rank=len(a.shape): (0,) * rank) for a in outputs
        ],
        out_shape=outputs,
        compiler_params=pltpu.CompilerParams(vmem_limit_bytes=VMEM_BYTES),
        cost_estimate=pl.CostEstimate(flops=flops, bytes_accessed=8 << 20, transcendentals=0),
        name=name,
    )(*inputs)


def entire(values):
    return pl.BlockSpec(values.shape, lambda step: (0,) * values.ndim)


def column_block(values, size, index):
    return pl.BlockSpec((values.shape[0], size), lambda step: (0, index))


def heads_body(groups, rep, rows_ref, gain_ref, kv_ref, cos_ref, sin_ref, out_ref, normed_ref):
    count, _, _, tok_rows, head = out_ref.shape
    size = kv_ref.shape[1] // (2 * count)
    per_head = head // size
    rows = rows_ref[0:tok_rows, :].astype(FULL)
    normed = norm_rows(rows, gain_ref[...]).astype(LOW)
    normed_ref[...] = normed
    both = dot(normed, kv_ref[...], 1, 0)

    def head_of(kind, index):
        pieces = [
            both[:, (2 * part + kind) * size : (2 * part + kind + 1) * size]
            for part in range(index * per_head, (index + 1) * per_head)
        ]
        return pieces[0] if per_head == 1 else jnp.concatenate(pieces, axis=1)

    for owner in range(count):
        for group in range(groups):
            index = (owner * groups + group) // rep
            keys = turn_heads(head_of(0, index), cos_ref[...], sin_ref[...])
            out_ref[owner, group, 0] = keys.astype(LOW)
            out_ref[owner, group, 1] = head_of(1, index).astype(LOW)


def make_heads(rows_low, gain_row, proj, cosine, sine, groups, rep):
    count = lax.axis_size("narrow")
    tok_rows, head = cosine.shape
    width = rows_low.shape[1]
    size = 2 * KVH * HD
    return local_call(
        functools.partial(heads_body, groups, rep),
        [rows_low, gain_row, proj, cosine, sine],
        [entire(rows_low), entire(gain_row), column_block(proj, size, 0)]
        + [entire(cosine), entire(sine)],
        [struct((count, groups, 2, tok_rows, head), LOW), struct((tok_rows, width), LOW)],
        2 * tok_rows * width * size,
        "make_heads",
    )


def attend_body(
    start_ref,
    gains_ref,
    q_ref,
    o_ref,
    kv_ref,
    cos_ref,
    sin_ref,
    seg_ref,
    seg_all_ref,
    pick_ref,
    queries_ref,
    probs_ref,
    mixed_ref,
    part_ref,
    normed_ref,
    early_ref,
):
    count, groups, _, tok_rows, head = kv_ref.shape
    heads_own = probs_ref.shape[0]
    start = start_ref[...].astype(FULL)
    root = lax.rsqrt(jnp.mean(start * start, axis=-1, keepdims=True) + NORM_EPS)
    normed = (start * root * gains_ref[0:1, :]).astype(LOW)
    normed_ref[...] = normed
    early_ref[...] = (start * root * gains_ref[2:3, :]).astype(LOW)
    queries = dot(normed, q_ref[...], 1, 0)
    spots = lax.broadcasted_iota(jnp.int32, (1, count * tok_rows), 1)
    allowed = (seg_ref[...] == seg_all_ref[...]) & (pick_ref[...] >= spots)
    for group in range(groups):
        keys = jnp.concatenate([kv_ref[part, group, 0] for part in range(count)], axis=0)
        values = jnp.concatenate([kv_ref[part, group, 1] for part in range(count)], axis=0)
        for member in range(heads_own // groups):
            at = group * (heads_own // groups) + member
            spot = slice(at * head, (at + 1) * head)
            query = turn_heads(queries[:, spot], cos_ref[...], sin_ref[...]).astype(LOW)
            queries_ref[:, spot] = query
            scores = jnp.where(allowed, dot(query, keys, 1, 1) * head ** (-0.5), MASKED)
            shifted = jnp.exp(scores - jnp.max(scores, axis=-1, keepdims=True))
            probs = shifted / jnp.sum(shifted, axis=-1, keepdims=True)
            probs_ref[at] = probs
            mixed_ref[:, spot] = dot(probs.astype(LOW), values, 1, 0).astype(LOW)
    part_ref[...] = dot(mixed_ref[...], o_ref[...], 1, 1).astype(LOW)


def attend(start_low, gains, proj, own_head, cosine, sine, seg, seg_all, picks):
    count, groups, _, tok_rows, head = own_head.shape
    sel, width = start_low.shape
    heads_own = HEADS // count
    size = heads_own * head
    first = 2 * KVH * HD // size
    seq_len = count * tok_rows
    return local_call(
        attend_body,
        [start_low, gains, proj, proj, own_head, cosine, sine, seg, seg_all, picks],
        [
            entire(start_low),
            entire(gains),
            column_block(proj, size, first),
            column_block(proj, size, first + 1),
        ]
        + [entire(a) for a in (own_head, cosine, sine, seg, seg_all, picks)],
        [
            struct((sel, size), LOW),
            struct((heads_own, sel, seq_len), FULL),
            struct((sel, size), LOW),
            struct((sel, width), LOW),
            struct((sel, width), LOW),
            struct((sel, width), LOW),
        ],
        4 * sel * size * (width + seq_len),
        "attend",
    )


def attend_back_body(
    grad_ref,
    q_ref,
    o_ref,
    kv_ref,
    queries_ref,
    probs_ref,
    cos_ref,
    sin_ref,
    cos_all_ref,
    sin_all_ref,
    out_ref,
    grad_q_ref,
    part_ref,
):
    count, groups, _, tok_rows, head = kv_ref.shape
    heads_own = probs_ref.shape[0]
    scale = head ** (-0.5)
    grad_mixed = dot(grad_ref[...], o_ref[...], 1, 0).astype(LOW)
    for group in range(groups):
        keys = jnp.concatenate([kv_ref[part, group, 0] for part in range(count)], axis=0)
        values = jnp.concatenate([kv_ref[part, group, 1] for part in range(count)], axis=0)
        grad_keys = jnp.zeros(keys.shape, FULL)
        grad_values = jnp.zeros(keys.shape, FULL)
        for member in range(heads_own // groups):
            at = group * (heads_own // groups) + member
            spot = slice(at * head, (at + 1) * head)
            probs = probs_ref[at]
            grad_probs = dot(grad_mixed[:, spot], values, 1, 1)
            inner = jnp.sum(probs * grad_probs, axis=-1, keepdims=True)
            grad_scores = (probs * (grad_probs - inner)).astype(LOW)
            grad_query = dot(grad_scores, keys, 1, 0) * scale
            grad_q_ref[:, spot] = turn_heads(grad_query, cos_ref[...], -sin_ref[...]).astype(LOW)
            grad_keys = grad_keys + dot(grad_scores, queries_ref[:, spot], 0, 0)
            grad_values = grad_values + dot(probs.astype(LOW), grad_mixed[:, spot], 0, 0)
        grad_keys = turn_heads(grad_keys * scale, cos_all_ref[...], -sin_all_ref[...])
        for part in range(count):
            rows = slice(part * tok_rows, (part + 1) * tok_rows)
            out_ref[part, group, 0] = grad_keys[rows].astype(LOW)
            out_ref[part, group, 1] = grad_values[rows].astype(LOW)
    part_ref[...] = dot(grad_q_ref[...], q_ref[...], 1, 1).astype(LOW)


def attend_back(grad, proj, own_head, queries, probs, cosine, sine, cosine_all, sine_all):
    count, groups, _, tok_rows, head = own_head.shape
    sel, width = grad.shape
    size = queries.shape[1]
    first = 2 * KVH * HD // size
    return local_call(
        attend_back_body,
        [grad, proj, proj, own_head, queries, probs, cosine, sine, cosine_all, sine_all],
        [entire(grad), column_block(proj, size, first), column_block(proj, size, first + 1)]
        + [
            entire(a)
            for a in (own_head, queries, probs, cosine, sine, cosine_all, sine_all)
        ],
        [struct(own_head.shape, LOW), struct((sel, size), LOW), struct((sel, width), LOW)],
        8 * sel * size * width,
        "attend_back",
    )


def norm_back_rows(values, gain_row, grad):
    root = lax.rsqrt(jnp.mean(values * values, axis=-1, keepdims=True) + NORM_EPS)
    scaled = gain_row * grad
    inner = jnp.mean(values * scaled, axis=-1, keepdims=True)
    result = root * scaled - values * (root * root * root * inner)
    return result, jnp.sum(values * root * grad, axis=0, keepdims=True)


def rows_back_body(
    rep,
    rows_ref,
    gains_ref,
    kv_ref,
    heads_ref,
    pick_ref,
    early_ref,
    base_ref,
    out_ref,
    attn_gain_ref,
    early_gain_ref,
    grad_kv_ref,
):
    count, groups, _, tok_rows, head = heads_ref.shape
    size = kv_ref.shape[1] // (2 * count)
    per_head = head // size
    for index in range(KVH):
        for kind in range(2):
            copies = [
                heads_ref[at // groups, at % groups, kind]
                for at in range(index * rep, (index + 1) * rep)
            ]
            total = copies[0]
            if rep > 1:
                total = sum(copy.astype(FULL) for copy in copies).astype(LOW)
            for piece in range(per_head):
                lane = (2 * (index * per_head + piece) + kind) * size
                grad_kv_ref[:, lane : lane + size] = total[:, piece * size : (piece + 1) * size]
    values = rows_ref[...].astype(FULL)
    own = values[tok_rows:]
    tok_part, tok_gain = norm_back_rows(
        values[:tok_rows], gains_ref[0:1, :], dot(grad_kv_ref[...], kv_ref[...], 1, 1)
    )
    pick_part, pick_gain = norm_back_rows(own, gains_ref[0:1, :], pick_ref[...])
    early_part, early_gain = norm_back_rows(own, gains_ref[2:3, :], early_ref[...])
    attn_gain_ref[...] = tok_gain + pick_gain
    early_gain_ref[...] = early_gain
    out_ref[0:tok_rows, :] = tok_part.astype(LOW)
    out_ref[tok_rows:, :] = (pick_part + early_part + base_ref[...]).astype(LOW)


def rows_back(rows_low, gains, proj, heads, grad_pick, grad_early, base, rep):
    tok_rows = heads.shape[3]
    width = rows_low.shape[1]
    size = 2 * KVH * HD
    return local_call(
        functools.partial(rows_back_body, rep),
        [rows_low, gains, proj, heads, grad_pick, grad_early, base],
        [entire(rows_low), entire(gains), column_block(proj, size, 0)]
        + [entire(a) for a in (heads, grad_pick, grad_early, base)],
        [
            struct(rows_low.shape, LOW),
            struct((1, width), FULL),
            struct((1, width), FULL),
            struct((tok_rows, size), LOW),
        ],
        2 * tok_rows * width * size,
        "rows_back",
    )


def assemble_body(out_columns, *refs):
    pieces, out_ref = refs[:-1], refs[-1]
    count = len(pieces)
    me = lax.axis_index("narrow")
    for step, piece in enumerate(pieces):
        source = lax.rem(me - step + count, count)
        spot = pl.ds(pl.multiple_of(source * out_columns, out_columns), out_columns)
        out_ref[:, spot] = piece[...]


def assemble(pieces):
    rows, columns = pieces[0].shape
    outputs = [struct((rows, columns * len(pieces)), pieces[0].dtype)]
    return local_call(
        functools.partial(assemble_body, columns),
        list(pieces),
        [entire(piece) for piece in pieces],
        outputs,
        0,
        "assemble",
    )[0]


def feed_body(inner_ref, weight_ref, gate_ref, up_ref, hidden_ref, out_ref, total):
    part = pl.program_id(0)
    inner = inner_ref[...]
    gate = dot(inner, weight_ref[0, 0], 1, 1)
    up = dot(inner, weight_ref[0, 1], 1, 1)
    hidden = (jax.nn.silu(gate) * up).astype(LOW)
    gate_ref[0] = gate
    up_ref[0] = up
    hidden_ref[0] = hidden
    product = dot(hidden, weight_ref[0, 2], 1, 0)

    @pl.when(part == 0)
    def _():
        total[...] = product

    @pl.when(part > 0)
    def _():
        total[...] = total[...] + product

    @pl.when(part == pl.num_programs(0) - 1)
    def _():
        out_ref[...] = total[...].astype(LOW)


def feed(inner, weight):
    parts, _, size, width = weight.shape
    sel = inner.shape[0]
    same = pl.BlockSpec((sel, width), lambda part: (0, 0))
    slab = pl.BlockSpec((1, sel, size), lambda part: (part, 0, 0))
    return pl.pallas_call(
        feed_body,
        grid=(parts,),
        in_specs=[same, pl.BlockSpec((1, 3, size, width), lambda part: (part, 0, 0, 0))],
        out_specs=[slab, slab, slab, same],
        out_shape=[
            struct((parts, sel, size), FULL),
            struct((parts, sel, size), FULL),
            struct((parts, sel, size), LOW),
            struct((sel, width), LOW),
        ],
        scratch_shapes=[pltpu.VMEM((sel, width), FULL)],
        compiler_params=pltpu.CompilerParams(vmem_limit_bytes=VMEM_BYTES),
        cost_estimate=pl.CostEstimate(
            flops=6 * sel * parts * size * width,
            bytes_accessed=weight.size * 2,
            transcendentals=0,
        ),
        name="feed",
    )(inner, weight)


def feed_back_body(grad_ref, weight_ref, gate_ref, up_ref, hidden_ref, acts_ref, out_ref, total):
    part = pl.program_id(0)
    grad_hidden = dot(grad_ref[...], weight_ref[0, 2], 1, 1)
    gate = gate_ref[0]
    sigma = jax.nn.sigmoid(gate)
    grad_gate = (grad_hidden * up_ref[0] * sigma * (1.0 + gate * (1.0 - sigma))).astype(LOW)
    grad_up = (grad_hidden * gate * sigma).astype(LOW)
    acts_ref[0, 0] = grad_gate
    acts_ref[0, 1] = grad_up
    acts_ref[0, 2] = hidden_ref[0]
    product = dot(grad_gate, weight_ref[0, 0], 1, 0) + dot(grad_up, weight_ref[0, 1], 1, 0)

    @pl.when(part == 0)
    def _():
        total[...] = product

    @pl.when(part > 0)
    def _():
        total[...] = total[...] + product

    @pl.when(part == pl.num_programs(0) - 1)
    def _():
        out_ref[...] = total[...].astype(LOW)


def feed_back(grad, weight, gate, up, hidden):
    parts, _, size, width = weight.shape
    sel = grad.shape[0]
    same = pl.BlockSpec((sel, width), lambda part: (0, 0))
    slab = pl.BlockSpec((1, sel, size), lambda part: (part, 0, 0))
    return pl.pallas_call(
        feed_back_body,
        grid=(parts,),
        in_specs=[same, pl.BlockSpec((1, 3, size, width), lambda part: (part, 0, 0, 0))]
        + [slab] * 3,
        out_specs=[pl.BlockSpec((1, 3, sel, size), lambda part: (part, 0, 0, 0)), same],
        out_shape=[struct((parts, 3, sel, size), LOW), struct((sel, width), LOW)],
        scratch_shapes=[pltpu.VMEM((sel, width), FULL)],
        compiler_params=pltpu.CompilerParams(vmem_limit_bytes=VMEM_BYTES),
        cost_estimate=pl.CostEstimate(
            flops=6 * sel * parts * size * width,
            bytes_accessed=weight.size * 2,
            transcendentals=0,
        ),
        name="feed_back",
    )(grad, weight, gate, up, hidden)


def newton_steps(problems):
    rows, width = problems[0][0].shape
    block = min(512, width)
    eye = lax.broadcasted_iota(jnp.int32, (rows, rows), 0) == lax.broadcasted_iota(
        jnp.int32, (rows, rows), 1
    )

    def strip(part):
        return pl.ds(pl.multiple_of(part * block, block), block)

    def over(function, start):
        return lax.fori_loop(0, width // block, function, start)

    def add_squares(part, totals):
        values = [current[:, strip(part)] for current, low, gram, rest in problems]
        return [total + jnp.sum(value * value) for total, value in zip(totals, values)]

    totals = over(add_squares, [jnp.float32(0.0)] * len(problems))
    scales = [1.0 / (jnp.sqrt(total) + 1e-07) for total in totals]

    def begin(part, carry):
        for scale, (current, low, gram, rest) in zip(scales, problems):
            values = current[:, strip(part)] * scale
            current[:, strip(part)] = values
            low[:, strip(part)] = values.astype(LOW)
        return carry

    over(begin, 0)

    def iteration(turn, carry):
        for current, low, gram, rest in problems:
            gram[...] = jnp.zeros_like(gram)

        def add_gram(part, carry):
            for current, low, gram, rest in problems:
                values = low[:, strip(part)]
                gram[...] = gram[...] + dot(values, values, 1, 1)
            return carry

        over(add_gram, 0)
        seconds = []
        for current, low, gram, rest in problems:
            whole = gram[...]
            middle = jnp.sum(jnp.where(eye, whole, 0.0)) / rows
            rest[...] = (whole - jnp.where(eye, middle, 0.0)).astype(LOW)
            square = dot(rest[...], rest[...], 1, 0)
            whole = gram[...]
            centred = whole - jnp.where(eye, middle, 0.0)
            square = square + 2.0 * middle * centred + jnp.where(eye, middle * middle, 0.0)
            whole = NEWTON_B * whole + NEWTON_C * square
            second = jnp.sum(jnp.where(eye, whole, 0.0)) / rows
            rest[...] = (whole - jnp.where(eye, second, 0.0)).astype(LOW)
            seconds.append(second)

        def apply(part, carry):
            for second, (current, low, gram, rest) in zip(seconds, problems):
                values = (NEWTON_A + second) * current[:, strip(part)] + dot(
                    rest[...], low[:, strip(part)], 1, 0
                )
                current[:, strip(part)] = values
                low[:, strip(part)] = values.astype(LOW)
            return carry

        over(apply, 0)
        return carry

    lax.fori_loop(0, NS_STEPS, iteration, 0)


def newton_scratch(rows, width):
    return [
        pltpu.VMEM((rows, width), FULL),
        pltpu.VMEM((rows, width), LOW),
        pltpu.VMEM((rows, rows), FULL),
        pltpu.VMEM((rows, rows), LOW),
    ]


def newton_cost(count, rows, width):
    return pl.CostEstimate(
        flops=NS_STEPS * count * (4 * rows * rows * width + 2 * rows * rows * rows),
        bytes_accessed=6 * count * rows * width,
        transcendentals=0,
    )


def newton_body(factor_ref, mom_ref, grad_ref, out_ref, *problem):
    current, low = problem[:2]
    parts, rows, columns = mom_ref.shape
    factor = factor_ref[0]
    for part in range(parts):
        spot = slice(part * columns, (part + 1) * columns)
        current[:, spot] = MOMENTUM * mom_ref[part].astype(FULL) + factor * grad_ref[
            :, spot
        ].astype(FULL)
    newton_steps([problem])
    for part in range(parts):
        out_ref[part] = low[:, part * columns : (part + 1) * columns]


def newton_small_body(rows, factor_ref, mom_ref, grad_ref, kv_ref, out_ref, *scratch):
    problems = [scratch[4 * at : 4 * at + 4] for at in range(4)]
    parts, _, columns = mom_ref.shape
    kv_columns = kv_ref.shape[2]
    half = rows // 2
    factor = factor_ref[0]
    for part in range(parts):
        spot = slice(part * columns, (part + 1) * columns)
        for member in range(2):
            current = problems[member][0]
            here = slice(member * rows, (member + 1) * rows)
            mom, grad = mom_ref[part, here, :], grad_ref[part, here, :]
            current[:, spot] = MOMENTUM * mom.astype(FULL) + factor * grad.astype(FULL)
        spot = slice(part * kv_columns, (part + 1) * kv_columns)
        for member in range(2):
            current = problems[2 + member][0]
            piece = kv_ref[part, member * rows : (member + 1) * rows, :].astype(FULL)
            for side in range(2):
                lane = (2 * member + side) * kv_columns
                mom = mom_ref[part, 2 * rows : 2 * rows + half, lane : lane + kv_columns]
                here = slice(side * half, (side + 1) * half)
                current[here, spot] = MOMENTUM * mom.astype(FULL) + factor * piece[here]
    newton_steps(problems[:2])
    newton_steps(problems[2:])
    out_ref[...] = jnp.zeros_like(out_ref)
    for part in range(parts):
        for member in range(2):
            out_ref[part, member * rows : (member + 1) * rows, :] = problems[member][1][
                :, part * columns : (part + 1) * columns
            ]
            low = problems[2 + member][1]
            for side in range(2):
                lane = (2 * member + side) * kv_columns
                out_ref[part, 2 * rows : 2 * rows + half, lane : lane + kv_columns] = low[
                    side * half : (side + 1) * half,
                    part * kv_columns : (part + 1) * kv_columns,
                ]


def newton_any_body(rows, factor_ref, mom_ref, grad_ref, qo_ref, kv_ref, out_ref, *scratch):
    parts = mom_ref.shape[0]
    owner = lax.rem(3 + lax.rem(lax.axis_index("wide"), 2), parts)
    small = lax.axis_index("narrow") == owner

    @pl.when(small)
    def _():
        newton_small_body(rows, factor_ref, mom_ref, qo_ref, kv_ref, out_ref, *scratch[4:])

    @pl.when(jnp.logical_not(small))
    def _():
        newton_body(factor_ref, mom_ref, grad_ref, out_ref, *scratch[:4])


def newton(factor, mom, grad, qo_grad, kv_grad):
    parts, slot_rows, columns = mom.shape
    width = parts * columns
    rows = kv_grad.shape[1] // 2
    kv_width = parts * kv_grad.shape[2]
    return pl.pallas_call(
        functools.partial(newton_any_body, rows),
        in_specs=[pl.BlockSpec(memory_space=pltpu.SMEM)] + [VMEM] * 4,
        out_specs=VMEM,
        out_shape=struct(mom.shape, LOW),
        scratch_shapes=newton_scratch(slot_rows, width)
        + newton_scratch(rows, width) * 2
        + newton_scratch(rows, kv_width) * 2,
        compiler_params=pltpu.CompilerParams(vmem_limit_bytes=VMEM_BYTES),
        cost_estimate=newton_cost(1, slot_rows, width),
        name="newton",
    )(factor.reshape(1), mom, grad, qo_grad, kv_grad)


def lookup_body(ids_ref, turn_ref, table_ref, out_ref, low_ref, list_ref, held, rows, sem):
    vocab = table_ref.shape[0]
    count = out_ref.shape[0]
    load = pltpu.make_async_copy(table_ref, held, sem)
    load.start()
    rows[...] = jnp.zeros_like(rows)

    found = turn_ref[count]

    def note(group, carry):
        for member in range(UNROLL):
            at = group * UNROLL + member
            list_ref[turn_ref[at]] = at
        return carry

    lax.fori_loop(0, count // UNROLL, note, 0)
    for member in range(UNROLL):
        list_ref[found + member] = count
    list_ref[count + UNROLL] = found
    load.wait()

    def step(group, carry):
        for member in range(UNROLL):
            at = list_ref[group * UNROLL + member]
            spot = jnp.minimum(ids_ref[jnp.minimum(at, count - 1)], vocab - 1)
            rows[pl.ds(at, 1), :] = held[pl.ds(spot, 1), :]
        return carry

    lax.fori_loop(0, (found + UNROLL - 1) // UNROLL, step, 0)
    out_ref[...] = rows[pl.ds(0, count), :].astype(LOW)
    low_ref[...] = held[...].astype(LOW)


def lookup(table, ids):
    vocab, columns = table.shape
    count = ids.shape[0]
    mine = (ids < vocab).reshape(-1, 128)
    before = jnp.arange(128)[:, None] < jnp.arange(128)[None, :]
    in_row = dot(mine.astype(LOW), before.astype(LOW), 1, 0)
    per_row = jnp.sum(mine.astype(FULL), axis=1)
    lines = jnp.arange(mine.shape[0])
    ahead = jnp.sum(jnp.where(lines[:, None] > lines[None, :], per_row[None, :], 0.0), axis=1)
    found = jnp.sum(per_row).astype(jnp.int32)
    turns = (in_row + ahead[:, None]).astype(jnp.int32)
    turns = jnp.where(mine, turns, count + UNROLL + 1).reshape(-1)
    turns = jnp.concatenate([turns, jnp.full((128,), found)])
    return pl.pallas_call(
        lookup_body,
        in_specs=[pl.BlockSpec(memory_space=pltpu.SMEM)] * 2 + [ANY],
        out_specs=[VMEM, VMEM, pl.BlockSpec(memory_space=pltpu.SMEM)],
        scratch_shapes=[
            pltpu.VMEM((vocab, columns), FULL),
            pltpu.VMEM((count + 8, columns), FULL),
            pltpu.SemaphoreType.DMA,
        ],
        out_shape=[
            struct((count, columns), LOW),
            struct((vocab, columns), LOW),
            struct((count + 2 * UNROLL,), jnp.int32),
        ],
        compiler_params=pltpu.CompilerParams(vmem_limit_bytes=VMEM_BYTES),
        cost_estimate=pl.CostEstimate(
            flops=0, bytes_accessed=vocab * columns * 4, transcendentals=0
        ),
        name="lookup",
    )(ids, turns, table)


def spread_body(
    ids_ref, list_ref, rows_ref, head_ref, out_ref, square_ref, even, odd, rows, sem
):
    vocab = out_ref.shape[0]
    count = rows_ref.shape[0]
    chunk = 256

    def strip(part):
        return pl.ds(pl.multiple_of(part * chunk, chunk), chunk)

    def begin(part, carry):
        even[strip(part), :] = head_ref[strip(part), :].astype(FULL)
        odd[strip(part), :] = jnp.zeros((chunk, odd.shape[1]), FULL)
        return carry

    lax.fori_loop(0, vocab // chunk, begin, 0)

    def widen(part, carry):
        rows[strip(part), :] = rows_ref[strip(part), :].astype(FULL)
        return carry

    lax.fori_loop(0, count // chunk, widen, 0)
    rows[pl.ds(count, 8), :] = jnp.zeros((8, rows.shape[1]), FULL)

    def step(group, carry):
        for member in range(UNROLL):
            at = list_ref[group * UNROLL + member]
            spot = jnp.minimum(ids_ref[jnp.minimum(at, count - 1)], vocab - 1)
            total = even if member % 2 == 0 else odd
            total[pl.ds(spot, 1), :] = total[pl.ds(spot, 1), :] + rows[pl.ds(at, 1), :]
        return carry

    found = list_ref[count + UNROLL]
    lax.fori_loop(0, (found + UNROLL - 1) // UNROLL, step, 0)

    def finish(part, squares):
        value = even[strip(part), :] + odd[strip(part), :]
        even[strip(part), :] = value
        return squares + jnp.sum((value * value).reshape(chunk // 8, 8, -1), axis=0)

    square_ref[...] = lax.fori_loop(
        0, vocab // chunk, finish, jnp.zeros((8, even.shape[1]), FULL)
    )
    store = pltpu.make_async_copy(even, out_ref, sem)
    store.start()
    store.wait()


def spread(ids, listed, rows, head):
    vocab, columns = head.shape
    count = ids.shape[0]
    smem = pl.BlockSpec(memory_space=pltpu.SMEM)
    return pl.pallas_call(
        spread_body,
        in_specs=[smem, smem, VMEM, VMEM],
        out_specs=[ANY, VMEM],
        scratch_shapes=[
            pltpu.VMEM((vocab, columns), FULL),
            pltpu.VMEM((vocab, columns), FULL),
            pltpu.VMEM((count + 8, columns), FULL),
            pltpu.SemaphoreType.DMA,
        ],
        out_shape=[struct((vocab, columns), FULL), struct((8, columns), FULL)],
        compiler_params=pltpu.CompilerParams(vmem_limit_bytes=VMEM_BYTES),
        cost_estimate=pl.CostEstimate(
            flops=count * columns, bytes_accessed=vocab * columns * 8, transcendentals=0
        ),
        name="spread",
    )(ids, listed, rows, head)


def adamw(weight, first_m, second_m, grad, rate, decay):
    first_new = BETA_ONE * first_m + (1.0 - BETA_ONE) * grad
    second_new = BETA_TWO * second_m + (1.0 - BETA_TWO) * grad * grad
    update = (
        first_new
        / (1.0 - BETA_ONE**STEP)
        / (jnp.sqrt(second_new / (1.0 - BETA_TWO**STEP)) + ADAM_EPS)
    )
    return (weight * (1.0 - rate * decay) - rate * update, first_new, second_new)


def cut_columns(values, count):
    rows, columns = values.shape
    return jnp.moveaxis(values.reshape(rows, count, columns // count), 1, 0)


def shifted(parts, axis, step):
    count = lax.axis_size(axis)
    pairs = [(source, (source + step) % count) for source in range(count)]
    return lax.ppermute(parts, axis, pairs)


def per_device(
    tokens,
    picks,
    targets,
    lengths,
    skip,
    embed,
    embed_m,
    embed_v,
    attn_qo,
    attn_qo_mom,
    attn_kv,
    attn_kv_mom,
    ffn,
    ffn_mom,
    gains,
    gains_m,
    gains_v,
):
    wide_count = lax.axis_size("wide")
    narrow_count = lax.axis_size("narrow")
    narrow_spot = lax.axis_index("narrow")
    wide_spot = lax.axis_index("wide")
    seq_len = tokens.shape[1]
    sel = picks.shape[1]
    vocab_rows, columns = embed.shape
    width = columns * wide_count
    own_rows = sel // narrow_count
    tok_rows = seq_len // narrow_count
    all_rows = own_rows + tok_rows
    heads_own = HEADS // narrow_count
    head_cols = heads_own * HD
    repeat = max(1, narrow_count // KVH)
    groups = KVH * repeat // narrow_count
    ffn_rows = ffn.shape[0]
    ffn_size = ffn_rows // narrow_count
    total_rows = wide_count * sel
    lens = lengths[0]
    pick_ids = picks[0]
    keep_layer = (1 - skip[0]).astype(FULL)
    keep_row = jnp.full((1, width), keep_layer)
    lanes = 128

    def box(flat):
        height = -(-flat.shape[0] // (8 * lanes)) * 8
        return jnp.pad(flat, (0, height * lanes - flat.shape[0])).reshape(height, lanes)

    ffn_low = jnp.moveaxis(ffn, 1, 0).astype(LOW)
    ffn_cut = ffn_low.reshape(3, narrow_count, ffn_size, ffn_low.shape[2])
    ffn_cut = jnp.moveaxis(ffn_cut, 1, 0).reshape(narrow_count, 3 * ffn_size, -1)
    kv_own = attn_kv.reshape(columns, -1).astype(LOW)

    where_at = jnp.arange(seq_len, dtype=jnp.int32)
    pick_tokens = jnp.sum(
        jnp.where(pick_ids[:, None] == where_at[None, :], tokens[0][None, :], 0), axis=1
    )
    ints = box(jnp.concatenate([tokens[0], pick_tokens, targets[0]]))
    all_ints, all_gains, kv_part = launch(
        [
            gather_wide(ints),
            gather_both(box(gains.astype(LOW).astype(FULL).reshape(-1))),
            gather_blocks("narrow", kv_own),
        ],
        0,
        "gather_ids",
    )
    kv_part = jnp.moveaxis(kv_part, 0, 1).reshape(columns, -1)
    proj_own = jnp.concatenate([kv_part, attn_qo.reshape(columns, -1).astype(LOW)], axis=1)
    proj = lax.all_gather(proj_own, "wide", axis=0, tiled=True)
    ffn_cut, all_ints = lax.optimization_barrier((ffn_cut, all_ints))
    ffn_pieces = [lax.dynamic_index_in_dim(ffn_cut, narrow_spot, 0, False)] + [
        shifted(
            lax.dynamic_index_in_dim(
                ffn_cut, lax.rem(narrow_spot + step, narrow_count), 0, False
            ),
            "narrow",
            step,
        )
        for step in range(1, narrow_count)
    ]
    gain_size = gains.shape[1]
    gain_w = all_gains.reshape(narrow_count, wide_count, -1)[:, :, : 3 * gain_size]
    gain_w = gain_w.reshape(narrow_count, wide_count, 3, gain_size)
    gain_w = jnp.transpose(gain_w, (2, 1, 0, 3)).reshape(3, width)
    all_ints = all_ints.reshape(wide_count, -1)
    tokens_all = all_ints[:, :seq_len].reshape(wide_count, narrow_count, tok_rows)
    picked_all = all_ints[:, seq_len : seq_len + sel].reshape(wide_count, narrow_count, own_rows)
    targets_all = all_ints[:, seq_len + sel : seq_len + 2 * sel].reshape(-1)
    wanted = jnp.moveaxis(jnp.concatenate([tokens_all, picked_all], axis=2), 1, 0).reshape(-1)
    local_ids = wanted - narrow_spot * vocab_rows
    inside = (local_ids >= 0) & (local_ids < vocab_rows)
    spots = jnp.where(inside, local_ids, vocab_rows)
    found, embed_low, listed = lookup(embed, spots)
    ffn_pieces, found = lax.optimization_barrier((ffn_pieces, found))
    ffn_sub = assemble(ffn_pieces).reshape(3, ffn_size, width)
    ffn_sub, found = lax.optimization_barrier((ffn_sub, found))
    ffn_w = lax.all_gather(ffn_sub, "wide", axis=0)
    found = found.reshape(narrow_count, wide_count * all_rows, columns)
    embed_cut = embed_low.reshape(wide_count, vocab_rows // wide_count, columns)
    table_half = embed_cut.shape[1] // 2
    rows_low = launch([fetch_rows(found, all_rows)], 1, "fetch_rows")[0]

    mom_qo = jnp.moveaxis(attn_qo_mom, 1, 0)
    mom_kv = jnp.moveaxis(attn_kv_mom, 1, 0)
    mom_ffn = jnp.moveaxis(ffn_mom, 1, 0)
    slot_rows, slot_cols = mom_ffn.shape[1:]

    block_rows, q_size = mom_qo.shape[1:]
    kv_size = mom_kv.shape[2]
    half_rows = block_rows // 2
    kv_box = jnp.moveaxis(mom_kv.reshape(4, half_rows, kv_size), 0, 1).reshape(half_rows, -1)
    small_box = jnp.concatenate([mom_qo.reshape(2 * block_rows, q_size), kv_box])
    small_box = jnp.pad(small_box, ((0, slot_rows - small_box.shape[0]), (0, 0)))
    mom_parts = jnp.concatenate([mom_ffn, small_box[None]]).astype(LOW)

    seg_all, cosine_all, sine_all = angles_at(lens, where_at)
    cosine_all, sine_all = wide_angles(cosine_all, sine_all)
    seg_mine, cosine, sine = angles_at(lens, pick_ids)
    cosine, sine = wide_angles(cosine, sine)

    def tok_part(angles):
        return lax.dynamic_slice_in_dim(angles, narrow_spot * tok_rows, tok_rows, 0)

    by_head, normed_tok = make_heads(
        rows_low, gain_w[0:1], proj, tok_part(cosine_all), tok_part(sine_all), groups, repeat
    )
    own_head, start_low, tok_cols, table_low = launch(
        [
            swap_blocks("narrow", by_head),
            gather_blocks("narrow", rows_low[tok_rows:]),
            split_columns("wide", normed_tok),
            join_columns("wide", embed_cut[:, table_half:]),
        ],
        2,
        "trade_heads",
    )
    start_low, ffn_w = lax.optimization_barrier((start_low, ffn_w))
    start_low = start_low.reshape(sel, width)
    queries, probs, mixed, attn_part, normed, early_part = attend(
        start_low,
        gain_w,
        proj,
        own_head,
        cosine,
        sine,
        seg_mine[:, None],
        seg_all[None, :],
        pick_ids[:, None],
    )
    early = lax.all_gather(early_part, "wide", axis=0, tiled=True)
    start_own = rows_low[tok_rows:].astype(FULL)
    middle, inner, mixed_wide, pick_cols = launch(
        [
            settle(
                attn_part,
                start_own,
                start_own,
                jnp.ones((1, width), FULL),
                gain_w[1:2],
            ),
            gather_wide(mixed),
            split_columns("wide", normed),
        ],
        3,
        "settle_middle",
    )
    inner = inner.reshape(sel, width)
    gate, up, hidden, fed = feed(inner, ffn_w)
    final_own, late_part, table_top = launch(
        [
            settle(fed, middle, start_own, keep_row, gain_w[2:3]),
            join_columns("wide", embed_cut[:, :table_half]),
        ],
        4,
        "settle_late",
    )
    table_own = jnp.concatenate([table_top, table_low])

    table_count = table_own.shape[0]
    local_target = targets_all - (narrow_spot * vocab_rows + wide_spot * table_count)
    has_target = local_target[:, None] == jnp.arange(table_count, dtype=jnp.int32)[None, :]
    counted = (targets_all >= 0).astype(FULL)
    loss_count = jnp.sum(counted)

    def exit_logits(features):
        logits = dot(features, table_own, 1, 1)
        peak = jnp.max(logits, axis=-1)
        total = jnp.sum(jnp.exp(logits - peak[:, None]), axis=-1)
        picked = jnp.sum(jnp.where(has_target, logits, 0.0), axis=-1)
        return logits, jnp.stack([peak, total, picked])

    half = slot_rows // 2
    late, mom_top = launch(
        [
            gather_wide(late_part.reshape(sel, width)),
            swap_turned(mom_parts[:, :half]),
        ],
        5,
        "gather_late",
    )
    late = late.reshape(total_rows, width)
    early_logits, early_stats = exit_logits(early)
    late_logits, late_stats = exit_logits(late)
    stats = jnp.concatenate([early_stats, late_stats], axis=1).reshape(3, 8, -1)
    stats = launch([combine(stats, merge_stats)], 6, "combine_stats")[0]
    stats = stats.reshape(3, -1)
    log_norms = stats[0] + jnp.log(stats[1])
    losses = log_norms - stats[2]
    loss_sum = jnp.sum(
        counted * (EXIT_EARLY * losses[:total_rows] + EXIT_LAST * losses[total_rows:])
    )

    def exit_back(logits, log_norm, weight):
        grad_logits = (
            (jnp.exp(logits - log_norm[:, None]) - has_target.astype(FULL))
            * (weight * counted)[:, None]
        ).astype(LOW)
        return dot(grad_logits, table_own, 1, 0).astype(LOW), grad_logits

    late_back, late_grad = exit_back(late_logits, log_norms[total_rows:], EXIT_LAST)
    grad_late, mom_low = launch(
        [sum_wide(late_back), swap_turned(mom_parts[:, half:])], 7, "sum_late"
    )
    early_norms, grad_late = lax.optimization_barrier((log_norms[:total_rows], grad_late))
    early_back, early_grad = exit_back(early_logits, early_norms, EXIT_EARLY)
    mom_owned = jnp.concatenate([mom_top, mom_low], axis=1)

    grad_early = lax.psum_scatter(early_back, "wide", scatter_dimension=0, tiled=True)
    grad_final, gain_late, grad_out = launch(
        [
            settle_back(
                grad_late.astype(LOW),
                final_own,
                jnp.zeros_like(final_own),
                keep_row,
                gain_w[2:3],
            ),
        ],
        8,
        "back_late",
    )
    grad_layer = grad_final * keep_layer
    grad_out = grad_out.reshape(sel, width)
    out_all = lax.all_gather(grad_out, "wide", axis=0, tiled=True)
    acts, fed_back = feed_back(grad_out, ffn_w, gate, up, hidden)
    grad_mid, gain_mid, grad_branch, acts = launch(
        [
            settle_back(fed_back, middle, grad_layer, keep_row, gain_w[1:2]),
            swap_blocks("wide", acts),
        ],
        9,
        "back_middle",
    )
    acts = jnp.moveaxis(acts, 1, 0).reshape(3, total_rows, ffn_size)
    grad_branch, grad_early, out_all = lax.optimization_barrier(
        (grad_branch, grad_early, out_all)
    )
    inner, out_all = lax.optimization_barrier((inner, out_all))
    inner_all = lax.all_gather(inner, "wide", axis=0, tiled=True)
    grad_branch = grad_branch.reshape(sel, width)

    kv_parts, grad_queries, pick_part = attend_back(
        grad_branch, proj, own_head, queries, probs, cosine, sine, cosine_all, sine_all
    )
    grad_kv, grad_pick, grad_early, queries_wide, branch_cols, grad_head, _ = launch(
        [
            swap_blocks("narrow", kv_parts),
            sum_narrow(pick_part),
            sum_narrow(grad_early),
            gather_wide(grad_queries),
            split_columns("wide", grad_branch),
            product([early_grad, late_grad], [early, late], True),
        ],
        10,
        "trade_grads",
    )
    grad_kv, inner_all = lax.optimization_barrier((grad_kv, inner_all))
    grad_base = grad_mid + grad_final * (1.0 - keep_layer)
    grad_rows, gain_attn, gain_early, grad_kv = rows_back(
        rows_low, gain_w, proj, grad_kv, grad_pick, grad_early, grad_base, repeat
    )
    rights = (inner_all, inner_all, out_all)
    summed_qo = jnp.stack(
        [
            jnp.einsum("wtc,wtf->cf", pick_cols, queries_wide, preferred_element_type=FULL),
            jnp.einsum("wtc,wtf->cf", branch_cols, mixed_wide, preferred_element_type=FULL),
        ]
    )
    grad_rows, acts_owned, kv_wide, head_cols_all, *grad_ffn, ffn_squares = launch(
        [
            return_rows(grad_rows),
            swap_owned(acts, 5),
            later(gather_wide(grad_kv, 3), 2),
            later(split_columns("wide", grad_head, 3), 2),
            product([acts[j] for j in range(3)], rights, False),
        ],
        11,
        "return_rows",
    )
    turn = lax.rem(wide_spot, 2)
    grad_kv_w = jnp.einsum(
        "wtc,wtf->cf", tok_cols, kv_wide, preferred_element_type=FULL
    ).reshape(columns, narrow_count, 2, kv_size)
    grad_kv_w = jnp.moveaxis(grad_kv_w, 0, 2)
    summed_kv = lax.psum_scatter(grad_kv_w, "narrow", scatter_dimension=0, tiled=True)[0]
    summed_table, table_squares = spread(
        spots, listed, grad_rows.reshape(-1, columns), head_cols_all.reshape(vocab_rows, columns)
    )

    squares = (
        jnp.sum(summed_qo * summed_qo)
        + jnp.sum(summed_kv * summed_kv)
        + jnp.sum(ffn_squares)
        + jnp.sum(table_squares)
    )
    sums = jnp.stack(
        [gain_attn[0], gain_mid[0], gain_early[0] + gain_late[0], jnp.full((width,), squares)]
    )
    sums, kv_owned, qo_owned = launch(
        [
            combine(sums.reshape(4, 8, -1), add_two),
            send_owner(summed_kv.astype(LOW).reshape(2 * block_rows, kv_size)),
            later(send_owner(summed_qo.astype(LOW).reshape(2 * columns, q_size)), 1),
        ],
        12,
        "combine_sums",
    )
    sums = sums.reshape(4, width)
    summed_gain = lax.dynamic_slice_in_dim(
        sums[:3], (wide_spot * narrow_count + narrow_spot) * gain_size, gain_size, 1
    )
    square_total = sums[3, 0] + jnp.sum(sums[:3] * sums[:3])
    grad_norm = jnp.sqrt(square_total) / loss_count
    factor = jnp.minimum(1.0, CLIP_NORM / (grad_norm + 1e-06)) / loss_count

    matrix = jnp.minimum(lax.rem(narrow_spot + narrow_count - turn, narrow_count), 2)
    right = jnp.where(matrix == 2, out_all, inner_all)
    owned = jnp.einsum("stf,td->sfd", acts_owned, right, preferred_element_type=FULL)
    final_parts, factor = lax.optimization_barrier((jnp.stack(grad_ffn), factor))
    size = width // narrow_count

    def final_piece(spot):
        return lax.dynamic_slice_in_dim(final_parts, spot * size, size, 2)

    pieces = [final_piece(narrow_spot)] + [
        shifted(final_piece(lax.rem(narrow_spot + step, narrow_count)), "narrow", step)
        for step in range(1, narrow_count)
    ]
    directions = newton(
        factor, mom_owned, owned.reshape(ffn_rows, width), qo_owned, kv_owned
    )
    directions, pieces, ffn, factor = lax.optimization_barrier(
        (directions, pieces, ffn, factor)
    )
    summed_ffn = jnp.zeros((3, narrow_count, ffn_size, size), LOW)
    for step, piece in enumerate(pieces):
        source = lax.rem(narrow_spot - step + narrow_count, narrow_count)
        summed_ffn = lax.dynamic_update_index_in_dim(summed_ffn, piece, source, 1)
    summed_ffn = summed_ffn.reshape(3, ffn_rows, size).astype(FULL)
    received = [lax.dynamic_index_in_dim(directions, narrow_spot, 0, False)] + [
        shifted(
            lax.dynamic_index_in_dim(
                directions, lax.rem(narrow_spot + step, narrow_count), 0, False
            ),
            "narrow",
            step,
        )
        for step in range(1, narrow_count)
    ]

    def direction_of(matrix):
        step = lax.rem(narrow_spot - matrix - turn + 2 * narrow_count, narrow_count)
        result = received[0]
        for at in range(1, narrow_count):
            result = jnp.where(step == at, received[at], result)
        return result

    dir_ffn = jnp.stack([direction_of(matrix) for matrix in range(3)]).astype(FULL)
    small = direction_of(3).astype(FULL)
    dir_qo = small[: 2 * block_rows].reshape(mom_qo.shape)
    dir_kv = small[2 * block_rows : 2 * block_rows + half_rows].reshape(half_rows, 4, kv_size)
    dir_kv = jnp.moveaxis(dir_kv, 1, 0).reshape(mom_kv.shape)

    embed_new, embed_m_new, embed_v_new = adamw(
        embed, embed_m, embed_v, summed_table * factor, RATE_ADAM, WEIGHT_DECAY
    )
    gains_new, gains_m_new, gains_v_new = adamw(
        gains, gains_m, gains_v, summed_gain * factor, RATE_GAIN, 0.0
    )

    def mom_next(mom, grad):
        return MOMENTUM * mom + jnp.moveaxis(grad * factor, 0, 1)

    shrink = 1.0 - RATE_MUON * WEIGHT_DECAY

    def weight_next(weight, direction):
        return weight * shrink - RATE_MUON * jnp.moveaxis(direction, 0, 1)

    return (
        loss_sum,
        loss_count,
        grad_norm,
        embed_new,
        embed_m_new,
        embed_v_new,
        weight_next(attn_qo, dir_qo),
        mom_next(attn_qo_mom, summed_qo),
        weight_next(attn_kv, dir_kv),
        mom_next(attn_kv_mom, summed_kv),
        weight_next(ffn, dir_ffn),
        mom_next(ffn_mom, summed_ffn),
        gains_new,
        gains_m_new,
        gains_v_new,
    )


def solution(mesh):
    by_pack = P("wide", None)
    table = P("narrow", "wide")
    layer = P("wide", None, "narrow")
    gain = P(None, ("wide", "narrow"))
    return jax.shard_map(
        per_device,
        mesh=mesh,
        in_specs=(by_pack,) * 4 + (P("wide"),) + (table,) * 3 + (layer,) * 6 + (gain,) * 3,
        out_specs=(P(),) * 3 + (table,) * 3 + (layer,) * 6 + (gain,) * 3,
        check_vma=False,
    )
```

```python
import functools

import jax
import jax.numpy as jnp
from jax import lax
from jax.experimental import pallas as pl
from jax.experimental.pallas import tpu as pltpu
from jax.sharding import PartitionSpec as P

HEADS = 16
HD = 128
KVH = 4
NS_STEPS = 5
STEP = 10


NORM_EPS = 1e-05
ROPE_BASE = 10000.0
EXIT_EARLY = 0.25
EXIT_LAST = 1.0
CLIP_NORM = 0.02
BETA_ONE = 0.9
BETA_TWO = 0.95
ADAM_EPS = 1e-08
RATE_ADAM = 0.02
RATE_GAIN = 0.3
RATE_MUON = 0.3
WEIGHT_DECAY = 0.1
MOMENTUM = 0.95
NEWTON_A = 3.4445
NEWTON_B = -4.775
NEWTON_C = 2.0315
MASKED = -1e30
LOW = jnp.bfloat16
FULL = jnp.float32
BOTH = ("wide", "narrow")
UNROLL = 16
VMEM_BYTES = 56 * 1024 * 1024


def dot(first, second, first_dim, second_dim):
    return lax.dot_general(
        first, second, (((first_dim,), (second_dim,)), ((), ())), preferred_element_type=FULL
    )


def norm_rows(values, gain_row):
    return (
        values * lax.rsqrt(jnp.mean(values * values, axis=-1, keepdims=True) + NORM_EPS) * gain_row
    )


def segments_at(lens, where_at):
    ends = jnp.cumsum(lens)
    return jnp.sum((where_at[:, None] >= ends[None, :]).astype(jnp.int32), axis=1)


def angles_at(lens, where_at):
    segment = segments_at(lens, where_at)
    starts = jnp.cumsum(lens) - lens
    member = segment[:, None] == jnp.arange(lens.shape[0], dtype=jnp.int32)[None, :]
    begin = jnp.sum(jnp.where(member, starts[None, :], 0), axis=1)
    offset_pos = (where_at - begin).astype(FULL)
    inverse = ROPE_BASE ** (-2.0 * jnp.arange(HD // 2, dtype=FULL) / HD)
    angle = offset_pos[:, None] * inverse[None, :]
    return (segment, jnp.cos(angle), jnp.sin(angle))


MESH = pl.DeviceIdType.MESH
ANY = pl.BlockSpec(memory_space=pl.ANY)
VMEM = pl.BlockSpec(memory_space=pltpu.VMEM)


def others(axis, count):
    me = lax.axis_index(axis)
    return [{axis: lax.rem(me + step, count)} for step in range(1, count)]


def push(source, target, send, receive, device):
    return pltpu.make_async_remote_copy(
        src_ref=source,
        dst_ref=target,
        send_sem=send,
        recv_sem=receive,
        device_id=device,
        device_id_type=MESH,
    )


def arrived(block, send, receive, device):
    push(block, block, send, receive, device).wait_recv()


def like(values):
    return jax.ShapeDtypeStruct(values.shape, values.dtype)


def struct(shape, dtype):
    return jax.ShapeDtypeStruct(shape, dtype)


def sems(*shape):
    return pltpu.SemaphoreType.DMA(shape)


class Task:
    def __init__(self, inputs, outputs, scratch, steps, place_in, place_out, axes):
        self.inputs, self.outputs, self.scratch, self.steps = inputs, outputs, scratch, steps
        self.place_in = [place_in] * len(inputs)
        self.place_out = [place_out] * len(outputs)
        self.axes = axes


def launch(tasks, ident, name):
    axes = sorted(set(axis for task in tasks for axis in task.axes))
    inputs = [a for task in tasks for a in task.inputs]
    outputs = [a for task in tasks for a in task.outputs]
    scratch = [a for task in tasks for a in task.scratch]

    def body(*refs):
        refs = list(refs)
        ins = refs[: len(inputs)]
        outs = refs[len(inputs) : len(inputs) + len(outputs)]
        extra = refs[len(inputs) + len(outputs) :]
        barrier = pltpu.get_barrier_semaphore()
        targets = [device for axis in axes for device in others(axis, lax.axis_size(axis))]
        for device in targets:
            pl.semaphore_signal(barrier, inc=1, device_id=device, device_id_type=MESH)
        pl.semaphore_wait(barrier, len(targets))
        live = []
        for task in tasks:
            counts = (len(task.inputs), len(task.outputs), len(task.scratch))
            live.append(task.steps(ins[: counts[0]], outs[: counts[1]], extra[: counts[2]]))
            ins, outs, extra = ins[counts[0] :], outs[counts[1] :], extra[counts[2] :]
        while live:
            live = [steps for steps in live if next(steps, 0) is None]

    size = sum(a.size * a.dtype.itemsize for a in list(inputs) + list(outputs))
    return pl.pallas_call(
        body,
        out_shape=outputs,
        in_specs=[place for task in tasks for place in task.place_in],
        out_specs=[place for task in tasks for place in task.place_out],
        scratch_shapes=scratch,
        compiler_params=pltpu.CompilerParams(
            collective_id=ident, has_side_effects=True, vmem_limit_bytes=VMEM_BYTES
        ),
        cost_estimate=pl.CostEstimate(flops=0, bytes_accessed=size // 8, transcendentals=0),
        name=name,
    )(*inputs)


def later(task, turns):
    begin = task.steps

    def steps(ins, outs, scratch):
        for turn in range(turns):
            yield
        yield from begin(ins, outs, scratch)

    task.steps = steps
    return task


def gather_wide(values, patience=1):
    count = lax.axis_size("wide")
    chips = count // 2

    def steps(ins, outs, scratch):
        (x_ref,), (out_ref,), (send, receive, local) = ins, outs, scratch
        me = lax.axis_index("wide")
        mate = me + 1 - 2 * lax.rem(me, 2)
        peers = [lax.rem(me + 2 * step, count) for step in range(1, chips)] + [mate]
        first = []
        for step, peer in enumerate(peers):
            copy = push(x_ref, out_ref.at[me], send.at[step], receive.at[me], {"wide": peer})
            copy.start()
            first.append(copy)
        keep = pltpu.make_async_copy(x_ref, out_ref.at[me], local)
        keep.start()
        for turn in range(patience):
            yield
        second = []
        for step in range(1, chips):
            source = lax.rem(me - 2 * step + count, count)
            block = out_ref.at[source]
            arrived(block, send.at[0], receive.at[source], {"wide": mate})
            copy = push(
                block, block, send.at[chips + step - 1], receive.at[source], {"wide": mate}
            )
            copy.start()
            second.append(copy)
        yield
        for step in range(chips):
            source = lax.rem(mate - 2 * step + count, count)
            arrived(out_ref.at[source], send.at[0], receive.at[source], {"wide": mate})
        for copy in first + second:
            copy.wait_send()
        keep.wait()

    shape = struct((count,) + values.shape, values.dtype)
    return Task(
        [values], [shape], [sems(count - 1), sems(count), sems()], steps, ANY, ANY, ["wide"]
    )


def trade(axis, values, source_of, target_of, shape, patience=2):
    count = lax.axis_size(axis)

    def steps(ins, outs, scratch):
        (x_ref,), (out_ref,), (send, receive, local) = ins, outs, scratch
        me = lax.axis_index(axis)
        copies = []
        for step in range(1, count):
            peer = lax.rem(me + step, count)
            copy = push(
                source_of(x_ref, peer),
                target_of(out_ref, me),
                send.at[step - 1],
                receive.at[me],
                {axis: peer},
            )
            copy.start()
            copies.append(copy)
        keep = pltpu.make_async_copy(source_of(x_ref, me), target_of(out_ref, me), local)
        keep.start()
        for turn in range(patience):
            yield
        for step in range(1, count):
            source = lax.rem(me - step + count, count)
            arrived(
                target_of(out_ref, source), send.at[0], receive.at[source], {axis: source}
            )
        for copy in copies:
            copy.wait_send()
        keep.wait()

    return Task(
        [values],
        [struct(shape, values.dtype)],
        [sems(count - 1), sems(count), sems()],
        steps,
        ANY,
        ANY,
        [axis],
    )


def block_at(ref, spot):
    return ref.at[spot]


def whole_at(ref, spot):
    return ref


def columns_of(size):
    def at(ref, spot):
        return ref.at[:, pl.ds(pl.multiple_of(spot * size, size), size)]

    return at


def turned(ref, spot):
    count = lax.axis_size("narrow")
    matrix = lax.rem(spot + count - lax.rem(lax.axis_index("wide"), 2), count)
    return ref.at[jnp.minimum(matrix, 3)]


def swap_turned(values, patience=2):
    shape = (lax.axis_size("narrow"),) + values.shape[1:]
    return trade("narrow", values, turned, block_at, shape, patience)


def product(lefts, rights, sums, dim=0):
    count = len(lefts)
    columns = rights[0].shape[1]
    block = min(512, columns)
    outputs = 1 if sums else count
    rows = lefts[0].shape[1 - dim]

    def steps(ins, outs, scratch):
        left_refs, right_refs = ins[:count], ins[count:]
        right_refs = [right_refs[at % len(right_refs)] for at in range(count)]
        result_refs, square_ref = outs[:outputs], outs[outputs]
        yield
        square_ref[...] = jnp.zeros_like(square_ref)
        for at in range(outputs):
            members = range(count) if sums else [at]

            def strip(part, carry):
                spot = pl.ds(pl.multiple_of(part * block, block), block)
                value = jnp.zeros((rows, block), FULL)
                for member in members:
                    value = value + dot(
                        left_refs[member][...], right_refs[member][:, spot], dim, 0
                    )
                result_refs[at][:, spot] = value.astype(LOW)
                if not sums:
                    square_ref[:, spot] = square_ref[:, spot] + jnp.sum(
                        value * value, axis=0, keepdims=True
                    )
                return carry

            lax.fori_loop(0, columns // block, strip, 0)
            yield

    return Task(
        list(lefts) + list(rights),
        [struct((rows, columns), LOW)] * outputs + [struct((1, columns), FULL)],
        [],
        steps,
        VMEM,
        VMEM,
        [],
    )


def exit_stats(features, table, targets):
    rows, vocab = features.shape[0], table.shape[0]
    block = min(256, vocab)

    def steps(ins, outs, scratch):
        features_ref, table_ref, targets_ref = ins
        logits_ref, stats_ref = outs
        yield

        def strip(part):
            return pl.ds(pl.multiple_of(part * block, block), block)

        def over(function, start):
            return lax.fori_loop(0, vocab // block, function, start)

        def fill(part, peak):
            logits = dot(table_ref[strip(part), :], features_ref[...], 1, 1)
            logits_ref[strip(part), :] = logits
            return jnp.maximum(peak, jnp.max(logits, axis=0, keepdims=True))

        peak = over(fill, jnp.full((1, rows), MASKED, FULL))
        lines = lax.broadcasted_iota(jnp.int32, (block, rows), 0)

        def add(part, carry):
            total, picked = carry
            logits = logits_ref[strip(part), :]
            hit = lines + part * block == targets_ref[...]
            return (
                total + jnp.sum(jnp.exp(logits - peak), axis=0, keepdims=True),
                picked + jnp.sum(jnp.where(hit, logits, 0.0), axis=0, keepdims=True),
            )

        zero = jnp.zeros((1, rows), FULL)
        total, picked = over(add, (zero, zero))
        stats_ref[0:1, :] = peak
        stats_ref[1:2, :] = total
        stats_ref[2:3, :] = picked

    return Task(
        [features, table, targets],
        [struct((vocab, rows), FULL), struct((3, rows), FULL)],
        [],
        steps,
        VMEM,
        VMEM,
        [],
    )


def swap_owned(values, patience):
    count = lax.axis_size("narrow")

    def steps(ins, outs, scratch):
        (x_ref,), (out_ref,), (send, receive, local) = ins, outs, scratch
        me = lax.axis_index("narrow")
        turn = lax.rem(lax.axis_index("wide"), 2)

        def matrix_of(device):
            return lax.rem(device + count - turn, count)

        def copy_to(step):
            peer = lax.rem(me + step, count)
            return push(
                x_ref.at[jnp.minimum(matrix_of(peer), 2)],
                out_ref.at[me],
                send.at[step - 1],
                receive.at[me],
                {"narrow": peer},
            )

        def keep():
            return pltpu.make_async_copy(
                x_ref.at[jnp.minimum(matrix_of(me), 2)], out_ref.at[me], local
            )

        keep().start()
        for step in range(1, count):

            @pl.when(matrix_of(lax.rem(me + step, count)) < 3)
            def _():
                copy_to(step).start()

        for turn_at in range(patience):
            yield

        @pl.when(matrix_of(me) < 3)
        def _():
            for step in range(1, count):
                source = lax.rem(me - step + count, count)
                arrived(out_ref.at[source], send.at[0], receive.at[source], {"narrow": source})

        for step in range(1, count):

            @pl.when(matrix_of(lax.rem(me + step, count)) < 3)
            def _():
                copy_to(step).wait_send()

        keep().wait()

    return Task(
        [values],
        [struct((count,) + values.shape[1:], values.dtype)],
        [sems(count - 1), sems(count), sems()],
        steps,
        ANY,
        ANY,
        ["narrow"],
    )


def send_owner(values):
    count = lax.axis_size("narrow")

    def steps(ins, outs, scratch):
        (x_ref,), (out_ref,), (send, receive, local) = ins, outs, scratch
        me = lax.axis_index("narrow")
        owner = lax.rem(3 + lax.rem(lax.axis_index("wide"), 2), count)
        keep = pltpu.make_async_copy(x_ref, out_ref.at[me], local)
        keep.start()

        def to_owner():
            return push(x_ref, out_ref.at[me], send.at[0], receive.at[me], {"narrow": owner})

        @pl.when(me != owner)
        def _():
            to_owner().start()

        yield
        yield

        @pl.when(me != owner)
        def _():
            to_owner().wait_send()

        @pl.when(me == owner)
        def _():
            for step in range(1, count):
                source = lax.rem(owner + step, count)
                arrived(out_ref.at[source], send.at[0], receive.at[source], {"narrow": source})

        keep.wait()

    return Task(
        [values],
        [struct((count,) + values.shape, values.dtype)],
        [sems(1), sems(count), sems()],
        steps,
        ANY,
        ANY,
        ["narrow"],
    )


def swap_blocks(axis, values):
    return trade(axis, values, block_at, block_at, values.shape)


def gather_blocks(axis, values):
    shape = (lax.axis_size(axis),) + values.shape
    return trade(axis, values, whole_at, block_at, shape)


def split_columns(axis, values, patience=2):
    count = lax.axis_size(axis)
    rows, size = values.shape[0], values.shape[1] // count
    return trade(axis, values, columns_of(size), block_at, (count, rows, size), patience)


def join_columns(axis, values):
    count, rows, size = values.shape
    return trade(axis, values, block_at, columns_of(size), (rows, count * size))


def collect(count, parts_ref, slots, send, receive):
    me = lax.axis_index("narrow")
    copies = []
    for step in range(1, count):
        peer = lax.rem(me + step, count)
        copy = push(
            parts_ref.at[peer],
            slots.at[me],
            send.at[step - 1],
            receive.at[me],
            {"narrow": peer},
        )
        copy.start()
        copies.append(copy)
    return copies


def collected(count, parts_ref, slots, send, receive):
    me = lax.axis_index("narrow")
    total = parts_ref[me].astype(FULL)
    for step in range(1, count):
        source = lax.rem(me - step + count, count)
        arrived(slots.at[source], send.at[0], receive.at[source], {"narrow": source})
        total = total + slots[source].astype(FULL)
    return total


def share(count, low, all_ref, send, receive):
    me = lax.axis_index("narrow")
    all_ref[me] = low
    copies = []
    for step in range(1, count):
        peer = lax.rem(me + step, count)
        copy = push(
            all_ref.at[me], all_ref.at[me], send.at[step - 1], receive.at[me], {"narrow": peer}
        )
        copy.start()
        copies.append(copy)
    return copies


def shared(count, all_ref, send, receive):
    me = lax.axis_index("narrow")
    for step in range(1, count):
        source = lax.rem(me - step + count, count)
        arrived(all_ref.at[source], send.at[0], receive.at[source], {"narrow": source})


def narrow_sems(count):
    return [sems(count - 1), sems(count)]


def settle(partial, base, other, keep_row, gain_row):
    count = lax.axis_size("narrow")
    rows, width = base.shape

    def steps(ins, outs, scratch):
        parts_ref, base_ref, other_ref, keep_ref, gain_ref = ins
        own_ref, all_ref = outs
        slots, send, receive, send_all, receive_all = scratch
        copies = collect(count, parts_ref, slots, send, receive)
        yield
        total = collected(count, parts_ref, slots, send, receive)
        total = jnp.where(keep_ref[...] > 0, total + base_ref[...], other_ref[...])
        own_ref[...] = total
        low = norm_rows(total, gain_ref[...]).astype(LOW)
        copies = copies + share(count, low, all_ref, send_all, receive_all)
        yield
        shared(count, all_ref, send_all, receive_all)
        for copy in copies:
            copy.wait_send()

    return Task(
        [partial.reshape(count, rows, width), base, other, keep_row, gain_row],
        [struct((rows, width), FULL), struct((count, rows, width), LOW)],
        [pltpu.VMEM((count, rows, width), partial.dtype)]
        + narrow_sems(count)
        + narrow_sems(count),
        steps,
        VMEM,
        VMEM,
        ["narrow"],
    )


def settle_back(partial, values, add, keep_row, gain_row):
    count = lax.axis_size("narrow")
    rows, width = values.shape

    def steps(ins, outs, scratch):
        parts_ref, values_ref, add_ref, keep_ref, gain_ref = ins
        own_ref, gain_grad_ref, all_ref = outs
        slots, send, receive, send_all, receive_all = scratch
        copies = collect(count, parts_ref, slots, send, receive)
        yield
        grad = collected(count, parts_ref, slots, send, receive)
        held = values_ref[...]
        root = lax.rsqrt(jnp.mean(held * held, axis=-1, keepdims=True) + NORM_EPS)
        scaled = gain_ref[...] * grad
        inner = jnp.mean(held * scaled, axis=-1, keepdims=True)
        own = add_ref[...] + root * scaled - held * (root * root * root * inner)
        gain_grad_ref[...] = jnp.sum(held * root * grad, axis=0, keepdims=True)
        own_ref[...] = own
        low = (own * keep_ref[...]).astype(LOW)
        copies = copies + share(count, low, all_ref, send_all, receive_all)
        yield
        shared(count, all_ref, send_all, receive_all)
        for copy in copies:
            copy.wait_send()

    return Task(
        [partial.reshape(count, rows, width), values, add, keep_row, gain_row],
        [
            struct((rows, width), FULL),
            struct((1, width), FULL),
            struct((count, rows, width), LOW),
        ],
        [pltpu.VMEM((count, rows, width), partial.dtype)]
        + narrow_sems(count)
        + narrow_sems(count),
        steps,
        VMEM,
        VMEM,
        ["narrow"],
    )


def sum_narrow(partial):
    count = lax.axis_size("narrow")
    rows, width = partial.shape[0] // count, partial.shape[1]

    def steps(ins, outs, scratch):
        (parts_ref,), (own_ref,), (slots, send, receive) = ins, outs, scratch
        copies = collect(count, parts_ref, slots, send, receive)
        yield
        yield
        own_ref[...] = collected(count, parts_ref, slots, send, receive)
        for copy in copies:
            copy.wait_send()

    return Task(
        [partial.reshape(count, rows, width)],
        [struct((rows, width), FULL)],
        [pltpu.VMEM((count, rows, width), partial.dtype)] + narrow_sems(count),
        steps,
        VMEM,
        VMEM,
        ["narrow"],
    )


def fetch_rows(found, rows):
    deep, wide = lax.axis_size("narrow"), lax.axis_size("wide")
    columns = found.shape[2]

    def steps(ins, outs, scratch):
        (found_ref,), (out_ref,) = ins, outs
        rightward, leftward, final = scratch[:3]
        send_right, receive_right, send_left, receive_left = scratch[3:7]
        send_wide, receive_wide, local = scratch[7:]
        spot = lax.axis_index("narrow")
        me = lax.axis_index("wide")

        def right_copy(part, source):
            return push(
                source,
                rightward.at[part],
                send_right.at[part],
                receive_right.at[part],
                {"narrow": lax.rem(spot + 1, deep)},
            )

        def left_copy(part, source):
            return push(
                source,
                leftward.at[part],
                send_left.at[part],
                receive_left.at[part],
                {"narrow": lax.rem(spot + deep - 1, deep)},
            )

        for step in range(deep - 1):
            right, left = deep - 1 - step, step

            @pl.when((spot == 0) & (right > 0))
            def _():
                right_copy(right, found_ref.at[right]).start()

            @pl.when((spot == deep - 1) & (left < deep - 1))
            def _():
                left_copy(left, found_ref.at[left]).start()

        yield
        for step in range(deep - 1):
            right, left = deep - 1 - step, step

            def pass_right():
                right_copy(right, rightward.at[right]).wait_recv()
                rightward[right] = rightward[right] + found_ref[right]
                right_copy(right, rightward.at[right]).start()

            pl.when((spot > 0) & (right > spot) & (2 * spot < deep))(pass_right)

            @pl.when((spot < deep - 1) & (left < spot))
            def _():
                left_copy(left, leftward.at[left]).wait_recv()
                leftward[left] = leftward[left] + found_ref[left]
                left_copy(left, leftward.at[left]).start()

            pl.when((right > spot) & (2 * spot >= deep))(pass_right)

        final[...] = found_ref[spot]

        @pl.when(spot > 0)
        def _():
            right_copy(spot, rightward.at[spot]).wait_recv()
            final[...] = final[...] + rightward[spot]

        @pl.when(spot < deep - 1)
        def _():
            left_copy(spot, leftward.at[spot]).wait_recv()
            final[...] = final[...] + leftward[spot]

        def rows_for(device):
            return final.at[pl.ds(pl.multiple_of(device * rows, rows), rows)]

        def columns_from(device):
            return columns_of(columns)(out_ref, device)

        copies = []
        for step in range(1, wide):
            peer = lax.rem(me + step, wide)
            copy = push(
                rows_for(peer),
                columns_from(me),
                send_wide.at[step - 1],
                receive_wide.at[me],
                {"wide": peer},
            )
            copy.start()
            copies.append(copy)
        keep = pltpu.make_async_copy(rows_for(me), columns_from(me), local)
        keep.start()
        yield
        for step in range(1, wide):
            source = lax.rem(me - step + wide, wide)
            arrived(
                columns_from(source), send_wide.at[0], receive_wide.at[source], {"wide": source}
            )
        yield
        for copy in copies:
            copy.wait_send()
        keep.wait()
        for step in range(deep - 1):
            right, left = deep - 1 - step, step

            @pl.when(right > spot)
            def _():
                right_copy(right, found_ref.at[right]).wait_send()

            @pl.when(left < spot)
            def _():
                left_copy(left, found_ref.at[left]).wait_send()

    task = Task(
        [found],
        [struct((rows, wide * columns), found.dtype)],
        [pltpu.VMEM(found.shape, found.dtype)] * 2
        + [pltpu.VMEM(found.shape[1:], found.dtype)]
        + [sems(deep)] * 4
        + [sems(wide - 1), sems(wide), sems()],
        steps,
        VMEM,
        ANY,
        ["narrow", "wide"],
    )
    return task


def return_rows(rows):
    deep, wide = lax.axis_size("narrow"), lax.axis_size("wide")
    count, width = rows.shape
    columns = width // wide

    def steps(ins, outs, scratch):
        (rows_ref,), (out_ref,) = ins, outs
        send_right, send_left, receive_deep, send_wide, receive_wide, local = scratch
        spot = lax.axis_index("narrow")
        me = lax.axis_index("wide")
        part_of = functools.partial(columns_of(columns), rows_ref)

        def landing(device):
            return out_ref.at[spot, pl.ds(pl.multiple_of(device * count, count), count)]

        copies = []
        for step in range(1, wide):
            peer = lax.rem(me + step, wide)
            copy = push(
                part_of(peer),
                landing(me),
                send_wide.at[step - 1],
                receive_wide.at[me],
                {"wide": peer},
            )
            copy.start()
            copies.append(copy)
        keep = pltpu.make_async_copy(part_of(me), landing(me), local)
        keep.start()
        yield
        for step in range(1, wide):
            source = lax.rem(me - step + wide, wide)
            arrived(landing(source), send_wide.at[0], receive_wide.at[source], {"wide": source})
        keep.wait()

        def right_copy(part):
            return push(
                out_ref.at[part],
                out_ref.at[part],
                send_right.at[part],
                receive_deep.at[part],
                {"narrow": lax.rem(spot + 1, deep)},
            )

        def left_copy(part):
            return push(
                out_ref.at[part],
                out_ref.at[part],
                send_left.at[part],
                receive_deep.at[part],
                {"narrow": lax.rem(spot + deep - 1, deep)},
            )

        @pl.when(spot < deep - 1)
        def _():
            right_copy(spot).start()

        @pl.when(spot > 0)
        def _():
            left_copy(spot).start()

        for step in range(1, deep):
            yield

            @pl.when(spot >= step)
            def _():
                right_copy(spot - step).wait_recv()

                @pl.when(spot < deep - 1)
                def _():
                    right_copy(spot - step).start()

            @pl.when(spot + step < deep)
            def _():
                left_copy(spot + step).wait_recv()

                @pl.when(spot > 0)
                def _():
                    left_copy(spot + step).start()

        for part in range(deep):

            @pl.when((part <= spot) & (spot < deep - 1))
            def _():
                right_copy(part).wait_send()

            @pl.when((part >= spot) & (spot > 0))
            def _():
                left_copy(part).wait_send()

        for copy in copies:
            copy.wait_send()

    return Task(
        [rows],
        [struct((deep, wide * count, columns), rows.dtype)],
        [sems(deep)] * 3 + [sems(wide - 1), sems(wide), sems()],
        steps,
        ANY,
        ANY,
        ["narrow", "wide"],
    )


def sum_wide(partial):
    count = lax.axis_size("wide")
    chips = count // 2
    rows, width = partial.shape[0] // count, partial.shape[1]

    def steps(ins, outs, scratch):
        (parts_ref,), (out_ref,) = ins, outs
        from_mate, paired, slots, send_mate, receive_mate, send, receive = scratch
        me = lax.axis_index("wide")
        side = lax.rem(me, 2)
        mate = me + 1 - 2 * side
        my_chip = me // 2
        mate_copies = []
        for step in range(chips):
            chip = lax.rem(my_chip + 1 + step, chips)
            copy = push(
                parts_ref.at[2 * chip + 1 - side],
                from_mate.at[chip],
                send_mate.at[step],
                receive_mate.at[chip],
                {"wide": mate},
            )
            copy.start()
            mate_copies.append(copy)
        yield
        copies = []
        for step in range(chips):
            chip = lax.rem(my_chip + 1 + step, chips)
            arrived(from_mate.at[chip], send_mate.at[0], receive_mate.at[chip], {"wide": mate})
            both = parts_ref[2 * chip + side].astype(FULL) + from_mate[chip].astype(FULL)
            if step < chips - 1:
                paired[chip] = both.astype(LOW)
                copy = push(
                    paired.at[chip],
                    slots.at[my_chip],
                    send.at[step],
                    receive.at[my_chip],
                    {"wide": 2 * chip + side},
                )
                copy.start()
                copies.append(copy)
            else:
                out_ref[...] = both
        yield
        for step in range(1, chips):
            chip = lax.rem(my_chip - step + chips, chips)
            arrived(slots.at[chip], send.at[0], receive.at[chip], {"wide": 2 * chip + side})
            out_ref[...] = out_ref[...] + slots[chip].astype(FULL)
        for copy in mate_copies + copies:
            copy.wait_send()

    return Task(
        [partial.reshape(count, rows, width)],
        [struct((rows, width), FULL)],
        [pltpu.VMEM((chips, rows, width), LOW)] * 3
        + [sems(chips), sems(chips), sems(max(chips - 1, 1)), sems(chips)],
        steps,
        VMEM,
        VMEM,
        ["wide"],
    )


def merge_stats(first, second):
    peak = jnp.maximum(first[0:1], second[0:1])
    total = first[1:2] * jnp.exp(first[0:1] - peak) + second[1:2] * jnp.exp(second[0:1] - peak)
    return jnp.concatenate([peak, total, first[2:3] + second[2:3]], axis=0)


def add_two(first, second):
    return first + second


def combine(values, join):
    deep, wide = lax.axis_size("narrow"), lax.axis_size("wide")

    def steps(ins, outs, scratch):
        (x_ref,), (out_ref,) = ins, outs
        wide_slots, deep_slots, send_wide, receive_wide, send_deep, receive_deep = scratch

        def start(axis, count, slots, value, send, receive):
            me = lax.axis_index(axis)
            slots[me] = value
            copies = []
            for step in range(1, count):
                peer = lax.rem(me + step, count)
                copy = push(
                    slots.at[me], slots.at[me], send.at[step - 1], receive.at[me], {axis: peer}
                )
                copy.start()
                copies.append(copy)
            return copies

        def finish(axis, count, slots, send, receive):
            me = lax.axis_index(axis)
            for step in range(1, count):
                source = lax.rem(me - step + count, count)
                arrived(slots.at[source], send.at[0], receive.at[source], {axis: source})
            total = slots[0]
            for source in range(1, count):
                total = join(total, slots[source])
            return total

        first = start("wide", wide, wide_slots, x_ref[...], send_wide, receive_wide)
        yield
        total = finish("wide", wide, wide_slots, send_wide, receive_wide)
        second = start("narrow", deep, deep_slots, total, send_deep, receive_deep)
        yield
        out_ref[...] = finish("narrow", deep, deep_slots, send_deep, receive_deep)
        for copy in first + second:
            copy.wait_send()

    return Task(
        [values],
        [like(values)],
        [
            pltpu.VMEM((wide,) + values.shape, values.dtype),
            pltpu.VMEM((deep,) + values.shape, values.dtype),
            sems(wide - 1),
            sems(wide),
            sems(deep - 1),
            sems(deep),
        ],
        steps,
        VMEM,
        VMEM,
        ["narrow", "wide"],
    )


def gather_both(values):
    deep, wide = lax.axis_size("narrow"), lax.axis_size("wide")

    def steps(ins, outs, scratch):
        (x_ref,), (out_ref,) = ins, outs
        send_wide, receive_wide, send_deep, receive_deep = scratch
        me = lax.axis_index("wide")
        spot = lax.axis_index("narrow")
        out_ref[spot, me] = x_ref[...]
        copies = []
        for step in range(1, wide):
            peer = lax.rem(me + step, wide)
            block = out_ref.at[spot, me]
            copy = push(block, block, send_wide.at[step - 1], receive_wide.at[me], {"wide": peer})
            copy.start()
            copies.append(copy)
        yield
        for step in range(1, wide):
            source = lax.rem(me - step + wide, wide)
            block = out_ref.at[spot, source]
            arrived(block, send_wide.at[0], receive_wide.at[source], {"wide": source})
        for step in range(1, deep):
            peer = lax.rem(spot + step, deep)
            block = out_ref.at[spot]
            copy = push(
                block, block, send_deep.at[step - 1], receive_deep.at[spot], {"narrow": peer}
            )
            copy.start()
            copies.append(copy)
        yield
        for step in range(1, deep):
            source = lax.rem(spot - step + deep, deep)
            block = out_ref.at[source]
            arrived(block, send_deep.at[0], receive_deep.at[source], {"narrow": source})
        for copy in copies:
            copy.wait_send()

    return Task(
        [values],
        [struct((deep, wide) + values.shape, values.dtype)],
        [sems(wide - 1), sems(wide), sems(deep - 1), sems(deep)],
        steps,
        VMEM,
        VMEM,
        ["narrow", "wide"],
    )


def turn_heads(values, cosine, sine):
    half = values.shape[1] // 2
    swapped = jnp.concatenate([values[:, half:], values[:, :half]], axis=1)
    return values * cosine + swapped * sine


def wide_angles(cosine, sine):
    return jnp.concatenate([cosine, cosine], axis=1), jnp.concatenate([-sine, sine], axis=1)


def local_call(body, inputs, specs, outputs, flops, name):
    return pl.pallas_call(
        body,
        grid=(1,),
        in_specs=specs,
        out_specs=[
            pl.BlockSpec(a.shape, lambda step, rank=len(a.shape): (0,) * rank) for a in outputs
        ],
        out_shape=outputs,
        compiler_params=pltpu.CompilerParams(vmem_limit_bytes=VMEM_BYTES),
        cost_estimate=pl.CostEstimate(flops=flops, bytes_accessed=8 << 20, transcendentals=0),
        name=name,
    )(*inputs)


def entire(values):
    return pl.BlockSpec(values.shape, lambda step: (0,) * values.ndim)


def column_block(values, size, index):
    return pl.BlockSpec((values.shape[0], size), lambda step: (0, index))


def heads_body(groups, rep, rows_ref, gain_ref, kv_ref, cos_ref, sin_ref, out_ref, normed_ref):
    count, _, _, tok_rows, head = out_ref.shape
    size = kv_ref.shape[1] // (2 * count)
    per_head = head // size
    rows = rows_ref[0:tok_rows, :].astype(FULL)
    normed = norm_rows(rows, gain_ref[...]).astype(LOW)
    normed_ref[...] = normed
    both = dot(normed, kv_ref[...], 1, 0)

    def head_of(kind, index):
        pieces = [
            both[:, (2 * part + kind) * size : (2 * part + kind + 1) * size]
            for part in range(index * per_head, (index + 1) * per_head)
        ]
        return pieces[0] if per_head == 1 else jnp.concatenate(pieces, axis=1)

    for owner in range(count):
        for group in range(groups):
            index = (owner * groups + group) // rep
            keys = turn_heads(head_of(0, index), cos_ref[...], sin_ref[...])
            out_ref[owner, group, 0] = keys.astype(LOW)
            out_ref[owner, group, 1] = head_of(1, index).astype(LOW)


def make_heads(rows_low, gain_row, proj, cosine, sine, groups, rep):
    count = lax.axis_size("narrow")
    tok_rows, head = cosine.shape
    width = rows_low.shape[1]
    size = 2 * KVH * HD
    return local_call(
        functools.partial(heads_body, groups, rep),
        [rows_low, gain_row, proj, cosine, sine],
        [entire(rows_low), entire(gain_row), column_block(proj, size, 0)]
        + [entire(cosine), entire(sine)],
        [struct((count, groups, 2, tok_rows, head), LOW), struct((tok_rows, width), LOW)],
        2 * tok_rows * width * size,
        "make_heads",
    )


def attend_body(
    start_ref,
    gains_ref,
    q_ref,
    o_ref,
    kv_ref,
    cos_ref,
    sin_ref,
    seg_ref,
    seg_all_ref,
    pick_ref,
    queries_ref,
    probs_ref,
    mixed_ref,
    part_ref,
    normed_ref,
    early_ref,
):
    count, groups, _, tok_rows, head = kv_ref.shape
    heads_own = probs_ref.shape[0]
    start = start_ref[...].astype(FULL)
    root = lax.rsqrt(jnp.mean(start * start, axis=-1, keepdims=True) + NORM_EPS)
    normed = (start * root * gains_ref[0:1, :]).astype(LOW)
    normed_ref[...] = normed
    early_ref[...] = (start * root * gains_ref[2:3, :]).astype(LOW)
    queries = dot(normed, q_ref[...], 1, 0)
    spots = lax.broadcasted_iota(jnp.int32, (1, count * tok_rows), 1)
    allowed = (seg_ref[...] == seg_all_ref[...]) & (pick_ref[...] >= spots)
    for group in range(groups):
        keys = jnp.concatenate([kv_ref[part, group, 0] for part in range(count)], axis=0)
        values = jnp.concatenate([kv_ref[part, group, 1] for part in range(count)], axis=0)
        for member in range(heads_own // groups):
            at = group * (heads_own // groups) + member
            spot = slice(at * head, (at + 1) * head)
            query = turn_heads(queries[:, spot], cos_ref[...], sin_ref[...]).astype(LOW)
            queries_ref[:, spot] = query
            scores = jnp.where(allowed, dot(query, keys, 1, 1) * head ** (-0.5), MASKED)
            shifted = jnp.exp(scores - jnp.max(scores, axis=-1, keepdims=True))
            probs = shifted / jnp.sum(shifted, axis=-1, keepdims=True)
            probs_ref[at] = probs
            mixed_ref[:, spot] = dot(probs.astype(LOW), values, 1, 0).astype(LOW)
    part_ref[...] = dot(mixed_ref[...], o_ref[...], 1, 1).astype(LOW)


def attend(start_low, gains, proj, own_head, cosine, sine, seg, seg_all, picks):
    count, groups, _, tok_rows, head = own_head.shape
    sel, width = start_low.shape
    heads_own = HEADS // count
    size = heads_own * head
    first = 2 * KVH * HD // size
    seq_len = count * tok_rows
    return local_call(
        attend_body,
        [start_low, gains, proj, proj, own_head, cosine, sine, seg, seg_all, picks],
        [
            entire(start_low),
            entire(gains),
            column_block(proj, size, first),
            column_block(proj, size, first + 1),
        ]
        + [entire(a) for a in (own_head, cosine, sine, seg, seg_all, picks)],
        [
            struct((sel, size), LOW),
            struct((heads_own, sel, seq_len), FULL),
            struct((sel, size), LOW),
            struct((sel, width), LOW),
            struct((sel, width), LOW),
            struct((sel, width), LOW),
        ],
        4 * sel * size * (width + seq_len),
        "attend",
    )


def attend_back_body(
    grad_ref,
    q_ref,
    o_ref,
    kv_ref,
    queries_ref,
    probs_ref,
    cos_ref,
    sin_ref,
    cos_all_ref,
    sin_all_ref,
    out_ref,
    grad_q_ref,
    part_ref,
):
    count, groups, _, tok_rows, head = kv_ref.shape
    heads_own = probs_ref.shape[0]
    scale = head ** (-0.5)
    grad_mixed = dot(grad_ref[...], o_ref[...], 1, 0).astype(LOW)
    for group in range(groups):
        keys = jnp.concatenate([kv_ref[part, group, 0] for part in range(count)], axis=0)
        values = jnp.concatenate([kv_ref[part, group, 1] for part in range(count)], axis=0)
        grad_keys = jnp.zeros(keys.shape, FULL)
        grad_values = jnp.zeros(keys.shape, FULL)
        for member in range(heads_own // groups):
            at = group * (heads_own // groups) + member
            spot = slice(at * head, (at + 1) * head)
            probs = probs_ref[at]
            grad_probs = dot(grad_mixed[:, spot], values, 1, 1)
            inner = jnp.sum(probs * grad_probs, axis=-1, keepdims=True)
            grad_scores = (probs * (grad_probs - inner)).astype(LOW)
            grad_query = dot(grad_scores, keys, 1, 0) * scale
            grad_q_ref[:, spot] = turn_heads(grad_query, cos_ref[...], -sin_ref[...]).astype(LOW)
            grad_keys = grad_keys + dot(grad_scores, queries_ref[:, spot], 0, 0)
            grad_values = grad_values + dot(probs.astype(LOW), grad_mixed[:, spot], 0, 0)
        grad_keys = turn_heads(grad_keys * scale, cos_all_ref[...], -sin_all_ref[...])
        for part in range(count):
            rows = slice(part * tok_rows, (part + 1) * tok_rows)
            out_ref[part, group, 0] = grad_keys[rows].astype(LOW)
            out_ref[part, group, 1] = grad_values[rows].astype(LOW)
    part_ref[...] = dot(grad_q_ref[...], q_ref[...], 1, 1).astype(LOW)


def attend_back(grad, proj, own_head, queries, probs, cosine, sine, cosine_all, sine_all):
    count, groups, _, tok_rows, head = own_head.shape
    sel, width = grad.shape
    size = queries.shape[1]
    first = 2 * KVH * HD // size
    return local_call(
        attend_back_body,
        [grad, proj, proj, own_head, queries, probs, cosine, sine, cosine_all, sine_all],
        [entire(grad), column_block(proj, size, first), column_block(proj, size, first + 1)]
        + [
            entire(a)
            for a in (own_head, queries, probs, cosine, sine, cosine_all, sine_all)
        ],
        [struct(own_head.shape, LOW), struct((sel, size), LOW), struct((sel, width), LOW)],
        8 * sel * size * width,
        "attend_back",
    )


def norm_back_rows(values, gain_row, grad):
    root = lax.rsqrt(jnp.mean(values * values, axis=-1, keepdims=True) + NORM_EPS)
    scaled = gain_row * grad
    inner = jnp.mean(values * scaled, axis=-1, keepdims=True)
    result = root * scaled - values * (root * root * root * inner)
    return result, jnp.sum(values * root * grad, axis=0, keepdims=True)


def rows_back_body(
    rep,
    rows_ref,
    gains_ref,
    kv_ref,
    heads_ref,
    pick_ref,
    early_ref,
    base_ref,
    out_ref,
    attn_gain_ref,
    early_gain_ref,
    grad_kv_ref,
):
    count, groups, _, tok_rows, head = heads_ref.shape
    size = kv_ref.shape[1] // (2 * count)
    per_head = head // size
    for index in range(KVH):
        for kind in range(2):
            copies = [
                heads_ref[at // groups, at % groups, kind]
                for at in range(index * rep, (index + 1) * rep)
            ]
            total = copies[0]
            if rep > 1:
                total = sum(copy.astype(FULL) for copy in copies).astype(LOW)
            for piece in range(per_head):
                lane = (2 * (index * per_head + piece) + kind) * size
                grad_kv_ref[:, lane : lane + size] = total[:, piece * size : (piece + 1) * size]
    values = rows_ref[...].astype(FULL)
    own = values[tok_rows:]
    tok_part, tok_gain = norm_back_rows(
        values[:tok_rows], gains_ref[0:1, :], dot(grad_kv_ref[...], kv_ref[...], 1, 1)
    )
    pick_part, pick_gain = norm_back_rows(own, gains_ref[0:1, :], pick_ref[...])
    early_part, early_gain = norm_back_rows(own, gains_ref[2:3, :], early_ref[...])
    attn_gain_ref[...] = tok_gain + pick_gain
    early_gain_ref[...] = early_gain
    out_ref[0:tok_rows, :] = tok_part.astype(LOW)
    out_ref[tok_rows:, :] = (pick_part + early_part + base_ref[...]).astype(LOW)


def rows_back(rows_low, gains, proj, heads, grad_pick, grad_early, base, rep):
    tok_rows = heads.shape[3]
    width = rows_low.shape[1]
    size = 2 * KVH * HD
    return local_call(
        functools.partial(rows_back_body, rep),
        [rows_low, gains, proj, heads, grad_pick, grad_early, base],
        [entire(rows_low), entire(gains), column_block(proj, size, 0)]
        + [entire(a) for a in (heads, grad_pick, grad_early, base)],
        [
            struct(rows_low.shape, LOW),
            struct((1, width), FULL),
            struct((1, width), FULL),
            struct((tok_rows, size), LOW),
        ],
        2 * tok_rows * width * size,
        "rows_back",
    )


def assemble_body(out_columns, *refs):
    pieces, out_ref = refs[:-1], refs[-1]
    count = len(pieces)
    me = lax.axis_index("narrow")
    for step, piece in enumerate(pieces):
        source = lax.rem(me - step + count, count)
        spot = pl.ds(pl.multiple_of(source * out_columns, out_columns), out_columns)
        out_ref[:, spot] = piece[...]


def assemble(pieces):
    rows, columns = pieces[0].shape
    outputs = [struct((rows, columns * len(pieces)), pieces[0].dtype)]
    return local_call(
        functools.partial(assemble_body, columns),
        list(pieces),
        [entire(piece) for piece in pieces],
        outputs,
        0,
        "assemble",
    )[0]


def feed_body(inner_ref, weight_ref, gate_ref, up_ref, hidden_ref, out_ref, total):
    part = pl.program_id(0)
    inner = inner_ref[...]
    gate = dot(inner, weight_ref[0, 0], 1, 1)
    up = dot(inner, weight_ref[0, 1], 1, 1)
    hidden = (jax.nn.silu(gate) * up).astype(LOW)
    gate_ref[0] = gate
    up_ref[0] = up
    hidden_ref[0] = hidden
    product = dot(hidden, weight_ref[0, 2], 1, 0)

    @pl.when(part == 0)
    def _():
        total[...] = product

    @pl.when(part > 0)
    def _():
        total[...] = total[...] + product

    @pl.when(part == pl.num_programs(0) - 1)
    def _():
        out_ref[...] = total[...].astype(LOW)


def feed(inner, weight):
    parts, _, size, width = weight.shape
    sel = inner.shape[0]
    same = pl.BlockSpec((sel, width), lambda part: (0, 0))
    slab = pl.BlockSpec((1, sel, size), lambda part: (part, 0, 0))
    return pl.pallas_call(
        feed_body,
        grid=(parts,),
        in_specs=[same, pl.BlockSpec((1, 3, size, width), lambda part: (part, 0, 0, 0))],
        out_specs=[slab, slab, slab, same],
        out_shape=[
            struct((parts, sel, size), FULL),
            struct((parts, sel, size), FULL),
            struct((parts, sel, size), LOW),
            struct((sel, width), LOW),
        ],
        scratch_shapes=[pltpu.VMEM((sel, width), FULL)],
        compiler_params=pltpu.CompilerParams(vmem_limit_bytes=VMEM_BYTES),
        cost_estimate=pl.CostEstimate(
            flops=6 * sel * parts * size * width,
            bytes_accessed=weight.size * 2,
            transcendentals=0,
        ),
        name="feed",
    )(inner, weight)


def feed_back_body(grad_ref, weight_ref, gate_ref, up_ref, hidden_ref, acts_ref, out_ref, total):
    part = pl.program_id(0)
    grad_hidden = dot(grad_ref[...], weight_ref[0, 2], 1, 1)
    gate = gate_ref[0]
    sigma = jax.nn.sigmoid(gate)
    grad_gate = (grad_hidden * up_ref[0] * sigma * (1.0 + gate * (1.0 - sigma))).astype(LOW)
    grad_up = (grad_hidden * gate * sigma).astype(LOW)
    acts_ref[0, 0] = grad_gate
    acts_ref[0, 1] = grad_up
    acts_ref[0, 2] = hidden_ref[0]
    product = dot(grad_gate, weight_ref[0, 0], 1, 0) + dot(grad_up, weight_ref[0, 1], 1, 0)

    @pl.when(part == 0)
    def _():
        total[...] = product

    @pl.when(part > 0)
    def _():
        total[...] = total[...] + product

    @pl.when(part == pl.num_programs(0) - 1)
    def _():
        out_ref[...] = total[...].astype(LOW)


def feed_back(grad, weight, gate, up, hidden):
    parts, _, size, width = weight.shape
    sel = grad.shape[0]
    same = pl.BlockSpec((sel, width), lambda part: (0, 0))
    slab = pl.BlockSpec((1, sel, size), lambda part: (part, 0, 0))
    return pl.pallas_call(
        feed_back_body,
        grid=(parts,),
        in_specs=[same, pl.BlockSpec((1, 3, size, width), lambda part: (part, 0, 0, 0))]
        + [slab] * 3,
        out_specs=[pl.BlockSpec((1, 3, sel, size), lambda part: (part, 0, 0, 0)), same],
        out_shape=[struct((parts, 3, sel, size), LOW), struct((sel, width), LOW)],
        scratch_shapes=[pltpu.VMEM((sel, width), FULL)],
        compiler_params=pltpu.CompilerParams(vmem_limit_bytes=VMEM_BYTES),
        cost_estimate=pl.CostEstimate(
            flops=6 * sel * parts * size * width,
            bytes_accessed=weight.size * 2,
            transcendentals=0,
        ),
        name="feed_back",
    )(grad, weight, gate, up, hidden)


def newton_steps(problems):
    rows, width = problems[0][0].shape
    block = min(512, width)
    eye = lax.broadcasted_iota(jnp.int32, (rows, rows), 0) == lax.broadcasted_iota(
        jnp.int32, (rows, rows), 1
    )

    def strip(part):
        return pl.ds(pl.multiple_of(part * block, block), block)

    def over(function, start):
        return lax.fori_loop(0, width // block, function, start)

    def add_squares(part, totals):
        values = [current[:, strip(part)] for current, low, gram, rest in problems]
        return [total + jnp.sum(value * value) for total, value in zip(totals, values)]

    totals = over(add_squares, [jnp.float32(0.0)] * len(problems))
    scales = [1.0 / (jnp.sqrt(total) + 1e-07) for total in totals]

    def begin(part, carry):
        for scale, (current, low, gram, rest) in zip(scales, problems):
            values = current[:, strip(part)] * scale
            current[:, strip(part)] = values
            low[:, strip(part)] = values.astype(LOW)
        return carry

    over(begin, 0)

    def iteration(turn, carry):
        for current, low, gram, rest in problems:
            gram[...] = jnp.zeros_like(gram)

        def add_gram(part, carry):
            for current, low, gram, rest in problems:
                values = low[:, strip(part)]
                gram[...] = gram[...] + dot(values, values, 1, 1)
            return carry

        over(add_gram, 0)
        seconds = []
        for current, low, gram, rest in problems:
            whole = gram[...]
            middle = jnp.sum(jnp.where(eye, whole, 0.0)) / rows
            rest[...] = (whole - jnp.where(eye, middle, 0.0)).astype(LOW)
            square = dot(rest[...], rest[...], 1, 0)
            whole = gram[...]
            centred = whole - jnp.where(eye, middle, 0.0)
            square = square + 2.0 * middle * centred + jnp.where(eye, middle * middle, 0.0)
            whole = NEWTON_B * whole + NEWTON_C * square
            second = jnp.sum(jnp.where(eye, whole, 0.0)) / rows
            rest[...] = (whole - jnp.where(eye, second, 0.0)).astype(LOW)
            seconds.append(second)

        def apply(part, carry):
            for second, (current, low, gram, rest) in zip(seconds, problems):
                values = (NEWTON_A + second) * current[:, strip(part)] + dot(
                    rest[...], low[:, strip(part)], 1, 0
                )
                current[:, strip(part)] = values
                low[:, strip(part)] = values.astype(LOW)
            return carry

        over(apply, 0)
        return carry

    lax.fori_loop(0, NS_STEPS, iteration, 0)


def newton_scratch(rows, width):
    return [
        pltpu.VMEM((rows, width), FULL),
        pltpu.VMEM((rows, width), LOW),
        pltpu.VMEM((rows, rows), FULL),
        pltpu.VMEM((rows, rows), LOW),
    ]


def newton_cost(count, rows, width):
    return pl.CostEstimate(
        flops=NS_STEPS * count * (4 * rows * rows * width + 2 * rows * rows * rows),
        bytes_accessed=6 * count * rows * width,
        transcendentals=0,
    )


def newton_body(factor_ref, mom_ref, grad_ref, out_ref, *problem):
    current, low = problem[:2]
    parts, rows, columns = mom_ref.shape
    factor = factor_ref[0]
    size = grad_ref.shape[1]
    for part in range(parts):
        spot = slice(part * columns, (part + 1) * columns)
        for source in range(parts):
            here = slice(source * size, (source + 1) * size)
            current[here, spot] = MOMENTUM * mom_ref[part, here, :].astype(
                FULL
            ) + factor * grad_ref[source, :, spot].astype(FULL)
    newton_steps([problem])
    for part in range(parts):
        out_ref[part] = low[:, part * columns : (part + 1) * columns]


def newton_small_body(rows, factor_ref, mom_ref, grad_ref, kv_ref, out_ref, *scratch):
    problems = [scratch[4 * at : 4 * at + 4] for at in range(4)]
    parts, _, columns = mom_ref.shape
    kv_columns = kv_ref.shape[2]
    half = rows // 2
    factor = factor_ref[0]
    for part in range(parts):
        spot = slice(part * columns, (part + 1) * columns)
        for member in range(2):
            current = problems[member][0]
            here = slice(member * rows, (member + 1) * rows)
            mom, grad = mom_ref[part, here, :], grad_ref[part, here, :]
            current[:, spot] = MOMENTUM * mom.astype(FULL) + factor * grad.astype(FULL)
        spot = slice(part * kv_columns, (part + 1) * kv_columns)
        for member in range(2):
            current = problems[2 + member][0]
            piece = kv_ref[part, member * rows : (member + 1) * rows, :].astype(FULL)
            for side in range(2):
                lane = (2 * member + side) * kv_columns
                mom = mom_ref[part, 2 * rows : 2 * rows + half, lane : lane + kv_columns]
                here = slice(side * half, (side + 1) * half)
                current[here, spot] = MOMENTUM * mom.astype(FULL) + factor * piece[here]
    newton_steps(problems[:2])
    newton_steps(problems[2:])
    out_ref[...] = jnp.zeros_like(out_ref)
    for part in range(parts):
        for member in range(2):
            out_ref[part, member * rows : (member + 1) * rows, :] = problems[member][1][
                :, part * columns : (part + 1) * columns
            ]
            low = problems[2 + member][1]
            for side in range(2):
                lane = (2 * member + side) * kv_columns
                out_ref[part, 2 * rows : 2 * rows + half, lane : lane + kv_columns] = low[
                    side * half : (side + 1) * half,
                    part * kv_columns : (part + 1) * kv_columns,
                ]


def newton_any_body(rows, factor_ref, mom_ref, grad_ref, qo_ref, kv_ref, out_ref, *scratch):
    parts = mom_ref.shape[0]
    owner = lax.rem(3 + lax.rem(lax.axis_index("wide"), 2), parts)
    small = lax.axis_index("narrow") == owner

    @pl.when(small)
    def _():
        newton_small_body(rows, factor_ref, mom_ref, qo_ref, kv_ref, out_ref, *scratch[4:])

    @pl.when(jnp.logical_not(small))
    def _():
        newton_body(factor_ref, mom_ref, grad_ref, out_ref, *scratch[:4])


def newton(factor, mom, grad, qo_grad, kv_grad):
    parts, slot_rows, columns = mom.shape
    width = parts * columns
    rows = kv_grad.shape[1] // 2
    kv_width = parts * kv_grad.shape[2]
    return pl.pallas_call(
        functools.partial(newton_any_body, rows),
        in_specs=[pl.BlockSpec(memory_space=pltpu.SMEM)] + [VMEM] * 4,
        out_specs=VMEM,
        out_shape=struct(mom.shape, LOW),
        scratch_shapes=newton_scratch(slot_rows, width)
        + newton_scratch(rows, width) * 2
        + newton_scratch(rows, kv_width) * 2,
        compiler_params=pltpu.CompilerParams(vmem_limit_bytes=VMEM_BYTES),
        cost_estimate=newton_cost(1, slot_rows, width),
        name="newton",
    )(factor.reshape(1), mom, grad, qo_grad, kv_grad)


def lookup_body(ids_ref, turn_ref, table_ref, out_ref, low_ref, list_ref, held, rows, sem):
    vocab = table_ref.shape[0]
    count = out_ref.shape[0]
    load = pltpu.make_async_copy(table_ref, held, sem)
    load.start()
    rows[...] = jnp.zeros_like(rows)

    found = turn_ref[count]

    def note(group, carry):
        for member in range(UNROLL):
            at = group * UNROLL + member
            list_ref[turn_ref[at]] = at
        return carry

    lax.fori_loop(0, count // UNROLL, note, 0)
    for member in range(UNROLL):
        list_ref[found + member] = count
    list_ref[count + UNROLL] = found
    load.wait()

    def step(group, carry):
        for member in range(UNROLL):
            at = list_ref[group * UNROLL + member]
            spot = jnp.minimum(ids_ref[jnp.minimum(at, count - 1)], vocab - 1)
            rows[pl.ds(at, 1), :] = held[pl.ds(spot, 1), :]
        return carry

    lax.fori_loop(0, (found + UNROLL - 1) // UNROLL, step, 0)
    out_ref[...] = rows[pl.ds(0, count), :].astype(LOW)
    low_ref[...] = held[...].astype(LOW)


def lookup(table, ids):
    vocab, columns = table.shape
    count = ids.shape[0]
    mine = (ids < vocab).reshape(-1, 128)
    before = jnp.arange(128)[:, None] < jnp.arange(128)[None, :]
    in_row = dot(mine.astype(LOW), before.astype(LOW), 1, 0)
    per_row = jnp.sum(mine.astype(FULL), axis=1)
    lines = jnp.arange(mine.shape[0])
    ahead = jnp.sum(jnp.where(lines[:, None] > lines[None, :], per_row[None, :], 0.0), axis=1)
    found = jnp.sum(per_row).astype(jnp.int32)
    turns = (in_row + ahead[:, None]).astype(jnp.int32)
    turns = jnp.where(mine, turns, count + UNROLL + 1).reshape(-1)
    turns = jnp.concatenate([turns, jnp.full((128,), found)])
    return pl.pallas_call(
        lookup_body,
        in_specs=[pl.BlockSpec(memory_space=pltpu.SMEM)] * 2 + [ANY],
        out_specs=[VMEM, VMEM, pl.BlockSpec(memory_space=pltpu.SMEM)],
        scratch_shapes=[
            pltpu.VMEM((vocab, columns), FULL),
            pltpu.VMEM((count + 8, columns), FULL),
            pltpu.SemaphoreType.DMA,
        ],
        out_shape=[
            struct((count, columns), LOW),
            struct((vocab, columns), LOW),
            struct((count + 2 * UNROLL,), jnp.int32),
        ],
        compiler_params=pltpu.CompilerParams(vmem_limit_bytes=VMEM_BYTES),
        cost_estimate=pl.CostEstimate(
            flops=0, bytes_accessed=vocab * columns * 4, transcendentals=0
        ),
        name="lookup",
    )(ids, turns, table)


def spread_body(
    ids_ref, list_ref, rows_ref, head_ref, out_ref, square_ref, even, odd, rows, sem
):
    vocab = out_ref.shape[0]
    count = rows_ref.shape[0]
    chunk = 256

    def strip(part):
        return pl.ds(pl.multiple_of(part * chunk, chunk), chunk)

    def begin(part, carry):
        even[strip(part), :] = head_ref[strip(part), :].astype(FULL)
        odd[strip(part), :] = jnp.zeros((chunk, odd.shape[1]), FULL)
        return carry

    lax.fori_loop(0, vocab // chunk, begin, 0)

    def widen(part, carry):
        rows[strip(part), :] = rows_ref[strip(part), :].astype(FULL)
        return carry

    lax.fori_loop(0, count // chunk, widen, 0)
    rows[pl.ds(count, 8), :] = jnp.zeros((8, rows.shape[1]), FULL)

    def step(group, carry):
        for member in range(UNROLL):
            at = list_ref[group * UNROLL + member]
            spot = jnp.minimum(ids_ref[jnp.minimum(at, count - 1)], vocab - 1)
            total = even if member % 2 == 0 else odd
            total[pl.ds(spot, 1), :] = total[pl.ds(spot, 1), :] + rows[pl.ds(at, 1), :]
        return carry

    found = list_ref[count + UNROLL]
    lax.fori_loop(0, (found + UNROLL - 1) // UNROLL, step, 0)

    def finish(part, squares):
        value = even[strip(part), :] + odd[strip(part), :]
        even[strip(part), :] = value
        return squares + jnp.sum((value * value).reshape(chunk // 8, 8, -1), axis=0)

    square_ref[...] = lax.fori_loop(
        0, vocab // chunk, finish, jnp.zeros((8, even.shape[1]), FULL)
    )
    store = pltpu.make_async_copy(even, out_ref, sem)
    store.start()
    store.wait()


def spread(ids, listed, rows, head):
    vocab, columns = head.shape
    count = ids.shape[0]
    smem = pl.BlockSpec(memory_space=pltpu.SMEM)
    return pl.pallas_call(
        spread_body,
        in_specs=[smem, smem, VMEM, VMEM],
        out_specs=[ANY, VMEM],
        scratch_shapes=[
            pltpu.VMEM((vocab, columns), FULL),
            pltpu.VMEM((vocab, columns), FULL),
            pltpu.VMEM((count + 8, columns), FULL),
            pltpu.SemaphoreType.DMA,
        ],
        out_shape=[struct((vocab, columns), FULL), struct((8, columns), FULL)],
        compiler_params=pltpu.CompilerParams(vmem_limit_bytes=VMEM_BYTES),
        cost_estimate=pl.CostEstimate(
            flops=count * columns, bytes_accessed=vocab * columns * 8, transcendentals=0
        ),
        name="spread",
    )(ids, listed, rows, head)


def adamw(weight, first_m, second_m, grad, rate, decay):
    first_new = BETA_ONE * first_m + (1.0 - BETA_ONE) * grad
    second_new = BETA_TWO * second_m + (1.0 - BETA_TWO) * grad * grad
    update = (
        first_new
        / (1.0 - BETA_ONE**STEP)
        / (jnp.sqrt(second_new / (1.0 - BETA_TWO**STEP)) + ADAM_EPS)
    )
    return (weight * (1.0 - rate * decay) - rate * update, first_new, second_new)


def cut_columns(values, count):
    rows, columns = values.shape
    return jnp.moveaxis(values.reshape(rows, count, columns // count), 1, 0)


def shifted(parts, axis, step):
    count = lax.axis_size(axis)
    pairs = [(source, (source + step) % count) for source in range(count)]
    return lax.ppermute(parts, axis, pairs)


def per_device(
    tokens,
    picks,
    targets,
    lengths,
    skip,
    embed,
    embed_m,
    embed_v,
    attn_qo,
    attn_qo_mom,
    attn_kv,
    attn_kv_mom,
    ffn,
    ffn_mom,
    gains,
    gains_m,
    gains_v,
):
    wide_count = lax.axis_size("wide")
    narrow_count = lax.axis_size("narrow")
    narrow_spot = lax.axis_index("narrow")
    wide_spot = lax.axis_index("wide")
    seq_len = tokens.shape[1]
    sel = picks.shape[1]
    vocab_rows, columns = embed.shape
    width = columns * wide_count
    own_rows = sel // narrow_count
    tok_rows = seq_len // narrow_count
    all_rows = own_rows + tok_rows
    heads_own = HEADS // narrow_count
    head_cols = heads_own * HD
    repeat = max(1, narrow_count // KVH)
    groups = KVH * repeat // narrow_count
    ffn_rows = ffn.shape[0]
    ffn_size = ffn_rows // narrow_count
    total_rows = wide_count * sel
    lens = lengths[0]
    pick_ids = picks[0]
    keep_layer = (1 - skip[0]).astype(FULL)
    keep_row = jnp.full((1, width), keep_layer)
    lanes = 128

    def box(flat):
        height = -(-flat.shape[0] // (8 * lanes)) * 8
        return jnp.pad(flat, (0, height * lanes - flat.shape[0])).reshape(height, lanes)

    ffn_low = jnp.moveaxis(ffn, 1, 0).astype(LOW)
    ffn_cut = ffn_low.reshape(3, narrow_count, ffn_size, ffn_low.shape[2])
    ffn_cut = jnp.moveaxis(ffn_cut, 1, 0).reshape(narrow_count, 3 * ffn_size, -1)
    kv_own = attn_kv.reshape(columns, -1).astype(LOW)

    where_at = jnp.arange(seq_len, dtype=jnp.int32)
    pick_tokens = jnp.sum(
        jnp.where(pick_ids[:, None] == where_at[None, :], tokens[0][None, :], 0), axis=1
    )
    ints = box(jnp.concatenate([tokens[0], pick_tokens, targets[0]]))
    all_ints, all_gains, kv_part = launch(
        [
            gather_wide(ints),
            gather_both(box(gains.astype(LOW).astype(FULL).reshape(-1))),
            gather_blocks("narrow", kv_own),
        ],
        0,
        "gather_ids",
    )
    kv_part = jnp.moveaxis(kv_part, 0, 1).reshape(columns, -1)
    proj_own = jnp.concatenate([kv_part, attn_qo.reshape(columns, -1).astype(LOW)], axis=1)
    proj = lax.all_gather(proj_own, "wide", axis=0, tiled=True)
    ffn_cut, all_ints = lax.optimization_barrier((ffn_cut, all_ints))
    ffn_pieces = [lax.dynamic_index_in_dim(ffn_cut, narrow_spot, 0, False)] + [
        shifted(
            lax.dynamic_index_in_dim(
                ffn_cut, lax.rem(narrow_spot + step, narrow_count), 0, False
            ),
            "narrow",
            step,
        )
        for step in range(1, narrow_count)
    ]
    gain_size = gains.shape[1]
    gain_w = all_gains.reshape(narrow_count, wide_count, -1)[:, :, : 3 * gain_size]
    gain_w = gain_w.reshape(narrow_count, wide_count, 3, gain_size)
    gain_w = jnp.transpose(gain_w, (2, 1, 0, 3)).reshape(3, width)
    all_ints = all_ints.reshape(wide_count, -1)
    tokens_all = all_ints[:, :seq_len].reshape(wide_count, narrow_count, tok_rows)
    picked_all = all_ints[:, seq_len : seq_len + sel].reshape(wide_count, narrow_count, own_rows)
    targets_all = all_ints[:, seq_len + sel : seq_len + 2 * sel].reshape(-1)
    wanted = jnp.moveaxis(jnp.concatenate([tokens_all, picked_all], axis=2), 1, 0).reshape(-1)
    local_ids = wanted - narrow_spot * vocab_rows
    inside = (local_ids >= 0) & (local_ids < vocab_rows)
    spots = jnp.where(inside, local_ids, vocab_rows)
    found, embed_low, listed = lookup(embed, spots)
    ffn_pieces, found = lax.optimization_barrier((ffn_pieces, found))
    ffn_sub = assemble(ffn_pieces).reshape(3, ffn_size, width)
    ffn_sub, found = lax.optimization_barrier((ffn_sub, found))
    ffn_w = lax.all_gather(ffn_sub, "wide", axis=0)
    found = found.reshape(narrow_count, wide_count * all_rows, columns)
    embed_cut = embed_low.reshape(wide_count, vocab_rows // wide_count, columns)
    table_half = embed_cut.shape[1] // 2
    rows_low = launch([fetch_rows(found, all_rows)], 1, "fetch_rows")[0]

    mom_qo = jnp.moveaxis(attn_qo_mom, 1, 0)
    mom_kv = jnp.moveaxis(attn_kv_mom, 1, 0)
    mom_ffn = jnp.moveaxis(ffn_mom, 1, 0)
    slot_rows, slot_cols = mom_ffn.shape[1:]

    block_rows, q_size = mom_qo.shape[1:]
    kv_size = mom_kv.shape[2]
    half_rows = block_rows // 2
    kv_box = jnp.moveaxis(mom_kv.reshape(4, half_rows, kv_size), 0, 1).reshape(half_rows, -1)
    small_box = jnp.concatenate([mom_qo.reshape(2 * block_rows, q_size), kv_box])
    small_box = jnp.pad(small_box, ((0, slot_rows - small_box.shape[0]), (0, 0)))
    mom_parts = jnp.concatenate([mom_ffn, small_box[None]]).astype(LOW)

    seg_all, cosine_all, sine_all = angles_at(lens, where_at)
    cosine_all, sine_all = wide_angles(cosine_all, sine_all)
    seg_mine, cosine, sine = angles_at(lens, pick_ids)
    cosine, sine = wide_angles(cosine, sine)

    def tok_part(angles):
        return lax.dynamic_slice_in_dim(angles, narrow_spot * tok_rows, tok_rows, 0)

    by_head, normed_tok = make_heads(
        rows_low, gain_w[0:1], proj, tok_part(cosine_all), tok_part(sine_all), groups, repeat
    )
    own_head, start_low, tok_cols, table_low = launch(
        [
            swap_blocks("narrow", by_head),
            gather_blocks("narrow", rows_low[tok_rows:]),
            split_columns("wide", normed_tok),
            join_columns("wide", embed_cut[:, table_half:]),
        ],
        2,
        "trade_heads",
    )
    start_low, ffn_w = lax.optimization_barrier((start_low, ffn_w))
    start_low = start_low.reshape(sel, width)
    queries, probs, mixed, attn_part, normed, early_part = attend(
        start_low,
        gain_w,
        proj,
        own_head,
        cosine,
        sine,
        seg_mine[:, None],
        seg_all[None, :],
        pick_ids[:, None],
    )
    early = lax.all_gather(early_part, "wide", axis=0, tiled=True)
    start_own = rows_low[tok_rows:].astype(FULL)
    middle, inner, mixed_wide, pick_cols = launch(
        [
            settle(
                attn_part,
                start_own,
                start_own,
                jnp.ones((1, width), FULL),
                gain_w[1:2],
            ),
            gather_wide(mixed),
            split_columns("wide", normed),
        ],
        3,
        "settle_middle",
    )
    inner = inner.reshape(sel, width)
    inner_all = lax.all_gather(inner, "wide", axis=0, tiled=True)
    gate, up, hidden, fed = feed(inner, ffn_w)
    final_own, late_part, table_top = launch(
        [
            settle(fed, middle, start_own, keep_row, gain_w[2:3]),
            join_columns("wide", embed_cut[:, :table_half]),
        ],
        4,
        "settle_late",
    )
    table_own = jnp.concatenate([table_top, table_low])

    table_count = table_own.shape[0]
    local_target = targets_all - (narrow_spot * vocab_rows + wide_spot * table_count)
    has_target = jnp.arange(table_count, dtype=jnp.int32)[:, None] == local_target[None, :]
    counted = (targets_all >= 0).astype(FULL)
    loss_count = jnp.sum(counted)

    def exit_logits(features):
        logits = dot(table_own, features, 1, 1)
        peak = jnp.max(logits, axis=0)
        total = jnp.sum(jnp.exp(logits - peak[None, :]), axis=0)
        picked = jnp.sum(jnp.where(has_target, logits, 0.0), axis=0)
        return logits, jnp.stack([peak, total, picked])

    half = slot_rows // 2
    late, mom_top, early_logits, early_stats = launch(
        [
            gather_wide(late_part.reshape(sel, width)),
            swap_turned(mom_parts[:, :half]),
            exit_stats(early, table_own, local_target[None, :]),
        ],
        5,
        "gather_late",
    )
    late = late.reshape(total_rows, width)
    late_logits, late_stats = exit_logits(late)
    stats = jnp.concatenate([early_stats, late_stats], axis=1).reshape(3, 8, -1)
    stats = launch([combine(stats, merge_stats)], 6, "combine_stats")[0]
    stats, inner_all = lax.optimization_barrier((stats, inner_all))
    stats = stats.reshape(3, -1)
    log_norms = stats[0] + jnp.log(stats[1])
    losses = log_norms - stats[2]
    loss_sum = jnp.sum(
        counted * (EXIT_EARLY * losses[:total_rows] + EXIT_LAST * losses[total_rows:])
    )

    def exit_back(logits, log_norm, weight):
        grad_logits = (
            (jnp.exp(logits - log_norm[None, :]) - has_target.astype(FULL))
            * (weight * counted)[None, :]
        ).astype(LOW)
        return dot(grad_logits, table_own, 0, 0).astype(LOW), grad_logits

    late_back, late_grad = exit_back(late_logits, log_norms[total_rows:], EXIT_LAST)
    grad_late, mom_low = launch(
        [sum_wide(late_back), swap_turned(mom_parts[:, half:])], 7, "sum_late"
    )
    early_norms, grad_late = lax.optimization_barrier((log_norms[:total_rows], grad_late))
    early_back, early_grad = exit_back(early_logits, early_norms, EXIT_EARLY)
    mom_owned = jnp.concatenate([mom_top, mom_low], axis=1)

    grad_early = lax.psum_scatter(early_back, "wide", scatter_dimension=0, tiled=True)
    grad_final, gain_late, grad_out = launch(
        [
            settle_back(
                grad_late.astype(LOW),
                final_own,
                jnp.zeros_like(final_own),
                keep_row,
                gain_w[2:3],
            ),
        ],
        8,
        "back_late",
    )
    grad_layer = grad_final * keep_layer
    grad_out = grad_out.reshape(sel, width)
    out_all = lax.all_gather(grad_out, "wide", axis=0, tiled=True)
    acts, fed_back = feed_back(grad_out, ffn_w, gate, up, hidden)
    grad_mid, gain_mid, grad_branch, acts = launch(
        [
            settle_back(fed_back, middle, grad_layer, keep_row, gain_w[1:2]),
            swap_blocks("wide", acts),
        ],
        9,
        "back_middle",
    )
    acts = jnp.moveaxis(acts, 1, 0).reshape(3, total_rows, ffn_size)
    grad_branch, grad_early = lax.optimization_barrier((grad_branch, grad_early))
    grad_branch = grad_branch.reshape(sel, width)

    kv_parts, grad_queries, pick_part = attend_back(
        grad_branch, proj, own_head, queries, probs, cosine, sine, cosine_all, sine_all
    )
    grad_kv, grad_pick, grad_early, queries_wide, branch_cols, grad_head, _ = launch(
        [
            swap_blocks("narrow", kv_parts),
            sum_narrow(pick_part),
            sum_narrow(grad_early),
            gather_wide(grad_queries),
            split_columns("wide", grad_branch),
            product([early_grad, late_grad], [early, late], True, 1),
        ],
        10,
        "trade_grads",
    )
    grad_kv, out_all = lax.optimization_barrier((grad_kv, out_all))
    grad_base = grad_mid + grad_final * (1.0 - keep_layer)
    grad_rows, gain_attn, gain_early, grad_kv = rows_back(
        rows_low, gain_w, proj, grad_kv, grad_pick, grad_early, grad_base, repeat
    )
    rights = (inner_all, inner_all, out_all)
    summed_qo = jnp.stack(
        [
            jnp.einsum("wtc,wtf->cf", pick_cols, queries_wide, preferred_element_type=FULL),
            jnp.einsum("wtc,wtf->cf", branch_cols, mixed_wide, preferred_element_type=FULL),
        ]
    )
    grad_rows, acts_owned, kv_wide, head_cols_all, *grad_ffn, ffn_squares = launch(
        [
            return_rows(grad_rows),
            swap_owned(acts, 5),
            later(gather_wide(grad_kv, 3), 2),
            later(split_columns("wide", grad_head, 3), 2),
            product([acts[j] for j in range(3)], rights, False),
        ],
        11,
        "return_rows",
    )
    turn = lax.rem(wide_spot, 2)
    grad_kv_w = jnp.einsum(
        "wtc,wtf->cf", tok_cols, kv_wide, preferred_element_type=FULL
    ).reshape(columns, narrow_count, 2, kv_size)
    grad_kv_w = jnp.moveaxis(grad_kv_w, 0, 2)
    summed_kv = lax.psum_scatter(grad_kv_w, "narrow", scatter_dimension=0, tiled=True)[0]
    summed_table, table_squares = spread(
        spots, listed, grad_rows.reshape(-1, columns), head_cols_all.reshape(vocab_rows, columns)
    )

    squares = (
        jnp.sum(summed_qo * summed_qo)
        + jnp.sum(summed_kv * summed_kv)
        + jnp.sum(ffn_squares)
        + jnp.sum(table_squares)
    )
    sums = jnp.stack(
        [gain_attn[0], gain_mid[0], gain_early[0] + gain_late[0], jnp.full((width,), squares)]
    )
    matrix = jnp.minimum(lax.rem(narrow_spot + narrow_count - turn, narrow_count), 2)
    right = jnp.where(matrix == 2, out_all, inner_all)
    sums, kv_owned, qo_owned, *owned, _ = launch(
        [
            combine(sums.reshape(4, 8, -1), add_two),
            send_owner(summed_kv.astype(LOW).reshape(2 * block_rows, kv_size)),
            later(send_owner(summed_qo.astype(LOW).reshape(2 * columns, q_size)), 1),
            product([acts_owned[at] for at in range(narrow_count)], [right], False),
        ],
        12,
        "combine_sums",
    )
    sums = sums.reshape(4, width)
    summed_gain = lax.dynamic_slice_in_dim(
        sums[:3], (wide_spot * narrow_count + narrow_spot) * gain_size, gain_size, 1
    )
    square_total = sums[3, 0] + jnp.sum(sums[:3] * sums[:3])
    grad_norm = jnp.sqrt(square_total) / loss_count
    factor = jnp.minimum(1.0, CLIP_NORM / (grad_norm + 1e-06)) / loss_count

    final_parts, factor = lax.optimization_barrier((jnp.stack(grad_ffn), factor))
    size = width // narrow_count

    def final_piece(spot):
        return lax.dynamic_slice_in_dim(final_parts, spot * size, size, 2)

    pieces = [final_piece(narrow_spot)] + [
        shifted(final_piece(lax.rem(narrow_spot + step, narrow_count)), "narrow", step)
        for step in range(1, narrow_count)
    ]
    directions = newton(
        factor, mom_owned, jnp.stack(owned), qo_owned, kv_owned
    )
    directions, pieces, ffn, factor = lax.optimization_barrier(
        (directions, pieces, ffn, factor)
    )
    summed_ffn = jnp.zeros((3, narrow_count, ffn_size, size), LOW)
    for step, piece in enumerate(pieces):
        source = lax.rem(narrow_spot - step + narrow_count, narrow_count)
        summed_ffn = lax.dynamic_update_index_in_dim(summed_ffn, piece, source, 1)
    summed_ffn = summed_ffn.reshape(3, ffn_rows, size).astype(FULL)
    received = [lax.dynamic_index_in_dim(directions, narrow_spot, 0, False)] + [
        shifted(
            lax.dynamic_index_in_dim(
                directions, lax.rem(narrow_spot + step, narrow_count), 0, False
            ),
            "narrow",
            step,
        )
        for step in range(1, narrow_count)
    ]

    def direction_of(matrix):
        step = lax.rem(narrow_spot - matrix - turn + 2 * narrow_count, narrow_count)
        result = received[0]
        for at in range(1, narrow_count):
            result = jnp.where(step == at, received[at], result)
        return result

    dir_ffn = jnp.stack([direction_of(matrix) for matrix in range(3)]).astype(FULL)
    small = direction_of(3).astype(FULL)
    dir_qo = small[: 2 * block_rows].reshape(mom_qo.shape)
    dir_kv = small[2 * block_rows : 2 * block_rows + half_rows].reshape(half_rows, 4, kv_size)
    dir_kv = jnp.moveaxis(dir_kv, 1, 0).reshape(mom_kv.shape)

    embed_new, embed_m_new, embed_v_new = adamw(
        embed, embed_m, embed_v, summed_table * factor, RATE_ADAM, WEIGHT_DECAY
    )
    gains_new, gains_m_new, gains_v_new = adamw(
        gains, gains_m, gains_v, summed_gain * factor, RATE_GAIN, 0.0
    )

    def mom_next(mom, grad):
        return MOMENTUM * mom + jnp.moveaxis(grad * factor, 0, 1)

    shrink = 1.0 - RATE_MUON * WEIGHT_DECAY

    def weight_next(weight, direction):
        return weight * shrink - RATE_MUON * jnp.moveaxis(direction, 0, 1)

    return (
        loss_sum,
        loss_count,
        grad_norm,
        embed_new,
        embed_m_new,
        embed_v_new,
        weight_next(attn_qo, dir_qo),
        mom_next(attn_qo_mom, summed_qo),
        weight_next(attn_kv, dir_kv),
        mom_next(attn_kv_mom, summed_kv),
        weight_next(ffn, dir_ffn),
        mom_next(ffn_mom, summed_ffn),
        gains_new,
        gains_m_new,
        gains_v_new,
    )


def solution(mesh):
    by_pack = P("wide", None)
    table = P("narrow", "wide")
    layer = P("wide", None, "narrow")
    gain = P(None, ("wide", "narrow"))
    return jax.shard_map(
        per_device,
        mesh=mesh,
        in_specs=(by_pack,) * 4 + (P("wide"),) + (table,) * 3 + (layer,) * 6 + (gain,) * 3,
        out_specs=(P(),) * 3 + (table,) * 3 + (layer,) * 6 + (gain,) * 3,
        check_vma=False,
    )
```

```python
import functools

import jax
import jax.numpy as jnp
from jax import lax
from jax.experimental import pallas as pl
from jax.experimental.pallas import tpu as pltpu
from jax.sharding import PartitionSpec as P

HEADS = 16
HD = 128
KVH = 4
NS_STEPS = 5
STEP = 10


NORM_EPS = 1e-05
ROPE_BASE = 10000.0
EXIT_EARLY = 0.25
EXIT_LAST = 1.0
CLIP_NORM = 0.02
BETA_ONE = 0.9
BETA_TWO = 0.95
ADAM_EPS = 1e-08
RATE_ADAM = 0.02
RATE_GAIN = 0.3
RATE_MUON = 0.3
WEIGHT_DECAY = 0.1
MOMENTUM = 0.95
NEWTON_A = 3.4445
NEWTON_B = -4.775
NEWTON_C = 2.0315
MASKED = -1e30
LOW = jnp.bfloat16
FULL = jnp.float32
BOTH = ("wide", "narrow")
UNROLL = 16
VMEM_BYTES = 56 * 1024 * 1024


def dot(first, second, first_dim, second_dim):
    return lax.dot_general(
        first, second, (((first_dim,), (second_dim,)), ((), ())), preferred_element_type=FULL
    )


def norm_rows(values, gain_row):
    return (
        values * lax.rsqrt(jnp.mean(values * values, axis=-1, keepdims=True) + NORM_EPS) * gain_row
    )


def segments_at(lens, where_at):
    ends = jnp.cumsum(lens)
    return jnp.sum((where_at[:, None] >= ends[None, :]).astype(jnp.int32), axis=1)


def angles_at(lens, where_at):
    segment = segments_at(lens, where_at)
    starts = jnp.cumsum(lens) - lens
    member = segment[:, None] == jnp.arange(lens.shape[0], dtype=jnp.int32)[None, :]
    begin = jnp.sum(jnp.where(member, starts[None, :], 0), axis=1)
    offset_pos = (where_at - begin).astype(FULL)
    inverse = ROPE_BASE ** (-2.0 * jnp.arange(HD // 2, dtype=FULL) / HD)
    angle = offset_pos[:, None] * inverse[None, :]
    return (segment, jnp.cos(angle), jnp.sin(angle))


MESH = pl.DeviceIdType.MESH
ANY = pl.BlockSpec(memory_space=pl.ANY)
VMEM = pl.BlockSpec(memory_space=pltpu.VMEM)


def others(axis, count):
    me = lax.axis_index(axis)
    return [{axis: lax.rem(me + step, count)} for step in range(1, count)]


def push(source, target, send, receive, device):
    return pltpu.make_async_remote_copy(
        src_ref=source,
        dst_ref=target,
        send_sem=send,
        recv_sem=receive,
        device_id=device,
        device_id_type=MESH,
    )


def arrived(block, send, receive, device):
    push(block, block, send, receive, device).wait_recv()


def like(values):
    return jax.ShapeDtypeStruct(values.shape, values.dtype)


def struct(shape, dtype):
    return jax.ShapeDtypeStruct(shape, dtype)


def sems(*shape):
    return pltpu.SemaphoreType.DMA(shape)


class Task:
    def __init__(self, inputs, outputs, scratch, steps, place_in, place_out, axes):
        self.inputs, self.outputs, self.scratch, self.steps = inputs, outputs, scratch, steps
        self.place_in = [place_in] * len(inputs)
        self.place_out = [place_out] * len(outputs)
        self.axes = axes


def launch(tasks, ident, name):
    axes = sorted(set(axis for task in tasks for axis in task.axes))
    inputs = [a for task in tasks for a in task.inputs]
    outputs = [a for task in tasks for a in task.outputs]
    scratch = [a for task in tasks for a in task.scratch]

    def body(*refs):
        refs = list(refs)
        ins = refs[: len(inputs)]
        outs = refs[len(inputs) : len(inputs) + len(outputs)]
        extra = refs[len(inputs) + len(outputs) :]
        barrier = pltpu.get_barrier_semaphore()
        targets = [device for axis in axes for device in others(axis, lax.axis_size(axis))]
        for device in targets:
            pl.semaphore_signal(barrier, inc=1, device_id=device, device_id_type=MESH)
        pl.semaphore_wait(barrier, len(targets))
        live = []
        for task in tasks:
            counts = (len(task.inputs), len(task.outputs), len(task.scratch))
            live.append(task.steps(ins[: counts[0]], outs[: counts[1]], extra[: counts[2]]))
            ins, outs, extra = ins[counts[0] :], outs[counts[1] :], extra[counts[2] :]
        while live:
            live = [steps for steps in live if next(steps, 0) is None]

    size = sum(a.size * a.dtype.itemsize for a in list(inputs) + list(outputs))
    return pl.pallas_call(
        body,
        out_shape=outputs,
        in_specs=[place for task in tasks for place in task.place_in],
        out_specs=[place for task in tasks for place in task.place_out],
        scratch_shapes=scratch,
        compiler_params=pltpu.CompilerParams(
            collective_id=ident, has_side_effects=True, vmem_limit_bytes=VMEM_BYTES
        ),
        cost_estimate=pl.CostEstimate(flops=0, bytes_accessed=size // 8, transcendentals=0),
        name=name,
    )(*inputs)


def later(task, turns):
    begin = task.steps

    def steps(ins, outs, scratch):
        for turn in range(turns):
            yield
        yield from begin(ins, outs, scratch)

    task.steps = steps
    return task


def gather_wide(values, patience=1):
    count = lax.axis_size("wide")
    chips = count // 2

    def steps(ins, outs, scratch):
        (x_ref,), (out_ref,), (send, receive, local) = ins, outs, scratch
        me = lax.axis_index("wide")
        mate = me + 1 - 2 * lax.rem(me, 2)
        peers = [lax.rem(me + 2 * step, count) for step in range(1, chips)] + [mate]
        first = []
        for step, peer in enumerate(peers):
            copy = push(x_ref, out_ref.at[me], send.at[step], receive.at[me], {"wide": peer})
            copy.start()
            first.append(copy)
        keep = pltpu.make_async_copy(x_ref, out_ref.at[me], local)
        keep.start()
        for turn in range(patience):
            yield
        second = []
        for step in range(1, chips):
            source = lax.rem(me - 2 * step + count, count)
            block = out_ref.at[source]
            arrived(block, send.at[0], receive.at[source], {"wide": mate})
            copy = push(
                block, block, send.at[chips + step - 1], receive.at[source], {"wide": mate}
            )
            copy.start()
            second.append(copy)
        yield
        for step in range(chips):
            source = lax.rem(mate - 2 * step + count, count)
            arrived(out_ref.at[source], send.at[0], receive.at[source], {"wide": mate})
        for copy in first + second:
            copy.wait_send()
        keep.wait()

    shape = struct((count,) + values.shape, values.dtype)
    return Task(
        [values], [shape], [sems(count - 1), sems(count), sems()], steps, ANY, ANY, ["wide"]
    )


def trade(axis, values, source_of, target_of, shape, patience=2):
    count = lax.axis_size(axis)

    def steps(ins, outs, scratch):
        (x_ref,), (out_ref,), (send, receive, local) = ins, outs, scratch
        me = lax.axis_index(axis)
        copies = []
        for step in range(1, count):
            peer = lax.rem(me + step, count)
            copy = push(
                source_of(x_ref, peer),
                target_of(out_ref, me),
                send.at[step - 1],
                receive.at[me],
                {axis: peer},
            )
            copy.start()
            copies.append(copy)
        keep = pltpu.make_async_copy(source_of(x_ref, me), target_of(out_ref, me), local)
        keep.start()
        for turn in range(patience):
            yield
        for step in range(1, count):
            source = lax.rem(me - step + count, count)
            arrived(
                target_of(out_ref, source), send.at[0], receive.at[source], {axis: source}
            )
        for copy in copies:
            copy.wait_send()
        keep.wait()

    return Task(
        [values],
        [struct(shape, values.dtype)],
        [sems(count - 1), sems(count), sems()],
        steps,
        ANY,
        ANY,
        [axis],
    )


def block_at(ref, spot):
    return ref.at[spot]


def whole_at(ref, spot):
    return ref


def columns_of(size):
    def at(ref, spot):
        return ref.at[:, pl.ds(pl.multiple_of(spot * size, size), size)]

    return at


def turned(ref, spot):
    count = lax.axis_size("narrow")
    matrix = lax.rem(spot + count - lax.rem(lax.axis_index("wide"), 2), count)
    return ref.at[jnp.minimum(matrix, 3)]


def swap_turned(values, patience=2):
    shape = (lax.axis_size("narrow"),) + values.shape[1:]
    return trade("narrow", values, turned, block_at, shape, patience)


def product(lefts, rights, dim, order):
    count, rows = len(order), lefts[0].shape[-1 if dim == 0 else -2]
    columns = rights[0].shape[1]
    block = min(512, columns)

    def steps(ins, outs, scratch):
        left_refs, right_refs = ins[: len(lefts)], ins[len(lefts) :]
        result_ref, square_ref = outs
        square_ref[...] = jnp.zeros_like(square_ref)

        def left_of(member):
            return left_refs[0][member] if lefts[0].ndim == 3 else left_refs[member][...]

        for at, members in enumerate(order):

            def strip(part, carry):
                spot = pl.ds(pl.multiple_of(part * block, block), block)
                value = jnp.zeros((rows, block), FULL)
                for left, right in members:
                    value = value + dot(left_of(left), right_refs[right][:, spot], dim, 0)
                result_ref[at, :, spot] = value.astype(LOW)
                square_ref[:, spot] = square_ref[:, spot] + jnp.sum(
                    value * value, axis=0, keepdims=True
                )
                return carry

            lax.fori_loop(0, columns // block, strip, 0)
            yield

    return Task(
        list(lefts) + list(rights),
        [struct((count, rows, columns), LOW), struct((1, columns), FULL)],
        [],
        steps,
        VMEM,
        VMEM,
        [],
    )


def exit_stats(features, table, targets):
    rows, vocab = features.shape[0], table.shape[0]
    block = min(256, vocab)

    def steps(ins, outs, scratch):
        features_ref, table_ref, targets_ref = ins
        logits_ref, stats_ref = outs

        def strip(part):
            return pl.ds(pl.multiple_of(part * block, block), block)

        def over(function, start):
            return lax.fori_loop(0, vocab // block, function, start)

        def fill(part, peak):
            logits = dot(table_ref[strip(part), :], features_ref[...], 1, 1)
            logits_ref[strip(part), :] = logits
            return jnp.maximum(peak, jnp.max(logits, axis=0, keepdims=True))

        peak = over(fill, jnp.full((1, rows), MASKED, FULL))
        lines = lax.broadcasted_iota(jnp.int32, (block, rows), 0)

        def add(part, carry):
            total, picked = carry
            logits = logits_ref[strip(part), :]
            hit = lines + part * block == targets_ref[...]
            return (
                total + jnp.sum(jnp.exp(logits - peak), axis=0, keepdims=True),
                picked + jnp.sum(jnp.where(hit, logits, 0.0), axis=0, keepdims=True),
            )

        zero = jnp.zeros((1, rows), FULL)
        total, picked = over(add, (zero, zero))
        stats_ref[0:1, :] = peak
        stats_ref[1:2, :] = total
        stats_ref[2:3, :] = picked
        yield

    return Task(
        [features, table, targets],
        [struct((vocab, rows), FULL), struct((3, rows), FULL)],
        [],
        steps,
        VMEM,
        VMEM,
        [],
    )


def swap_owned(values, patience):
    count = lax.axis_size("narrow")

    def steps(ins, outs, scratch):
        (x_ref,), (out_ref,), (send, receive, local) = ins, outs, scratch
        me = lax.axis_index("narrow")
        turn = lax.rem(lax.axis_index("wide"), 2)

        def matrix_of(device):
            return lax.rem(device + count - turn, count)

        def copy_to(step):
            peer = lax.rem(me + step, count)
            return push(
                x_ref.at[jnp.minimum(matrix_of(peer), 2)],
                out_ref.at[me],
                send.at[step - 1],
                receive.at[me],
                {"narrow": peer},
            )

        def keep():
            return pltpu.make_async_copy(
                x_ref.at[jnp.minimum(matrix_of(me), 2)], out_ref.at[me], local
            )

        keep().start()
        for step in range(1, count):

            @pl.when(matrix_of(lax.rem(me + step, count)) < 3)
            def _():
                copy_to(step).start()

        for turn_at in range(patience):
            yield

        @pl.when(matrix_of(me) < 3)
        def _():
            for step in range(1, count):
                source = lax.rem(me - step + count, count)
                arrived(out_ref.at[source], send.at[0], receive.at[source], {"narrow": source})

        for step in range(1, count):

            @pl.when(matrix_of(lax.rem(me + step, count)) < 3)
            def _():
                copy_to(step).wait_send()

        keep().wait()

    return Task(
        [values],
        [struct((count,) + values.shape[1:], values.dtype)],
        [sems(count - 1), sems(count), sems()],
        steps,
        ANY,
        ANY,
        ["narrow"],
    )


def send_owner(values):
    count = lax.axis_size("narrow")

    def steps(ins, outs, scratch):
        (x_ref,), (out_ref,), (send, receive, local) = ins, outs, scratch
        me = lax.axis_index("narrow")
        owner = lax.rem(3 + lax.rem(lax.axis_index("wide"), 2), count)
        keep = pltpu.make_async_copy(x_ref, out_ref.at[me], local)
        keep.start()

        def to_owner():
            return push(x_ref, out_ref.at[me], send.at[0], receive.at[me], {"narrow": owner})

        @pl.when(me != owner)
        def _():
            to_owner().start()

        yield
        yield

        @pl.when(me != owner)
        def _():
            to_owner().wait_send()

        @pl.when(me == owner)
        def _():
            for step in range(1, count):
                source = lax.rem(owner + step, count)
                arrived(out_ref.at[source], send.at[0], receive.at[source], {"narrow": source})

        keep.wait()

    return Task(
        [values],
        [struct((count,) + values.shape, values.dtype)],
        [sems(1), sems(count), sems()],
        steps,
        ANY,
        ANY,
        ["narrow"],
    )


def swap_blocks(axis, values):
    return trade(axis, values, block_at, block_at, values.shape)


def gather_blocks(axis, values):
    shape = (lax.axis_size(axis),) + values.shape
    return trade(axis, values, whole_at, block_at, shape)


def split_columns(axis, values, patience=2):
    count = lax.axis_size(axis)
    rows, size = values.shape[0], values.shape[1] // count
    return trade(axis, values, columns_of(size), block_at, (count, rows, size), patience)


def join_columns(axis, values):
    count, rows, size = values.shape
    return trade(axis, values, block_at, columns_of(size), (rows, count * size))


def collect(count, parts_ref, slots, send, receive):
    me = lax.axis_index("narrow")
    copies = []
    for step in range(1, count):
        peer = lax.rem(me + step, count)
        copy = push(
            parts_ref.at[peer],
            slots.at[me],
            send.at[step - 1],
            receive.at[me],
            {"narrow": peer},
        )
        copy.start()
        copies.append(copy)
    return copies


def collected(count, parts_ref, slots, send, receive):
    me = lax.axis_index("narrow")
    total = parts_ref[me].astype(FULL)
    for step in range(1, count):
        source = lax.rem(me - step + count, count)
        arrived(slots.at[source], send.at[0], receive.at[source], {"narrow": source})
        total = total + slots[source].astype(FULL)
    return total


def share(count, low, all_ref, send, receive):
    me = lax.axis_index("narrow")
    all_ref[me] = low
    copies = []
    for step in range(1, count):
        peer = lax.rem(me + step, count)
        copy = push(
            all_ref.at[me], all_ref.at[me], send.at[step - 1], receive.at[me], {"narrow": peer}
        )
        copy.start()
        copies.append(copy)
    return copies


def shared(count, all_ref, send, receive):
    me = lax.axis_index("narrow")
    for step in range(1, count):
        source = lax.rem(me - step + count, count)
        arrived(all_ref.at[source], send.at[0], receive.at[source], {"narrow": source})


def narrow_sems(count):
    return [sems(count - 1), sems(count)]


def settle(partial, base, other, keep_row, gain_row):
    count = lax.axis_size("narrow")
    rows, width = base.shape

    def steps(ins, outs, scratch):
        parts_ref, base_ref, other_ref, keep_ref, gain_ref = ins
        own_ref, all_ref = outs
        slots, send, receive, send_all, receive_all = scratch
        copies = collect(count, parts_ref, slots, send, receive)
        yield
        total = collected(count, parts_ref, slots, send, receive)
        total = jnp.where(keep_ref[...] > 0, total + base_ref[...], other_ref[...])
        own_ref[...] = total
        low = norm_rows(total, gain_ref[...]).astype(LOW)
        copies = copies + share(count, low, all_ref, send_all, receive_all)
        yield
        shared(count, all_ref, send_all, receive_all)
        for copy in copies:
            copy.wait_send()

    return Task(
        [partial.reshape(count, rows, width), base, other, keep_row, gain_row],
        [struct((rows, width), FULL), struct((count, rows, width), LOW)],
        [pltpu.VMEM((count, rows, width), partial.dtype)]
        + narrow_sems(count)
        + narrow_sems(count),
        steps,
        VMEM,
        VMEM,
        ["narrow"],
    )


def settle_back(partial, values, add, keep_row, gain_row):
    count = lax.axis_size("narrow")
    rows, width = values.shape

    def steps(ins, outs, scratch):
        parts_ref, values_ref, add_ref, keep_ref, gain_ref = ins
        own_ref, gain_grad_ref, all_ref = outs
        slots, send, receive, send_all, receive_all = scratch
        copies = collect(count, parts_ref, slots, send, receive)
        yield
        grad = collected(count, parts_ref, slots, send, receive)
        held = values_ref[...]
        root = lax.rsqrt(jnp.mean(held * held, axis=-1, keepdims=True) + NORM_EPS)
        scaled = gain_ref[...] * grad
        inner = jnp.mean(held * scaled, axis=-1, keepdims=True)
        own = add_ref[...] + root * scaled - held * (root * root * root * inner)
        gain_grad_ref[...] = jnp.sum(held * root * grad, axis=0, keepdims=True)
        own_ref[...] = own
        low = (own * keep_ref[...]).astype(LOW)
        copies = copies + share(count, low, all_ref, send_all, receive_all)
        yield
        shared(count, all_ref, send_all, receive_all)
        for copy in copies:
            copy.wait_send()

    return Task(
        [partial.reshape(count, rows, width), values, add, keep_row, gain_row],
        [
            struct((rows, width), FULL),
            struct((1, width), FULL),
            struct((count, rows, width), LOW),
        ],
        [pltpu.VMEM((count, rows, width), partial.dtype)]
        + narrow_sems(count)
        + narrow_sems(count),
        steps,
        VMEM,
        VMEM,
        ["narrow"],
    )


def sum_narrow(partial):
    count = lax.axis_size("narrow")
    rows, width = partial.shape[0] // count, partial.shape[1]

    def steps(ins, outs, scratch):
        (parts_ref,), (own_ref,), (slots, send, receive) = ins, outs, scratch
        copies = collect(count, parts_ref, slots, send, receive)
        yield
        yield
        own_ref[...] = collected(count, parts_ref, slots, send, receive)
        for copy in copies:
            copy.wait_send()

    return Task(
        [partial.reshape(count, rows, width)],
        [struct((rows, width), FULL)],
        [pltpu.VMEM((count, rows, width), partial.dtype)] + narrow_sems(count),
        steps,
        VMEM,
        VMEM,
        ["narrow"],
    )


def fetch_rows(found, rows):
    deep, wide = lax.axis_size("narrow"), lax.axis_size("wide")
    columns = found.shape[2]

    def steps(ins, outs, scratch):
        (found_ref,), (out_ref,) = ins, outs
        rightward, leftward, final = scratch[:3]
        send_right, receive_right, send_left, receive_left = scratch[3:7]
        send_wide, receive_wide, local = scratch[7:]
        spot = lax.axis_index("narrow")
        me = lax.axis_index("wide")

        def right_copy(part, source):
            return push(
                source,
                rightward.at[part],
                send_right.at[part],
                receive_right.at[part],
                {"narrow": lax.rem(spot + 1, deep)},
            )

        def left_copy(part, source):
            return push(
                source,
                leftward.at[part],
                send_left.at[part],
                receive_left.at[part],
                {"narrow": lax.rem(spot + deep - 1, deep)},
            )

        for step in range(deep - 1):
            right, left = deep - 1 - step, step

            @pl.when((spot == 0) & (right > 0))
            def _():
                right_copy(right, found_ref.at[right]).start()

            @pl.when((spot == deep - 1) & (left < deep - 1))
            def _():
                left_copy(left, found_ref.at[left]).start()

        yield
        for step in range(deep - 1):
            right, left = deep - 1 - step, step

            def pass_right():
                right_copy(right, rightward.at[right]).wait_recv()
                rightward[right] = rightward[right] + found_ref[right]
                right_copy(right, rightward.at[right]).start()

            pl.when((spot > 0) & (right > spot) & (2 * spot < deep))(pass_right)

            @pl.when((spot < deep - 1) & (left < spot))
            def _():
                left_copy(left, leftward.at[left]).wait_recv()
                leftward[left] = leftward[left] + found_ref[left]
                left_copy(left, leftward.at[left]).start()

            pl.when((right > spot) & (2 * spot >= deep))(pass_right)

        final[...] = found_ref[spot]

        @pl.when(spot > 0)
        def _():
            right_copy(spot, rightward.at[spot]).wait_recv()
            final[...] = final[...] + rightward[spot]

        @pl.when(spot < deep - 1)
        def _():
            left_copy(spot, leftward.at[spot]).wait_recv()
            final[...] = final[...] + leftward[spot]

        def rows_for(device):
            return final.at[pl.ds(pl.multiple_of(device * rows, rows), rows)]

        def columns_from(device):
            return columns_of(columns)(out_ref, device)

        copies = []
        for step in range(1, wide):
            peer = lax.rem(me + step, wide)
            copy = push(
                rows_for(peer),
                columns_from(me),
                send_wide.at[step - 1],
                receive_wide.at[me],
                {"wide": peer},
            )
            copy.start()
            copies.append(copy)
        keep = pltpu.make_async_copy(rows_for(me), columns_from(me), local)
        keep.start()
        yield
        for step in range(1, wide):
            source = lax.rem(me - step + wide, wide)
            arrived(
                columns_from(source), send_wide.at[0], receive_wide.at[source], {"wide": source}
            )
        yield
        for copy in copies:
            copy.wait_send()
        keep.wait()
        for step in range(deep - 1):
            right, left = deep - 1 - step, step

            @pl.when(right > spot)
            def _():
                right_copy(right, found_ref.at[right]).wait_send()

            @pl.when(left < spot)
            def _():
                left_copy(left, found_ref.at[left]).wait_send()

    task = Task(
        [found],
        [struct((rows, wide * columns), found.dtype)],
        [pltpu.VMEM(found.shape, found.dtype)] * 2
        + [pltpu.VMEM(found.shape[1:], found.dtype)]
        + [sems(deep)] * 4
        + [sems(wide - 1), sems(wide), sems()],
        steps,
        VMEM,
        ANY,
        ["narrow", "wide"],
    )
    return task


def return_rows(rows):
    deep, wide = lax.axis_size("narrow"), lax.axis_size("wide")
    count, width = rows.shape
    columns = width // wide

    def steps(ins, outs, scratch):
        (rows_ref,), (out_ref,) = ins, outs
        send_right, send_left, receive_deep, send_wide, receive_wide, local = scratch
        spot = lax.axis_index("narrow")
        me = lax.axis_index("wide")
        part_of = functools.partial(columns_of(columns), rows_ref)

        def landing(device):
            return out_ref.at[spot, pl.ds(pl.multiple_of(device * count, count), count)]

        copies = []
        for step in range(1, wide):
            peer = lax.rem(me + step, wide)
            copy = push(
                part_of(peer),
                landing(me),
                send_wide.at[step - 1],
                receive_wide.at[me],
                {"wide": peer},
            )
            copy.start()
            copies.append(copy)
        keep = pltpu.make_async_copy(part_of(me), landing(me), local)
        keep.start()
        yield
        for step in range(1, wide):
            source = lax.rem(me - step + wide, wide)
            arrived(landing(source), send_wide.at[0], receive_wide.at[source], {"wide": source})
        keep.wait()

        def right_copy(part):
            return push(
                out_ref.at[part],
                out_ref.at[part],
                send_right.at[part],
                receive_deep.at[part],
                {"narrow": lax.rem(spot + 1, deep)},
            )

        def left_copy(part):
            return push(
                out_ref.at[part],
                out_ref.at[part],
                send_left.at[part],
                receive_deep.at[part],
                {"narrow": lax.rem(spot + deep - 1, deep)},
            )

        @pl.when(spot < deep - 1)
        def _():
            right_copy(spot).start()

        @pl.when(spot > 0)
        def _():
            left_copy(spot).start()

        for step in range(1, deep):
            yield

            @pl.when(spot >= step)
            def _():
                right_copy(spot - step).wait_recv()

                @pl.when(spot < deep - 1)
                def _():
                    right_copy(spot - step).start()

            @pl.when(spot + step < deep)
            def _():
                left_copy(spot + step).wait_recv()

                @pl.when(spot > 0)
                def _():
                    left_copy(spot + step).start()

        for part in range(deep):

            @pl.when((part <= spot) & (spot < deep - 1))
            def _():
                right_copy(part).wait_send()

            @pl.when((part >= spot) & (spot > 0))
            def _():
                left_copy(part).wait_send()

        for copy in copies:
            copy.wait_send()

    return Task(
        [rows],
        [struct((deep, wide * count, columns), rows.dtype)],
        [sems(deep)] * 3 + [sems(wide - 1), sems(wide), sems()],
        steps,
        ANY,
        ANY,
        ["narrow", "wide"],
    )


def sum_wide(partial):
    count = lax.axis_size("wide")
    chips = count // 2
    rows, width = partial.shape[0] // count, partial.shape[1]

    def steps(ins, outs, scratch):
        (parts_ref,), (out_ref,) = ins, outs
        from_mate, paired, slots, send_mate, receive_mate, send, receive = scratch
        me = lax.axis_index("wide")
        side = lax.rem(me, 2)
        mate = me + 1 - 2 * side
        my_chip = me // 2
        mate_copies = []
        for step in range(chips):
            chip = lax.rem(my_chip + 1 + step, chips)
            copy = push(
                parts_ref.at[2 * chip + 1 - side],
                from_mate.at[chip],
                send_mate.at[step],
                receive_mate.at[chip],
                {"wide": mate},
            )
            copy.start()
            mate_copies.append(copy)
        yield
        copies = []
        for step in range(chips):
            chip = lax.rem(my_chip + 1 + step, chips)
            arrived(from_mate.at[chip], send_mate.at[0], receive_mate.at[chip], {"wide": mate})
            both = parts_ref[2 * chip + side].astype(FULL) + from_mate[chip].astype(FULL)
            if step < chips - 1:
                paired[chip] = both.astype(LOW)
                copy = push(
                    paired.at[chip],
                    slots.at[my_chip],
                    send.at[step],
                    receive.at[my_chip],
                    {"wide": 2 * chip + side},
                )
                copy.start()
                copies.append(copy)
            else:
                out_ref[...] = both
        yield
        for step in range(1, chips):
            chip = lax.rem(my_chip - step + chips, chips)
            arrived(slots.at[chip], send.at[0], receive.at[chip], {"wide": 2 * chip + side})
            out_ref[...] = out_ref[...] + slots[chip].astype(FULL)
        for copy in mate_copies + copies:
            copy.wait_send()

    return Task(
        [partial.reshape(count, rows, width)],
        [struct((rows, width), FULL)],
        [pltpu.VMEM((chips, rows, width), LOW)] * 3
        + [sems(chips), sems(chips), sems(max(chips - 1, 1)), sems(chips)],
        steps,
        VMEM,
        VMEM,
        ["wide"],
    )


def merge_stats(first, second):
    peak = jnp.maximum(first[0:1], second[0:1])
    total = first[1:2] * jnp.exp(first[0:1] - peak) + second[1:2] * jnp.exp(second[0:1] - peak)
    return jnp.concatenate([peak, total, first[2:3] + second[2:3]], axis=0)


def add_two(first, second):
    return first + second


def combine(values, join):
    deep, wide = lax.axis_size("narrow"), lax.axis_size("wide")

    def steps(ins, outs, scratch):
        (x_ref,), (out_ref,) = ins, outs
        wide_slots, deep_slots, send_wide, receive_wide, send_deep, receive_deep = scratch

        def start(axis, count, slots, value, send, receive):
            me = lax.axis_index(axis)
            slots[me] = value
            copies = []
            for step in range(1, count):
                peer = lax.rem(me + step, count)
                copy = push(
                    slots.at[me], slots.at[me], send.at[step - 1], receive.at[me], {axis: peer}
                )
                copy.start()
                copies.append(copy)
            return copies

        def finish(axis, count, slots, send, receive):
            me = lax.axis_index(axis)
            for step in range(1, count):
                source = lax.rem(me - step + count, count)
                arrived(slots.at[source], send.at[0], receive.at[source], {axis: source})
            total = slots[0]
            for source in range(1, count):
                total = join(total, slots[source])
            return total

        first = start("wide", wide, wide_slots, x_ref[...], send_wide, receive_wide)
        yield
        total = finish("wide", wide, wide_slots, send_wide, receive_wide)
        second = start("narrow", deep, deep_slots, total, send_deep, receive_deep)
        yield
        out_ref[...] = finish("narrow", deep, deep_slots, send_deep, receive_deep)
        for copy in first + second:
            copy.wait_send()

    return Task(
        [values],
        [like(values)],
        [
            pltpu.VMEM((wide,) + values.shape, values.dtype),
            pltpu.VMEM((deep,) + values.shape, values.dtype),
            sems(wide - 1),
            sems(wide),
            sems(deep - 1),
            sems(deep),
        ],
        steps,
        VMEM,
        VMEM,
        ["narrow", "wide"],
    )


def gather_both(values):
    deep, wide = lax.axis_size("narrow"), lax.axis_size("wide")

    def steps(ins, outs, scratch):
        (x_ref,), (out_ref,) = ins, outs
        send_wide, receive_wide, send_deep, receive_deep = scratch
        me = lax.axis_index("wide")
        spot = lax.axis_index("narrow")
        out_ref[spot, me] = x_ref[...]
        copies = []
        for step in range(1, wide):
            peer = lax.rem(me + step, wide)
            block = out_ref.at[spot, me]
            copy = push(block, block, send_wide.at[step - 1], receive_wide.at[me], {"wide": peer})
            copy.start()
            copies.append(copy)
        yield
        for step in range(1, wide):
            source = lax.rem(me - step + wide, wide)
            block = out_ref.at[spot, source]
            arrived(block, send_wide.at[0], receive_wide.at[source], {"wide": source})
        for step in range(1, deep):
            peer = lax.rem(spot + step, deep)
            block = out_ref.at[spot]
            copy = push(
                block, block, send_deep.at[step - 1], receive_deep.at[spot], {"narrow": peer}
            )
            copy.start()
            copies.append(copy)
        yield
        for step in range(1, deep):
            source = lax.rem(spot - step + deep, deep)
            block = out_ref.at[source]
            arrived(block, send_deep.at[0], receive_deep.at[source], {"narrow": source})
        for copy in copies:
            copy.wait_send()

    return Task(
        [values],
        [struct((deep, wide) + values.shape, values.dtype)],
        [sems(wide - 1), sems(wide), sems(deep - 1), sems(deep)],
        steps,
        VMEM,
        VMEM,
        ["narrow", "wide"],
    )


def turn_heads(values, cosine, sine):
    half = values.shape[1] // 2
    swapped = jnp.concatenate([values[:, half:], values[:, :half]], axis=1)
    return values * cosine + swapped * sine


def wide_angles(cosine, sine):
    return jnp.concatenate([cosine, cosine], axis=1), jnp.concatenate([-sine, sine], axis=1)


def local_call(body, inputs, specs, outputs, flops, name):
    return pl.pallas_call(
        body,
        grid=(1,),
        in_specs=specs,
        out_specs=[
            pl.BlockSpec(a.shape, lambda step, rank=len(a.shape): (0,) * rank) for a in outputs
        ],
        out_shape=outputs,
        compiler_params=pltpu.CompilerParams(vmem_limit_bytes=VMEM_BYTES),
        cost_estimate=pl.CostEstimate(flops=flops, bytes_accessed=8 << 20, transcendentals=0),
        name=name,
    )(*inputs)


def entire(values):
    return pl.BlockSpec(values.shape, lambda step: (0,) * values.ndim)


def column_block(values, size, index):
    return pl.BlockSpec((values.shape[0], size), lambda step: (0, index))


def heads_body(groups, rep, rows_ref, gain_ref, kv_ref, cos_ref, sin_ref, out_ref, normed_ref):
    count, _, _, tok_rows, head = out_ref.shape
    size = kv_ref.shape[1] // (2 * count)
    per_head = head // size
    rows = rows_ref[0:tok_rows, :].astype(FULL)
    normed = norm_rows(rows, gain_ref[...]).astype(LOW)
    normed_ref[...] = normed
    both = dot(normed, kv_ref[...], 1, 0)

    def head_of(kind, index):
        pieces = [
            both[:, (2 * part + kind) * size : (2 * part + kind + 1) * size]
            for part in range(index * per_head, (index + 1) * per_head)
        ]
        return pieces[0] if per_head == 1 else jnp.concatenate(pieces, axis=1)

    for owner in range(count):
        for group in range(groups):
            index = (owner * groups + group) // rep
            keys = turn_heads(head_of(0, index), cos_ref[...], sin_ref[...])
            out_ref[owner, group, 0] = keys.astype(LOW)
            out_ref[owner, group, 1] = head_of(1, index).astype(LOW)


def make_heads(rows_low, gain_row, proj, cosine, sine, groups, rep):
    count = lax.axis_size("narrow")
    tok_rows, head = cosine.shape
    width = rows_low.shape[1]
    size = 2 * KVH * HD
    return local_call(
        functools.partial(heads_body, groups, rep),
        [rows_low, gain_row, proj, cosine, sine],
        [entire(rows_low), entire(gain_row), column_block(proj, size, 0)]
        + [entire(cosine), entire(sine)],
        [struct((count, groups, 2, tok_rows, head), LOW), struct((tok_rows, width), LOW)],
        2 * tok_rows * width * size,
        "make_heads",
    )


def attend_body(
    start_ref,
    gains_ref,
    q_ref,
    o_ref,
    kv_ref,
    cos_ref,
    sin_ref,
    seg_ref,
    seg_all_ref,
    pick_ref,
    queries_ref,
    probs_ref,
    mixed_ref,
    part_ref,
    normed_ref,
    early_ref,
):
    count, groups, _, tok_rows, head = kv_ref.shape
    heads_own = probs_ref.shape[0]
    start = start_ref[...].astype(FULL)
    root = lax.rsqrt(jnp.mean(start * start, axis=-1, keepdims=True) + NORM_EPS)
    normed = (start * root * gains_ref[0:1, :]).astype(LOW)
    normed_ref[...] = normed
    early_ref[...] = (start * root * gains_ref[2:3, :]).astype(LOW)
    queries = dot(normed, q_ref[...], 1, 0)
    spots = lax.broadcasted_iota(jnp.int32, (1, count * tok_rows), 1)
    allowed = (seg_ref[...] == seg_all_ref[...]) & (pick_ref[...] >= spots)
    for group in range(groups):
        keys = jnp.concatenate([kv_ref[part, group, 0] for part in range(count)], axis=0)
        values = jnp.concatenate([kv_ref[part, group, 1] for part in range(count)], axis=0)
        for member in range(heads_own // groups):
            at = group * (heads_own // groups) + member
            spot = slice(at * head, (at + 1) * head)
            query = turn_heads(queries[:, spot], cos_ref[...], sin_ref[...]).astype(LOW)
            queries_ref[:, spot] = query
            scores = jnp.where(allowed, dot(query, keys, 1, 1) * head ** (-0.5), MASKED)
            shifted = jnp.exp(scores - jnp.max(scores, axis=-1, keepdims=True))
            probs = shifted / jnp.sum(shifted, axis=-1, keepdims=True)
            probs_ref[at] = probs
            mixed_ref[:, spot] = dot(probs.astype(LOW), values, 1, 0).astype(LOW)
    part_ref[...] = dot(mixed_ref[...], o_ref[...], 1, 1).astype(LOW)


def attend(start_low, gains, proj, own_head, cosine, sine, seg, seg_all, picks):
    count, groups, _, tok_rows, head = own_head.shape
    sel, width = start_low.shape
    heads_own = HEADS // count
    size = heads_own * head
    first = 2 * KVH * HD // size
    seq_len = count * tok_rows
    return local_call(
        attend_body,
        [start_low, gains, proj, proj, own_head, cosine, sine, seg, seg_all, picks],
        [
            entire(start_low),
            entire(gains),
            column_block(proj, size, first),
            column_block(proj, size, first + 1),
        ]
        + [entire(a) for a in (own_head, cosine, sine, seg, seg_all, picks)],
        [
            struct((sel, size), LOW),
            struct((heads_own, sel, seq_len), FULL),
            struct((sel, size), LOW),
            struct((sel, width), LOW),
            struct((sel, width), LOW),
            struct((sel, width), LOW),
        ],
        4 * sel * size * (width + seq_len),
        "attend",
    )


def attend_back_body(
    grad_ref,
    q_ref,
    o_ref,
    kv_ref,
    queries_ref,
    probs_ref,
    cos_ref,
    sin_ref,
    cos_all_ref,
    sin_all_ref,
    out_ref,
    grad_q_ref,
    part_ref,
):
    count, groups, _, tok_rows, head = kv_ref.shape
    heads_own = probs_ref.shape[0]
    scale = head ** (-0.5)
    grad_mixed = dot(grad_ref[...], o_ref[...], 1, 0).astype(LOW)
    for group in range(groups):
        keys = jnp.concatenate([kv_ref[part, group, 0] for part in range(count)], axis=0)
        values = jnp.concatenate([kv_ref[part, group, 1] for part in range(count)], axis=0)
        grad_keys = jnp.zeros(keys.shape, FULL)
        grad_values = jnp.zeros(keys.shape, FULL)
        for member in range(heads_own // groups):
            at = group * (heads_own // groups) + member
            spot = slice(at * head, (at + 1) * head)
            probs = probs_ref[at]
            grad_probs = dot(grad_mixed[:, spot], values, 1, 1)
            inner = jnp.sum(probs * grad_probs, axis=-1, keepdims=True)
            grad_scores = (probs * (grad_probs - inner)).astype(LOW)
            grad_query = dot(grad_scores, keys, 1, 0) * scale
            grad_q_ref[:, spot] = turn_heads(grad_query, cos_ref[...], -sin_ref[...]).astype(LOW)
            grad_keys = grad_keys + dot(grad_scores, queries_ref[:, spot], 0, 0)
            grad_values = grad_values + dot(probs.astype(LOW), grad_mixed[:, spot], 0, 0)
        grad_keys = turn_heads(grad_keys * scale, cos_all_ref[...], -sin_all_ref[...])
        for part in range(count):
            rows = slice(part * tok_rows, (part + 1) * tok_rows)
            out_ref[part, group, 0] = grad_keys[rows].astype(LOW)
            out_ref[part, group, 1] = grad_values[rows].astype(LOW)
    part_ref[...] = dot(grad_q_ref[...], q_ref[...], 1, 1).astype(LOW)


def attend_back(grad, proj, own_head, queries, probs, cosine, sine, cosine_all, sine_all):
    count, groups, _, tok_rows, head = own_head.shape
    sel, width = grad.shape
    size = queries.shape[1]
    first = 2 * KVH * HD // size
    return local_call(
        attend_back_body,
        [grad, proj, proj, own_head, queries, probs, cosine, sine, cosine_all, sine_all],
        [entire(grad), column_block(proj, size, first), column_block(proj, size, first + 1)]
        + [
            entire(a)
            for a in (own_head, queries, probs, cosine, sine, cosine_all, sine_all)
        ],
        [struct(own_head.shape, LOW), struct((sel, size), LOW), struct((sel, width), LOW)],
        8 * sel * size * width,
        "attend_back",
    )


def norm_back_rows(values, gain_row, grad):
    root = lax.rsqrt(jnp.mean(values * values, axis=-1, keepdims=True) + NORM_EPS)
    scaled = gain_row * grad
    inner = jnp.mean(values * scaled, axis=-1, keepdims=True)
    result = root * scaled - values * (root * root * root * inner)
    return result, jnp.sum(values * root * grad, axis=0, keepdims=True)


def rows_back_body(
    rep,
    rows_ref,
    gains_ref,
    kv_ref,
    heads_ref,
    pick_ref,
    early_ref,
    base_ref,
    out_ref,
    attn_gain_ref,
    early_gain_ref,
    grad_kv_ref,
):
    count, groups, _, tok_rows, head = heads_ref.shape
    size = kv_ref.shape[1] // (2 * count)
    per_head = head // size
    for index in range(KVH):
        for kind in range(2):
            copies = [
                heads_ref[at // groups, at % groups, kind]
                for at in range(index * rep, (index + 1) * rep)
            ]
            total = copies[0]
            if rep > 1:
                total = sum(copy.astype(FULL) for copy in copies).astype(LOW)
            for piece in range(per_head):
                lane = (2 * (index * per_head + piece) + kind) * size
                grad_kv_ref[:, lane : lane + size] = total[:, piece * size : (piece + 1) * size]
    values = rows_ref[...].astype(FULL)
    own = values[tok_rows:]
    tok_part, tok_gain = norm_back_rows(
        values[:tok_rows], gains_ref[0:1, :], dot(grad_kv_ref[...], kv_ref[...], 1, 1)
    )
    pick_part, pick_gain = norm_back_rows(own, gains_ref[0:1, :], pick_ref[...])
    early_part, early_gain = norm_back_rows(own, gains_ref[2:3, :], early_ref[...])
    attn_gain_ref[...] = tok_gain + pick_gain
    early_gain_ref[...] = early_gain
    out_ref[0:tok_rows, :] = tok_part.astype(LOW)
    out_ref[tok_rows:, :] = (pick_part + early_part + base_ref[...]).astype(LOW)


def rows_back(rows_low, gains, proj, heads, grad_pick, grad_early, base, rep):
    tok_rows = heads.shape[3]
    width = rows_low.shape[1]
    size = 2 * KVH * HD
    return local_call(
        functools.partial(rows_back_body, rep),
        [rows_low, gains, proj, heads, grad_pick, grad_early, base],
        [entire(rows_low), entire(gains), column_block(proj, size, 0)]
        + [entire(a) for a in (heads, grad_pick, grad_early, base)],
        [
            struct(rows_low.shape, LOW),
            struct((1, width), FULL),
            struct((1, width), FULL),
            struct((tok_rows, size), LOW),
        ],
        2 * tok_rows * width * size,
        "rows_back",
    )


def assemble_body(out_columns, *refs):
    pieces, out_ref = refs[:-1], refs[-1]
    count = len(pieces)
    me = lax.axis_index("narrow")
    for step, piece in enumerate(pieces):
        source = lax.rem(me - step + count, count)
        spot = pl.ds(pl.multiple_of(source * out_columns, out_columns), out_columns)
        out_ref[:, spot] = piece[...]


def assemble(pieces):
    rows, columns = pieces[0].shape
    outputs = [struct((rows, columns * len(pieces)), pieces[0].dtype)]
    return local_call(
        functools.partial(assemble_body, columns),
        list(pieces),
        [entire(piece) for piece in pieces],
        outputs,
        0,
        "assemble",
    )[0]


def feed_body(inner_ref, weight_ref, gate_ref, up_ref, hidden_ref, out_ref, total):
    part = pl.program_id(0)
    inner = inner_ref[...]
    gate = dot(inner, weight_ref[0, 0], 1, 1)
    up = dot(inner, weight_ref[0, 1], 1, 1)
    hidden = (jax.nn.silu(gate) * up).astype(LOW)
    gate_ref[0] = gate
    up_ref[0] = up
    hidden_ref[0] = hidden
    product = dot(hidden, weight_ref[0, 2], 1, 0)

    @pl.when(part == 0)
    def _():
        total[...] = product

    @pl.when(part > 0)
    def _():
        total[...] = total[...] + product

    @pl.when(part == pl.num_programs(0) - 1)
    def _():
        out_ref[...] = total[...].astype(LOW)


def feed(inner, weight):
    parts, _, size, width = weight.shape
    sel = inner.shape[0]
    same = pl.BlockSpec((sel, width), lambda part: (0, 0))
    slab = pl.BlockSpec((1, sel, size), lambda part: (part, 0, 0))
    return pl.pallas_call(
        feed_body,
        grid=(parts,),
        in_specs=[same, pl.BlockSpec((1, 3, size, width), lambda part: (part, 0, 0, 0))],
        out_specs=[slab, slab, slab, same],
        out_shape=[
            struct((parts, sel, size), FULL),
            struct((parts, sel, size), FULL),
            struct((parts, sel, size), LOW),
            struct((sel, width), LOW),
        ],
        scratch_shapes=[pltpu.VMEM((sel, width), FULL)],
        compiler_params=pltpu.CompilerParams(vmem_limit_bytes=VMEM_BYTES),
        cost_estimate=pl.CostEstimate(
            flops=6 * sel * parts * size * width,
            bytes_accessed=weight.size * 2,
            transcendentals=0,
        ),
        name="feed",
    )(inner, weight)


def feed_back_body(grad_ref, weight_ref, gate_ref, up_ref, hidden_ref, acts_ref, out_ref, total):
    part = pl.program_id(0)
    grad_hidden = dot(grad_ref[...], weight_ref[0, 2], 1, 1)
    gate = gate_ref[0]
    sigma = jax.nn.sigmoid(gate)
    grad_gate = (grad_hidden * up_ref[0] * sigma * (1.0 + gate * (1.0 - sigma))).astype(LOW)
    grad_up = (grad_hidden * gate * sigma).astype(LOW)
    acts_ref[0, 0] = grad_gate
    acts_ref[0, 1] = grad_up
    acts_ref[0, 2] = hidden_ref[0]
    product = dot(grad_gate, weight_ref[0, 0], 1, 0) + dot(grad_up, weight_ref[0, 1], 1, 0)

    @pl.when(part == 0)
    def _():
        total[...] = product

    @pl.when(part > 0)
    def _():
        total[...] = total[...] + product

    @pl.when(part == pl.num_programs(0) - 1)
    def _():
        out_ref[...] = total[...].astype(LOW)


def feed_back(grad, weight, gate, up, hidden):
    parts, _, size, width = weight.shape
    sel = grad.shape[0]
    same = pl.BlockSpec((sel, width), lambda part: (0, 0))
    slab = pl.BlockSpec((1, sel, size), lambda part: (part, 0, 0))
    return pl.pallas_call(
        feed_back_body,
        grid=(parts,),
        in_specs=[same, pl.BlockSpec((1, 3, size, width), lambda part: (part, 0, 0, 0))]
        + [slab] * 3,
        out_specs=[pl.BlockSpec((1, 3, sel, size), lambda part: (part, 0, 0, 0)), same],
        out_shape=[struct((parts, 3, sel, size), LOW), struct((sel, width), LOW)],
        scratch_shapes=[pltpu.VMEM((sel, width), FULL)],
        compiler_params=pltpu.CompilerParams(vmem_limit_bytes=VMEM_BYTES),
        cost_estimate=pl.CostEstimate(
            flops=6 * sel * parts * size * width,
            bytes_accessed=weight.size * 2,
            transcendentals=0,
        ),
        name="feed_back",
    )(grad, weight, gate, up, hidden)


def newton_steps(problems):
    rows, width = problems[0][0].shape
    block = min(512, width)
    eye = lax.broadcasted_iota(jnp.int32, (rows, rows), 0) == lax.broadcasted_iota(
        jnp.int32, (rows, rows), 1
    )

    def strip(part):
        return pl.ds(pl.multiple_of(part * block, block), block)

    def over(function, start):
        return lax.fori_loop(0, width // block, function, start)

    def add_squares(part, totals):
        values = [current[:, strip(part)] for current, low, gram, rest in problems]
        return [total + jnp.sum(value * value) for total, value in zip(totals, values)]

    totals = over(add_squares, [jnp.float32(0.0)] * len(problems))
    scales = [1.0 / (jnp.sqrt(total) + 1e-07) for total in totals]

    def begin(part, carry):
        for scale, (current, low, gram, rest) in zip(scales, problems):
            values = current[:, strip(part)] * scale
            current[:, strip(part)] = values
            low[:, strip(part)] = values.astype(LOW)
        return carry

    over(begin, 0)

    def iteration(turn, carry):
        for current, low, gram, rest in problems:
            gram[...] = jnp.zeros_like(gram)

        def add_gram(part, carry):
            for current, low, gram, rest in problems:
                values = low[:, strip(part)]
                gram[...] = gram[...] + dot(values, values, 1, 1)
            return carry

        over(add_gram, 0)
        seconds = []
        for current, low, gram, rest in problems:
            whole = gram[...]
            middle = jnp.sum(jnp.where(eye, whole, 0.0)) / rows
            rest[...] = (whole - jnp.where(eye, middle, 0.0)).astype(LOW)
            square = dot(rest[...], rest[...], 1, 0)
            whole = gram[...]
            centred = whole - jnp.where(eye, middle, 0.0)
            square = square + 2.0 * middle * centred + jnp.where(eye, middle * middle, 0.0)
            whole = NEWTON_B * whole + NEWTON_C * square
            second = jnp.sum(jnp.where(eye, whole, 0.0)) / rows
            rest[...] = (whole - jnp.where(eye, second, 0.0)).astype(LOW)
            seconds.append(second)

        def apply(part, carry):
            for second, (current, low, gram, rest) in zip(seconds, problems):
                values = (NEWTON_A + second) * current[:, strip(part)] + dot(
                    rest[...], low[:, strip(part)], 1, 0
                )
                current[:, strip(part)] = values
                low[:, strip(part)] = values.astype(LOW)
            return carry

        over(apply, 0)
        return carry

    lax.fori_loop(0, NS_STEPS, iteration, 0)


def newton_scratch(rows, width):
    return [
        pltpu.VMEM((rows, width), FULL),
        pltpu.VMEM((rows, width), LOW),
        pltpu.VMEM((rows, rows), FULL),
        pltpu.VMEM((rows, rows), LOW),
    ]


def newton_cost(count, rows, width):
    return pl.CostEstimate(
        flops=NS_STEPS * count * (4 * rows * rows * width + 2 * rows * rows * rows),
        bytes_accessed=6 * count * rows * width,
        transcendentals=0,
    )


def newton_body(factor_ref, mom_ref, grad_ref, out_ref, *problem):
    current, low = problem[:2]
    parts, rows, columns = mom_ref.shape
    factor = factor_ref[0]
    size = grad_ref.shape[1]
    for part in range(parts):
        spot = slice(part * columns, (part + 1) * columns)
        for source in range(parts):
            here = slice(source * size, (source + 1) * size)
            current[here, spot] = MOMENTUM * mom_ref[part, here, :].astype(
                FULL
            ) + factor * grad_ref[source, :, spot].astype(FULL)
    newton_steps([problem])
    for part in range(parts):
        out_ref[part] = low[:, part * columns : (part + 1) * columns]


def newton_small_body(rows, factor_ref, mom_ref, grad_ref, kv_ref, out_ref, *scratch):
    problems = [scratch[4 * at : 4 * at + 4] for at in range(4)]
    parts, _, columns = mom_ref.shape
    kv_columns = kv_ref.shape[2]
    half = rows // 2
    factor = factor_ref[0]
    for part in range(parts):
        spot = slice(part * columns, (part + 1) * columns)
        for member in range(2):
            current = problems[member][0]
            here = slice(member * rows, (member + 1) * rows)
            mom, grad = mom_ref[part, here, :], grad_ref[part, here, :]
            current[:, spot] = MOMENTUM * mom.astype(FULL) + factor * grad.astype(FULL)
        spot = slice(part * kv_columns, (part + 1) * kv_columns)
        for member in range(2):
            current = problems[2 + member][0]
            piece = kv_ref[part, member * rows : (member + 1) * rows, :].astype(FULL)
            for side in range(2):
                lane = (2 * member + side) * kv_columns
                mom = mom_ref[part, 2 * rows : 2 * rows + half, lane : lane + kv_columns]
                here = slice(side * half, (side + 1) * half)
                current[here, spot] = MOMENTUM * mom.astype(FULL) + factor * piece[here]
    newton_steps(problems[:2])
    newton_steps(problems[2:])
    out_ref[...] = jnp.zeros_like(out_ref)
    for part in range(parts):
        for member in range(2):
            out_ref[part, member * rows : (member + 1) * rows, :] = problems[member][1][
                :, part * columns : (part + 1) * columns
            ]
            low = problems[2 + member][1]
            for side in range(2):
                lane = (2 * member + side) * kv_columns
                out_ref[part, 2 * rows : 2 * rows + half, lane : lane + kv_columns] = low[
                    side * half : (side + 1) * half,
                    part * kv_columns : (part + 1) * kv_columns,
                ]


def newton_any_body(rows, factor_ref, mom_ref, grad_ref, qo_ref, kv_ref, out_ref, *scratch):
    parts = mom_ref.shape[0]
    owner = lax.rem(3 + lax.rem(lax.axis_index("wide"), 2), parts)
    small = lax.axis_index("narrow") == owner

    @pl.when(small)
    def _():
        newton_small_body(rows, factor_ref, mom_ref, qo_ref, kv_ref, out_ref, *scratch[4:])

    @pl.when(jnp.logical_not(small))
    def _():
        newton_body(factor_ref, mom_ref, grad_ref, out_ref, *scratch[:4])


def newton(factor, mom, grad, qo_grad, kv_grad):
    parts, slot_rows, columns = mom.shape
    width = parts * columns
    rows = kv_grad.shape[1] // 2
    kv_width = parts * kv_grad.shape[2]
    return pl.pallas_call(
        functools.partial(newton_any_body, rows),
        in_specs=[pl.BlockSpec(memory_space=pltpu.SMEM)] + [VMEM] * 4,
        out_specs=VMEM,
        out_shape=struct(mom.shape, LOW),
        scratch_shapes=newton_scratch(slot_rows, width)
        + newton_scratch(rows, width) * 2
        + newton_scratch(rows, kv_width) * 2,
        compiler_params=pltpu.CompilerParams(vmem_limit_bytes=VMEM_BYTES),
        cost_estimate=newton_cost(1, slot_rows, width),
        name="newton",
    )(factor.reshape(1), mom, grad, qo_grad, kv_grad)


def lookup_body(ids_ref, turn_ref, table_ref, out_ref, low_ref, list_ref, held, rows, sem):
    vocab = table_ref.shape[0]
    count = out_ref.shape[0]
    load = pltpu.make_async_copy(table_ref, held, sem)
    load.start()
    rows[...] = jnp.zeros_like(rows)

    found = turn_ref[count]

    def note(group, carry):
        for member in range(UNROLL):
            at = group * UNROLL + member
            list_ref[turn_ref[at]] = at
        return carry

    lax.fori_loop(0, count // UNROLL, note, 0)
    for member in range(UNROLL):
        list_ref[found + member] = count
    list_ref[count + UNROLL] = found
    load.wait()

    def step(group, carry):
        for member in range(UNROLL):
            at = list_ref[group * UNROLL + member]
            spot = jnp.minimum(ids_ref[jnp.minimum(at, count - 1)], vocab - 1)
            rows[pl.ds(at, 1), :] = held[pl.ds(spot, 1), :]
        return carry

    lax.fori_loop(0, (found + UNROLL - 1) // UNROLL, step, 0)
    out_ref[...] = rows[pl.ds(0, count), :].astype(LOW)
    low_ref[...] = held[...].astype(LOW)


def lookup(table, ids):
    vocab, columns = table.shape
    count = ids.shape[0]
    mine = (ids < vocab).reshape(-1, 128)
    before = jnp.arange(128)[:, None] < jnp.arange(128)[None, :]
    in_row = dot(mine.astype(LOW), before.astype(LOW), 1, 0)
    per_row = jnp.sum(mine.astype(FULL), axis=1)
    lines = jnp.arange(mine.shape[0])
    ahead = jnp.sum(jnp.where(lines[:, None] > lines[None, :], per_row[None, :], 0.0), axis=1)
    found = jnp.sum(per_row).astype(jnp.int32)
    turns = (in_row + ahead[:, None]).astype(jnp.int32)
    turns = jnp.where(mine, turns, count + UNROLL + 1).reshape(-1)
    turns = jnp.concatenate([turns, jnp.full((128,), found)])
    return pl.pallas_call(
        lookup_body,
        in_specs=[pl.BlockSpec(memory_space=pltpu.SMEM)] * 2 + [ANY],
        out_specs=[VMEM, VMEM, pl.BlockSpec(memory_space=pltpu.SMEM)],
        scratch_shapes=[
            pltpu.VMEM((vocab, columns), FULL),
            pltpu.VMEM((count + 8, columns), FULL),
            pltpu.SemaphoreType.DMA,
        ],
        out_shape=[
            struct((count, columns), LOW),
            struct((vocab, columns), LOW),
            struct((count + 2 * UNROLL,), jnp.int32),
        ],
        compiler_params=pltpu.CompilerParams(vmem_limit_bytes=VMEM_BYTES),
        cost_estimate=pl.CostEstimate(
            flops=0, bytes_accessed=vocab * columns * 4, transcendentals=0
        ),
        name="lookup",
    )(ids, turns, table)


def spread_body(
    ids_ref, list_ref, rows_ref, head_ref, out_ref, square_ref, even, odd, rows, sem
):
    vocab = out_ref.shape[0]
    count = rows_ref.shape[0]
    chunk = 256

    def strip(part):
        return pl.ds(pl.multiple_of(part * chunk, chunk), chunk)

    def begin(part, carry):
        even[strip(part), :] = head_ref[strip(part), :].astype(FULL)
        odd[strip(part), :] = jnp.zeros((chunk, odd.shape[1]), FULL)
        return carry

    lax.fori_loop(0, vocab // chunk, begin, 0)

    def widen(part, carry):
        rows[strip(part), :] = rows_ref[strip(part), :].astype(FULL)
        return carry

    lax.fori_loop(0, count // chunk, widen, 0)
    rows[pl.ds(count, 8), :] = jnp.zeros((8, rows.shape[1]), FULL)

    def step(group, carry):
        for member in range(UNROLL):
            at = list_ref[group * UNROLL + member]
            spot = jnp.minimum(ids_ref[jnp.minimum(at, count - 1)], vocab - 1)
            total = even if member % 2 == 0 else odd
            total[pl.ds(spot, 1), :] = total[pl.ds(spot, 1), :] + rows[pl.ds(at, 1), :]
        return carry

    found = list_ref[count + UNROLL]
    lax.fori_loop(0, (found + UNROLL - 1) // UNROLL, step, 0)

    def finish(part, squares):
        value = even[strip(part), :] + odd[strip(part), :]
        even[strip(part), :] = value
        return squares + jnp.sum((value * value).reshape(chunk // 8, 8, -1), axis=0)

    square_ref[...] = lax.fori_loop(
        0, vocab // chunk, finish, jnp.zeros((8, even.shape[1]), FULL)
    )
    store = pltpu.make_async_copy(even, out_ref, sem)
    store.start()
    store.wait()


def spread(ids, listed, rows, head):
    vocab, columns = head.shape
    count = ids.shape[0]
    smem = pl.BlockSpec(memory_space=pltpu.SMEM)
    return pl.pallas_call(
        spread_body,
        in_specs=[smem, smem, VMEM, VMEM],
        out_specs=[ANY, VMEM],
        scratch_shapes=[
            pltpu.VMEM((vocab, columns), FULL),
            pltpu.VMEM((vocab, columns), FULL),
            pltpu.VMEM((count + 8, columns), FULL),
            pltpu.SemaphoreType.DMA,
        ],
        out_shape=[struct((vocab, columns), FULL), struct((8, columns), FULL)],
        compiler_params=pltpu.CompilerParams(vmem_limit_bytes=VMEM_BYTES),
        cost_estimate=pl.CostEstimate(
            flops=count * columns, bytes_accessed=vocab * columns * 8, transcendentals=0
        ),
        name="spread",
    )(ids, listed, rows, head)


def adamw(weight, first_m, second_m, grad, rate, decay):
    first_new = BETA_ONE * first_m + (1.0 - BETA_ONE) * grad
    second_new = BETA_TWO * second_m + (1.0 - BETA_TWO) * grad * grad
    update = (
        first_new
        / (1.0 - BETA_ONE**STEP)
        / (jnp.sqrt(second_new / (1.0 - BETA_TWO**STEP)) + ADAM_EPS)
    )
    return (weight * (1.0 - rate * decay) - rate * update, first_new, second_new)


def cut_columns(values, count):
    rows, columns = values.shape
    return jnp.moveaxis(values.reshape(rows, count, columns // count), 1, 0)


def shifted(parts, axis, step):
    count = lax.axis_size(axis)
    pairs = [(source, (source + step) % count) for source in range(count)]
    return lax.ppermute(parts, axis, pairs)


def per_device(
    tokens,
    picks,
    targets,
    lengths,
    skip,
    embed,
    embed_m,
    embed_v,
    attn_qo,
    attn_qo_mom,
    attn_kv,
    attn_kv_mom,
    ffn,
    ffn_mom,
    gains,
    gains_m,
    gains_v,
):
    wide_count = lax.axis_size("wide")
    narrow_count = lax.axis_size("narrow")
    narrow_spot = lax.axis_index("narrow")
    wide_spot = lax.axis_index("wide")
    seq_len = tokens.shape[1]
    sel = picks.shape[1]
    vocab_rows, columns = embed.shape
    width = columns * wide_count
    own_rows = sel // narrow_count
    tok_rows = seq_len // narrow_count
    all_rows = own_rows + tok_rows
    heads_own = HEADS // narrow_count
    head_cols = heads_own * HD
    repeat = max(1, narrow_count // KVH)
    groups = KVH * repeat // narrow_count
    ffn_rows = ffn.shape[0]
    ffn_size = ffn_rows // narrow_count
    total_rows = wide_count * sel
    lens = lengths[0]
    pick_ids = picks[0]
    keep_layer = (1 - skip[0]).astype(FULL)
    keep_row = jnp.full((1, width), keep_layer)
    lanes = 128

    def box(flat):
        height = -(-flat.shape[0] // (8 * lanes)) * 8
        return jnp.pad(flat, (0, height * lanes - flat.shape[0])).reshape(height, lanes)

    ffn_low = jnp.moveaxis(ffn, 1, 0).astype(LOW)
    ffn_cut = ffn_low.reshape(3, narrow_count, ffn_size, ffn_low.shape[2])
    ffn_cut = jnp.moveaxis(ffn_cut, 1, 0).reshape(narrow_count, 3 * ffn_size, -1)
    kv_own = attn_kv.reshape(columns, -1).astype(LOW)

    where_at = jnp.arange(seq_len, dtype=jnp.int32)
    pick_tokens = jnp.sum(
        jnp.where(pick_ids[:, None] == where_at[None, :], tokens[0][None, :], 0), axis=1
    )
    ints = box(jnp.concatenate([tokens[0], pick_tokens, targets[0]]))
    all_ints, all_gains, kv_part = launch(
        [
            gather_wide(ints),
            gather_both(box(gains.astype(LOW).astype(FULL).reshape(-1))),
            gather_blocks("narrow", kv_own),
        ],
        0,
        "gather_ids",
    )
    kv_part = jnp.moveaxis(kv_part, 0, 1).reshape(columns, -1)
    proj_own = jnp.concatenate([kv_part, attn_qo.reshape(columns, -1).astype(LOW)], axis=1)
    proj = lax.all_gather(proj_own, "wide", axis=0, tiled=True)
    ffn_cut, all_ints = lax.optimization_barrier((ffn_cut, all_ints))
    ffn_pieces = [lax.dynamic_index_in_dim(ffn_cut, narrow_spot, 0, False)] + [
        shifted(
            lax.dynamic_index_in_dim(
                ffn_cut, lax.rem(narrow_spot + step, narrow_count), 0, False
            ),
            "narrow",
            step,
        )
        for step in range(1, narrow_count)
    ]
    gain_size = gains.shape[1]
    gain_w = all_gains.reshape(narrow_count, wide_count, -1)[:, :, : 3 * gain_size]
    gain_w = gain_w.reshape(narrow_count, wide_count, 3, gain_size)
    gain_w = jnp.transpose(gain_w, (2, 1, 0, 3)).reshape(3, width)
    all_ints = all_ints.reshape(wide_count, -1)
    tokens_all = all_ints[:, :seq_len].reshape(wide_count, narrow_count, tok_rows)
    picked_all = all_ints[:, seq_len : seq_len + sel].reshape(wide_count, narrow_count, own_rows)
    targets_all = all_ints[:, seq_len + sel : seq_len + 2 * sel].reshape(-1)
    wanted = jnp.moveaxis(jnp.concatenate([tokens_all, picked_all], axis=2), 1, 0).reshape(-1)
    local_ids = wanted - narrow_spot * vocab_rows
    inside = (local_ids >= 0) & (local_ids < vocab_rows)
    spots = jnp.where(inside, local_ids, vocab_rows)
    found, embed_low, listed = lookup(embed, spots)
    ffn_pieces, found = lax.optimization_barrier((ffn_pieces, found))
    ffn_sub = assemble(ffn_pieces).reshape(3, ffn_size, width)
    ffn_sub, found = lax.optimization_barrier((ffn_sub, found))
    ffn_w = lax.all_gather(ffn_sub, "wide", axis=0)
    found = found.reshape(narrow_count, wide_count * all_rows, columns)
    embed_cut = embed_low.reshape(wide_count, vocab_rows // wide_count, columns)
    table_half = embed_cut.shape[1] // 2
    rows_low = launch([fetch_rows(found, all_rows)], 1, "fetch_rows")[0]

    mom_qo = jnp.moveaxis(attn_qo_mom, 1, 0)
    mom_kv = jnp.moveaxis(attn_kv_mom, 1, 0)
    mom_ffn = jnp.moveaxis(ffn_mom, 1, 0)
    slot_rows, slot_cols = mom_ffn.shape[1:]

    block_rows, q_size = mom_qo.shape[1:]
    kv_size = mom_kv.shape[2]
    half_rows = block_rows // 2
    kv_box = jnp.moveaxis(mom_kv.reshape(4, half_rows, kv_size), 0, 1).reshape(half_rows, -1)
    small_box = jnp.concatenate([mom_qo.reshape(2 * block_rows, q_size), kv_box])
    small_box = jnp.pad(small_box, ((0, slot_rows - small_box.shape[0]), (0, 0)))
    mom_parts = jnp.concatenate([mom_ffn, small_box[None]]).astype(LOW)

    seg_all, cosine_all, sine_all = angles_at(lens, where_at)
    cosine_all, sine_all = wide_angles(cosine_all, sine_all)
    seg_mine, cosine, sine = angles_at(lens, pick_ids)
    cosine, sine = wide_angles(cosine, sine)

    def tok_part(angles):
        return lax.dynamic_slice_in_dim(angles, narrow_spot * tok_rows, tok_rows, 0)

    by_head, normed_tok = make_heads(
        rows_low, gain_w[0:1], proj, tok_part(cosine_all), tok_part(sine_all), groups, repeat
    )
    own_head, start_low, tok_cols, table_low = launch(
        [
            swap_blocks("narrow", by_head),
            gather_blocks("narrow", rows_low[tok_rows:]),
            split_columns("wide", normed_tok),
            join_columns("wide", embed_cut[:, table_half:]),
        ],
        2,
        "trade_heads",
    )
    start_low, ffn_w = lax.optimization_barrier((start_low, ffn_w))
    start_low = start_low.reshape(sel, width)
    queries, probs, mixed, attn_part, normed, early_part = attend(
        start_low,
        gain_w,
        proj,
        own_head,
        cosine,
        sine,
        seg_mine[:, None],
        seg_all[None, :],
        pick_ids[:, None],
    )
    early = lax.all_gather(early_part, "wide", axis=0, tiled=True)
    start_own = rows_low[tok_rows:].astype(FULL)
    middle, inner, mixed_wide, pick_cols = launch(
        [
            settle(
                attn_part,
                start_own,
                start_own,
                jnp.ones((1, width), FULL),
                gain_w[1:2],
            ),
            gather_wide(mixed),
            split_columns("wide", normed),
        ],
        3,
        "settle_middle",
    )
    inner = inner.reshape(sel, width)
    inner_all = lax.all_gather(inner, "wide", axis=0, tiled=True)
    gate, up, hidden, fed = feed(inner, ffn_w)
    final_own, late_part, table_top = launch(
        [
            settle(fed, middle, start_own, keep_row, gain_w[2:3]),
            join_columns("wide", embed_cut[:, :table_half]),
        ],
        4,
        "settle_late",
    )
    table_own = jnp.concatenate([table_top, table_low])

    table_count = table_own.shape[0]
    local_target = targets_all - (narrow_spot * vocab_rows + wide_spot * table_count)
    has_target = jnp.arange(table_count, dtype=jnp.int32)[:, None] == local_target[None, :]
    counted = (targets_all >= 0).astype(FULL)
    loss_count = jnp.sum(counted)

    def exit_logits(features):
        logits = dot(table_own, features, 1, 1)
        peak = jnp.max(logits, axis=0)
        total = jnp.sum(jnp.exp(logits - peak[None, :]), axis=0)
        picked = jnp.sum(jnp.where(has_target, logits, 0.0), axis=0)
        return logits, jnp.stack([peak, total, picked])

    half = slot_rows // 2
    late, mom_top, early_logits, early_stats = launch(
        [
            gather_wide(late_part.reshape(sel, width)),
            swap_turned(mom_parts[:, :half]),
            exit_stats(early, table_own, local_target[None, :]),
        ],
        5,
        "gather_late",
    )
    late = late.reshape(total_rows, width)
    late_logits, late_stats = exit_logits(late)
    stats = jnp.concatenate([early_stats, late_stats], axis=1).reshape(3, 8, -1)
    stats = launch([combine(stats, merge_stats)], 6, "combine_stats")[0]
    stats, inner_all = lax.optimization_barrier((stats, inner_all))
    stats = stats.reshape(3, -1)
    log_norms = stats[0] + jnp.log(stats[1])
    losses = log_norms - stats[2]
    loss_sum = jnp.sum(
        counted * (EXIT_EARLY * losses[:total_rows] + EXIT_LAST * losses[total_rows:])
    )

    def exit_back(logits, log_norm, weight):
        grad_logits = (
            (jnp.exp(logits - log_norm[None, :]) - has_target.astype(FULL))
            * (weight * counted)[None, :]
        ).astype(LOW)
        return grad_logits

    late_grad = exit_back(late_logits, log_norms[total_rows:], EXIT_LAST)
    late_back = dot(late_grad, table_own, 0, 0).astype(LOW)
    grad_late, mom_low = launch(
        [sum_wide(late_back), swap_turned(mom_parts[:, half:])], 7, "sum_late"
    )
    early_norms, grad_late = lax.optimization_barrier((log_norms[:total_rows], grad_late))
    early_grad = exit_back(early_logits, early_norms, EXIT_EARLY)
    mom_owned = jnp.concatenate([mom_top, mom_low], axis=1)

    grad_final, gain_late, grad_out, early_back, _ = launch(
        [
            settle_back(
                grad_late.astype(LOW),
                final_own,
                jnp.zeros_like(final_own),
                keep_row,
                gain_w[2:3],
            ),
            product([early_grad], [table_own], 0, [[(0, 0)]]),
        ],
        8,
        "back_late",
    )
    grad_early = lax.psum_scatter(early_back[0], "wide", scatter_dimension=0, tiled=True)
    grad_layer = grad_final * keep_layer
    grad_out = grad_out.reshape(sel, width)
    out_all = lax.all_gather(grad_out, "wide", axis=0, tiled=True)
    acts, fed_back = feed_back(grad_out, ffn_w, gate, up, hidden)
    grad_mid, gain_mid, grad_branch, acts = launch(
        [
            settle_back(fed_back, middle, grad_layer, keep_row, gain_w[1:2]),
            swap_blocks("wide", acts),
        ],
        9,
        "back_middle",
    )
    acts = jnp.moveaxis(acts, 1, 0).reshape(3, total_rows, ffn_size)
    grad_branch, grad_early = lax.optimization_barrier((grad_branch, grad_early))
    grad_branch = grad_branch.reshape(sel, width)

    kv_parts, grad_queries, pick_part = attend_back(
        grad_branch, proj, own_head, queries, probs, cosine, sine, cosine_all, sine_all
    )
    grad_kv, grad_pick, grad_early, queries_wide, branch_cols, grad_head, _ = launch(
        [
            swap_blocks("narrow", kv_parts),
            sum_narrow(pick_part),
            sum_narrow(grad_early),
            gather_wide(grad_queries),
            split_columns("wide", grad_branch),
            product([early_grad, late_grad], [early, late], 1, [[(0, 0), (1, 1)]]),
        ],
        10,
        "trade_grads",
    )
    grad_kv, out_all = lax.optimization_barrier((grad_kv, out_all))
    grad_base = grad_mid + grad_final * (1.0 - keep_layer)
    grad_rows, gain_attn, gain_early, grad_kv = rows_back(
        rows_low, gain_w, proj, grad_kv, grad_pick, grad_early, grad_base, repeat
    )
    summed_qo = jnp.stack(
        [
            jnp.einsum("wtc,wtf->cf", pick_cols, queries_wide, preferred_element_type=FULL),
            jnp.einsum("wtc,wtf->cf", branch_cols, mixed_wide, preferred_element_type=FULL),
        ]
    )
    grad_rows, acts_owned, kv_wide, head_cols_all, grad_ffn, ffn_squares = launch(
        [
            return_rows(grad_rows),
            swap_owned(acts, 5),
            later(gather_wide(grad_kv, 3), 2),
            later(split_columns("wide", grad_head[0], 3), 2),
            product([acts], [inner_all, out_all], 0, [[(0, 0)], [(1, 0)], [(2, 1)]]),
        ],
        11,
        "return_rows",
    )
    turn = lax.rem(wide_spot, 2)
    grad_kv_w = jnp.einsum(
        "wtc,wtf->cf", tok_cols, kv_wide, preferred_element_type=FULL
    ).reshape(columns, narrow_count, 2, kv_size)
    grad_kv_w = jnp.moveaxis(grad_kv_w, 0, 2)
    summed_kv = lax.psum_scatter(grad_kv_w, "narrow", scatter_dimension=0, tiled=True)[0]
    summed_table, table_squares = spread(
        spots, listed, grad_rows.reshape(-1, columns), head_cols_all.reshape(vocab_rows, columns)
    )

    squares = (
        jnp.sum(summed_qo * summed_qo)
        + jnp.sum(summed_kv * summed_kv)
        + jnp.sum(ffn_squares)
        + jnp.sum(table_squares)
    )
    sums = jnp.stack(
        [gain_attn[0], gain_mid[0], gain_early[0] + gain_late[0], jnp.full((width,), squares)]
    )
    matrix = jnp.minimum(lax.rem(narrow_spot + narrow_count - turn, narrow_count), 2)
    right = jnp.where(matrix == 2, out_all, inner_all)
    sums, kv_owned, qo_owned, owned, _ = launch(
        [
            combine(sums.reshape(4, 8, -1), add_two),
            send_owner(summed_kv.astype(LOW).reshape(2 * block_rows, kv_size)),
            later(send_owner(summed_qo.astype(LOW).reshape(2 * columns, q_size)), 1),
            later(product([acts_owned], [right], 0, [[(at, 0)] for at in range(narrow_count)]), 2),
        ],
        12,
        "combine_sums",
    )
    sums = sums.reshape(4, width)
    summed_gain = lax.dynamic_slice_in_dim(
        sums[:3], (wide_spot * narrow_count + narrow_spot) * gain_size, gain_size, 1
    )
    square_total = sums[3, 0] + jnp.sum(sums[:3] * sums[:3])
    grad_norm = jnp.sqrt(square_total) / loss_count
    factor = jnp.minimum(1.0, CLIP_NORM / (grad_norm + 1e-06)) / loss_count

    final_parts, factor = lax.optimization_barrier((grad_ffn, factor))
    size = width // narrow_count

    def final_piece(spot):
        return lax.dynamic_slice_in_dim(final_parts, spot * size, size, 2)

    pieces = [final_piece(narrow_spot)] + [
        shifted(final_piece(lax.rem(narrow_spot + step, narrow_count)), "narrow", step)
        for step in range(1, narrow_count)
    ]
    directions = newton(
        factor, mom_owned, owned, qo_owned, kv_owned
    )
    directions, pieces, ffn, factor = lax.optimization_barrier(
        (directions, pieces, ffn, factor)
    )
    summed_ffn = jnp.zeros((3, narrow_count, ffn_size, size), LOW)
    for step, piece in enumerate(pieces):
        source = lax.rem(narrow_spot - step + narrow_count, narrow_count)
        summed_ffn = lax.dynamic_update_index_in_dim(summed_ffn, piece, source, 1)
    summed_ffn = summed_ffn.reshape(3, ffn_rows, size).astype(FULL)
    received = [lax.dynamic_index_in_dim(directions, narrow_spot, 0, False)] + [
        shifted(
            lax.dynamic_index_in_dim(
                directions, lax.rem(narrow_spot + step, narrow_count), 0, False
            ),
            "narrow",
            step,
        )
        for step in range(1, narrow_count)
    ]

    def direction_of(matrix):
        step = lax.rem(narrow_spot - matrix - turn + 2 * narrow_count, narrow_count)
        result = received[0]
        for at in range(1, narrow_count):
            result = jnp.where(step == at, received[at], result)
        return result

    dir_ffn = jnp.stack([direction_of(matrix) for matrix in range(3)]).astype(FULL)
    small = direction_of(3).astype(FULL)
    dir_qo = small[: 2 * block_rows].reshape(mom_qo.shape)
    dir_kv = small[2 * block_rows : 2 * block_rows + half_rows].reshape(half_rows, 4, kv_size)
    dir_kv = jnp.moveaxis(dir_kv, 1, 0).reshape(mom_kv.shape)

    embed_new, embed_m_new, embed_v_new = adamw(
        embed, embed_m, embed_v, summed_table * factor, RATE_ADAM, WEIGHT_DECAY
    )
    gains_new, gains_m_new, gains_v_new = adamw(
        gains, gains_m, gains_v, summed_gain * factor, RATE_GAIN, 0.0
    )

    def mom_next(mom, grad):
        return MOMENTUM * mom + jnp.moveaxis(grad * factor, 0, 1)

    shrink = 1.0 - RATE_MUON * WEIGHT_DECAY

    def weight_next(weight, direction):
        return weight * shrink - RATE_MUON * jnp.moveaxis(direction, 0, 1)

    return (
        loss_sum,
        loss_count,
        grad_norm,
        embed_new,
        embed_m_new,
        embed_v_new,
        weight_next(attn_qo, dir_qo),
        mom_next(attn_qo_mom, summed_qo),
        weight_next(attn_kv, dir_kv),
        mom_next(attn_kv_mom, summed_kv),
        weight_next(ffn, dir_ffn),
        mom_next(ffn_mom, summed_ffn),
        gains_new,
        gains_m_new,
        gains_v_new,
    )


def solution(mesh):
    by_pack = P("wide", None)
    table = P("narrow", "wide")
    layer = P("wide", None, "narrow")
    gain = P(None, ("wide", "narrow"))
    return jax.shard_map(
        per_device,
        mesh=mesh,
        in_specs=(by_pack,) * 4 + (P("wide"),) + (table,) * 3 + (layer,) * 6 + (gain,) * 3,
        out_specs=(P(),) * 3 + (table,) * 3 + (layer,) * 6 + (gain,) * 3,
        check_vma=False,
    )
```

```python
import functools

import jax
import jax.numpy as jnp
from jax import lax
from jax.experimental import pallas as pl
from jax.experimental.pallas import tpu as pltpu
from jax.sharding import PartitionSpec as P

HEADS = 16
HD = 128
KVH = 4
NS_STEPS = 5
STEP = 10


NORM_EPS = 1e-05
ROPE_BASE = 10000.0
EXIT_EARLY = 0.25
EXIT_LAST = 1.0
CLIP_NORM = 0.02
BETA_ONE = 0.9
BETA_TWO = 0.95
ADAM_EPS = 1e-08
RATE_ADAM = 0.02
RATE_GAIN = 0.3
RATE_MUON = 0.3
WEIGHT_DECAY = 0.1
MOMENTUM = 0.95
NEWTON_A = 3.4445
NEWTON_B = -4.775
NEWTON_C = 2.0315
MASKED = -1e30
LOW = jnp.bfloat16
FULL = jnp.float32
BOTH = ("wide", "narrow")
UNROLL = 16
VMEM_BYTES = 56 * 1024 * 1024


def dot(first, second, first_dim, second_dim):
    return lax.dot_general(
        first, second, (((first_dim,), (second_dim,)), ((), ())), preferred_element_type=FULL
    )


def norm_rows(values, gain_row):
    return (
        values * lax.rsqrt(jnp.mean(values * values, axis=-1, keepdims=True) + NORM_EPS) * gain_row
    )


def segments_at(lens, where_at):
    ends = jnp.cumsum(lens)
    return jnp.sum((where_at[:, None] >= ends[None, :]).astype(jnp.int32), axis=1)


def angles_at(lens, where_at):
    segment = segments_at(lens, where_at)
    starts = jnp.cumsum(lens) - lens
    member = segment[:, None] == jnp.arange(lens.shape[0], dtype=jnp.int32)[None, :]
    begin = jnp.sum(jnp.where(member, starts[None, :], 0), axis=1)
    offset_pos = (where_at - begin).astype(FULL)
    inverse = ROPE_BASE ** (-2.0 * jnp.arange(HD // 2, dtype=FULL) / HD)
    angle = offset_pos[:, None] * inverse[None, :]
    return (segment, jnp.cos(angle), jnp.sin(angle))


MESH = pl.DeviceIdType.MESH
ANY = pl.BlockSpec(memory_space=pl.ANY)
VMEM = pl.BlockSpec(memory_space=pltpu.VMEM)


def others(axis, count):
    me = lax.axis_index(axis)
    return [{axis: lax.rem(me + step, count)} for step in range(1, count)]


def push(source, target, send, receive, device):
    return pltpu.make_async_remote_copy(
        src_ref=source,
        dst_ref=target,
        send_sem=send,
        recv_sem=receive,
        device_id=device,
        device_id_type=MESH,
    )


def arrived(block, send, receive, device):
    push(block, block, send, receive, device).wait_recv()


def like(values):
    return jax.ShapeDtypeStruct(values.shape, values.dtype)


def struct(shape, dtype):
    return jax.ShapeDtypeStruct(shape, dtype)


def sems(*shape):
    return pltpu.SemaphoreType.DMA(shape)


class Task:
    def __init__(self, inputs, outputs, scratch, steps, place_in, place_out, axes):
        self.inputs, self.outputs, self.scratch, self.steps = inputs, outputs, scratch, steps
        self.place_in = [place_in] * len(inputs)
        self.place_out = [place_out] * len(outputs)
        self.axes = axes


def launch(tasks, ident, name):
    axes = sorted(set(axis for task in tasks for axis in task.axes))
    inputs = [a for task in tasks for a in task.inputs]
    outputs = [a for task in tasks for a in task.outputs]
    scratch = [a for task in tasks for a in task.scratch]

    def body(*refs):
        refs = list(refs)
        ins = refs[: len(inputs)]
        outs = refs[len(inputs) : len(inputs) + len(outputs)]
        extra = refs[len(inputs) + len(outputs) :]
        barrier = pltpu.get_barrier_semaphore()
        targets = [device for axis in axes for device in others(axis, lax.axis_size(axis))]
        for device in targets:
            pl.semaphore_signal(barrier, inc=1, device_id=device, device_id_type=MESH)
        pl.semaphore_wait(barrier, len(targets))
        live = []
        for task in tasks:
            counts = (len(task.inputs), len(task.outputs), len(task.scratch))
            live.append(task.steps(ins[: counts[0]], outs[: counts[1]], extra[: counts[2]]))
            ins, outs, extra = ins[counts[0] :], outs[counts[1] :], extra[counts[2] :]
        while live:
            live = [steps for steps in live if next(steps, 0) is None]

    size = sum(a.size * a.dtype.itemsize for a in list(inputs) + list(outputs))
    return pl.pallas_call(
        body,
        out_shape=outputs,
        in_specs=[place for task in tasks for place in task.place_in],
        out_specs=[place for task in tasks for place in task.place_out],
        scratch_shapes=scratch,
        compiler_params=pltpu.CompilerParams(
            collective_id=ident, has_side_effects=True, vmem_limit_bytes=VMEM_BYTES
        ),
        cost_estimate=pl.CostEstimate(flops=0, bytes_accessed=size // 8, transcendentals=0),
        name=name,
    )(*inputs)


def later(task, turns):
    begin = task.steps

    def steps(ins, outs, scratch):
        for turn in range(turns):
            yield
        yield from begin(ins, outs, scratch)

    task.steps = steps
    return task


def gather_wide(values, patience=1):
    count = lax.axis_size("wide")
    chips = count // 2

    def steps(ins, outs, scratch):
        (x_ref,), (out_ref,), (send, receive, local) = ins, outs, scratch
        me = lax.axis_index("wide")
        mate = me + 1 - 2 * lax.rem(me, 2)
        peers = [lax.rem(me + 2 * step, count) for step in range(1, chips)] + [mate]
        first = []
        for step, peer in enumerate(peers):
            copy = push(x_ref, out_ref.at[me], send.at[step], receive.at[me], {"wide": peer})
            copy.start()
            first.append(copy)
        keep = pltpu.make_async_copy(x_ref, out_ref.at[me], local)
        keep.start()
        for turn in range(patience):
            yield
        second = []
        for step in range(1, chips):
            source = lax.rem(me - 2 * step + count, count)
            block = out_ref.at[source]
            arrived(block, send.at[0], receive.at[source], {"wide": mate})
            copy = push(
                block, block, send.at[chips + step - 1], receive.at[source], {"wide": mate}
            )
            copy.start()
            second.append(copy)
        yield
        for step in range(chips):
            source = lax.rem(mate - 2 * step + count, count)
            arrived(out_ref.at[source], send.at[0], receive.at[source], {"wide": mate})
        for copy in first + second:
            copy.wait_send()
        keep.wait()

    shape = struct((count,) + values.shape, values.dtype)
    return Task(
        [values], [shape], [sems(count - 1), sems(count), sems()], steps, ANY, ANY, ["wide"]
    )


def trade(axis, values, source_of, target_of, shape, patience=2, rest=None, rest_at=None):
    count = lax.axis_size(axis)
    inputs = [values] if rest is None else [values, rest]

    def steps(ins, outs, scratch):
        (x_ref, *rest_ref), (out_ref,), (send, receive, local) = ins, outs, scratch
        me = lax.axis_index(axis)
        copies = []
        for step in range(1, count):
            peer = lax.rem(me + step, count)
            copy = push(
                source_of(x_ref, peer),
                target_of(out_ref, me),
                send.at[step - 1],
                receive.at[me],
                {axis: peer},
            )
            copy.start()
            copies.append(copy)
        keeps = [pltpu.make_async_copy(source_of(x_ref, me), target_of(out_ref, me), local.at[0])]
        if rest is not None:
            keeps.append(pltpu.make_async_copy(rest_ref[0], rest_at(out_ref), local.at[1]))
        for keep in keeps:
            keep.start()
        for turn in range(patience):
            yield
        for step in range(1, count):
            source = lax.rem(me - step + count, count)
            arrived(
                target_of(out_ref, source), send.at[0], receive.at[source], {axis: source}
            )
        for copy in copies:
            copy.wait_send()
        for keep in keeps:
            keep.wait()

    return Task(
        inputs,
        [struct(shape, values.dtype)],
        [sems(count - 1), sems(count), sems(2)],
        steps,
        ANY,
        ANY,
        [axis],
    )


def block_at(ref, spot):
    return ref.at[spot]


def whole_at(ref, spot):
    return ref


def columns_of(size):
    def at(ref, spot):
        return ref.at[:, pl.ds(pl.multiple_of(spot * size, size), size)]

    return at


def turned(ref, spot):
    count = lax.axis_size("narrow")
    matrix = lax.rem(spot + count - lax.rem(lax.axis_index("wide"), 2), count)
    return ref.at[jnp.minimum(matrix, 3)]


def swap_turned(values, patience=2):
    shape = (lax.axis_size("narrow"),) + values.shape[1:]
    return trade("narrow", values, turned, block_at, shape, patience)


def product(lefts, rights, dim, order, pause=True, last=None):
    count, rows = len(order), lefts[0].shape[-1 if dim == 0 else -2]
    columns = rights[0].shape[1]
    block = min(512, columns)

    def steps(ins, outs, scratch):
        left_refs, right_refs = ins[: len(lefts)], ins[len(lefts) :]
        result_ref, square_ref = outs
        square_ref[...] = jnp.zeros_like(square_ref)

        def left_of(member):
            return left_refs[0][member] if lefts[0].ndim == 3 else left_refs[member][...]

        def fill(at, members, shift):
            def strip(part, carry):
                spot = pl.ds(pl.multiple_of(part * block, block), block)
                value = jnp.zeros((rows, block), FULL)
                for left, right in members:
                    value = value + dot(left_of(left), right_refs[right + shift][:, spot], dim, 0)
                result_ref[at, :, spot] = value.astype(LOW)
                square_ref[:, spot] = square_ref[:, spot] + jnp.sum(
                    value * value, axis=0, keepdims=True
                )
                return carry

            lax.fori_loop(0, columns // block, strip, 0)

        for at, members in enumerate(order):
            if last is None:
                fill(at, members, 0)
            else:
                pl.when(last())(functools.partial(fill, at, members, 1))
                pl.when(jnp.logical_not(last()))(functools.partial(fill, at, members, 0))
            if pause:
                yield

    return Task(
        list(lefts) + list(rights),
        [struct((count, rows, columns), LOW), struct((1, columns), FULL)],
        [],
        steps,
        VMEM,
        VMEM,
        [],
    )


def exit_stats(features, table, targets):
    rows, vocab = features.shape[0], table.shape[0]
    block = min(256, vocab)

    def steps(ins, outs, scratch):
        features_ref, table_ref, targets_ref = ins
        logits_ref, stats_ref = outs

        def strip(part):
            return pl.ds(pl.multiple_of(part * block, block), block)

        def over(function, start):
            return lax.fori_loop(0, vocab // block, function, start)

        def fill(part, peak):
            logits = dot(table_ref[strip(part), :], features_ref[...], 1, 1)
            logits_ref[strip(part), :] = logits
            return jnp.maximum(peak, jnp.max(logits, axis=0, keepdims=True))

        peak = over(fill, jnp.full((1, rows), MASKED, FULL))
        lines = lax.broadcasted_iota(jnp.int32, (block, rows), 0)

        def add(part, carry):
            total, picked = carry
            logits = logits_ref[strip(part), :]
            hit = lines + part * block == targets_ref[...]
            return (
                total + jnp.sum(jnp.exp(logits - peak), axis=0, keepdims=True),
                picked + jnp.sum(jnp.where(hit, logits, 0.0), axis=0, keepdims=True),
            )

        zero = jnp.zeros((1, rows), FULL)
        total, picked = over(add, (zero, zero))
        stats_ref[0:1, :] = peak
        stats_ref[1:2, :] = total
        stats_ref[2:3, :] = picked
        yield

    return Task(
        [features, table, targets],
        [struct((vocab, rows), FULL), struct((3, rows), FULL)],
        [],
        steps,
        VMEM,
        VMEM,
        [],
    )


def swap_owned(values, patience):
    count = lax.axis_size("narrow")

    def steps(ins, outs, scratch):
        (x_ref,), (out_ref,), (send, receive, local) = ins, outs, scratch
        me = lax.axis_index("narrow")
        turn = lax.rem(lax.axis_index("wide"), 2)

        def matrix_of(device):
            return lax.rem(device + count - turn, count)

        def copy_to(step):
            peer = lax.rem(me + step, count)
            return push(
                x_ref.at[jnp.minimum(matrix_of(peer), 2)],
                out_ref.at[me],
                send.at[step - 1],
                receive.at[me],
                {"narrow": peer},
            )

        def keep():
            return pltpu.make_async_copy(
                x_ref.at[jnp.minimum(matrix_of(me), 2)], out_ref.at[me], local
            )

        keep().start()
        for step in range(1, count):

            @pl.when(matrix_of(lax.rem(me + step, count)) < 3)
            def _():
                copy_to(step).start()

        for turn_at in range(patience):
            yield

        @pl.when(matrix_of(me) < 3)
        def _():
            for step in range(1, count):
                source = lax.rem(me - step + count, count)
                arrived(out_ref.at[source], send.at[0], receive.at[source], {"narrow": source})

        for step in range(1, count):

            @pl.when(matrix_of(lax.rem(me + step, count)) < 3)
            def _():
                copy_to(step).wait_send()

        keep().wait()

    return Task(
        [values],
        [struct((count,) + values.shape[1:], values.dtype)],
        [sems(count - 1), sems(count), sems()],
        steps,
        ANY,
        ANY,
        ["narrow"],
    )


def send_owner(values):
    count = lax.axis_size("narrow")

    def steps(ins, outs, scratch):
        (x_ref,), (out_ref,), (send, receive, local) = ins, outs, scratch
        me = lax.axis_index("narrow")
        owner = lax.rem(3 + lax.rem(lax.axis_index("wide"), 2), count)
        keep = pltpu.make_async_copy(x_ref, out_ref.at[me], local)
        keep.start()

        def to_owner():
            return push(x_ref, out_ref.at[me], send.at[0], receive.at[me], {"narrow": owner})

        @pl.when(me != owner)
        def _():
            to_owner().start()

        yield
        yield

        @pl.when(me != owner)
        def _():
            to_owner().wait_send()

        @pl.when(me == owner)
        def _():
            for step in range(1, count):
                source = lax.rem(owner + step, count)
                arrived(out_ref.at[source], send.at[0], receive.at[source], {"narrow": source})

        keep.wait()

    return Task(
        [values],
        [struct((count,) + values.shape, values.dtype)],
        [sems(1), sems(count), sems()],
        steps,
        ANY,
        ANY,
        ["narrow"],
    )


def swap_blocks(axis, values):
    return trade(axis, values, block_at, block_at, values.shape)


def gather_blocks(axis, values):
    shape = (lax.axis_size(axis),) + values.shape
    return trade(axis, values, whole_at, block_at, shape)


def split_columns(axis, values, patience=2):
    count = lax.axis_size(axis)
    rows, size = values.shape[0], values.shape[1] // count
    return trade(axis, values, columns_of(size), block_at, (count, rows, size), patience)


def join_columns(axis, values):
    count, rows, size = values.shape
    return trade(axis, values, block_at, columns_of(size), (rows, count * size))


def join_below(axis, values, rest):
    count, rows, size = values.shape
    above = rest.shape[0]

    def target_of(ref, spot):
        return ref.at[above:, pl.ds(pl.multiple_of(spot * size, size), size)]

    shape = (above + rows, count * size)
    return trade(
        axis, values, block_at, target_of, shape, 2, rest, lambda ref: ref.at[:above]
    )


def swap_below(values, rest):
    count, above, size = rest.shape
    shape = (count, above + values.shape[1], size)

    def target_of(ref, spot):
        return ref.at[spot, above:]

    return trade(
        "narrow", values, turned, target_of, shape, 2, rest, lambda ref: ref.at[:, :above]
    )


def collect(count, parts_ref, slots, send, receive):
    me = lax.axis_index("narrow")
    copies = []
    for step in range(1, count):
        peer = lax.rem(me + step, count)
        copy = push(
            parts_ref.at[peer],
            slots.at[me],
            send.at[step - 1],
            receive.at[me],
            {"narrow": peer},
        )
        copy.start()
        copies.append(copy)
    return copies


def collected(count, parts_ref, slots, send, receive):
    me = lax.axis_index("narrow")
    total = parts_ref[me].astype(FULL)
    for step in range(1, count):
        source = lax.rem(me - step + count, count)
        arrived(slots.at[source], send.at[0], receive.at[source], {"narrow": source})
        total = total + slots[source].astype(FULL)
    return total


def share(count, low, all_ref, send, receive):
    me = lax.axis_index("narrow")
    all_ref[me] = low
    copies = []
    for step in range(1, count):
        peer = lax.rem(me + step, count)
        copy = push(
            all_ref.at[me], all_ref.at[me], send.at[step - 1], receive.at[me], {"narrow": peer}
        )
        copy.start()
        copies.append(copy)
    return copies


def shared(count, all_ref, send, receive):
    me = lax.axis_index("narrow")
    for step in range(1, count):
        source = lax.rem(me - step + count, count)
        arrived(all_ref.at[source], send.at[0], receive.at[source], {"narrow": source})


def narrow_sems(count):
    return [sems(count - 1), sems(count)]


def settle(partial, base, other, keep_row, gain_row):
    count = lax.axis_size("narrow")
    rows, width = base.shape

    def steps(ins, outs, scratch):
        parts_ref, base_ref, other_ref, keep_ref, gain_ref = ins
        own_ref, all_ref = outs
        slots, send, receive, send_all, receive_all = scratch
        copies = collect(count, parts_ref, slots, send, receive)
        yield
        total = collected(count, parts_ref, slots, send, receive)
        total = jnp.where(keep_ref[...] > 0, total + base_ref[...], other_ref[...])
        own_ref[...] = total
        low = norm_rows(total, gain_ref[...]).astype(LOW)
        copies = copies + share(count, low, all_ref, send_all, receive_all)
        yield
        shared(count, all_ref, send_all, receive_all)
        for copy in copies:
            copy.wait_send()

    return Task(
        [partial.reshape(count, rows, width), base, other, keep_row, gain_row],
        [struct((rows, width), FULL), struct((count, rows, width), LOW)],
        [pltpu.VMEM((count, rows, width), partial.dtype)]
        + narrow_sems(count)
        + narrow_sems(count),
        steps,
        VMEM,
        VMEM,
        ["narrow"],
    )


def settle_back(partial, values, add, keep_row, gain_row):
    count = lax.axis_size("narrow")
    rows, width = values.shape

    def steps(ins, outs, scratch):
        parts_ref, values_ref, add_ref, keep_ref, gain_ref = ins
        own_ref, gain_grad_ref, all_ref = outs
        slots, send, receive, send_all, receive_all = scratch
        copies = collect(count, parts_ref, slots, send, receive)
        yield
        grad = collected(count, parts_ref, slots, send, receive)
        held = values_ref[...]
        root = lax.rsqrt(jnp.mean(held * held, axis=-1, keepdims=True) + NORM_EPS)
        scaled = gain_ref[...] * grad
        inner = jnp.mean(held * scaled, axis=-1, keepdims=True)
        own = add_ref[...] + root * scaled - held * (root * root * root * inner)
        gain_grad_ref[...] = jnp.sum(held * root * grad, axis=0, keepdims=True)
        own_ref[...] = own
        low = (own * keep_ref[...]).astype(LOW)
        copies = copies + share(count, low, all_ref, send_all, receive_all)
        yield
        shared(count, all_ref, send_all, receive_all)
        for copy in copies:
            copy.wait_send()

    return Task(
        [partial.reshape(count, rows, width), values, add, keep_row, gain_row],
        [
            struct((rows, width), FULL),
            struct((1, width), FULL),
            struct((count, rows, width), LOW),
        ],
        [pltpu.VMEM((count, rows, width), partial.dtype)]
        + narrow_sems(count)
        + narrow_sems(count),
        steps,
        VMEM,
        VMEM,
        ["narrow"],
    )


def sum_narrow(partial):
    count = lax.axis_size("narrow")
    rows, width = partial.shape[0] // count, partial.shape[1]

    def steps(ins, outs, scratch):
        (parts_ref,), (own_ref,), (slots, send, receive) = ins, outs, scratch
        copies = collect(count, parts_ref, slots, send, receive)
        yield
        yield
        own_ref[...] = collected(count, parts_ref, slots, send, receive)
        for copy in copies:
            copy.wait_send()

    return Task(
        [partial.reshape(count, rows, width)],
        [struct((rows, width), FULL)],
        [pltpu.VMEM((count, rows, width), partial.dtype)] + narrow_sems(count),
        steps,
        VMEM,
        VMEM,
        ["narrow"],
    )


def fetch_rows(found, rows):
    deep, wide = lax.axis_size("narrow"), lax.axis_size("wide")
    columns = found.shape[2]

    def steps(ins, outs, scratch):
        (found_ref,), (out_ref,) = ins, outs
        rightward, leftward, final = scratch[:3]
        send_right, receive_right, send_left, receive_left = scratch[3:7]
        send_wide, receive_wide, local = scratch[7:]
        spot = lax.axis_index("narrow")
        me = lax.axis_index("wide")

        def right_copy(part, source):
            return push(
                source,
                rightward.at[part],
                send_right.at[part],
                receive_right.at[part],
                {"narrow": lax.rem(spot + 1, deep)},
            )

        def left_copy(part, source):
            return push(
                source,
                leftward.at[part],
                send_left.at[part],
                receive_left.at[part],
                {"narrow": lax.rem(spot + deep - 1, deep)},
            )

        for step in range(deep - 1):
            right, left = deep - 1 - step, step

            @pl.when((spot == 0) & (right > 0))
            def _():
                right_copy(right, found_ref.at[right]).start()

            @pl.when((spot == deep - 1) & (left < deep - 1))
            def _():
                left_copy(left, found_ref.at[left]).start()

        yield
        for step in range(deep - 1):
            right, left = deep - 1 - step, step

            def pass_right():
                right_copy(right, rightward.at[right]).wait_recv()
                rightward[right] = rightward[right] + found_ref[right]
                right_copy(right, rightward.at[right]).start()

            pl.when((spot > 0) & (right > spot) & (2 * spot < deep))(pass_right)

            @pl.when((spot < deep - 1) & (left < spot))
            def _():
                left_copy(left, leftward.at[left]).wait_recv()
                leftward[left] = leftward[left] + found_ref[left]
                left_copy(left, leftward.at[left]).start()

            pl.when((right > spot) & (2 * spot >= deep))(pass_right)

        final[...] = found_ref[spot]

        @pl.when(spot > 0)
        def _():
            right_copy(spot, rightward.at[spot]).wait_recv()
            final[...] = final[...] + rightward[spot]

        @pl.when(spot < deep - 1)
        def _():
            left_copy(spot, leftward.at[spot]).wait_recv()
            final[...] = final[...] + leftward[spot]

        def rows_for(device):
            return final.at[pl.ds(pl.multiple_of(device * rows, rows), rows)]

        def columns_from(device):
            return columns_of(columns)(out_ref, device)

        copies = []
        for step in range(1, wide):
            peer = lax.rem(me + step, wide)
            copy = push(
                rows_for(peer),
                columns_from(me),
                send_wide.at[step - 1],
                receive_wide.at[me],
                {"wide": peer},
            )
            copy.start()
            copies.append(copy)
        keep = pltpu.make_async_copy(rows_for(me), columns_from(me), local)
        keep.start()
        yield
        for step in range(1, wide):
            source = lax.rem(me - step + wide, wide)
            arrived(
                columns_from(source), send_wide.at[0], receive_wide.at[source], {"wide": source}
            )
        yield
        for copy in copies:
            copy.wait_send()
        keep.wait()
        for step in range(deep - 1):
            right, left = deep - 1 - step, step

            @pl.when(right > spot)
            def _():
                right_copy(right, found_ref.at[right]).wait_send()

            @pl.when(left < spot)
            def _():
                left_copy(left, found_ref.at[left]).wait_send()

    task = Task(
        [found],
        [struct((rows, wide * columns), found.dtype)],
        [pltpu.VMEM(found.shape, found.dtype)] * 2
        + [pltpu.VMEM(found.shape[1:], found.dtype)]
        + [sems(deep)] * 4
        + [sems(wide - 1), sems(wide), sems()],
        steps,
        VMEM,
        ANY,
        ["narrow", "wide"],
    )
    return task


def return_rows(rows):
    deep, wide = lax.axis_size("narrow"), lax.axis_size("wide")
    count, width = rows.shape
    columns = width // wide

    def steps(ins, outs, scratch):
        (rows_ref,), (out_ref,) = ins, outs
        send_right, send_left, receive_deep, send_wide, receive_wide, local = scratch
        spot = lax.axis_index("narrow")
        me = lax.axis_index("wide")
        part_of = functools.partial(columns_of(columns), rows_ref)

        def landing(device):
            return out_ref.at[spot, pl.ds(pl.multiple_of(device * count, count), count)]

        copies = []
        for step in range(1, wide):
            peer = lax.rem(me + step, wide)
            copy = push(
                part_of(peer),
                landing(me),
                send_wide.at[step - 1],
                receive_wide.at[me],
                {"wide": peer},
            )
            copy.start()
            copies.append(copy)
        keep = pltpu.make_async_copy(part_of(me), landing(me), local)
        keep.start()
        yield
        for step in range(1, wide):
            source = lax.rem(me - step + wide, wide)
            arrived(landing(source), send_wide.at[0], receive_wide.at[source], {"wide": source})
        keep.wait()

        def right_copy(part):
            return push(
                out_ref.at[part],
                out_ref.at[part],
                send_right.at[part],
                receive_deep.at[part],
                {"narrow": lax.rem(spot + 1, deep)},
            )

        def left_copy(part):
            return push(
                out_ref.at[part],
                out_ref.at[part],
                send_left.at[part],
                receive_deep.at[part],
                {"narrow": lax.rem(spot + deep - 1, deep)},
            )

        @pl.when(spot < deep - 1)
        def _():
            right_copy(spot).start()

        @pl.when(spot > 0)
        def _():
            left_copy(spot).start()

        for step in range(1, deep):
            yield

            @pl.when(spot >= step)
            def _():
                right_copy(spot - step).wait_recv()

                @pl.when(spot < deep - 1)
                def _():
                    right_copy(spot - step).start()

            @pl.when(spot + step < deep)
            def _():
                left_copy(spot + step).wait_recv()

                @pl.when(spot > 0)
                def _():
                    left_copy(spot + step).start()

        for part in range(deep):

            @pl.when((part <= spot) & (spot < deep - 1))
            def _():
                right_copy(part).wait_send()

            @pl.when((part >= spot) & (spot > 0))
            def _():
                left_copy(part).wait_send()

        for copy in copies:
            copy.wait_send()

    return Task(
        [rows],
        [struct((deep, wide * count, columns), rows.dtype)],
        [sems(deep)] * 3 + [sems(wide - 1), sems(wide), sems()],
        steps,
        ANY,
        ANY,
        ["narrow", "wide"],
    )


def sum_wide(partial):
    count = lax.axis_size("wide")
    chips = count // 2
    rows, width = partial.shape[0] // count, partial.shape[1]

    def steps(ins, outs, scratch):
        (parts_ref,), (out_ref,) = ins, outs
        from_mate, paired, slots, send_mate, receive_mate, send, receive = scratch
        me = lax.axis_index("wide")
        side = lax.rem(me, 2)
        mate = me + 1 - 2 * side
        my_chip = me // 2
        mate_copies = []
        for step in range(chips):
            chip = lax.rem(my_chip + 1 + step, chips)
            copy = push(
                parts_ref.at[2 * chip + 1 - side],
                from_mate.at[chip],
                send_mate.at[step],
                receive_mate.at[chip],
                {"wide": mate},
            )
            copy.start()
            mate_copies.append(copy)
        yield
        copies = []
        for step in range(chips):
            chip = lax.rem(my_chip + 1 + step, chips)
            arrived(from_mate.at[chip], send_mate.at[0], receive_mate.at[chip], {"wide": mate})
            both = parts_ref[2 * chip + side].astype(FULL) + from_mate[chip].astype(FULL)
            if step < chips - 1:
                paired[chip] = both.astype(LOW)
                copy = push(
                    paired.at[chip],
                    slots.at[my_chip],
                    send.at[step],
                    receive.at[my_chip],
                    {"wide": 2 * chip + side},
                )
                copy.start()
                copies.append(copy)
            else:
                out_ref[...] = both
        yield
        for step in range(1, chips):
            chip = lax.rem(my_chip - step + chips, chips)
            arrived(slots.at[chip], send.at[0], receive.at[chip], {"wide": 2 * chip + side})
            out_ref[...] = out_ref[...] + slots[chip].astype(FULL)
        for copy in mate_copies + copies:
            copy.wait_send()

    return Task(
        [partial.reshape(count, rows, width)],
        [struct((rows, width), FULL)],
        [pltpu.VMEM((chips, rows, width), LOW)] * 3
        + [sems(chips), sems(chips), sems(max(chips - 1, 1)), sems(chips)],
        steps,
        VMEM,
        VMEM,
        ["wide"],
    )


def merge_stats(first, second):
    peak = jnp.maximum(first[0:1], second[0:1])
    total = first[1:2] * jnp.exp(first[0:1] - peak) + second[1:2] * jnp.exp(second[0:1] - peak)
    return jnp.concatenate([peak, total, first[2:3] + second[2:3]], axis=0)


def add_two(first, second):
    return first + second


def combine(values, join):
    deep, wide = lax.axis_size("narrow"), lax.axis_size("wide")

    def steps(ins, outs, scratch):
        (x_ref,), (out_ref,) = ins, outs
        wide_slots, deep_slots, send_wide, receive_wide, send_deep, receive_deep = scratch

        def start(axis, count, slots, value, send, receive):
            me = lax.axis_index(axis)
            slots[me] = value
            copies = []
            for step in range(1, count):
                peer = lax.rem(me + step, count)
                copy = push(
                    slots.at[me], slots.at[me], send.at[step - 1], receive.at[me], {axis: peer}
                )
                copy.start()
                copies.append(copy)
            return copies

        def finish(axis, count, slots, send, receive):
            me = lax.axis_index(axis)
            for step in range(1, count):
                source = lax.rem(me - step + count, count)
                arrived(slots.at[source], send.at[0], receive.at[source], {axis: source})
            total = slots[0]
            for source in range(1, count):
                total = join(total, slots[source])
            return total

        first = start("wide", wide, wide_slots, x_ref[...], send_wide, receive_wide)
        yield
        total = finish("wide", wide, wide_slots, send_wide, receive_wide)
        second = start("narrow", deep, deep_slots, total, send_deep, receive_deep)
        yield
        out_ref[...] = finish("narrow", deep, deep_slots, send_deep, receive_deep)
        for copy in first + second:
            copy.wait_send()

    return Task(
        [values],
        [like(values)],
        [
            pltpu.VMEM((wide,) + values.shape, values.dtype),
            pltpu.VMEM((deep,) + values.shape, values.dtype),
            sems(wide - 1),
            sems(wide),
            sems(deep - 1),
            sems(deep),
        ],
        steps,
        VMEM,
        VMEM,
        ["narrow", "wide"],
    )


def gather_both(values):
    deep, wide = lax.axis_size("narrow"), lax.axis_size("wide")

    def steps(ins, outs, scratch):
        (x_ref,), (out_ref,) = ins, outs
        send_wide, receive_wide, send_deep, receive_deep = scratch
        me = lax.axis_index("wide")
        spot = lax.axis_index("narrow")
        out_ref[spot, me] = x_ref[...]
        copies = []
        for step in range(1, wide):
            peer = lax.rem(me + step, wide)
            block = out_ref.at[spot, me]
            copy = push(block, block, send_wide.at[step - 1], receive_wide.at[me], {"wide": peer})
            copy.start()
            copies.append(copy)
        yield
        for step in range(1, wide):
            source = lax.rem(me - step + wide, wide)
            block = out_ref.at[spot, source]
            arrived(block, send_wide.at[0], receive_wide.at[source], {"wide": source})
        for step in range(1, deep):
            peer = lax.rem(spot + step, deep)
            block = out_ref.at[spot]
            copy = push(
                block, block, send_deep.at[step - 1], receive_deep.at[spot], {"narrow": peer}
            )
            copy.start()
            copies.append(copy)
        yield
        for step in range(1, deep):
            source = lax.rem(spot - step + deep, deep)
            block = out_ref.at[source]
            arrived(block, send_deep.at[0], receive_deep.at[source], {"narrow": source})
        for copy in copies:
            copy.wait_send()

    return Task(
        [values],
        [struct((deep, wide) + values.shape, values.dtype)],
        [sems(wide - 1), sems(wide), sems(deep - 1), sems(deep)],
        steps,
        VMEM,
        VMEM,
        ["narrow", "wide"],
    )


def turn_heads(values, cosine, sine):
    half = values.shape[1] // 2
    swapped = jnp.concatenate([values[:, half:], values[:, :half]], axis=1)
    return values * cosine + swapped * sine


def wide_angles(cosine, sine):
    return jnp.concatenate([cosine, cosine], axis=1), jnp.concatenate([-sine, sine], axis=1)


def local_call(body, inputs, specs, outputs, flops, name):
    return pl.pallas_call(
        body,
        grid=(1,),
        in_specs=specs,
        out_specs=[
            pl.BlockSpec(a.shape, lambda step, rank=len(a.shape): (0,) * rank) for a in outputs
        ],
        out_shape=outputs,
        compiler_params=pltpu.CompilerParams(vmem_limit_bytes=VMEM_BYTES),
        cost_estimate=pl.CostEstimate(flops=flops, bytes_accessed=8 << 20, transcendentals=0),
        name=name,
    )(*inputs)


def entire(values):
    return pl.BlockSpec(values.shape, lambda step: (0,) * values.ndim)


def column_block(values, size, index):
    return pl.BlockSpec((values.shape[0], size), lambda step: (0, index))


def heads_body(groups, rep, rows_ref, gain_ref, kv_ref, cos_ref, sin_ref, out_ref, normed_ref):
    count, _, _, tok_rows, head = out_ref.shape
    size = kv_ref.shape[1] // (2 * count)
    per_head = head // size
    rows = rows_ref[0:tok_rows, :].astype(FULL)
    normed = norm_rows(rows, gain_ref[...]).astype(LOW)
    normed_ref[...] = normed
    both = dot(normed, kv_ref[...], 1, 0)

    def head_of(kind, index):
        pieces = [
            both[:, (2 * part + kind) * size : (2 * part + kind + 1) * size]
            for part in range(index * per_head, (index + 1) * per_head)
        ]
        return pieces[0] if per_head == 1 else jnp.concatenate(pieces, axis=1)

    for owner in range(count):
        for group in range(groups):
            index = (owner * groups + group) // rep
            keys = turn_heads(head_of(0, index), cos_ref[...], sin_ref[...])
            out_ref[owner, group, 0] = keys.astype(LOW)
            out_ref[owner, group, 1] = head_of(1, index).astype(LOW)


def make_heads(rows_low, gain_row, proj, cosine, sine, groups, rep):
    count = lax.axis_size("narrow")
    tok_rows, head = cosine.shape
    width = rows_low.shape[1]
    size = 2 * KVH * HD
    return local_call(
        functools.partial(heads_body, groups, rep),
        [rows_low, gain_row, proj, cosine, sine],
        [entire(rows_low), entire(gain_row), column_block(proj, size, 0)]
        + [entire(cosine), entire(sine)],
        [struct((count, groups, 2, tok_rows, head), LOW), struct((tok_rows, width), LOW)],
        2 * tok_rows * width * size,
        "make_heads",
    )


def attend_body(
    start_ref,
    gains_ref,
    q_ref,
    o_ref,
    kv_ref,
    cos_ref,
    sin_ref,
    seg_ref,
    seg_all_ref,
    pick_ref,
    queries_ref,
    probs_ref,
    mixed_ref,
    part_ref,
    normed_ref,
    early_ref,
):
    count, groups, _, tok_rows, head = kv_ref.shape
    heads_own = probs_ref.shape[0]
    start = start_ref[...].astype(FULL)
    root = lax.rsqrt(jnp.mean(start * start, axis=-1, keepdims=True) + NORM_EPS)
    normed = (start * root * gains_ref[0:1, :]).astype(LOW)
    normed_ref[...] = normed
    early_ref[...] = (start * root * gains_ref[2:3, :]).astype(LOW)
    queries = dot(normed, q_ref[...], 1, 0)
    spots = lax.broadcasted_iota(jnp.int32, (1, count * tok_rows), 1)
    allowed = (seg_ref[...] == seg_all_ref[...]) & (pick_ref[...] >= spots)
    for group in range(groups):
        keys = jnp.concatenate([kv_ref[part, group, 0] for part in range(count)], axis=0)
        values = jnp.concatenate([kv_ref[part, group, 1] for part in range(count)], axis=0)
        for member in range(heads_own // groups):
            at = group * (heads_own // groups) + member
            spot = slice(at * head, (at + 1) * head)
            query = turn_heads(queries[:, spot], cos_ref[...], sin_ref[...]).astype(LOW)
            queries_ref[:, spot] = query
            scores = jnp.where(allowed, dot(query, keys, 1, 1) * head ** (-0.5), MASKED)
            shifted = jnp.exp(scores - jnp.max(scores, axis=-1, keepdims=True))
            probs = shifted / jnp.sum(shifted, axis=-1, keepdims=True)
            probs_ref[at] = probs
            mixed_ref[:, spot] = dot(probs.astype(LOW), values, 1, 0).astype(LOW)
    part_ref[...] = dot(mixed_ref[...], o_ref[...], 1, 1).astype(LOW)


def attend(start_low, gains, proj, own_head, cosine, sine, seg, seg_all, picks):
    count, groups, _, tok_rows, head = own_head.shape
    sel, width = start_low.shape
    heads_own = HEADS // count
    size = heads_own * head
    first = 2 * KVH * HD // size
    seq_len = count * tok_rows
    return local_call(
        attend_body,
        [start_low, gains, proj, proj, own_head, cosine, sine, seg, seg_all, picks],
        [
            entire(start_low),
            entire(gains),
            column_block(proj, size, first),
            column_block(proj, size, first + 1),
        ]
        + [entire(a) for a in (own_head, cosine, sine, seg, seg_all, picks)],
        [
            struct((sel, size), LOW),
            struct((heads_own, sel, seq_len), FULL),
            struct((sel, size), LOW),
            struct((sel, width), LOW),
            struct((sel, width), LOW),
            struct((sel, width), LOW),
        ],
        4 * sel * size * (width + seq_len),
        "attend",
    )


def attend_back_body(
    grad_ref,
    q_ref,
    o_ref,
    kv_ref,
    queries_ref,
    probs_ref,
    cos_ref,
    sin_ref,
    cos_all_ref,
    sin_all_ref,
    out_ref,
    grad_q_ref,
    part_ref,
):
    count, groups, _, tok_rows, head = kv_ref.shape
    heads_own = probs_ref.shape[0]
    scale = head ** (-0.5)
    grad_mixed = dot(grad_ref[...], o_ref[...], 1, 0).astype(LOW)
    for group in range(groups):
        keys = jnp.concatenate([kv_ref[part, group, 0] for part in range(count)], axis=0)
        values = jnp.concatenate([kv_ref[part, group, 1] for part in range(count)], axis=0)
        grad_keys = jnp.zeros(keys.shape, FULL)
        grad_values = jnp.zeros(keys.shape, FULL)
        for member in range(heads_own // groups):
            at = group * (heads_own // groups) + member
            spot = slice(at * head, (at + 1) * head)
            probs = probs_ref[at]
            grad_probs = dot(grad_mixed[:, spot], values, 1, 1)
            inner = jnp.sum(probs * grad_probs, axis=-1, keepdims=True)
            grad_scores = (probs * (grad_probs - inner)).astype(LOW)
            grad_query = dot(grad_scores, keys, 1, 0) * scale
            grad_q_ref[:, spot] = turn_heads(grad_query, cos_ref[...], -sin_ref[...]).astype(LOW)
            grad_keys = grad_keys + dot(grad_scores, queries_ref[:, spot], 0, 0)
            grad_values = grad_values + dot(probs.astype(LOW), grad_mixed[:, spot], 0, 0)
        grad_keys = turn_heads(grad_keys * scale, cos_all_ref[...], -sin_all_ref[...])
        for part in range(count):
            rows = slice(part * tok_rows, (part + 1) * tok_rows)
            out_ref[part, group, 0] = grad_keys[rows].astype(LOW)
            out_ref[part, group, 1] = grad_values[rows].astype(LOW)
    part_ref[...] = dot(grad_q_ref[...], q_ref[...], 1, 1).astype(LOW)


def attend_back(grad, proj, own_head, queries, probs, cosine, sine, cosine_all, sine_all):
    count, groups, _, tok_rows, head = own_head.shape
    sel, width = grad.shape
    size = queries.shape[1]
    first = 2 * KVH * HD // size
    return local_call(
        attend_back_body,
        [grad, proj, proj, own_head, queries, probs, cosine, sine, cosine_all, sine_all],
        [entire(grad), column_block(proj, size, first), column_block(proj, size, first + 1)]
        + [
            entire(a)
            for a in (own_head, queries, probs, cosine, sine, cosine_all, sine_all)
        ],
        [struct(own_head.shape, LOW), struct((sel, size), LOW), struct((sel, width), LOW)],
        8 * sel * size * width,
        "attend_back",
    )


def norm_back_rows(values, gain_row, grad):
    root = lax.rsqrt(jnp.mean(values * values, axis=-1, keepdims=True) + NORM_EPS)
    scaled = gain_row * grad
    inner = jnp.mean(values * scaled, axis=-1, keepdims=True)
    result = root * scaled - values * (root * root * root * inner)
    return result, jnp.sum(values * root * grad, axis=0, keepdims=True)


def rows_back_body(
    rep,
    rows_ref,
    gains_ref,
    kv_ref,
    heads_ref,
    pick_ref,
    early_ref,
    base_ref,
    out_ref,
    attn_gain_ref,
    early_gain_ref,
    grad_kv_ref,
):
    count, groups, _, tok_rows, head = heads_ref.shape
    size = kv_ref.shape[1] // (2 * count)
    per_head = head // size
    for index in range(KVH):
        for kind in range(2):
            copies = [
                heads_ref[at // groups, at % groups, kind]
                for at in range(index * rep, (index + 1) * rep)
            ]
            total = copies[0]
            if rep > 1:
                total = sum(copy.astype(FULL) for copy in copies).astype(LOW)
            for piece in range(per_head):
                lane = (2 * (index * per_head + piece) + kind) * size
                grad_kv_ref[:, lane : lane + size] = total[:, piece * size : (piece + 1) * size]
    values = rows_ref[...].astype(FULL)
    own = values[tok_rows:]
    tok_part, tok_gain = norm_back_rows(
        values[:tok_rows], gains_ref[0:1, :], dot(grad_kv_ref[...], kv_ref[...], 1, 1)
    )
    pick_part, pick_gain = norm_back_rows(own, gains_ref[0:1, :], pick_ref[...])
    early_part, early_gain = norm_back_rows(own, gains_ref[2:3, :], early_ref[...])
    attn_gain_ref[...] = tok_gain + pick_gain
    early_gain_ref[...] = early_gain
    out_ref[0:tok_rows, :] = tok_part.astype(LOW)
    out_ref[tok_rows:, :] = (pick_part + early_part + base_ref[...]).astype(LOW)


def rows_back(rows_low, gains, proj, heads, grad_pick, grad_early, base, rep):
    tok_rows = heads.shape[3]
    width = rows_low.shape[1]
    size = 2 * KVH * HD
    return local_call(
        functools.partial(rows_back_body, rep),
        [rows_low, gains, proj, heads, grad_pick, grad_early, base],
        [entire(rows_low), entire(gains), column_block(proj, size, 0)]
        + [entire(a) for a in (heads, grad_pick, grad_early, base)],
        [
            struct(rows_low.shape, LOW),
            struct((1, width), FULL),
            struct((1, width), FULL),
            struct((tok_rows, size), LOW),
        ],
        2 * tok_rows * width * size,
        "rows_back",
    )


def assemble_body(out_columns, *refs):
    pieces, out_ref = refs[:-1], refs[-1]
    count = len(pieces)
    me = lax.axis_index("narrow")
    for step, piece in enumerate(pieces):
        source = lax.rem(me - step + count, count)
        spot = pl.ds(pl.multiple_of(source * out_columns, out_columns), out_columns)
        out_ref[:, spot] = piece[...]


def assemble(pieces):
    rows, columns = pieces[0].shape
    outputs = [struct((rows, columns * len(pieces)), pieces[0].dtype)]
    return local_call(
        functools.partial(assemble_body, columns),
        list(pieces),
        [entire(piece) for piece in pieces],
        outputs,
        0,
        "assemble",
    )[0]


def feed_body(inner_ref, weight_ref, gate_ref, up_ref, hidden_ref, out_ref, total):
    part = pl.program_id(0)
    inner = inner_ref[...]
    gate = dot(inner, weight_ref[0, 0], 1, 1)
    up = dot(inner, weight_ref[0, 1], 1, 1)
    hidden = (jax.nn.silu(gate) * up).astype(LOW)
    gate_ref[0] = gate
    up_ref[0] = up
    hidden_ref[0] = hidden
    product = dot(hidden, weight_ref[0, 2], 1, 0)

    @pl.when(part == 0)
    def _():
        total[...] = product

    @pl.when(part > 0)
    def _():
        total[...] = total[...] + product

    @pl.when(part == pl.num_programs(0) - 1)
    def _():
        out_ref[...] = total[...].astype(LOW)


def feed(inner, weight):
    parts, _, size, width = weight.shape
    sel = inner.shape[0]
    same = pl.BlockSpec((sel, width), lambda part: (0, 0))
    slab = pl.BlockSpec((1, sel, size), lambda part: (part, 0, 0))
    return pl.pallas_call(
        feed_body,
        grid=(parts,),
        in_specs=[same, pl.BlockSpec((1, 3, size, width), lambda part: (part, 0, 0, 0))],
        out_specs=[slab, slab, slab, same],
        out_shape=[
            struct((parts, sel, size), FULL),
            struct((parts, sel, size), FULL),
            struct((parts, sel, size), LOW),
            struct((sel, width), LOW),
        ],
        scratch_shapes=[pltpu.VMEM((sel, width), FULL)],
        compiler_params=pltpu.CompilerParams(vmem_limit_bytes=VMEM_BYTES),
        cost_estimate=pl.CostEstimate(
            flops=6 * sel * parts * size * width,
            bytes_accessed=weight.size * 2,
            transcendentals=0,
        ),
        name="feed",
    )(inner, weight)


def feed_back_body(grad_ref, weight_ref, gate_ref, up_ref, hidden_ref, acts_ref, out_ref, total):
    part = pl.program_id(0)
    grad_hidden = dot(grad_ref[...], weight_ref[0, 2], 1, 1)
    gate = gate_ref[0]
    sigma = jax.nn.sigmoid(gate)
    grad_gate = (grad_hidden * up_ref[0] * sigma * (1.0 + gate * (1.0 - sigma))).astype(LOW)
    grad_up = (grad_hidden * gate * sigma).astype(LOW)
    acts_ref[0, 0] = grad_gate
    acts_ref[0, 1] = grad_up
    acts_ref[0, 2] = hidden_ref[0]
    product = dot(grad_gate, weight_ref[0, 0], 1, 0) + dot(grad_up, weight_ref[0, 1], 1, 0)

    @pl.when(part == 0)
    def _():
        total[...] = product

    @pl.when(part > 0)
    def _():
        total[...] = total[...] + product

    @pl.when(part == pl.num_programs(0) - 1)
    def _():
        out_ref[...] = total[...].astype(LOW)


def feed_back(grad, weight, gate, up, hidden):
    parts, _, size, width = weight.shape
    sel = grad.shape[0]
    same = pl.BlockSpec((sel, width), lambda part: (0, 0))
    slab = pl.BlockSpec((1, sel, size), lambda part: (part, 0, 0))
    return pl.pallas_call(
        feed_back_body,
        grid=(parts,),
        in_specs=[same, pl.BlockSpec((1, 3, size, width), lambda part: (part, 0, 0, 0))]
        + [slab] * 3,
        out_specs=[pl.BlockSpec((1, 3, sel, size), lambda part: (part, 0, 0, 0)), same],
        out_shape=[struct((parts, 3, sel, size), LOW), struct((sel, width), LOW)],
        scratch_shapes=[pltpu.VMEM((sel, width), FULL)],
        compiler_params=pltpu.CompilerParams(vmem_limit_bytes=VMEM_BYTES),
        cost_estimate=pl.CostEstimate(
            flops=6 * sel * parts * size * width,
            bytes_accessed=weight.size * 2,
            transcendentals=0,
        ),
        name="feed_back",
    )(grad, weight, gate, up, hidden)


def newton_steps(problems):
    rows, width = problems[0][0].shape
    block = min(1024, width)
    eye = lax.broadcasted_iota(jnp.int32, (rows, rows), 0) == lax.broadcasted_iota(
        jnp.int32, (rows, rows), 1
    )

    def strip(part):
        return pl.ds(pl.multiple_of(part * block, block), block)

    def over(function, start):
        return lax.fori_loop(0, width // block, function, start)

    def add_squares(part, totals):
        values = [current[:, strip(part)] for current, low, gram, rest in problems]
        return [total + jnp.sum(value * value) for total, value in zip(totals, values)]

    totals = over(add_squares, [jnp.float32(0.0)] * len(problems))
    scales = [1.0 / (jnp.sqrt(total) + 1e-07) for total in totals]

    def begin(part, carry):
        for scale, (current, low, gram, rest) in zip(scales, problems):
            values = current[:, strip(part)] * scale
            current[:, strip(part)] = values
            low[:, strip(part)] = values.astype(LOW)
        return carry

    over(begin, 0)

    def iteration(turn, carry):
        for current, low, gram, rest in problems:
            gram[...] = jnp.zeros_like(gram)

        def add_gram(part, carry):
            for current, low, gram, rest in problems:
                values = low[:, strip(part)]
                gram[...] = gram[...] + dot(values, values, 1, 1)
            return carry

        over(add_gram, 0)
        seconds = []
        for current, low, gram, rest in problems:
            whole = gram[...]
            middle = jnp.sum(jnp.where(eye, whole, 0.0)) / rows
            rest[...] = (whole - jnp.where(eye, middle, 0.0)).astype(LOW)
            square = dot(rest[...], rest[...], 1, 0)
            whole = gram[...]
            centred = whole - jnp.where(eye, middle, 0.0)
            square = square + 2.0 * middle * centred + jnp.where(eye, middle * middle, 0.0)
            whole = NEWTON_B * whole + NEWTON_C * square
            second = jnp.sum(jnp.where(eye, whole, 0.0)) / rows
            rest[...] = (whole - jnp.where(eye, second, 0.0)).astype(LOW)
            seconds.append(second)

        def apply(part, carry):
            for second, (current, low, gram, rest) in zip(seconds, problems):
                values = (NEWTON_A + second) * current[:, strip(part)] + dot(
                    rest[...], low[:, strip(part)], 1, 0
                )
                current[:, strip(part)] = values
                low[:, strip(part)] = values.astype(LOW)
            return carry

        over(apply, 0)
        return carry

    lax.fori_loop(0, NS_STEPS, iteration, 0)


def newton_scratch(rows, width):
    return [
        pltpu.VMEM((rows, width), FULL),
        pltpu.VMEM((rows, width), LOW),
        pltpu.VMEM((rows, rows), FULL),
        pltpu.VMEM((rows, rows), LOW),
    ]


def newton_cost(count, rows, width):
    return pl.CostEstimate(
        flops=NS_STEPS * count * (4 * rows * rows * width + 2 * rows * rows * rows),
        bytes_accessed=6 * count * rows * width,
        transcendentals=0,
    )


def newton_body(factor_ref, mom_ref, grad_ref, out_ref, *problem):
    current, low = problem[:2]
    parts, rows, columns = mom_ref.shape
    factor = factor_ref[0]
    size = grad_ref.shape[1]
    for part in range(parts):
        spot = slice(part * columns, (part + 1) * columns)
        for source in range(parts):
            here = slice(source * size, (source + 1) * size)
            current[here, spot] = MOMENTUM * mom_ref[part, here, :].astype(
                FULL
            ) + factor * grad_ref[source, :, spot].astype(FULL)
    newton_steps([problem])
    for part in range(parts):
        out_ref[part] = low[:, part * columns : (part + 1) * columns]


def newton_small_body(rows, factor_ref, mom_ref, grad_ref, kv_ref, out_ref, *scratch):
    problems = [scratch[4 * at : 4 * at + 4] for at in range(4)]
    parts, _, columns = mom_ref.shape
    kv_columns = kv_ref.shape[2]
    half = rows // 2
    factor = factor_ref[0]
    for part in range(parts):
        spot = slice(part * columns, (part + 1) * columns)
        for member in range(2):
            current = problems[member][0]
            here = slice(member * rows, (member + 1) * rows)
            mom, grad = mom_ref[part, here, :], grad_ref[part, here, :]
            current[:, spot] = MOMENTUM * mom.astype(FULL) + factor * grad.astype(FULL)
        spot = slice(part * kv_columns, (part + 1) * kv_columns)
        for member in range(2):
            current = problems[2 + member][0]
            piece = kv_ref[part, member * rows : (member + 1) * rows, :].astype(FULL)
            for side in range(2):
                lane = (2 * member + side) * kv_columns
                mom = mom_ref[part, 2 * rows : 2 * rows + half, lane : lane + kv_columns]
                here = slice(side * half, (side + 1) * half)
                current[here, spot] = MOMENTUM * mom.astype(FULL) + factor * piece[here]
    newton_steps(problems[:2])
    newton_steps(problems[2:])
    out_ref[...] = jnp.zeros_like(out_ref)
    for part in range(parts):
        for member in range(2):
            out_ref[part, member * rows : (member + 1) * rows, :] = problems[member][1][
                :, part * columns : (part + 1) * columns
            ]
            low = problems[2 + member][1]
            for side in range(2):
                lane = (2 * member + side) * kv_columns
                out_ref[part, 2 * rows : 2 * rows + half, lane : lane + kv_columns] = low[
                    side * half : (side + 1) * half,
                    part * kv_columns : (part + 1) * kv_columns,
                ]


def newton_any_body(rows, factor_ref, mom_ref, grad_ref, qo_ref, kv_ref, out_ref, *scratch):
    parts = mom_ref.shape[0]
    owner = lax.rem(3 + lax.rem(lax.axis_index("wide"), 2), parts)
    small = lax.axis_index("narrow") == owner

    @pl.when(small)
    def _():
        newton_small_body(rows, factor_ref, mom_ref, qo_ref, kv_ref, out_ref, *scratch[4:])

    @pl.when(jnp.logical_not(small))
    def _():
        newton_body(factor_ref, mom_ref, grad_ref, out_ref, *scratch[:4])


def newton(factor, mom, grad, qo_grad, kv_grad):
    parts, slot_rows, columns = mom.shape
    width = parts * columns
    rows = kv_grad.shape[1] // 2
    kv_width = parts * kv_grad.shape[2]
    return pl.pallas_call(
        functools.partial(newton_any_body, rows),
        in_specs=[pl.BlockSpec(memory_space=pltpu.SMEM)] + [VMEM] * 4,
        out_specs=VMEM,
        out_shape=struct(mom.shape, LOW),
        scratch_shapes=newton_scratch(slot_rows, width)
        + newton_scratch(rows, width) * 2
        + newton_scratch(rows, kv_width) * 2,
        compiler_params=pltpu.CompilerParams(vmem_limit_bytes=VMEM_BYTES),
        cost_estimate=newton_cost(1, slot_rows, width),
        name="newton",
    )(factor.reshape(1), mom, grad, qo_grad, kv_grad)


def lookup_body(ids_ref, turn_ref, table_ref, out_ref, low_ref, list_ref, held, rows, sem):
    vocab = table_ref.shape[0]
    count = out_ref.shape[0]
    load = pltpu.make_async_copy(table_ref, held, sem)
    load.start()
    rows[...] = jnp.zeros_like(rows)

    found = turn_ref[count]

    def note(group, carry):
        for member in range(UNROLL):
            at = group * UNROLL + member
            list_ref[turn_ref[at]] = at
        return carry

    lax.fori_loop(0, count // UNROLL, note, 0)
    for member in range(UNROLL):
        list_ref[found + member] = count
    list_ref[count + UNROLL] = found
    load.wait()

    def step(group, carry):
        for member in range(UNROLL):
            at = list_ref[group * UNROLL + member]
            spot = jnp.minimum(ids_ref[jnp.minimum(at, count - 1)], vocab - 1)
            rows[pl.ds(at, 1), :] = held[pl.ds(spot, 1), :]
        return carry

    lax.fori_loop(0, (found + UNROLL - 1) // UNROLL, step, 0)
    out_ref[...] = rows[pl.ds(0, count), :].astype(LOW)
    low_ref[...] = held[...].astype(LOW)


def lookup(table, ids):
    vocab, columns = table.shape
    count = ids.shape[0]
    mine = (ids < vocab).reshape(-1, 128)
    before = jnp.arange(128)[:, None] < jnp.arange(128)[None, :]
    in_row = dot(mine.astype(LOW), before.astype(LOW), 1, 0)
    per_row = jnp.sum(mine.astype(FULL), axis=1)
    lines = jnp.arange(mine.shape[0])
    ahead = jnp.sum(jnp.where(lines[:, None] > lines[None, :], per_row[None, :], 0.0), axis=1)
    found = jnp.sum(per_row).astype(jnp.int32)
    turns = (in_row + ahead[:, None]).astype(jnp.int32)
    turns = jnp.where(mine, turns, count + UNROLL + 1).reshape(-1)
    turns = jnp.concatenate([turns, jnp.full((128,), found)])
    return pl.pallas_call(
        lookup_body,
        in_specs=[pl.BlockSpec(memory_space=pltpu.SMEM)] * 2 + [ANY],
        out_specs=[VMEM, VMEM, pl.BlockSpec(memory_space=pltpu.SMEM)],
        scratch_shapes=[
            pltpu.VMEM((vocab, columns), FULL),
            pltpu.VMEM((count + 8, columns), FULL),
            pltpu.SemaphoreType.DMA,
        ],
        out_shape=[
            struct((count, columns), LOW),
            struct((vocab, columns), LOW),
            struct((count + 2 * UNROLL,), jnp.int32),
        ],
        compiler_params=pltpu.CompilerParams(vmem_limit_bytes=VMEM_BYTES),
        cost_estimate=pl.CostEstimate(
            flops=0, bytes_accessed=vocab * columns * 4, transcendentals=0
        ),
        name="lookup",
    )(ids, turns, table)


def spread_body(
    ids_ref, list_ref, rows_ref, head_ref, out_ref, square_ref, even, odd, rows, sem
):
    vocab = out_ref.shape[0]
    count = rows_ref.shape[0]
    chunk = 256

    def strip(part):
        return pl.ds(pl.multiple_of(part * chunk, chunk), chunk)

    def begin(part, carry):
        even[strip(part), :] = head_ref[strip(part), :].astype(FULL)
        odd[strip(part), :] = jnp.zeros((chunk, odd.shape[1]), FULL)
        return carry

    lax.fori_loop(0, vocab // chunk, begin, 0)

    def widen(part, carry):
        rows[strip(part), :] = rows_ref[strip(part), :].astype(FULL)
        return carry

    lax.fori_loop(0, count // chunk, widen, 0)
    rows[pl.ds(count, 8), :] = jnp.zeros((8, rows.shape[1]), FULL)

    def step(group, carry):
        for member in range(UNROLL):
            at = list_ref[group * UNROLL + member]
            spot = jnp.minimum(ids_ref[jnp.minimum(at, count - 1)], vocab - 1)
            total = even if member % 2 == 0 else odd
            total[pl.ds(spot, 1), :] = total[pl.ds(spot, 1), :] + rows[pl.ds(at, 1), :]
        return carry

    found = list_ref[count + UNROLL]
    lax.fori_loop(0, (found + UNROLL - 1) // UNROLL, step, 0)

    def finish(part, squares):
        value = even[strip(part), :] + odd[strip(part), :]
        even[strip(part), :] = value
        return squares + jnp.sum((value * value).reshape(chunk // 8, 8, -1), axis=0)

    square_ref[...] = lax.fori_loop(
        0, vocab // chunk, finish, jnp.zeros((8, even.shape[1]), FULL)
    )
    store = pltpu.make_async_copy(even, out_ref, sem)
    store.start()
    store.wait()


def spread(ids, listed, rows, head):
    vocab, columns = head.shape
    count = ids.shape[0]
    smem = pl.BlockSpec(memory_space=pltpu.SMEM)
    return pl.pallas_call(
        spread_body,
        in_specs=[smem, smem, VMEM, VMEM],
        out_specs=[ANY, VMEM],
        scratch_shapes=[
            pltpu.VMEM((vocab, columns), FULL),
            pltpu.VMEM((vocab, columns), FULL),
            pltpu.VMEM((count + 8, columns), FULL),
            pltpu.SemaphoreType.DMA,
        ],
        out_shape=[struct((vocab, columns), FULL), struct((8, columns), FULL)],
        compiler_params=pltpu.CompilerParams(vmem_limit_bytes=VMEM_BYTES),
        cost_estimate=pl.CostEstimate(
            flops=count * columns, bytes_accessed=vocab * columns * 8, transcendentals=0
        ),
        name="spread",
    )(ids, listed, rows, head)


def adamw(weight, first_m, second_m, grad, rate, decay):
    first_new = BETA_ONE * first_m + (1.0 - BETA_ONE) * grad
    second_new = BETA_TWO * second_m + (1.0 - BETA_TWO) * grad * grad
    update = (
        first_new
        / (1.0 - BETA_ONE**STEP)
        / (jnp.sqrt(second_new / (1.0 - BETA_TWO**STEP)) + ADAM_EPS)
    )
    return (weight * (1.0 - rate * decay) - rate * update, first_new, second_new)


def cut_columns(values, count):
    rows, columns = values.shape
    return jnp.moveaxis(values.reshape(rows, count, columns // count), 1, 0)


def shifted(parts, axis, step):
    count = lax.axis_size(axis)
    pairs = [(source, (source + step) % count) for source in range(count)]
    return lax.ppermute(parts, axis, pairs)


def per_device(
    tokens,
    picks,
    targets,
    lengths,
    skip,
    embed,
    embed_m,
    embed_v,
    attn_qo,
    attn_qo_mom,
    attn_kv,
    attn_kv_mom,
    ffn,
    ffn_mom,
    gains,
    gains_m,
    gains_v,
):
    wide_count = lax.axis_size("wide")
    narrow_count = lax.axis_size("narrow")
    narrow_spot = lax.axis_index("narrow")
    wide_spot = lax.axis_index("wide")
    seq_len = tokens.shape[1]
    sel = picks.shape[1]
    vocab_rows, columns = embed.shape
    width = columns * wide_count
    own_rows = sel // narrow_count
    tok_rows = seq_len // narrow_count
    all_rows = own_rows + tok_rows
    heads_own = HEADS // narrow_count
    head_cols = heads_own * HD
    repeat = max(1, narrow_count // KVH)
    groups = KVH * repeat // narrow_count
    ffn_rows = ffn.shape[0]
    ffn_size = ffn_rows // narrow_count
    total_rows = wide_count * sel
    lens = lengths[0]
    pick_ids = picks[0]
    keep_layer = (1 - skip[0]).astype(FULL)
    keep_row = jnp.full((1, width), keep_layer)
    lanes = 128

    def box(flat):
        height = -(-flat.shape[0] // (8 * lanes)) * 8
        return jnp.pad(flat, (0, height * lanes - flat.shape[0])).reshape(height, lanes)

    ffn_low = jnp.moveaxis(ffn, 1, 0).astype(LOW)
    ffn_cut = ffn_low.reshape(3, narrow_count, ffn_size, ffn_low.shape[2])
    ffn_cut = jnp.moveaxis(ffn_cut, 1, 0).reshape(narrow_count, 3 * ffn_size, -1)
    kv_own = attn_kv.reshape(columns, -1).astype(LOW)

    where_at = jnp.arange(seq_len, dtype=jnp.int32)
    pick_tokens = jnp.sum(
        jnp.where(pick_ids[:, None] == where_at[None, :], tokens[0][None, :], 0), axis=1
    )
    ints = box(jnp.concatenate([tokens[0], pick_tokens, targets[0]]))
    all_ints, all_gains, kv_part = launch(
        [
            gather_wide(ints),
            gather_both(box(gains.astype(LOW).astype(FULL).reshape(-1))),
            gather_blocks("narrow", kv_own),
        ],
        0,
        "gather_ids",
    )
    kv_part = jnp.moveaxis(kv_part, 0, 1).reshape(columns, -1)
    proj_own = jnp.concatenate([kv_part, attn_qo.reshape(columns, -1).astype(LOW)], axis=1)
    proj = lax.all_gather(proj_own, "wide", axis=0, tiled=True)
    ffn_cut, all_ints = lax.optimization_barrier((ffn_cut, all_ints))
    ffn_pieces = [lax.dynamic_index_in_dim(ffn_cut, narrow_spot, 0, False)] + [
        shifted(
            lax.dynamic_index_in_dim(
                ffn_cut, lax.rem(narrow_spot + step, narrow_count), 0, False
            ),
            "narrow",
            step,
        )
        for step in range(1, narrow_count)
    ]
    gain_size = gains.shape[1]
    gain_w = all_gains.reshape(narrow_count, wide_count, -1)[:, :, : 3 * gain_size]
    gain_w = gain_w.reshape(narrow_count, wide_count, 3, gain_size)
    gain_w = jnp.transpose(gain_w, (2, 1, 0, 3)).reshape(3, width)
    all_ints = all_ints.reshape(wide_count, -1)
    tokens_all = all_ints[:, :seq_len].reshape(wide_count, narrow_count, tok_rows)
    picked_all = all_ints[:, seq_len : seq_len + sel].reshape(wide_count, narrow_count, own_rows)
    targets_all = all_ints[:, seq_len + sel : seq_len + 2 * sel].reshape(-1)
    wanted = jnp.moveaxis(jnp.concatenate([tokens_all, picked_all], axis=2), 1, 0).reshape(-1)
    local_ids = wanted - narrow_spot * vocab_rows
    inside = (local_ids >= 0) & (local_ids < vocab_rows)
    spots = jnp.where(inside, local_ids, vocab_rows)
    found, embed_low, listed = lookup(embed, spots)
    ffn_pieces, found = lax.optimization_barrier((ffn_pieces, found))
    ffn_sub = assemble(ffn_pieces).reshape(3, ffn_size, width)
    ffn_sub, found = lax.optimization_barrier((ffn_sub, found))
    ffn_w = lax.all_gather(ffn_sub, "wide", axis=0)
    found = found.reshape(narrow_count, wide_count * all_rows, columns)
    embed_cut = embed_low.reshape(wide_count, vocab_rows // wide_count, columns)
    table_half = embed_cut.shape[1] // 2
    rows_low = launch([fetch_rows(found, all_rows)], 1, "fetch_rows")[0]

    mom_qo = jnp.moveaxis(attn_qo_mom, 1, 0)
    mom_kv = jnp.moveaxis(attn_kv_mom, 1, 0)
    mom_ffn = jnp.moveaxis(ffn_mom, 1, 0)
    slot_rows, slot_cols = mom_ffn.shape[1:]

    block_rows, q_size = mom_qo.shape[1:]
    kv_size = mom_kv.shape[2]
    half_rows = block_rows // 2
    kv_box = jnp.moveaxis(mom_kv.reshape(4, half_rows, kv_size), 0, 1).reshape(half_rows, -1)
    small_box = jnp.concatenate([mom_qo.reshape(2 * block_rows, q_size), kv_box])
    small_box = jnp.pad(small_box, ((0, slot_rows - small_box.shape[0]), (0, 0)))
    mom_parts = jnp.concatenate([mom_ffn, small_box[None]]).astype(LOW)

    seg_all, cosine_all, sine_all = angles_at(lens, where_at)
    cosine_all, sine_all = wide_angles(cosine_all, sine_all)
    seg_mine, cosine, sine = angles_at(lens, pick_ids)
    cosine, sine = wide_angles(cosine, sine)

    def tok_part(angles):
        return lax.dynamic_slice_in_dim(angles, narrow_spot * tok_rows, tok_rows, 0)

    by_head, normed_tok = make_heads(
        rows_low, gain_w[0:1], proj, tok_part(cosine_all), tok_part(sine_all), groups, repeat
    )
    own_head, start_low, tok_cols, table_top = launch(
        [
            swap_blocks("narrow", by_head),
            gather_blocks("narrow", rows_low[tok_rows:]),
            split_columns("wide", normed_tok),
            join_columns("wide", embed_cut[:, :table_half]),
        ],
        2,
        "trade_heads",
    )
    start_low, ffn_w = lax.optimization_barrier((start_low, ffn_w))
    start_low = start_low.reshape(sel, width)
    queries, probs, mixed, attn_part, normed, early_part = attend(
        start_low,
        gain_w,
        proj,
        own_head,
        cosine,
        sine,
        seg_mine[:, None],
        seg_all[None, :],
        pick_ids[:, None],
    )
    early = lax.all_gather(early_part, "wide", axis=0, tiled=True)
    start_own = rows_low[tok_rows:].astype(FULL)
    middle, inner, mixed_wide, pick_cols = launch(
        [
            settle(
                attn_part,
                start_own,
                start_own,
                jnp.ones((1, width), FULL),
                gain_w[1:2],
            ),
            gather_wide(mixed),
            split_columns("wide", normed),
        ],
        3,
        "settle_middle",
    )
    inner = inner.reshape(sel, width)
    inner_all = lax.all_gather(inner, "wide", axis=0, tiled=True)
    gate, up, hidden, fed = feed(inner, ffn_w)
    final_own, late_part, table_own = launch(
        [
            settle(fed, middle, start_own, keep_row, gain_w[2:3]),
            join_below("wide", embed_cut[:, table_half:], table_top),
        ],
        4,
        "settle_late",
    )

    table_count = table_own.shape[0]
    local_target = targets_all - (narrow_spot * vocab_rows + wide_spot * table_count)
    has_target = jnp.arange(table_count, dtype=jnp.int32)[:, None] == local_target[None, :]
    counted = (targets_all >= 0).astype(FULL)
    loss_count = jnp.sum(counted)

    def exit_logits(features):
        logits = dot(table_own, features, 1, 1)
        peak = jnp.max(logits, axis=0)
        total = jnp.sum(jnp.exp(logits - peak[None, :]), axis=0)
        picked = jnp.sum(jnp.where(has_target, logits, 0.0), axis=0)
        return logits, jnp.stack([peak, total, picked])

    half = slot_rows // 2
    late, mom_top, early_logits, early_stats = launch(
        [
            gather_wide(late_part.reshape(sel, width)),
            swap_turned(mom_parts[:, :half]),
            exit_stats(early, table_own, local_target[None, :]),
        ],
        5,
        "gather_late",
    )
    late = late.reshape(total_rows, width)
    late_logits, late_stats = exit_logits(late)
    stats = jnp.concatenate([early_stats, late_stats], axis=1).reshape(3, 8, -1)
    stats = launch([combine(stats, merge_stats)], 6, "combine_stats")[0]
    stats, inner_all = lax.optimization_barrier((stats, inner_all))
    stats = stats.reshape(3, -1)
    log_norms = stats[0] + jnp.log(stats[1])
    losses = log_norms - stats[2]
    loss_sum = jnp.sum(
        counted * (EXIT_EARLY * losses[:total_rows] + EXIT_LAST * losses[total_rows:])
    )

    def exit_back(logits, log_norm, weight):
        grad_logits = (
            (jnp.exp(logits - log_norm[None, :]) - has_target.astype(FULL))
            * (weight * counted)[None, :]
        ).astype(LOW)
        return grad_logits

    late_grad = exit_back(late_logits, log_norms[total_rows:], EXIT_LAST)
    late_back = dot(late_grad, table_own, 0, 0).astype(LOW)
    early_grad = exit_back(early_logits, log_norms[:total_rows], EXIT_EARLY)
    grad_late, mom_owned, early_back, _ = launch(
        [
            sum_wide(late_back),
            swap_below(mom_parts[:, half:], mom_top),
            later(product([early_grad], [table_own], 0, [[(0, 0)]]), 1),
        ],
        7,
        "sum_late",
    )
    early_back, grad_late = lax.optimization_barrier((early_back, grad_late))
    grad_early = lax.psum_scatter(early_back[0], "wide", scatter_dimension=0, tiled=True)
    grad_final, gain_late, grad_out = launch(
        [
            settle_back(
                grad_late.astype(LOW),
                final_own,
                jnp.zeros_like(final_own),
                keep_row,
                gain_w[2:3],
            ),
        ],
        8,
        "back_late",
    )
    grad_layer = grad_final * keep_layer
    grad_out = grad_out.reshape(sel, width)
    out_all = lax.all_gather(grad_out, "wide", axis=0, tiled=True)
    acts, fed_back = feed_back(grad_out, ffn_w, gate, up, hidden)
    grad_mid, gain_mid, grad_branch, acts = launch(
        [
            settle_back(fed_back, middle, grad_layer, keep_row, gain_w[1:2]),
            swap_blocks("wide", acts),
        ],
        9,
        "back_middle",
    )
    acts = jnp.moveaxis(acts, 1, 0).reshape(3, total_rows, ffn_size)
    grad_branch, grad_early = lax.optimization_barrier((grad_branch, grad_early))
    grad_branch = grad_branch.reshape(sel, width)

    kv_parts, grad_queries, pick_part = attend_back(
        grad_branch, proj, own_head, queries, probs, cosine, sine, cosine_all, sine_all
    )
    grad_kv, grad_pick, grad_early, queries_wide, branch_cols, grad_head, _ = launch(
        [
            swap_blocks("narrow", kv_parts),
            sum_narrow(pick_part),
            sum_narrow(grad_early),
            gather_wide(grad_queries),
            split_columns("wide", grad_branch),
            product([early_grad, late_grad], [early, late], 1, [[(0, 0), (1, 1)]]),
        ],
        10,
        "trade_grads",
    )
    grad_kv, out_all = lax.optimization_barrier((grad_kv, out_all))
    grad_base = grad_mid + grad_final * (1.0 - keep_layer)
    grad_rows, gain_attn, gain_early, grad_kv = rows_back(
        rows_low, gain_w, proj, grad_kv, grad_pick, grad_early, grad_base, repeat
    )
    summed_qo = jnp.stack(
        [
            jnp.einsum("wtc,wtf->cf", pick_cols, queries_wide, preferred_element_type=FULL),
            jnp.einsum("wtc,wtf->cf", branch_cols, mixed_wide, preferred_element_type=FULL),
        ]
    )
    grad_rows, acts_owned, kv_wide, head_cols_all, grad_ffn, ffn_squares = launch(
        [
            return_rows(grad_rows),
            swap_owned(acts, 5),
            later(gather_wide(grad_kv, 3), 2),
            later(split_columns("wide", grad_head[0], 3), 2),
            product([acts], [inner_all, out_all], 0, [[(0, 0)], [(1, 0)], [(2, 1)]]),
        ],
        11,
        "return_rows",
    )
    turn = lax.rem(wide_spot, 2)
    grad_kv_w = jnp.einsum(
        "wtc,wtf->cf", tok_cols, kv_wide, preferred_element_type=FULL
    ).reshape(columns, narrow_count, 2, kv_size)
    grad_kv_w = jnp.moveaxis(grad_kv_w, 0, 2)
    summed_kv = lax.psum_scatter(grad_kv_w, "narrow", scatter_dimension=0, tiled=True)[0]
    summed_table, table_squares = spread(
        spots, listed, grad_rows.reshape(-1, columns), head_cols_all.reshape(vocab_rows, columns)
    )

    squares = (
        jnp.sum(summed_qo * summed_qo)
        + jnp.sum(summed_kv * summed_kv)
        + jnp.sum(ffn_squares)
        + jnp.sum(table_squares)
    )
    sums = jnp.stack(
        [gain_attn[0], gain_mid[0], gain_early[0] + gain_late[0], jnp.full((width,), squares)]
    )
    def owns_last():
        away = lax.axis_index("narrow") + narrow_count - lax.rem(lax.axis_index("wide"), 2)
        return lax.rem(away, narrow_count) >= 2

    sums, kv_owned, qo_owned, owned, _ = launch(
        [
            combine(sums.reshape(4, 8, -1), add_two),
            send_owner(summed_kv.astype(LOW).reshape(2 * block_rows, kv_size)),
            later(send_owner(summed_qo.astype(LOW).reshape(2 * columns, q_size)), 1),
            later(
                product(
                    [acts_owned],
                    [inner_all, out_all],
                    0,
                    [[(at, 0)] for at in range(narrow_count)],
                    False,
                    owns_last,
                ),
                1,
            ),
        ],
        12,
        "combine_sums",
    )
    sums = sums.reshape(4, width)
    summed_gain = lax.dynamic_slice_in_dim(
        sums[:3], (wide_spot * narrow_count + narrow_spot) * gain_size, gain_size, 1
    )
    square_total = sums[3, 0] + jnp.sum(sums[:3] * sums[:3])
    grad_norm = jnp.sqrt(square_total) / loss_count
    factor = jnp.minimum(1.0, CLIP_NORM / (grad_norm + 1e-06)) / loss_count

    final_parts, factor = lax.optimization_barrier((grad_ffn, factor))
    size = width // narrow_count

    def final_piece(spot):
        return lax.dynamic_slice_in_dim(final_parts, spot * size, size, 2)

    pieces = [final_piece(narrow_spot)] + [
        shifted(final_piece(lax.rem(narrow_spot + step, narrow_count)), "narrow", step)
        for step in range(1, narrow_count)
    ]
    directions = newton(
        factor, mom_owned, owned, qo_owned, kv_owned
    )
    directions, pieces, ffn, factor = lax.optimization_barrier(
        (directions, pieces, ffn, factor)
    )
    summed_ffn = jnp.zeros((3, narrow_count, ffn_size, size), LOW)
    for step, piece in enumerate(pieces):
        source = lax.rem(narrow_spot - step + narrow_count, narrow_count)
        summed_ffn = lax.dynamic_update_index_in_dim(summed_ffn, piece, source, 1)
    summed_ffn = summed_ffn.reshape(3, ffn_rows, size).astype(FULL)
    received = [lax.dynamic_index_in_dim(directions, narrow_spot, 0, False)] + [
        shifted(
            lax.dynamic_index_in_dim(
                directions, lax.rem(narrow_spot + step, narrow_count), 0, False
            ),
            "narrow",
            step,
        )
        for step in range(1, narrow_count)
    ]

    def direction_of(matrix):
        step = lax.rem(narrow_spot - matrix - turn + 2 * narrow_count, narrow_count)
        result = received[0]
        for at in range(1, narrow_count):
            result = jnp.where(step == at, received[at], result)
        return result

    dir_ffn = jnp.stack([direction_of(matrix) for matrix in range(3)]).astype(FULL)
    small = direction_of(3).astype(FULL)
    dir_qo = small[: 2 * block_rows].reshape(mom_qo.shape)
    dir_kv = small[2 * block_rows : 2 * block_rows + half_rows].reshape(half_rows, 4, kv_size)
    dir_kv = jnp.moveaxis(dir_kv, 1, 0).reshape(mom_kv.shape)

    embed_new, embed_m_new, embed_v_new = adamw(
        embed, embed_m, embed_v, summed_table * factor, RATE_ADAM, WEIGHT_DECAY
    )
    gains_new, gains_m_new, gains_v_new = adamw(
        gains, gains_m, gains_v, summed_gain * factor, RATE_GAIN, 0.0
    )

    def mom_next(mom, grad):
        return MOMENTUM * mom + jnp.moveaxis(grad * factor, 0, 1)

    shrink = 1.0 - RATE_MUON * WEIGHT_DECAY

    def weight_next(weight, direction):
        return weight * shrink - RATE_MUON * jnp.moveaxis(direction, 0, 1)

    return (
        loss_sum,
        loss_count,
        grad_norm,
        embed_new,
        embed_m_new,
        embed_v_new,
        weight_next(attn_qo, dir_qo),
        mom_next(attn_qo_mom, summed_qo),
        weight_next(attn_kv, dir_kv),
        mom_next(attn_kv_mom, summed_kv),
        weight_next(ffn, dir_ffn),
        mom_next(ffn_mom, summed_ffn),
        gains_new,
        gains_m_new,
        gains_v_new,
    )


def solution(mesh):
    by_pack = P("wide", None)
    table = P("narrow", "wide")
    layer = P("wide", None, "narrow")
    gain = P(None, ("wide", "narrow"))
    return jax.shard_map(
        per_device,
        mesh=mesh,
        in_specs=(by_pack,) * 4 + (P("wide"),) + (table,) * 3 + (layer,) * 6 + (gain,) * 3,
        out_specs=(P(),) * 3 + (table,) * 3 + (layer,) * 6 + (gain,) * 3,
        check_vma=False,
    )
```

```python
import functools

import jax
import jax.numpy as jnp
from jax import lax
from jax.experimental import pallas as pl
from jax.experimental.pallas import tpu as pltpu
from jax.sharding import PartitionSpec as P

HEADS = 16
HD = 128
KVH = 4
NS_STEPS = 5
STEP = 10


NORM_EPS = 1e-05
ROPE_BASE = 10000.0
EXIT_EARLY = 0.25
EXIT_LAST = 1.0
CLIP_NORM = 0.02
BETA_ONE = 0.9
BETA_TWO = 0.95
ADAM_EPS = 1e-08
RATE_ADAM = 0.02
RATE_GAIN = 0.3
RATE_MUON = 0.3
WEIGHT_DECAY = 0.1
MOMENTUM = 0.95
NEWTON_A = 3.4445
NEWTON_B = -4.775
NEWTON_C = 2.0315
MASKED = -1e30
LOW = jnp.bfloat16
FULL = jnp.float32
BOTH = ("wide", "narrow")
UNROLL = 16
VMEM_BYTES = 56 * 1024 * 1024


def dot(first, second, first_dim, second_dim):
    return lax.dot_general(
        first, second, (((first_dim,), (second_dim,)), ((), ())), preferred_element_type=FULL
    )


def norm_rows(values, gain_row):
    return (
        values * lax.rsqrt(jnp.mean(values * values, axis=-1, keepdims=True) + NORM_EPS) * gain_row
    )


def segments_at(lens, where_at):
    ends = jnp.cumsum(lens)
    return jnp.sum((where_at[:, None] >= ends[None, :]).astype(jnp.int32), axis=1)


def angles_at(lens, where_at):
    segment = segments_at(lens, where_at)
    starts = jnp.cumsum(lens) - lens
    member = segment[:, None] == jnp.arange(lens.shape[0], dtype=jnp.int32)[None, :]
    begin = jnp.sum(jnp.where(member, starts[None, :], 0), axis=1)
    offset_pos = (where_at - begin).astype(FULL)
    inverse = ROPE_BASE ** (-2.0 * jnp.arange(HD // 2, dtype=FULL) / HD)
    angle = offset_pos[:, None] * inverse[None, :]
    return (segment, jnp.cos(angle), jnp.sin(angle))


MESH = pl.DeviceIdType.MESH
ANY = pl.BlockSpec(memory_space=pl.ANY)
VMEM = pl.BlockSpec(memory_space=pltpu.VMEM)


def others(axis, count):
    me = lax.axis_index(axis)
    return [{axis: lax.rem(me + step, count)} for step in range(1, count)]


def push(source, target, send, receive, device):
    return pltpu.make_async_remote_copy(
        src_ref=source,
        dst_ref=target,
        send_sem=send,
        recv_sem=receive,
        device_id=device,
        device_id_type=MESH,
    )


def arrived(block, send, receive, device):
    push(block, block, send, receive, device).wait_recv()


def like(values):
    return jax.ShapeDtypeStruct(values.shape, values.dtype)


def struct(shape, dtype):
    return jax.ShapeDtypeStruct(shape, dtype)


def sems(*shape):
    return pltpu.SemaphoreType.DMA(shape)


class Task:
    def __init__(self, inputs, outputs, scratch, steps, place_in, place_out, axes):
        self.inputs, self.outputs, self.scratch, self.steps = inputs, outputs, scratch, steps
        self.place_in = [place_in] * len(inputs)
        self.place_out = [place_out] * len(outputs)
        self.axes = axes


def launch(tasks, ident, name):
    axes = sorted(set(axis for task in tasks for axis in task.axes))
    inputs = [a for task in tasks for a in task.inputs]
    outputs = [a for task in tasks for a in task.outputs]
    scratch = [a for task in tasks for a in task.scratch]

    def body(*refs):
        refs = list(refs)
        ins = refs[: len(inputs)]
        outs = refs[len(inputs) : len(inputs) + len(outputs)]
        extra = refs[len(inputs) + len(outputs) :]
        barrier = pltpu.get_barrier_semaphore()
        targets = [device for axis in axes for device in others(axis, lax.axis_size(axis))]
        for device in targets:
            pl.semaphore_signal(barrier, inc=1, device_id=device, device_id_type=MESH)
        pl.semaphore_wait(barrier, len(targets))
        live = []
        for task in tasks:
            counts = (len(task.inputs), len(task.outputs), len(task.scratch))
            live.append(task.steps(ins[: counts[0]], outs[: counts[1]], extra[: counts[2]]))
            ins, outs, extra = ins[counts[0] :], outs[counts[1] :], extra[counts[2] :]
        while live:
            live = [steps for steps in live if next(steps, 0) is None]

    size = sum(a.size * a.dtype.itemsize for a in list(inputs) + list(outputs))
    return pl.pallas_call(
        body,
        out_shape=outputs,
        in_specs=[place for task in tasks for place in task.place_in],
        out_specs=[place for task in tasks for place in task.place_out],
        scratch_shapes=scratch,
        compiler_params=pltpu.CompilerParams(
            collective_id=ident, has_side_effects=True, vmem_limit_bytes=VMEM_BYTES
        ),
        cost_estimate=pl.CostEstimate(flops=0, bytes_accessed=size // 8, transcendentals=0),
        name=name,
    )(*inputs)


def later(task, turns):
    begin = task.steps

    def steps(ins, outs, scratch):
        for turn in range(turns):
            yield
        yield from begin(ins, outs, scratch)

    task.steps = steps
    return task


def gather_wide(values, patience=1):
    count = lax.axis_size("wide")
    chips = count // 2

    def steps(ins, outs, scratch):
        (x_ref,), (out_ref,), (send, receive, local) = ins, outs, scratch
        me = lax.axis_index("wide")
        mate = me + 1 - 2 * lax.rem(me, 2)
        peers = [lax.rem(me + 2 * step, count) for step in range(1, chips)] + [mate]
        first = []
        for step, peer in enumerate(peers):
            copy = push(x_ref, out_ref.at[me], send.at[step], receive.at[me], {"wide": peer})
            copy.start()
            first.append(copy)
        keep = pltpu.make_async_copy(x_ref, out_ref.at[me], local)
        keep.start()
        for turn in range(patience):
            yield
        second = []
        for step in range(1, chips):
            source = lax.rem(me - 2 * step + count, count)
            block = out_ref.at[source]
            arrived(block, send.at[0], receive.at[source], {"wide": mate})
            copy = push(
                block, block, send.at[chips + step - 1], receive.at[source], {"wide": mate}
            )
            copy.start()
            second.append(copy)
        yield
        for step in range(chips):
            source = lax.rem(mate - 2 * step + count, count)
            arrived(out_ref.at[source], send.at[0], receive.at[source], {"wide": mate})
        for copy in first + second:
            copy.wait_send()
        keep.wait()

    shape = struct((count,) + values.shape, values.dtype)
    return Task(
        [values], [shape], [sems(count - 1), sems(count), sems()], steps, VMEM, VMEM, ["wide"]
    )


def trade(axis, values, source_of, target_of, shape, patience=2):
    count = lax.axis_size(axis)

    def steps(ins, outs, scratch):
        (x_ref,), (out_ref,), (send, receive, local) = ins, outs, scratch
        me = lax.axis_index(axis)
        copies = []
        for step in range(1, count):
            peer = lax.rem(me + step, count)
            copy = push(
                source_of(x_ref, peer),
                target_of(out_ref, me),
                send.at[step - 1],
                receive.at[me],
                {axis: peer},
            )
            copy.start()
            copies.append(copy)
        keep = pltpu.make_async_copy(source_of(x_ref, me), target_of(out_ref, me), local)
        keep.start()
        for turn in range(patience):
            yield
        for step in range(1, count):
            source = lax.rem(me - step + count, count)
            arrived(
                target_of(out_ref, source), send.at[0], receive.at[source], {axis: source}
            )
        for copy in copies:
            copy.wait_send()
        keep.wait()

    return Task(
        [values],
        [struct(shape, values.dtype)],
        [sems(count - 1), sems(count), sems()],
        steps,
        ANY,
        ANY,
        [axis],
    )


def block_at(ref, spot):
    return ref.at[spot]


def whole_at(ref, spot):
    return ref


def columns_of(size):
    def at(ref, spot):
        return ref.at[:, pl.ds(pl.multiple_of(spot * size, size), size)]

    return at


def turned(ref, spot):
    count = lax.axis_size("narrow")
    matrix = lax.rem(spot + count - lax.rem(lax.axis_index("wide"), 2), count)
    return ref.at[jnp.minimum(matrix, 3)]


def swap_turned(values, patience=2):
    shape = (lax.axis_size("narrow"),) + values.shape[1:]
    return trade("narrow", values, turned, block_at, shape, patience)


def product(lefts, rights, dim, order, pause=True, last=None):
    count, rows = len(order), lefts[0].shape[-1 if dim == 0 else -2]
    columns = rights[0].shape[1]
    block = min(512, columns)

    def steps(ins, outs, scratch):
        left_refs, right_refs = ins[: len(lefts)], ins[len(lefts) :]
        result_ref, square_ref = outs
        square_ref[...] = jnp.zeros_like(square_ref)

        def left_of(member):
            return left_refs[0][member] if lefts[0].ndim == 3 else left_refs[member][...]

        def fill(at, members, shift):
            def strip(part, carry):
                spot = pl.ds(pl.multiple_of(part * block, block), block)
                value = jnp.zeros((rows, block), FULL)
                for left, right in members:
                    value = value + dot(left_of(left), right_refs[right + shift][:, spot], dim, 0)
                result_ref[at, :, spot] = value.astype(LOW)
                square_ref[:, spot] = square_ref[:, spot] + jnp.sum(
                    value * value, axis=0, keepdims=True
                )
                return carry

            lax.fori_loop(0, columns // block, strip, 0)

        for at, members in enumerate(order):
            if last is None:
                fill(at, members, 0)
            else:
                pl.when(last())(functools.partial(fill, at, members, 1))
                pl.when(jnp.logical_not(last()))(functools.partial(fill, at, members, 0))
            if pause:
                yield

    return Task(
        list(lefts) + list(rights),
        [struct((count, rows, columns), LOW), struct((1, columns), FULL)],
        [],
        steps,
        VMEM,
        VMEM,
        [],
    )


def exit_stats(features, table, targets):
    rows, vocab = features.shape[0], table.shape[0]
    block = min(256, vocab)

    def steps(ins, outs, scratch):
        features_ref, table_ref, targets_ref = ins
        logits_ref, stats_ref = outs

        def strip(part):
            return pl.ds(pl.multiple_of(part * block, block), block)

        def over(function, start):
            return lax.fori_loop(0, vocab // block, function, start)

        def fill(part, peak):
            logits = dot(table_ref[strip(part), :], features_ref[...], 1, 1)
            logits_ref[strip(part), :] = logits
            return jnp.maximum(peak, jnp.max(logits, axis=0, keepdims=True))

        peak = over(fill, jnp.full((1, rows), MASKED, FULL))
        lines = lax.broadcasted_iota(jnp.int32, (block, rows), 0)

        def add(part, carry):
            total, picked = carry
            logits = logits_ref[strip(part), :]
            hit = lines + part * block == targets_ref[...]
            return (
                total + jnp.sum(jnp.exp(logits - peak), axis=0, keepdims=True),
                picked + jnp.sum(jnp.where(hit, logits, 0.0), axis=0, keepdims=True),
            )

        zero = jnp.zeros((1, rows), FULL)
        total, picked = over(add, (zero, zero))
        stats_ref[0:1, :] = peak
        stats_ref[1:2, :] = total
        stats_ref[2:3, :] = picked
        yield

    return Task(
        [features, table, targets],
        [struct((vocab, rows), FULL), struct((3, rows), FULL)],
        [],
        steps,
        VMEM,
        VMEM,
        [],
    )


def swap_owned(values, patience):
    count = lax.axis_size("narrow")

    def steps(ins, outs, scratch):
        (x_ref,), (out_ref,), (send, receive, local) = ins, outs, scratch
        me = lax.axis_index("narrow")
        turn = lax.rem(lax.axis_index("wide"), 2)

        def matrix_of(device):
            return lax.rem(device + count - turn, count)

        def copy_to(step):
            peer = lax.rem(me + step, count)
            return push(
                x_ref.at[jnp.minimum(matrix_of(peer), 2)],
                out_ref.at[me],
                send.at[step - 1],
                receive.at[me],
                {"narrow": peer},
            )

        def keep():
            return pltpu.make_async_copy(
                x_ref.at[jnp.minimum(matrix_of(me), 2)], out_ref.at[me], local
            )

        keep().start()
        for step in range(1, count):

            @pl.when(matrix_of(lax.rem(me + step, count)) < 3)
            def _():
                copy_to(step).start()

        for turn_at in range(patience):
            yield

        @pl.when(matrix_of(me) < 3)
        def _():
            for step in range(1, count):
                source = lax.rem(me - step + count, count)
                arrived(out_ref.at[source], send.at[0], receive.at[source], {"narrow": source})

        for step in range(1, count):

            @pl.when(matrix_of(lax.rem(me + step, count)) < 3)
            def _():
                copy_to(step).wait_send()

        keep().wait()

    return Task(
        [values],
        [struct((count,) + values.shape[1:], values.dtype)],
        [sems(count - 1), sems(count), sems()],
        steps,
        ANY,
        ANY,
        ["narrow"],
    )


def send_owner(values):
    count = lax.axis_size("narrow")

    def steps(ins, outs, scratch):
        (x_ref,), (out_ref,), (send, receive, local) = ins, outs, scratch
        me = lax.axis_index("narrow")
        owner = lax.rem(3 + lax.rem(lax.axis_index("wide"), 2), count)
        keep = pltpu.make_async_copy(x_ref, out_ref.at[me], local)
        keep.start()

        def to_owner():
            return push(x_ref, out_ref.at[me], send.at[0], receive.at[me], {"narrow": owner})

        @pl.when(me != owner)
        def _():
            to_owner().start()

        yield
        yield

        @pl.when(me != owner)
        def _():
            to_owner().wait_send()

        @pl.when(me == owner)
        def _():
            for step in range(1, count):
                source = lax.rem(owner + step, count)
                arrived(out_ref.at[source], send.at[0], receive.at[source], {"narrow": source})

        keep.wait()

    return Task(
        [values],
        [struct((count,) + values.shape, values.dtype)],
        [sems(1), sems(count), sems()],
        steps,
        ANY,
        ANY,
        ["narrow"],
    )


def swap_blocks(axis, values):
    return trade(axis, values, block_at, block_at, values.shape)


def gather_blocks(axis, values):
    shape = (lax.axis_size(axis),) + values.shape
    return trade(axis, values, whole_at, block_at, shape)


def split_columns(axis, values, patience=2):
    count = lax.axis_size(axis)
    rows, size = values.shape[0], values.shape[1] // count
    return trade(axis, values, columns_of(size), block_at, (count, rows, size), patience)


def join_columns(axis, values):
    count, rows, size = values.shape
    return trade(axis, values, block_at, columns_of(size), (rows, count * size))


def collect(count, parts_ref, slots, send, receive):
    me = lax.axis_index("narrow")
    copies = []
    for step in range(1, count):
        peer = lax.rem(me + step, count)
        copy = push(
            parts_ref.at[peer],
            slots.at[me],
            send.at[step - 1],
            receive.at[me],
            {"narrow": peer},
        )
        copy.start()
        copies.append(copy)
    return copies


def collected(count, parts_ref, slots, send, receive):
    me = lax.axis_index("narrow")
    total = parts_ref[me].astype(FULL)
    for step in range(1, count):
        source = lax.rem(me - step + count, count)
        arrived(slots.at[source], send.at[0], receive.at[source], {"narrow": source})
        total = total + slots[source].astype(FULL)
    return total


def share(count, low, all_ref, send, receive):
    me = lax.axis_index("narrow")
    all_ref[me] = low
    copies = []
    for step in range(1, count):
        peer = lax.rem(me + step, count)
        copy = push(
            all_ref.at[me], all_ref.at[me], send.at[step - 1], receive.at[me], {"narrow": peer}
        )
        copy.start()
        copies.append(copy)
    return copies


def shared(count, all_ref, send, receive):
    me = lax.axis_index("narrow")
    for step in range(1, count):
        source = lax.rem(me - step + count, count)
        arrived(all_ref.at[source], send.at[0], receive.at[source], {"narrow": source})


def narrow_sems(count):
    return [sems(count - 1), sems(count)]


def settle(partial, base, other, keep_row, gain_row):
    count = lax.axis_size("narrow")
    rows, width = base.shape

    def steps(ins, outs, scratch):
        parts_ref, base_ref, other_ref, keep_ref, gain_ref = ins
        own_ref, all_ref = outs
        slots, send, receive, send_all, receive_all = scratch
        copies = collect(count, parts_ref, slots, send, receive)
        yield
        total = collected(count, parts_ref, slots, send, receive)
        total = jnp.where(keep_ref[...] > 0, total + base_ref[...], other_ref[...])
        own_ref[...] = total
        low = norm_rows(total, gain_ref[...]).astype(LOW)
        copies = copies + share(count, low, all_ref, send_all, receive_all)
        yield
        shared(count, all_ref, send_all, receive_all)
        for copy in copies:
            copy.wait_send()

    return Task(
        [partial.reshape(count, rows, width), base, other, keep_row, gain_row],
        [struct((rows, width), FULL), struct((count, rows, width), LOW)],
        [pltpu.VMEM((count, rows, width), partial.dtype)]
        + narrow_sems(count)
        + narrow_sems(count),
        steps,
        VMEM,
        VMEM,
        ["narrow"],
    )


def settle_back(partial, values, add, keep_row, gain_row):
    count = lax.axis_size("narrow")
    rows, width = values.shape

    def steps(ins, outs, scratch):
        parts_ref, values_ref, add_ref, keep_ref, gain_ref = ins
        own_ref, gain_grad_ref, all_ref = outs
        slots, send, receive, send_all, receive_all = scratch
        copies = collect(count, parts_ref, slots, send, receive)
        yield
        grad = collected(count, parts_ref, slots, send, receive)
        held = values_ref[...]
        root = lax.rsqrt(jnp.mean(held * held, axis=-1, keepdims=True) + NORM_EPS)
        scaled = gain_ref[...] * grad
        inner = jnp.mean(held * scaled, axis=-1, keepdims=True)
        own = add_ref[...] + root * scaled - held * (root * root * root * inner)
        gain_grad_ref[...] = jnp.sum(held * root * grad, axis=0, keepdims=True)
        own_ref[...] = own
        low = (own * keep_ref[...]).astype(LOW)
        copies = copies + share(count, low, all_ref, send_all, receive_all)
        yield
        shared(count, all_ref, send_all, receive_all)
        for copy in copies:
            copy.wait_send()

    return Task(
        [partial.reshape(count, rows, width), values, add, keep_row, gain_row],
        [
            struct((rows, width), FULL),
            struct((1, width), FULL),
            struct((count, rows, width), LOW),
        ],
        [pltpu.VMEM((count, rows, width), partial.dtype)]
        + narrow_sems(count)
        + narrow_sems(count),
        steps,
        VMEM,
        VMEM,
        ["narrow"],
    )


def sum_narrow(partial):
    count = lax.axis_size("narrow")
    rows, width = partial.shape[0] // count, partial.shape[1]

    def steps(ins, outs, scratch):
        (parts_ref,), (own_ref,), (slots, send, receive) = ins, outs, scratch
        copies = collect(count, parts_ref, slots, send, receive)
        yield
        yield
        own_ref[...] = collected(count, parts_ref, slots, send, receive)
        for copy in copies:
            copy.wait_send()

    return Task(
        [partial.reshape(count, rows, width)],
        [struct((rows, width), FULL)],
        [pltpu.VMEM((count, rows, width), partial.dtype)] + narrow_sems(count),
        steps,
        VMEM,
        VMEM,
        ["narrow"],
    )


def fetch_rows(found, rows):
    deep, wide = lax.axis_size("narrow"), lax.axis_size("wide")
    columns = found.shape[2]

    def steps(ins, outs, scratch):
        (found_ref,), (out_ref,) = ins, outs
        rightward, leftward, final = scratch[:3]
        send_right, receive_right, send_left, receive_left = scratch[3:7]
        send_wide, receive_wide, local = scratch[7:]
        spot = lax.axis_index("narrow")
        me = lax.axis_index("wide")

        def right_copy(part, source):
            return push(
                source,
                rightward.at[part],
                send_right.at[part],
                receive_right.at[part],
                {"narrow": lax.rem(spot + 1, deep)},
            )

        def left_copy(part, source):
            return push(
                source,
                leftward.at[part],
                send_left.at[part],
                receive_left.at[part],
                {"narrow": lax.rem(spot + deep - 1, deep)},
            )

        for step in range(deep - 1):
            right, left = deep - 1 - step, step

            @pl.when((spot == 0) & (right > 0))
            def _():
                right_copy(right, found_ref.at[right]).start()

            @pl.when((spot == deep - 1) & (left < deep - 1))
            def _():
                left_copy(left, found_ref.at[left]).start()

        yield
        for step in range(deep - 1):
            right, left = deep - 1 - step, step

            def pass_right():
                right_copy(right, rightward.at[right]).wait_recv()
                rightward[right] = rightward[right] + found_ref[right]
                right_copy(right, rightward.at[right]).start()

            pl.when((spot > 0) & (right > spot) & (2 * spot < deep))(pass_right)

            @pl.when((spot < deep - 1) & (left < spot))
            def _():
                left_copy(left, leftward.at[left]).wait_recv()
                leftward[left] = leftward[left] + found_ref[left]
                left_copy(left, leftward.at[left]).start()

            pl.when((right > spot) & (2 * spot >= deep))(pass_right)

        final[...] = found_ref[spot]

        @pl.when(spot > 0)
        def _():
            right_copy(spot, rightward.at[spot]).wait_recv()
            final[...] = final[...] + rightward[spot]

        @pl.when(spot < deep - 1)
        def _():
            left_copy(spot, leftward.at[spot]).wait_recv()
            final[...] = final[...] + leftward[spot]

        def rows_for(device):
            return final.at[pl.ds(pl.multiple_of(device * rows, rows), rows)]

        def columns_from(device):
            return columns_of(columns)(out_ref, device)

        copies = []
        for step in range(1, wide):
            peer = lax.rem(me + step, wide)
            copy = push(
                rows_for(peer),
                columns_from(me),
                send_wide.at[step - 1],
                receive_wide.at[me],
                {"wide": peer},
            )
            copy.start()
            copies.append(copy)
        keep = pltpu.make_async_copy(rows_for(me), columns_from(me), local)
        keep.start()
        yield
        for step in range(1, wide):
            source = lax.rem(me - step + wide, wide)
            arrived(
                columns_from(source), send_wide.at[0], receive_wide.at[source], {"wide": source}
            )
        yield
        for copy in copies:
            copy.wait_send()
        keep.wait()
        for step in range(deep - 1):
            right, left = deep - 1 - step, step

            @pl.when(right > spot)
            def _():
                right_copy(right, found_ref.at[right]).wait_send()

            @pl.when(left < spot)
            def _():
                left_copy(left, found_ref.at[left]).wait_send()

    task = Task(
        [found],
        [struct((rows, wide * columns), found.dtype)],
        [pltpu.VMEM(found.shape, found.dtype)] * 2
        + [pltpu.VMEM(found.shape[1:], found.dtype)]
        + [sems(deep)] * 4
        + [sems(wide - 1), sems(wide), sems()],
        steps,
        VMEM,
        ANY,
        ["narrow", "wide"],
    )
    return task


def return_rows(rows):
    deep, wide = lax.axis_size("narrow"), lax.axis_size("wide")
    count, width = rows.shape
    columns = width // wide

    def steps(ins, outs, scratch):
        (rows_ref,), (out_ref,) = ins, outs
        send_right, send_left, receive_deep, send_wide, receive_wide, local = scratch
        spot = lax.axis_index("narrow")
        me = lax.axis_index("wide")
        part_of = functools.partial(columns_of(columns), rows_ref)

        def landing(device):
            return out_ref.at[spot, pl.ds(pl.multiple_of(device * count, count), count)]

        copies = []
        for step in range(1, wide):
            peer = lax.rem(me + step, wide)
            copy = push(
                part_of(peer),
                landing(me),
                send_wide.at[step - 1],
                receive_wide.at[me],
                {"wide": peer},
            )
            copy.start()
            copies.append(copy)
        keep = pltpu.make_async_copy(part_of(me), landing(me), local)
        keep.start()
        yield
        for step in range(1, wide):
            source = lax.rem(me - step + wide, wide)
            arrived(landing(source), send_wide.at[0], receive_wide.at[source], {"wide": source})
        keep.wait()

        def right_copy(part):
            return push(
                out_ref.at[part],
                out_ref.at[part],
                send_right.at[part],
                receive_deep.at[part],
                {"narrow": lax.rem(spot + 1, deep)},
            )

        def left_copy(part):
            return push(
                out_ref.at[part],
                out_ref.at[part],
                send_left.at[part],
                receive_deep.at[part],
                {"narrow": lax.rem(spot + deep - 1, deep)},
            )

        @pl.when(spot < deep - 1)
        def _():
            right_copy(spot).start()

        @pl.when(spot > 0)
        def _():
            left_copy(spot).start()

        for step in range(1, deep):
            yield

            @pl.when(spot >= step)
            def _():
                right_copy(spot - step).wait_recv()

                @pl.when(spot < deep - 1)
                def _():
                    right_copy(spot - step).start()

            @pl.when(spot + step < deep)
            def _():
                left_copy(spot + step).wait_recv()

                @pl.when(spot > 0)
                def _():
                    left_copy(spot + step).start()

        for part in range(deep):

            @pl.when((part <= spot) & (spot < deep - 1))
            def _():
                right_copy(part).wait_send()

            @pl.when((part >= spot) & (spot > 0))
            def _():
                left_copy(part).wait_send()

        for copy in copies:
            copy.wait_send()

    return Task(
        [rows],
        [struct((deep, wide * count, columns), rows.dtype)],
        [sems(deep)] * 3 + [sems(wide - 1), sems(wide), sems()],
        steps,
        ANY,
        ANY,
        ["narrow", "wide"],
    )


def sum_wide(partial):
    count = lax.axis_size("wide")
    chips = count // 2
    rows, width = partial.shape[0] // count, partial.shape[1]

    def steps(ins, outs, scratch):
        (parts_ref,), (out_ref,) = ins, outs
        from_mate, paired, slots, send_mate, receive_mate, send, receive = scratch
        me = lax.axis_index("wide")
        side = lax.rem(me, 2)
        mate = me + 1 - 2 * side
        my_chip = me // 2
        mate_copies = []
        for step in range(chips):
            chip = lax.rem(my_chip + 1 + step, chips)
            copy = push(
                parts_ref.at[2 * chip + 1 - side],
                from_mate.at[chip],
                send_mate.at[step],
                receive_mate.at[chip],
                {"wide": mate},
            )
            copy.start()
            mate_copies.append(copy)
        yield
        copies = []
        for step in range(chips):
            chip = lax.rem(my_chip + 1 + step, chips)
            arrived(from_mate.at[chip], send_mate.at[0], receive_mate.at[chip], {"wide": mate})
            both = parts_ref[2 * chip + side].astype(FULL) + from_mate[chip].astype(FULL)
            if step < chips - 1:
                paired[chip] = both.astype(LOW)
                copy = push(
                    paired.at[chip],
                    slots.at[my_chip],
                    send.at[step],
                    receive.at[my_chip],
                    {"wide": 2 * chip + side},
                )
                copy.start()
                copies.append(copy)
            else:
                out_ref[...] = both
        yield
        for step in range(1, chips):
            chip = lax.rem(my_chip - step + chips, chips)
            arrived(slots.at[chip], send.at[0], receive.at[chip], {"wide": 2 * chip + side})
            out_ref[...] = out_ref[...] + slots[chip].astype(FULL)
        for copy in mate_copies + copies:
            copy.wait_send()

    return Task(
        [partial.reshape(count, rows, width)],
        [struct((rows, width), FULL)],
        [pltpu.VMEM((chips, rows, width), LOW)] * 3
        + [sems(chips), sems(chips), sems(max(chips - 1, 1)), sems(chips)],
        steps,
        VMEM,
        VMEM,
        ["wide"],
    )


def merge_stats(first, second):
    peak = jnp.maximum(first[0:1], second[0:1])
    total = first[1:2] * jnp.exp(first[0:1] - peak) + second[1:2] * jnp.exp(second[0:1] - peak)
    return jnp.concatenate([peak, total, first[2:3] + second[2:3]], axis=0)


def add_two(first, second):
    return first + second


def combine(values, join):
    deep, wide = lax.axis_size("narrow"), lax.axis_size("wide")

    def steps(ins, outs, scratch):
        (x_ref,), (out_ref,) = ins, outs
        wide_slots, deep_slots, send_wide, receive_wide, send_deep, receive_deep = scratch

        def start(axis, count, slots, value, send, receive):
            me = lax.axis_index(axis)
            slots[me] = value
            copies = []
            for step in range(1, count):
                peer = lax.rem(me + step, count)
                copy = push(
                    slots.at[me], slots.at[me], send.at[step - 1], receive.at[me], {axis: peer}
                )
                copy.start()
                copies.append(copy)
            return copies

        def finish(axis, count, slots, send, receive):
            me = lax.axis_index(axis)
            for step in range(1, count):
                source = lax.rem(me - step + count, count)
                arrived(slots.at[source], send.at[0], receive.at[source], {axis: source})
            total = slots[0]
            for source in range(1, count):
                total = join(total, slots[source])
            return total

        first = start("wide", wide, wide_slots, x_ref[...], send_wide, receive_wide)
        yield
        total = finish("wide", wide, wide_slots, send_wide, receive_wide)
        second = start("narrow", deep, deep_slots, total, send_deep, receive_deep)
        yield
        out_ref[...] = finish("narrow", deep, deep_slots, send_deep, receive_deep)
        for copy in first + second:
            copy.wait_send()

    return Task(
        [values],
        [like(values)],
        [
            pltpu.VMEM((wide,) + values.shape, values.dtype),
            pltpu.VMEM((deep,) + values.shape, values.dtype),
            sems(wide - 1),
            sems(wide),
            sems(deep - 1),
            sems(deep),
        ],
        steps,
        VMEM,
        VMEM,
        ["narrow", "wide"],
    )


def gather_both(values):
    deep, wide = lax.axis_size("narrow"), lax.axis_size("wide")

    def steps(ins, outs, scratch):
        (x_ref,), (out_ref,) = ins, outs
        send_wide, receive_wide, send_deep, receive_deep = scratch
        me = lax.axis_index("wide")
        spot = lax.axis_index("narrow")
        out_ref[spot, me] = x_ref[...]
        copies = []
        for step in range(1, wide):
            peer = lax.rem(me + step, wide)
            block = out_ref.at[spot, me]
            copy = push(block, block, send_wide.at[step - 1], receive_wide.at[me], {"wide": peer})
            copy.start()
            copies.append(copy)
        yield
        for step in range(1, wide):
            source = lax.rem(me - step + wide, wide)
            block = out_ref.at[spot, source]
            arrived(block, send_wide.at[0], receive_wide.at[source], {"wide": source})
        for step in range(1, deep):
            peer = lax.rem(spot + step, deep)
            block = out_ref.at[spot]
            copy = push(
                block, block, send_deep.at[step - 1], receive_deep.at[spot], {"narrow": peer}
            )
            copy.start()
            copies.append(copy)
        yield
        for step in range(1, deep):
            source = lax.rem(spot - step + deep, deep)
            block = out_ref.at[source]
            arrived(block, send_deep.at[0], receive_deep.at[source], {"narrow": source})
        for copy in copies:
            copy.wait_send()

    return Task(
        [values],
        [struct((deep, wide) + values.shape, values.dtype)],
        [sems(wide - 1), sems(wide), sems(deep - 1), sems(deep)],
        steps,
        VMEM,
        VMEM,
        ["narrow", "wide"],
    )


def turn_heads(values, cosine, sine):
    half = values.shape[1] // 2
    swapped = jnp.concatenate([values[:, half:], values[:, :half]], axis=1)
    return values * cosine + swapped * sine


def wide_angles(cosine, sine):
    return jnp.concatenate([cosine, cosine], axis=1), jnp.concatenate([-sine, sine], axis=1)


def local_call(body, inputs, specs, outputs, flops, name):
    return pl.pallas_call(
        body,
        grid=(1,),
        in_specs=specs,
        out_specs=[
            pl.BlockSpec(a.shape, lambda step, rank=len(a.shape): (0,) * rank) for a in outputs
        ],
        out_shape=outputs,
        compiler_params=pltpu.CompilerParams(vmem_limit_bytes=VMEM_BYTES),
        cost_estimate=pl.CostEstimate(flops=flops, bytes_accessed=8 << 20, transcendentals=0),
        name=name,
    )(*inputs)


def entire(values):
    return pl.BlockSpec(values.shape, lambda step: (0,) * values.ndim)


def column_block(values, size, index):
    return pl.BlockSpec((values.shape[0], size), lambda step: (0, index))


def heads_body(groups, rep, rows_ref, gain_ref, kv_ref, cos_ref, sin_ref, out_ref, normed_ref):
    count, _, _, tok_rows, head = out_ref.shape
    size = kv_ref.shape[1] // (2 * count)
    per_head = head // size
    rows = rows_ref[0:tok_rows, :].astype(FULL)
    normed = norm_rows(rows, gain_ref[...]).astype(LOW)
    normed_ref[...] = normed
    both = dot(normed, kv_ref[...], 1, 0)

    def head_of(kind, index):
        pieces = [
            both[:, (2 * part + kind) * size : (2 * part + kind + 1) * size]
            for part in range(index * per_head, (index + 1) * per_head)
        ]
        return pieces[0] if per_head == 1 else jnp.concatenate(pieces, axis=1)

    for owner in range(count):
        for group in range(groups):
            index = (owner * groups + group) // rep
            keys = turn_heads(head_of(0, index), cos_ref[...], sin_ref[...])
            out_ref[owner, group, 0] = keys.astype(LOW)
            out_ref[owner, group, 1] = head_of(1, index).astype(LOW)


def make_heads(rows_low, gain_row, proj, cosine, sine, groups, rep):
    count = lax.axis_size("narrow")
    tok_rows, head = cosine.shape
    width = rows_low.shape[1]
    size = 2 * KVH * HD
    return local_call(
        functools.partial(heads_body, groups, rep),
        [rows_low, gain_row, proj, cosine, sine],
        [entire(rows_low), entire(gain_row), column_block(proj, size, 0)]
        + [entire(cosine), entire(sine)],
        [struct((count, groups, 2, tok_rows, head), LOW), struct((tok_rows, width), LOW)],
        2 * tok_rows * width * size,
        "make_heads",
    )


def attend_body(
    start_ref,
    gains_ref,
    q_ref,
    o_ref,
    kv_ref,
    cos_ref,
    sin_ref,
    seg_ref,
    seg_all_ref,
    pick_ref,
    queries_ref,
    probs_ref,
    mixed_ref,
    part_ref,
    normed_ref,
    early_ref,
):
    count, groups, _, tok_rows, head = kv_ref.shape
    heads_own = probs_ref.shape[0]
    start = start_ref[...].astype(FULL)
    root = lax.rsqrt(jnp.mean(start * start, axis=-1, keepdims=True) + NORM_EPS)
    normed = (start * root * gains_ref[0:1, :]).astype(LOW)
    normed_ref[...] = normed
    early_ref[...] = (start * root * gains_ref[2:3, :]).astype(LOW)
    queries = dot(normed, q_ref[...], 1, 0)
    spots = lax.broadcasted_iota(jnp.int32, (1, count * tok_rows), 1)
    allowed = (seg_ref[...] == seg_all_ref[...]) & (pick_ref[...] >= spots)
    for group in range(groups):
        keys = jnp.concatenate([kv_ref[part, group, 0] for part in range(count)], axis=0)
        values = jnp.concatenate([kv_ref[part, group, 1] for part in range(count)], axis=0)
        for member in range(heads_own // groups):
            at = group * (heads_own // groups) + member
            spot = slice(at * head, (at + 1) * head)
            query = turn_heads(queries[:, spot], cos_ref[...], sin_ref[...]).astype(LOW)
            queries_ref[:, spot] = query
            scores = jnp.where(allowed, dot(query, keys, 1, 1) * head ** (-0.5), MASKED)
            shifted = jnp.exp(scores - jnp.max(scores, axis=-1, keepdims=True))
            probs = shifted / jnp.sum(shifted, axis=-1, keepdims=True)
            probs_ref[at] = probs
            mixed_ref[:, spot] = dot(probs.astype(LOW), values, 1, 0).astype(LOW)
    part_ref[...] = dot(mixed_ref[...], o_ref[...], 1, 1).astype(LOW)


def attend(start_low, gains, proj, own_head, cosine, sine, seg, seg_all, picks):
    count, groups, _, tok_rows, head = own_head.shape
    sel, width = start_low.shape
    heads_own = HEADS // count
    size = heads_own * head
    first = 2 * KVH * HD // size
    seq_len = count * tok_rows
    return local_call(
        attend_body,
        [start_low, gains, proj, proj, own_head, cosine, sine, seg, seg_all, picks],
        [
            entire(start_low),
            entire(gains),
            column_block(proj, size, first),
            column_block(proj, size, first + 1),
        ]
        + [entire(a) for a in (own_head, cosine, sine, seg, seg_all, picks)],
        [
            struct((sel, size), LOW),
            struct((heads_own, sel, seq_len), FULL),
            struct((sel, size), LOW),
            struct((sel, width), LOW),
            struct((sel, width), LOW),
            struct((sel, width), LOW),
        ],
        4 * sel * size * (width + seq_len),
        "attend",
    )


def attend_back_body(
    grad_ref,
    q_ref,
    o_ref,
    kv_ref,
    queries_ref,
    probs_ref,
    cos_ref,
    sin_ref,
    cos_all_ref,
    sin_all_ref,
    out_ref,
    grad_q_ref,
    part_ref,
):
    count, groups, _, tok_rows, head = kv_ref.shape
    heads_own = probs_ref.shape[0]
    scale = head ** (-0.5)
    grad_mixed = dot(grad_ref[...], o_ref[...], 1, 0).astype(LOW)
    for group in range(groups):
        keys = jnp.concatenate([kv_ref[part, group, 0] for part in range(count)], axis=0)
        values = jnp.concatenate([kv_ref[part, group, 1] for part in range(count)], axis=0)
        grad_keys = jnp.zeros(keys.shape, FULL)
        grad_values = jnp.zeros(keys.shape, FULL)
        for member in range(heads_own // groups):
            at = group * (heads_own // groups) + member
            spot = slice(at * head, (at + 1) * head)
            probs = probs_ref[at]
            grad_probs = dot(grad_mixed[:, spot], values, 1, 1)
            inner = jnp.sum(probs * grad_probs, axis=-1, keepdims=True)
            grad_scores = (probs * (grad_probs - inner)).astype(LOW)
            grad_query = dot(grad_scores, keys, 1, 0) * scale
            grad_q_ref[:, spot] = turn_heads(grad_query, cos_ref[...], -sin_ref[...]).astype(LOW)
            grad_keys = grad_keys + dot(grad_scores, queries_ref[:, spot], 0, 0)
            grad_values = grad_values + dot(probs.astype(LOW), grad_mixed[:, spot], 0, 0)
        grad_keys = turn_heads(grad_keys * scale, cos_all_ref[...], -sin_all_ref[...])
        for part in range(count):
            rows = slice(part * tok_rows, (part + 1) * tok_rows)
            out_ref[part, group, 0] = grad_keys[rows].astype(LOW)
            out_ref[part, group, 1] = grad_values[rows].astype(LOW)
    part_ref[...] = dot(grad_q_ref[...], q_ref[...], 1, 1).astype(LOW)


def attend_back(grad, proj, own_head, queries, probs, cosine, sine, cosine_all, sine_all):
    count, groups, _, tok_rows, head = own_head.shape
    sel, width = grad.shape
    size = queries.shape[1]
    first = 2 * KVH * HD // size
    return local_call(
        attend_back_body,
        [grad, proj, proj, own_head, queries, probs, cosine, sine, cosine_all, sine_all],
        [entire(grad), column_block(proj, size, first), column_block(proj, size, first + 1)]
        + [
            entire(a)
            for a in (own_head, queries, probs, cosine, sine, cosine_all, sine_all)
        ],
        [struct(own_head.shape, LOW), struct((sel, size), LOW), struct((sel, width), LOW)],
        8 * sel * size * width,
        "attend_back",
    )


def norm_back_rows(values, gain_row, grad):
    root = lax.rsqrt(jnp.mean(values * values, axis=-1, keepdims=True) + NORM_EPS)
    scaled = gain_row * grad
    inner = jnp.mean(values * scaled, axis=-1, keepdims=True)
    result = root * scaled - values * (root * root * root * inner)
    return result, jnp.sum(values * root * grad, axis=0, keepdims=True)


def rows_back_body(
    rep,
    rows_ref,
    gains_ref,
    kv_ref,
    heads_ref,
    pick_ref,
    early_ref,
    base_ref,
    out_ref,
    attn_gain_ref,
    early_gain_ref,
    grad_kv_ref,
):
    count, groups, _, tok_rows, head = heads_ref.shape
    size = kv_ref.shape[1] // (2 * count)
    per_head = head // size
    for index in range(KVH):
        for kind in range(2):
            copies = [
                heads_ref[at // groups, at % groups, kind]
                for at in range(index * rep, (index + 1) * rep)
            ]
            total = copies[0]
            if rep > 1:
                total = sum(copy.astype(FULL) for copy in copies).astype(LOW)
            for piece in range(per_head):
                lane = (2 * (index * per_head + piece) + kind) * size
                grad_kv_ref[:, lane : lane + size] = total[:, piece * size : (piece + 1) * size]
    values = rows_ref[...].astype(FULL)
    own = values[tok_rows:]
    tok_part, tok_gain = norm_back_rows(
        values[:tok_rows], gains_ref[0:1, :], dot(grad_kv_ref[...], kv_ref[...], 1, 1)
    )
    pick_part, pick_gain = norm_back_rows(own, gains_ref[0:1, :], pick_ref[...])
    early_part, early_gain = norm_back_rows(own, gains_ref[2:3, :], early_ref[...])
    attn_gain_ref[...] = tok_gain + pick_gain
    early_gain_ref[...] = early_gain
    out_ref[0:tok_rows, :] = tok_part.astype(LOW)
    out_ref[tok_rows:, :] = (pick_part + early_part + base_ref[...]).astype(LOW)


def rows_back(rows_low, gains, proj, heads, grad_pick, grad_early, base, rep):
    tok_rows = heads.shape[3]
    width = rows_low.shape[1]
    size = 2 * KVH * HD
    return local_call(
        functools.partial(rows_back_body, rep),
        [rows_low, gains, proj, heads, grad_pick, grad_early, base],
        [entire(rows_low), entire(gains), column_block(proj, size, 0)]
        + [entire(a) for a in (heads, grad_pick, grad_early, base)],
        [
            struct(rows_low.shape, LOW),
            struct((1, width), FULL),
            struct((1, width), FULL),
            struct((tok_rows, size), LOW),
        ],
        2 * tok_rows * width * size,
        "rows_back",
    )


def assemble_body(out_columns, *refs):
    pieces, out_ref = refs[:-1], refs[-1]
    count = len(pieces)
    me = lax.axis_index("narrow")
    for step, piece in enumerate(pieces):
        source = lax.rem(me - step + count, count)
        spot = pl.ds(pl.multiple_of(source * out_columns, out_columns), out_columns)
        out_ref[:, spot] = piece[...]


def assemble(pieces):
    rows, columns = pieces[0].shape
    outputs = [struct((rows, columns * len(pieces)), pieces[0].dtype)]
    return local_call(
        functools.partial(assemble_body, columns),
        list(pieces),
        [entire(piece) for piece in pieces],
        outputs,
        0,
        "assemble",
    )[0]


def feed_body(inner_ref, weight_ref, gate_ref, up_ref, hidden_ref, out_ref, total):
    part = pl.program_id(0)
    inner = inner_ref[...]
    gate = dot(inner, weight_ref[0, 0], 1, 1)
    up = dot(inner, weight_ref[0, 1], 1, 1)
    hidden = (jax.nn.silu(gate) * up).astype(LOW)
    gate_ref[0] = gate
    up_ref[0] = up
    hidden_ref[0] = hidden
    product = dot(hidden, weight_ref[0, 2], 1, 0)

    @pl.when(part == 0)
    def _():
        total[...] = product

    @pl.when(part > 0)
    def _():
        total[...] = total[...] + product

    @pl.when(part == pl.num_programs(0) - 1)
    def _():
        out_ref[...] = total[...].astype(LOW)


def feed(inner, weight):
    parts, _, size, width = weight.shape
    sel = inner.shape[0]
    same = pl.BlockSpec((sel, width), lambda part: (0, 0))
    slab = pl.BlockSpec((1, sel, size), lambda part: (part, 0, 0))
    return pl.pallas_call(
        feed_body,
        grid=(parts,),
        in_specs=[same, pl.BlockSpec((1, 3, size, width), lambda part: (part, 0, 0, 0))],
        out_specs=[slab, slab, slab, same],
        out_shape=[
            struct((parts, sel, size), FULL),
            struct((parts, sel, size), FULL),
            struct((parts, sel, size), LOW),
            struct((sel, width), LOW),
        ],
        scratch_shapes=[pltpu.VMEM((sel, width), FULL)],
        compiler_params=pltpu.CompilerParams(vmem_limit_bytes=VMEM_BYTES),
        cost_estimate=pl.CostEstimate(
            flops=6 * sel * parts * size * width,
            bytes_accessed=weight.size * 2,
            transcendentals=0,
        ),
        name="feed",
    )(inner, weight)


def feed_back_body(grad_ref, weight_ref, gate_ref, up_ref, hidden_ref, acts_ref, out_ref, total):
    part = pl.program_id(0)
    grad_hidden = dot(grad_ref[...], weight_ref[0, 2], 1, 1)
    gate = gate_ref[0]
    sigma = jax.nn.sigmoid(gate)
    grad_gate = (grad_hidden * up_ref[0] * sigma * (1.0 + gate * (1.0 - sigma))).astype(LOW)
    grad_up = (grad_hidden * gate * sigma).astype(LOW)
    acts_ref[0, 0] = grad_gate
    acts_ref[0, 1] = grad_up
    acts_ref[0, 2] = hidden_ref[0]
    product = dot(grad_gate, weight_ref[0, 0], 1, 0) + dot(grad_up, weight_ref[0, 1], 1, 0)

    @pl.when(part == 0)
    def _():
        total[...] = product

    @pl.when(part > 0)
    def _():
        total[...] = total[...] + product

    @pl.when(part == pl.num_programs(0) - 1)
    def _():
        out_ref[...] = total[...].astype(LOW)


def feed_back(grad, weight, gate, up, hidden):
    parts, _, size, width = weight.shape
    sel = grad.shape[0]
    same = pl.BlockSpec((sel, width), lambda part: (0, 0))
    slab = pl.BlockSpec((1, sel, size), lambda part: (part, 0, 0))
    return pl.pallas_call(
        feed_back_body,
        grid=(parts,),
        in_specs=[same, pl.BlockSpec((1, 3, size, width), lambda part: (part, 0, 0, 0))]
        + [slab] * 3,
        out_specs=[pl.BlockSpec((1, 3, sel, size), lambda part: (part, 0, 0, 0)), same],
        out_shape=[struct((parts, 3, sel, size), LOW), struct((sel, width), LOW)],
        scratch_shapes=[pltpu.VMEM((sel, width), FULL)],
        compiler_params=pltpu.CompilerParams(vmem_limit_bytes=VMEM_BYTES),
        cost_estimate=pl.CostEstimate(
            flops=6 * sel * parts * size * width,
            bytes_accessed=weight.size * 2,
            transcendentals=0,
        ),
        name="feed_back",
    )(grad, weight, gate, up, hidden)


def newton_steps(problems):
    rows, width = problems[0][0].shape
    block = min(1024, width)
    eye = lax.broadcasted_iota(jnp.int32, (rows, rows), 0) == lax.broadcasted_iota(
        jnp.int32, (rows, rows), 1
    )

    def strip(part):
        return pl.ds(pl.multiple_of(part * block, block), block)

    def over(function, start):
        return lax.fori_loop(0, width // block, function, start)

    def add_squares(part, totals):
        values = [current[:, strip(part)] for current, low, gram, rest in problems]
        return [total + jnp.sum(value * value) for total, value in zip(totals, values)]

    totals = over(add_squares, [jnp.float32(0.0)] * len(problems))
    scales = [1.0 / (jnp.sqrt(total) + 1e-07) for total in totals]

    def begin(part, carry):
        for scale, (current, low, gram, rest) in zip(scales, problems):
            values = current[:, strip(part)] * scale
            current[:, strip(part)] = values
            low[:, strip(part)] = values.astype(LOW)
        return carry

    over(begin, 0)

    def iteration(turn, carry):
        for current, low, gram, rest in problems:
            gram[...] = jnp.zeros_like(gram)

        def add_gram(part, carry):
            for current, low, gram, rest in problems:
                values = low[:, strip(part)]
                gram[...] = gram[...] + dot(values, values, 1, 1)
            return carry

        over(add_gram, 0)
        seconds = []
        for current, low, gram, rest in problems:
            whole = gram[...]
            middle = jnp.sum(jnp.where(eye, whole, 0.0)) / rows
            rest[...] = (whole - jnp.where(eye, middle, 0.0)).astype(LOW)
            square = dot(rest[...], rest[...], 1, 0)
            whole = gram[...]
            centred = whole - jnp.where(eye, middle, 0.0)
            square = square + 2.0 * middle * centred + jnp.where(eye, middle * middle, 0.0)
            whole = NEWTON_B * whole + NEWTON_C * square
            second = jnp.sum(jnp.where(eye, whole, 0.0)) / rows
            rest[...] = (whole - jnp.where(eye, second, 0.0)).astype(LOW)
            seconds.append(second)

        def apply(part, carry):
            for second, (current, low, gram, rest) in zip(seconds, problems):
                values = (NEWTON_A + second) * current[:, strip(part)] + dot(
                    rest[...], low[:, strip(part)], 1, 0
                )
                current[:, strip(part)] = values
                low[:, strip(part)] = values.astype(LOW)
            return carry

        over(apply, 0)
        return carry

    lax.fori_loop(0, NS_STEPS, iteration, 0)


def newton_scratch(rows, width):
    return [
        pltpu.VMEM((rows, width), FULL),
        pltpu.VMEM((rows, width), LOW),
        pltpu.VMEM((rows, rows), FULL),
        pltpu.VMEM((rows, rows), LOW),
    ]


def newton_cost(count, rows, width):
    return pl.CostEstimate(
        flops=NS_STEPS * count * (4 * rows * rows * width + 2 * rows * rows * rows),
        bytes_accessed=6 * count * rows * width,
        transcendentals=0,
    )


def newton_body(factor_ref, mom_ref, grad_ref, out_ref, *problem):
    current, low = problem[:2]
    parts, rows, columns = mom_ref.shape
    factor = factor_ref[0]
    size = grad_ref.shape[1]
    for part in range(parts):
        spot = slice(part * columns, (part + 1) * columns)
        for source in range(parts):
            here = slice(source * size, (source + 1) * size)
            current[here, spot] = MOMENTUM * mom_ref[part, here, :].astype(
                FULL
            ) + factor * grad_ref[source, :, spot].astype(FULL)
    newton_steps([problem])
    for part in range(parts):
        out_ref[part] = low[:, part * columns : (part + 1) * columns]


def newton_small_body(rows, factor_ref, mom_ref, grad_ref, kv_ref, out_ref, *scratch):
    problems = [scratch[4 * at : 4 * at + 4] for at in range(4)]
    parts, _, columns = mom_ref.shape
    kv_columns = kv_ref.shape[2]
    half = rows // 2
    factor = factor_ref[0]
    for part in range(parts):
        spot = slice(part * columns, (part + 1) * columns)
        for member in range(2):
            current = problems[member][0]
            here = slice(member * rows, (member + 1) * rows)
            mom, grad = mom_ref[part, here, :], grad_ref[part, here, :]
            current[:, spot] = MOMENTUM * mom.astype(FULL) + factor * grad.astype(FULL)
        spot = slice(part * kv_columns, (part + 1) * kv_columns)
        for member in range(2):
            current = problems[2 + member][0]
            piece = kv_ref[part, member * rows : (member + 1) * rows, :].astype(FULL)
            for side in range(2):
                lane = (2 * member + side) * kv_columns
                mom = mom_ref[part, 2 * rows : 2 * rows + half, lane : lane + kv_columns]
                here = slice(side * half, (side + 1) * half)
                current[here, spot] = MOMENTUM * mom.astype(FULL) + factor * piece[here]
    newton_steps(problems[:2])
    newton_steps(problems[2:])
    out_ref[...] = jnp.zeros_like(out_ref)
    for part in range(parts):
        for member in range(2):
            out_ref[part, member * rows : (member + 1) * rows, :] = problems[member][1][
                :, part * columns : (part + 1) * columns
            ]
            low = problems[2 + member][1]
            for side in range(2):
                lane = (2 * member + side) * kv_columns
                out_ref[part, 2 * rows : 2 * rows + half, lane : lane + kv_columns] = low[
                    side * half : (side + 1) * half,
                    part * kv_columns : (part + 1) * kv_columns,
                ]


def newton_any_body(rows, factor_ref, mom_ref, grad_ref, qo_ref, kv_ref, out_ref, *scratch):
    parts = mom_ref.shape[0]
    owner = lax.rem(3 + lax.rem(lax.axis_index("wide"), 2), parts)
    small = lax.axis_index("narrow") == owner

    @pl.when(small)
    def _():
        newton_small_body(rows, factor_ref, mom_ref, qo_ref, kv_ref, out_ref, *scratch[4:])

    @pl.when(jnp.logical_not(small))
    def _():
        newton_body(factor_ref, mom_ref, grad_ref, out_ref, *scratch[:4])


def newton(factor, mom, grad, qo_grad, kv_grad):
    parts, slot_rows, columns = mom.shape
    width = parts * columns
    rows = kv_grad.shape[1] // 2
    kv_width = parts * kv_grad.shape[2]
    return pl.pallas_call(
        functools.partial(newton_any_body, rows),
        in_specs=[pl.BlockSpec(memory_space=pltpu.SMEM)] + [VMEM] * 4,
        out_specs=VMEM,
        out_shape=struct(mom.shape, LOW),
        scratch_shapes=newton_scratch(slot_rows, width)
        + newton_scratch(rows, width) * 2
        + newton_scratch(rows, kv_width) * 2,
        compiler_params=pltpu.CompilerParams(vmem_limit_bytes=VMEM_BYTES),
        cost_estimate=newton_cost(1, slot_rows, width),
        name="newton",
    )(factor.reshape(1), mom, grad, qo_grad, kv_grad)


def lookup_body(ids_ref, turn_ref, table_ref, out_ref, low_ref, list_ref, held, rows, sem):
    vocab = table_ref.shape[0]
    count = out_ref.shape[0]
    load = pltpu.make_async_copy(table_ref, held, sem)
    load.start()
    rows[...] = jnp.zeros_like(rows)

    found = turn_ref[count]

    def note(group, carry):
        for member in range(UNROLL):
            at = group * UNROLL + member
            list_ref[turn_ref[at]] = at
        return carry

    lax.fori_loop(0, count // UNROLL, note, 0)
    for member in range(UNROLL):
        list_ref[found + member] = count
    list_ref[count + UNROLL] = found
    load.wait()

    def step(group, carry):
        for member in range(UNROLL):
            at = list_ref[group * UNROLL + member]
            spot = jnp.minimum(ids_ref[jnp.minimum(at, count - 1)], vocab - 1)
            rows[pl.ds(at, 1), :] = held[pl.ds(spot, 1), :]
        return carry

    lax.fori_loop(0, (found + UNROLL - 1) // UNROLL, step, 0)
    out_ref[...] = rows[pl.ds(0, count), :].astype(LOW)
    low_ref[...] = held[...].astype(LOW)


def lookup(table, ids):
    vocab, columns = table.shape
    count = ids.shape[0]
    mine = (ids < vocab).reshape(-1, 128)
    before = jnp.arange(128)[:, None] < jnp.arange(128)[None, :]
    in_row = dot(mine.astype(LOW), before.astype(LOW), 1, 0)
    per_row = jnp.sum(mine.astype(FULL), axis=1)
    lines = jnp.arange(mine.shape[0])
    ahead = jnp.sum(jnp.where(lines[:, None] > lines[None, :], per_row[None, :], 0.0), axis=1)
    found = jnp.sum(per_row).astype(jnp.int32)
    turns = (in_row + ahead[:, None]).astype(jnp.int32)
    turns = jnp.where(mine, turns, count + UNROLL + 1).reshape(-1)
    turns = jnp.concatenate([turns, jnp.full((128,), found)])
    return pl.pallas_call(
        lookup_body,
        in_specs=[pl.BlockSpec(memory_space=pltpu.SMEM)] * 2 + [ANY],
        out_specs=[VMEM, VMEM, pl.BlockSpec(memory_space=pltpu.SMEM)],
        scratch_shapes=[
            pltpu.VMEM((vocab, columns), FULL),
            pltpu.VMEM((count + 8, columns), FULL),
            pltpu.SemaphoreType.DMA,
        ],
        out_shape=[
            struct((count, columns), LOW),
            struct((vocab, columns), LOW),
            struct((count + 2 * UNROLL,), jnp.int32),
        ],
        compiler_params=pltpu.CompilerParams(vmem_limit_bytes=VMEM_BYTES),
        cost_estimate=pl.CostEstimate(
            flops=0, bytes_accessed=vocab * columns * 4, transcendentals=0
        ),
        name="lookup",
    )(ids, turns, table)


def spread_body(
    ids_ref, list_ref, rows_ref, head_ref, out_ref, square_ref, even, odd, rows, sem
):
    vocab = out_ref.shape[0]
    count = rows_ref.shape[0]
    chunk = 256

    def strip(part):
        return pl.ds(pl.multiple_of(part * chunk, chunk), chunk)

    def begin(part, carry):
        even[strip(part), :] = head_ref[strip(part), :].astype(FULL)
        odd[strip(part), :] = jnp.zeros((chunk, odd.shape[1]), FULL)
        return carry

    lax.fori_loop(0, vocab // chunk, begin, 0)

    def widen(part, carry):
        rows[strip(part), :] = rows_ref[strip(part), :].astype(FULL)
        return carry

    lax.fori_loop(0, count // chunk, widen, 0)
    rows[pl.ds(count, 8), :] = jnp.zeros((8, rows.shape[1]), FULL)

    def step(group, carry):
        for member in range(UNROLL):
            at = list_ref[group * UNROLL + member]
            spot = jnp.minimum(ids_ref[jnp.minimum(at, count - 1)], vocab - 1)
            total = even if member % 2 == 0 else odd
            total[pl.ds(spot, 1), :] = total[pl.ds(spot, 1), :] + rows[pl.ds(at, 1), :]
        return carry

    found = list_ref[count + UNROLL]
    lax.fori_loop(0, (found + UNROLL - 1) // UNROLL, step, 0)

    def finish(part, squares):
        value = even[strip(part), :] + odd[strip(part), :]
        even[strip(part), :] = value
        return squares + jnp.sum((value * value).reshape(chunk // 8, 8, -1), axis=0)

    square_ref[...] = lax.fori_loop(
        0, vocab // chunk, finish, jnp.zeros((8, even.shape[1]), FULL)
    )
    store = pltpu.make_async_copy(even, out_ref, sem)
    store.start()
    store.wait()


def spread(ids, listed, rows, head):
    vocab, columns = head.shape
    count = ids.shape[0]
    smem = pl.BlockSpec(memory_space=pltpu.SMEM)
    return pl.pallas_call(
        spread_body,
        in_specs=[smem, smem, VMEM, VMEM],
        out_specs=[ANY, VMEM],
        scratch_shapes=[
            pltpu.VMEM((vocab, columns), FULL),
            pltpu.VMEM((vocab, columns), FULL),
            pltpu.VMEM((count + 8, columns), FULL),
            pltpu.SemaphoreType.DMA,
        ],
        out_shape=[struct((vocab, columns), FULL), struct((8, columns), FULL)],
        compiler_params=pltpu.CompilerParams(vmem_limit_bytes=VMEM_BYTES),
        cost_estimate=pl.CostEstimate(
            flops=count * columns, bytes_accessed=vocab * columns * 8, transcendentals=0
        ),
        name="spread",
    )(ids, listed, rows, head)


def adamw(weight, first_m, second_m, grad, rate, decay):
    first_new = BETA_ONE * first_m + (1.0 - BETA_ONE) * grad
    second_new = BETA_TWO * second_m + (1.0 - BETA_TWO) * grad * grad
    update = (
        first_new
        / (1.0 - BETA_ONE**STEP)
        / (jnp.sqrt(second_new / (1.0 - BETA_TWO**STEP)) + ADAM_EPS)
    )
    return (weight * (1.0 - rate * decay) - rate * update, first_new, second_new)


def cut_columns(values, count):
    rows, columns = values.shape
    return jnp.moveaxis(values.reshape(rows, count, columns // count), 1, 0)


def shifted(parts, axis, step):
    count = lax.axis_size(axis)
    pairs = [(source, (source + step) % count) for source in range(count)]
    return lax.ppermute(parts, axis, pairs)


def per_device(
    tokens,
    picks,
    targets,
    lengths,
    skip,
    embed,
    embed_m,
    embed_v,
    attn_qo,
    attn_qo_mom,
    attn_kv,
    attn_kv_mom,
    ffn,
    ffn_mom,
    gains,
    gains_m,
    gains_v,
):
    wide_count = lax.axis_size("wide")
    narrow_count = lax.axis_size("narrow")
    narrow_spot = lax.axis_index("narrow")
    wide_spot = lax.axis_index("wide")
    seq_len = tokens.shape[1]
    sel = picks.shape[1]
    vocab_rows, columns = embed.shape
    width = columns * wide_count
    own_rows = sel // narrow_count
    tok_rows = seq_len // narrow_count
    all_rows = own_rows + tok_rows
    heads_own = HEADS // narrow_count
    head_cols = heads_own * HD
    repeat = max(1, narrow_count // KVH)
    groups = KVH * repeat // narrow_count
    ffn_rows = ffn.shape[0]
    ffn_size = ffn_rows // narrow_count
    total_rows = wide_count * sel
    lens = lengths[0]
    pick_ids = picks[0]
    keep_layer = (1 - skip[0]).astype(FULL)
    keep_row = jnp.full((1, width), keep_layer)
    lanes = 128

    def box(flat):
        height = -(-flat.shape[0] // (8 * lanes)) * 8
        return jnp.pad(flat, (0, height * lanes - flat.shape[0])).reshape(height, lanes)

    ffn_low = jnp.moveaxis(ffn, 1, 0).astype(LOW)
    ffn_cut = ffn_low.reshape(3, narrow_count, ffn_size, ffn_low.shape[2])
    ffn_cut = jnp.moveaxis(ffn_cut, 1, 0).reshape(narrow_count, 3 * ffn_size, -1)
    kv_own = attn_kv.reshape(columns, -1).astype(LOW)

    where_at = jnp.arange(seq_len, dtype=jnp.int32)
    pick_tokens = jnp.sum(
        jnp.where(pick_ids[:, None] == where_at[None, :], tokens[0][None, :], 0), axis=1
    )
    ints = box(jnp.concatenate([tokens[0], pick_tokens, targets[0]]))
    all_ints, all_gains, kv_part = launch(
        [
            gather_wide(ints),
            gather_both(box(gains.astype(LOW).astype(FULL).reshape(-1))),
            gather_blocks("narrow", kv_own),
        ],
        0,
        "gather_ids",
    )
    kv_part = jnp.moveaxis(kv_part, 0, 1).reshape(columns, -1)
    proj_own = jnp.concatenate([kv_part, attn_qo.reshape(columns, -1).astype(LOW)], axis=1)
    proj = lax.all_gather(proj_own, "wide", axis=0, tiled=True)
    ffn_cut, all_ints = lax.optimization_barrier((ffn_cut, all_ints))
    ffn_pieces = [lax.dynamic_index_in_dim(ffn_cut, narrow_spot, 0, False)] + [
        shifted(
            lax.dynamic_index_in_dim(
                ffn_cut, lax.rem(narrow_spot + step, narrow_count), 0, False
            ),
            "narrow",
            step,
        )
        for step in range(1, narrow_count)
    ]
    gain_size = gains.shape[1]
    gain_w = all_gains.reshape(narrow_count, wide_count, -1)[:, :, : 3 * gain_size]
    gain_w = gain_w.reshape(narrow_count, wide_count, 3, gain_size)
    gain_w = jnp.transpose(gain_w, (2, 1, 0, 3)).reshape(3, width)
    all_ints = all_ints.reshape(wide_count, -1)
    tokens_all = all_ints[:, :seq_len].reshape(wide_count, narrow_count, tok_rows)
    picked_all = all_ints[:, seq_len : seq_len + sel].reshape(wide_count, narrow_count, own_rows)
    targets_all = all_ints[:, seq_len + sel : seq_len + 2 * sel].reshape(-1)
    wanted = jnp.moveaxis(jnp.concatenate([tokens_all, picked_all], axis=2), 1, 0).reshape(-1)
    local_ids = wanted - narrow_spot * vocab_rows
    inside = (local_ids >= 0) & (local_ids < vocab_rows)
    spots = jnp.where(inside, local_ids, vocab_rows)
    found, embed_low, listed = lookup(embed, spots)
    ffn_pieces, found = lax.optimization_barrier((ffn_pieces, found))
    ffn_sub = assemble(ffn_pieces).reshape(3, ffn_size, width)
    ffn_sub, found = lax.optimization_barrier((ffn_sub, found))
    ffn_w = lax.all_gather(ffn_sub, "wide", axis=0)
    found = found.reshape(narrow_count, wide_count * all_rows, columns)
    embed_cut = embed_low.reshape(wide_count, vocab_rows // wide_count, columns)
    table_half = embed_cut.shape[1] // 2
    rows_low = launch([fetch_rows(found, all_rows)], 1, "fetch_rows")[0]

    mom_qo = jnp.moveaxis(attn_qo_mom, 1, 0)
    mom_kv = jnp.moveaxis(attn_kv_mom, 1, 0)
    mom_ffn = jnp.moveaxis(ffn_mom, 1, 0)
    slot_rows, slot_cols = mom_ffn.shape[1:]

    block_rows, q_size = mom_qo.shape[1:]
    kv_size = mom_kv.shape[2]
    half_rows = block_rows // 2
    kv_box = jnp.moveaxis(mom_kv.reshape(4, half_rows, kv_size), 0, 1).reshape(half_rows, -1)
    small_box = jnp.concatenate([mom_qo.reshape(2 * block_rows, q_size), kv_box])
    small_box = jnp.pad(small_box, ((0, slot_rows - small_box.shape[0]), (0, 0)))
    mom_parts = jnp.concatenate([mom_ffn, small_box[None]]).astype(LOW)

    seg_all, cosine_all, sine_all = angles_at(lens, where_at)
    cosine_all, sine_all = wide_angles(cosine_all, sine_all)
    seg_mine, cosine, sine = angles_at(lens, pick_ids)
    cosine, sine = wide_angles(cosine, sine)

    def tok_part(angles):
        return lax.dynamic_slice_in_dim(angles, narrow_spot * tok_rows, tok_rows, 0)

    by_head, normed_tok = make_heads(
        rows_low, gain_w[0:1], proj, tok_part(cosine_all), tok_part(sine_all), groups, repeat
    )
    own_head, start_low, tok_cols, table_top = launch(
        [
            swap_blocks("narrow", by_head),
            gather_blocks("narrow", rows_low[tok_rows:]),
            split_columns("wide", normed_tok),
            join_columns("wide", embed_cut[:, :table_half]),
        ],
        2,
        "trade_heads",
    )
    start_low, ffn_w = lax.optimization_barrier((start_low, ffn_w))
    start_low = start_low.reshape(sel, width)
    queries, probs, mixed, attn_part, normed, early_part = attend(
        start_low,
        gain_w,
        proj,
        own_head,
        cosine,
        sine,
        seg_mine[:, None],
        seg_all[None, :],
        pick_ids[:, None],
    )
    early = lax.all_gather(early_part, "wide", axis=0, tiled=True)
    start_own = rows_low[tok_rows:].astype(FULL)
    middle, inner, mixed_wide, pick_cols = launch(
        [
            settle(
                attn_part,
                start_own,
                start_own,
                jnp.ones((1, width), FULL),
                gain_w[1:2],
            ),
            gather_wide(mixed),
            split_columns("wide", normed),
        ],
        3,
        "settle_middle",
    )
    inner = inner.reshape(sel, width)
    inner_all = lax.all_gather(inner, "wide", axis=0, tiled=True)
    gate, up, hidden, fed = feed(inner, ffn_w)
    final_own, late_part, table_low = launch(
        [
            settle(fed, middle, start_own, keep_row, gain_w[2:3]),
            join_columns("wide", embed_cut[:, table_half:]),
        ],
        4,
        "settle_late",
    )
    table_own = jnp.concatenate([table_top, table_low])

    table_count = table_own.shape[0]
    local_target = targets_all - (narrow_spot * vocab_rows + wide_spot * table_count)
    has_target = jnp.arange(table_count, dtype=jnp.int32)[:, None] == local_target[None, :]
    counted = (targets_all >= 0).astype(FULL)
    loss_count = jnp.sum(counted)

    def exit_logits(features):
        logits = dot(table_own, features, 1, 1)
        peak = jnp.max(logits, axis=0)
        total = jnp.sum(jnp.exp(logits - peak[None, :]), axis=0)
        picked = jnp.sum(jnp.where(has_target, logits, 0.0), axis=0)
        return logits, jnp.stack([peak, total, picked])

    half = slot_rows // 2
    late, mom_top, early_logits, early_stats = launch(
        [
            gather_wide(late_part.reshape(sel, width)),
            swap_turned(mom_parts[:, :half]),
            exit_stats(early, table_own, local_target[None, :]),
        ],
        5,
        "gather_late",
    )
    late = late.reshape(total_rows, width)
    late_logits, late_stats = exit_logits(late)
    stats = jnp.concatenate([early_stats, late_stats], axis=1).reshape(3, 8, -1)
    stats = launch([combine(stats, merge_stats)], 6, "combine_stats")[0]
    stats, inner_all = lax.optimization_barrier((stats, inner_all))
    stats = stats.reshape(3, -1)
    log_norms = stats[0] + jnp.log(stats[1])
    losses = log_norms - stats[2]
    loss_sum = jnp.sum(
        counted * (EXIT_EARLY * losses[:total_rows] + EXIT_LAST * losses[total_rows:])
    )

    def exit_back(logits, log_norm, weight):
        grad_logits = (
            (jnp.exp(logits - log_norm[None, :]) - has_target.astype(FULL))
            * (weight * counted)[None, :]
        ).astype(LOW)
        return grad_logits

    late_grad = exit_back(late_logits, log_norms[total_rows:], EXIT_LAST)
    late_back = dot(late_grad, table_own, 0, 0).astype(LOW)
    early_grad = exit_back(early_logits, log_norms[:total_rows], EXIT_EARLY)
    grad_late, mom_low, early_back, _ = launch(
        [
            sum_wide(late_back),
            swap_turned(mom_parts[:, half:]),
            later(product([early_grad], [table_own], 0, [[(0, 0)]]), 1),
        ],
        7,
        "sum_late",
    )
    mom_owned = jnp.concatenate([mom_top, mom_low], axis=1)
    early_back, grad_late = lax.optimization_barrier((early_back, grad_late))
    grad_early = lax.psum_scatter(early_back[0], "wide", scatter_dimension=0, tiled=True)
    grad_final, gain_late, grad_out = launch(
        [
            settle_back(
                grad_late.astype(LOW),
                final_own,
                jnp.zeros_like(final_own),
                keep_row,
                gain_w[2:3],
            ),
        ],
        8,
        "back_late",
    )
    grad_layer = grad_final * keep_layer
    grad_out = grad_out.reshape(sel, width)
    out_all = lax.all_gather(grad_out, "wide", axis=0, tiled=True)
    acts, fed_back = feed_back(grad_out, ffn_w, gate, up, hidden)
    grad_mid, gain_mid, grad_branch, acts = launch(
        [
            settle_back(fed_back, middle, grad_layer, keep_row, gain_w[1:2]),
            swap_blocks("wide", acts),
        ],
        9,
        "back_middle",
    )
    acts = jnp.moveaxis(acts, 1, 0).reshape(3, total_rows, ffn_size)
    grad_branch, grad_early = lax.optimization_barrier((grad_branch, grad_early))
    grad_branch = grad_branch.reshape(sel, width)

    kv_parts, grad_queries, pick_part = attend_back(
        grad_branch, proj, own_head, queries, probs, cosine, sine, cosine_all, sine_all
    )
    grad_kv, grad_pick, grad_early, queries_wide, branch_cols, grad_head, _ = launch(
        [
            swap_blocks("narrow", kv_parts),
            sum_narrow(pick_part),
            sum_narrow(grad_early),
            gather_wide(grad_queries),
            split_columns("wide", grad_branch),
            product([early_grad, late_grad], [early, late], 1, [[(0, 0), (1, 1)]]),
        ],
        10,
        "trade_grads",
    )
    grad_kv, out_all = lax.optimization_barrier((grad_kv, out_all))
    grad_base = grad_mid + grad_final * (1.0 - keep_layer)
    grad_rows, gain_attn, gain_early, grad_kv = rows_back(
        rows_low, gain_w, proj, grad_kv, grad_pick, grad_early, grad_base, repeat
    )
    summed_qo = jnp.stack(
        [
            jnp.einsum("wtc,wtf->cf", pick_cols, queries_wide, preferred_element_type=FULL),
            jnp.einsum("wtc,wtf->cf", branch_cols, mixed_wide, preferred_element_type=FULL),
        ]
    )
    grad_rows, acts_owned, kv_wide, head_cols_all, grad_ffn, ffn_squares = launch(
        [
            return_rows(grad_rows),
            swap_owned(acts, 5),
            later(gather_wide(grad_kv, 3), 2),
            later(split_columns("wide", grad_head[0], 3), 2),
            product([acts], [inner_all, out_all], 0, [[(0, 0)], [(1, 0)], [(2, 1)]]),
        ],
        11,
        "return_rows",
    )
    turn = lax.rem(wide_spot, 2)
    grad_kv_w = jnp.einsum(
        "wtc,wtf->cf", tok_cols, kv_wide, preferred_element_type=FULL
    ).reshape(columns, narrow_count, 2, kv_size)
    grad_kv_w = jnp.moveaxis(grad_kv_w, 0, 2)
    summed_kv = lax.psum_scatter(grad_kv_w, "narrow", scatter_dimension=0, tiled=True)[0]
    summed_table, table_squares = spread(
        spots, listed, grad_rows.reshape(-1, columns), head_cols_all.reshape(vocab_rows, columns)
    )

    squares = (
        jnp.sum(summed_qo * summed_qo)
        + jnp.sum(summed_kv * summed_kv)
        + jnp.sum(ffn_squares)
        + jnp.sum(table_squares)
    )
    sums = jnp.stack(
        [gain_attn[0], gain_mid[0], gain_early[0] + gain_late[0], jnp.full((width,), squares)]
    )
    def owns_last():
        away = lax.axis_index("narrow") + narrow_count - lax.rem(lax.axis_index("wide"), 2)
        return lax.rem(away, narrow_count) >= 2

    sums, kv_owned, qo_owned, owned, _ = launch(
        [
            combine(sums.reshape(4, 8, -1), add_two),
            send_owner(summed_kv.astype(LOW).reshape(2 * block_rows, kv_size)),
            later(send_owner(summed_qo.astype(LOW).reshape(2 * columns, q_size)), 1),
            later(
                product(
                    [acts_owned],
                    [inner_all, out_all],
                    0,
                    [[(at, 0)] for at in range(narrow_count)],
                    False,
                    owns_last,
                ),
                1,
            ),
        ],
        12,
        "combine_sums",
    )
    sums = sums.reshape(4, width)
    summed_gain = lax.dynamic_slice_in_dim(
        sums[:3], (wide_spot * narrow_count + narrow_spot) * gain_size, gain_size, 1
    )
    square_total = sums[3, 0] + jnp.sum(sums[:3] * sums[:3])
    grad_norm = jnp.sqrt(square_total) / loss_count
    factor = jnp.minimum(1.0, CLIP_NORM / (grad_norm + 1e-06)) / loss_count

    final_parts, factor = lax.optimization_barrier((grad_ffn, factor))
    size = width // narrow_count

    def final_piece(spot):
        return lax.dynamic_slice_in_dim(final_parts, spot * size, size, 2)

    pieces = [final_piece(narrow_spot)] + [
        shifted(final_piece(lax.rem(narrow_spot + step, narrow_count)), "narrow", step)
        for step in range(1, narrow_count)
    ]
    directions = newton(
        factor, mom_owned, owned, qo_owned, kv_owned
    )
    directions, pieces, ffn, factor = lax.optimization_barrier(
        (directions, pieces, ffn, factor)
    )
    summed_ffn = jnp.zeros((3, narrow_count, ffn_size, size), LOW)
    for step, piece in enumerate(pieces):
        source = lax.rem(narrow_spot - step + narrow_count, narrow_count)
        summed_ffn = lax.dynamic_update_index_in_dim(summed_ffn, piece, source, 1)
    summed_ffn = summed_ffn.reshape(3, ffn_rows, size).astype(FULL)
    received = [lax.dynamic_index_in_dim(directions, narrow_spot, 0, False)] + [
        shifted(
            lax.dynamic_index_in_dim(
                directions, lax.rem(narrow_spot + step, narrow_count), 0, False
            ),
            "narrow",
            step,
        )
        for step in range(1, narrow_count)
    ]

    def direction_of(matrix):
        step = lax.rem(narrow_spot - matrix - turn + 2 * narrow_count, narrow_count)
        result = received[0]
        for at in range(1, narrow_count):
            result = jnp.where(step == at, received[at], result)
        return result

    dir_ffn = jnp.stack([direction_of(matrix) for matrix in range(3)]).astype(FULL)
    small = direction_of(3).astype(FULL)
    dir_qo = small[: 2 * block_rows].reshape(mom_qo.shape)
    dir_kv = small[2 * block_rows : 2 * block_rows + half_rows].reshape(half_rows, 4, kv_size)
    dir_kv = jnp.moveaxis(dir_kv, 1, 0).reshape(mom_kv.shape)

    embed_new, embed_m_new, embed_v_new = adamw(
        embed, embed_m, embed_v, summed_table * factor, RATE_ADAM, WEIGHT_DECAY
    )
    gains_new, gains_m_new, gains_v_new = adamw(
        gains, gains_m, gains_v, summed_gain * factor, RATE_GAIN, 0.0
    )

    def mom_next(mom, grad):
        return MOMENTUM * mom + jnp.moveaxis(grad * factor, 0, 1)

    shrink = 1.0 - RATE_MUON * WEIGHT_DECAY

    def weight_next(weight, direction):
        return weight * shrink - RATE_MUON * jnp.moveaxis(direction, 0, 1)

    return (
        loss_sum,
        loss_count,
        grad_norm,
        embed_new,
        embed_m_new,
        embed_v_new,
        weight_next(attn_qo, dir_qo),
        mom_next(attn_qo_mom, summed_qo),
        weight_next(attn_kv, dir_kv),
        mom_next(attn_kv_mom, summed_kv),
        weight_next(ffn, dir_ffn),
        mom_next(ffn_mom, summed_ffn),
        gains_new,
        gains_m_new,
        gains_v_new,
    )


def solution(mesh):
    by_pack = P("wide", None)
    table = P("narrow", "wide")
    layer = P("wide", None, "narrow")
    gain = P(None, ("wide", "narrow"))
    return jax.shard_map(
        per_device,
        mesh=mesh,
        in_specs=(by_pack,) * 4 + (P("wide"),) + (table,) * 3 + (layer,) * 6 + (gain,) * 3,
        out_specs=(P(),) * 3 + (table,) * 3 + (layer,) * 6 + (gain,) * 3,
        check_vma=False,
    )
```

```python
import functools

import jax
import jax.numpy as jnp
from jax import lax
from jax.experimental import pallas as pl
from jax.experimental.pallas import tpu as pltpu
from jax.sharding import PartitionSpec as P

HEADS = 16
HD = 128
KVH = 4
NS_STEPS = 5
STEP = 10


NORM_EPS = 1e-05
ROPE_BASE = 10000.0
EXIT_EARLY = 0.25
EXIT_LAST = 1.0
CLIP_NORM = 0.02
BETA_ONE = 0.9
BETA_TWO = 0.95
ADAM_EPS = 1e-08
RATE_ADAM = 0.02
RATE_GAIN = 0.3
RATE_MUON = 0.3
WEIGHT_DECAY = 0.1
MOMENTUM = 0.95
NEWTON_A = 3.4445
NEWTON_B = -4.775
NEWTON_C = 2.0315
MASKED = -1e30
LOW = jnp.bfloat16
FULL = jnp.float32
BOTH = ("wide", "narrow")
UNROLL = 16
VMEM_BYTES = 56 * 1024 * 1024


def dot(first, second, first_dim, second_dim):
    return lax.dot_general(
        first, second, (((first_dim,), (second_dim,)), ((), ())), preferred_element_type=FULL
    )


def norm_rows(values, gain_row):
    return (
        values * lax.rsqrt(jnp.mean(values * values, axis=-1, keepdims=True) + NORM_EPS) * gain_row
    )


def segments_at(lens, where_at):
    ends = jnp.cumsum(lens)
    return jnp.sum((where_at[:, None] >= ends[None, :]).astype(jnp.int32), axis=1)


def angles_at(lens, where_at):
    segment = segments_at(lens, where_at)
    starts = jnp.cumsum(lens) - lens
    member = segment[:, None] == jnp.arange(lens.shape[0], dtype=jnp.int32)[None, :]
    begin = jnp.sum(jnp.where(member, starts[None, :], 0), axis=1)
    offset_pos = (where_at - begin).astype(FULL)
    inverse = ROPE_BASE ** (-2.0 * jnp.arange(HD // 2, dtype=FULL) / HD)
    angle = offset_pos[:, None] * inverse[None, :]
    return (segment, jnp.cos(angle), jnp.sin(angle))


MESH = pl.DeviceIdType.MESH
ANY = pl.BlockSpec(memory_space=pl.ANY)
VMEM = pl.BlockSpec(memory_space=pltpu.VMEM)


def others(axis, count):
    me = lax.axis_index(axis)
    return [{axis: lax.rem(me + step, count)} for step in range(1, count)]


def push(source, target, send, receive, device):
    return pltpu.make_async_remote_copy(
        src_ref=source,
        dst_ref=target,
        send_sem=send,
        recv_sem=receive,
        device_id=device,
        device_id_type=MESH,
    )


def arrived(block, send, receive, device):
    push(block, block, send, receive, device).wait_recv()


def like(values):
    return jax.ShapeDtypeStruct(values.shape, values.dtype)


def struct(shape, dtype):
    return jax.ShapeDtypeStruct(shape, dtype)


def sems(*shape):
    return pltpu.SemaphoreType.DMA(shape)


class Task:
    def __init__(self, inputs, outputs, scratch, steps, place_in, place_out, axes):
        self.inputs, self.outputs, self.scratch, self.steps = inputs, outputs, scratch, steps
        self.place_in = [place_in] * len(inputs)
        self.place_out = [place_out] * len(outputs)
        self.axes = axes


def launch(tasks, ident, name):
    axes = sorted(set(axis for task in tasks for axis in task.axes))
    inputs = [a for task in tasks for a in task.inputs]
    outputs = [a for task in tasks for a in task.outputs]
    scratch = [a for task in tasks for a in task.scratch]

    def body(*refs):
        refs = list(refs)
        ins = refs[: len(inputs)]
        outs = refs[len(inputs) : len(inputs) + len(outputs)]
        extra = refs[len(inputs) + len(outputs) :]
        barrier = pltpu.get_barrier_semaphore()
        targets = [device for axis in axes for device in others(axis, lax.axis_size(axis))]
        for device in targets:
            pl.semaphore_signal(barrier, inc=1, device_id=device, device_id_type=MESH)
        pl.semaphore_wait(barrier, len(targets))
        live = []
        for task in tasks:
            counts = (len(task.inputs), len(task.outputs), len(task.scratch))
            live.append(task.steps(ins[: counts[0]], outs[: counts[1]], extra[: counts[2]]))
            ins, outs, extra = ins[counts[0] :], outs[counts[1] :], extra[counts[2] :]
        while live:
            live = [steps for steps in live if next(steps, 0) is None]

    size = sum(a.size * a.dtype.itemsize for a in list(inputs) + list(outputs))
    return pl.pallas_call(
        body,
        out_shape=outputs,
        in_specs=[place for task in tasks for place in task.place_in],
        out_specs=[place for task in tasks for place in task.place_out],
        scratch_shapes=scratch,
        compiler_params=pltpu.CompilerParams(
            collective_id=ident, has_side_effects=True, vmem_limit_bytes=VMEM_BYTES
        ),
        cost_estimate=pl.CostEstimate(flops=0, bytes_accessed=size // 8, transcendentals=0),
        name=name,
    )(*inputs)


def later(task, turns):
    begin = task.steps

    def steps(ins, outs, scratch):
        for turn in range(turns):
            yield
        yield from begin(ins, outs, scratch)

    task.steps = steps
    return task


def gather_wide(values, patience=1):
    count = lax.axis_size("wide")
    chips = count // 2

    def steps(ins, outs, scratch):
        (x_ref,), (out_ref,), (send, receive, local) = ins, outs, scratch
        me = lax.axis_index("wide")
        mate = me + 1 - 2 * lax.rem(me, 2)
        peers = [lax.rem(me + 2 * step, count) for step in range(1, chips)] + [mate]
        first = []
        for step, peer in enumerate(peers):
            copy = push(x_ref, out_ref.at[me], send.at[step], receive.at[me], {"wide": peer})
            copy.start()
            first.append(copy)
        keep = pltpu.make_async_copy(x_ref, out_ref.at[me], local)
        keep.start()
        for turn in range(patience):
            yield
        second = []
        for step in range(1, chips):
            source = lax.rem(me - 2 * step + count, count)
            block = out_ref.at[source]
            arrived(block, send.at[0], receive.at[source], {"wide": mate})
            copy = push(
                block, block, send.at[chips + step - 1], receive.at[source], {"wide": mate}
            )
            copy.start()
            second.append(copy)
        yield
        for step in range(chips):
            source = lax.rem(mate - 2 * step + count, count)
            arrived(out_ref.at[source], send.at[0], receive.at[source], {"wide": mate})
        for copy in first + second:
            copy.wait_send()
        keep.wait()

    shape = struct((count,) + values.shape, values.dtype)
    return Task(
        [values], [shape], [sems(count - 1), sems(count), sems()], steps, VMEM, VMEM, ["wide"]
    )


def trade(axis, values, source_of, target_of, shape, patience=2):
    count = lax.axis_size(axis)

    def steps(ins, outs, scratch):
        (x_ref,), (out_ref,), (send, receive, local) = ins, outs, scratch
        me = lax.axis_index(axis)
        copies = []
        for step in range(1, count):
            peer = lax.rem(me + step, count)
            copy = push(
                source_of(x_ref, peer),
                target_of(out_ref, me),
                send.at[step - 1],
                receive.at[me],
                {axis: peer},
            )
            copy.start()
            copies.append(copy)
        keep = pltpu.make_async_copy(source_of(x_ref, me), target_of(out_ref, me), local)
        keep.start()
        for turn in range(patience):
            yield
        for step in range(1, count):
            source = lax.rem(me - step + count, count)
            arrived(
                target_of(out_ref, source), send.at[0], receive.at[source], {axis: source}
            )
        for copy in copies:
            copy.wait_send()
        keep.wait()

    return Task(
        [values],
        [struct(shape, values.dtype)],
        [sems(count - 1), sems(count), sems()],
        steps,
        ANY,
        ANY,
        [axis],
    )


def block_at(ref, spot):
    return ref.at[spot]


def whole_at(ref, spot):
    return ref


def columns_of(size):
    def at(ref, spot):
        return ref.at[:, pl.ds(pl.multiple_of(spot * size, size), size)]

    return at


def turned(ref, spot):
    count = lax.axis_size("narrow")
    matrix = lax.rem(spot + count - lax.rem(lax.axis_index("wide"), 2), count)
    return ref.at[jnp.minimum(matrix, 3)]


def swap_turned(values, patience=2):
    shape = (lax.axis_size("narrow"),) + values.shape[1:]
    return trade("narrow", values, turned, block_at, shape, patience)


def product(lefts, rights, dim, order, pause=True, last=None):
    count, rows = len(order), lefts[0].shape[-1 if dim == 0 else -2]
    columns = rights[0].shape[1]
    block = min(512, columns)

    def steps(ins, outs, scratch):
        left_refs, right_refs = ins[: len(lefts)], ins[len(lefts) :]
        result_ref, square_ref = outs
        square_ref[...] = jnp.zeros_like(square_ref)

        def left_of(member):
            return left_refs[0][member] if lefts[0].ndim == 3 else left_refs[member][...]

        def fill(at, members, shift):
            def strip(part, carry):
                spot = pl.ds(pl.multiple_of(part * block, block), block)
                value = jnp.zeros((rows, block), FULL)
                for left, right in members:
                    value = value + dot(left_of(left), right_refs[right + shift][:, spot], dim, 0)
                result_ref[at, :, spot] = value.astype(LOW)
                square_ref[:, spot] = square_ref[:, spot] + jnp.sum(
                    value * value, axis=0, keepdims=True
                )
                return carry

            lax.fori_loop(0, columns // block, strip, 0)

        for at, members in enumerate(order):
            if last is None:
                fill(at, members, 0)
            else:
                pl.when(last())(functools.partial(fill, at, members, 1))
                pl.when(jnp.logical_not(last()))(functools.partial(fill, at, members, 0))
            if pause:
                yield

    return Task(
        list(lefts) + list(rights),
        [struct((count, rows, columns), LOW), struct((1, columns), FULL)],
        [],
        steps,
        VMEM,
        VMEM,
        [],
    )


def exit_stats(features, table, targets):
    rows, vocab = features.shape[0], table.shape[0]
    block = min(256, vocab)

    def steps(ins, outs, scratch):
        features_ref, table_ref, targets_ref = ins
        logits_ref, stats_ref = outs

        def strip(part):
            return pl.ds(pl.multiple_of(part * block, block), block)

        def over(function, start):
            return lax.fori_loop(0, vocab // block, function, start)

        def fill(part, peak):
            logits = dot(table_ref[strip(part), :], features_ref[...], 1, 1)
            logits_ref[strip(part), :] = logits
            return jnp.maximum(peak, jnp.max(logits, axis=0, keepdims=True))

        peak = over(fill, jnp.full((1, rows), MASKED, FULL))
        lines = lax.broadcasted_iota(jnp.int32, (block, rows), 0)

        def add(part, carry):
            total, picked = carry
            logits = logits_ref[strip(part), :]
            hit = lines + part * block == targets_ref[...]
            return (
                total + jnp.sum(jnp.exp(logits - peak), axis=0, keepdims=True),
                picked + jnp.sum(jnp.where(hit, logits, 0.0), axis=0, keepdims=True),
            )

        zero = jnp.zeros((1, rows), FULL)
        total, picked = over(add, (zero, zero))
        stats_ref[0:1, :] = peak
        stats_ref[1:2, :] = total
        stats_ref[2:3, :] = picked
        yield

    return Task(
        [features, table, targets],
        [struct((vocab, rows), FULL), struct((3, rows), FULL)],
        [],
        steps,
        VMEM,
        VMEM,
        [],
    )


def swap_owned(values, patience):
    count = lax.axis_size("narrow")

    def steps(ins, outs, scratch):
        (x_ref,), (out_ref,), (send, receive, local) = ins, outs, scratch
        me = lax.axis_index("narrow")
        turn = lax.rem(lax.axis_index("wide"), 2)

        def matrix_of(device):
            return lax.rem(device + count - turn, count)

        def copy_to(step):
            peer = lax.rem(me + step, count)
            return push(
                x_ref.at[jnp.minimum(matrix_of(peer), 2)],
                out_ref.at[me],
                send.at[step - 1],
                receive.at[me],
                {"narrow": peer},
            )

        def keep():
            return pltpu.make_async_copy(
                x_ref.at[jnp.minimum(matrix_of(me), 2)], out_ref.at[me], local
            )

        keep().start()
        for step in range(1, count):

            @pl.when(matrix_of(lax.rem(me + step, count)) < 3)
            def _():
                copy_to(step).start()

        for turn_at in range(patience):
            yield

        @pl.when(matrix_of(me) < 3)
        def _():
            for step in range(1, count):
                source = lax.rem(me - step + count, count)
                arrived(out_ref.at[source], send.at[0], receive.at[source], {"narrow": source})

        for step in range(1, count):

            @pl.when(matrix_of(lax.rem(me + step, count)) < 3)
            def _():
                copy_to(step).wait_send()

        keep().wait()

    return Task(
        [values],
        [struct((count,) + values.shape[1:], values.dtype)],
        [sems(count - 1), sems(count), sems()],
        steps,
        ANY,
        ANY,
        ["narrow"],
    )


def send_owner(values):
    count = lax.axis_size("narrow")

    def steps(ins, outs, scratch):
        (x_ref,), (out_ref,), (send, receive, local) = ins, outs, scratch
        me = lax.axis_index("narrow")
        owner = lax.rem(3 + lax.rem(lax.axis_index("wide"), 2), count)
        keep = pltpu.make_async_copy(x_ref, out_ref.at[me], local)
        keep.start()

        def to_owner():
            return push(x_ref, out_ref.at[me], send.at[0], receive.at[me], {"narrow": owner})

        @pl.when(me != owner)
        def _():
            to_owner().start()

        yield
        yield

        @pl.when(me != owner)
        def _():
            to_owner().wait_send()

        @pl.when(me == owner)
        def _():
            for step in range(1, count):
                source = lax.rem(owner + step, count)
                arrived(out_ref.at[source], send.at[0], receive.at[source], {"narrow": source})

        keep.wait()

    return Task(
        [values],
        [struct((count,) + values.shape, values.dtype)],
        [sems(1), sems(count), sems()],
        steps,
        ANY,
        ANY,
        ["narrow"],
    )


def swap_blocks(axis, values):
    return trade(axis, values, block_at, block_at, values.shape)


def gather_blocks(axis, values):
    shape = (lax.axis_size(axis),) + values.shape
    return trade(axis, values, whole_at, block_at, shape)


def split_columns(axis, values, patience=2):
    count = lax.axis_size(axis)
    rows, size = values.shape[0], values.shape[1] // count
    return trade(axis, values, columns_of(size), block_at, (count, rows, size), patience)


def join_columns(axis, values):
    count, rows, size = values.shape
    return trade(axis, values, block_at, columns_of(size), (rows, count * size))


def collect(count, parts_ref, slots, send, receive):
    me = lax.axis_index("narrow")
    copies = []
    for step in range(1, count):
        peer = lax.rem(me + step, count)
        copy = push(
            parts_ref.at[peer],
            slots.at[me],
            send.at[step - 1],
            receive.at[me],
            {"narrow": peer},
        )
        copy.start()
        copies.append(copy)
    return copies


def collected(count, parts_ref, slots, send, receive):
    me = lax.axis_index("narrow")
    total = parts_ref[me].astype(FULL)
    for step in range(1, count):
        source = lax.rem(me - step + count, count)
        arrived(slots.at[source], send.at[0], receive.at[source], {"narrow": source})
        total = total + slots[source].astype(FULL)
    return total


def share(count, low, all_ref, send, receive):
    me = lax.axis_index("narrow")
    all_ref[me] = low
    copies = []
    for step in range(1, count):
        peer = lax.rem(me + step, count)
        copy = push(
            all_ref.at[me], all_ref.at[me], send.at[step - 1], receive.at[me], {"narrow": peer}
        )
        copy.start()
        copies.append(copy)
    return copies


def shared(count, all_ref, send, receive):
    me = lax.axis_index("narrow")
    for step in range(1, count):
        source = lax.rem(me - step + count, count)
        arrived(all_ref.at[source], send.at[0], receive.at[source], {"narrow": source})


def narrow_sems(count):
    return [sems(count - 1), sems(count)]


def settle(partial, base, other, keep_row, gain_row):
    count = lax.axis_size("narrow")
    rows, width = base.shape

    def steps(ins, outs, scratch):
        parts_ref, base_ref, other_ref, keep_ref, gain_ref = ins
        own_ref, all_ref = outs
        slots, send, receive, send_all, receive_all = scratch
        copies = collect(count, parts_ref, slots, send, receive)
        yield
        total = collected(count, parts_ref, slots, send, receive)
        total = jnp.where(keep_ref[...] > 0, total + base_ref[...], other_ref[...])
        own_ref[...] = total
        low = norm_rows(total, gain_ref[...]).astype(LOW)
        copies = copies + share(count, low, all_ref, send_all, receive_all)
        yield
        shared(count, all_ref, send_all, receive_all)
        for copy in copies:
            copy.wait_send()

    return Task(
        [partial.reshape(count, rows, width), base, other, keep_row, gain_row],
        [struct((rows, width), FULL), struct((count, rows, width), LOW)],
        [pltpu.VMEM((count, rows, width), partial.dtype)]
        + narrow_sems(count)
        + narrow_sems(count),
        steps,
        VMEM,
        VMEM,
        ["narrow"],
    )


def settle_back(partial, values, add, keep_row, gain_row):
    count = lax.axis_size("narrow")
    rows, width = values.shape

    def steps(ins, outs, scratch):
        parts_ref, values_ref, add_ref, keep_ref, gain_ref = ins
        own_ref, gain_grad_ref, all_ref = outs
        slots, send, receive, send_all, receive_all = scratch
        copies = collect(count, parts_ref, slots, send, receive)
        yield
        grad = collected(count, parts_ref, slots, send, receive)
        held = values_ref[...]
        root = lax.rsqrt(jnp.mean(held * held, axis=-1, keepdims=True) + NORM_EPS)
        scaled = gain_ref[...] * grad
        inner = jnp.mean(held * scaled, axis=-1, keepdims=True)
        own = add_ref[...] + root * scaled - held * (root * root * root * inner)
        gain_grad_ref[...] = jnp.sum(held * root * grad, axis=0, keepdims=True)
        own_ref[...] = own
        low = (own * keep_ref[...]).astype(LOW)
        copies = copies + share(count, low, all_ref, send_all, receive_all)
        yield
        shared(count, all_ref, send_all, receive_all)
        for copy in copies:
            copy.wait_send()

    return Task(
        [partial.reshape(count, rows, width), values, add, keep_row, gain_row],
        [
            struct((rows, width), FULL),
            struct((1, width), FULL),
            struct((count, rows, width), LOW),
        ],
        [pltpu.VMEM((count, rows, width), partial.dtype)]
        + narrow_sems(count)
        + narrow_sems(count),
        steps,
        VMEM,
        VMEM,
        ["narrow"],
    )


def sum_narrow(partial):
    count = lax.axis_size("narrow")
    rows, width = partial.shape[0] // count, partial.shape[1]

    def steps(ins, outs, scratch):
        (parts_ref,), (own_ref,), (slots, send, receive) = ins, outs, scratch
        copies = collect(count, parts_ref, slots, send, receive)
        yield
        yield
        own_ref[...] = collected(count, parts_ref, slots, send, receive)
        for copy in copies:
            copy.wait_send()

    return Task(
        [partial.reshape(count, rows, width)],
        [struct((rows, width), FULL)],
        [pltpu.VMEM((count, rows, width), partial.dtype)] + narrow_sems(count),
        steps,
        VMEM,
        VMEM,
        ["narrow"],
    )


def fetch_rows(found, rows):
    deep, wide = lax.axis_size("narrow"), lax.axis_size("wide")
    columns = found.shape[2]

    def steps(ins, outs, scratch):
        (found_ref,), (out_ref,) = ins, outs
        rightward, leftward, final = scratch[:3]
        send_right, receive_right, send_left, receive_left = scratch[3:7]
        send_wide, receive_wide, local = scratch[7:]
        spot = lax.axis_index("narrow")
        me = lax.axis_index("wide")

        def right_copy(part, source):
            return push(
                source,
                rightward.at[part],
                send_right.at[part],
                receive_right.at[part],
                {"narrow": lax.rem(spot + 1, deep)},
            )

        def left_copy(part, source):
            return push(
                source,
                leftward.at[part],
                send_left.at[part],
                receive_left.at[part],
                {"narrow": lax.rem(spot + deep - 1, deep)},
            )

        for step in range(deep - 1):
            right, left = deep - 1 - step, step

            @pl.when((spot == 0) & (right > 0))
            def _():
                right_copy(right, found_ref.at[right]).start()

            @pl.when((spot == deep - 1) & (left < deep - 1))
            def _():
                left_copy(left, found_ref.at[left]).start()

        yield
        for step in range(deep - 1):
            right, left = deep - 1 - step, step

            def pass_right():
                right_copy(right, rightward.at[right]).wait_recv()
                rightward[right] = rightward[right] + found_ref[right]
                right_copy(right, rightward.at[right]).start()

            pl.when((spot > 0) & (right > spot) & (2 * spot < deep))(pass_right)

            @pl.when((spot < deep - 1) & (left < spot))
            def _():
                left_copy(left, leftward.at[left]).wait_recv()
                leftward[left] = leftward[left] + found_ref[left]
                left_copy(left, leftward.at[left]).start()

            pl.when((right > spot) & (2 * spot >= deep))(pass_right)

        final[...] = found_ref[spot]

        @pl.when(spot > 0)
        def _():
            right_copy(spot, rightward.at[spot]).wait_recv()
            final[...] = final[...] + rightward[spot]

        @pl.when(spot < deep - 1)
        def _():
            left_copy(spot, leftward.at[spot]).wait_recv()
            final[...] = final[...] + leftward[spot]

        def rows_for(device):
            return final.at[pl.ds(pl.multiple_of(device * rows, rows), rows)]

        def columns_from(device):
            return columns_of(columns)(out_ref, device)

        copies = []
        for step in range(1, wide):
            peer = lax.rem(me + step, wide)
            copy = push(
                rows_for(peer),
                columns_from(me),
                send_wide.at[step - 1],
                receive_wide.at[me],
                {"wide": peer},
            )
            copy.start()
            copies.append(copy)
        keep = pltpu.make_async_copy(rows_for(me), columns_from(me), local)
        keep.start()
        yield
        for step in range(1, wide):
            source = lax.rem(me - step + wide, wide)
            arrived(
                columns_from(source), send_wide.at[0], receive_wide.at[source], {"wide": source}
            )
        yield
        for copy in copies:
            copy.wait_send()
        keep.wait()
        for step in range(deep - 1):
            right, left = deep - 1 - step, step

            @pl.when(right > spot)
            def _():
                right_copy(right, found_ref.at[right]).wait_send()

            @pl.when(left < spot)
            def _():
                left_copy(left, found_ref.at[left]).wait_send()

    task = Task(
        [found],
        [struct((rows, wide * columns), found.dtype)],
        [pltpu.VMEM(found.shape, found.dtype)] * 2
        + [pltpu.VMEM(found.shape[1:], found.dtype)]
        + [sems(deep)] * 4
        + [sems(wide - 1), sems(wide), sems()],
        steps,
        VMEM,
        ANY,
        ["narrow", "wide"],
    )
    return task


def return_rows(rows):
    deep, wide = lax.axis_size("narrow"), lax.axis_size("wide")
    count, width = rows.shape
    columns = width // wide

    def steps(ins, outs, scratch):
        (rows_ref,), (out_ref,) = ins, outs
        send_right, send_left, receive_deep, send_wide, receive_wide, local = scratch
        spot = lax.axis_index("narrow")
        me = lax.axis_index("wide")
        part_of = functools.partial(columns_of(columns), rows_ref)

        def landing(device):
            return out_ref.at[spot, pl.ds(pl.multiple_of(device * count, count), count)]

        copies = []
        for step in range(1, wide):
            peer = lax.rem(me + step, wide)
            copy = push(
                part_of(peer),
                landing(me),
                send_wide.at[step - 1],
                receive_wide.at[me],
                {"wide": peer},
            )
            copy.start()
            copies.append(copy)
        keep = pltpu.make_async_copy(part_of(me), landing(me), local)
        keep.start()
        yield
        for step in range(1, wide):
            source = lax.rem(me - step + wide, wide)
            arrived(landing(source), send_wide.at[0], receive_wide.at[source], {"wide": source})
        keep.wait()

        def right_copy(part):
            return push(
                out_ref.at[part],
                out_ref.at[part],
                send_right.at[part],
                receive_deep.at[part],
                {"narrow": lax.rem(spot + 1, deep)},
            )

        def left_copy(part):
            return push(
                out_ref.at[part],
                out_ref.at[part],
                send_left.at[part],
                receive_deep.at[part],
                {"narrow": lax.rem(spot + deep - 1, deep)},
            )

        @pl.when(spot < deep - 1)
        def _():
            right_copy(spot).start()

        @pl.when(spot > 0)
        def _():
            left_copy(spot).start()

        for step in range(1, deep):
            yield

            @pl.when(spot >= step)
            def _():
                right_copy(spot - step).wait_recv()

                @pl.when(spot < deep - 1)
                def _():
                    right_copy(spot - step).start()

            @pl.when(spot + step < deep)
            def _():
                left_copy(spot + step).wait_recv()

                @pl.when(spot > 0)
                def _():
                    left_copy(spot + step).start()

        for part in range(deep):

            @pl.when((part <= spot) & (spot < deep - 1))
            def _():
                right_copy(part).wait_send()

            @pl.when((part >= spot) & (spot > 0))
            def _():
                left_copy(part).wait_send()

        for copy in copies:
            copy.wait_send()

    return Task(
        [rows],
        [struct((deep, wide * count, columns), rows.dtype)],
        [sems(deep)] * 3 + [sems(wide - 1), sems(wide), sems()],
        steps,
        ANY,
        ANY,
        ["narrow", "wide"],
    )


def sum_wide(partial):
    count = lax.axis_size("wide")
    chips = count // 2
    rows, width = partial.shape[0] // count, partial.shape[1]

    def steps(ins, outs, scratch):
        (parts_ref,), (out_ref,) = ins, outs
        from_mate, paired, slots, send_mate, receive_mate, send, receive = scratch
        me = lax.axis_index("wide")
        side = lax.rem(me, 2)
        mate = me + 1 - 2 * side
        my_chip = me // 2
        mate_copies = []
        for step in range(chips):
            chip = lax.rem(my_chip + 1 + step, chips)
            copy = push(
                parts_ref.at[2 * chip + 1 - side],
                from_mate.at[chip],
                send_mate.at[step],
                receive_mate.at[chip],
                {"wide": mate},
            )
            copy.start()
            mate_copies.append(copy)
        yield
        copies = []
        for step in range(chips):
            chip = lax.rem(my_chip + 1 + step, chips)
            arrived(from_mate.at[chip], send_mate.at[0], receive_mate.at[chip], {"wide": mate})
            both = parts_ref[2 * chip + side].astype(FULL) + from_mate[chip].astype(FULL)
            if step < chips - 1:
                paired[chip] = both.astype(LOW)
                copy = push(
                    paired.at[chip],
                    slots.at[my_chip],
                    send.at[step],
                    receive.at[my_chip],
                    {"wide": 2 * chip + side},
                )
                copy.start()
                copies.append(copy)
            else:
                out_ref[...] = both
        yield
        for step in range(1, chips):
            chip = lax.rem(my_chip - step + chips, chips)
            arrived(slots.at[chip], send.at[0], receive.at[chip], {"wide": 2 * chip + side})
            out_ref[...] = out_ref[...] + slots[chip].astype(FULL)
        for copy in mate_copies + copies:
            copy.wait_send()

    return Task(
        [partial.reshape(count, rows, width)],
        [struct((rows, width), FULL)],
        [pltpu.VMEM((chips, rows, width), LOW)] * 3
        + [sems(chips), sems(chips), sems(max(chips - 1, 1)), sems(chips)],
        steps,
        VMEM,
        VMEM,
        ["wide"],
    )


def merge_stats(first, second):
    peak = jnp.maximum(first[0:1], second[0:1])
    total = first[1:2] * jnp.exp(first[0:1] - peak) + second[1:2] * jnp.exp(second[0:1] - peak)
    return jnp.concatenate([peak, total, first[2:3] + second[2:3]], axis=0)


def add_two(first, second):
    return first + second


def combine(values, join):
    deep, wide = lax.axis_size("narrow"), lax.axis_size("wide")

    def steps(ins, outs, scratch):
        (x_ref,), (out_ref,) = ins, outs
        wide_slots, deep_slots, send_wide, receive_wide, send_deep, receive_deep = scratch

        def start(axis, count, slots, value, send, receive):
            me = lax.axis_index(axis)
            slots[me] = value
            copies = []
            for step in range(1, count):
                peer = lax.rem(me + step, count)
                copy = push(
                    slots.at[me], slots.at[me], send.at[step - 1], receive.at[me], {axis: peer}
                )
                copy.start()
                copies.append(copy)
            return copies

        def finish(axis, count, slots, send, receive):
            me = lax.axis_index(axis)
            for step in range(1, count):
                source = lax.rem(me - step + count, count)
                arrived(slots.at[source], send.at[0], receive.at[source], {axis: source})
            total = slots[0]
            for source in range(1, count):
                total = join(total, slots[source])
            return total

        first = start("wide", wide, wide_slots, x_ref[...], send_wide, receive_wide)
        yield
        total = finish("wide", wide, wide_slots, send_wide, receive_wide)
        second = start("narrow", deep, deep_slots, total, send_deep, receive_deep)
        yield
        out_ref[...] = finish("narrow", deep, deep_slots, send_deep, receive_deep)
        for copy in first + second:
            copy.wait_send()

    return Task(
        [values],
        [like(values)],
        [
            pltpu.VMEM((wide,) + values.shape, values.dtype),
            pltpu.VMEM((deep,) + values.shape, values.dtype),
            sems(wide - 1),
            sems(wide),
            sems(deep - 1),
            sems(deep),
        ],
        steps,
        VMEM,
        VMEM,
        ["narrow", "wide"],
    )


def gather_both(values):
    deep, wide = lax.axis_size("narrow"), lax.axis_size("wide")

    def steps(ins, outs, scratch):
        (x_ref,), (out_ref,) = ins, outs
        send_wide, receive_wide, send_deep, receive_deep = scratch
        me = lax.axis_index("wide")
        spot = lax.axis_index("narrow")
        out_ref[spot, me] = x_ref[...]
        copies = []
        for step in range(1, wide):
            peer = lax.rem(me + step, wide)
            block = out_ref.at[spot, me]
            copy = push(block, block, send_wide.at[step - 1], receive_wide.at[me], {"wide": peer})
            copy.start()
            copies.append(copy)
        yield
        for step in range(1, wide):
            source = lax.rem(me - step + wide, wide)
            block = out_ref.at[spot, source]
            arrived(block, send_wide.at[0], receive_wide.at[source], {"wide": source})
        for step in range(1, deep):
            peer = lax.rem(spot + step, deep)
            block = out_ref.at[spot]
            copy = push(
                block, block, send_deep.at[step - 1], receive_deep.at[spot], {"narrow": peer}
            )
            copy.start()
            copies.append(copy)
        yield
        for step in range(1, deep):
            source = lax.rem(spot - step + deep, deep)
            block = out_ref.at[source]
            arrived(block, send_deep.at[0], receive_deep.at[source], {"narrow": source})
        for copy in copies:
            copy.wait_send()

    return Task(
        [values],
        [struct((deep, wide) + values.shape, values.dtype)],
        [sems(wide - 1), sems(wide), sems(deep - 1), sems(deep)],
        steps,
        VMEM,
        VMEM,
        ["narrow", "wide"],
    )


def turn_heads(values, cosine, sine):
    half = values.shape[1] // 2
    swapped = jnp.concatenate([values[:, half:], values[:, :half]], axis=1)
    return values * cosine + swapped * sine


def wide_angles(cosine, sine):
    return jnp.concatenate([cosine, cosine], axis=1), jnp.concatenate([-sine, sine], axis=1)


def local_call(body, inputs, specs, outputs, flops, name):
    return pl.pallas_call(
        body,
        grid=(1,),
        in_specs=specs,
        out_specs=[
            pl.BlockSpec(a.shape, lambda step, rank=len(a.shape): (0,) * rank) for a in outputs
        ],
        out_shape=outputs,
        compiler_params=pltpu.CompilerParams(vmem_limit_bytes=VMEM_BYTES),
        cost_estimate=pl.CostEstimate(flops=flops, bytes_accessed=8 << 20, transcendentals=0),
        name=name,
    )(*inputs)


def entire(values):
    return pl.BlockSpec(values.shape, lambda step: (0,) * values.ndim)


def column_block(values, size, index):
    return pl.BlockSpec((values.shape[0], size), lambda step: (0, index))


def heads_body(groups, rep, rows_ref, gain_ref, kv_ref, cos_ref, sin_ref, out_ref, normed_ref):
    count, _, _, tok_rows, head = out_ref.shape
    size = kv_ref.shape[1] // (2 * count)
    per_head = head // size
    rows = rows_ref[0:tok_rows, :].astype(FULL)
    normed = norm_rows(rows, gain_ref[...]).astype(LOW)
    normed_ref[...] = normed
    both = dot(normed, kv_ref[...], 1, 0)

    def head_of(kind, index):
        pieces = [
            both[:, (2 * part + kind) * size : (2 * part + kind + 1) * size]
            for part in range(index * per_head, (index + 1) * per_head)
        ]
        return pieces[0] if per_head == 1 else jnp.concatenate(pieces, axis=1)

    for owner in range(count):
        for group in range(groups):
            index = (owner * groups + group) // rep
            keys = turn_heads(head_of(0, index), cos_ref[...], sin_ref[...])
            out_ref[owner, group, 0] = keys.astype(LOW)
            out_ref[owner, group, 1] = head_of(1, index).astype(LOW)


def make_heads(rows_low, gain_row, proj, cosine, sine, groups, rep):
    count = lax.axis_size("narrow")
    tok_rows, head = cosine.shape
    width = rows_low.shape[1]
    size = 2 * KVH * HD
    return local_call(
        functools.partial(heads_body, groups, rep),
        [rows_low, gain_row, proj, cosine, sine],
        [entire(rows_low), entire(gain_row), column_block(proj, size, 0)]
        + [entire(cosine), entire(sine)],
        [struct((count, groups, 2, tok_rows, head), LOW), struct((tok_rows, width), LOW)],
        2 * tok_rows * width * size,
        "make_heads",
    )


def attend_body(
    start_ref,
    gains_ref,
    q_ref,
    o_ref,
    kv_ref,
    cos_ref,
    sin_ref,
    seg_ref,
    seg_all_ref,
    pick_ref,
    queries_ref,
    probs_ref,
    mixed_ref,
    part_ref,
    normed_ref,
    early_ref,
):
    count, groups, _, tok_rows, head = kv_ref.shape
    heads_own = probs_ref.shape[0]
    start = start_ref[...].astype(FULL)
    root = lax.rsqrt(jnp.mean(start * start, axis=-1, keepdims=True) + NORM_EPS)
    normed = (start * root * gains_ref[0:1, :]).astype(LOW)
    normed_ref[...] = normed
    early_ref[...] = (start * root * gains_ref[2:3, :]).astype(LOW)
    queries = dot(normed, q_ref[...], 1, 0)
    spots = lax.broadcasted_iota(jnp.int32, (1, count * tok_rows), 1)
    allowed = (seg_ref[...] == seg_all_ref[...]) & (pick_ref[...] >= spots)
    for group in range(groups):
        keys = jnp.concatenate([kv_ref[part, group, 0] for part in range(count)], axis=0)
        values = jnp.concatenate([kv_ref[part, group, 1] for part in range(count)], axis=0)
        for member in range(heads_own // groups):
            at = group * (heads_own // groups) + member
            spot = slice(at * head, (at + 1) * head)
            query = turn_heads(queries[:, spot], cos_ref[...], sin_ref[...]).astype(LOW)
            queries_ref[:, spot] = query
            scores = jnp.where(allowed, dot(query, keys, 1, 1) * head ** (-0.5), MASKED)
            shifted = jnp.exp(scores - jnp.max(scores, axis=-1, keepdims=True))
            probs = shifted / jnp.sum(shifted, axis=-1, keepdims=True)
            probs_ref[at] = probs
            mixed_ref[:, spot] = dot(probs.astype(LOW), values, 1, 0).astype(LOW)
    part_ref[...] = dot(mixed_ref[...], o_ref[...], 1, 1).astype(LOW)


def attend(start_low, gains, proj, own_head, cosine, sine, seg, seg_all, picks):
    count, groups, _, tok_rows, head = own_head.shape
    sel, width = start_low.shape
    heads_own = HEADS // count
    size = heads_own * head
    first = 2 * KVH * HD // size
    seq_len = count * tok_rows
    return local_call(
        attend_body,
        [start_low, gains, proj, proj, own_head, cosine, sine, seg, seg_all, picks],
        [
            entire(start_low),
            entire(gains),
            column_block(proj, size, first),
            column_block(proj, size, first + 1),
        ]
        + [entire(a) for a in (own_head, cosine, sine, seg, seg_all, picks)],
        [
            struct((sel, size), LOW),
            struct((heads_own, sel, seq_len), FULL),
            struct((sel, size), LOW),
            struct((sel, width), LOW),
            struct((sel, width), LOW),
            struct((sel, width), LOW),
        ],
        4 * sel * size * (width + seq_len),
        "attend",
    )


def attend_back_body(
    grad_ref,
    q_ref,
    o_ref,
    kv_ref,
    queries_ref,
    probs_ref,
    cos_ref,
    sin_ref,
    cos_all_ref,
    sin_all_ref,
    start_ref,
    gains_ref,
    early_ref,
    out_ref,
    grad_q_ref,
    part_ref,
    attn_gain_ref,
    early_gain_ref,
):
    count, groups, _, tok_rows, head = kv_ref.shape
    heads_own = probs_ref.shape[0]
    scale = head ** (-0.5)
    grad_mixed = dot(grad_ref[...], o_ref[...], 1, 0).astype(LOW)
    for group in range(groups):
        keys = jnp.concatenate([kv_ref[part, group, 0] for part in range(count)], axis=0)
        values = jnp.concatenate([kv_ref[part, group, 1] for part in range(count)], axis=0)
        grad_keys = jnp.zeros(keys.shape, FULL)
        grad_values = jnp.zeros(keys.shape, FULL)
        for member in range(heads_own // groups):
            at = group * (heads_own // groups) + member
            spot = slice(at * head, (at + 1) * head)
            probs = probs_ref[at]
            grad_probs = dot(grad_mixed[:, spot], values, 1, 1)
            inner = jnp.sum(probs * grad_probs, axis=-1, keepdims=True)
            grad_scores = (probs * (grad_probs - inner)).astype(LOW)
            grad_query = dot(grad_scores, keys, 1, 0) * scale
            grad_q_ref[:, spot] = turn_heads(grad_query, cos_ref[...], -sin_ref[...]).astype(LOW)
            grad_keys = grad_keys + dot(grad_scores, queries_ref[:, spot], 0, 0)
            grad_values = grad_values + dot(probs.astype(LOW), grad_mixed[:, spot], 0, 0)
        grad_keys = turn_heads(grad_keys * scale, cos_all_ref[...], -sin_all_ref[...])
        for part in range(count):
            rows = slice(part * tok_rows, (part + 1) * tok_rows)
            out_ref[part, group, 0] = grad_keys[rows].astype(LOW)
            out_ref[part, group, 1] = grad_values[rows].astype(LOW)
    pick = dot(grad_q_ref[...], q_ref[...], 1, 1)
    early = early_ref[...].astype(FULL)
    start = start_ref[...].astype(FULL)
    start = start * lax.rsqrt(jnp.mean(start * start, axis=-1, keepdims=True) + NORM_EPS)
    attn_gain_ref[...] = jnp.sum(start * pick, axis=0, keepdims=True)
    early_gain_ref[...] = jnp.sum(start * early, axis=0, keepdims=True)
    part_ref[...] = (gains_ref[0:1, :] * pick + gains_ref[2:3, :] * early).astype(LOW)


def attend_back(
    grad,
    proj,
    own_head,
    queries,
    probs,
    cosine,
    sine,
    cosine_all,
    sine_all,
    start_low,
    gains,
    early,
):
    count, groups, _, tok_rows, head = own_head.shape
    sel, width = grad.shape
    size = queries.shape[1]
    first = 2 * KVH * HD // size
    return local_call(
        attend_back_body,
        [grad, proj, proj, own_head, queries, probs, cosine, sine, cosine_all, sine_all]
        + [start_low, gains, early],
        [entire(grad), column_block(proj, size, first), column_block(proj, size, first + 1)]
        + [
            entire(a)
            for a in (own_head, queries, probs, cosine, sine, cosine_all, sine_all)
            + (start_low, gains, early)
        ],
        [struct(own_head.shape, LOW), struct((sel, size), LOW), struct((sel, width), LOW)]
        + [struct((1, width), FULL)] * 2,
        8 * sel * size * width,
        "attend_back",
    )


def norm_back_rows(values, gain_row, grad):
    root = lax.rsqrt(jnp.mean(values * values, axis=-1, keepdims=True) + NORM_EPS)
    scaled = gain_row * grad
    inner = jnp.mean(values * scaled, axis=-1, keepdims=True)
    result = root * scaled - values * (root * root * root * inner)
    return result, jnp.sum(values * root * grad, axis=0, keepdims=True)


def rows_back_body(
    rep,
    rows_ref,
    gains_ref,
    kv_ref,
    heads_ref,
    pick_ref,
    base_ref,
    out_ref,
    gain_grad_ref,
    grad_kv_ref,
):
    count, groups, _, tok_rows, head = heads_ref.shape
    size = kv_ref.shape[1] // (2 * count)
    per_head = head // size
    for index in range(KVH):
        for kind in range(2):
            copies = [
                heads_ref[at // groups, at % groups, kind]
                for at in range(index * rep, (index + 1) * rep)
            ]
            total = copies[0]
            if rep > 1:
                total = sum(copy.astype(FULL) for copy in copies).astype(LOW)
            for piece in range(per_head):
                lane = (2 * (index * per_head + piece) + kind) * size
                grad_kv_ref[:, lane : lane + size] = total[:, piece * size : (piece + 1) * size]
    values = rows_ref[...].astype(FULL)
    own = values[tok_rows:]
    tok_part, tok_gain = norm_back_rows(
        values[:tok_rows], gains_ref[0:1, :], dot(grad_kv_ref[...], kv_ref[...], 1, 1)
    )
    pick_part, _ = norm_back_rows(own, 1.0, pick_ref[...])
    gain_grad_ref[...] = tok_gain
    out_ref[0:tok_rows, :] = tok_part.astype(LOW)
    out_ref[tok_rows:, :] = (pick_part + base_ref[...]).astype(LOW)


def rows_back(rows_low, gains, proj, heads, grad_pick, base, rep):
    tok_rows = heads.shape[3]
    width = rows_low.shape[1]
    size = 2 * KVH * HD
    return local_call(
        functools.partial(rows_back_body, rep),
        [rows_low, gains, proj, heads, grad_pick, base],
        [entire(rows_low), entire(gains), column_block(proj, size, 0)]
        + [entire(a) for a in (heads, grad_pick, base)],
        [
            struct(rows_low.shape, LOW),
            struct((1, width), FULL),
            struct((tok_rows, size), LOW),
        ],
        2 * tok_rows * width * size,
        "rows_back",
    )


def assemble_body(out_columns, *refs):
    pieces, out_ref = refs[:-1], refs[-1]
    count = len(pieces)
    me = lax.axis_index("narrow")
    for step, piece in enumerate(pieces):
        source = lax.rem(me - step + count, count)
        spot = pl.ds(pl.multiple_of(source * out_columns, out_columns), out_columns)
        out_ref[:, spot] = piece[...]


def assemble(pieces):
    rows, columns = pieces[0].shape
    outputs = [struct((rows, columns * len(pieces)), pieces[0].dtype)]
    return local_call(
        functools.partial(assemble_body, columns),
        list(pieces),
        [entire(piece) for piece in pieces],
        outputs,
        0,
        "assemble",
    )[0]


def feed_body(inner_ref, weight_ref, gate_ref, up_ref, hidden_ref, out_ref, total):
    part = pl.program_id(0)
    inner = inner_ref[...]
    gate = dot(inner, weight_ref[0, 0], 1, 1)
    up = dot(inner, weight_ref[0, 1], 1, 1)
    hidden = (jax.nn.silu(gate) * up).astype(LOW)
    gate_ref[0] = gate
    up_ref[0] = up
    hidden_ref[0] = hidden
    product = dot(hidden, weight_ref[0, 2], 1, 0)

    @pl.when(part == 0)
    def _():
        total[...] = product

    @pl.when(part > 0)
    def _():
        total[...] = total[...] + product

    @pl.when(part == pl.num_programs(0) - 1)
    def _():
        out_ref[...] = total[...].astype(LOW)


def feed(inner, weight):
    parts, _, size, width = weight.shape
    sel = inner.shape[0]
    same = pl.BlockSpec((sel, width), lambda part: (0, 0))
    slab = pl.BlockSpec((1, sel, size), lambda part: (part, 0, 0))
    return pl.pallas_call(
        feed_body,
        grid=(parts,),
        in_specs=[same, pl.BlockSpec((1, 3, size, width), lambda part: (part, 0, 0, 0))],
        out_specs=[slab, slab, slab, same],
        out_shape=[
            struct((parts, sel, size), FULL),
            struct((parts, sel, size), FULL),
            struct((parts, sel, size), LOW),
            struct((sel, width), LOW),
        ],
        scratch_shapes=[pltpu.VMEM((sel, width), FULL)],
        compiler_params=pltpu.CompilerParams(vmem_limit_bytes=VMEM_BYTES),
        cost_estimate=pl.CostEstimate(
            flops=6 * sel * parts * size * width,
            bytes_accessed=weight.size * 2,
            transcendentals=0,
        ),
        name="feed",
    )(inner, weight)


def feed_back_body(grad_ref, weight_ref, gate_ref, up_ref, hidden_ref, acts_ref, out_ref, total):
    part = pl.program_id(0)
    grad_hidden = dot(grad_ref[...], weight_ref[0, 2], 1, 1)
    gate = gate_ref[0]
    sigma = jax.nn.sigmoid(gate)
    grad_gate = (grad_hidden * up_ref[0] * sigma * (1.0 + gate * (1.0 - sigma))).astype(LOW)
    grad_up = (grad_hidden * gate * sigma).astype(LOW)
    acts_ref[0, 0] = grad_gate
    acts_ref[0, 1] = grad_up
    acts_ref[0, 2] = hidden_ref[0]
    product = dot(grad_gate, weight_ref[0, 0], 1, 0) + dot(grad_up, weight_ref[0, 1], 1, 0)

    @pl.when(part == 0)
    def _():
        total[...] = product

    @pl.when(part > 0)
    def _():
        total[...] = total[...] + product

    @pl.when(part == pl.num_programs(0) - 1)
    def _():
        out_ref[...] = total[...].astype(LOW)


def feed_back(grad, weight, gate, up, hidden):
    parts, _, size, width = weight.shape
    sel = grad.shape[0]
    same = pl.BlockSpec((sel, width), lambda part: (0, 0))
    slab = pl.BlockSpec((1, sel, size), lambda part: (part, 0, 0))
    return pl.pallas_call(
        feed_back_body,
        grid=(parts,),
        in_specs=[same, pl.BlockSpec((1, 3, size, width), lambda part: (part, 0, 0, 0))]
        + [slab] * 3,
        out_specs=[pl.BlockSpec((1, 3, sel, size), lambda part: (part, 0, 0, 0)), same],
        out_shape=[struct((parts, 3, sel, size), LOW), struct((sel, width), LOW)],
        scratch_shapes=[pltpu.VMEM((sel, width), FULL)],
        compiler_params=pltpu.CompilerParams(vmem_limit_bytes=VMEM_BYTES),
        cost_estimate=pl.CostEstimate(
            flops=6 * sel * parts * size * width,
            bytes_accessed=weight.size * 2,
            transcendentals=0,
        ),
        name="feed_back",
    )(grad, weight, gate, up, hidden)


def newton_steps(problems):
    rows, width = problems[0][0].shape
    block = min(1024, width)
    eye = lax.broadcasted_iota(jnp.int32, (rows, rows), 0) == lax.broadcasted_iota(
        jnp.int32, (rows, rows), 1
    )

    def strip(part):
        return pl.ds(pl.multiple_of(part * block, block), block)

    def over(function, start):
        return lax.fori_loop(0, width // block, function, start)

    def add_squares(part, totals):
        values = [current[:, strip(part)] for current, low, gram, rest in problems]
        return [total + jnp.sum(value * value) for total, value in zip(totals, values)]

    totals = over(add_squares, [jnp.float32(0.0)] * len(problems))
    scales = [1.0 / (jnp.sqrt(total) + 1e-07) for total in totals]

    def begin(part, carry):
        for scale, (current, low, gram, rest) in zip(scales, problems):
            values = current[:, strip(part)] * scale
            current[:, strip(part)] = values
            low[:, strip(part)] = values.astype(LOW)
        return carry

    over(begin, 0)

    def iteration(turn, carry):
        for current, low, gram, rest in problems:
            gram[...] = jnp.zeros_like(gram)

        def add_gram(part, carry):
            for current, low, gram, rest in problems:
                values = low[:, strip(part)]
                gram[...] = gram[...] + dot(values, values, 1, 1)
            return carry

        over(add_gram, 0)
        seconds = []
        for current, low, gram, rest in problems:
            whole = gram[...]
            middle = jnp.sum(jnp.where(eye, whole, 0.0)) / rows
            rest[...] = (whole - jnp.where(eye, middle, 0.0)).astype(LOW)
            square = dot(rest[...], rest[...], 1, 0)
            whole = gram[...]
            centred = whole - jnp.where(eye, middle, 0.0)
            square = square + 2.0 * middle * centred + jnp.where(eye, middle * middle, 0.0)
            whole = NEWTON_B * whole + NEWTON_C * square
            second = jnp.sum(jnp.where(eye, whole, 0.0)) / rows
            rest[...] = (whole - jnp.where(eye, second, 0.0)).astype(LOW)
            seconds.append(second)

        def apply(part, carry):
            for second, (current, low, gram, rest) in zip(seconds, problems):
                values = (NEWTON_A + second) * current[:, strip(part)] + dot(
                    rest[...], low[:, strip(part)], 1, 0
                )
                current[:, strip(part)] = values
                low[:, strip(part)] = values.astype(LOW)
            return carry

        over(apply, 0)
        return carry

    lax.fori_loop(0, NS_STEPS, iteration, 0)


def newton_scratch(rows, width):
    return [
        pltpu.VMEM((rows, width), FULL),
        pltpu.VMEM((rows, width), LOW),
        pltpu.VMEM((rows, rows), FULL),
        pltpu.VMEM((rows, rows), LOW),
    ]


def newton_cost(count, rows, width):
    return pl.CostEstimate(
        flops=NS_STEPS * count * (4 * rows * rows * width + 2 * rows * rows * rows),
        bytes_accessed=6 * count * rows * width,
        transcendentals=0,
    )


def newton_body(factor_ref, mom_ref, grad_ref, out_ref, *problem):
    current, low = problem[:2]
    parts, rows, columns = mom_ref.shape
    factor = factor_ref[0]
    size = grad_ref.shape[1]
    for part in range(parts):
        spot = slice(part * columns, (part + 1) * columns)
        for source in range(parts):
            here = slice(source * size, (source + 1) * size)
            current[here, spot] = MOMENTUM * mom_ref[part, here, :].astype(
                FULL
            ) + factor * grad_ref[source, :, spot].astype(FULL)
    newton_steps([problem])
    for part in range(parts):
        out_ref[part] = low[:, part * columns : (part + 1) * columns]


def newton_small_body(rows, factor_ref, mom_ref, grad_ref, kv_ref, out_ref, *scratch):
    problems = [scratch[4 * at : 4 * at + 4] for at in range(4)]
    parts, _, columns = mom_ref.shape
    kv_columns = kv_ref.shape[2]
    half = rows // 2
    factor = factor_ref[0]
    for part in range(parts):
        spot = slice(part * columns, (part + 1) * columns)
        for member in range(2):
            current = problems[member][0]
            here = slice(member * rows, (member + 1) * rows)
            mom, grad = mom_ref[part, here, :], grad_ref[part, here, :]
            current[:, spot] = MOMENTUM * mom.astype(FULL) + factor * grad.astype(FULL)
        spot = slice(part * kv_columns, (part + 1) * kv_columns)
        for member in range(2):
            current = problems[2 + member][0]
            piece = kv_ref[part, member * rows : (member + 1) * rows, :].astype(FULL)
            for side in range(2):
                lane = (2 * member + side) * kv_columns
                mom = mom_ref[part, 2 * rows : 2 * rows + half, lane : lane + kv_columns]
                here = slice(side * half, (side + 1) * half)
                current[here, spot] = MOMENTUM * mom.astype(FULL) + factor * piece[here]
    newton_steps(problems[:2])
    newton_steps(problems[2:])
    out_ref[...] = jnp.zeros_like(out_ref)
    for part in range(parts):
        for member in range(2):
            out_ref[part, member * rows : (member + 1) * rows, :] = problems[member][1][
                :, part * columns : (part + 1) * columns
            ]
            low = problems[2 + member][1]
            for side in range(2):
                lane = (2 * member + side) * kv_columns
                out_ref[part, 2 * rows : 2 * rows + half, lane : lane + kv_columns] = low[
                    side * half : (side + 1) * half,
                    part * kv_columns : (part + 1) * kv_columns,
                ]


def newton_any_body(rows, factor_ref, mom_ref, grad_ref, qo_ref, kv_ref, out_ref, *scratch):
    parts = mom_ref.shape[0]
    owner = lax.rem(3 + lax.rem(lax.axis_index("wide"), 2), parts)
    small = lax.axis_index("narrow") == owner

    @pl.when(small)
    def _():
        newton_small_body(rows, factor_ref, mom_ref, qo_ref, kv_ref, out_ref, *scratch[4:])

    @pl.when(jnp.logical_not(small))
    def _():
        newton_body(factor_ref, mom_ref, grad_ref, out_ref, *scratch[:4])


def newton(factor, mom, grad, qo_grad, kv_grad):
    parts, slot_rows, columns = mom.shape
    width = parts * columns
    rows = kv_grad.shape[1] // 2
    kv_width = parts * kv_grad.shape[2]
    return pl.pallas_call(
        functools.partial(newton_any_body, rows),
        in_specs=[pl.BlockSpec(memory_space=pltpu.SMEM)] + [VMEM] * 4,
        out_specs=VMEM,
        out_shape=struct(mom.shape, LOW),
        scratch_shapes=newton_scratch(slot_rows, width)
        + newton_scratch(rows, width) * 2
        + newton_scratch(rows, kv_width) * 2,
        compiler_params=pltpu.CompilerParams(vmem_limit_bytes=VMEM_BYTES),
        cost_estimate=newton_cost(1, slot_rows, width),
        name="newton",
    )(factor.reshape(1), mom, grad, qo_grad, kv_grad)


def lookup_body(ids_ref, turn_ref, table_ref, out_ref, low_ref, list_ref, held, rows, sem):
    vocab = table_ref.shape[0]
    count = out_ref.shape[0]
    load = pltpu.make_async_copy(table_ref, held, sem)
    load.start()
    rows[...] = jnp.zeros_like(rows)

    found = turn_ref[count]

    def note(group, carry):
        for member in range(UNROLL):
            at = group * UNROLL + member
            list_ref[turn_ref[at]] = at
        return carry

    lax.fori_loop(0, count // UNROLL, note, 0)
    for member in range(UNROLL):
        list_ref[found + member] = count
    list_ref[count + UNROLL] = found
    load.wait()

    def step(group, carry):
        for member in range(UNROLL):
            at = list_ref[group * UNROLL + member]
            spot = jnp.minimum(ids_ref[jnp.minimum(at, count - 1)], vocab - 1)
            rows[pl.ds(at, 1), :] = held[pl.ds(spot, 1), :]
        return carry

    lax.fori_loop(0, (found + UNROLL - 1) // UNROLL, step, 0)
    out_ref[...] = rows[pl.ds(0, count), :].astype(LOW)
    low_ref[...] = held[...].astype(LOW)


def lookup(table, ids):
    vocab, columns = table.shape
    count = ids.shape[0]
    mine = (ids < vocab).reshape(-1, 128)
    before = jnp.arange(128)[:, None] < jnp.arange(128)[None, :]
    in_row = dot(mine.astype(LOW), before.astype(LOW), 1, 0)
    per_row = jnp.sum(mine.astype(FULL), axis=1)
    lines = jnp.arange(mine.shape[0])
    ahead = jnp.sum(jnp.where(lines[:, None] > lines[None, :], per_row[None, :], 0.0), axis=1)
    found = jnp.sum(per_row).astype(jnp.int32)
    turns = (in_row + ahead[:, None]).astype(jnp.int32)
    turns = jnp.where(mine, turns, count + UNROLL + 1).reshape(-1)
    turns = jnp.concatenate([turns, jnp.full((128,), found)])
    return pl.pallas_call(
        lookup_body,
        in_specs=[pl.BlockSpec(memory_space=pltpu.SMEM)] * 2 + [ANY],
        out_specs=[VMEM, VMEM, pl.BlockSpec(memory_space=pltpu.SMEM)],
        scratch_shapes=[
            pltpu.VMEM((vocab, columns), FULL),
            pltpu.VMEM((count + 8, columns), FULL),
            pltpu.SemaphoreType.DMA,
        ],
        out_shape=[
            struct((count, columns), LOW),
            struct((vocab, columns), LOW),
            struct((count + 2 * UNROLL,), jnp.int32),
        ],
        compiler_params=pltpu.CompilerParams(vmem_limit_bytes=VMEM_BYTES),
        cost_estimate=pl.CostEstimate(
            flops=0, bytes_accessed=vocab * columns * 4, transcendentals=0
        ),
        name="lookup",
    )(ids, turns, table)


def spread_body(
    ids_ref, list_ref, rows_ref, head_ref, out_ref, square_ref, even, odd, rows, sem
):
    vocab = out_ref.shape[0]
    count = rows_ref.shape[0]
    chunk = 256

    def strip(part):
        return pl.ds(pl.multiple_of(part * chunk, chunk), chunk)

    def begin(part, carry):
        even[strip(part), :] = head_ref[strip(part), :].astype(FULL)
        odd[strip(part), :] = jnp.zeros((chunk, odd.shape[1]), FULL)
        return carry

    lax.fori_loop(0, vocab // chunk, begin, 0)

    def widen(part, carry):
        rows[strip(part), :] = rows_ref[strip(part), :].astype(FULL)
        return carry

    lax.fori_loop(0, count // chunk, widen, 0)
    rows[pl.ds(count, 8), :] = jnp.zeros((8, rows.shape[1]), FULL)

    def step(group, carry):
        for member in range(UNROLL):
            at = list_ref[group * UNROLL + member]
            spot = jnp.minimum(ids_ref[jnp.minimum(at, count - 1)], vocab - 1)
            total = even if member % 2 == 0 else odd
            total[pl.ds(spot, 1), :] = total[pl.ds(spot, 1), :] + rows[pl.ds(at, 1), :]
        return carry

    found = list_ref[count + UNROLL]
    lax.fori_loop(0, (found + UNROLL - 1) // UNROLL, step, 0)

    def finish(part, squares):
        value = even[strip(part), :] + odd[strip(part), :]
        even[strip(part), :] = value
        return squares + jnp.sum((value * value).reshape(chunk // 8, 8, -1), axis=0)

    square_ref[...] = lax.fori_loop(
        0, vocab // chunk, finish, jnp.zeros((8, even.shape[1]), FULL)
    )
    store = pltpu.make_async_copy(even, out_ref, sem)
    store.start()
    store.wait()


def spread(ids, listed, rows, head):
    vocab, columns = head.shape
    count = ids.shape[0]
    smem = pl.BlockSpec(memory_space=pltpu.SMEM)
    return pl.pallas_call(
        spread_body,
        in_specs=[smem, smem, VMEM, VMEM],
        out_specs=[ANY, VMEM],
        scratch_shapes=[
            pltpu.VMEM((vocab, columns), FULL),
            pltpu.VMEM((vocab, columns), FULL),
            pltpu.VMEM((count + 8, columns), FULL),
            pltpu.SemaphoreType.DMA,
        ],
        out_shape=[struct((vocab, columns), FULL), struct((8, columns), FULL)],
        compiler_params=pltpu.CompilerParams(vmem_limit_bytes=VMEM_BYTES),
        cost_estimate=pl.CostEstimate(
            flops=count * columns, bytes_accessed=vocab * columns * 8, transcendentals=0
        ),
        name="spread",
    )(ids, listed, rows, head)


def adamw(weight, first_m, second_m, grad, rate, decay):
    first_new = BETA_ONE * first_m + (1.0 - BETA_ONE) * grad
    second_new = BETA_TWO * second_m + (1.0 - BETA_TWO) * grad * grad
    update = (
        first_new
        / (1.0 - BETA_ONE**STEP)
        / (jnp.sqrt(second_new / (1.0 - BETA_TWO**STEP)) + ADAM_EPS)
    )
    return (weight * (1.0 - rate * decay) - rate * update, first_new, second_new)


def cut_columns(values, count):
    rows, columns = values.shape
    return jnp.moveaxis(values.reshape(rows, count, columns // count), 1, 0)


def shifted(parts, axis, step):
    count = lax.axis_size(axis)
    pairs = [(source, (source + step) % count) for source in range(count)]
    return lax.ppermute(parts, axis, pairs)


def per_device(
    tokens,
    picks,
    targets,
    lengths,
    skip,
    embed,
    embed_m,
    embed_v,
    attn_qo,
    attn_qo_mom,
    attn_kv,
    attn_kv_mom,
    ffn,
    ffn_mom,
    gains,
    gains_m,
    gains_v,
):
    wide_count = lax.axis_size("wide")
    narrow_count = lax.axis_size("narrow")
    narrow_spot = lax.axis_index("narrow")
    wide_spot = lax.axis_index("wide")
    seq_len = tokens.shape[1]
    sel = picks.shape[1]
    vocab_rows, columns = embed.shape
    width = columns * wide_count
    own_rows = sel // narrow_count
    tok_rows = seq_len // narrow_count
    all_rows = own_rows + tok_rows
    heads_own = HEADS // narrow_count
    head_cols = heads_own * HD
    repeat = max(1, narrow_count // KVH)
    groups = KVH * repeat // narrow_count
    ffn_rows = ffn.shape[0]
    ffn_size = ffn_rows // narrow_count
    total_rows = wide_count * sel
    lens = lengths[0]
    pick_ids = picks[0]
    keep_layer = (1 - skip[0]).astype(FULL)
    keep_row = jnp.full((1, width), keep_layer)
    lanes = 128

    def box(flat):
        height = -(-flat.shape[0] // (8 * lanes)) * 8
        return jnp.pad(flat, (0, height * lanes - flat.shape[0])).reshape(height, lanes)

    ffn_low = jnp.moveaxis(ffn, 1, 0).astype(LOW)
    ffn_cut = ffn_low.reshape(3, narrow_count, ffn_size, ffn_low.shape[2])
    ffn_cut = jnp.moveaxis(ffn_cut, 1, 0).reshape(narrow_count, 3 * ffn_size, -1)
    kv_own = attn_kv.reshape(columns, -1).astype(LOW)

    where_at = jnp.arange(seq_len, dtype=jnp.int32)
    pick_tokens = jnp.sum(
        jnp.where(pick_ids[:, None] == where_at[None, :], tokens[0][None, :], 0), axis=1
    )
    ints = box(jnp.concatenate([tokens[0], pick_tokens, targets[0]]))
    all_ints, all_gains, kv_part = launch(
        [
            gather_wide(ints),
            gather_both(box(gains.astype(LOW).astype(FULL).reshape(-1))),
            gather_blocks("narrow", kv_own),
        ],
        0,
        "gather_ids",
    )
    kv_part = jnp.moveaxis(kv_part, 0, 1).reshape(columns, -1)
    proj_own = jnp.concatenate([kv_part, attn_qo.reshape(columns, -1).astype(LOW)], axis=1)
    proj = lax.all_gather(proj_own, "wide", axis=0, tiled=True)
    ffn_cut, all_ints = lax.optimization_barrier((ffn_cut, all_ints))
    ffn_pieces = [lax.dynamic_index_in_dim(ffn_cut, narrow_spot, 0, False)] + [
        shifted(
            lax.dynamic_index_in_dim(
                ffn_cut, lax.rem(narrow_spot + step, narrow_count), 0, False
            ),
            "narrow",
            step,
        )
        for step in range(1, narrow_count)
    ]
    gain_size = gains.shape[1]
    gain_w = all_gains.reshape(narrow_count, wide_count, -1)[:, :, : 3 * gain_size]
    gain_w = gain_w.reshape(narrow_count, wide_count, 3, gain_size)
    gain_w = jnp.transpose(gain_w, (2, 1, 0, 3)).reshape(3, width)
    all_ints = all_ints.reshape(wide_count, -1)
    tokens_all = all_ints[:, :seq_len].reshape(wide_count, narrow_count, tok_rows)
    picked_all = all_ints[:, seq_len : seq_len + sel].reshape(wide_count, narrow_count, own_rows)
    targets_all = all_ints[:, seq_len + sel : seq_len + 2 * sel].reshape(-1)
    wanted = jnp.moveaxis(jnp.concatenate([tokens_all, picked_all], axis=2), 1, 0).reshape(-1)
    local_ids = wanted - narrow_spot * vocab_rows
    inside = (local_ids >= 0) & (local_ids < vocab_rows)
    spots = jnp.where(inside, local_ids, vocab_rows)
    found, embed_low, listed = lookup(embed, spots)
    ffn_pieces, found = lax.optimization_barrier((ffn_pieces, found))
    ffn_sub = assemble(ffn_pieces).reshape(3, ffn_size, width)
    ffn_sub, found = lax.optimization_barrier((ffn_sub, found))
    ffn_w = lax.all_gather(ffn_sub, "wide", axis=0)
    found = found.reshape(narrow_count, wide_count * all_rows, columns)
    embed_cut = embed_low.reshape(wide_count, vocab_rows // wide_count, columns)
    table_half = embed_cut.shape[1] // 2
    rows_low = launch([fetch_rows(found, all_rows)], 1, "fetch_rows")[0]

    mom_qo = jnp.moveaxis(attn_qo_mom, 1, 0)
    mom_kv = jnp.moveaxis(attn_kv_mom, 1, 0)
    mom_ffn = jnp.moveaxis(ffn_mom, 1, 0)
    slot_rows, slot_cols = mom_ffn.shape[1:]

    block_rows, q_size = mom_qo.shape[1:]
    kv_size = mom_kv.shape[2]
    half_rows = block_rows // 2
    kv_box = jnp.moveaxis(mom_kv.reshape(4, half_rows, kv_size), 0, 1).reshape(half_rows, -1)
    small_box = jnp.concatenate([mom_qo.reshape(2 * block_rows, q_size), kv_box])
    small_box = jnp.pad(small_box, ((0, slot_rows - small_box.shape[0]), (0, 0)))
    mom_parts = jnp.concatenate([mom_ffn, small_box[None]]).astype(LOW)

    seg_all, cosine_all, sine_all = angles_at(lens, where_at)
    cosine_all, sine_all = wide_angles(cosine_all, sine_all)
    seg_mine, cosine, sine = angles_at(lens, pick_ids)
    cosine, sine = wide_angles(cosine, sine)

    def tok_part(angles):
        return lax.dynamic_slice_in_dim(angles, narrow_spot * tok_rows, tok_rows, 0)

    by_head, normed_tok = make_heads(
        rows_low, gain_w[0:1], proj, tok_part(cosine_all), tok_part(sine_all), groups, repeat
    )
    own_head, start_low, tok_cols, table_top = launch(
        [
            swap_blocks("narrow", by_head),
            gather_blocks("narrow", rows_low[tok_rows:]),
            split_columns("wide", normed_tok),
            join_columns("wide", embed_cut[:, :table_half]),
        ],
        2,
        "trade_heads",
    )
    start_low, ffn_w = lax.optimization_barrier((start_low, ffn_w))
    start_low = start_low.reshape(sel, width)
    queries, probs, mixed, attn_part, normed, early_part = attend(
        start_low,
        gain_w,
        proj,
        own_head,
        cosine,
        sine,
        seg_mine[:, None],
        seg_all[None, :],
        pick_ids[:, None],
    )
    early = lax.all_gather(early_part, "wide", axis=0, tiled=True)
    start_own = rows_low[tok_rows:].astype(FULL)
    middle, inner, mixed_wide, pick_cols = launch(
        [
            settle(
                attn_part,
                start_own,
                start_own,
                jnp.ones((1, width), FULL),
                gain_w[1:2],
            ),
            gather_wide(mixed),
            split_columns("wide", normed),
        ],
        3,
        "settle_middle",
    )
    inner = inner.reshape(sel, width)
    inner_all = lax.all_gather(inner, "wide", axis=0, tiled=True)
    gate, up, hidden, fed = feed(inner, ffn_w)
    final_own, late_part, table_low = launch(
        [
            settle(fed, middle, start_own, keep_row, gain_w[2:3]),
            join_columns("wide", embed_cut[:, table_half:]),
        ],
        4,
        "settle_late",
    )
    table_own = jnp.concatenate([table_top, table_low])

    table_count = table_own.shape[0]
    local_target = targets_all - (narrow_spot * vocab_rows + wide_spot * table_count)
    has_target = jnp.arange(table_count, dtype=jnp.int32)[:, None] == local_target[None, :]
    counted = (targets_all >= 0).astype(FULL)
    loss_count = jnp.sum(counted)

    def exit_logits(features):
        logits = dot(table_own, features, 1, 1)
        peak = jnp.max(logits, axis=0)
        total = jnp.sum(jnp.exp(logits - peak[None, :]), axis=0)
        picked = jnp.sum(jnp.where(has_target, logits, 0.0), axis=0)
        return logits, jnp.stack([peak, total, picked])

    half = slot_rows // 2
    late, mom_top, early_logits, early_stats = launch(
        [
            gather_wide(late_part.reshape(sel, width)),
            swap_turned(mom_parts[:, :half]),
            exit_stats(early, table_own, local_target[None, :]),
        ],
        5,
        "gather_late",
    )
    late = late.reshape(total_rows, width)
    late_logits, late_stats = exit_logits(late)
    stats = jnp.concatenate([early_stats, late_stats], axis=1).reshape(3, 8, -1)
    stats = launch([combine(stats, merge_stats)], 6, "combine_stats")[0]
    stats, inner_all = lax.optimization_barrier((stats, inner_all))
    stats = stats.reshape(3, -1)
    log_norms = stats[0] + jnp.log(stats[1])
    losses = log_norms - stats[2]
    loss_sum = jnp.sum(
        counted * (EXIT_EARLY * losses[:total_rows] + EXIT_LAST * losses[total_rows:])
    )

    def exit_back(logits, log_norm, weight):
        grad_logits = (
            (jnp.exp(logits - log_norm[None, :]) - has_target.astype(FULL))
            * (weight * counted)[None, :]
        ).astype(LOW)
        return grad_logits

    late_grad = exit_back(late_logits, log_norms[total_rows:], EXIT_LAST)
    late_back = dot(late_grad, table_own, 0, 0).astype(LOW)
    early_grad = exit_back(early_logits, log_norms[:total_rows], EXIT_EARLY)
    grad_late, mom_low, early_back, _ = launch(
        [
            sum_wide(late_back),
            swap_turned(mom_parts[:, half:]),
            later(product([early_grad], [table_own], 0, [[(0, 0)]]), 1),
        ],
        7,
        "sum_late",
    )
    mom_owned = jnp.concatenate([mom_top, mom_low], axis=1)
    early_back, grad_late = lax.optimization_barrier((early_back, grad_late))
    grad_early = lax.psum_scatter(early_back[0], "wide", scatter_dimension=0, tiled=True)
    grad_final, gain_late, grad_out = launch(
        [
            settle_back(
                grad_late.astype(LOW),
                final_own,
                jnp.zeros_like(final_own),
                keep_row,
                gain_w[2:3],
            ),
        ],
        8,
        "back_late",
    )
    grad_layer = grad_final * keep_layer
    grad_out = grad_out.reshape(sel, width)
    out_all = lax.all_gather(grad_out, "wide", axis=0, tiled=True)
    acts, fed_back = feed_back(grad_out, ffn_w, gate, up, hidden)
    grad_mid, gain_mid, grad_branch, acts = launch(
        [
            settle_back(fed_back, middle, grad_layer, keep_row, gain_w[1:2]),
            swap_blocks("wide", acts),
        ],
        9,
        "back_middle",
    )
    acts = jnp.moveaxis(acts, 1, 0).reshape(3, total_rows, ffn_size)
    grad_branch, grad_early = lax.optimization_barrier((grad_branch, grad_early))
    grad_branch = grad_branch.reshape(sel, width)

    kv_parts, grad_queries, pick_part, gain_pick, gain_early = attend_back(
        grad_branch,
        proj,
        own_head,
        queries,
        probs,
        cosine,
        sine,
        cosine_all,
        sine_all,
        start_low,
        gain_w,
        grad_early,
    )
    grad_kv, grad_pick, queries_wide, branch_cols, grad_head, _ = launch(
        [
            swap_blocks("narrow", kv_parts),
            sum_narrow(pick_part),
            gather_wide(grad_queries),
            split_columns("wide", grad_branch),
            product([early_grad, late_grad], [early, late], 1, [[(0, 0), (1, 1)]]),
        ],
        10,
        "trade_grads",
    )
    grad_kv, out_all = lax.optimization_barrier((grad_kv, out_all))
    grad_base = grad_mid + grad_final * (1.0 - keep_layer)
    grad_rows, gain_attn, grad_kv = rows_back(
        rows_low, gain_w, proj, grad_kv, grad_pick, grad_base, repeat
    )
    gain_attn = gain_attn + gain_pick
    summed_qo = jnp.stack(
        [
            jnp.einsum("wtc,wtf->cf", pick_cols, queries_wide, preferred_element_type=FULL),
            jnp.einsum("wtc,wtf->cf", branch_cols, mixed_wide, preferred_element_type=FULL),
        ]
    )
    grad_rows, acts_owned, kv_wide, head_cols_all, grad_ffn, ffn_squares = launch(
        [
            return_rows(grad_rows),
            swap_owned(acts, 5),
            later(gather_wide(grad_kv, 3), 2),
            later(split_columns("wide", grad_head[0], 3), 2),
            product([acts], [inner_all, out_all], 0, [[(0, 0)], [(1, 0)], [(2, 1)]]),
        ],
        11,
        "return_rows",
    )
    turn = lax.rem(wide_spot, 2)
    grad_kv_w = jnp.einsum(
        "wtc,wtf->cf", tok_cols, kv_wide, preferred_element_type=FULL
    ).reshape(columns, narrow_count, 2, kv_size)
    grad_kv_w = jnp.moveaxis(grad_kv_w, 0, 2)
    summed_kv = lax.psum_scatter(grad_kv_w, "narrow", scatter_dimension=0, tiled=True)[0]
    summed_table, table_squares = spread(
        spots, listed, grad_rows.reshape(-1, columns), head_cols_all.reshape(vocab_rows, columns)
    )

    squares = (
        jnp.sum(summed_qo * summed_qo)
        + jnp.sum(summed_kv * summed_kv)
        + jnp.sum(ffn_squares)
        + jnp.sum(table_squares)
    )
    sums = jnp.stack(
        [gain_attn[0], gain_mid[0], gain_early[0] + gain_late[0], jnp.full((width,), squares)]
    )
    def owns_last():
        away = lax.axis_index("narrow") + narrow_count - lax.rem(lax.axis_index("wide"), 2)
        return lax.rem(away, narrow_count) >= 2

    sums, kv_owned, qo_owned, owned, _ = launch(
        [
            combine(sums.reshape(4, 8, -1), add_two),
            send_owner(summed_kv.astype(LOW).reshape(2 * block_rows, kv_size)),
            later(send_owner(summed_qo.astype(LOW).reshape(2 * columns, q_size)), 1),
            later(
                product(
                    [acts_owned],
                    [inner_all, out_all],
                    0,
                    [[(at, 0)] for at in range(narrow_count)],
                    False,
                    owns_last,
                ),
                1,
            ),
        ],
        12,
        "combine_sums",
    )
    sums = sums.reshape(4, width)
    summed_gain = lax.dynamic_slice_in_dim(
        sums[:3], (wide_spot * narrow_count + narrow_spot) * gain_size, gain_size, 1
    )
    square_total = sums[3, 0] + jnp.sum(sums[:3] * sums[:3])
    grad_norm = jnp.sqrt(square_total) / loss_count
    factor = jnp.minimum(1.0, CLIP_NORM / (grad_norm + 1e-06)) / loss_count

    final_parts, factor = lax.optimization_barrier((grad_ffn, factor))
    size = width // narrow_count

    def final_piece(spot):
        return lax.dynamic_slice_in_dim(final_parts, spot * size, size, 2)

    pieces = [final_piece(narrow_spot)] + [
        shifted(final_piece(lax.rem(narrow_spot + step, narrow_count)), "narrow", step)
        for step in range(1, narrow_count)
    ]
    directions = newton(
        factor, mom_owned, owned, qo_owned, kv_owned
    )
    directions, pieces, ffn, factor = lax.optimization_barrier(
        (directions, pieces, ffn, factor)
    )
    summed_ffn = jnp.zeros((3, narrow_count, ffn_size, size), LOW)
    for step, piece in enumerate(pieces):
        source = lax.rem(narrow_spot - step + narrow_count, narrow_count)
        summed_ffn = lax.dynamic_update_index_in_dim(summed_ffn, piece, source, 1)
    summed_ffn = summed_ffn.reshape(3, ffn_rows, size).astype(FULL)
    received = [lax.dynamic_index_in_dim(directions, narrow_spot, 0, False)] + [
        shifted(
            lax.dynamic_index_in_dim(
                directions, lax.rem(narrow_spot + step, narrow_count), 0, False
            ),
            "narrow",
            step,
        )
        for step in range(1, narrow_count)
    ]

    def direction_of(matrix):
        step = lax.rem(narrow_spot - matrix - turn + 2 * narrow_count, narrow_count)
        result = received[0]
        for at in range(1, narrow_count):
            result = jnp.where(step == at, received[at], result)
        return result

    dir_ffn = jnp.stack([direction_of(matrix) for matrix in range(3)]).astype(FULL)
    small = direction_of(3).astype(FULL)
    dir_qo = small[: 2 * block_rows].reshape(mom_qo.shape)
    dir_kv = small[2 * block_rows : 2 * block_rows + half_rows].reshape(half_rows, 4, kv_size)
    dir_kv = jnp.moveaxis(dir_kv, 1, 0).reshape(mom_kv.shape)

    embed_new, embed_m_new, embed_v_new = adamw(
        embed, embed_m, embed_v, summed_table * factor, RATE_ADAM, WEIGHT_DECAY
    )
    gains_new, gains_m_new, gains_v_new = adamw(
        gains, gains_m, gains_v, summed_gain * factor, RATE_GAIN, 0.0
    )

    def mom_next(mom, grad):
        return MOMENTUM * mom + jnp.moveaxis(grad * factor, 0, 1)

    shrink = 1.0 - RATE_MUON * WEIGHT_DECAY

    def weight_next(weight, direction):
        return weight * shrink - RATE_MUON * jnp.moveaxis(direction, 0, 1)

    return (
        loss_sum,
        loss_count,
        grad_norm,
        embed_new,
        embed_m_new,
        embed_v_new,
        weight_next(attn_qo, dir_qo),
        mom_next(attn_qo_mom, summed_qo),
        weight_next(attn_kv, dir_kv),
        mom_next(attn_kv_mom, summed_kv),
        weight_next(ffn, dir_ffn),
        mom_next(ffn_mom, summed_ffn),
        gains_new,
        gains_m_new,
        gains_v_new,
    )


def solution(mesh):
    by_pack = P("wide", None)
    table = P("narrow", "wide")
    layer = P("wide", None, "narrow")
    gain = P(None, ("wide", "narrow"))
    return jax.shard_map(
        per_device,
        mesh=mesh,
        in_specs=(by_pack,) * 4 + (P("wide"),) + (table,) * 3 + (layer,) * 6 + (gain,) * 3,
        out_specs=(P(),) * 3 + (table,) * 3 + (layer,) * 6 + (gain,) * 3,
        check_vma=False,
    )
```

```python
import functools

import jax
import jax.numpy as jnp
from jax import lax
from jax.experimental import pallas as pl
from jax.experimental.pallas import tpu as pltpu
from jax.sharding import PartitionSpec as P

HEADS = 16
HD = 128
KVH = 4
NS_STEPS = 5
STEP = 10


NORM_EPS = 1e-05
ROPE_BASE = 10000.0
EXIT_EARLY = 0.25
EXIT_LAST = 1.0
CLIP_NORM = 0.02
BETA_ONE = 0.9
BETA_TWO = 0.95
ADAM_EPS = 1e-08
RATE_ADAM = 0.02
RATE_GAIN = 0.3
RATE_MUON = 0.3
WEIGHT_DECAY = 0.1
MOMENTUM = 0.95
NEWTON_A = 3.4445
NEWTON_B = -4.775
NEWTON_C = 2.0315
MASKED = -1e30
LOW = jnp.bfloat16
FULL = jnp.float32
BOTH = ("wide", "narrow")
UNROLL = 16
VMEM_BYTES = 56 * 1024 * 1024


def dot(first, second, first_dim, second_dim):
    return lax.dot_general(
        first, second, (((first_dim,), (second_dim,)), ((), ())), preferred_element_type=FULL
    )


def norm_rows(values, gain_row):
    return (
        values * lax.rsqrt(jnp.mean(values * values, axis=-1, keepdims=True) + NORM_EPS) * gain_row
    )


def segments_at(lens, where_at):
    ends = jnp.cumsum(lens)
    return jnp.sum((where_at[:, None] >= ends[None, :]).astype(jnp.int32), axis=1)


def angles_at(lens, where_at):
    segment = segments_at(lens, where_at)
    starts = jnp.cumsum(lens) - lens
    member = segment[:, None] == jnp.arange(lens.shape[0], dtype=jnp.int32)[None, :]
    begin = jnp.sum(jnp.where(member, starts[None, :], 0), axis=1)
    offset_pos = (where_at - begin).astype(FULL)
    inverse = ROPE_BASE ** (-2.0 * jnp.arange(HD // 2, dtype=FULL) / HD)
    angle = offset_pos[:, None] * inverse[None, :]
    return (segment, jnp.cos(angle), jnp.sin(angle))


MESH = pl.DeviceIdType.MESH
ANY = pl.BlockSpec(memory_space=pl.ANY)
VMEM = pl.BlockSpec(memory_space=pltpu.VMEM)


def others(axis, count):
    me = lax.axis_index(axis)
    return [{axis: lax.rem(me + step, count)} for step in range(1, count)]


def push(source, target, send, receive, device):
    return pltpu.make_async_remote_copy(
        src_ref=source,
        dst_ref=target,
        send_sem=send,
        recv_sem=receive,
        device_id=device,
        device_id_type=MESH,
    )


def arrived(block, send, receive, device):
    push(block, block, send, receive, device).wait_recv()


def like(values):
    return jax.ShapeDtypeStruct(values.shape, values.dtype)


def struct(shape, dtype):
    return jax.ShapeDtypeStruct(shape, dtype)


def sems(*shape):
    return pltpu.SemaphoreType.DMA(shape)


class Task:
    def __init__(self, inputs, outputs, scratch, steps, place_in, place_out, axes):
        self.inputs, self.outputs, self.scratch, self.steps = inputs, outputs, scratch, steps
        self.place_in = [place_in] * len(inputs)
        self.place_out = [place_out] * len(outputs)
        self.axes = axes


def launch(tasks, ident, name):
    axes = sorted(set(axis for task in tasks for axis in task.axes))
    inputs = [a for task in tasks for a in task.inputs]
    outputs = [a for task in tasks for a in task.outputs]
    scratch = [a for task in tasks for a in task.scratch]

    def body(*refs):
        refs = list(refs)
        ins = refs[: len(inputs)]
        outs = refs[len(inputs) : len(inputs) + len(outputs)]
        extra = refs[len(inputs) + len(outputs) :]
        barrier = pltpu.get_barrier_semaphore()
        targets = [device for axis in axes for device in others(axis, lax.axis_size(axis))]
        for device in targets:
            pl.semaphore_signal(barrier, inc=1, device_id=device, device_id_type=MESH)
        pl.semaphore_wait(barrier, len(targets))
        live = []
        for task in tasks:
            counts = (len(task.inputs), len(task.outputs), len(task.scratch))
            live.append(task.steps(ins[: counts[0]], outs[: counts[1]], extra[: counts[2]]))
            ins, outs, extra = ins[counts[0] :], outs[counts[1] :], extra[counts[2] :]
        while live:
            live = [steps for steps in live if next(steps, 0) is None]

    size = sum(a.size * a.dtype.itemsize for a in list(inputs) + list(outputs))
    return pl.pallas_call(
        body,
        out_shape=outputs,
        in_specs=[place for task in tasks for place in task.place_in],
        out_specs=[place for task in tasks for place in task.place_out],
        scratch_shapes=scratch,
        compiler_params=pltpu.CompilerParams(
            collective_id=ident, has_side_effects=True, vmem_limit_bytes=VMEM_BYTES
        ),
        cost_estimate=pl.CostEstimate(flops=0, bytes_accessed=size // 8, transcendentals=0),
        name=name,
    )(*inputs)


def later(task, turns):
    begin = task.steps

    def steps(ins, outs, scratch):
        for turn in range(turns):
            yield
        yield from begin(ins, outs, scratch)

    task.steps = steps
    return task


def gather_wide(values, patience=1):
    count = lax.axis_size("wide")
    chips = count // 2

    def steps(ins, outs, scratch):
        (x_ref,), (out_ref,), (send, receive, local) = ins, outs, scratch
        me = lax.axis_index("wide")
        mate = me + 1 - 2 * lax.rem(me, 2)
        peers = [lax.rem(me + 2 * step, count) for step in range(1, chips)] + [mate]
        first = []
        for step, peer in enumerate(peers):
            copy = push(x_ref, out_ref.at[me], send.at[step], receive.at[me], {"wide": peer})
            copy.start()
            first.append(copy)
        keep = pltpu.make_async_copy(x_ref, out_ref.at[me], local)
        keep.start()
        for turn in range(patience):
            yield
        second = []
        for step in range(1, chips):
            source = lax.rem(me - 2 * step + count, count)
            block = out_ref.at[source]
            arrived(block, send.at[0], receive.at[source], {"wide": mate})
            copy = push(
                block, block, send.at[chips + step - 1], receive.at[source], {"wide": mate}
            )
            copy.start()
            second.append(copy)
        yield
        for step in range(chips):
            source = lax.rem(mate - 2 * step + count, count)
            arrived(out_ref.at[source], send.at[0], receive.at[source], {"wide": mate})
        for copy in first + second:
            copy.wait_send()
        keep.wait()

    shape = struct((count,) + values.shape, values.dtype)
    return Task(
        [values], [shape], [sems(count - 1), sems(count), sems()], steps, VMEM, VMEM, ["wide"]
    )


def trade(axis, values, source_of, target_of, shape, patience=2):
    count = lax.axis_size(axis)

    def steps(ins, outs, scratch):
        (x_ref,), (out_ref,), (send, receive, local) = ins, outs, scratch
        me = lax.axis_index(axis)
        copies = []
        for step in range(1, count):
            peer = lax.rem(me + step, count)
            copy = push(
                source_of(x_ref, peer),
                target_of(out_ref, me),
                send.at[step - 1],
                receive.at[me],
                {axis: peer},
            )
            copy.start()
            copies.append(copy)
        keep = pltpu.make_async_copy(source_of(x_ref, me), target_of(out_ref, me), local)
        keep.start()
        for turn in range(patience):
            yield
        for step in range(1, count):
            source = lax.rem(me - step + count, count)
            arrived(
                target_of(out_ref, source), send.at[0], receive.at[source], {axis: source}
            )
        for copy in copies:
            copy.wait_send()
        keep.wait()

    return Task(
        [values],
        [struct(shape, values.dtype)],
        [sems(count - 1), sems(count), sems()],
        steps,
        ANY,
        ANY,
        [axis],
    )


def block_at(ref, spot):
    return ref.at[spot]


def whole_at(ref, spot):
    return ref


def columns_of(size):
    def at(ref, spot):
        return ref.at[:, pl.ds(pl.multiple_of(spot * size, size), size)]

    return at


def turned(ref, spot):
    count = lax.axis_size("narrow")
    matrix = lax.rem(spot + count - lax.rem(lax.axis_index("wide"), 2), count)
    return ref.at[jnp.minimum(matrix, 3)]


def swap_turned(values, patience=2):
    shape = (lax.axis_size("narrow"),) + values.shape[1:]
    return trade("narrow", values, turned, block_at, shape, patience)


def product(lefts, rights, dim, order, pause=True, last=None):
    count, rows = len(order), lefts[0].shape[-1 if dim == 0 else -2]
    columns = rights[0].shape[1]
    block = min(512, columns)

    def steps(ins, outs, scratch):
        left_refs, right_refs = ins[: len(lefts)], ins[len(lefts) :]
        result_ref, square_ref = outs
        square_ref[...] = jnp.zeros_like(square_ref)

        def left_of(member):
            return left_refs[0][member] if lefts[0].ndim == 3 else left_refs[member][...]

        def fill(at, members, shift):
            def strip(part, carry):
                spot = pl.ds(pl.multiple_of(part * block, block), block)
                value = jnp.zeros((rows, block), FULL)
                for left, right in members:
                    value = value + dot(left_of(left), right_refs[right + shift][:, spot], dim, 0)
                result_ref[at, :, spot] = value.astype(LOW)
                square_ref[:, spot] = square_ref[:, spot] + jnp.sum(
                    value * value, axis=0, keepdims=True
                )
                return carry

            lax.fori_loop(0, columns // block, strip, 0)

        for at, members in enumerate(order):
            if last is None:
                fill(at, members, 0)
            else:
                pl.when(last())(functools.partial(fill, at, members, 1))
                pl.when(jnp.logical_not(last()))(functools.partial(fill, at, members, 0))
            if pause:
                yield

    return Task(
        list(lefts) + list(rights),
        [struct((count, rows, columns), LOW), struct((1, columns), FULL)],
        [],
        steps,
        VMEM,
        VMEM,
        [],
    )


def exit_stats(features, table, targets):
    rows, vocab = features.shape[0], table.shape[0]
    block = min(256, vocab)

    def steps(ins, outs, scratch):
        features_ref, table_ref, targets_ref = ins
        logits_ref, stats_ref = outs

        def strip(part):
            return pl.ds(pl.multiple_of(part * block, block), block)

        def over(function, start):
            return lax.fori_loop(0, vocab // block, function, start)

        def fill(part, peak):
            logits = dot(table_ref[strip(part), :], features_ref[...], 1, 1)
            logits_ref[strip(part), :] = logits
            return jnp.maximum(peak, jnp.max(logits, axis=0, keepdims=True))

        peak = over(fill, jnp.full((1, rows), MASKED, FULL))
        lines = lax.broadcasted_iota(jnp.int32, (block, rows), 0)

        def add(part, carry):
            total, picked = carry
            logits = logits_ref[strip(part), :]
            hit = lines + part * block == targets_ref[...]
            return (
                total + jnp.sum(jnp.exp(logits - peak), axis=0, keepdims=True),
                picked + jnp.sum(jnp.where(hit, logits, 0.0), axis=0, keepdims=True),
            )

        zero = jnp.zeros((1, rows), FULL)
        total, picked = over(add, (zero, zero))
        stats_ref[0:1, :] = peak
        stats_ref[1:2, :] = total
        stats_ref[2:3, :] = picked
        yield

    return Task(
        [features, table, targets],
        [struct((vocab, rows), FULL), struct((3, rows), FULL)],
        [],
        steps,
        VMEM,
        VMEM,
        [],
    )


def swap_owned(values, patience):
    count = lax.axis_size("narrow")

    def steps(ins, outs, scratch):
        (x_ref,), (out_ref,), (send, receive, local) = ins, outs, scratch
        me = lax.axis_index("narrow")
        turn = lax.rem(lax.axis_index("wide"), 2)

        def matrix_of(device):
            return lax.rem(device + count - turn, count)

        def copy_to(step):
            peer = lax.rem(me + step, count)
            return push(
                x_ref.at[jnp.minimum(matrix_of(peer), 2)],
                out_ref.at[me],
                send.at[step - 1],
                receive.at[me],
                {"narrow": peer},
            )

        def keep():
            return pltpu.make_async_copy(
                x_ref.at[jnp.minimum(matrix_of(me), 2)], out_ref.at[me], local
            )

        keep().start()
        for step in range(1, count):

            @pl.when(matrix_of(lax.rem(me + step, count)) < 3)
            def _():
                copy_to(step).start()

        for turn_at in range(patience):
            yield

        @pl.when(matrix_of(me) < 3)
        def _():
            for step in range(1, count):
                source = lax.rem(me - step + count, count)
                arrived(out_ref.at[source], send.at[0], receive.at[source], {"narrow": source})

        for step in range(1, count):

            @pl.when(matrix_of(lax.rem(me + step, count)) < 3)
            def _():
                copy_to(step).wait_send()

        keep().wait()

    return Task(
        [values],
        [struct((count,) + values.shape[1:], values.dtype)],
        [sems(count - 1), sems(count), sems()],
        steps,
        ANY,
        ANY,
        ["narrow"],
    )


def send_owner(values):
    count = lax.axis_size("narrow")

    def steps(ins, outs, scratch):
        (x_ref,), (out_ref,), (send, receive, local) = ins, outs, scratch
        me = lax.axis_index("narrow")
        owner = lax.rem(3 + lax.rem(lax.axis_index("wide"), 2), count)
        keep = pltpu.make_async_copy(x_ref, out_ref.at[me], local)
        keep.start()

        def to_owner():
            return push(x_ref, out_ref.at[me], send.at[0], receive.at[me], {"narrow": owner})

        @pl.when(me != owner)
        def _():
            to_owner().start()

        yield
        yield

        @pl.when(me != owner)
        def _():
            to_owner().wait_send()

        @pl.when(me == owner)
        def _():
            for step in range(1, count):
                source = lax.rem(owner + step, count)
                arrived(out_ref.at[source], send.at[0], receive.at[source], {"narrow": source})

        keep.wait()

    return Task(
        [values],
        [struct((count,) + values.shape, values.dtype)],
        [sems(1), sems(count), sems()],
        steps,
        ANY,
        ANY,
        ["narrow"],
    )


def swap_blocks(axis, values):
    return trade(axis, values, block_at, block_at, values.shape)


def gather_blocks(axis, values):
    shape = (lax.axis_size(axis),) + values.shape
    return trade(axis, values, whole_at, block_at, shape)


def split_columns(axis, values, patience=2):
    count = lax.axis_size(axis)
    rows, size = values.shape[0], values.shape[1] // count
    return trade(axis, values, columns_of(size), block_at, (count, rows, size), patience)


def join_columns(axis, values):
    count, rows, size = values.shape
    return trade(axis, values, block_at, columns_of(size), (rows, count * size))


def collect(count, parts_ref, slots, send, receive):
    me = lax.axis_index("narrow")
    copies = []
    for step in range(1, count):
        peer = lax.rem(me + step, count)
        copy = push(
            parts_ref.at[peer],
            slots.at[me],
            send.at[step - 1],
            receive.at[me],
            {"narrow": peer},
        )
        copy.start()
        copies.append(copy)
    return copies


def collected(count, parts_ref, slots, send, receive):
    me = lax.axis_index("narrow")
    total = parts_ref[me].astype(FULL)
    for step in range(1, count):
        source = lax.rem(me - step + count, count)
        arrived(slots.at[source], send.at[0], receive.at[source], {"narrow": source})
        total = total + slots[source].astype(FULL)
    return total


def share(count, low, all_ref, send, receive):
    me = lax.axis_index("narrow")
    all_ref[me] = low
    copies = []
    for step in range(1, count):
        peer = lax.rem(me + step, count)
        copy = push(
            all_ref.at[me], all_ref.at[me], send.at[step - 1], receive.at[me], {"narrow": peer}
        )
        copy.start()
        copies.append(copy)
    return copies


def shared(count, all_ref, send, receive):
    me = lax.axis_index("narrow")
    for step in range(1, count):
        source = lax.rem(me - step + count, count)
        arrived(all_ref.at[source], send.at[0], receive.at[source], {"narrow": source})


def narrow_sems(count):
    return [sems(count - 1), sems(count)]


def settle(partial, base, other, keep_row, gain_row):
    count = lax.axis_size("narrow")
    rows, width = base.shape

    def steps(ins, outs, scratch):
        parts_ref, base_ref, other_ref, keep_ref, gain_ref = ins
        own_ref, all_ref = outs
        slots, send, receive, send_all, receive_all = scratch
        copies = collect(count, parts_ref, slots, send, receive)
        yield
        total = collected(count, parts_ref, slots, send, receive)
        total = jnp.where(keep_ref[...] > 0, total + base_ref[...], other_ref[...])
        own_ref[...] = total
        low = norm_rows(total, gain_ref[...]).astype(LOW)
        copies = copies + share(count, low, all_ref, send_all, receive_all)
        yield
        shared(count, all_ref, send_all, receive_all)
        for copy in copies:
            copy.wait_send()

    return Task(
        [partial.reshape(count, rows, width), base, other, keep_row, gain_row],
        [struct((rows, width), FULL), struct((count, rows, width), LOW)],
        [pltpu.VMEM((count, rows, width), partial.dtype)]
        + narrow_sems(count)
        + narrow_sems(count),
        steps,
        VMEM,
        VMEM,
        ["narrow"],
    )


def settle_back(partial, values, add, keep_row, gain_row):
    count = lax.axis_size("narrow")
    rows, width = values.shape

    def steps(ins, outs, scratch):
        parts_ref, values_ref, add_ref, keep_ref, gain_ref = ins
        own_ref, gain_grad_ref, all_ref = outs
        slots, send, receive, send_all, receive_all = scratch
        copies = collect(count, parts_ref, slots, send, receive)
        yield
        grad = collected(count, parts_ref, slots, send, receive)
        held = values_ref[...]
        root = lax.rsqrt(jnp.mean(held * held, axis=-1, keepdims=True) + NORM_EPS)
        scaled = gain_ref[...] * grad
        inner = jnp.mean(held * scaled, axis=-1, keepdims=True)
        own = add_ref[...] + root * scaled - held * (root * root * root * inner)
        gain_grad_ref[...] = jnp.sum(held * root * grad, axis=0, keepdims=True)
        own_ref[...] = own
        low = (own * keep_ref[...]).astype(LOW)
        copies = copies + share(count, low, all_ref, send_all, receive_all)
        yield
        shared(count, all_ref, send_all, receive_all)
        for copy in copies:
            copy.wait_send()

    return Task(
        [partial.reshape(count, rows, width), values, add, keep_row, gain_row],
        [
            struct((rows, width), FULL),
            struct((1, width), FULL),
            struct((count, rows, width), LOW),
        ],
        [pltpu.VMEM((count, rows, width), partial.dtype)]
        + narrow_sems(count)
        + narrow_sems(count),
        steps,
        VMEM,
        VMEM,
        ["narrow"],
    )


def sum_narrow(partial):
    count = lax.axis_size("narrow")
    rows, width = partial.shape[0] // count, partial.shape[1]

    def steps(ins, outs, scratch):
        (parts_ref,), (own_ref,), (slots, send, receive) = ins, outs, scratch
        copies = collect(count, parts_ref, slots, send, receive)
        yield
        yield
        own_ref[...] = collected(count, parts_ref, slots, send, receive)
        for copy in copies:
            copy.wait_send()

    return Task(
        [partial.reshape(count, rows, width)],
        [struct((rows, width), FULL)],
        [pltpu.VMEM((count, rows, width), partial.dtype)] + narrow_sems(count),
        steps,
        VMEM,
        VMEM,
        ["narrow"],
    )


def fetch_rows(found, rows):
    deep, wide = lax.axis_size("narrow"), lax.axis_size("wide")
    columns = found.shape[2]

    def steps(ins, outs, scratch):
        (found_ref,), (out_ref,) = ins, outs
        rightward, leftward, final = scratch[:3]
        send_right, receive_right, send_left, receive_left = scratch[3:7]
        send_wide, receive_wide, local = scratch[7:]
        spot = lax.axis_index("narrow")
        me = lax.axis_index("wide")

        def right_copy(part, source):
            return push(
                source,
                rightward.at[part],
                send_right.at[part],
                receive_right.at[part],
                {"narrow": lax.rem(spot + 1, deep)},
            )

        def left_copy(part, source):
            return push(
                source,
                leftward.at[part],
                send_left.at[part],
                receive_left.at[part],
                {"narrow": lax.rem(spot + deep - 1, deep)},
            )

        for step in range(deep - 1):
            right, left = deep - 1 - step, step

            @pl.when((spot == 0) & (right > 0))
            def _():
                right_copy(right, found_ref.at[right]).start()

            @pl.when((spot == deep - 1) & (left < deep - 1))
            def _():
                left_copy(left, found_ref.at[left]).start()

        yield
        for step in range(deep - 1):
            right, left = deep - 1 - step, step

            def pass_right():
                right_copy(right, rightward.at[right]).wait_recv()
                rightward[right] = rightward[right] + found_ref[right]
                right_copy(right, rightward.at[right]).start()

            pl.when((spot > 0) & (right > spot) & (2 * spot < deep))(pass_right)

            @pl.when((spot < deep - 1) & (left < spot))
            def _():
                left_copy(left, leftward.at[left]).wait_recv()
                leftward[left] = leftward[left] + found_ref[left]
                left_copy(left, leftward.at[left]).start()

            pl.when((right > spot) & (2 * spot >= deep))(pass_right)

        final[...] = found_ref[spot]

        @pl.when(spot > 0)
        def _():
            right_copy(spot, rightward.at[spot]).wait_recv()
            final[...] = final[...] + rightward[spot]

        @pl.when(spot < deep - 1)
        def _():
            left_copy(spot, leftward.at[spot]).wait_recv()
            final[...] = final[...] + leftward[spot]

        def rows_for(device):
            return final.at[pl.ds(pl.multiple_of(device * rows, rows), rows)]

        def columns_from(device):
            return columns_of(columns)(out_ref, device)

        copies = []
        for step in range(1, wide):
            peer = lax.rem(me + step, wide)
            copy = push(
                rows_for(peer),
                columns_from(me),
                send_wide.at[step - 1],
                receive_wide.at[me],
                {"wide": peer},
            )
            copy.start()
            copies.append(copy)
        keep = pltpu.make_async_copy(rows_for(me), columns_from(me), local)
        keep.start()
        yield
        for step in range(1, wide):
            source = lax.rem(me - step + wide, wide)
            arrived(
                columns_from(source), send_wide.at[0], receive_wide.at[source], {"wide": source}
            )
        yield
        for copy in copies:
            copy.wait_send()
        keep.wait()
        for step in range(deep - 1):
            right, left = deep - 1 - step, step

            @pl.when(right > spot)
            def _():
                right_copy(right, found_ref.at[right]).wait_send()

            @pl.when(left < spot)
            def _():
                left_copy(left, found_ref.at[left]).wait_send()

    task = Task(
        [found],
        [struct((rows, wide * columns), found.dtype)],
        [pltpu.VMEM(found.shape, found.dtype)] * 2
        + [pltpu.VMEM(found.shape[1:], found.dtype)]
        + [sems(deep)] * 4
        + [sems(wide - 1), sems(wide), sems()],
        steps,
        VMEM,
        ANY,
        ["narrow", "wide"],
    )
    return task


def return_rows(rows):
    deep, wide = lax.axis_size("narrow"), lax.axis_size("wide")
    count, width = rows.shape
    columns = width // wide

    def steps(ins, outs, scratch):
        (rows_ref,), (out_ref,) = ins, outs
        send_right, send_left, receive_deep, send_wide, receive_wide, local = scratch
        spot = lax.axis_index("narrow")
        me = lax.axis_index("wide")
        part_of = functools.partial(columns_of(columns), rows_ref)

        def landing(device):
            return out_ref.at[spot, pl.ds(pl.multiple_of(device * count, count), count)]

        copies = []
        for step in range(1, wide):
            peer = lax.rem(me + step, wide)
            copy = push(
                part_of(peer),
                landing(me),
                send_wide.at[step - 1],
                receive_wide.at[me],
                {"wide": peer},
            )
            copy.start()
            copies.append(copy)
        keep = pltpu.make_async_copy(part_of(me), landing(me), local)
        keep.start()
        yield
        for step in range(1, wide):
            source = lax.rem(me - step + wide, wide)
            arrived(landing(source), send_wide.at[0], receive_wide.at[source], {"wide": source})
        keep.wait()

        def right_copy(part):
            return push(
                out_ref.at[part],
                out_ref.at[part],
                send_right.at[part],
                receive_deep.at[part],
                {"narrow": lax.rem(spot + 1, deep)},
            )

        def left_copy(part):
            return push(
                out_ref.at[part],
                out_ref.at[part],
                send_left.at[part],
                receive_deep.at[part],
                {"narrow": lax.rem(spot + deep - 1, deep)},
            )

        @pl.when(spot < deep - 1)
        def _():
            right_copy(spot).start()

        @pl.when(spot > 0)
        def _():
            left_copy(spot).start()

        for step in range(1, deep):
            yield

            @pl.when(spot >= step)
            def _():
                right_copy(spot - step).wait_recv()

                @pl.when(spot < deep - 1)
                def _():
                    right_copy(spot - step).start()

            @pl.when(spot + step < deep)
            def _():
                left_copy(spot + step).wait_recv()

                @pl.when(spot > 0)
                def _():
                    left_copy(spot + step).start()

        for part in range(deep):

            @pl.when((part <= spot) & (spot < deep - 1))
            def _():
                right_copy(part).wait_send()

            @pl.when((part >= spot) & (spot > 0))
            def _():
                left_copy(part).wait_send()

        for copy in copies:
            copy.wait_send()

    return Task(
        [rows],
        [struct((deep, wide * count, columns), rows.dtype)],
        [sems(deep)] * 3 + [sems(wide - 1), sems(wide), sems()],
        steps,
        ANY,
        ANY,
        ["narrow", "wide"],
    )


def sum_wide(partial):
    count = lax.axis_size("wide")
    chips = count // 2
    rows, width = partial.shape[0] // count, partial.shape[1]

    def steps(ins, outs, scratch):
        (parts_ref,), (out_ref,) = ins, outs
        from_mate, paired, slots, send_mate, receive_mate, send, receive = scratch
        me = lax.axis_index("wide")
        side = lax.rem(me, 2)
        mate = me + 1 - 2 * side
        my_chip = me // 2
        mate_copies = []
        for step in range(chips):
            chip = lax.rem(my_chip + 1 + step, chips)
            copy = push(
                parts_ref.at[2 * chip + 1 - side],
                from_mate.at[chip],
                send_mate.at[step],
                receive_mate.at[chip],
                {"wide": mate},
            )
            copy.start()
            mate_copies.append(copy)
        yield
        copies = []
        for step in range(chips):
            chip = lax.rem(my_chip + 1 + step, chips)
            arrived(from_mate.at[chip], send_mate.at[0], receive_mate.at[chip], {"wide": mate})
            both = parts_ref[2 * chip + side].astype(FULL) + from_mate[chip].astype(FULL)
            if step < chips - 1:
                paired[chip] = both.astype(LOW)
                copy = push(
                    paired.at[chip],
                    slots.at[my_chip],
                    send.at[step],
                    receive.at[my_chip],
                    {"wide": 2 * chip + side},
                )
                copy.start()
                copies.append(copy)
            else:
                out_ref[...] = both
        yield
        for step in range(1, chips):
            chip = lax.rem(my_chip - step + chips, chips)
            arrived(slots.at[chip], send.at[0], receive.at[chip], {"wide": 2 * chip + side})
            out_ref[...] = out_ref[...] + slots[chip].astype(FULL)
        for copy in mate_copies + copies:
            copy.wait_send()

    return Task(
        [partial.reshape(count, rows, width)],
        [struct((rows, width), FULL)],
        [pltpu.VMEM((chips, rows, width), LOW)] * 3
        + [sems(chips), sems(chips), sems(max(chips - 1, 1)), sems(chips)],
        steps,
        VMEM,
        VMEM,
        ["wide"],
    )


def merge_stats(first, second):
    peak = jnp.maximum(first[0:1], second[0:1])
    total = first[1:2] * jnp.exp(first[0:1] - peak) + second[1:2] * jnp.exp(second[0:1] - peak)
    return jnp.concatenate([peak, total, first[2:3] + second[2:3]], axis=0)


def add_two(first, second):
    return first + second


def combine(values, join):
    deep, wide = lax.axis_size("narrow"), lax.axis_size("wide")

    def steps(ins, outs, scratch):
        (x_ref,), (out_ref,) = ins, outs
        wide_slots, deep_slots, send_wide, receive_wide, send_deep, receive_deep = scratch

        def start(axis, count, slots, value, send, receive):
            me = lax.axis_index(axis)
            slots[me] = value
            copies = []
            for step in range(1, count):
                peer = lax.rem(me + step, count)
                copy = push(
                    slots.at[me], slots.at[me], send.at[step - 1], receive.at[me], {axis: peer}
                )
                copy.start()
                copies.append(copy)
            return copies

        def finish(axis, count, slots, send, receive):
            me = lax.axis_index(axis)
            for step in range(1, count):
                source = lax.rem(me - step + count, count)
                arrived(slots.at[source], send.at[0], receive.at[source], {axis: source})
            total = slots[0]
            for source in range(1, count):
                total = join(total, slots[source])
            return total

        first = start("wide", wide, wide_slots, x_ref[...], send_wide, receive_wide)
        yield
        total = finish("wide", wide, wide_slots, send_wide, receive_wide)
        second = start("narrow", deep, deep_slots, total, send_deep, receive_deep)
        yield
        out_ref[...] = finish("narrow", deep, deep_slots, send_deep, receive_deep)
        for copy in first + second:
            copy.wait_send()

    return Task(
        [values],
        [like(values)],
        [
            pltpu.VMEM((wide,) + values.shape, values.dtype),
            pltpu.VMEM((deep,) + values.shape, values.dtype),
            sems(wide - 1),
            sems(wide),
            sems(deep - 1),
            sems(deep),
        ],
        steps,
        VMEM,
        VMEM,
        ["narrow", "wide"],
    )


def gather_both(values):
    deep, wide = lax.axis_size("narrow"), lax.axis_size("wide")

    def steps(ins, outs, scratch):
        (x_ref,), (out_ref,) = ins, outs
        send_wide, receive_wide, send_deep, receive_deep = scratch
        me = lax.axis_index("wide")
        spot = lax.axis_index("narrow")
        out_ref[spot, me] = x_ref[...]
        copies = []
        for step in range(1, wide):
            peer = lax.rem(me + step, wide)
            block = out_ref.at[spot, me]
            copy = push(block, block, send_wide.at[step - 1], receive_wide.at[me], {"wide": peer})
            copy.start()
            copies.append(copy)
        yield
        for step in range(1, wide):
            source = lax.rem(me - step + wide, wide)
            block = out_ref.at[spot, source]
            arrived(block, send_wide.at[0], receive_wide.at[source], {"wide": source})
        for step in range(1, deep):
            peer = lax.rem(spot + step, deep)
            block = out_ref.at[spot]
            copy = push(
                block, block, send_deep.at[step - 1], receive_deep.at[spot], {"narrow": peer}
            )
            copy.start()
            copies.append(copy)
        yield
        for step in range(1, deep):
            source = lax.rem(spot - step + deep, deep)
            block = out_ref.at[source]
            arrived(block, send_deep.at[0], receive_deep.at[source], {"narrow": source})
        for copy in copies:
            copy.wait_send()

    return Task(
        [values],
        [struct((deep, wide) + values.shape, values.dtype)],
        [sems(wide - 1), sems(wide), sems(deep - 1), sems(deep)],
        steps,
        VMEM,
        VMEM,
        ["narrow", "wide"],
    )


def turn_heads(values, cosine, sine):
    half = values.shape[1] // 2
    swapped = jnp.concatenate([values[:, half:], values[:, :half]], axis=1)
    return values * cosine + swapped * sine


def wide_angles(cosine, sine):
    return jnp.concatenate([cosine, cosine], axis=1), jnp.concatenate([-sine, sine], axis=1)


def local_call(body, inputs, specs, outputs, flops, name):
    return pl.pallas_call(
        body,
        grid=(1,),
        in_specs=specs,
        out_specs=[
            pl.BlockSpec(a.shape, lambda step, rank=len(a.shape): (0,) * rank) for a in outputs
        ],
        out_shape=outputs,
        compiler_params=pltpu.CompilerParams(vmem_limit_bytes=VMEM_BYTES),
        cost_estimate=pl.CostEstimate(flops=flops, bytes_accessed=8 << 20, transcendentals=0),
        name=name,
    )(*inputs)


def entire(values):
    return pl.BlockSpec(values.shape, lambda step: (0,) * values.ndim)


def column_block(values, size, index):
    return pl.BlockSpec((values.shape[0], size), lambda step: (0, index))


def heads_body(groups, rep, rows_ref, gain_ref, kv_ref, cos_ref, sin_ref, out_ref, normed_ref):
    count, _, _, tok_rows, head = out_ref.shape
    size = kv_ref.shape[1] // (2 * count)
    per_head = head // size
    rows = rows_ref[0:tok_rows, :].astype(FULL)
    normed = norm_rows(rows, gain_ref[...]).astype(LOW)
    normed_ref[...] = normed
    both = dot(normed, kv_ref[...], 1, 0)

    def head_of(kind, index):
        pieces = [
            both[:, (2 * part + kind) * size : (2 * part + kind + 1) * size]
            for part in range(index * per_head, (index + 1) * per_head)
        ]
        return pieces[0] if per_head == 1 else jnp.concatenate(pieces, axis=1)

    for owner in range(count):
        for group in range(groups):
            index = (owner * groups + group) // rep
            keys = turn_heads(head_of(0, index), cos_ref[...], sin_ref[...])
            out_ref[owner, group, 0] = keys.astype(LOW)
            out_ref[owner, group, 1] = head_of(1, index).astype(LOW)


def make_heads(rows_low, gain_row, proj, cosine, sine, groups, rep):
    count = lax.axis_size("narrow")
    tok_rows, head = cosine.shape
    width = rows_low.shape[1]
    size = 2 * KVH * HD
    return local_call(
        functools.partial(heads_body, groups, rep),
        [rows_low, gain_row, proj, cosine, sine],
        [entire(rows_low), entire(gain_row), column_block(proj, size, 0)]
        + [entire(cosine), entire(sine)],
        [struct((count, groups, 2, tok_rows, head), LOW), struct((tok_rows, width), LOW)],
        2 * tok_rows * width * size,
        "make_heads",
    )


def attend_body(
    start_ref,
    gains_ref,
    q_ref,
    o_ref,
    kv_ref,
    cos_ref,
    sin_ref,
    seg_ref,
    seg_all_ref,
    pick_ref,
    queries_ref,
    probs_ref,
    mixed_ref,
    part_ref,
    normed_ref,
    early_ref,
):
    count, groups, _, tok_rows, head = kv_ref.shape
    heads_own = probs_ref.shape[0]
    start = start_ref[...].astype(FULL)
    root = lax.rsqrt(jnp.mean(start * start, axis=-1, keepdims=True) + NORM_EPS)
    normed = (start * root * gains_ref[0:1, :]).astype(LOW)
    normed_ref[...] = normed
    early_ref[...] = (start * root * gains_ref[2:3, :]).astype(LOW)
    queries = dot(normed, q_ref[...], 1, 0)
    spots = lax.broadcasted_iota(jnp.int32, (1, count * tok_rows), 1)
    allowed = (seg_ref[...] == seg_all_ref[...]) & (pick_ref[...] >= spots)
    for group in range(groups):
        keys = jnp.concatenate([kv_ref[part, group, 0] for part in range(count)], axis=0)
        values = jnp.concatenate([kv_ref[part, group, 1] for part in range(count)], axis=0)
        for member in range(heads_own // groups):
            at = group * (heads_own // groups) + member
            spot = slice(at * head, (at + 1) * head)
            query = turn_heads(queries[:, spot], cos_ref[...], sin_ref[...]).astype(LOW)
            queries_ref[:, spot] = query
            scores = jnp.where(allowed, dot(query, keys, 1, 1) * head ** (-0.5), MASKED)
            shifted = jnp.exp(scores - jnp.max(scores, axis=-1, keepdims=True))
            probs = shifted / jnp.sum(shifted, axis=-1, keepdims=True)
            probs_ref[at] = probs
            mixed_ref[:, spot] = dot(probs.astype(LOW), values, 1, 0).astype(LOW)
    part_ref[...] = dot(mixed_ref[...], o_ref[...], 1, 1).astype(LOW)


def attend(start_low, gains, proj, own_head, cosine, sine, seg, seg_all, picks):
    count, groups, _, tok_rows, head = own_head.shape
    sel, width = start_low.shape
    heads_own = HEADS // count
    size = heads_own * head
    first = 2 * KVH * HD // size
    seq_len = count * tok_rows
    return local_call(
        attend_body,
        [start_low, gains, proj, proj, own_head, cosine, sine, seg, seg_all, picks],
        [
            entire(start_low),
            entire(gains),
            column_block(proj, size, first),
            column_block(proj, size, first + 1),
        ]
        + [entire(a) for a in (own_head, cosine, sine, seg, seg_all, picks)],
        [
            struct((sel, size), LOW),
            struct((heads_own, sel, seq_len), FULL),
            struct((sel, size), LOW),
            struct((sel, width), LOW),
            struct((sel, width), LOW),
            struct((sel, width), LOW),
        ],
        4 * sel * size * (width + seq_len),
        "attend",
    )


def attend_back_body(
    grad_ref,
    q_ref,
    o_ref,
    kv_ref,
    queries_ref,
    probs_ref,
    cos_ref,
    sin_ref,
    cos_all_ref,
    sin_all_ref,
    start_ref,
    gains_ref,
    early_ref,
    out_ref,
    grad_q_ref,
    part_ref,
    attn_gain_ref,
    early_gain_ref,
):
    count, groups, _, tok_rows, head = kv_ref.shape
    heads_own = probs_ref.shape[0]
    scale = head ** (-0.5)
    grad_mixed = dot(grad_ref[...], o_ref[...], 1, 0).astype(LOW)
    for group in range(groups):
        keys = jnp.concatenate([kv_ref[part, group, 0] for part in range(count)], axis=0)
        values = jnp.concatenate([kv_ref[part, group, 1] for part in range(count)], axis=0)
        grad_keys = jnp.zeros(keys.shape, FULL)
        grad_values = jnp.zeros(keys.shape, FULL)
        for member in range(heads_own // groups):
            at = group * (heads_own // groups) + member
            spot = slice(at * head, (at + 1) * head)
            probs = probs_ref[at]
            grad_probs = dot(grad_mixed[:, spot], values, 1, 1)
            inner = jnp.sum(probs * grad_probs, axis=-1, keepdims=True)
            grad_scores = (probs * (grad_probs - inner)).astype(LOW)
            grad_query = dot(grad_scores, keys, 1, 0) * scale
            grad_q_ref[:, spot] = turn_heads(grad_query, cos_ref[...], -sin_ref[...]).astype(LOW)
            grad_keys = grad_keys + dot(grad_scores, queries_ref[:, spot], 0, 0)
            grad_values = grad_values + dot(probs.astype(LOW), grad_mixed[:, spot], 0, 0)
        grad_keys = turn_heads(grad_keys * scale, cos_all_ref[...], -sin_all_ref[...])
        for part in range(count):
            rows = slice(part * tok_rows, (part + 1) * tok_rows)
            out_ref[part, group, 0] = grad_keys[rows].astype(LOW)
            out_ref[part, group, 1] = grad_values[rows].astype(LOW)
    pick = dot(grad_q_ref[...], q_ref[...], 1, 1)
    early = early_ref[...].astype(FULL)
    start = start_ref[...].astype(FULL)
    start = start * lax.rsqrt(jnp.mean(start * start, axis=-1, keepdims=True) + NORM_EPS)
    attn_gain_ref[...] = jnp.sum(start * pick, axis=0, keepdims=True)
    early_gain_ref[...] = jnp.sum(start * early, axis=0, keepdims=True)
    part_ref[...] = (gains_ref[0:1, :] * pick + gains_ref[2:3, :] * early).astype(LOW)


def attend_back(
    grad,
    proj,
    own_head,
    queries,
    probs,
    cosine,
    sine,
    cosine_all,
    sine_all,
    start_low,
    gains,
    early,
):
    count, groups, _, tok_rows, head = own_head.shape
    sel, width = grad.shape
    size = queries.shape[1]
    first = 2 * KVH * HD // size
    return local_call(
        attend_back_body,
        [grad, proj, proj, own_head, queries, probs, cosine, sine, cosine_all, sine_all]
        + [start_low, gains, early],
        [entire(grad), column_block(proj, size, first), column_block(proj, size, first + 1)]
        + [
            entire(a)
            for a in (own_head, queries, probs, cosine, sine, cosine_all, sine_all)
            + (start_low, gains, early)
        ],
        [struct(own_head.shape, LOW), struct((sel, size), LOW), struct((sel, width), LOW)]
        + [struct((1, width), FULL)] * 2,
        8 * sel * size * width,
        "attend_back",
    )


def norm_back_rows(values, gain_row, grad):
    root = lax.rsqrt(jnp.mean(values * values, axis=-1, keepdims=True) + NORM_EPS)
    scaled = gain_row * grad
    inner = jnp.mean(values * scaled, axis=-1, keepdims=True)
    result = root * scaled - values * (root * root * root * inner)
    return result, jnp.sum(values * root * grad, axis=0, keepdims=True)


def rows_back_body(
    rep,
    rows_ref,
    gains_ref,
    kv_ref,
    heads_ref,
    pick_ref,
    base_ref,
    out_ref,
    gain_grad_ref,
    grad_kv_ref,
):
    count, groups, _, tok_rows, head = heads_ref.shape
    size = kv_ref.shape[1] // (2 * count)
    per_head = head // size
    for index in range(KVH):
        for kind in range(2):
            copies = [
                heads_ref[at // groups, at % groups, kind]
                for at in range(index * rep, (index + 1) * rep)
            ]
            total = copies[0]
            if rep > 1:
                total = sum(copy.astype(FULL) for copy in copies).astype(LOW)
            for piece in range(per_head):
                lane = (2 * (index * per_head + piece) + kind) * size
                grad_kv_ref[:, lane : lane + size] = total[:, piece * size : (piece + 1) * size]
    values = rows_ref[...].astype(FULL)
    own = values[tok_rows:]
    tok_part, tok_gain = norm_back_rows(
        values[:tok_rows], gains_ref[0:1, :], dot(grad_kv_ref[...], kv_ref[...], 1, 1)
    )
    pick_part, _ = norm_back_rows(own, 1.0, pick_ref[...])
    gain_grad_ref[...] = tok_gain
    out_ref[0:tok_rows, :] = tok_part.astype(LOW)
    out_ref[tok_rows:, :] = (pick_part + base_ref[...]).astype(LOW)


def rows_back(rows_low, gains, proj, heads, grad_pick, base, rep):
    tok_rows = heads.shape[3]
    width = rows_low.shape[1]
    size = 2 * KVH * HD
    return local_call(
        functools.partial(rows_back_body, rep),
        [rows_low, gains, proj, heads, grad_pick, base],
        [entire(rows_low), entire(gains), column_block(proj, size, 0)]
        + [entire(a) for a in (heads, grad_pick, base)],
        [
            struct(rows_low.shape, LOW),
            struct((1, width), FULL),
            struct((tok_rows, size), LOW),
        ],
        2 * tok_rows * width * size,
        "rows_back",
    )


def assemble_body(out_columns, *refs):
    pieces, out_ref = refs[:-1], refs[-1]
    count = len(pieces)
    me = lax.axis_index("narrow")
    for step, piece in enumerate(pieces):
        source = lax.rem(me - step + count, count)
        spot = pl.ds(pl.multiple_of(source * out_columns, out_columns), out_columns)
        out_ref[:, spot] = piece[...]


def assemble(pieces):
    rows, columns = pieces[0].shape
    outputs = [struct((rows, columns * len(pieces)), pieces[0].dtype)]
    return local_call(
        functools.partial(assemble_body, columns),
        list(pieces),
        [entire(piece) for piece in pieces],
        outputs,
        0,
        "assemble",
    )[0]


def feed_body(inner_ref, weight_ref, gate_ref, up_ref, hidden_ref, out_ref, total):
    part = pl.program_id(0)
    inner = inner_ref[...]
    gate = dot(inner, weight_ref[0, 0], 1, 1)
    up = dot(inner, weight_ref[0, 1], 1, 1)
    hidden = (jax.nn.silu(gate) * up).astype(LOW)
    gate_ref[0] = gate
    up_ref[0] = up
    hidden_ref[0] = hidden
    product = dot(hidden, weight_ref[0, 2], 1, 0)

    @pl.when(part == 0)
    def _():
        total[...] = product

    @pl.when(part > 0)
    def _():
        total[...] = total[...] + product

    @pl.when(part == pl.num_programs(0) - 1)
    def _():
        out_ref[...] = total[...].astype(LOW)


def feed(inner, weight):
    parts, _, size, width = weight.shape
    sel = inner.shape[0]
    same = pl.BlockSpec((sel, width), lambda part: (0, 0))
    slab = pl.BlockSpec((1, sel, size), lambda part: (part, 0, 0))
    return pl.pallas_call(
        feed_body,
        grid=(parts,),
        in_specs=[same, pl.BlockSpec((1, 3, size, width), lambda part: (part, 0, 0, 0))],
        out_specs=[slab, slab, slab, same],
        out_shape=[
            struct((parts, sel, size), FULL),
            struct((parts, sel, size), FULL),
            struct((parts, sel, size), LOW),
            struct((sel, width), LOW),
        ],
        scratch_shapes=[pltpu.VMEM((sel, width), FULL)],
        compiler_params=pltpu.CompilerParams(vmem_limit_bytes=VMEM_BYTES),
        cost_estimate=pl.CostEstimate(
            flops=6 * sel * parts * size * width,
            bytes_accessed=weight.size * 2,
            transcendentals=0,
        ),
        name="feed",
    )(inner, weight)


def feed_back_body(grad_ref, weight_ref, gate_ref, up_ref, hidden_ref, acts_ref, out_ref, total):
    part = pl.program_id(0)
    grad_hidden = dot(grad_ref[...], weight_ref[0, 2], 1, 1)
    gate = gate_ref[0]
    sigma = jax.nn.sigmoid(gate)
    grad_gate = (grad_hidden * up_ref[0] * sigma * (1.0 + gate * (1.0 - sigma))).astype(LOW)
    grad_up = (grad_hidden * gate * sigma).astype(LOW)
    acts_ref[0, 0] = grad_gate
    acts_ref[0, 1] = grad_up
    acts_ref[0, 2] = hidden_ref[0]
    product = dot(grad_gate, weight_ref[0, 0], 1, 0) + dot(grad_up, weight_ref[0, 1], 1, 0)

    @pl.when(part == 0)
    def _():
        total[...] = product

    @pl.when(part > 0)
    def _():
        total[...] = total[...] + product

    @pl.when(part == pl.num_programs(0) - 1)
    def _():
        out_ref[...] = total[...].astype(LOW)


def feed_back(grad, weight, gate, up, hidden):
    parts, _, size, width = weight.shape
    sel = grad.shape[0]
    same = pl.BlockSpec((sel, width), lambda part: (0, 0))
    slab = pl.BlockSpec((1, sel, size), lambda part: (part, 0, 0))
    return pl.pallas_call(
        feed_back_body,
        grid=(parts,),
        in_specs=[same, pl.BlockSpec((1, 3, size, width), lambda part: (part, 0, 0, 0))]
        + [slab] * 3,
        out_specs=[pl.BlockSpec((1, 3, sel, size), lambda part: (part, 0, 0, 0)), same],
        out_shape=[struct((parts, 3, sel, size), LOW), struct((sel, width), LOW)],
        scratch_shapes=[pltpu.VMEM((sel, width), FULL)],
        compiler_params=pltpu.CompilerParams(vmem_limit_bytes=VMEM_BYTES),
        cost_estimate=pl.CostEstimate(
            flops=6 * sel * parts * size * width,
            bytes_accessed=weight.size * 2,
            transcendentals=0,
        ),
        name="feed_back",
    )(grad, weight, gate, up, hidden)


def newton_steps(problems):
    rows, width = problems[0][0].shape
    block = min(1024, width)
    eye = lax.broadcasted_iota(jnp.int32, (rows, rows), 0) == lax.broadcasted_iota(
        jnp.int32, (rows, rows), 1
    )

    def strip(part):
        return pl.ds(pl.multiple_of(part * block, block), block)

    def over(function, start):
        return lax.fori_loop(0, width // block, function, start)

    def add_squares(part, totals):
        values = [current[:, strip(part)] for current, low, gram, rest in problems]
        return [total + jnp.sum(value * value) for total, value in zip(totals, values)]

    totals = over(add_squares, [jnp.float32(0.0)] * len(problems))
    scales = [1.0 / (jnp.sqrt(total) + 1e-07) for total in totals]

    def begin(part, carry):
        for scale, (current, low, gram, rest) in zip(scales, problems):
            values = current[:, strip(part)] * scale
            current[:, strip(part)] = values
            low[:, strip(part)] = values.astype(LOW)
        return carry

    over(begin, 0)

    def iteration(turn, carry):
        for current, low, gram, rest in problems:
            gram[...] = jnp.zeros_like(gram)

        def add_gram(part, carry):
            for current, low, gram, rest in problems:
                values = low[:, strip(part)]
                gram[...] = gram[...] + dot(values, values, 1, 1)
            return carry

        over(add_gram, 0)
        seconds = []
        for current, low, gram, rest in problems:
            whole = gram[...]
            middle = jnp.sum(jnp.where(eye, whole, 0.0)) / rows
            rest[...] = (whole - jnp.where(eye, middle, 0.0)).astype(LOW)
            square = dot(rest[...], rest[...], 1, 0)
            whole = gram[...]
            centred = whole - jnp.where(eye, middle, 0.0)
            square = square + 2.0 * middle * centred + jnp.where(eye, middle * middle, 0.0)
            whole = NEWTON_B * whole + NEWTON_C * square
            second = jnp.sum(jnp.where(eye, whole, 0.0)) / rows
            rest[...] = (whole - jnp.where(eye, second, 0.0)).astype(LOW)
            seconds.append(second)

        def apply(part, carry):
            for second, (current, low, gram, rest) in zip(seconds, problems):
                values = (NEWTON_A + second) * current[:, strip(part)] + dot(
                    rest[...], low[:, strip(part)], 1, 0
                )
                current[:, strip(part)] = values
                low[:, strip(part)] = values.astype(LOW)
            return carry

        over(apply, 0)
        return carry

    lax.fori_loop(0, NS_STEPS, iteration, 0)


def newton_scratch(rows, width):
    return [
        pltpu.VMEM((rows, width), FULL),
        pltpu.VMEM((rows, width), LOW),
        pltpu.VMEM((rows, rows), FULL),
        pltpu.VMEM((rows, rows), LOW),
    ]


def newton_cost(count, rows, width):
    return pl.CostEstimate(
        flops=NS_STEPS * count * (4 * rows * rows * width + 2 * rows * rows * rows),
        bytes_accessed=6 * count * rows * width,
        transcendentals=0,
    )


def newton_body(factor_ref, mom_ref, grad_ref, out_ref, *problem):
    current, low = problem[:2]
    parts, rows, columns = mom_ref.shape
    factor = factor_ref[0]
    size = grad_ref.shape[1]
    for part in range(parts):
        spot = slice(part * columns, (part + 1) * columns)
        for source in range(parts):
            here = slice(source * size, (source + 1) * size)
            current[here, spot] = MOMENTUM * mom_ref[part, here, :].astype(
                FULL
            ) + factor * grad_ref[source, :, spot].astype(FULL)
    newton_steps([problem])
    for part in range(parts):
        out_ref[part] = low[:, part * columns : (part + 1) * columns]


def newton_small_body(rows, factor_ref, mom_ref, grad_ref, kv_ref, out_ref, *scratch):
    problems = [scratch[4 * at : 4 * at + 4] for at in range(4)]
    parts, _, columns = mom_ref.shape
    kv_columns = kv_ref.shape[2]
    half = rows // 2
    factor = factor_ref[0]
    for part in range(parts):
        spot = slice(part * columns, (part + 1) * columns)
        for member in range(2):
            current = problems[member][0]
            here = slice(member * rows, (member + 1) * rows)
            mom, grad = mom_ref[part, here, :], grad_ref[part, here, :]
            current[:, spot] = MOMENTUM * mom.astype(FULL) + factor * grad.astype(FULL)
        spot = slice(part * kv_columns, (part + 1) * kv_columns)
        for member in range(2):
            current = problems[2 + member][0]
            piece = kv_ref[part, member * rows : (member + 1) * rows, :].astype(FULL)
            for side in range(2):
                lane = (2 * member + side) * kv_columns
                mom = mom_ref[part, 2 * rows : 2 * rows + half, lane : lane + kv_columns]
                here = slice(side * half, (side + 1) * half)
                current[here, spot] = MOMENTUM * mom.astype(FULL) + factor * piece[here]
    newton_steps(problems[:2])
    newton_steps(problems[2:])
    out_ref[...] = jnp.zeros_like(out_ref)
    for part in range(parts):
        for member in range(2):
            out_ref[part, member * rows : (member + 1) * rows, :] = problems[member][1][
                :, part * columns : (part + 1) * columns
            ]
            low = problems[2 + member][1]
            for side in range(2):
                lane = (2 * member + side) * kv_columns
                out_ref[part, 2 * rows : 2 * rows + half, lane : lane + kv_columns] = low[
                    side * half : (side + 1) * half,
                    part * kv_columns : (part + 1) * kv_columns,
                ]


def newton_any_body(rows, factor_ref, mom_ref, grad_ref, qo_ref, kv_ref, out_ref, *scratch):
    parts = mom_ref.shape[0]
    owner = lax.rem(3 + lax.rem(lax.axis_index("wide"), 2), parts)
    small = lax.axis_index("narrow") == owner

    @pl.when(small)
    def _():
        newton_small_body(rows, factor_ref, mom_ref, qo_ref, kv_ref, out_ref, *scratch[4:])

    @pl.when(jnp.logical_not(small))
    def _():
        newton_body(factor_ref, mom_ref, grad_ref, out_ref, *scratch[:4])


def newton(factor, mom, grad, qo_grad, kv_grad):
    parts, slot_rows, columns = mom.shape
    width = parts * columns
    rows = kv_grad.shape[1] // 2
    kv_width = parts * kv_grad.shape[2]
    return pl.pallas_call(
        functools.partial(newton_any_body, rows),
        in_specs=[pl.BlockSpec(memory_space=pltpu.SMEM)] + [VMEM] * 4,
        out_specs=VMEM,
        out_shape=struct(mom.shape, LOW),
        scratch_shapes=newton_scratch(slot_rows, width)
        + newton_scratch(rows, width) * 2
        + newton_scratch(rows, kv_width) * 2,
        compiler_params=pltpu.CompilerParams(vmem_limit_bytes=VMEM_BYTES),
        cost_estimate=newton_cost(1, slot_rows, width),
        name="newton",
    )(factor.reshape(1), mom, grad, qo_grad, kv_grad)


def lookup_body(ids_ref, turn_ref, table_ref, out_ref, low_ref, list_ref, held, rows, sem):
    vocab = table_ref.shape[0]
    count = out_ref.shape[0]
    load = pltpu.make_async_copy(table_ref, held, sem)
    load.start()
    rows[...] = jnp.zeros_like(rows)

    found = turn_ref[count]

    def note(group, carry):
        for member in range(UNROLL):
            at = group * UNROLL + member
            list_ref[turn_ref[at]] = at
        return carry

    lax.fori_loop(0, count // UNROLL, note, 0)
    for member in range(UNROLL):
        list_ref[found + member] = count
    list_ref[count + UNROLL] = found
    load.wait()

    def step(group, carry):
        for member in range(UNROLL):
            at = list_ref[group * UNROLL + member]
            spot = jnp.minimum(ids_ref[jnp.minimum(at, count - 1)], vocab - 1)
            rows[pl.ds(at, 1), :] = held[pl.ds(spot, 1), :]
        return carry

    lax.fori_loop(0, (found + UNROLL - 1) // UNROLL, step, 0)
    out_ref[...] = rows[pl.ds(0, count), :].astype(LOW)
    low_ref[...] = held[...].astype(LOW)


def lookup(table, ids):
    vocab, columns = table.shape
    count = ids.shape[0]
    mine = (ids < vocab).reshape(-1, 128)
    before = jnp.arange(128)[:, None] < jnp.arange(128)[None, :]
    in_row = dot(mine.astype(LOW), before.astype(LOW), 1, 0)
    per_row = jnp.sum(mine.astype(FULL), axis=1)
    lines = jnp.arange(mine.shape[0])
    ahead = jnp.sum(jnp.where(lines[:, None] > lines[None, :], per_row[None, :], 0.0), axis=1)
    found = jnp.sum(per_row).astype(jnp.int32)
    turns = (in_row + ahead[:, None]).astype(jnp.int32)
    turns = jnp.where(mine, turns, count + UNROLL + 1).reshape(-1)
    turns = jnp.concatenate([turns, jnp.full((128,), found)])
    return pl.pallas_call(
        lookup_body,
        in_specs=[pl.BlockSpec(memory_space=pltpu.SMEM)] * 2 + [ANY],
        out_specs=[VMEM, VMEM, pl.BlockSpec(memory_space=pltpu.SMEM)],
        scratch_shapes=[
            pltpu.VMEM((vocab, columns), FULL),
            pltpu.VMEM((count + 8, columns), FULL),
            pltpu.SemaphoreType.DMA,
        ],
        out_shape=[
            struct((count, columns), LOW),
            struct((vocab, columns), LOW),
            struct((count + 2 * UNROLL,), jnp.int32),
        ],
        compiler_params=pltpu.CompilerParams(vmem_limit_bytes=VMEM_BYTES),
        cost_estimate=pl.CostEstimate(
            flops=0, bytes_accessed=vocab * columns * 4, transcendentals=0
        ),
        name="lookup",
    )(ids, turns, table)


def spread_body(
    ids_ref, list_ref, rows_ref, head_ref, out_ref, square_ref, even, odd, rows, sem
):
    vocab = out_ref.shape[0]
    count = rows_ref.shape[0]
    chunk = 256

    def strip(part):
        return pl.ds(pl.multiple_of(part * chunk, chunk), chunk)

    def begin(part, carry):
        even[strip(part), :] = head_ref[strip(part), :].astype(FULL)
        odd[strip(part), :] = jnp.zeros((chunk, odd.shape[1]), FULL)
        return carry

    lax.fori_loop(0, vocab // chunk, begin, 0)

    def widen(part, carry):
        rows[strip(part), :] = rows_ref[strip(part), :].astype(FULL)
        return carry

    lax.fori_loop(0, count // chunk, widen, 0)
    rows[pl.ds(count, 8), :] = jnp.zeros((8, rows.shape[1]), FULL)

    def step(group, carry):
        for member in range(UNROLL):
            at = list_ref[group * UNROLL + member]
            spot = jnp.minimum(ids_ref[jnp.minimum(at, count - 1)], vocab - 1)
            total = even if member % 2 == 0 else odd
            total[pl.ds(spot, 1), :] = total[pl.ds(spot, 1), :] + rows[pl.ds(at, 1), :]
        return carry

    found = list_ref[count + UNROLL]
    lax.fori_loop(0, (found + UNROLL - 1) // UNROLL, step, 0)

    def finish(part, squares):
        value = even[strip(part), :] + odd[strip(part), :]
        even[strip(part), :] = value
        return squares + jnp.sum((value * value).reshape(chunk // 8, 8, -1), axis=0)

    square_ref[...] = lax.fori_loop(
        0, vocab // chunk, finish, jnp.zeros((8, even.shape[1]), FULL)
    )
    store = pltpu.make_async_copy(even, out_ref, sem)
    store.start()
    store.wait()


def spread(ids, listed, rows, head):
    vocab, columns = head.shape
    count = ids.shape[0]
    smem = pl.BlockSpec(memory_space=pltpu.SMEM)
    return pl.pallas_call(
        spread_body,
        in_specs=[smem, smem, VMEM, VMEM],
        out_specs=[ANY, VMEM],
        scratch_shapes=[
            pltpu.VMEM((vocab, columns), FULL),
            pltpu.VMEM((vocab, columns), FULL),
            pltpu.VMEM((count + 8, columns), FULL),
            pltpu.SemaphoreType.DMA,
        ],
        out_shape=[struct((vocab, columns), FULL), struct((8, columns), FULL)],
        compiler_params=pltpu.CompilerParams(vmem_limit_bytes=VMEM_BYTES),
        cost_estimate=pl.CostEstimate(
            flops=count * columns, bytes_accessed=vocab * columns * 8, transcendentals=0
        ),
        name="spread",
    )(ids, listed, rows, head)


def adamw(weight, first_m, second_m, grad, rate, decay):
    first_new = BETA_ONE * first_m + (1.0 - BETA_ONE) * grad
    second_new = BETA_TWO * second_m + (1.0 - BETA_TWO) * grad * grad
    update = (
        first_new
        / (1.0 - BETA_ONE**STEP)
        / (jnp.sqrt(second_new / (1.0 - BETA_TWO**STEP)) + ADAM_EPS)
    )
    return (weight * (1.0 - rate * decay) - rate * update, first_new, second_new)


def cut_columns(values, count):
    rows, columns = values.shape
    return jnp.moveaxis(values.reshape(rows, count, columns // count), 1, 0)


def shifted(parts, axis, step):
    count = lax.axis_size(axis)
    pairs = [(source, (source + step) % count) for source in range(count)]
    return lax.ppermute(parts, axis, pairs)


def per_device(
    tokens,
    picks,
    targets,
    lengths,
    skip,
    embed,
    embed_m,
    embed_v,
    attn_qo,
    attn_qo_mom,
    attn_kv,
    attn_kv_mom,
    ffn,
    ffn_mom,
    gains,
    gains_m,
    gains_v,
):
    wide_count = lax.axis_size("wide")
    narrow_count = lax.axis_size("narrow")
    narrow_spot = lax.axis_index("narrow")
    wide_spot = lax.axis_index("wide")
    seq_len = tokens.shape[1]
    sel = picks.shape[1]
    vocab_rows, columns = embed.shape
    width = columns * wide_count
    own_rows = sel // narrow_count
    tok_rows = seq_len // narrow_count
    all_rows = own_rows + tok_rows
    heads_own = HEADS // narrow_count
    head_cols = heads_own * HD
    repeat = max(1, narrow_count // KVH)
    groups = KVH * repeat // narrow_count
    ffn_rows = ffn.shape[0]
    ffn_size = ffn_rows // narrow_count
    total_rows = wide_count * sel
    lens = lengths[0]
    pick_ids = picks[0]
    keep_layer = (1 - skip[0]).astype(FULL)
    keep_row = jnp.full((1, width), keep_layer)
    lanes = 128

    def box(flat):
        height = -(-flat.shape[0] // (8 * lanes)) * 8
        return jnp.pad(flat, (0, height * lanes - flat.shape[0])).reshape(height, lanes)

    ffn_low = jnp.moveaxis(ffn, 1, 0).astype(LOW)
    ffn_cut = ffn_low.reshape(3, narrow_count, ffn_size, ffn_low.shape[2])
    ffn_cut = jnp.moveaxis(ffn_cut, 1, 0).reshape(narrow_count, 3 * ffn_size, -1)
    kv_own = attn_kv.reshape(columns, -1).astype(LOW)

    where_at = jnp.arange(seq_len, dtype=jnp.int32)
    pick_tokens = jnp.sum(
        jnp.where(pick_ids[:, None] == where_at[None, :], tokens[0][None, :], 0), axis=1
    )
    ints = box(jnp.concatenate([tokens[0], pick_tokens, targets[0]]))
    all_ints, all_gains, kv_part = launch(
        [
            gather_wide(ints),
            gather_both(box(gains.astype(LOW).astype(FULL).reshape(-1))),
            gather_blocks("narrow", kv_own),
        ],
        0,
        "gather_ids",
    )
    kv_part = jnp.moveaxis(kv_part, 0, 1).reshape(columns, -1)
    proj_own = jnp.concatenate([kv_part, attn_qo.reshape(columns, -1).astype(LOW)], axis=1)
    proj = lax.all_gather(proj_own, "wide", axis=0, tiled=True)
    ffn_cut, all_ints = lax.optimization_barrier((ffn_cut, all_ints))
    ffn_pieces = [lax.dynamic_index_in_dim(ffn_cut, narrow_spot, 0, False)] + [
        shifted(
            lax.dynamic_index_in_dim(
                ffn_cut, lax.rem(narrow_spot + step, narrow_count), 0, False
            ),
            "narrow",
            step,
        )
        for step in range(1, narrow_count)
    ]
    gain_size = gains.shape[1]
    gain_w = all_gains.reshape(narrow_count, wide_count, -1)[:, :, : 3 * gain_size]
    gain_w = gain_w.reshape(narrow_count, wide_count, 3, gain_size)
    gain_w = jnp.transpose(gain_w, (2, 1, 0, 3)).reshape(3, width)
    all_ints = all_ints.reshape(wide_count, -1)
    tokens_all = all_ints[:, :seq_len].reshape(wide_count, narrow_count, tok_rows)
    picked_all = all_ints[:, seq_len : seq_len + sel].reshape(wide_count, narrow_count, own_rows)
    targets_all = all_ints[:, seq_len + sel : seq_len + 2 * sel].reshape(-1)
    wanted = jnp.moveaxis(jnp.concatenate([tokens_all, picked_all], axis=2), 1, 0).reshape(-1)
    local_ids = wanted - narrow_spot * vocab_rows
    inside = (local_ids >= 0) & (local_ids < vocab_rows)
    spots = jnp.where(inside, local_ids, vocab_rows)
    found, embed_low, listed = lookup(embed, spots)
    ffn_pieces, found = lax.optimization_barrier((ffn_pieces, found))
    ffn_sub = assemble(ffn_pieces).reshape(3, ffn_size, width)
    ffn_sub, found = lax.optimization_barrier((ffn_sub, found))
    ffn_w = lax.all_gather(ffn_sub, "wide", axis=0)
    found = found.reshape(narrow_count, wide_count * all_rows, columns)
    embed_cut = embed_low.reshape(wide_count, vocab_rows // wide_count, columns)
    third = embed_cut.shape[1] // 48 * 16
    rows_low = launch([fetch_rows(found, all_rows)], 1, "fetch_rows")[0]

    mom_qo = jnp.moveaxis(attn_qo_mom, 1, 0)
    mom_kv = jnp.moveaxis(attn_kv_mom, 1, 0)
    mom_ffn = jnp.moveaxis(ffn_mom, 1, 0)
    slot_rows, slot_cols = mom_ffn.shape[1:]

    block_rows, q_size = mom_qo.shape[1:]
    kv_size = mom_kv.shape[2]
    half_rows = block_rows // 2
    kv_box = jnp.moveaxis(mom_kv.reshape(4, half_rows, kv_size), 0, 1).reshape(half_rows, -1)
    small_box = jnp.concatenate([mom_qo.reshape(2 * block_rows, q_size), kv_box])
    small_box = jnp.pad(small_box, ((0, slot_rows - small_box.shape[0]), (0, 0)))
    mom_parts = jnp.concatenate([mom_ffn, small_box[None]]).astype(LOW)

    seg_all, cosine_all, sine_all = angles_at(lens, where_at)
    cosine_all, sine_all = wide_angles(cosine_all, sine_all)
    seg_mine, cosine, sine = angles_at(lens, pick_ids)
    cosine, sine = wide_angles(cosine, sine)

    def tok_part(angles):
        return lax.dynamic_slice_in_dim(angles, narrow_spot * tok_rows, tok_rows, 0)

    by_head, normed_tok = make_heads(
        rows_low, gain_w[0:1], proj, tok_part(cosine_all), tok_part(sine_all), groups, repeat
    )
    own_head, start_low, table_top = launch(
        [
            swap_blocks("narrow", by_head),
            gather_blocks("narrow", rows_low[tok_rows:]),
            join_columns("wide", embed_cut[:, :third]),
        ],
        2,
        "trade_heads",
    )
    start_low, ffn_w = lax.optimization_barrier((start_low, ffn_w))
    start_low = start_low.reshape(sel, width)
    queries, probs, mixed, attn_part, normed, early_part = attend(
        start_low,
        gain_w,
        proj,
        own_head,
        cosine,
        sine,
        seg_mine[:, None],
        seg_all[None, :],
        pick_ids[:, None],
    )
    early = lax.all_gather(early_part, "wide", axis=0, tiled=True)
    start_own = rows_low[tok_rows:].astype(FULL)
    middle, inner, table_middle = launch(
        [
            settle(
                attn_part,
                start_own,
                start_own,
                jnp.ones((1, width), FULL),
                gain_w[1:2],
            ),
            join_columns("wide", embed_cut[:, third : 2 * third]),
        ],
        3,
        "settle_middle",
    )
    inner = inner.reshape(sel, width)
    inner_all = lax.all_gather(inner, "wide", axis=0, tiled=True)
    gate, up, hidden, fed = feed(inner, ffn_w)
    final_own, late_part, table_low = launch(
        [
            settle(fed, middle, start_own, keep_row, gain_w[2:3]),
            join_columns("wide", embed_cut[:, 2 * third :]),
        ],
        4,
        "settle_late",
    )
    table_own = jnp.concatenate([table_top, table_middle, table_low])

    table_count = table_own.shape[0]
    local_target = targets_all - (narrow_spot * vocab_rows + wide_spot * table_count)
    has_target = jnp.arange(table_count, dtype=jnp.int32)[:, None] == local_target[None, :]
    counted = (targets_all >= 0).astype(FULL)
    loss_count = jnp.sum(counted)

    def exit_logits(features):
        logits = dot(table_own, features, 1, 1)
        peak = jnp.max(logits, axis=0)
        total = jnp.sum(jnp.exp(logits - peak[None, :]), axis=0)
        picked = jnp.sum(jnp.where(has_target, logits, 0.0), axis=0)
        return logits, jnp.stack([peak, total, picked])

    half = slot_rows // 2
    late, mom_top, early_logits, early_stats = launch(
        [
            gather_wide(late_part.reshape(sel, width)),
            swap_turned(mom_parts[:, :half]),
            exit_stats(early, table_own, local_target[None, :]),
        ],
        5,
        "gather_late",
    )
    late = late.reshape(total_rows, width)
    late_logits, late_stats = exit_logits(late)
    stats = jnp.concatenate([early_stats, late_stats], axis=1).reshape(3, 8, -1)
    stats = launch([combine(stats, merge_stats)], 6, "combine_stats")[0]
    stats, inner_all = lax.optimization_barrier((stats, inner_all))
    stats = stats.reshape(3, -1)
    log_norms = stats[0] + jnp.log(stats[1])
    losses = log_norms - stats[2]
    loss_sum = jnp.sum(
        counted * (EXIT_EARLY * losses[:total_rows] + EXIT_LAST * losses[total_rows:])
    )

    def exit_back(logits, log_norm, weight):
        grad_logits = (
            (jnp.exp(logits - log_norm[None, :]) - has_target.astype(FULL))
            * (weight * counted)[None, :]
        ).astype(LOW)
        return grad_logits

    late_grad = exit_back(late_logits, log_norms[total_rows:], EXIT_LAST)
    late_back = dot(late_grad, table_own, 0, 0).astype(LOW)
    early_grad = exit_back(early_logits, log_norms[:total_rows], EXIT_EARLY)
    grad_late, mom_low, early_back, _ = launch(
        [
            sum_wide(late_back),
            swap_turned(mom_parts[:, half:]),
            later(product([early_grad], [table_own], 0, [[(0, 0)]]), 1),
        ],
        7,
        "sum_late",
    )
    mom_owned = jnp.concatenate([mom_top, mom_low], axis=1)
    early_back, grad_late = lax.optimization_barrier((early_back, grad_late))
    grad_early = lax.psum_scatter(early_back[0], "wide", scatter_dimension=0, tiled=True)
    grad_final, gain_late, grad_out, mixed_wide, pick_cols = launch(
        [
            settle_back(
                grad_late.astype(LOW),
                final_own,
                jnp.zeros_like(final_own),
                keep_row,
                gain_w[2:3],
            ),
            gather_wide(mixed),
            split_columns("wide", normed),
        ],
        8,
        "back_late",
    )
    grad_layer = grad_final * keep_layer
    grad_out = grad_out.reshape(sel, width)
    out_all = lax.all_gather(grad_out, "wide", axis=0, tiled=True)
    acts, fed_back = feed_back(grad_out, ffn_w, gate, up, hidden)
    grad_mid, gain_mid, grad_branch, acts, tok_cols = launch(
        [
            settle_back(fed_back, middle, grad_layer, keep_row, gain_w[1:2]),
            swap_blocks("wide", acts),
            split_columns("wide", normed_tok),
        ],
        9,
        "back_middle",
    )
    acts = jnp.moveaxis(acts, 1, 0).reshape(3, total_rows, ffn_size)
    grad_branch, grad_early = lax.optimization_barrier((grad_branch, grad_early))
    grad_branch = grad_branch.reshape(sel, width)

    kv_parts, grad_queries, pick_part, gain_pick, gain_early = attend_back(
        grad_branch,
        proj,
        own_head,
        queries,
        probs,
        cosine,
        sine,
        cosine_all,
        sine_all,
        start_low,
        gain_w,
        grad_early,
    )
    grad_kv, grad_pick, queries_wide, branch_cols, grad_head, _ = launch(
        [
            swap_blocks("narrow", kv_parts),
            sum_narrow(pick_part),
            gather_wide(grad_queries),
            split_columns("wide", grad_branch),
            product([early_grad, late_grad], [early, late], 1, [[(0, 0), (1, 1)]]),
        ],
        10,
        "trade_grads",
    )
    grad_kv, out_all = lax.optimization_barrier((grad_kv, out_all))
    grad_base = grad_mid + grad_final * (1.0 - keep_layer)
    grad_rows, gain_attn, grad_kv = rows_back(
        rows_low, gain_w, proj, grad_kv, grad_pick, grad_base, repeat
    )
    gain_attn = gain_attn + gain_pick
    summed_qo = jnp.stack(
        [
            jnp.einsum("wtc,wtf->cf", pick_cols, queries_wide, preferred_element_type=FULL),
            jnp.einsum("wtc,wtf->cf", branch_cols, mixed_wide, preferred_element_type=FULL),
        ]
    )
    grad_rows, acts_owned, kv_wide, head_cols_all, grad_ffn, ffn_squares = launch(
        [
            return_rows(grad_rows),
            swap_owned(acts, 5),
            later(gather_wide(grad_kv, 3), 2),
            later(split_columns("wide", grad_head[0], 3), 2),
            product([acts], [inner_all, out_all], 0, [[(0, 0)], [(1, 0)], [(2, 1)]]),
        ],
        11,
        "return_rows",
    )
    turn = lax.rem(wide_spot, 2)
    grad_kv_w = jnp.einsum(
        "wtc,wtf->cf", tok_cols, kv_wide, preferred_element_type=FULL
    ).reshape(columns, narrow_count, 2, kv_size)
    grad_kv_w = jnp.moveaxis(grad_kv_w, 0, 2)
    summed_kv = lax.psum_scatter(grad_kv_w, "narrow", scatter_dimension=0, tiled=True)[0]
    summed_table, table_squares = spread(
        spots, listed, grad_rows.reshape(-1, columns), head_cols_all.reshape(vocab_rows, columns)
    )

    squares = (
        jnp.sum(summed_qo * summed_qo)
        + jnp.sum(summed_kv * summed_kv)
        + jnp.sum(ffn_squares)
        + jnp.sum(table_squares)
    )
    sums = jnp.stack(
        [gain_attn[0], gain_mid[0], gain_early[0] + gain_late[0], jnp.full((width,), squares)]
    )
    def owns_last():
        away = lax.axis_index("narrow") + narrow_count - lax.rem(lax.axis_index("wide"), 2)
        return lax.rem(away, narrow_count) >= 2

    sums, kv_owned, qo_owned, owned, _ = launch(
        [
            combine(sums.reshape(4, 8, -1), add_two),
            send_owner(summed_kv.astype(LOW).reshape(2 * block_rows, kv_size)),
            later(send_owner(summed_qo.astype(LOW).reshape(2 * columns, q_size)), 1),
            later(
                product(
                    [acts_owned],
                    [inner_all, out_all],
                    0,
                    [[(at, 0)] for at in range(narrow_count)],
                    False,
                    owns_last,
                ),
                1,
            ),
        ],
        12,
        "combine_sums",
    )
    sums = sums.reshape(4, width)
    summed_gain = lax.dynamic_slice_in_dim(
        sums[:3], (wide_spot * narrow_count + narrow_spot) * gain_size, gain_size, 1
    )
    square_total = sums[3, 0] + jnp.sum(sums[:3] * sums[:3])
    grad_norm = jnp.sqrt(square_total) / loss_count
    factor = jnp.minimum(1.0, CLIP_NORM / (grad_norm + 1e-06)) / loss_count

    final_parts, factor = lax.optimization_barrier((grad_ffn, factor))
    size = width // narrow_count

    def final_piece(spot):
        return lax.dynamic_slice_in_dim(final_parts, spot * size, size, 2)

    pieces = [final_piece(narrow_spot)] + [
        shifted(final_piece(lax.rem(narrow_spot + step, narrow_count)), "narrow", step)
        for step in range(1, narrow_count)
    ]
    directions = newton(
        factor, mom_owned, owned, qo_owned, kv_owned
    )
    directions, pieces, ffn, factor = lax.optimization_barrier(
        (directions, pieces, ffn, factor)
    )
    summed_ffn = jnp.zeros((3, narrow_count, ffn_size, size), LOW)
    for step, piece in enumerate(pieces):
        source = lax.rem(narrow_spot - step + narrow_count, narrow_count)
        summed_ffn = lax.dynamic_update_index_in_dim(summed_ffn, piece, source, 1)
    summed_ffn = summed_ffn.reshape(3, ffn_rows, size).astype(FULL)
    received = [lax.dynamic_index_in_dim(directions, narrow_spot, 0, False)] + [
        shifted(
            lax.dynamic_index_in_dim(
                directions, lax.rem(narrow_spot + step, narrow_count), 0, False
            ),
            "narrow",
            step,
        )
        for step in range(1, narrow_count)
    ]

    def direction_of(matrix):
        step = lax.rem(narrow_spot - matrix - turn + 2 * narrow_count, narrow_count)
        result = received[0]
        for at in range(1, narrow_count):
            result = jnp.where(step == at, received[at], result)
        return result

    dir_ffn = jnp.stack([direction_of(matrix) for matrix in range(3)]).astype(FULL)
    small = direction_of(3).astype(FULL)
    dir_qo = small[: 2 * block_rows].reshape(mom_qo.shape)
    dir_kv = small[2 * block_rows : 2 * block_rows + half_rows].reshape(half_rows, 4, kv_size)
    dir_kv = jnp.moveaxis(dir_kv, 1, 0).reshape(mom_kv.shape)

    embed_new, embed_m_new, embed_v_new = adamw(
        embed, embed_m, embed_v, summed_table * factor, RATE_ADAM, WEIGHT_DECAY
    )
    gains_new, gains_m_new, gains_v_new = adamw(
        gains, gains_m, gains_v, summed_gain * factor, RATE_GAIN, 0.0
    )

    def mom_next(mom, grad):
        return MOMENTUM * mom + jnp.moveaxis(grad * factor, 0, 1)

    shrink = 1.0 - RATE_MUON * WEIGHT_DECAY

    def weight_next(weight, direction):
        return weight * shrink - RATE_MUON * jnp.moveaxis(direction, 0, 1)

    return (
        loss_sum,
        loss_count,
        grad_norm,
        embed_new,
        embed_m_new,
        embed_v_new,
        weight_next(attn_qo, dir_qo),
        mom_next(attn_qo_mom, summed_qo),
        weight_next(attn_kv, dir_kv),
        mom_next(attn_kv_mom, summed_kv),
        weight_next(ffn, dir_ffn),
        mom_next(ffn_mom, summed_ffn),
        gains_new,
        gains_m_new,
        gains_v_new,
    )


def solution(mesh):
    by_pack = P("wide", None)
    table = P("narrow", "wide")
    layer = P("wide", None, "narrow")
    gain = P(None, ("wide", "narrow"))
    return jax.shard_map(
        per_device,
        mesh=mesh,
        in_specs=(by_pack,) * 4 + (P("wide"),) + (table,) * 3 + (layer,) * 6 + (gain,) * 3,
        out_specs=(P(),) * 3 + (table,) * 3 + (layer,) * 6 + (gain,) * 3,
        check_vma=False,
    )
```

```python
import functools

import jax
import jax.numpy as jnp
from jax import lax
from jax.experimental import pallas as pl
from jax.experimental.pallas import tpu as pltpu
from jax.sharding import PartitionSpec as P

HEADS = 16
HD = 128
KVH = 4
NS_STEPS = 5
STEP = 10


NORM_EPS = 1e-05
ROPE_BASE = 10000.0
EXIT_EARLY = 0.25
EXIT_LAST = 1.0
CLIP_NORM = 0.02
BETA_ONE = 0.9
BETA_TWO = 0.95
ADAM_EPS = 1e-08
RATE_ADAM = 0.02
RATE_GAIN = 0.3
RATE_MUON = 0.3
WEIGHT_DECAY = 0.1
MOMENTUM = 0.95
NEWTON_A = 3.4445
NEWTON_B = -4.775
NEWTON_C = 2.0315
MASKED = -1e30
LOW = jnp.bfloat16
FULL = jnp.float32
BOTH = ("wide", "narrow")
UNROLL = 16
VMEM_BYTES = 56 * 1024 * 1024


def dot(first, second, first_dim, second_dim):
    return lax.dot_general(
        first, second, (((first_dim,), (second_dim,)), ((), ())), preferred_element_type=FULL
    )


def norm_rows(values, gain_row):
    return (
        values * lax.rsqrt(jnp.mean(values * values, axis=-1, keepdims=True) + NORM_EPS) * gain_row
    )


def segments_at(lens, where_at):
    ends = jnp.cumsum(lens)
    return jnp.sum((where_at[:, None] >= ends[None, :]).astype(jnp.int32), axis=1)


def angles_at(lens, where_at):
    segment = segments_at(lens, where_at)
    starts = jnp.cumsum(lens) - lens
    member = segment[:, None] == jnp.arange(lens.shape[0], dtype=jnp.int32)[None, :]
    begin = jnp.sum(jnp.where(member, starts[None, :], 0), axis=1)
    offset_pos = (where_at - begin).astype(FULL)
    inverse = ROPE_BASE ** (-2.0 * jnp.arange(HD // 2, dtype=FULL) / HD)
    angle = offset_pos[:, None] * inverse[None, :]
    return (segment, jnp.cos(angle), jnp.sin(angle))


MESH = pl.DeviceIdType.MESH
ANY = pl.BlockSpec(memory_space=pl.ANY)
VMEM = pl.BlockSpec(memory_space=pltpu.VMEM)


def others(axis, count):
    me = lax.axis_index(axis)
    return [{axis: lax.rem(me + step, count)} for step in range(1, count)]


def push(source, target, send, receive, device):
    return pltpu.make_async_remote_copy(
        src_ref=source,
        dst_ref=target,
        send_sem=send,
        recv_sem=receive,
        device_id=device,
        device_id_type=MESH,
    )


def arrived(block, send, receive, device):
    push(block, block, send, receive, device).wait_recv()


def like(values):
    return jax.ShapeDtypeStruct(values.shape, values.dtype)


def struct(shape, dtype):
    return jax.ShapeDtypeStruct(shape, dtype)


def sems(*shape):
    return pltpu.SemaphoreType.DMA(shape)


class Task:
    def __init__(self, inputs, outputs, scratch, steps, place_in, place_out, axes):
        self.inputs, self.outputs, self.scratch, self.steps = inputs, outputs, scratch, steps
        self.place_in = [place_in] * len(inputs)
        self.place_out = [place_out] * len(outputs)
        self.axes = axes


def launch(tasks, ident, name):
    axes = sorted(set(axis for task in tasks for axis in task.axes))
    inputs = [a for task in tasks for a in task.inputs]
    outputs = [a for task in tasks for a in task.outputs]
    scratch = [a for task in tasks for a in task.scratch]

    def body(*refs):
        refs = list(refs)
        ins = refs[: len(inputs)]
        outs = refs[len(inputs) : len(inputs) + len(outputs)]
        extra = refs[len(inputs) + len(outputs) :]
        barrier = pltpu.get_barrier_semaphore()
        targets = [device for axis in axes for device in others(axis, lax.axis_size(axis))]
        for device in targets:
            pl.semaphore_signal(barrier, inc=1, device_id=device, device_id_type=MESH)
        pl.semaphore_wait(barrier, len(targets))
        live = []
        for task in tasks:
            counts = (len(task.inputs), len(task.outputs), len(task.scratch))
            live.append(task.steps(ins[: counts[0]], outs[: counts[1]], extra[: counts[2]]))
            ins, outs, extra = ins[counts[0] :], outs[counts[1] :], extra[counts[2] :]
        while live:
            live = [steps for steps in live if next(steps, 0) is None]

    size = sum(a.size * a.dtype.itemsize for a in list(inputs) + list(outputs))
    return pl.pallas_call(
        body,
        out_shape=outputs,
        in_specs=[place for task in tasks for place in task.place_in],
        out_specs=[place for task in tasks for place in task.place_out],
        scratch_shapes=scratch,
        compiler_params=pltpu.CompilerParams(
            collective_id=ident, has_side_effects=True, vmem_limit_bytes=VMEM_BYTES
        ),
        cost_estimate=pl.CostEstimate(flops=0, bytes_accessed=size // 8, transcendentals=0),
        name=name,
    )(*inputs)


def later(task, turns):
    begin = task.steps

    def steps(ins, outs, scratch):
        for turn in range(turns):
            yield
        yield from begin(ins, outs, scratch)

    task.steps = steps
    return task


def gather_wide(values, patience=1):
    count = lax.axis_size("wide")
    chips = count // 2

    def steps(ins, outs, scratch):
        (x_ref,), (out_ref,), (send, receive, local) = ins, outs, scratch
        me = lax.axis_index("wide")
        mate = me + 1 - 2 * lax.rem(me, 2)
        peers = [lax.rem(me + 2 * step, count) for step in range(1, chips)] + [mate]
        first = []
        for step, peer in enumerate(peers):
            copy = push(x_ref, out_ref.at[me], send.at[step], receive.at[me], {"wide": peer})
            copy.start()
            first.append(copy)
        keep = pltpu.make_async_copy(x_ref, out_ref.at[me], local)
        keep.start()
        for turn in range(patience):
            yield
        second = []
        for step in range(1, chips):
            source = lax.rem(me - 2 * step + count, count)
            block = out_ref.at[source]
            arrived(block, send.at[0], receive.at[source], {"wide": mate})
            copy = push(
                block, block, send.at[chips + step - 1], receive.at[source], {"wide": mate}
            )
            copy.start()
            second.append(copy)
        yield
        for step in range(chips):
            source = lax.rem(mate - 2 * step + count, count)
            arrived(out_ref.at[source], send.at[0], receive.at[source], {"wide": mate})
        for copy in first + second:
            copy.wait_send()
        keep.wait()

    shape = struct((count,) + values.shape, values.dtype)
    return Task(
        [values], [shape], [sems(count - 1), sems(count), sems()], steps, VMEM, VMEM, ["wide"]
    )


def trade(axis, values, source_of, target_of, shape, patience=2):
    count = lax.axis_size(axis)

    def steps(ins, outs, scratch):
        (x_ref,), (out_ref,), (send, receive, local) = ins, outs, scratch
        me = lax.axis_index(axis)
        copies = []
        for step in range(1, count):
            peer = lax.rem(me + step, count)
            copy = push(
                source_of(x_ref, peer),
                target_of(out_ref, me),
                send.at[step - 1],
                receive.at[me],
                {axis: peer},
            )
            copy.start()
            copies.append(copy)
        keep = pltpu.make_async_copy(source_of(x_ref, me), target_of(out_ref, me), local)
        keep.start()
        for turn in range(patience):
            yield
        for step in range(1, count):
            source = lax.rem(me - step + count, count)
            arrived(
                target_of(out_ref, source), send.at[0], receive.at[source], {axis: source}
            )
        for copy in copies:
            copy.wait_send()
        keep.wait()

    return Task(
        [values],
        [struct(shape, values.dtype)],
        [sems(count - 1), sems(count), sems()],
        steps,
        ANY,
        ANY,
        [axis],
    )


def block_at(ref, spot):
    return ref.at[spot]


def whole_at(ref, spot):
    return ref


def columns_of(size):
    def at(ref, spot):
        return ref.at[:, pl.ds(pl.multiple_of(spot * size, size), size)]

    return at


def turned(ref, spot):
    count = lax.axis_size("narrow")
    matrix = lax.rem(spot + count - lax.rem(lax.axis_index("wide"), 2), count)
    return ref.at[jnp.minimum(matrix, 3)]


def swap_turned(values, patience=2):
    shape = (lax.axis_size("narrow"),) + values.shape[1:]
    return trade("narrow", values, turned, block_at, shape, patience)


def product(lefts, rights, dim, order, pause=True, last=None):
    count, rows = len(order), lefts[0].shape[-1 if dim == 0 else -2]
    columns = rights[0].shape[1]
    block = min(512, columns)

    def steps(ins, outs, scratch):
        left_refs, right_refs = ins[: len(lefts)], ins[len(lefts) :]
        result_ref, square_ref = outs
        square_ref[...] = jnp.zeros_like(square_ref)

        def left_of(member):
            return left_refs[0][member] if lefts[0].ndim == 3 else left_refs[member][...]

        def fill(at, members, shift):
            def strip(part, carry):
                spot = pl.ds(pl.multiple_of(part * block, block), block)
                value = jnp.zeros((rows, block), FULL)
                for left, right in members:
                    value = value + dot(left_of(left), right_refs[right + shift][:, spot], dim, 0)
                result_ref[at, :, spot] = value.astype(LOW)
                square_ref[:, spot] = square_ref[:, spot] + jnp.sum(
                    value * value, axis=0, keepdims=True
                )
                return carry

            lax.fori_loop(0, columns // block, strip, 0)

        for at, members in enumerate(order):
            if last is None:
                fill(at, members, 0)
            else:
                pl.when(last())(functools.partial(fill, at, members, 1))
                pl.when(jnp.logical_not(last()))(functools.partial(fill, at, members, 0))
            if pause:
                yield

    return Task(
        list(lefts) + list(rights),
        [struct((count, rows, columns), LOW), struct((1, columns), FULL)],
        [],
        steps,
        VMEM,
        VMEM,
        [],
    )


def exit_stats(features, table, targets):
    rows, vocab = features.shape[0], table.shape[0]
    block = min(256, vocab)

    def steps(ins, outs, scratch):
        features_ref, table_ref, targets_ref = ins
        logits_ref, stats_ref = outs

        def strip(part):
            return pl.ds(pl.multiple_of(part * block, block), block)

        def over(function, start):
            return lax.fori_loop(0, vocab // block, function, start)

        def fill(part, peak):
            logits = dot(table_ref[strip(part), :], features_ref[...], 1, 1)
            logits_ref[strip(part), :] = logits
            return jnp.maximum(peak, jnp.max(logits, axis=0, keepdims=True))

        peak = over(fill, jnp.full((1, rows), MASKED, FULL))
        lines = lax.broadcasted_iota(jnp.int32, (block, rows), 0)

        def add(part, carry):
            total, picked = carry
            logits = logits_ref[strip(part), :]
            hit = lines + part * block == targets_ref[...]
            return (
                total + jnp.sum(jnp.exp(logits - peak), axis=0, keepdims=True),
                picked + jnp.sum(jnp.where(hit, logits, 0.0), axis=0, keepdims=True),
            )

        zero = jnp.zeros((1, rows), FULL)
        total, picked = over(add, (zero, zero))
        stats_ref[0:1, :] = peak
        stats_ref[1:2, :] = total
        stats_ref[2:3, :] = picked
        yield

    return Task(
        [features, table, targets],
        [struct((vocab, rows), FULL), struct((3, rows), FULL)],
        [],
        steps,
        VMEM,
        VMEM,
        [],
    )


def swap_owned(values, patience):
    count = lax.axis_size("narrow")

    def steps(ins, outs, scratch):
        (x_ref,), (out_ref,), (send, receive, local) = ins, outs, scratch
        me = lax.axis_index("narrow")
        turn = lax.rem(lax.axis_index("wide"), 2)

        def matrix_of(device):
            return lax.rem(device + count - turn, count)

        def copy_to(step):
            peer = lax.rem(me + step, count)
            return push(
                x_ref.at[jnp.minimum(matrix_of(peer), 2)],
                out_ref.at[me],
                send.at[step - 1],
                receive.at[me],
                {"narrow": peer},
            )

        def keep():
            return pltpu.make_async_copy(
                x_ref.at[jnp.minimum(matrix_of(me), 2)], out_ref.at[me], local
            )

        keep().start()
        for step in range(1, count):

            @pl.when(matrix_of(lax.rem(me + step, count)) < 3)
            def _():
                copy_to(step).start()

        for turn_at in range(patience):
            yield

        @pl.when(matrix_of(me) < 3)
        def _():
            for step in range(1, count):
                source = lax.rem(me - step + count, count)
                arrived(out_ref.at[source], send.at[0], receive.at[source], {"narrow": source})

        for step in range(1, count):

            @pl.when(matrix_of(lax.rem(me + step, count)) < 3)
            def _():
                copy_to(step).wait_send()

        keep().wait()

    return Task(
        [values],
        [struct((count,) + values.shape[1:], values.dtype)],
        [sems(count - 1), sems(count), sems()],
        steps,
        ANY,
        ANY,
        ["narrow"],
    )


def send_owner(values):
    count = lax.axis_size("narrow")

    def steps(ins, outs, scratch):
        (x_ref,), (out_ref,), (send, receive, local) = ins, outs, scratch
        me = lax.axis_index("narrow")
        owner = lax.rem(3 + lax.rem(lax.axis_index("wide"), 2), count)
        keep = pltpu.make_async_copy(x_ref, out_ref.at[me], local)
        keep.start()

        def to_owner():
            return push(x_ref, out_ref.at[me], send.at[0], receive.at[me], {"narrow": owner})

        @pl.when(me != owner)
        def _():
            to_owner().start()

        yield
        yield

        @pl.when(me != owner)
        def _():
            to_owner().wait_send()

        @pl.when(me == owner)
        def _():
            for step in range(1, count):
                source = lax.rem(owner + step, count)
                arrived(out_ref.at[source], send.at[0], receive.at[source], {"narrow": source})

        keep.wait()

    return Task(
        [values],
        [struct((count,) + values.shape, values.dtype)],
        [sems(1), sems(count), sems()],
        steps,
        ANY,
        ANY,
        ["narrow"],
    )


def swap_blocks(axis, values):
    return trade(axis, values, block_at, block_at, values.shape)


def gather_blocks(axis, values):
    shape = (lax.axis_size(axis),) + values.shape
    return trade(axis, values, whole_at, block_at, shape)


def split_columns(axis, values, patience=2):
    count = lax.axis_size(axis)
    rows, size = values.shape[0], values.shape[1] // count
    return trade(axis, values, columns_of(size), block_at, (count, rows, size), patience)


def join_columns(axis, values):
    count, rows, size = values.shape
    return trade(axis, values, block_at, columns_of(size), (rows, count * size))


def collect(count, parts_ref, slots, send, receive):
    me = lax.axis_index("narrow")
    copies = []
    for step in range(1, count):
        peer = lax.rem(me + step, count)
        copy = push(
            parts_ref.at[peer],
            slots.at[me],
            send.at[step - 1],
            receive.at[me],
            {"narrow": peer},
        )
        copy.start()
        copies.append(copy)
    return copies


def collected(count, parts_ref, slots, send, receive):
    me = lax.axis_index("narrow")
    total = parts_ref[me].astype(FULL)
    for step in range(1, count):
        source = lax.rem(me - step + count, count)
        arrived(slots.at[source], send.at[0], receive.at[source], {"narrow": source})
        total = total + slots[source].astype(FULL)
    return total


def share(count, low, all_ref, send, receive):
    me = lax.axis_index("narrow")
    all_ref[me] = low
    copies = []
    for step in range(1, count):
        peer = lax.rem(me + step, count)
        copy = push(
            all_ref.at[me], all_ref.at[me], send.at[step - 1], receive.at[me], {"narrow": peer}
        )
        copy.start()
        copies.append(copy)
    return copies


def shared(count, all_ref, send, receive):
    me = lax.axis_index("narrow")
    for step in range(1, count):
        source = lax.rem(me - step + count, count)
        arrived(all_ref.at[source], send.at[0], receive.at[source], {"narrow": source})


def narrow_sems(count):
    return [sems(count - 1), sems(count)]


def settle(partial, base, other, keep_row, gain_row):
    count = lax.axis_size("narrow")
    rows, width = base.shape

    def steps(ins, outs, scratch):
        parts_ref, base_ref, other_ref, keep_ref, gain_ref = ins
        own_ref, all_ref = outs
        slots, send, receive, send_all, receive_all = scratch
        copies = collect(count, parts_ref, slots, send, receive)
        yield
        total = collected(count, parts_ref, slots, send, receive)
        total = jnp.where(keep_ref[...] > 0, total + base_ref[...], other_ref[...])
        own_ref[...] = total
        low = norm_rows(total, gain_ref[...]).astype(LOW)
        copies = copies + share(count, low, all_ref, send_all, receive_all)
        yield
        shared(count, all_ref, send_all, receive_all)
        for copy in copies:
            copy.wait_send()

    return Task(
        [partial.reshape(count, rows, width), base, other, keep_row, gain_row],
        [struct((rows, width), FULL), struct((count, rows, width), LOW)],
        [pltpu.VMEM((count, rows, width), partial.dtype)]
        + narrow_sems(count)
        + narrow_sems(count),
        steps,
        VMEM,
        VMEM,
        ["narrow"],
    )


def settle_back(partial, values, add, keep_row, gain_row):
    count = lax.axis_size("narrow")
    rows, width = values.shape

    def steps(ins, outs, scratch):
        parts_ref, values_ref, add_ref, keep_ref, gain_ref = ins
        own_ref, gain_grad_ref, all_ref = outs
        slots, send, receive, send_all, receive_all = scratch
        copies = collect(count, parts_ref, slots, send, receive)
        yield
        grad = collected(count, parts_ref, slots, send, receive)
        held = values_ref[...]
        root = lax.rsqrt(jnp.mean(held * held, axis=-1, keepdims=True) + NORM_EPS)
        scaled = gain_ref[...] * grad
        inner = jnp.mean(held * scaled, axis=-1, keepdims=True)
        own = add_ref[...] + root * scaled - held * (root * root * root * inner)
        gain_grad_ref[...] = jnp.sum(held * root * grad, axis=0, keepdims=True)
        own_ref[...] = own
        low = (own * keep_ref[...]).astype(LOW)
        copies = copies + share(count, low, all_ref, send_all, receive_all)
        yield
        shared(count, all_ref, send_all, receive_all)
        for copy in copies:
            copy.wait_send()

    return Task(
        [partial.reshape(count, rows, width), values, add, keep_row, gain_row],
        [
            struct((rows, width), FULL),
            struct((1, width), FULL),
            struct((count, rows, width), LOW),
        ],
        [pltpu.VMEM((count, rows, width), partial.dtype)]
        + narrow_sems(count)
        + narrow_sems(count),
        steps,
        VMEM,
        VMEM,
        ["narrow"],
    )


def sum_narrow(partial):
    count = lax.axis_size("narrow")
    rows, width = partial.shape[0] // count, partial.shape[1]

    def steps(ins, outs, scratch):
        (parts_ref,), (own_ref,), (slots, send, receive) = ins, outs, scratch
        copies = collect(count, parts_ref, slots, send, receive)
        yield
        yield
        own_ref[...] = collected(count, parts_ref, slots, send, receive)
        for copy in copies:
            copy.wait_send()

    return Task(
        [partial.reshape(count, rows, width)],
        [struct((rows, width), FULL)],
        [pltpu.VMEM((count, rows, width), partial.dtype)] + narrow_sems(count),
        steps,
        VMEM,
        VMEM,
        ["narrow"],
    )


def fetch_rows(found, rows):
    deep, wide = lax.axis_size("narrow"), lax.axis_size("wide")
    columns = found.shape[2]

    def steps(ins, outs, scratch):
        (found_ref,), (out_ref,) = ins, outs
        rightward, leftward, final = scratch[:3]
        send_right, receive_right, send_left, receive_left = scratch[3:7]
        send_wide, receive_wide, local = scratch[7:]
        spot = lax.axis_index("narrow")
        me = lax.axis_index("wide")

        def right_copy(part, source):
            return push(
                source,
                rightward.at[part],
                send_right.at[part],
                receive_right.at[part],
                {"narrow": lax.rem(spot + 1, deep)},
            )

        def left_copy(part, source):
            return push(
                source,
                leftward.at[part],
                send_left.at[part],
                receive_left.at[part],
                {"narrow": lax.rem(spot + deep - 1, deep)},
            )

        for step in range(deep - 1):
            right, left = deep - 1 - step, step

            @pl.when((spot == 0) & (right > 0))
            def _():
                right_copy(right, found_ref.at[right]).start()

            @pl.when((spot == deep - 1) & (left < deep - 1))
            def _():
                left_copy(left, found_ref.at[left]).start()

        yield
        for step in range(deep - 1):
            right, left = deep - 1 - step, step

            def pass_right():
                right_copy(right, rightward.at[right]).wait_recv()
                rightward[right] = rightward[right] + found_ref[right]
                right_copy(right, rightward.at[right]).start()

            pl.when((spot > 0) & (right > spot) & (2 * spot < deep))(pass_right)

            @pl.when((spot < deep - 1) & (left < spot))
            def _():
                left_copy(left, leftward.at[left]).wait_recv()
                leftward[left] = leftward[left] + found_ref[left]
                left_copy(left, leftward.at[left]).start()

            pl.when((right > spot) & (2 * spot >= deep))(pass_right)

        final[...] = found_ref[spot]

        @pl.when(spot > 0)
        def _():
            right_copy(spot, rightward.at[spot]).wait_recv()
            final[...] = final[...] + rightward[spot]

        @pl.when(spot < deep - 1)
        def _():
            left_copy(spot, leftward.at[spot]).wait_recv()
            final[...] = final[...] + leftward[spot]

        def rows_for(device):
            return final.at[pl.ds(pl.multiple_of(device * rows, rows), rows)]

        def columns_from(device):
            return columns_of(columns)(out_ref, device)

        copies = []
        for step in range(1, wide):
            peer = lax.rem(me + step, wide)
            copy = push(
                rows_for(peer),
                columns_from(me),
                send_wide.at[step - 1],
                receive_wide.at[me],
                {"wide": peer},
            )
            copy.start()
            copies.append(copy)
        keep = pltpu.make_async_copy(rows_for(me), columns_from(me), local)
        keep.start()
        yield
        for step in range(1, wide):
            source = lax.rem(me - step + wide, wide)
            arrived(
                columns_from(source), send_wide.at[0], receive_wide.at[source], {"wide": source}
            )
        yield
        for copy in copies:
            copy.wait_send()
        keep.wait()
        for step in range(deep - 1):
            right, left = deep - 1 - step, step

            @pl.when(right > spot)
            def _():
                right_copy(right, found_ref.at[right]).wait_send()

            @pl.when(left < spot)
            def _():
                left_copy(left, found_ref.at[left]).wait_send()

    task = Task(
        [found],
        [struct((rows, wide * columns), found.dtype)],
        [pltpu.VMEM(found.shape, found.dtype)] * 2
        + [pltpu.VMEM(found.shape[1:], found.dtype)]
        + [sems(deep)] * 4
        + [sems(wide - 1), sems(wide), sems()],
        steps,
        VMEM,
        ANY,
        ["narrow", "wide"],
    )
    return task


def return_rows(rows):
    deep, wide = lax.axis_size("narrow"), lax.axis_size("wide")
    count, width = rows.shape
    columns = width // wide

    def steps(ins, outs, scratch):
        (rows_ref,), (out_ref,) = ins, outs
        send_right, send_left, receive_deep, send_wide, receive_wide, local = scratch
        spot = lax.axis_index("narrow")
        me = lax.axis_index("wide")
        part_of = functools.partial(columns_of(columns), rows_ref)

        def landing(device):
            return out_ref.at[spot, pl.ds(pl.multiple_of(device * count, count), count)]

        copies = []
        for step in range(1, wide):
            peer = lax.rem(me + step, wide)
            copy = push(
                part_of(peer),
                landing(me),
                send_wide.at[step - 1],
                receive_wide.at[me],
                {"wide": peer},
            )
            copy.start()
            copies.append(copy)
        keep = pltpu.make_async_copy(part_of(me), landing(me), local)
        keep.start()
        yield
        for step in range(1, wide):
            source = lax.rem(me - step + wide, wide)
            arrived(landing(source), send_wide.at[0], receive_wide.at[source], {"wide": source})
        keep.wait()

        def right_copy(part):
            return push(
                out_ref.at[part],
                out_ref.at[part],
                send_right.at[part],
                receive_deep.at[part],
                {"narrow": lax.rem(spot + 1, deep)},
            )

        def left_copy(part):
            return push(
                out_ref.at[part],
                out_ref.at[part],
                send_left.at[part],
                receive_deep.at[part],
                {"narrow": lax.rem(spot + deep - 1, deep)},
            )

        @pl.when(spot < deep - 1)
        def _():
            right_copy(spot).start()

        @pl.when(spot > 0)
        def _():
            left_copy(spot).start()

        for step in range(1, deep):
            yield

            @pl.when(spot >= step)
            def _():
                right_copy(spot - step).wait_recv()

                @pl.when(spot < deep - 1)
                def _():
                    right_copy(spot - step).start()

            @pl.when(spot + step < deep)
            def _():
                left_copy(spot + step).wait_recv()

                @pl.when(spot > 0)
                def _():
                    left_copy(spot + step).start()

        for part in range(deep):

            @pl.when((part <= spot) & (spot < deep - 1))
            def _():
                right_copy(part).wait_send()

            @pl.when((part >= spot) & (spot > 0))
            def _():
                left_copy(part).wait_send()

        for copy in copies:
            copy.wait_send()

    return Task(
        [rows],
        [struct((deep, wide * count, columns), rows.dtype)],
        [sems(deep)] * 3 + [sems(wide - 1), sems(wide), sems()],
        steps,
        ANY,
        ANY,
        ["narrow", "wide"],
    )


def sum_wide(partial):
    count = lax.axis_size("wide")
    chips = count // 2
    rows, width = partial.shape[0] // count, partial.shape[1]

    def steps(ins, outs, scratch):
        (parts_ref,), (out_ref,) = ins, outs
        from_mate, paired, slots, send_mate, receive_mate, send, receive = scratch
        me = lax.axis_index("wide")
        side = lax.rem(me, 2)
        mate = me + 1 - 2 * side
        my_chip = me // 2
        mate_copies = []
        for step in range(chips):
            chip = lax.rem(my_chip + 1 + step, chips)
            copy = push(
                parts_ref.at[2 * chip + 1 - side],
                from_mate.at[chip],
                send_mate.at[step],
                receive_mate.at[chip],
                {"wide": mate},
            )
            copy.start()
            mate_copies.append(copy)
        yield
        copies = []
        for step in range(chips):
            chip = lax.rem(my_chip + 1 + step, chips)
            arrived(from_mate.at[chip], send_mate.at[0], receive_mate.at[chip], {"wide": mate})
            both = parts_ref[2 * chip + side].astype(FULL) + from_mate[chip].astype(FULL)
            if step < chips - 1:
                paired[chip] = both.astype(LOW)
                copy = push(
                    paired.at[chip],
                    slots.at[my_chip],
                    send.at[step],
                    receive.at[my_chip],
                    {"wide": 2 * chip + side},
                )
                copy.start()
                copies.append(copy)
            else:
                out_ref[...] = both
        yield
        for step in range(1, chips):
            chip = lax.rem(my_chip - step + chips, chips)
            arrived(slots.at[chip], send.at[0], receive.at[chip], {"wide": 2 * chip + side})
            out_ref[...] = out_ref[...] + slots[chip].astype(FULL)
        for copy in mate_copies + copies:
            copy.wait_send()

    return Task(
        [partial.reshape(count, rows, width)],
        [struct((rows, width), FULL)],
        [pltpu.VMEM((chips, rows, width), LOW)] * 3
        + [sems(chips), sems(chips), sems(max(chips - 1, 1)), sems(chips)],
        steps,
        VMEM,
        VMEM,
        ["wide"],
    )


def merge_stats(first, second):
    peak = jnp.maximum(first[0:1], second[0:1])
    total = first[1:2] * jnp.exp(first[0:1] - peak) + second[1:2] * jnp.exp(second[0:1] - peak)
    return jnp.concatenate([peak, total, first[2:3] + second[2:3]], axis=0)


def add_two(first, second):
    return first + second


def combine(values, join):
    deep, wide = lax.axis_size("narrow"), lax.axis_size("wide")

    def steps(ins, outs, scratch):
        (x_ref,), (out_ref,) = ins, outs
        wide_slots, deep_slots, send_wide, receive_wide, send_deep, receive_deep = scratch

        def start(axis, count, slots, value, send, receive):
            me = lax.axis_index(axis)
            slots[me] = value
            copies = []
            for step in range(1, count):
                peer = lax.rem(me + step, count)
                copy = push(
                    slots.at[me], slots.at[me], send.at[step - 1], receive.at[me], {axis: peer}
                )
                copy.start()
                copies.append(copy)
            return copies

        def finish(axis, count, slots, send, receive):
            me = lax.axis_index(axis)
            for step in range(1, count):
                source = lax.rem(me - step + count, count)
                arrived(slots.at[source], send.at[0], receive.at[source], {axis: source})
            total = slots[0]
            for source in range(1, count):
                total = join(total, slots[source])
            return total

        first = start("wide", wide, wide_slots, x_ref[...], send_wide, receive_wide)
        yield
        total = finish("wide", wide, wide_slots, send_wide, receive_wide)
        second = start("narrow", deep, deep_slots, total, send_deep, receive_deep)
        yield
        out_ref[...] = finish("narrow", deep, deep_slots, send_deep, receive_deep)
        for copy in first + second:
            copy.wait_send()

    return Task(
        [values],
        [like(values)],
        [
            pltpu.VMEM((wide,) + values.shape, values.dtype),
            pltpu.VMEM((deep,) + values.shape, values.dtype),
            sems(wide - 1),
            sems(wide),
            sems(deep - 1),
            sems(deep),
        ],
        steps,
        VMEM,
        VMEM,
        ["narrow", "wide"],
    )


def gather_both(values):
    deep, wide = lax.axis_size("narrow"), lax.axis_size("wide")

    def steps(ins, outs, scratch):
        (x_ref,), (out_ref,) = ins, outs
        send_wide, receive_wide, send_deep, receive_deep = scratch
        me = lax.axis_index("wide")
        spot = lax.axis_index("narrow")
        out_ref[spot, me] = x_ref[...]
        copies = []
        for step in range(1, wide):
            peer = lax.rem(me + step, wide)
            block = out_ref.at[spot, me]
            copy = push(block, block, send_wide.at[step - 1], receive_wide.at[me], {"wide": peer})
            copy.start()
            copies.append(copy)
        yield
        for step in range(1, wide):
            source = lax.rem(me - step + wide, wide)
            block = out_ref.at[spot, source]
            arrived(block, send_wide.at[0], receive_wide.at[source], {"wide": source})
        for step in range(1, deep):
            peer = lax.rem(spot + step, deep)
            block = out_ref.at[spot]
            copy = push(
                block, block, send_deep.at[step - 1], receive_deep.at[spot], {"narrow": peer}
            )
            copy.start()
            copies.append(copy)
        yield
        for step in range(1, deep):
            source = lax.rem(spot - step + deep, deep)
            block = out_ref.at[source]
            arrived(block, send_deep.at[0], receive_deep.at[source], {"narrow": source})
        for copy in copies:
            copy.wait_send()

    return Task(
        [values],
        [struct((deep, wide) + values.shape, values.dtype)],
        [sems(wide - 1), sems(wide), sems(deep - 1), sems(deep)],
        steps,
        VMEM,
        VMEM,
        ["narrow", "wide"],
    )


def turn_heads(values, cosine, sine):
    half = values.shape[1] // 2
    swapped = jnp.concatenate([values[:, half:], values[:, :half]], axis=1)
    return values * cosine + swapped * sine


def wide_angles(cosine, sine):
    return jnp.concatenate([cosine, cosine], axis=1), jnp.concatenate([-sine, sine], axis=1)


def local_call(body, inputs, specs, outputs, flops, name):
    return pl.pallas_call(
        body,
        grid=(1,),
        in_specs=specs,
        out_specs=[
            pl.BlockSpec(a.shape, lambda step, rank=len(a.shape): (0,) * rank) for a in outputs
        ],
        out_shape=outputs,
        compiler_params=pltpu.CompilerParams(vmem_limit_bytes=VMEM_BYTES),
        cost_estimate=pl.CostEstimate(flops=flops, bytes_accessed=8 << 20, transcendentals=0),
        name=name,
    )(*inputs)


def entire(values):
    return pl.BlockSpec(values.shape, lambda step: (0,) * values.ndim)


def column_block(values, size, index):
    return pl.BlockSpec((values.shape[0], size), lambda step: (0, index))


def heads_body(groups, rep, rows_ref, gain_ref, kv_ref, cos_ref, sin_ref, out_ref, normed_ref):
    count, _, _, tok_rows, head = out_ref.shape
    size = kv_ref.shape[1] // (2 * count)
    per_head = head // size
    rows = rows_ref[0:tok_rows, :].astype(FULL)
    normed = norm_rows(rows, gain_ref[...]).astype(LOW)
    normed_ref[...] = normed
    both = dot(normed, kv_ref[...], 1, 0)

    def head_of(kind, index):
        pieces = [
            both[:, (2 * part + kind) * size : (2 * part + kind + 1) * size]
            for part in range(index * per_head, (index + 1) * per_head)
        ]
        return pieces[0] if per_head == 1 else jnp.concatenate(pieces, axis=1)

    for owner in range(count):
        for group in range(groups):
            index = (owner * groups + group) // rep
            keys = turn_heads(head_of(0, index), cos_ref[...], sin_ref[...])
            out_ref[owner, group, 0] = keys.astype(LOW)
            out_ref[owner, group, 1] = head_of(1, index).astype(LOW)


def make_heads(rows_low, gain_row, proj, cosine, sine, groups, rep):
    count = lax.axis_size("narrow")
    tok_rows, head = cosine.shape
    width = rows_low.shape[1]
    size = 2 * KVH * HD
    return local_call(
        functools.partial(heads_body, groups, rep),
        [rows_low, gain_row, proj, cosine, sine],
        [entire(rows_low), entire(gain_row), column_block(proj, size, 0)]
        + [entire(cosine), entire(sine)],
        [struct((count, groups, 2, tok_rows, head), LOW), struct((tok_rows, width), LOW)],
        2 * tok_rows * width * size,
        "make_heads",
    )


def attend_body(
    start_ref,
    gains_ref,
    q_ref,
    o_ref,
    kv_ref,
    cos_ref,
    sin_ref,
    seg_ref,
    seg_all_ref,
    pick_ref,
    queries_ref,
    probs_ref,
    mixed_ref,
    part_ref,
    normed_ref,
    early_ref,
):
    count, groups, _, tok_rows, head = kv_ref.shape
    heads_own = probs_ref.shape[0]
    start = start_ref[...].astype(FULL)
    root = lax.rsqrt(jnp.mean(start * start, axis=-1, keepdims=True) + NORM_EPS)
    normed = (start * root * gains_ref[0:1, :]).astype(LOW)
    normed_ref[...] = normed
    early_ref[...] = (start * root * gains_ref[2:3, :]).astype(LOW)
    queries = dot(normed, q_ref[...], 1, 0)
    spots = lax.broadcasted_iota(jnp.int32, (1, count * tok_rows), 1)
    allowed = (seg_ref[...] == seg_all_ref[...]) & (pick_ref[...] >= spots)
    for group in range(groups):
        keys = jnp.concatenate([kv_ref[part, group, 0] for part in range(count)], axis=0)
        values = jnp.concatenate([kv_ref[part, group, 1] for part in range(count)], axis=0)
        for member in range(heads_own // groups):
            at = group * (heads_own // groups) + member
            spot = slice(at * head, (at + 1) * head)
            query = turn_heads(queries[:, spot], cos_ref[...], sin_ref[...]).astype(LOW)
            queries_ref[:, spot] = query
            scores = jnp.where(allowed, dot(query, keys, 1, 1) * head ** (-0.5), MASKED)
            shifted = jnp.exp(scores - jnp.max(scores, axis=-1, keepdims=True))
            probs = shifted / jnp.sum(shifted, axis=-1, keepdims=True)
            probs_ref[at] = probs
            mixed_ref[:, spot] = dot(probs.astype(LOW), values, 1, 0).astype(LOW)
    part_ref[...] = dot(mixed_ref[...], o_ref[...], 1, 1).astype(LOW)


def attend(start_low, gains, proj, own_head, cosine, sine, seg, seg_all, picks):
    count, groups, _, tok_rows, head = own_head.shape
    sel, width = start_low.shape
    heads_own = HEADS // count
    size = heads_own * head
    first = 2 * KVH * HD // size
    seq_len = count * tok_rows
    return local_call(
        attend_body,
        [start_low, gains, proj, proj, own_head, cosine, sine, seg, seg_all, picks],
        [
            entire(start_low),
            entire(gains),
            column_block(proj, size, first),
            column_block(proj, size, first + 1),
        ]
        + [entire(a) for a in (own_head, cosine, sine, seg, seg_all, picks)],
        [
            struct((sel, size), LOW),
            struct((heads_own, sel, seq_len), FULL),
            struct((sel, size), LOW),
            struct((sel, width), LOW),
            struct((sel, width), LOW),
            struct((sel, width), LOW),
        ],
        4 * sel * size * (width + seq_len),
        "attend",
    )


def attend_back_body(
    grad_ref,
    q_ref,
    o_ref,
    kv_ref,
    queries_ref,
    probs_ref,
    cos_ref,
    sin_ref,
    cos_all_ref,
    sin_all_ref,
    start_ref,
    gains_ref,
    early_ref,
    out_ref,
    grad_q_ref,
    part_ref,
    attn_gain_ref,
    early_gain_ref,
):
    count, groups, _, tok_rows, head = kv_ref.shape
    heads_own = probs_ref.shape[0]
    scale = head ** (-0.5)
    grad_mixed = dot(grad_ref[...], o_ref[...], 1, 0).astype(LOW)
    for group in range(groups):
        keys = jnp.concatenate([kv_ref[part, group, 0] for part in range(count)], axis=0)
        values = jnp.concatenate([kv_ref[part, group, 1] for part in range(count)], axis=0)
        grad_keys = jnp.zeros(keys.shape, FULL)
        grad_values = jnp.zeros(keys.shape, FULL)
        for member in range(heads_own // groups):
            at = group * (heads_own // groups) + member
            spot = slice(at * head, (at + 1) * head)
            probs = probs_ref[at]
            grad_probs = dot(grad_mixed[:, spot], values, 1, 1)
            inner = jnp.sum(probs * grad_probs, axis=-1, keepdims=True)
            grad_scores = (probs * (grad_probs - inner)).astype(LOW)
            grad_query = dot(grad_scores, keys, 1, 0) * scale
            grad_q_ref[:, spot] = turn_heads(grad_query, cos_ref[...], -sin_ref[...]).astype(LOW)
            grad_keys = grad_keys + dot(grad_scores, queries_ref[:, spot], 0, 0)
            grad_values = grad_values + dot(probs.astype(LOW), grad_mixed[:, spot], 0, 0)
        grad_keys = turn_heads(grad_keys * scale, cos_all_ref[...], -sin_all_ref[...])
        for part in range(count):
            rows = slice(part * tok_rows, (part + 1) * tok_rows)
            out_ref[part, group, 0] = grad_keys[rows].astype(LOW)
            out_ref[part, group, 1] = grad_values[rows].astype(LOW)
    pick = dot(grad_q_ref[...], q_ref[...], 1, 1)
    early = early_ref[...].astype(FULL)
    start = start_ref[...].astype(FULL)
    start = start * lax.rsqrt(jnp.mean(start * start, axis=-1, keepdims=True) + NORM_EPS)
    attn_gain_ref[...] = jnp.sum(start * pick, axis=0, keepdims=True)
    early_gain_ref[...] = jnp.sum(start * early, axis=0, keepdims=True)
    part_ref[...] = (gains_ref[0:1, :] * pick + gains_ref[2:3, :] * early).astype(LOW)


def attend_back(
    grad,
    proj,
    own_head,
    queries,
    probs,
    cosine,
    sine,
    cosine_all,
    sine_all,
    start_low,
    gains,
    early,
):
    count, groups, _, tok_rows, head = own_head.shape
    sel, width = grad.shape
    size = queries.shape[1]
    first = 2 * KVH * HD // size
    return local_call(
        attend_back_body,
        [grad, proj, proj, own_head, queries, probs, cosine, sine, cosine_all, sine_all]
        + [start_low, gains, early],
        [entire(grad), column_block(proj, size, first), column_block(proj, size, first + 1)]
        + [
            entire(a)
            for a in (own_head, queries, probs, cosine, sine, cosine_all, sine_all)
            + (start_low, gains, early)
        ],
        [struct(own_head.shape, LOW), struct((sel, size), LOW), struct((sel, width), LOW)]
        + [struct((1, width), FULL)] * 2,
        8 * sel * size * width,
        "attend_back",
    )


def norm_back_rows(values, gain_row, grad):
    root = lax.rsqrt(jnp.mean(values * values, axis=-1, keepdims=True) + NORM_EPS)
    scaled = gain_row * grad
    inner = jnp.mean(values * scaled, axis=-1, keepdims=True)
    result = root * scaled - values * (root * root * root * inner)
    return result, jnp.sum(values * root * grad, axis=0, keepdims=True)


def rows_back_body(
    rep,
    rows_ref,
    gains_ref,
    kv_ref,
    heads_ref,
    pick_ref,
    base_ref,
    out_ref,
    gain_grad_ref,
    grad_kv_ref,
):
    count, groups, _, tok_rows, head = heads_ref.shape
    size = kv_ref.shape[1] // (2 * count)
    per_head = head // size
    for index in range(KVH):
        for kind in range(2):
            copies = [
                heads_ref[at // groups, at % groups, kind]
                for at in range(index * rep, (index + 1) * rep)
            ]
            total = copies[0]
            if rep > 1:
                total = sum(copy.astype(FULL) for copy in copies).astype(LOW)
            for piece in range(per_head):
                lane = (2 * (index * per_head + piece) + kind) * size
                grad_kv_ref[:, lane : lane + size] = total[:, piece * size : (piece + 1) * size]
    values = rows_ref[...].astype(FULL)
    own = values[tok_rows:]
    tok_part, tok_gain = norm_back_rows(
        values[:tok_rows], gains_ref[0:1, :], dot(grad_kv_ref[...], kv_ref[...], 1, 1)
    )
    pick_part, _ = norm_back_rows(own, 1.0, pick_ref[...])
    gain_grad_ref[...] = tok_gain
    out_ref[0:tok_rows, :] = tok_part.astype(LOW)
    out_ref[tok_rows:, :] = (pick_part + base_ref[...]).astype(LOW)


def rows_back(rows_low, gains, proj, heads, grad_pick, base, rep):
    tok_rows = heads.shape[3]
    width = rows_low.shape[1]
    size = 2 * KVH * HD
    return local_call(
        functools.partial(rows_back_body, rep),
        [rows_low, gains, proj, heads, grad_pick, base],
        [entire(rows_low), entire(gains), column_block(proj, size, 0)]
        + [entire(a) for a in (heads, grad_pick, base)],
        [
            struct(rows_low.shape, LOW),
            struct((1, width), FULL),
            struct((tok_rows, size), LOW),
        ],
        2 * tok_rows * width * size,
        "rows_back",
    )


def assemble_body(out_columns, *refs):
    pieces, out_ref = refs[:-1], refs[-1]
    count = len(pieces)
    me = lax.axis_index("narrow")
    for step, piece in enumerate(pieces):
        source = lax.rem(me - step + count, count)
        spot = pl.ds(pl.multiple_of(source * out_columns, out_columns), out_columns)
        out_ref[:, spot] = piece[...]


def assemble(pieces):
    rows, columns = pieces[0].shape
    outputs = [struct((rows, columns * len(pieces)), pieces[0].dtype)]
    return local_call(
        functools.partial(assemble_body, columns),
        list(pieces),
        [entire(piece) for piece in pieces],
        outputs,
        0,
        "assemble",
    )[0]


def feed_body(inner_ref, weight_ref, gate_ref, up_ref, hidden_ref, out_ref, total):
    part = pl.program_id(0)
    inner = inner_ref[...]
    gate = dot(inner, weight_ref[0, 0], 1, 1)
    up = dot(inner, weight_ref[0, 1], 1, 1)
    hidden = (jax.nn.silu(gate) * up).astype(LOW)
    gate_ref[0] = gate
    up_ref[0] = up
    hidden_ref[0] = hidden
    product = dot(hidden, weight_ref[0, 2], 1, 0)

    @pl.when(part == 0)
    def _():
        total[...] = product

    @pl.when(part > 0)
    def _():
        total[...] = total[...] + product

    @pl.when(part == pl.num_programs(0) - 1)
    def _():
        out_ref[...] = total[...].astype(LOW)


def feed(inner, weight):
    parts, _, size, width = weight.shape
    sel = inner.shape[0]
    same = pl.BlockSpec((sel, width), lambda part: (0, 0))
    slab = pl.BlockSpec((1, sel, size), lambda part: (part, 0, 0))
    return pl.pallas_call(
        feed_body,
        grid=(parts,),
        in_specs=[same, pl.BlockSpec((1, 3, size, width), lambda part: (part, 0, 0, 0))],
        out_specs=[slab, slab, slab, same],
        out_shape=[
            struct((parts, sel, size), FULL),
            struct((parts, sel, size), FULL),
            struct((parts, sel, size), LOW),
            struct((sel, width), LOW),
        ],
        scratch_shapes=[pltpu.VMEM((sel, width), FULL)],
        compiler_params=pltpu.CompilerParams(vmem_limit_bytes=VMEM_BYTES),
        cost_estimate=pl.CostEstimate(
            flops=6 * sel * parts * size * width,
            bytes_accessed=weight.size * 2,
            transcendentals=0,
        ),
        name="feed",
    )(inner, weight)


def feed_back_body(grad_ref, weight_ref, gate_ref, up_ref, hidden_ref, acts_ref, out_ref, total):
    part = pl.program_id(0)
    grad_hidden = dot(grad_ref[...], weight_ref[0, 2], 1, 1)
    gate = gate_ref[0]
    sigma = jax.nn.sigmoid(gate)
    grad_gate = (grad_hidden * up_ref[0] * sigma * (1.0 + gate * (1.0 - sigma))).astype(LOW)
    grad_up = (grad_hidden * gate * sigma).astype(LOW)
    acts_ref[0, 0] = grad_gate
    acts_ref[0, 1] = grad_up
    acts_ref[0, 2] = hidden_ref[0]
    product = dot(grad_gate, weight_ref[0, 0], 1, 0) + dot(grad_up, weight_ref[0, 1], 1, 0)

    @pl.when(part == 0)
    def _():
        total[...] = product

    @pl.when(part > 0)
    def _():
        total[...] = total[...] + product

    @pl.when(part == pl.num_programs(0) - 1)
    def _():
        out_ref[...] = total[...].astype(LOW)


def feed_back(grad, weight, gate, up, hidden):
    parts, _, size, width = weight.shape
    sel = grad.shape[0]
    same = pl.BlockSpec((sel, width), lambda part: (0, 0))
    slab = pl.BlockSpec((1, sel, size), lambda part: (part, 0, 0))
    return pl.pallas_call(
        feed_back_body,
        grid=(parts,),
        in_specs=[same, pl.BlockSpec((1, 3, size, width), lambda part: (part, 0, 0, 0))]
        + [slab] * 3,
        out_specs=[pl.BlockSpec((1, 3, sel, size), lambda part: (part, 0, 0, 0)), same],
        out_shape=[struct((parts, 3, sel, size), LOW), struct((sel, width), LOW)],
        scratch_shapes=[pltpu.VMEM((sel, width), FULL)],
        compiler_params=pltpu.CompilerParams(vmem_limit_bytes=VMEM_BYTES),
        cost_estimate=pl.CostEstimate(
            flops=6 * sel * parts * size * width,
            bytes_accessed=weight.size * 2,
            transcendentals=0,
        ),
        name="feed_back",
    )(grad, weight, gate, up, hidden)


def newton_steps(problems):
    rows, width = problems[0][0].shape
    block = min(1024, width)
    eye = lax.broadcasted_iota(jnp.int32, (rows, rows), 0) == lax.broadcasted_iota(
        jnp.int32, (rows, rows), 1
    )

    def strip(part):
        return pl.ds(pl.multiple_of(part * block, block), block)

    def over(function, start):
        return lax.fori_loop(0, width // block, function, start)

    def add_squares(part, totals):
        values = [current[:, strip(part)] for current, low, gram, rest in problems]
        return [total + jnp.sum(value * value) for total, value in zip(totals, values)]

    totals = over(add_squares, [jnp.float32(0.0)] * len(problems))
    scales = [1.0 / (jnp.sqrt(total) + 1e-07) for total in totals]

    def begin(part, carry):
        for scale, (current, low, gram, rest) in zip(scales, problems):
            values = current[:, strip(part)] * scale
            current[:, strip(part)] = values
            low[:, strip(part)] = values.astype(LOW)
        return carry

    over(begin, 0)

    def iteration(turn, carry):
        for current, low, gram, rest in problems:
            gram[...] = jnp.zeros_like(gram)

        def add_gram(part, carry):
            for current, low, gram, rest in problems:
                values = low[:, strip(part)]
                gram[...] = gram[...] + dot(values, values, 1, 1)
            return carry

        over(add_gram, 0)
        seconds = []
        for current, low, gram, rest in problems:
            whole = gram[...]
            middle = jnp.sum(jnp.where(eye, whole, 0.0)) / rows
            rest[...] = (whole - jnp.where(eye, middle, 0.0)).astype(LOW)
            square = dot(rest[...], rest[...], 1, 0)
            whole = gram[...]
            centred = whole - jnp.where(eye, middle, 0.0)
            square = square + 2.0 * middle * centred + jnp.where(eye, middle * middle, 0.0)
            whole = NEWTON_B * whole + NEWTON_C * square
            second = jnp.sum(jnp.where(eye, whole, 0.0)) / rows
            rest[...] = (whole - jnp.where(eye, second, 0.0)).astype(LOW)
            seconds.append(second)

        def apply(part, carry):
            for second, (current, low, gram, rest) in zip(seconds, problems):
                values = (NEWTON_A + second) * current[:, strip(part)] + dot(
                    rest[...], low[:, strip(part)], 1, 0
                )
                current[:, strip(part)] = values
                low[:, strip(part)] = values.astype(LOW)
            return carry

        over(apply, 0)
        return carry

    lax.fori_loop(0, NS_STEPS, iteration, 0)


def newton_scratch(rows, width):
    return [
        pltpu.VMEM((rows, width), FULL),
        pltpu.VMEM((rows, width), LOW),
        pltpu.VMEM((rows, rows), FULL),
        pltpu.VMEM((rows, rows), LOW),
    ]


def newton_cost(count, rows, width):
    return pl.CostEstimate(
        flops=NS_STEPS * count * (4 * rows * rows * width + 2 * rows * rows * rows),
        bytes_accessed=6 * count * rows * width,
        transcendentals=0,
    )


def newton_body(factor_ref, mom_ref, grad_ref, out_ref, *problem):
    current, low = problem[:2]
    parts, rows, columns = mom_ref.shape
    factor = factor_ref[0]
    size = grad_ref.shape[1]
    for part in range(parts):
        spot = slice(part * columns, (part + 1) * columns)
        for source in range(parts):
            here = slice(source * size, (source + 1) * size)
            current[here, spot] = MOMENTUM * mom_ref[part, here, :].astype(
                FULL
            ) + factor * grad_ref[source, :, spot].astype(FULL)
    newton_steps([problem])
    for part in range(parts):
        out_ref[part] = low[:, part * columns : (part + 1) * columns]


def newton_small_body(rows, factor_ref, mom_ref, grad_ref, kv_ref, out_ref, *scratch):
    problems = [scratch[4 * at : 4 * at + 4] for at in range(4)]
    parts, _, columns = mom_ref.shape
    kv_columns = kv_ref.shape[2]
    half = rows // 2
    factor = factor_ref[0]
    for part in range(parts):
        spot = slice(part * columns, (part + 1) * columns)
        for member in range(2):
            current = problems[member][0]
            here = slice(member * rows, (member + 1) * rows)
            mom, grad = mom_ref[part, here, :], grad_ref[part, here, :]
            current[:, spot] = MOMENTUM * mom.astype(FULL) + factor * grad.astype(FULL)
        spot = slice(part * kv_columns, (part + 1) * kv_columns)
        for member in range(2):
            current = problems[2 + member][0]
            piece = kv_ref[part, member * rows : (member + 1) * rows, :].astype(FULL)
            for side in range(2):
                lane = (2 * member + side) * kv_columns
                mom = mom_ref[part, 2 * rows : 2 * rows + half, lane : lane + kv_columns]
                here = slice(side * half, (side + 1) * half)
                current[here, spot] = MOMENTUM * mom.astype(FULL) + factor * piece[here]
    newton_steps(problems[:2])
    newton_steps(problems[2:])
    out_ref[...] = jnp.zeros_like(out_ref)
    for part in range(parts):
        for member in range(2):
            out_ref[part, member * rows : (member + 1) * rows, :] = problems[member][1][
                :, part * columns : (part + 1) * columns
            ]
            low = problems[2 + member][1]
            for side in range(2):
                lane = (2 * member + side) * kv_columns
                out_ref[part, 2 * rows : 2 * rows + half, lane : lane + kv_columns] = low[
                    side * half : (side + 1) * half,
                    part * kv_columns : (part + 1) * kv_columns,
                ]


def newton_any_body(rows, factor_ref, mom_ref, grad_ref, qo_ref, kv_ref, out_ref, *scratch):
    parts = mom_ref.shape[0]
    owner = lax.rem(3 + lax.rem(lax.axis_index("wide"), 2), parts)
    small = lax.axis_index("narrow") == owner

    @pl.when(small)
    def _():
        newton_small_body(rows, factor_ref, mom_ref, qo_ref, kv_ref, out_ref, *scratch[4:])

    @pl.when(jnp.logical_not(small))
    def _():
        newton_body(factor_ref, mom_ref, grad_ref, out_ref, *scratch[:4])


def newton(factor, mom, grad, qo_grad, kv_grad):
    parts, slot_rows, columns = mom.shape
    width = parts * columns
    rows = kv_grad.shape[1] // 2
    kv_width = parts * kv_grad.shape[2]
    return pl.pallas_call(
        functools.partial(newton_any_body, rows),
        in_specs=[pl.BlockSpec(memory_space=pltpu.SMEM)] + [VMEM] * 4,
        out_specs=VMEM,
        out_shape=struct(mom.shape, LOW),
        scratch_shapes=newton_scratch(slot_rows, width)
        + newton_scratch(rows, width) * 2
        + newton_scratch(rows, kv_width) * 2,
        compiler_params=pltpu.CompilerParams(vmem_limit_bytes=VMEM_BYTES),
        cost_estimate=newton_cost(1, slot_rows, width),
        name="newton",
    )(factor.reshape(1), mom, grad, qo_grad, kv_grad)


def lookup_body(ids_ref, turn_ref, table_ref, out_ref, low_ref, list_ref, held, rows, sem):
    vocab = table_ref.shape[0]
    count = out_ref.shape[0]
    load = pltpu.make_async_copy(table_ref, held, sem)
    load.start()
    rows[...] = jnp.zeros_like(rows)

    found = turn_ref[count]

    def note(group, carry):
        for member in range(UNROLL):
            at = group * UNROLL + member
            list_ref[turn_ref[at]] = at
        return carry

    lax.fori_loop(0, count // UNROLL, note, 0)
    for member in range(UNROLL):
        list_ref[found + member] = count
    list_ref[count + UNROLL] = found
    load.wait()

    def step(group, carry):
        for member in range(UNROLL):
            at = list_ref[group * UNROLL + member]
            spot = jnp.minimum(ids_ref[jnp.minimum(at, count - 1)], vocab - 1)
            rows[pl.ds(at, 1), :] = held[pl.ds(spot, 1), :]
        return carry

    lax.fori_loop(0, (found + UNROLL - 1) // UNROLL, step, 0)
    out_ref[...] = rows[pl.ds(0, count), :].astype(LOW)
    low_ref[...] = held[...].astype(LOW)


def lookup(table, ids):
    vocab, columns = table.shape
    count = ids.shape[0]
    mine = (ids < vocab).reshape(-1, 128)
    before = jnp.arange(128)[:, None] < jnp.arange(128)[None, :]
    in_row = dot(mine.astype(LOW), before.astype(LOW), 1, 0)
    per_row = jnp.sum(mine.astype(FULL), axis=1)
    lines = jnp.arange(mine.shape[0])
    ahead = jnp.sum(jnp.where(lines[:, None] > lines[None, :], per_row[None, :], 0.0), axis=1)
    found = jnp.sum(per_row).astype(jnp.int32)
    turns = (in_row + ahead[:, None]).astype(jnp.int32)
    turns = jnp.where(mine, turns, count + UNROLL + 1).reshape(-1)
    turns = jnp.concatenate([turns, jnp.full((128,), found)])
    return pl.pallas_call(
        lookup_body,
        in_specs=[pl.BlockSpec(memory_space=pltpu.SMEM)] * 2 + [ANY],
        out_specs=[VMEM, VMEM, pl.BlockSpec(memory_space=pltpu.SMEM)],
        scratch_shapes=[
            pltpu.VMEM((vocab, columns), FULL),
            pltpu.VMEM((count + 8, columns), FULL),
            pltpu.SemaphoreType.DMA,
        ],
        out_shape=[
            struct((count, columns), LOW),
            struct((vocab, columns), LOW),
            struct((count + 2 * UNROLL,), jnp.int32),
        ],
        compiler_params=pltpu.CompilerParams(vmem_limit_bytes=VMEM_BYTES),
        cost_estimate=pl.CostEstimate(
            flops=0, bytes_accessed=vocab * columns * 4, transcendentals=0
        ),
        name="lookup",
    )(ids, turns, table)


def spread_body(
    ids_ref, list_ref, rows_ref, head_ref, out_ref, square_ref, even, odd, rows, sem
):
    vocab = out_ref.shape[0]
    count = rows_ref.shape[0]
    chunk = 256

    def strip(part):
        return pl.ds(pl.multiple_of(part * chunk, chunk), chunk)

    def begin(part, carry):
        even[strip(part), :] = head_ref[strip(part), :].astype(FULL)
        odd[strip(part), :] = jnp.zeros((chunk, odd.shape[1]), FULL)
        return carry

    lax.fori_loop(0, vocab // chunk, begin, 0)

    def widen(part, carry):
        rows[strip(part), :] = rows_ref[strip(part), :].astype(FULL)
        return carry

    lax.fori_loop(0, count // chunk, widen, 0)
    rows[pl.ds(count, 8), :] = jnp.zeros((8, rows.shape[1]), FULL)

    def step(group, carry):
        for member in range(UNROLL):
            at = list_ref[group * UNROLL + member]
            spot = jnp.minimum(ids_ref[jnp.minimum(at, count - 1)], vocab - 1)
            total = even if member % 2 == 0 else odd
            total[pl.ds(spot, 1), :] = total[pl.ds(spot, 1), :] + rows[pl.ds(at, 1), :]
        return carry

    found = list_ref[count + UNROLL]
    lax.fori_loop(0, (found + UNROLL - 1) // UNROLL, step, 0)

    def finish(part, squares):
        value = even[strip(part), :] + odd[strip(part), :]
        even[strip(part), :] = value
        return squares + jnp.sum((value * value).reshape(chunk // 8, 8, -1), axis=0)

    square_ref[...] = lax.fori_loop(
        0, vocab // chunk, finish, jnp.zeros((8, even.shape[1]), FULL)
    )
    store = pltpu.make_async_copy(even, out_ref, sem)
    store.start()
    store.wait()


def spread(ids, listed, rows, head):
    vocab, columns = head.shape
    count = ids.shape[0]
    smem = pl.BlockSpec(memory_space=pltpu.SMEM)
    return pl.pallas_call(
        spread_body,
        in_specs=[smem, smem, VMEM, VMEM],
        out_specs=[ANY, VMEM],
        scratch_shapes=[
            pltpu.VMEM((vocab, columns), FULL),
            pltpu.VMEM((vocab, columns), FULL),
            pltpu.VMEM((count + 8, columns), FULL),
            pltpu.SemaphoreType.DMA,
        ],
        out_shape=[struct((vocab, columns), FULL), struct((8, columns), FULL)],
        compiler_params=pltpu.CompilerParams(vmem_limit_bytes=VMEM_BYTES),
        cost_estimate=pl.CostEstimate(
            flops=count * columns, bytes_accessed=vocab * columns * 8, transcendentals=0
        ),
        name="spread",
    )(ids, listed, rows, head)


def adamw(weight, first_m, second_m, grad, rate, decay):
    first_new = BETA_ONE * first_m + (1.0 - BETA_ONE) * grad
    second_new = BETA_TWO * second_m + (1.0 - BETA_TWO) * grad * grad
    update = (
        first_new
        / (1.0 - BETA_ONE**STEP)
        / (jnp.sqrt(second_new / (1.0 - BETA_TWO**STEP)) + ADAM_EPS)
    )
    return (weight * (1.0 - rate * decay) - rate * update, first_new, second_new)


def cut_columns(values, count):
    rows, columns = values.shape
    return jnp.moveaxis(values.reshape(rows, count, columns // count), 1, 0)


def shifted(parts, axis, step):
    count = lax.axis_size(axis)
    pairs = [(source, (source + step) % count) for source in range(count)]
    return lax.ppermute(parts, axis, pairs)


def per_device(
    tokens,
    picks,
    targets,
    lengths,
    skip,
    embed,
    embed_m,
    embed_v,
    attn_qo,
    attn_qo_mom,
    attn_kv,
    attn_kv_mom,
    ffn,
    ffn_mom,
    gains,
    gains_m,
    gains_v,
):
    wide_count = lax.axis_size("wide")
    narrow_count = lax.axis_size("narrow")
    narrow_spot = lax.axis_index("narrow")
    wide_spot = lax.axis_index("wide")
    seq_len = tokens.shape[1]
    sel = picks.shape[1]
    vocab_rows, columns = embed.shape
    width = columns * wide_count
    own_rows = sel // narrow_count
    tok_rows = seq_len // narrow_count
    all_rows = own_rows + tok_rows
    heads_own = HEADS // narrow_count
    head_cols = heads_own * HD
    repeat = max(1, narrow_count // KVH)
    groups = KVH * repeat // narrow_count
    ffn_rows = ffn.shape[0]
    ffn_size = ffn_rows // narrow_count
    total_rows = wide_count * sel
    lens = lengths[0]
    pick_ids = picks[0]
    keep_layer = (1 - skip[0]).astype(FULL)
    keep_row = jnp.full((1, width), keep_layer)
    lanes = 128

    def box(flat):
        height = -(-flat.shape[0] // (8 * lanes)) * 8
        return jnp.pad(flat, (0, height * lanes - flat.shape[0])).reshape(height, lanes)

    ffn_low = jnp.moveaxis(ffn, 1, 0).astype(LOW)
    ffn_cut = ffn_low.reshape(3, narrow_count, ffn_size, ffn_low.shape[2])
    ffn_cut = jnp.moveaxis(ffn_cut, 1, 0).reshape(narrow_count, 3 * ffn_size, -1)
    kv_own = attn_kv.reshape(columns, -1).astype(LOW)

    where_at = jnp.arange(seq_len, dtype=jnp.int32)
    pick_tokens = jnp.sum(
        jnp.where(pick_ids[:, None] == where_at[None, :], tokens[0][None, :], 0), axis=1
    )
    ints = box(jnp.concatenate([tokens[0], pick_tokens, targets[0]]))
    all_ints, all_gains, kv_part = launch(
        [
            gather_wide(ints),
            gather_both(box(gains.astype(LOW).astype(FULL).reshape(-1))),
            gather_blocks("narrow", kv_own),
        ],
        0,
        "gather_ids",
    )
    kv_part = jnp.moveaxis(kv_part, 0, 1).reshape(columns, -1)
    proj_own = jnp.concatenate([kv_part, attn_qo.reshape(columns, -1).astype(LOW)], axis=1)
    proj = lax.all_gather(proj_own, "wide", axis=0, tiled=True)
    ffn_cut, all_ints = lax.optimization_barrier((ffn_cut, all_ints))
    ffn_pieces = [lax.dynamic_index_in_dim(ffn_cut, narrow_spot, 0, False)] + [
        shifted(
            lax.dynamic_index_in_dim(
                ffn_cut, lax.rem(narrow_spot + step, narrow_count), 0, False
            ),
            "narrow",
            step,
        )
        for step in range(1, narrow_count)
    ]
    gain_size = gains.shape[1]
    gain_w = all_gains.reshape(narrow_count, wide_count, -1)[:, :, : 3 * gain_size]
    gain_w = gain_w.reshape(narrow_count, wide_count, 3, gain_size)
    gain_w = jnp.transpose(gain_w, (2, 1, 0, 3)).reshape(3, width)
    all_ints = all_ints.reshape(wide_count, -1)
    tokens_all = all_ints[:, :seq_len].reshape(wide_count, narrow_count, tok_rows)
    picked_all = all_ints[:, seq_len : seq_len + sel].reshape(wide_count, narrow_count, own_rows)
    targets_all = all_ints[:, seq_len + sel : seq_len + 2 * sel].reshape(-1)
    wanted = jnp.moveaxis(jnp.concatenate([tokens_all, picked_all], axis=2), 1, 0).reshape(-1)
    local_ids = wanted - narrow_spot * vocab_rows
    inside = (local_ids >= 0) & (local_ids < vocab_rows)
    spots = jnp.where(inside, local_ids, vocab_rows)
    found, embed_low, listed = lookup(embed, spots)
    ffn_pieces, found = lax.optimization_barrier((ffn_pieces, found))
    ffn_sub = assemble(ffn_pieces).reshape(3, ffn_size, width)
    ffn_sub, found = lax.optimization_barrier((ffn_sub, found))
    ffn_w = lax.all_gather(ffn_sub, "wide", axis=0)
    found = found.reshape(narrow_count, wide_count * all_rows, columns)
    embed_cut = embed_low.reshape(wide_count, vocab_rows // wide_count, columns)
    third = embed_cut.shape[1] // 48 * 16
    rows_low = launch([fetch_rows(found, all_rows)], 1, "fetch_rows")[0]

    mom_qo = jnp.moveaxis(attn_qo_mom, 1, 0)
    mom_kv = jnp.moveaxis(attn_kv_mom, 1, 0)
    mom_ffn = jnp.moveaxis(ffn_mom, 1, 0)
    slot_rows, slot_cols = mom_ffn.shape[1:]

    block_rows, q_size = mom_qo.shape[1:]
    kv_size = mom_kv.shape[2]
    half_rows = block_rows // 2
    kv_box = jnp.moveaxis(mom_kv.reshape(4, half_rows, kv_size), 0, 1).reshape(half_rows, -1)
    small_box = jnp.concatenate([mom_qo.reshape(2 * block_rows, q_size), kv_box])
    small_box = jnp.pad(small_box, ((0, slot_rows - small_box.shape[0]), (0, 0)))
    mom_parts = jnp.concatenate([mom_ffn, small_box[None]]).astype(LOW)

    seg_all, cosine_all, sine_all = angles_at(lens, where_at)
    cosine_all, sine_all = wide_angles(cosine_all, sine_all)
    seg_mine, cosine, sine = angles_at(lens, pick_ids)
    cosine, sine = wide_angles(cosine, sine)

    def tok_part(angles):
        return lax.dynamic_slice_in_dim(angles, narrow_spot * tok_rows, tok_rows, 0)

    by_head, normed_tok = make_heads(
        rows_low, gain_w[0:1], proj, tok_part(cosine_all), tok_part(sine_all), groups, repeat
    )
    own_head, start_low, tok_cols, table_top = launch(
        [
            swap_blocks("narrow", by_head),
            gather_blocks("narrow", rows_low[tok_rows:]),
            split_columns("wide", normed_tok),
            join_columns("wide", embed_cut[:, :third]),
        ],
        2,
        "trade_heads",
    )
    start_low, ffn_w = lax.optimization_barrier((start_low, ffn_w))
    start_low = start_low.reshape(sel, width)
    queries, probs, mixed, attn_part, normed, early_part = attend(
        start_low,
        gain_w,
        proj,
        own_head,
        cosine,
        sine,
        seg_mine[:, None],
        seg_all[None, :],
        pick_ids[:, None],
    )
    early = lax.all_gather(early_part, "wide", axis=0, tiled=True)
    start_own = rows_low[tok_rows:].astype(FULL)
    middle, inner, table_middle = launch(
        [
            settle(
                attn_part,
                start_own,
                start_own,
                jnp.ones((1, width), FULL),
                gain_w[1:2],
            ),
            join_columns("wide", embed_cut[:, third : 2 * third]),
        ],
        3,
        "settle_middle",
    )
    inner = inner.reshape(sel, width)
    inner_all = lax.all_gather(inner, "wide", axis=0, tiled=True)
    gate, up, hidden, fed = feed(inner, ffn_w)
    final_own, late_part, table_low = launch(
        [
            settle(fed, middle, start_own, keep_row, gain_w[2:3]),
            join_columns("wide", embed_cut[:, 2 * third :]),
        ],
        4,
        "settle_late",
    )
    table_own = jnp.concatenate([table_top, table_middle, table_low])

    table_count = table_own.shape[0]
    local_target = targets_all - (narrow_spot * vocab_rows + wide_spot * table_count)
    has_target = jnp.arange(table_count, dtype=jnp.int32)[:, None] == local_target[None, :]
    counted = (targets_all >= 0).astype(FULL)
    loss_count = jnp.sum(counted)

    def exit_logits(features):
        logits = dot(table_own, features, 1, 1)
        peak = jnp.max(logits, axis=0)
        total = jnp.sum(jnp.exp(logits - peak[None, :]), axis=0)
        picked = jnp.sum(jnp.where(has_target, logits, 0.0), axis=0)
        return logits, jnp.stack([peak, total, picked])

    half = slot_rows // 2
    late, mom_top, early_logits, early_stats = launch(
        [
            gather_wide(late_part.reshape(sel, width)),
            swap_turned(mom_parts[:, :half]),
            exit_stats(early, table_own, local_target[None, :]),
        ],
        5,
        "gather_late",
    )
    late = late.reshape(total_rows, width)
    late_logits, late_stats = exit_logits(late)
    stats = jnp.concatenate([early_stats, late_stats], axis=1).reshape(3, 8, -1)
    stats = launch([combine(stats, merge_stats)], 6, "combine_stats")[0]
    stats, inner_all = lax.optimization_barrier((stats, inner_all))
    stats = stats.reshape(3, -1)
    log_norms = stats[0] + jnp.log(stats[1])
    losses = log_norms - stats[2]
    loss_sum = jnp.sum(
        counted * (EXIT_EARLY * losses[:total_rows] + EXIT_LAST * losses[total_rows:])
    )

    def exit_back(logits, log_norm, weight):
        grad_logits = (
            (jnp.exp(logits - log_norm[None, :]) - has_target.astype(FULL))
            * (weight * counted)[None, :]
        ).astype(LOW)
        return grad_logits

    late_grad = exit_back(late_logits, log_norms[total_rows:], EXIT_LAST)
    late_back = dot(late_grad, table_own, 0, 0).astype(LOW)
    early_grad = exit_back(early_logits, log_norms[:total_rows], EXIT_EARLY)
    grad_late, mom_low, early_back, _ = launch(
        [
            sum_wide(late_back),
            swap_turned(mom_parts[:, half:]),
            later(product([early_grad], [table_own], 0, [[(0, 0)]]), 1),
        ],
        7,
        "sum_late",
    )
    mom_owned = jnp.concatenate([mom_top, mom_low], axis=1)
    early_back, grad_late = lax.optimization_barrier((early_back, grad_late))
    grad_early = lax.psum_scatter(early_back[0], "wide", scatter_dimension=0, tiled=True)
    grad_final, gain_late, grad_out, mixed_wide, pick_cols = launch(
        [
            settle_back(
                grad_late.astype(LOW),
                final_own,
                jnp.zeros_like(final_own),
                keep_row,
                gain_w[2:3],
            ),
            gather_wide(mixed),
            split_columns("wide", normed),
        ],
        8,
        "back_late",
    )
    grad_layer = grad_final * keep_layer
    grad_out = grad_out.reshape(sel, width)
    out_all = lax.all_gather(grad_out, "wide", axis=0, tiled=True)
    acts, fed_back = feed_back(grad_out, ffn_w, gate, up, hidden)
    grad_mid, gain_mid, grad_branch, acts = launch(
        [
            settle_back(fed_back, middle, grad_layer, keep_row, gain_w[1:2]),
            swap_blocks("wide", acts),
        ],
        9,
        "back_middle",
    )
    acts = jnp.moveaxis(acts, 1, 0).reshape(3, total_rows, ffn_size)
    grad_branch, grad_early = lax.optimization_barrier((grad_branch, grad_early))
    grad_branch = grad_branch.reshape(sel, width)

    kv_parts, grad_queries, pick_part, gain_pick, gain_early = attend_back(
        grad_branch,
        proj,
        own_head,
        queries,
        probs,
        cosine,
        sine,
        cosine_all,
        sine_all,
        start_low,
        gain_w,
        grad_early,
    )
    grad_kv, grad_pick, queries_wide, branch_cols, grad_head, _ = launch(
        [
            swap_blocks("narrow", kv_parts),
            sum_narrow(pick_part),
            gather_wide(grad_queries),
            split_columns("wide", grad_branch),
            product([early_grad, late_grad], [early, late], 1, [[(0, 0), (1, 1)]]),
        ],
        10,
        "trade_grads",
    )
    grad_kv, out_all = lax.optimization_barrier((grad_kv, out_all))
    grad_base = grad_mid + grad_final * (1.0 - keep_layer)
    grad_rows, gain_attn, grad_kv = rows_back(
        rows_low, gain_w, proj, grad_kv, grad_pick, grad_base, repeat
    )
    gain_attn = gain_attn + gain_pick
    summed_qo = jnp.stack(
        [
            jnp.einsum("wtc,wtf->cf", pick_cols, queries_wide, preferred_element_type=FULL),
            jnp.einsum("wtc,wtf->cf", branch_cols, mixed_wide, preferred_element_type=FULL),
        ]
    )
    grad_rows, acts_owned, kv_wide, head_cols_all, grad_ffn, ffn_squares = launch(
        [
            return_rows(grad_rows),
            swap_owned(acts, 5),
            later(gather_wide(grad_kv, 3), 2),
            later(split_columns("wide", grad_head[0], 3), 2),
            product([acts], [inner_all, out_all], 0, [[(0, 0)], [(1, 0)], [(2, 1)]]),
        ],
        11,
        "return_rows",
    )
    turn = lax.rem(wide_spot, 2)
    grad_kv_w = jnp.einsum(
        "wtc,wtf->cf", tok_cols, kv_wide, preferred_element_type=FULL
    ).reshape(columns, narrow_count, 2, kv_size)
    grad_kv_w = jnp.moveaxis(grad_kv_w, 0, 2)
    summed_kv = lax.psum_scatter(grad_kv_w, "narrow", scatter_dimension=0, tiled=True)[0]
    summed_table, table_squares = spread(
        spots, listed, grad_rows.reshape(-1, columns), head_cols_all.reshape(vocab_rows, columns)
    )

    squares = (
        jnp.sum(summed_qo * summed_qo)
        + jnp.sum(summed_kv * summed_kv)
        + jnp.sum(ffn_squares)
        + jnp.sum(table_squares)
    )
    sums = jnp.stack(
        [gain_attn[0], gain_mid[0], gain_early[0] + gain_late[0], jnp.full((width,), squares)]
    )
    def owns_last():
        away = lax.axis_index("narrow") + narrow_count - lax.rem(lax.axis_index("wide"), 2)
        return lax.rem(away, narrow_count) >= 2

    sums, kv_owned, qo_owned, owned, _ = launch(
        [
            combine(sums.reshape(4, 8, -1), add_two),
            send_owner(summed_kv.astype(LOW).reshape(2 * block_rows, kv_size)),
            later(send_owner(summed_qo.astype(LOW).reshape(2 * columns, q_size)), 1),
            later(
                product(
                    [acts_owned],
                    [inner_all, out_all],
                    0,
                    [[(at, 0)] for at in range(narrow_count)],
                    False,
                    owns_last,
                ),
                1,
            ),
        ],
        12,
        "combine_sums",
    )
    sums = sums.reshape(4, width)
    summed_gain = lax.dynamic_slice_in_dim(
        sums[:3], (wide_spot * narrow_count + narrow_spot) * gain_size, gain_size, 1
    )
    square_total = sums[3, 0] + jnp.sum(sums[:3] * sums[:3])
    grad_norm = jnp.sqrt(square_total) / loss_count
    factor = jnp.minimum(1.0, CLIP_NORM / (grad_norm + 1e-06)) / loss_count

    final_parts, factor = lax.optimization_barrier((grad_ffn, factor))
    size = width // narrow_count

    def final_piece(spot):
        return lax.dynamic_slice_in_dim(final_parts, spot * size, size, 2)

    pieces = [final_piece(narrow_spot)] + [
        shifted(final_piece(lax.rem(narrow_spot + step, narrow_count)), "narrow", step)
        for step in range(1, narrow_count)
    ]
    directions = newton(
        factor, mom_owned, owned, qo_owned, kv_owned
    )
    directions, pieces, ffn, factor = lax.optimization_barrier(
        (directions, pieces, ffn, factor)
    )
    summed_ffn = jnp.zeros((3, narrow_count, ffn_size, size), LOW)
    for step, piece in enumerate(pieces):
        source = lax.rem(narrow_spot - step + narrow_count, narrow_count)
        summed_ffn = lax.dynamic_update_index_in_dim(summed_ffn, piece, source, 1)
    summed_ffn = summed_ffn.reshape(3, ffn_rows, size).astype(FULL)
    received = [lax.dynamic_index_in_dim(directions, narrow_spot, 0, False)] + [
        shifted(
            lax.dynamic_index_in_dim(
                directions, lax.rem(narrow_spot + step, narrow_count), 0, False
            ),
            "narrow",
            step,
        )
        for step in range(1, narrow_count)
    ]

    def direction_of(matrix):
        step = lax.rem(narrow_spot - matrix - turn + 2 * narrow_count, narrow_count)
        result = received[0]
        for at in range(1, narrow_count):
            result = jnp.where(step == at, received[at], result)
        return result

    dir_ffn = jnp.stack([direction_of(matrix) for matrix in range(3)]).astype(FULL)
    small = direction_of(3).astype(FULL)
    dir_qo = small[: 2 * block_rows].reshape(mom_qo.shape)
    dir_kv = small[2 * block_rows : 2 * block_rows + half_rows].reshape(half_rows, 4, kv_size)
    dir_kv = jnp.moveaxis(dir_kv, 1, 0).reshape(mom_kv.shape)

    embed_new, embed_m_new, embed_v_new = adamw(
        embed, embed_m, embed_v, summed_table * factor, RATE_ADAM, WEIGHT_DECAY
    )
    gains_new, gains_m_new, gains_v_new = adamw(
        gains, gains_m, gains_v, summed_gain * factor, RATE_GAIN, 0.0
    )

    def mom_next(mom, grad):
        return MOMENTUM * mom + jnp.moveaxis(grad * factor, 0, 1)

    shrink = 1.0 - RATE_MUON * WEIGHT_DECAY

    def weight_next(weight, direction):
        return weight * shrink - RATE_MUON * jnp.moveaxis(direction, 0, 1)

    return (
        loss_sum,
        loss_count,
        grad_norm,
        embed_new,
        embed_m_new,
        embed_v_new,
        weight_next(attn_qo, dir_qo),
        mom_next(attn_qo_mom, summed_qo),
        weight_next(attn_kv, dir_kv),
        mom_next(attn_kv_mom, summed_kv),
        weight_next(ffn, dir_ffn),
        mom_next(ffn_mom, summed_ffn),
        gains_new,
        gains_m_new,
        gains_v_new,
    )


def solution(mesh):
    by_pack = P("wide", None)
    table = P("narrow", "wide")
    layer = P("wide", None, "narrow")
    gain = P(None, ("wide", "narrow"))
    return jax.shard_map(
        per_device,
        mesh=mesh,
        in_specs=(by_pack,) * 4 + (P("wide"),) + (table,) * 3 + (layer,) * 6 + (gain,) * 3,
        out_specs=(P(),) * 3 + (table,) * 3 + (layer,) * 6 + (gain,) * 3,
        check_vma=False,
    )
```
